32 devices in a mesh: bead: 16 (over z, x, core), space: 2 (over y).
Axes of the slice: x: 2, y: 2, z: 4, core: 2. Of those that a mesh axis runs over, the one named last changes fastest.
Arguments:
- positions: float32 [16, 3, 1024], P('bead', None, 'space'), may hold values from -6 to 6
- momenta: float32 [16, 3, 1024], P('bead', None, 'space'), may hold values from -6 to 6
- species: int32 [1024], P('space'), may hold values from 0 to 1
- neighbours: int32 [8, 1024], P(None, 'space'), may hold values from 0 to 1023
- send_list: int32 [1024], P('space'), may hold values from 0 to 511
- embedding: float32 [2, 128], replicated, may hold values from -4 to 4
- radial_one: float32 [8, 128], replicated, may hold values from -4 to 4
- radial_two: float32 [8, 128], replicated, may hold values from -4 to 4
- mix_one: float32 [128, 384], replicated, may hold values from -0.3125 to 0.3125
- mix_two: float32 [128, 384], replicated, may hold values from -0.3125 to 0.3125
- read_one: float32 [128], replicated, may hold values from -0.5 to 0.5
- read_two: float32 [128], replicated, may hold values from -0.5 to 0.5
Outputs:
- new_positions: float32 [16, 3, 1024], P('bead', None, 'space')
- new_momenta: float32 [16, 3, 1024], P('bead', None, 'space')
The draws below stay inside these ranges and needn't reach their ends.
Inputs may be any that keep to these rules, and one draw needn't show every extreme that they name: `neighbours`: positions in the extended set of the atom's own domain: below 256 the ghosts from the lower domain, then the 512 own atoms, then the ghosts from the upper domain. `send_list`: entries d * 512 to d * 512 + 255 are sent to domain d - 1, the next 256 to domain d + 1.
All inputs are finite; a program needn't handle non-finite values.
Results may differ from the reference program's by a relative error of at most 0.0003.
Values sent between devices are 32-bit elements; how exact they have to be, the bound alone decides.
No kernel may reach another device: no remote copies, remote signals or barrier semaphores. Data moves between devices by JAX's collectives and lax.ppermute only.
A program may use at most 128 MiB of HBM per device.

```python
import math
import jax
import jax.numpy as jnp
from jax import lax

C = 128
NB = 8
K = 8
ATOMS_DEV = 512
ATOMS = 1024
BEADS = 16
N_SPACE = 2


def plant(values, key, least, high):
    shape = values.shape
    index_at = [jax.random.randint(jax.random.fold_in(key, axis), (), 0, shape[axis]) for axis in range(len(shape))]
    values = values.at[tuple(index_at)].set(least)
    longest = shape.index(max(shape))
    index_at[longest] = (index_at[longest] + 1) % shape[longest]
    return values.at[tuple(index_at)].set(high)


def shard_levels(key, extent, shards, smallest, top_value):
    loudness = 1.0
    for position, shards_of in shards:
        draws = jax.random.uniform(jax.random.fold_in(jax.random.fold_in(key, 6), position), (shards_of,), jnp.float32, smallest / len(shards), top_value / len(shards))
        loudness = loudness * jnp.repeat(jnp.exp(draws), extent[position] // shards_of).reshape((-1,) + (1,) * (len(extent) - 1 - position))
    return loudness


def gaussian(key, extent, deviation, most, cuts=(), held_as=jnp.bfloat16):
    array = jax.random.normal(key, extent, jnp.float32) * deviation
    if len(cuts) > 0:
        array = shard_levels(key, extent, cuts, -0.22, 0.18) * array
    return jnp.clip(array, min=-most, max=most).astype(held_as)


def setup_inputs(seed: int = 0) -> dict:
    arg_keys = jax.random.split(jax.random.key(seed), 13)
    positions = gaussian(arg_keys[0], (BEADS, 3, ATOMS), 1.5, 6.0, ((0, 16), (2, 2)), jnp.float32)
    momenta = gaussian(arg_keys[1], (BEADS, 3, ATOMS), 1.0, 6.0, ((0, 16), (2, 2)), jnp.float32)
    species = plant(jax.random.randint(arg_keys[2], (ATOMS,), 0, 2), jax.random.fold_in(arg_keys[2], 1), 0, 1).astype(jnp.int32)
    neighbours = plant(jax.random.randint(arg_keys[3], (K, ATOMS), 0, 2 * ATOMS_DEV), jax.random.fold_in(arg_keys[3], 1), 0, (2 * ATOMS_DEV) - 1).astype(jnp.int32)
    send_list = plant(jax.random.randint(arg_keys[4], (ATOMS,), 0, ATOMS_DEV), jax.random.fold_in(arg_keys[4], 1), 0, ATOMS_DEV - 1).astype(jnp.int32)
    embedding = gaussian(arg_keys[5], (2, C), 1.0, 4.0, (), jnp.float32)
    radial_one = gaussian(arg_keys[6], (NB, C), 1.0, 4.0, (), jnp.float32)
    radial_two = gaussian(arg_keys[7], (NB, C), 1.0, 4.0, (), jnp.float32)
    mix_one = gaussian(arg_keys[8], (C, 3 * C), (3 * C) ** -0.5, 0.3125, (), jnp.float32)
    mix_two = gaussian(arg_keys[9], (C, 3 * C), (3 * C) ** -0.5, 0.3125, (), jnp.float32)
    read_one = gaussian(arg_keys[10], (C,), C ** -0.5, 0.5, (), jnp.float32)
    read_two = gaussian(arg_keys[11], (C,), C ** -0.5, 0.5, (), jnp.float32)
    return dict(positions=positions, momenta=momenta, species=species, neighbours=neighbours, send_list=send_list, embedding=embedding, radial_one=radial_one, radial_two=radial_two, mix_one=mix_one, mix_two=mix_two, read_one=read_one, read_two=read_two)


EXACT = lax.Precision.HIGHEST
STEP = 2.0
HALF_STEP = 1.0
HEAVY = 16.0
SQRT3 = math.sqrt(3.0)
SQRT5 = math.sqrt(5.0)
SQRT15 = math.sqrt(15.0)

def harmonics(unit):
    ux, uy, uz = (unit[0], unit[1], unit[2])
    return jnp.stack([jnp.ones_like(ux), SQRT3 * ux, SQRT3 * uy, SQRT3 * uz, SQRT15 * ux * uy, SQRT15 * uy * uz, 0.5 * SQRT5 * (2.0 * uz * uz - ux * ux - uy * uy), SQRT15 * ux * uz, 0.5 * SQRT15 * (ux * ux - uy * uy)])

def interaction(ext_coords, centre, slots, ext_feat, radial, mixing):
    neigh_count = slots.shape[0]
    atom_count = slots.shape[1]
    flat_slots = slots.reshape(-1)
    relative = jnp.take(ext_coords, flat_slots, axis=1).reshape(3, neigh_count, atom_count) - centre[:, None, :]
    soft_dist = jnp.sqrt(lax.optimization_barrier(jnp.sum(relative * relative, axis=0)) + 1.0)
    sphere = harmonics(relative / soft_dist)
    centres = 1.0 + jnp.arange(radial.shape[0]).astype(jnp.float32)
    basis = jnp.exp(-0.5 * (soft_dist[None] - centres[:, None, None]) ** 2)
    edge_weight = jnp.einsum('nc,nka->cka', radial, basis, precision=EXACT)
    carried = edge_weight * jnp.take(ext_feat, flat_slots, axis=1).reshape(-1, neigh_count, atom_count)
    moments = jnp.einsum('lka,cka->lca', sphere, carried, precision=EXACT) / neigh_count
    squares = moments * moments
    invariants = jnp.concatenate([squares[0], lax.optimization_barrier(jnp.sum(squares[1:4], axis=0)), lax.optimization_barrier(jnp.sum(squares[4:9], axis=0))], axis=0)
    return jnp.dot(mixing, invariants, precision=EXACT)

def embed(embedding, flags):
    return embedding[0][:, None] + flags[None, :] * (embedding[1] - embedding[0])[:, None]

def normal_modes(bead_total):
    bead_idx = jnp.arange(bead_total).astype(jnp.float32)[:, None]
    mode_idx = jnp.arange(bead_total).astype(jnp.float32)[None, :]
    phase = 2.0 * jnp.pi * bead_idx * mode_idx / bead_total
    half_total = bead_total // 2
    table = jnp.where(mode_idx < half_total, math.sqrt(2.0 / bead_total) * jnp.cos(phase), math.sqrt(2.0 / bead_total) * jnp.sin(phase))
    table = jnp.where(mode_idx == half_total, jnp.cos(jnp.pi * bead_idx) / math.sqrt(bead_total), table)
    table = jnp.where(mode_idx == 0, 1.0 / math.sqrt(bead_total), table)
    return table

def mode_factors(bead_total):
    mode_idx = jnp.arange(bead_total).astype(jnp.float32)
    angles = float(bead_total) * jnp.sin(jnp.pi * mode_idx / bead_total)
    safe_angles = jnp.where(mode_idx == 0, 1.0, angles)
    cosine = jnp.cos(angles)
    reach = jnp.where(mode_idx == 0, STEP, STEP * jnp.sin(angles) / safe_angles)
    stiff = angles * jnp.sin(angles) / STEP
    return (cosine, reach, stiff)

def reference(positions, momenta, species, neighbours, send_list, embedding, radial_one, radial_two, mix_one, mix_two, read_one, read_two):
    domains = N_SPACE
    per_domain = ATOMS_DEV
    ghost_rows = per_domain // 2
    neigh_count = neighbours.shape[0]
    sends = send_list.reshape(domains, per_domain)
    offsets = (jnp.arange(domains).astype(jnp.int32) * per_domain)[:, None]
    lower_ids = jnp.roll(offsets, 1, axis=0) + jnp.roll(sends, 1, axis=0)[:, ghost_rows:]
    own_ids = offsets + jnp.arange(per_domain).astype(jnp.int32)[None, :]
    upper_ids = jnp.roll(offsets, -1, axis=0) + jnp.roll(sends, -1, axis=0)[:, :ghost_rows]
    extended = jnp.concatenate([lower_ids, own_ids, upper_ids], axis=1).astype(jnp.int32)
    local_ids = neighbours.reshape(neigh_count, domains, per_domain)
    wide_ext = jnp.broadcast_to(extended[None], (neigh_count, domains, 2 * per_domain))
    global_ids = jnp.take_along_axis(wide_ext, local_ids, axis=2).reshape(neigh_count, domains * per_domain).astype(jnp.int32)
    flags = species.astype(jnp.float32)
    masses = HEAVY - (HEAVY - 1.0) * flags
    base_feat = embed(embedding, flags)

    def energy(coords):
        hidden = base_feat + jax.nn.silu(interaction(coords, coords, global_ids, base_feat, radial_one, mix_one))
        top = interaction(coords, coords, global_ids, hidden, radial_two, mix_two)
        return jnp.sum(jnp.dot(read_two, jax.nn.silu(top), precision=EXACT)) + jnp.sum(jnp.dot(read_one, hidden, precision=EXACT))

    def bead_force(coords):
        return -jax.grad(energy)(coords)
    forces = lax.map(bead_force, positions)
    kicked = momenta + HALF_STEP * forces
    bead_total = positions.shape[0]
    modes_mat = normal_modes(bead_total)
    cosine, reach, stiff = mode_factors(bead_total)
    mode_q = jnp.einsum('bk,bca->kca', modes_mat, positions, precision=EXACT)
    mode_p = jnp.einsum('bk,bca->kca', modes_mat, kicked, precision=EXACT)
    moved_q = cosine[:, None, None] * mode_q + reach[:, None, None] * mode_p / masses[None, None, :]
    moved_p = cosine[:, None, None] * mode_p - stiff[:, None, None] * masses[None, None, :] * mode_q
    new_positions = jnp.einsum('bk,kca->bca', modes_mat, moved_q, precision=EXACT)
    new_momenta = jnp.einsum('bk,kca->bca', modes_mat, moved_p, precision=EXACT)
    return (new_positions, new_momenta)
```

```python
import functools
import math

import jax
import jax.numpy as jnp
import numpy as np
from jax import lax
from jax.experimental import pallas as pl
from jax.experimental.pallas import tpu as pltpu
from jax.sharding import PartitionSpec as P

STEP = 2.0
HALF_STEP = 1.0
HEAVY = 16.0
SQRT3 = math.sqrt(3.0)
SQRT5 = math.sqrt(5.0)
SQRT15 = math.sqrt(15.0)
LANES = 128
ORDERS = 9
GROUP = (0, 1, 1, 1, 2, 2, 2, 2, 2)
HEAD = 8
VMEM_BYTES = 56 * 1024 * 1024
f32 = jnp.float32
bf16 = jnp.bfloat16
HIGH = lax.Precision.HIGH


def split(x):
    hi = x.astype(bf16)
    return hi, (x - hi.astype(f32)).astype(bf16)


def split_rows(x):
    hi = x.astype(bf16).astype(f32)
    return jnp.concatenate([hi, x - hi], axis=0)


def dot(a, b, precision=None):
    return jnp.dot(a, b, preferred_element_type=f32, precision=precision)


def dot_nt(a, b):
    return lax.dot_general(a, b, (((1,), (1,)), ((), ())), preferred_element_type=f32)


def row(x, rows=8):
    return jnp.broadcast_to(x, (rows, x.shape[1]))


def lookup(chunks, wanted, position):
    out = None
    for number, chunk in chunks:
        got = jnp.take_along_axis(row(chunk), position, axis=1, mode="promise_in_bounds")
        out = got if out is None else jnp.where(wanted == number, got, out)
    return out


def harmonics(ux, uy, uz):
    return [
        None,
        SQRT3 * ux,
        SQRT3 * uy,
        SQRT3 * uz,
        SQRT15 * ux * uy,
        SQRT15 * uy * uz,
        0.5 * SQRT5 * (2.0 * uz * uz - ux * ux - uy * uy),
        SQRT15 * ux * uz,
        0.5 * SQRT15 * (ux * ux - uy * uy),
    ]


def silu_parts(v):
    gate = 1.0 / (1.0 + jnp.exp(-v))
    return v * gate, gate * (1.0 + v * (1.0 - gate))


def force_kernel(plan, *refs):
    atoms, near, wide, before, after = plan
    n_wide = len(wide)
    blocks = refs[:n_wide]
    emb_ref, rad1_ref, rad2_ref, mix1_ref, mix2_ref, read1_ref, read2_ref = refs[n_wide : n_wide + 7]
    grad_ref = refs[n_wide + 7]
    (
        geo_ref, y_ref, yb_ref, bk_ref, bt_ref, gidx_ref, as_ref, m1_ref, sp1_ref, hs_ref, oh_ref,
        hj_ref, w_ref, car_ref, m2_ref, inv_ref, dinv_ref, p_ref, dhe_ref, dw_ref, da_ref, q_ref,
        val_ref, ohlo_ref,
    ) = refs[n_wide + 8 :]
    chan = emb_ref.shape[1]
    bases = rad1_ref.shape[0]
    slots = gidx_ref.shape[0]
    n_near = len(near) * atoms
    tiles = atoms // LANES
    half = atoms // 2
    half_tiles = half // LANES
    edges = slots * atoms
    top_rows = val_ref.shape[0] // 6

    emb0 = emb_ref[0:1, :]
    emb_d = emb_ref[1:2, :] - emb0
    rr = jnp.concatenate([rad1_ref[...] * emb0, rad1_ref[...] * emb_d], axis=0) * (1.0 / slots)
    rr_hi = rr.astype(bf16).astype(f32)
    rr_lo = rr - rr_hi
    r2 = rad2_ref[...] * (1.0 / slots)
    r2_hi = r2.astype(bf16).astype(f32)
    r2_lo = r2 - r2_hi
    zeros = jnp.zeros((8, chan), f32)
    turned1 = jnp.concatenate([rr_hi, rr_hi, rr_lo, rr_lo] + [zeros] * 8, axis=0).T
    sides = jnp.concatenate([emb0, emb_d, read1_ref[...], read2_ref[...], zeros[:4]], axis=0)
    turned2 = jnp.concatenate([r2_hi, r2_hi, r2_lo, r2_lo, sides] + [zeros] * 11, axis=0).T
    rr_cols = turned1[:, : 8 * bases].astype(bf16)
    r2_cols = turned2[:, : 4 * bases].astype(bf16)
    emb0_col = turned2[:, 4 * bases : 4 * bases + 1]
    embd_col = turned2[:, 4 * bases + 1 : 4 * bases + 2]
    read1_col = turned2[:, 4 * bases + 2 : 4 * bases + 3]
    read2_col = turned2[:, 4 * bases + 3 : 4 * bases + 4]
    rr_rows = jnp.concatenate(
        [jnp.concatenate([rr_hi, rr_hi], axis=1), jnp.concatenate([rr_lo, jnp.zeros_like(rr_lo)], axis=1)], axis=0
    ).astype(bf16)
    r2_rows = jnp.concatenate(
        [jnp.concatenate([r2_hi, r2_hi], axis=1), jnp.concatenate([r2_lo, jnp.zeros_like(r2_lo)], axis=1)], axis=0
    ).astype(bf16)
    order_col = lax.broadcasted_iota(jnp.int32, (bases, LANES), 0).astype(f32)

    tables = []
    for quantity in range(4):
        chunks = []
        for g in range(n_wide):
            for t in range(tiles):
                chunks.append((g * tiles + t, blocks[g][quantity : quantity + 1, t * LANES : (t + 1) * LANES]))
        tables.append(chunks)
    for q in range(len(near)):
        ghosts = []
        for t in range(half_tiles):
            ghosts.append(
                (t, blocks[before[q]][4:5, half + t * LANES : half + (t + 1) * LANES] + float(before[q] * atoms))
            )
        for t in range(half_tiles):
            ghosts.append(
                (
                    half_tiles + tiles + t,
                    blocks[after[q]][4:5, t * LANES : (t + 1) * LANES] + float(after[q] * atoms),
                )
            )
        for t in range(tiles):
            cols = slice(t * LANES, (t + 1) * LANES)
            here = slice(q * atoms + t * LANES, q * atoms + (t + 1) * LANES)
            slot = blocks[q][HEAD : HEAD + slots, cols].astype(jnp.int32)
            chunk_no = slot >> 7
            far = lookup(ghosts, chunk_no, slot & 127).astype(jnp.int32)
            own = (slot >= half) & (slot < half + atoms)
            gidx = jnp.where(own, slot + (q * atoms - half), far)
            gidx_ref[:, here] = gidx
            chunk_no = gidx >> 7
            place = gidx & 127
            xj, yj, zj, fj = [lookup(tables[i], chunk_no, place) for i in range(4)]
            rx = xj - row(blocks[q][0:1, cols])
            ry = yj - row(blocks[q][1:2, cols])
            rz = zj - row(blocks[q][2:3, cols])
            soft = jnp.sqrt(rx * rx + ry * ry + rz * rz + 1.0)
            back = 1.0 / soft
            ux, uy, uz = rx * back, ry * back, rz * back
            for i, value in enumerate((ux, uy, uz, back, soft, fj)):
                geo_ref[i, :, here] = value
            sphere = harmonics(ux, uy, uz)
            for l in range(1, ORDERS):
                y_ref[l, :, here] = sphere[l]
                if q == 0:
                    for k in range(slots):
                        yb_ref[l, k, :, cols] = row(sphere[l][k : k + 1, :])
            for n in range(bases):
                bk_ref[n, :, here] = jnp.exp(-0.5 * (soft - (1.0 + n)) ** 2)
            for k in range(slots):
                basis = jnp.exp(-0.5 * (row(soft[k : k + 1, :], bases) - (1.0 + order_col)) ** 2)
                bt_ref[k, 0:bases, here] = basis
                bt_ref[k, bases : 2 * bases, here] = basis * row(fj[k : k + 1, :], bases)

    def sums(t, carry):
        here = pl.ds(pl.multiple_of(t * LANES, LANES), LANES)
        low = [None] * ORDERS
        for k in range(slots):
            basis = bt_ref[k, :, here]
            for l in range(ORDERS):
                term = basis if l == 0 else basis * row(y_ref[l, k : k + 1, here], 2 * bases)
                low[l] = term if low[l] is None else low[l] + term
        for l in range(ORDERS):
            both = split_rows(low[l]).astype(bf16)
            as_ref[l, 0 : 4 * bases, here] = both
            as_ref[l, 4 * bases : 8 * bases, here] = both
        return carry

    lax.fori_loop(0, n_near // LANES, sums, 0)

    flags_row = jnp.concatenate([blocks[q][3:4, :] for q in range(len(near))], axis=1)
    wide_cols = 2 * LANES

    def first(j, carry):
        here = pl.ds(pl.multiple_of(j * wide_cols, wide_cols), wide_cols)
        inv = [None, None, None]
        for l in range(ORDERS):
            m = dot(rr_cols, as_ref[l, :, here])
            m1_ref[l, :, here] = m
            inv[GROUP[l]] = m * m if inv[GROUP[l]] is None else inv[GROUP[l]] + m * m
        value = dot(mix1_ref[...], jnp.concatenate(inv, axis=0), HIGH)
        act, slope = silu_parts(value)
        sp1_ref[:, here] = slope
        hidden = act + emb0_col + embd_col * q_ref[0:1, here]
        hi, lo = split(hidden)
        hs_ref[0:chan, here] = hi
        hs_ref[chan : 2 * chan, here] = lo
        return carry

    q_ref[0:1, :] = flags_row
    lax.fori_loop(0, n_near // wide_cols, first, 0)

    def gather(k, carry):
        here = pl.ds(pl.multiple_of(k * atoms, atoms), atoms)
        wanted = gidx_ref[pl.ds(k, 1), 0:atoms]
        for r in range(n_near // LANES):
            ids = lax.broadcasted_iota(jnp.int32, (LANES, atoms), 0) + r * LANES
            oh_ref[r * LANES : (r + 1) * LANES, here] = jnp.where(ids == wanted, 1.0, 0.0).astype(bf16)
        both = dot(hs_ref[...], oh_ref[:, here])
        feat = both[:chan] + both[chan:]
        basis = split_rows(bt_ref[k, 0:bases, 0:atoms])
        weight = dot(r2_cols, jnp.concatenate([basis, basis], axis=0).astype(bf16))
        hj_ref[:, here] = feat
        w_ref[:, here] = weight
        car_ref[:, here] = feat * weight
        return carry

    lax.fori_loop(0, slots, gather, 0)

    pairs = chan // 16

    def moments(step, carry):
        t = step // pairs
        c = step % pairs
        cols = pl.ds(pl.multiple_of(t * LANES, LANES), LANES)
        base = pl.multiple_of(c * 16, 16)
        acc = [[None] * ORDERS, [None] * ORDERS]
        for k in range(slots):
            at = pl.ds(pl.multiple_of(k * atoms + t * LANES, LANES), LANES)
            got = car_ref[pl.ds(base, 16), at]
            for l in range(ORDERS):
                yb = yb_ref[l, k, :, cols] if l else None
                for h in range(2):
                    part = got[8 * h : 8 * h + 8]
                    term = part * yb if l else part
                    acc[h][l] = term if acc[h][l] is None else acc[h][l] + term
        inv = [[None] * 3, [None] * 3]
        for l in range(ORDERS):
            m2_ref[l, pl.ds(base, 16), cols] = jnp.concatenate([acc[0][l], acc[1][l]], axis=0)
            for h in range(2):
                sq = acc[h][l] * acc[h][l]
                g = GROUP[l]
                inv[h][g] = sq if inv[h][g] is None else inv[h][g] + sq
        for g in range(3):
            inv_ref[pl.ds(pl.multiple_of(g * chan + c * 16, 16), 16), cols] = jnp.concatenate(
                [inv[0][g], inv[1][g]], axis=0
            )
        return carry

    lax.fori_loop(0, tiles * pairs, moments, 0)

    for t in range(atoms // wide_cols):
        cols = slice(t * wide_cols, (t + 1) * wide_cols)
        value = dot(mix2_ref[...], inv_ref[:, cols], HIGH)
        _, slope = silu_parts(value)
        slope = slope * (2.0 * read2_col)
        for g in range(3):
            mixed = mix2_ref[:, g * chan : (g + 1) * chan].T
            dinv_ref[g * chan : (g + 1) * chan, cols] = dot(mixed, slope, HIGH)

    k_step = slots // 2

    def back_moments(step, carry):
        t = step // 2
        k0 = (step % 2) * k_step
        cols = pl.ds(pl.multiple_of(t * LANES, LANES), LANES)

        def over(c, acc):
            acc = list(acc)
            base = pl.multiple_of(c * 16, 16)
            dm = []
            scale = [dinv_ref[pl.ds(pl.multiple_of(g * chan + c * 16, 16), 16), cols] for g in range(3)]
            for l in range(ORDERS):
                dm.append(m2_ref[l, pl.ds(base, 16), cols] * scale[GROUP[l]])
            for kk in range(k_step):
                k = k0 + kk
                at = pl.ds(pl.multiple_of(k * atoms + t * LANES, LANES), LANES)
                got = car_ref[pl.ds(base, 16), at]
                out = [dm[0][:8], dm[0][8:]]
                for l in range(1, ORDERS):
                    yb = yb_ref[l, k, :, cols]
                    i = kk * (ORDERS - 1) + l - 1
                    for h in range(2):
                        part = dm[l][8 * h : 8 * h + 8]
                        out[h] = out[h] + part * yb
                        acc[i] = acc[i] + part * got[8 * h : 8 * h + 8]
                dcar = jnp.concatenate(out, axis=0)
                for ref, other in ((dhe_ref, w_ref), (dw_ref, hj_ref)):
                    hi, lo = split(dcar * other[pl.ds(base, 16), at])
                    ref[pl.ds(base, 16), at] = hi
                    ref[pl.ds(pl.multiple_of(chan + c * 16, 16), 16), at] = lo
            return tuple(acc)

        start = tuple(jnp.zeros((8, LANES), f32) for _ in range(k_step * (ORDERS - 1)))
        acc = lax.fori_loop(0, pairs, over, start)
        for kk in range(k_step):
            for l in range(1, ORDERS):
                p_ref[l, pl.ds(pl.multiple_of((k0 + kk) * 8, 8), 8), cols] = acc[kk * (ORDERS - 1) + l - 1]
        return carry

    lax.fori_loop(0, tiles * 2, back_moments, 0)

    for k in range(slots):
        here = slice(k * atoms, (k + 1) * atoms)
        both = dot(r2_rows, dw_ref[:, here])
        dbasis = both[:bases] + both[bases:]
        basis = bt_ref[k, 0:bases, 0:atoms]
        reach = 1.0 + lax.broadcasted_iota(jnp.int32, (bases, atoms), 0).astype(f32)
        p_ref[0, k * 8 : k * 8 + 8, :] = dbasis * basis * (reach - row(geo_ref[4, k : k + 1, 0:atoms], bases))

    def back_first(j, carry):
        start = pl.multiple_of(j * wide_cols, wide_cols)
        here = pl.ds(start, wide_cols)
        both = dot_nt(dhe_ref[...], oh_ref[here, :])
        dh = both[:chan] + both[chan:]
        mine = jnp.where(start < atoms, 1.0, 0.0)
        dtop = (dh + read1_col * mine) * sp1_ref[:, here] * 2.0
        scale = []
        for g in range(3):
            scale.append(dot(mix1_ref[:, g * chan : (g + 1) * chan].T, dtop, HIGH))
        for l in range(ORDERS):
            hi, lo = split(m1_ref[l, :, here] * scale[GROUP[l]])
            out = dot(rr_rows, jnp.concatenate([hi, lo], axis=0))
            da_ref[l, :, here] = out[: 2 * bases] + out[2 * bases :]
        return carry

    lax.fori_loop(0, n_near // wide_cols, back_first, 0)

    lane = lax.broadcasted_iota(jnp.int32, (slots, 16 * slots), 1)
    sub = lax.broadcasted_iota(jnp.int32, (slots, 16 * slots), 0)
    adder = jnp.where(((lane >> 3) & (slots - 1)) == sub, 1.0, 0.0).astype(bf16)
    for l in range(ORDERS):
        q_ref[8 * l : 8 * l + 8, 0:atoms] = dot(adder, split_rows(p_ref[l, :, :]).astype(bf16))

    def back_geometry(t, mine):
        here = pl.ds(pl.multiple_of(t * LANES, LANES), LANES)
        ux, uy, uz, back, soft, fj = [geo_ref[i, :, here] for i in range(6)]
        dy = [None] * ORDERS
        ds = None
        for n in range(bases):
            basis = bk_ref[n, :, here]
            db = None
            for l in range(ORDERS):
                g = row(da_ref[l, n : n + 1, here]) + fj * row(da_ref[l, bases + n : bases + n + 1, here])
                if l:
                    dy[l] = g * basis if dy[l] is None else dy[l] + g * basis
                    db = db + g * y_ref[l, :, here]
                else:
                    db = g
            db = db * basis * ((1.0 + n) - soft)
            ds = db if ds is None else ds + db
        if mine:
            ds = ds + q_ref[0:8, here]
            for l in range(1, ORDERS):
                dy[l] = dy[l] + q_ref[8 * l : 8 * l + 8, here]
        dux = SQRT3 * dy[1] + SQRT15 * (uy * dy[4] + uz * dy[7] + ux * dy[8]) - SQRT5 * ux * dy[6]
        duy = SQRT3 * dy[2] + SQRT15 * (ux * dy[4] + uz * dy[5] - uy * dy[8]) - SQRT5 * uy * dy[6]
        duz = SQRT3 * dy[3] + SQRT15 * (uy * dy[5] + ux * dy[7]) + 2.0 * SQRT5 * uz * dy[6]
        along = ds - (ux * dux + uy * duy + uz * duz) * back
        dr = [dux * back + along * ux, duy * back + along * uy, duz * back + along * uz]
        for i in range(3):
            geo_ref[i, :, here] = dr[i]
        return dr

    def mine_tile(t, carry):
        back_geometry(t, True)
        return carry

    def other_tile(t, carry):
        back_geometry(t, False)
        return carry

    lax.fori_loop(0, tiles, mine_tile, 0)
    lax.fori_loop(tiles, n_near // LANES, other_tile, 0)

    def place_tile(t, carry):
        here = pl.ds(pl.multiple_of(t * LANES, LANES), LANES)
        gidx = gidx_ref[:, here]
        chunk_no = gidx >> 7
        place = gidx & 127
        parts = []
        for i in range(3):
            value = geo_ref[i, :, here]
            hi = value.astype(bf16).astype(f32)
            parts.append((hi, value - hi))
        chunk_ids = lax.broadcasted_iota(jnp.int32, (top_rows, LANES), 0)
        place_ids = lax.broadcasted_iota(jnp.int32, (LANES, LANES), 0)
        for k in range(slots):
            at = pl.ds(pl.multiple_of(k * n_near + t * LANES, LANES), LANES)
            hit = chunk_ids == row(chunk_no[k : k + 1, :], top_rows)
            for i in range(3):
                both = [jnp.where(hit, row(part[k : k + 1, :], top_rows), 0.0) for part in parts[i]]
                val_ref[2 * i * top_rows : 2 * (i + 1) * top_rows, at] = jnp.concatenate(both, axis=0).astype(bf16)
            ohlo_ref[:, at] = jnp.where(place_ids == row(place[k : k + 1, :], LANES), 1.0, 0.0).astype(bf16)
        return carry

    lax.fori_loop(0, n_near // LANES, place_tile, 0)
    landed = dot_nt(val_ref[...], ohlo_ref[...])
    for i in range(3):
        total = (
            landed[2 * i * top_rows : (2 * i + 1) * top_rows] + landed[(2 * i + 1) * top_rows : (2 * i + 2) * top_rows]
        )
        for g in range(n_wide):
            for t in range(tiles):
                line = total[g * tiles + t : g * tiles + t + 1, :]
                if g < len(near):
                    here = slice(g * atoms + t * LANES, g * atoms + (t + 1) * LANES)
                    line = line - jnp.sum(geo_ref[i, :, here], axis=0, keepdims=True)
                grad_ref[g, i : i + 1, t * LANES : (t + 1) * LANES] = line


def ring_plan(domains, atoms):
    near = list(dict.fromkeys(o % domains for o in (0, 1, -1)))
    wide = list(dict.fromkeys(near + [o % domains for o in (2, -2)]))
    before = tuple(wide.index((o - 1) % domains) for o in near)
    after = tuple(wide.index((o + 1) % domains) for o in near)
    return atoms, tuple(near), tuple(wide), before, after


def forces(plan, blocks, embedding, radial_one, radial_two, mix_one, mix_two, read_one, read_two):
    atoms, near, wide, _, _ = plan
    chan = embedding.shape[1]
    bases = radial_one.shape[0]
    slots = blocks[0].shape[0] - HEAD
    n_near = len(near) * atoms
    edges = slots * atoms
    top_rows = -(-len(wide) * atoms // LANES // 8) * 8
    vmem = pl.BlockSpec(memory_space=pltpu.VMEM)
    return pl.pallas_call(
        functools.partial(force_kernel, plan),
        out_shape=jax.ShapeDtypeStruct((len(wide), 3, atoms), f32),
        in_specs=[vmem] * (len(wide) + 7),
        out_specs=vmem,
        scratch_shapes=[
            pltpu.VMEM((6, slots, n_near), f32),
            pltpu.VMEM((ORDERS, slots, n_near), f32),
            pltpu.VMEM((ORDERS, slots, 8, atoms), f32),
            pltpu.VMEM((bases, slots, n_near), f32),
            pltpu.VMEM((slots, 2 * bases, n_near), f32),
            pltpu.VMEM((slots, n_near), jnp.int32),
            pltpu.VMEM((ORDERS, 8 * bases, n_near), bf16),
            pltpu.VMEM((ORDERS, chan, n_near), f32),
            pltpu.VMEM((chan, n_near), f32),
            pltpu.VMEM((2 * chan, n_near), bf16),
            pltpu.VMEM((n_near, edges), bf16),
            pltpu.VMEM((chan, edges), f32),
            pltpu.VMEM((chan, edges), f32),
            pltpu.VMEM((chan, edges), f32),
            pltpu.VMEM((ORDERS, chan, atoms), f32),
            pltpu.VMEM((3 * chan, atoms), f32),
            pltpu.VMEM((3 * chan, atoms), f32),
            pltpu.VMEM((ORDERS, 8 * slots, atoms), f32),
            pltpu.VMEM((2 * chan, edges), bf16),
            pltpu.VMEM((2 * chan, edges), bf16),
            pltpu.VMEM((ORDERS, 2 * bases, n_near), f32),
            pltpu.VMEM((8 * ORDERS, n_near), f32),
            pltpu.VMEM((6 * top_rows, slots * n_near), bf16),
            pltpu.VMEM((LANES, slots * n_near), bf16),
        ],
        compiler_params=pltpu.CompilerParams(vmem_limit_bytes=VMEM_BYTES),
        name="forces",
    )(*blocks, embedding, radial_one, radial_two, mix_one, mix_two, read_one[None], read_two[None])


def mode_tables(bead_total):
    bead = np.arange(bead_total, dtype=np.float64)[:, None]
    mode = np.arange(bead_total, dtype=np.float64)[None, :]
    phase = 2.0 * np.pi * bead * mode / bead_total
    half_total = bead_total // 2
    table = math.sqrt(2.0 / bead_total) * np.where(mode < half_total, np.cos(phase), np.sin(phase))
    table = np.where(mode == half_total, np.cos(np.pi * bead) / math.sqrt(bead_total), table)
    table = np.where(mode == 0, 1.0 / math.sqrt(bead_total), table)
    angles = bead_total * np.sin(np.pi * mode[0] / bead_total)
    safe = np.where(mode[0] == 0, 1.0, angles)
    reach = np.where(mode[0] == 0, STEP, STEP * np.sin(angles) / safe)
    stiff = angles * np.sin(angles) / STEP
    turns = [(table * factor[None, :]) @ table.T for factor in (np.cos(angles), reach, stiff)]
    return np.stack(turns, axis=1).astype(np.float32)


def step_kernel(table_ref, gathered_ref, species_ref, q_ref, p_ref):
    bead_total = gathered_ref.shape[0]
    sums = [None] * 4
    for b in range(bead_total):
        coord = gathered_ref[b, 0:3, :]
        moment = gathered_ref[b, 3:6, :]
        for i, (weight, value) in enumerate(((0, coord), (0, moment), (1, moment), (2, coord))):
            term = table_ref[weight, b] * value
            sums[i] = term if sums[i] is None else sums[i] + term
    mass = HEAVY - (HEAVY - 1.0) * species_ref[...].astype(f32)
    q_ref[0] = sums[0] + sums[2] / mass
    p_ref[0] = sums[1] - mass * sums[3]


def shards(
    positions, momenta, species, neighbours, send_list, embedding, radial_one, radial_two, mix_one, mix_two,
    read_one, read_two,
):
    atoms = neighbours.shape[1]
    domains = lax.axis_size("space")
    plan = ring_plan(domains, atoms)
    wide = plan[2]
    block = jnp.concatenate(
        [
            positions[0],
            species.astype(f32)[None],
            send_list.astype(f32)[None],
            jnp.zeros((HEAD - 5, atoms), f32),
            neighbours.astype(f32),
        ],
        axis=0,
    )
    blocks = [block]
    for offset in wide[1:]:
        blocks.append(lax.ppermute(block, "space", [(i, (i - offset) % domains) for i in range(domains)]))
    grads = forces(plan, blocks, embedding, radial_one, radial_two, mix_one, mix_two, read_one, read_two)
    grad = grads[0]
    for g, offset in enumerate(wide):
        if g:
            grad = grad + lax.ppermute(grads[g], "space", [(i, (i + offset) % domains) for i in range(domains)])
    kicked = momenta[0] - HALF_STEP * grad
    bead_total = lax.axis_size("bead")
    tables = jnp.asarray(mode_tables(bead_total))
    my_table = lax.dynamic_index_in_dim(tables, lax.axis_index("bead"), axis=0, keepdims=False)
    mine = jnp.concatenate([positions[0], kicked], axis=0)
    gathered = lax.all_gather(mine[None], "bead", axis=0, tiled=True)
    vmem = pl.BlockSpec(memory_space=pltpu.VMEM)
    return pl.pallas_call(
        step_kernel,
        out_shape=(jax.ShapeDtypeStruct((1, 3, atoms), f32),) * 2,
        in_specs=[pl.BlockSpec(memory_space=pltpu.SMEM), vmem, vmem],
        out_specs=(vmem, vmem),
        name="step",
    )(my_table, gathered, species[None])


def solution(mesh):
    placed = (
        P("bead", None, "space"),
        P("bead", None, "space"),
        P("space"),
        P(None, "space"),
        P("space"),
        P(),
        P(),
        P(),
        P(),
        P(),
        P(),
        P(),
    )
    return jax.shard_map(
        shards,
        mesh=mesh,
        in_specs=placed,
        out_specs=(P("bead", None, "space"), P("bead", None, "space")),
        check_vma=False,
    )
```

```python
import functools
import math

import jax
import jax.numpy as jnp
import numpy as np
from jax import lax
from jax.experimental import pallas as pl
from jax.experimental.pallas import tpu as pltpu
from jax.sharding import PartitionSpec as P

STEP = 2.0
HALF_STEP = 1.0
HEAVY = 16.0
SQRT3 = math.sqrt(3.0)
SQRT5 = math.sqrt(5.0)
SQRT15 = math.sqrt(15.0)
LANES = 128
ORDERS = 9
GROUP = (0, 1, 1, 1, 2, 2, 2, 2, 2)
HEAD = 8
MIB = 1024 * 1024
f32 = jnp.float32
bf16 = jnp.bfloat16
HIGH = lax.Precision.HIGH


def split(x):
    hi = x.astype(bf16)
    return hi, (x - hi.astype(f32)).astype(bf16)


def split_rows(x):
    hi = x.astype(bf16).astype(f32)
    return jnp.concatenate([hi, x - hi], axis=0)


def dot(a, b, precision=None):
    return jnp.dot(a, b, preferred_element_type=f32, precision=precision)


def dot_nt(a, b):
    return lax.dot_general(a, b, (((1,), (1,)), ((), ())), preferred_element_type=f32)


def row(x, rows=8):
    return jnp.broadcast_to(x, (rows, x.shape[1]))


def lookup(chunks, wanted, position):
    out = None
    for number, chunk in chunks:
        got = jnp.take_along_axis(row(chunk), position, axis=1, mode="promise_in_bounds")
        out = got if out is None else jnp.where(wanted == number, got, out)
    return out


def harmonics(ux, uy, uz):
    return [
        None,
        SQRT3 * ux,
        SQRT3 * uy,
        SQRT3 * uz,
        SQRT15 * ux * uy,
        SQRT15 * uy * uz,
        0.5 * SQRT5 * (2.0 * uz * uz - ux * ux - uy * uy),
        SQRT15 * ux * uz,
        0.5 * SQRT15 * (ux * ux - uy * uy),
    ]


def silu_parts(v):
    gate = 1.0 / (1.0 + jnp.exp(-v))
    return v * gate, gate * (1.0 + v * (1.0 - gate))


def force_kernel(plan, *refs):
    atoms, near, wide, before, after = plan
    n_wide = len(wide)
    blocks = refs[:n_wide]
    moment_ref, emb_ref, rad1_ref, rad2_ref, mix1_ref, mix2_ref, read1_ref, read2_ref = refs[n_wide : n_wide + 8]
    push_refs = refs[n_wide + 8 : 2 * n_wide + 8]
    (
        geo_ref, y_ref, yb_ref, bk_ref, bt_ref, gidx_ref, as_ref, m1_ref, sp1_ref, hs_ref, oh_ref,
        hj_ref, w_ref, car_ref, m2_ref, inv_ref, dinv_ref, p_ref, dhe_ref, dw_ref, da_ref, q_ref,
        val_ref, ohlo_ref,
    ) = refs[2 * n_wide + 8 :]
    chan = emb_ref.shape[1]
    bases = rad1_ref.shape[0]
    slots = gidx_ref.shape[0]
    n_near = len(near) * atoms
    tiles = atoms // LANES
    half = atoms // 2
    half_tiles = half // LANES
    edges = slots * atoms
    top_rows = val_ref.shape[0] // 6

    emb0 = emb_ref[0:1, :]
    emb_d = emb_ref[1:2, :] - emb0
    rr = jnp.concatenate([rad1_ref[...] * emb0, rad1_ref[...] * emb_d], axis=0) * (1.0 / slots)
    rr_hi = rr.astype(bf16).astype(f32)
    rr_lo = rr - rr_hi
    r2 = rad2_ref[...] * (1.0 / slots)
    r2_hi = r2.astype(bf16).astype(f32)
    r2_lo = r2 - r2_hi
    zeros = jnp.zeros((8, chan), f32)
    turned1 = jnp.concatenate([rr_hi, rr_hi, rr_lo, rr_lo] + [zeros] * 8, axis=0).T
    sides = jnp.concatenate([emb0, emb_d, read1_ref[...], read2_ref[...], zeros[:4]], axis=0)
    turned2 = jnp.concatenate([r2_hi, r2_hi, r2_lo, r2_lo, sides] + [zeros] * 11, axis=0).T
    rr_cols = turned1[:, : 8 * bases].astype(bf16)
    r2_cols = turned2[:, : 4 * bases].astype(bf16)
    emb0_col = turned2[:, 4 * bases : 4 * bases + 1]
    embd_col = turned2[:, 4 * bases + 1 : 4 * bases + 2]
    read1_col = turned2[:, 4 * bases + 2 : 4 * bases + 3]
    read2_col = turned2[:, 4 * bases + 3 : 4 * bases + 4]
    rr_rows = jnp.concatenate(
        [jnp.concatenate([rr_hi, rr_hi], axis=1), jnp.concatenate([rr_lo, jnp.zeros_like(rr_lo)], axis=1)], axis=0
    ).astype(bf16)
    r2_rows = jnp.concatenate(
        [jnp.concatenate([r2_hi, r2_hi], axis=1), jnp.concatenate([r2_lo, jnp.zeros_like(r2_lo)], axis=1)], axis=0
    ).astype(bf16)
    order_col = lax.broadcasted_iota(jnp.int32, (bases, LANES), 0).astype(f32)

    tables = []
    for quantity in range(4):
        chunks = []
        for g in range(n_wide):
            for t in range(tiles):
                chunks.append((g * tiles + t, blocks[g][quantity : quantity + 1, t * LANES : (t + 1) * LANES]))
        tables.append(chunks)
    for q in range(len(near)):
        ghosts = []
        for t in range(half_tiles):
            ghosts.append(
                (t, blocks[before[q]][4:5, half + t * LANES : half + (t + 1) * LANES] + float(before[q] * atoms))
            )
        for t in range(half_tiles):
            ghosts.append(
                (
                    half_tiles + tiles + t,
                    blocks[after[q]][4:5, t * LANES : (t + 1) * LANES] + float(after[q] * atoms),
                )
            )
        for t in range(tiles):
            cols = slice(t * LANES, (t + 1) * LANES)
            here = slice(q * atoms + t * LANES, q * atoms + (t + 1) * LANES)
            slot = blocks[q][HEAD : HEAD + slots, cols].astype(jnp.int32)
            chunk_no = slot >> 7
            far = lookup(ghosts, chunk_no, slot & 127).astype(jnp.int32)
            own = (slot >= half) & (slot < half + atoms)
            gidx = jnp.where(own, slot + (q * atoms - half), far)
            gidx_ref[:, here] = gidx
            chunk_no = gidx >> 7
            place = gidx & 127
            xj, yj, zj, fj = [lookup(tables[i], chunk_no, place) for i in range(4)]
            rx = xj - row(blocks[q][0:1, cols])
            ry = yj - row(blocks[q][1:2, cols])
            rz = zj - row(blocks[q][2:3, cols])
            soft = jnp.sqrt(rx * rx + ry * ry + rz * rz + 1.0)
            back = 1.0 / soft
            ux, uy, uz = rx * back, ry * back, rz * back
            for i, value in enumerate((ux, uy, uz, back, soft, fj)):
                geo_ref[i, :, here] = value
            sphere = harmonics(ux, uy, uz)
            for l in range(1, ORDERS):
                y_ref[l, :, here] = sphere[l]
                if q == 0:
                    for k in range(slots):
                        yb_ref[l, k, :, cols] = row(sphere[l][k : k + 1, :])
            for n in range(bases):
                bk_ref[n, :, here] = jnp.exp(-0.5 * (soft - (1.0 + n)) ** 2)
            for k in range(slots):
                basis = jnp.exp(-0.5 * (row(soft[k : k + 1, :], bases) - (1.0 + order_col)) ** 2)
                bt_ref[k, 0:bases, here] = basis
                bt_ref[k, bases : 2 * bases, here] = basis * row(fj[k : k + 1, :], bases)

    def sums(t, carry):
        here = pl.ds(pl.multiple_of(t * LANES, LANES), LANES)
        low = [None] * ORDERS
        for k in range(slots):
            basis = bt_ref[k, :, here]
            for l in range(ORDERS):
                term = basis if l == 0 else basis * row(y_ref[l, k : k + 1, here], 2 * bases)
                low[l] = term if low[l] is None else low[l] + term
        for l in range(ORDERS):
            both = split_rows(low[l]).astype(bf16)
            as_ref[l, 0 : 4 * bases, here] = both
            as_ref[l, 4 * bases : 8 * bases, here] = both
        return carry

    lax.fori_loop(0, n_near // LANES, sums, 0)

    flags_row = jnp.concatenate([blocks[q][3:4, :] for q in range(len(near))], axis=1)
    wide_cols = 2 * LANES

    def first(j, carry):
        here = pl.ds(pl.multiple_of(j * wide_cols, wide_cols), wide_cols)
        inv = [None, None, None]
        for l in range(ORDERS):
            m = dot(rr_cols, as_ref[l, :, here])
            m1_ref[l, :, here] = m
            inv[GROUP[l]] = m * m if inv[GROUP[l]] is None else inv[GROUP[l]] + m * m
        value = dot(mix1_ref[...], jnp.concatenate(inv, axis=0), HIGH)
        act, slope = silu_parts(value)
        sp1_ref[:, here] = slope
        hidden = act + emb0_col + embd_col * q_ref[0:1, here]
        hi, lo = split(hidden)
        hs_ref[0:chan, here] = hi
        hs_ref[chan : 2 * chan, here] = lo
        return carry

    q_ref[0:1, :] = flags_row
    lax.fori_loop(0, n_near // wide_cols, first, 0)

    def gather(k, carry):
        here = pl.ds(pl.multiple_of(k * atoms, atoms), atoms)
        wanted = gidx_ref[pl.ds(k, 1), 0:atoms]
        for r in range(n_near // LANES):
            ids = lax.broadcasted_iota(jnp.int32, (LANES, atoms), 0) + r * LANES
            oh_ref[r * LANES : (r + 1) * LANES, here] = jnp.where(ids == wanted, 1.0, 0.0).astype(bf16)
        both = dot(hs_ref[...], oh_ref[:, here])
        feat = both[:chan] + both[chan:]
        basis = split_rows(bt_ref[k, 0:bases, 0:atoms])
        weight = dot(r2_cols, jnp.concatenate([basis, basis], axis=0).astype(bf16))
        hj_ref[:, here] = feat
        w_ref[:, here] = weight
        car_ref[:, here] = feat * weight
        return carry

    lax.fori_loop(0, slots, gather, 0)

    pairs = chan // 16

    def moments(step, carry):
        t = step // pairs
        c = step % pairs
        cols = pl.ds(pl.multiple_of(t * LANES, LANES), LANES)
        base = pl.multiple_of(c * 16, 16)
        acc = [[None] * ORDERS, [None] * ORDERS]
        for k in range(slots):
            at = pl.ds(pl.multiple_of(k * atoms + t * LANES, LANES), LANES)
            got = car_ref[pl.ds(base, 16), at]
            for l in range(ORDERS):
                yb = yb_ref[l, k, :, cols] if l else None
                for h in range(2):
                    part = got[8 * h : 8 * h + 8]
                    term = part * yb if l else part
                    acc[h][l] = term if acc[h][l] is None else acc[h][l] + term
        inv = [[None] * 3, [None] * 3]
        for l in range(ORDERS):
            m2_ref[l, pl.ds(base, 16), cols] = jnp.concatenate([acc[0][l], acc[1][l]], axis=0)
            for h in range(2):
                sq = acc[h][l] * acc[h][l]
                g = GROUP[l]
                inv[h][g] = sq if inv[h][g] is None else inv[h][g] + sq
        for g in range(3):
            inv_ref[pl.ds(pl.multiple_of(g * chan + c * 16, 16), 16), cols] = jnp.concatenate(
                [inv[0][g], inv[1][g]], axis=0
            )
        return carry

    lax.fori_loop(0, tiles * pairs, moments, 0)

    for t in range(atoms // wide_cols):
        cols = slice(t * wide_cols, (t + 1) * wide_cols)
        value = dot(mix2_ref[...], inv_ref[:, cols], HIGH)
        _, slope = silu_parts(value)
        slope = slope * (2.0 * read2_col)
        for g in range(3):
            mixed = mix2_ref[:, g * chan : (g + 1) * chan].T
            dinv_ref[g * chan : (g + 1) * chan, cols] = dot(mixed, slope, HIGH)

    k_step = slots // 2

    def back_moments(step, carry):
        t = step // 2
        k0 = (step % 2) * k_step
        cols = pl.ds(pl.multiple_of(t * LANES, LANES), LANES)

        def over(c, acc):
            acc = list(acc)
            base = pl.multiple_of(c * 16, 16)
            dm = []
            scale = [dinv_ref[pl.ds(pl.multiple_of(g * chan + c * 16, 16), 16), cols] for g in range(3)]
            for l in range(ORDERS):
                dm.append(m2_ref[l, pl.ds(base, 16), cols] * scale[GROUP[l]])
            for kk in range(k_step):
                k = k0 + kk
                at = pl.ds(pl.multiple_of(k * atoms + t * LANES, LANES), LANES)
                got = car_ref[pl.ds(base, 16), at]
                out = [dm[0][:8], dm[0][8:]]
                for l in range(1, ORDERS):
                    yb = yb_ref[l, k, :, cols]
                    i = kk * (ORDERS - 1) + l - 1
                    for h in range(2):
                        part = dm[l][8 * h : 8 * h + 8]
                        out[h] = out[h] + part * yb
                        acc[i] = acc[i] + part * got[8 * h : 8 * h + 8]
                dcar = jnp.concatenate(out, axis=0)
                for ref, other in ((dhe_ref, w_ref), (dw_ref, hj_ref)):
                    hi, lo = split(dcar * other[pl.ds(base, 16), at])
                    ref[pl.ds(base, 16), at] = hi
                    ref[pl.ds(pl.multiple_of(chan + c * 16, 16), 16), at] = lo
            return tuple(acc)

        start = tuple(jnp.zeros((8, LANES), f32) for _ in range(k_step * (ORDERS - 1)))
        acc = lax.fori_loop(0, pairs, over, start)
        for kk in range(k_step):
            for l in range(1, ORDERS):
                p_ref[l, pl.ds(pl.multiple_of((k0 + kk) * 8, 8), 8), cols] = acc[kk * (ORDERS - 1) + l - 1]
        return carry

    lax.fori_loop(0, tiles * 2, back_moments, 0)

    for k in range(slots):
        here = slice(k * atoms, (k + 1) * atoms)
        both = dot(r2_rows, dw_ref[:, here])
        dbasis = both[:bases] + both[bases:]
        basis = bt_ref[k, 0:bases, 0:atoms]
        reach = 1.0 + lax.broadcasted_iota(jnp.int32, (bases, atoms), 0).astype(f32)
        p_ref[0, k * 8 : k * 8 + 8, :] = dbasis * basis * (reach - row(geo_ref[4, k : k + 1, 0:atoms], bases))

    def back_first(j, carry):
        start = pl.multiple_of(j * wide_cols, wide_cols)
        here = pl.ds(start, wide_cols)
        both = dot_nt(dhe_ref[...], oh_ref[here, :])
        dh = both[:chan] + both[chan:]
        mine = jnp.where(start < atoms, 1.0, 0.0)
        dtop = (dh + read1_col * mine) * sp1_ref[:, here] * 2.0
        scale = []
        for g in range(3):
            scale.append(dot(mix1_ref[:, g * chan : (g + 1) * chan].T, dtop, HIGH))
        for l in range(ORDERS):
            hi, lo = split(m1_ref[l, :, here] * scale[GROUP[l]])
            out = dot(rr_rows, jnp.concatenate([hi, lo], axis=0))
            da_ref[l, :, here] = out[: 2 * bases] + out[2 * bases :]
        return carry

    lax.fori_loop(0, n_near // wide_cols, back_first, 0)

    lane = lax.broadcasted_iota(jnp.int32, (slots, 16 * slots), 1)
    sub = lax.broadcasted_iota(jnp.int32, (slots, 16 * slots), 0)
    adder = jnp.where(((lane >> 3) & (slots - 1)) == sub, 1.0, 0.0).astype(bf16)
    for l in range(ORDERS):
        q_ref[8 * l : 8 * l + 8, 0:atoms] = dot(adder, split_rows(p_ref[l, :, :]).astype(bf16))

    def back_geometry(t, mine):
        here = pl.ds(pl.multiple_of(t * LANES, LANES), LANES)
        ux, uy, uz, back, soft, fj = [geo_ref[i, :, here] for i in range(6)]
        dy = [None] * ORDERS
        ds = None
        for n in range(bases):
            basis = bk_ref[n, :, here]
            db = None
            for l in range(ORDERS):
                g = row(da_ref[l, n : n + 1, here]) + fj * row(da_ref[l, bases + n : bases + n + 1, here])
                if l:
                    dy[l] = g * basis if dy[l] is None else dy[l] + g * basis
                    db = db + g * y_ref[l, :, here]
                else:
                    db = g
            db = db * basis * ((1.0 + n) - soft)
            ds = db if ds is None else ds + db
        if mine:
            ds = ds + q_ref[0:8, here]
            for l in range(1, ORDERS):
                dy[l] = dy[l] + q_ref[8 * l : 8 * l + 8, here]
        dux = SQRT3 * dy[1] + SQRT15 * (uy * dy[4] + uz * dy[7] + ux * dy[8]) - SQRT5 * ux * dy[6]
        duy = SQRT3 * dy[2] + SQRT15 * (ux * dy[4] + uz * dy[5] - uy * dy[8]) - SQRT5 * uy * dy[6]
        duz = SQRT3 * dy[3] + SQRT15 * (uy * dy[5] + ux * dy[7]) + 2.0 * SQRT5 * uz * dy[6]
        along = ds - (ux * dux + uy * duy + uz * duz) * back
        dr = [dux * back + along * ux, duy * back + along * uy, duz * back + along * uz]
        for i in range(3):
            geo_ref[i, :, here] = dr[i]
        return dr

    def mine_tile(t, carry):
        back_geometry(t, True)
        return carry

    def other_tile(t, carry):
        back_geometry(t, False)
        return carry

    lax.fori_loop(0, tiles, mine_tile, 0)
    lax.fori_loop(tiles, n_near // LANES, other_tile, 0)

    def place_tile(t, carry):
        here = pl.ds(pl.multiple_of(t * LANES, LANES), LANES)
        gidx = gidx_ref[:, here]
        chunk_no = gidx >> 7
        place = gidx & 127
        parts = []
        for i in range(3):
            value = geo_ref[i, :, here]
            hi = value.astype(bf16).astype(f32)
            parts.append((hi, value - hi))
        chunk_ids = lax.broadcasted_iota(jnp.int32, (top_rows, LANES), 0)
        place_ids = lax.broadcasted_iota(jnp.int32, (LANES, LANES), 0)
        for k in range(slots):
            at = pl.ds(pl.multiple_of(k * n_near + t * LANES, LANES), LANES)
            hit = chunk_ids == row(chunk_no[k : k + 1, :], top_rows)
            for i in range(3):
                both = [jnp.where(hit, row(part[k : k + 1, :], top_rows), 0.0) for part in parts[i]]
                val_ref[2 * i * top_rows : 2 * (i + 1) * top_rows, at] = jnp.concatenate(both, axis=0).astype(bf16)
            ohlo_ref[:, at] = jnp.where(place_ids == row(place[k : k + 1, :], LANES), 1.0, 0.0).astype(bf16)
        return carry

    lax.fori_loop(0, n_near // LANES, place_tile, 0)
    landed = dot_nt(val_ref[...], ohlo_ref[...])
    for i in range(3):
        total = (
            landed[2 * i * top_rows : (2 * i + 1) * top_rows] + landed[(2 * i + 1) * top_rows : (2 * i + 2) * top_rows]
        )
        for g in range(n_wide):
            for t in range(tiles):
                line = total[g * tiles + t : g * tiles + t + 1, :]
                if g < len(near):
                    here = slice(g * atoms + t * LANES, g * atoms + (t + 1) * LANES)
                    line = line - jnp.sum(geo_ref[i, :, here], axis=0, keepdims=True)
                cols = slice(t * LANES, (t + 1) * LANES)
                start = moment_ref[i, :, cols] if g == 0 else 0.0
                push_refs[g][i : i + 1, cols] = start - HALF_STEP * line


def ring_plan(domains, atoms):
    near = list(dict.fromkeys(o % domains for o in (0, 1, -1)))
    wide = list(dict.fromkeys(near + [o % domains for o in (2, -2)]))
    before = tuple(wide.index((o - 1) % domains) for o in near)
    after = tuple(wide.index((o + 1) % domains) for o in near)
    return atoms, tuple(near), tuple(wide), before, after


def pushes(plan, blocks, momenta, embedding, radial_one, radial_two, mix_one, mix_two, read_one, read_two):
    atoms, near, wide, _, _ = plan
    chan = embedding.shape[1]
    bases = radial_one.shape[0]
    slots = blocks[0].shape[0] - HEAD
    n_near = len(near) * atoms
    edges = slots * atoms
    top_rows = -(-len(wide) * atoms // LANES // 8) * 8
    vmem = pl.BlockSpec(memory_space=pltpu.VMEM)
    return pl.pallas_call(
        functools.partial(force_kernel, plan),
        out_shape=(jax.ShapeDtypeStruct((3, atoms), f32),) * len(wide),
        in_specs=[vmem] * (len(wide) + 8),
        out_specs=(vmem,) * len(wide),
        scratch_shapes=[
            pltpu.VMEM((6, slots, n_near), f32),
            pltpu.VMEM((ORDERS, slots, n_near), f32),
            pltpu.VMEM((ORDERS, slots, 8, atoms), f32),
            pltpu.VMEM((bases, slots, n_near), f32),
            pltpu.VMEM((slots, 2 * bases, n_near), f32),
            pltpu.VMEM((slots, n_near), jnp.int32),
            pltpu.VMEM((ORDERS, 8 * bases, n_near), bf16),
            pltpu.VMEM((ORDERS, chan, n_near), f32),
            pltpu.VMEM((chan, n_near), f32),
            pltpu.VMEM((2 * chan, n_near), bf16),
            pltpu.VMEM((n_near, edges), bf16),
            pltpu.VMEM((chan, edges), f32),
            pltpu.VMEM((chan, edges), f32),
            pltpu.VMEM((chan, edges), f32),
            pltpu.VMEM((ORDERS, chan, atoms), f32),
            pltpu.VMEM((3 * chan, atoms), f32),
            pltpu.VMEM((3 * chan, atoms), f32),
            pltpu.VMEM((ORDERS, 8 * slots, atoms), f32),
            pltpu.VMEM((2 * chan, edges), bf16),
            pltpu.VMEM((2 * chan, edges), bf16),
            pltpu.VMEM((ORDERS, 2 * bases, n_near), f32),
            pltpu.VMEM((8 * ORDERS, n_near), f32),
            pltpu.VMEM((6 * top_rows, slots * n_near), bf16),
            pltpu.VMEM((LANES, slots * n_near), bf16),
        ],
        compiler_params=pltpu.CompilerParams(vmem_limit_bytes=(26 + 10 * len(near)) * MIB),
        name="forces",
    )(*blocks, momenta, embedding, radial_one, radial_two, mix_one, mix_two, read_one[None], read_two[None])


def mode_tables(bead_total):
    bead = np.arange(bead_total, dtype=np.float64)[:, None]
    mode = np.arange(bead_total, dtype=np.float64)[None, :]
    phase = 2.0 * np.pi * bead * mode / bead_total
    half_total = bead_total // 2
    table = math.sqrt(2.0 / bead_total) * np.where(mode < half_total, np.cos(phase), np.sin(phase))
    table = np.where(mode == half_total, np.cos(np.pi * bead) / math.sqrt(bead_total), table)
    table = np.where(mode == 0, 1.0 / math.sqrt(bead_total), table)
    angles = bead_total * np.sin(np.pi * mode[0] / bead_total)
    safe = np.where(mode[0] == 0, 1.0, angles)
    reach = np.where(mode[0] == 0, STEP, STEP * np.sin(angles) / safe)
    stiff = angles * np.sin(angles) / STEP
    turns = [(table * factor[None, :]) @ table.T for factor in (np.cos(angles), reach, stiff)]
    return np.stack(turns, axis=1).astype(np.float32)


def kick_kernel(*refs):
    total = refs[0][...]
    for ref in refs[1:-1]:
        total = total + ref[...]
    for b in range(refs[-1].shape[0]):
        refs[-1][b] = total


def step_kernel(bead_ref, table_ref, coord_ref, moment_ref, species_ref, q_ref, p_ref):
    bead_total = coord_ref.shape[0]
    first = bead_ref[0] * (3 * bead_total)
    sums = [None] * 4
    for b in range(bead_total):
        coord = coord_ref[b]
        moment = moment_ref[b]
        for i, (weight, value) in enumerate(((0, coord), (0, moment), (1, moment), (2, coord))):
            term = table_ref[first + weight * bead_total + b] * value
            sums[i] = term if sums[i] is None else sums[i] + term
    mass = HEAVY - (HEAVY - 1.0) * species_ref[...].astype(f32)
    new_q = sums[0] + sums[2] / mass
    new_p = sums[1] - mass * sums[3]
    for i in range(3):
        q_ref[i] = new_q[i : i + 1]
        p_ref[i] = new_p[i : i + 1]


def shards(
    positions, momenta, species, neighbours, send_list, embedding, radial_one, radial_two, mix_one, mix_two,
    read_one, read_two,
):
    atoms = neighbours.shape[1]
    domains = lax.axis_size("space")
    bead_total = lax.axis_size("bead")
    plan = ring_plan(domains, atoms)
    wide = plan[2]
    vmem = pl.BlockSpec(memory_space=pltpu.VMEM)
    smem = pl.BlockSpec(memory_space=pltpu.SMEM)
    block = jnp.concatenate(
        [
            positions[0],
            species.astype(f32)[None],
            send_list.astype(f32)[None],
            jnp.zeros((HEAD - 5, atoms), f32),
            neighbours.astype(f32),
        ],
        axis=0,
    )
    blocks = [block]
    for offset in wide[1:]:
        blocks.append(lax.ppermute(block, "space", [(i, (i - offset) % domains) for i in range(domains)]))
    spread = jnp.broadcast_to(positions, (bead_total, 3, atoms))
    coords = lax.all_to_all(spread, "bead", 0, 0, tiled=True)
    moment_rows = jnp.transpose(momenta, (1, 0, 2))
    pushed = pushes(
        plan, blocks, moment_rows, embedding, radial_one, radial_two, mix_one, mix_two, read_one, read_two
    )
    parts = [pushed[0]]
    for piece, offset in zip(pushed[1:], wide[1:]):
        parts.append(lax.ppermute(piece, "space", [(i, (i + offset) % domains) for i in range(domains)]))
    kicked = pl.pallas_call(
        kick_kernel,
        out_shape=jax.ShapeDtypeStruct((bead_total, 3, atoms), f32),
        in_specs=[vmem] * len(parts),
        out_specs=vmem,
        name="kick",
    )(*parts)
    moments = lax.all_to_all(kicked, "bead", 0, 0, tiled=True)
    bead = lax.axis_index("bead").astype(jnp.int32).reshape(1)
    new_q, new_p = pl.pallas_call(
        step_kernel,
        out_shape=(jax.ShapeDtypeStruct((3, 1, atoms), f32),) * 2,
        in_specs=[smem, smem, vmem, vmem, vmem],
        out_specs=(vmem, vmem),
        name="step",
    )(bead, jnp.asarray(mode_tables(bead_total).reshape(-1)), coords, moments, species[None])
    return (jnp.transpose(new_q, (1, 0, 2)), jnp.transpose(new_p, (1, 0, 2)))


def solution(mesh):
    placed = (
        P("bead", None, "space"),
        P("bead", None, "space"),
        P("space"),
        P(None, "space"),
        P("space"),
        P(),
        P(),
        P(),
        P(),
        P(),
        P(),
        P(),
    )
    return jax.shard_map(
        shards,
        mesh=mesh,
        in_specs=placed,
        out_specs=(P("bead", None, "space"), P("bead", None, "space")),
        check_vma=False,
    )
```

```python
import functools
import math

import jax
import jax.numpy as jnp
import numpy as np
from jax import lax
from jax.experimental import pallas as pl
from jax.experimental.pallas import tpu as pltpu
from jax.sharding import PartitionSpec as P

STEP = 2.0
HALF_STEP = 1.0
HEAVY = 16.0
SQRT3 = math.sqrt(3.0)
SQRT5 = math.sqrt(5.0)
SQRT15 = math.sqrt(15.0)
LANES = 128
ORDERS = 9
GROUP = (0, 1, 1, 1, 2, 2, 2, 2, 2)
HEAD = 8
MIB = 1024 * 1024
f32 = jnp.float32
bf16 = jnp.bfloat16
HIGH = lax.Precision.HIGH


def split(x):
    hi = x.astype(bf16)
    return hi, (x - hi.astype(f32)).astype(bf16)


def split_rows(x):
    hi = x.astype(bf16).astype(f32)
    return jnp.concatenate([hi, x - hi], axis=0)


def dot(a, b, precision=None):
    return jnp.dot(a, b, preferred_element_type=f32, precision=precision)


def dot_nt(a, b):
    return lax.dot_general(a, b, (((1,), (1,)), ((), ())), preferred_element_type=f32)


def row(x, rows=8):
    return jnp.broadcast_to(x, (rows, x.shape[1]))


def lookup(chunks, wanted, position):
    out = None
    for number, chunk in chunks:
        got = jnp.take_along_axis(row(chunk), position, axis=1, mode="promise_in_bounds")
        out = got if out is None else jnp.where(wanted == number, got, out)
    return out


def harmonics(ux, uy, uz):
    return [
        None,
        SQRT3 * ux,
        SQRT3 * uy,
        SQRT3 * uz,
        SQRT15 * ux * uy,
        SQRT15 * uy * uz,
        0.5 * SQRT5 * (2.0 * uz * uz - ux * ux - uy * uy),
        SQRT15 * ux * uz,
        0.5 * SQRT15 * (ux * ux - uy * uy),
    ]


def silu_parts(v):
    gate = 1.0 / (1.0 + jnp.exp(-v))
    return v * gate, gate * (1.0 + v * (1.0 - gate))


def force_kernel(plan, *refs):
    atoms, near, wide, before, after = plan
    n_wide = len(wide)
    blocks = refs[:n_wide]
    sources = refs[n_wide : n_wide + 8]
    push_ref, mass_ref = refs[n_wide + 8 : n_wide + 10]
    (
        geo_ref, y_ref, yb_ref, bk_ref, bt_ref, gidx_ref, as_ref, m1_ref, sp1_ref, hs_ref, oh_ref,
        hj_ref, w_ref, car_ref, m2_ref, inv_ref, dinv_ref, p_ref, dhe_ref, dw_ref, da_ref, q_ref,
        val_ref, ohlo_ref, moment_ref, emb_ref, rad1_ref, rad2_ref, mix1_ref, mix2_ref, read1_ref, read2_ref, sems,
    ) = refs[n_wide + 10 :]
    held = (moment_ref, emb_ref, rad1_ref, rad2_ref, mix1_ref, mix2_ref, read1_ref, read2_ref)
    fetches = [pltpu.make_async_copy(src, dst, sems.at[i]) for i, (src, dst) in enumerate(zip(sources, held))]
    for fetch in fetches:
        fetch.start()
    chan = emb_ref.shape[1]
    bases = rad1_ref.shape[0]
    slots = gidx_ref.shape[0]
    n_near = len(near) * atoms
    tiles = atoms // LANES
    half = atoms // 2
    half_tiles = half // LANES
    edges = slots * atoms
    top_rows = val_ref.shape[0] // 6

    order_col = lax.broadcasted_iota(jnp.int32, (bases, LANES), 0).astype(f32)
    tables = []
    for quantity in range(4):
        chunks = []
        for g in range(n_wide):
            for t in range(tiles):
                chunks.append((g * tiles + t, blocks[g][quantity : quantity + 1, t * LANES : (t + 1) * LANES]))
        tables.append(chunks)
    for q in range(len(near)):
        ghosts = []
        for t in range(half_tiles):
            ghosts.append(
                (t, blocks[before[q]][4:5, half + t * LANES : half + (t + 1) * LANES] + float(before[q] * atoms))
            )
        for t in range(half_tiles):
            ghosts.append(
                (
                    half_tiles + tiles + t,
                    blocks[after[q]][4:5, t * LANES : (t + 1) * LANES] + float(after[q] * atoms),
                )
            )
        for t in range(tiles):
            cols = slice(t * LANES, (t + 1) * LANES)
            here = slice(q * atoms + t * LANES, q * atoms + (t + 1) * LANES)
            slot = blocks[q][HEAD : HEAD + slots, cols].astype(jnp.int32)
            chunk_no = slot >> 7
            far = lookup(ghosts, chunk_no, slot & 127).astype(jnp.int32)
            own = (slot >= half) & (slot < half + atoms)
            gidx = jnp.where(own, slot + (q * atoms - half), far)
            gidx_ref[:, here] = gidx
            chunk_no = gidx >> 7
            place = gidx & 127
            xj, yj, zj, fj = [lookup(tables[i], chunk_no, place) for i in range(4)]
            rx = xj - row(blocks[q][0:1, cols])
            ry = yj - row(blocks[q][1:2, cols])
            rz = zj - row(blocks[q][2:3, cols])
            soft = jnp.sqrt(rx * rx + ry * ry + rz * rz + 1.0)
            back = 1.0 / soft
            ux, uy, uz = rx * back, ry * back, rz * back
            for i, value in enumerate((ux, uy, uz, back, soft, fj)):
                geo_ref[i, :, here] = value
            sphere = harmonics(ux, uy, uz)
            for l in range(1, ORDERS):
                y_ref[l, :, here] = sphere[l]
                if q == 0:
                    for k in range(slots):
                        yb_ref[l, k, :, cols] = row(sphere[l][k : k + 1, :])
            for n in range(bases):
                bk_ref[n, :, here] = jnp.exp(-0.5 * (soft - (1.0 + n)) ** 2)
            for k in range(slots):
                basis = jnp.exp(-0.5 * (row(soft[k : k + 1, :], bases) - (1.0 + order_col)) ** 2)
                bt_ref[k, 0:bases, here] = basis
                bt_ref[k, bases : 2 * bases, here] = basis * row(fj[k : k + 1, :], bases)

    for fetch in fetches:
        fetch.wait()
    emb0 = emb_ref[0:1, :]
    emb_d = emb_ref[1:2, :] - emb0
    rr = jnp.concatenate([rad1_ref[...] * emb0, rad1_ref[...] * emb_d], axis=0) * (1.0 / slots)
    rr_hi = rr.astype(bf16).astype(f32)
    rr_lo = rr - rr_hi
    r2 = rad2_ref[...] * (1.0 / slots)
    r2_hi = r2.astype(bf16).astype(f32)
    r2_lo = r2 - r2_hi
    zeros = jnp.zeros((8, chan), f32)
    turned1 = jnp.concatenate([rr_hi, rr_hi, rr_lo, rr_lo] + [zeros] * 8, axis=0).T
    sides = jnp.concatenate([emb0, emb_d, read1_ref[...], read2_ref[...], zeros[:4]], axis=0)
    turned2 = jnp.concatenate([r2_hi, r2_hi, r2_lo, r2_lo, sides] + [zeros] * 11, axis=0).T
    rr_cols = turned1[:, : 8 * bases].astype(bf16)
    r2_cols = turned2[:, : 4 * bases].astype(bf16)
    emb0_col = turned2[:, 4 * bases : 4 * bases + 1]
    embd_col = turned2[:, 4 * bases + 1 : 4 * bases + 2]
    read1_col = turned2[:, 4 * bases + 2 : 4 * bases + 3]
    read2_col = turned2[:, 4 * bases + 3 : 4 * bases + 4]
    rr_rows = jnp.concatenate(
        [jnp.concatenate([rr_hi, rr_hi], axis=1), jnp.concatenate([rr_lo, jnp.zeros_like(rr_lo)], axis=1)], axis=0
    ).astype(bf16)
    r2_rows = jnp.concatenate(
        [jnp.concatenate([r2_hi, r2_hi], axis=1), jnp.concatenate([r2_lo, jnp.zeros_like(r2_lo)], axis=1)], axis=0
    ).astype(bf16)

    def sums(t, carry):
        here = pl.ds(pl.multiple_of(t * LANES, LANES), LANES)
        low = [None] * ORDERS
        for k in range(slots):
            basis = bt_ref[k, :, here]
            for l in range(ORDERS):
                term = basis if l == 0 else basis * row(y_ref[l, k : k + 1, here], 2 * bases)
                low[l] = term if low[l] is None else low[l] + term
        for l in range(ORDERS):
            both = split_rows(low[l]).astype(bf16)
            as_ref[l, 0 : 4 * bases, here] = both
            as_ref[l, 4 * bases : 8 * bases, here] = both
        return carry

    lax.fori_loop(0, n_near // LANES, sums, 0)

    flags_row = jnp.concatenate([blocks[q][3:4, :] for q in range(len(near))], axis=1)
    wide_cols = 2 * LANES

    def first(j, carry):
        here = pl.ds(pl.multiple_of(j * wide_cols, wide_cols), wide_cols)
        inv = [None, None, None]
        for l in range(ORDERS):
            m = dot(rr_cols, as_ref[l, :, here])
            m1_ref[l, :, here] = m
            inv[GROUP[l]] = m * m if inv[GROUP[l]] is None else inv[GROUP[l]] + m * m
        value = dot(mix1_ref[...], jnp.concatenate(inv, axis=0), HIGH)
        act, slope = silu_parts(value)
        sp1_ref[:, here] = slope
        hidden = act + emb0_col + embd_col * q_ref[0:1, here]
        hi, lo = split(hidden)
        hs_ref[0:chan, here] = hi
        hs_ref[chan : 2 * chan, here] = lo
        return carry

    q_ref[0:1, :] = flags_row
    lax.fori_loop(0, n_near // wide_cols, first, 0)

    def gather(k, carry):
        here = pl.ds(pl.multiple_of(k * atoms, atoms), atoms)
        wanted = gidx_ref[pl.ds(k, 1), 0:atoms]
        for r in range(n_near // LANES):
            ids = lax.broadcasted_iota(jnp.int32, (LANES, atoms), 0) + r * LANES
            oh_ref[r * LANES : (r + 1) * LANES, here] = jnp.where(ids == wanted, 1.0, 0.0).astype(bf16)
        both = dot(hs_ref[...], oh_ref[:, here])
        feat = both[:chan] + both[chan:]
        basis = split_rows(bt_ref[k, 0:bases, 0:atoms])
        weight = dot(r2_cols, jnp.concatenate([basis, basis], axis=0).astype(bf16))
        hj_ref[:, here] = feat
        w_ref[:, here] = weight
        car_ref[:, here] = feat * weight
        return carry

    lax.fori_loop(0, slots, gather, 0)

    pairs = chan // 16

    def moments(step, carry):
        t = step // pairs
        c = step % pairs
        cols = pl.ds(pl.multiple_of(t * LANES, LANES), LANES)
        base = pl.multiple_of(c * 16, 16)
        acc = [[None] * ORDERS, [None] * ORDERS]
        for k in range(slots):
            at = pl.ds(pl.multiple_of(k * atoms + t * LANES, LANES), LANES)
            got = car_ref[pl.ds(base, 16), at]
            for l in range(ORDERS):
                yb = yb_ref[l, k, :, cols] if l else None
                for h in range(2):
                    part = got[8 * h : 8 * h + 8]
                    term = part * yb if l else part
                    acc[h][l] = term if acc[h][l] is None else acc[h][l] + term
        inv = [[None] * 3, [None] * 3]
        for l in range(ORDERS):
            m2_ref[l, pl.ds(base, 16), cols] = jnp.concatenate([acc[0][l], acc[1][l]], axis=0)
            for h in range(2):
                sq = acc[h][l] * acc[h][l]
                g = GROUP[l]
                inv[h][g] = sq if inv[h][g] is None else inv[h][g] + sq
        for g in range(3):
            inv_ref[pl.ds(pl.multiple_of(g * chan + c * 16, 16), 16), cols] = jnp.concatenate(
                [inv[0][g], inv[1][g]], axis=0
            )
        return carry

    lax.fori_loop(0, tiles * pairs, moments, 0)

    for t in range(atoms // wide_cols):
        cols = slice(t * wide_cols, (t + 1) * wide_cols)
        value = dot(mix2_ref[...], inv_ref[:, cols], HIGH)
        _, slope = silu_parts(value)
        slope = slope * (2.0 * read2_col)
        for g in range(3):
            mixed = mix2_ref[:, g * chan : (g + 1) * chan].T
            dinv_ref[g * chan : (g + 1) * chan, cols] = dot(mixed, slope, HIGH)

    k_step = slots // 2

    def back_moments(step, carry):
        t = step // 2
        k0 = (step % 2) * k_step
        cols = pl.ds(pl.multiple_of(t * LANES, LANES), LANES)

        def over(c, acc):
            acc = list(acc)
            base = pl.multiple_of(c * 16, 16)
            dm = []
            scale = [dinv_ref[pl.ds(pl.multiple_of(g * chan + c * 16, 16), 16), cols] for g in range(3)]
            for l in range(ORDERS):
                dm.append(m2_ref[l, pl.ds(base, 16), cols] * scale[GROUP[l]])
            for kk in range(k_step):
                k = k0 + kk
                at = pl.ds(pl.multiple_of(k * atoms + t * LANES, LANES), LANES)
                got = car_ref[pl.ds(base, 16), at]
                out = [dm[0][:8], dm[0][8:]]
                for l in range(1, ORDERS):
                    yb = yb_ref[l, k, :, cols]
                    i = kk * (ORDERS - 1) + l - 1
                    for h in range(2):
                        part = dm[l][8 * h : 8 * h + 8]
                        out[h] = out[h] + part * yb
                        acc[i] = acc[i] + part * got[8 * h : 8 * h + 8]
                dcar = jnp.concatenate(out, axis=0)
                for ref, other in ((dhe_ref, w_ref), (dw_ref, hj_ref)):
                    hi, lo = split(dcar * other[pl.ds(base, 16), at])
                    ref[pl.ds(base, 16), at] = hi
                    ref[pl.ds(pl.multiple_of(chan + c * 16, 16), 16), at] = lo
            return tuple(acc)

        start = tuple(jnp.zeros((8, LANES), f32) for _ in range(k_step * (ORDERS - 1)))
        acc = lax.fori_loop(0, pairs, over, start)
        for kk in range(k_step):
            for l in range(1, ORDERS):
                p_ref[l, pl.ds(pl.multiple_of((k0 + kk) * 8, 8), 8), cols] = acc[kk * (ORDERS - 1) + l - 1]
        return carry

    lax.fori_loop(0, tiles * 2, back_moments, 0)

    for k in range(slots):
        here = slice(k * atoms, (k + 1) * atoms)
        both = dot(r2_rows, dw_ref[:, here])
        dbasis = both[:bases] + both[bases:]
        basis = bt_ref[k, 0:bases, 0:atoms]
        reach = 1.0 + lax.broadcasted_iota(jnp.int32, (bases, atoms), 0).astype(f32)
        p_ref[0, k * 8 : k * 8 + 8, :] = dbasis * basis * (reach - row(geo_ref[4, k : k + 1, 0:atoms], bases))

    def back_first(j, carry):
        start = pl.multiple_of(j * wide_cols, wide_cols)
        here = pl.ds(start, wide_cols)
        both = dot_nt(dhe_ref[...], oh_ref[here, :])
        dh = both[:chan] + both[chan:]
        mine = jnp.where(start < atoms, 1.0, 0.0)
        dtop = (dh + read1_col * mine) * sp1_ref[:, here] * 2.0
        scale = []
        for g in range(3):
            scale.append(dot(mix1_ref[:, g * chan : (g + 1) * chan].T, dtop, HIGH))
        for l in range(ORDERS):
            hi, lo = split(m1_ref[l, :, here] * scale[GROUP[l]])
            out = dot(rr_rows, jnp.concatenate([hi, lo], axis=0))
            da_ref[l, :, here] = out[: 2 * bases] + out[2 * bases :]
        return carry

    lax.fori_loop(0, n_near // wide_cols, back_first, 0)

    lane = lax.broadcasted_iota(jnp.int32, (slots, 16 * slots), 1)
    sub = lax.broadcasted_iota(jnp.int32, (slots, 16 * slots), 0)
    adder = jnp.where(((lane >> 3) & (slots - 1)) == sub, 1.0, 0.0).astype(bf16)
    for l in range(ORDERS):
        q_ref[8 * l : 8 * l + 8, 0:atoms] = dot(adder, split_rows(p_ref[l, :, :]).astype(bf16))

    def back_geometry(t, mine):
        here = pl.ds(pl.multiple_of(t * LANES, LANES), LANES)
        ux, uy, uz, back, soft, fj = [geo_ref[i, :, here] for i in range(6)]
        dy = [None] * ORDERS
        ds = None
        for n in range(bases):
            basis = bk_ref[n, :, here]
            db = None
            for l in range(ORDERS):
                g = row(da_ref[l, n : n + 1, here]) + fj * row(da_ref[l, bases + n : bases + n + 1, here])
                if l:
                    dy[l] = g * basis if dy[l] is None else dy[l] + g * basis
                    db = db + g * y_ref[l, :, here]
                else:
                    db = g
            db = db * basis * ((1.0 + n) - soft)
            ds = db if ds is None else ds + db
        if mine:
            ds = ds + q_ref[0:8, here]
            for l in range(1, ORDERS):
                dy[l] = dy[l] + q_ref[8 * l : 8 * l + 8, here]
        dux = SQRT3 * dy[1] + SQRT15 * (uy * dy[4] + uz * dy[7] + ux * dy[8]) - SQRT5 * ux * dy[6]
        duy = SQRT3 * dy[2] + SQRT15 * (ux * dy[4] + uz * dy[5] - uy * dy[8]) - SQRT5 * uy * dy[6]
        duz = SQRT3 * dy[3] + SQRT15 * (uy * dy[5] + ux * dy[7]) + 2.0 * SQRT5 * uz * dy[6]
        along = ds - (ux * dux + uy * duy + uz * duz) * back
        dr = [dux * back + along * ux, duy * back + along * uy, duz * back + along * uz]
        for i in range(3):
            geo_ref[i, :, here] = dr[i]
        return dr

    def mine_tile(t, carry):
        back_geometry(t, True)
        return carry

    def other_tile(t, carry):
        back_geometry(t, False)
        return carry

    lax.fori_loop(0, tiles, mine_tile, 0)
    lax.fori_loop(tiles, n_near // LANES, other_tile, 0)

    def place_tile(t, carry):
        here = pl.ds(pl.multiple_of(t * LANES, LANES), LANES)
        gidx = gidx_ref[:, here]
        chunk_no = gidx >> 7
        place = gidx & 127
        parts = []
        for i in range(3):
            value = geo_ref[i, :, here]
            hi = value.astype(bf16).astype(f32)
            parts.append((hi, value - hi))
        chunk_ids = lax.broadcasted_iota(jnp.int32, (top_rows, LANES), 0)
        place_ids = lax.broadcasted_iota(jnp.int32, (LANES, LANES), 0)
        for k in range(slots):
            at = pl.ds(pl.multiple_of(k * n_near + t * LANES, LANES), LANES)
            hit = chunk_ids == row(chunk_no[k : k + 1, :], top_rows)
            for i in range(3):
                both = [jnp.where(hit, row(part[k : k + 1, :], top_rows), 0.0) for part in parts[i]]
                val_ref[2 * i * top_rows : 2 * (i + 1) * top_rows, at] = jnp.concatenate(both, axis=0).astype(bf16)
            ohlo_ref[:, at] = jnp.where(place_ids == row(place[k : k + 1, :], LANES), 1.0, 0.0).astype(bf16)
        return carry

    lax.fori_loop(0, n_near // LANES, place_tile, 0)
    landed = dot_nt(val_ref[...], ohlo_ref[...])
    lines = push_ref.shape[0] // (n_wide + 1)
    for i in range(3):
        total = (
            landed[2 * i * top_rows : (2 * i + 1) * top_rows] + landed[(2 * i + 1) * top_rows : (2 * i + 2) * top_rows]
        )
        for g in range(n_wide):
            for t in range(tiles):
                cols = slice(t * LANES, (t + 1) * LANES)
                line = total[g * tiles + t : g * tiles + t + 1, :]
                if g < len(near):
                    here = slice(g * atoms + t * LANES, g * atoms + (t + 1) * LANES)
                    line = line - jnp.sum(geo_ref[i, :, here], axis=0, keepdims=True)
                line = -HALF_STEP * line
                at = i * tiles + t
                if g == 0:
                    line = line + moment_ref[i, :, cols]
                    push_ref[at : at + 1, :] = blocks[0][i : i + 1, cols]
                push_ref[(1 + g) * lines + at : (1 + g) * lines + at + 1, :] = line
                mass = HEAVY - (HEAVY - 1.0) * blocks[g][3:4, cols]
                mass_ref[g * lines + at : g * lines + at + 1, :] = mass
    if lines > 3 * tiles:
        for g in range(n_wide + 1):
            blank = slice(g * lines + 3 * tiles, (g + 1) * lines)
            push_ref[blank, :] = jnp.zeros((lines - 3 * tiles, LANES), f32)
            if g < n_wide:
                mass_ref[blank, :] = jnp.ones((lines - 3 * tiles, LANES), f32)


def line_count(atoms):
    return -(-3 * (atoms // LANES) // 8) * 8


def ring_plan(domains, atoms):
    near = list(dict.fromkeys(o % domains for o in (0, 1, -1)))
    wide = list(dict.fromkeys(near + [o % domains for o in (2, -2)]))
    before = tuple(wide.index((o - 1) % domains) for o in near)
    after = tuple(wide.index((o + 1) % domains) for o in near)
    return atoms, tuple(near), tuple(wide), before, after


def pushes(plan, blocks, momenta, embedding, radial_one, radial_two, mix_one, mix_two, read_one, read_two):
    atoms, near, wide, _, _ = plan
    chan = embedding.shape[1]
    bases = radial_one.shape[0]
    slots = blocks[0].shape[0] - HEAD
    n_near = len(near) * atoms
    edges = slots * atoms
    top_rows = -(-len(wide) * atoms // LANES // 8) * 8
    lines = line_count(atoms)
    vmem = pl.BlockSpec(memory_space=pltpu.VMEM)
    far = pl.BlockSpec(memory_space=pltpu.HBM)
    sources = (momenta, embedding, radial_one, radial_two, mix_one, mix_two, read_one[None], read_two[None])
    return pl.pallas_call(
        functools.partial(force_kernel, plan),
        out_shape=(
            jax.ShapeDtypeStruct(((len(wide) + 1) * lines, LANES), f32),
            jax.ShapeDtypeStruct((len(wide) * lines, LANES), f32),
        ),
        in_specs=[vmem] * len(wide) + [far] * len(sources),
        out_specs=(vmem, vmem),
        scratch_shapes=[
            pltpu.VMEM((6, slots, n_near), f32),
            pltpu.VMEM((ORDERS, slots, n_near), f32),
            pltpu.VMEM((ORDERS, slots, 8, atoms), f32),
            pltpu.VMEM((bases, slots, n_near), f32),
            pltpu.VMEM((slots, 2 * bases, n_near), f32),
            pltpu.VMEM((slots, n_near), jnp.int32),
            pltpu.VMEM((ORDERS, 8 * bases, n_near), bf16),
            pltpu.VMEM((ORDERS, chan, n_near), f32),
            pltpu.VMEM((chan, n_near), f32),
            pltpu.VMEM((2 * chan, n_near), bf16),
            pltpu.VMEM((n_near, edges), bf16),
            pltpu.VMEM((chan, edges), f32),
            pltpu.VMEM((chan, edges), f32),
            pltpu.VMEM((chan, edges), f32),
            pltpu.VMEM((ORDERS, chan, atoms), f32),
            pltpu.VMEM((3 * chan, atoms), f32),
            pltpu.VMEM((3 * chan, atoms), f32),
            pltpu.VMEM((ORDERS, 8 * slots, atoms), f32),
            pltpu.VMEM((2 * chan, edges), bf16),
            pltpu.VMEM((2 * chan, edges), bf16),
            pltpu.VMEM((ORDERS, 2 * bases, n_near), f32),
            pltpu.VMEM((8 * ORDERS, n_near), f32),
            pltpu.VMEM((6 * top_rows, slots * n_near), bf16),
            pltpu.VMEM((LANES, slots * n_near), bf16),
        ]
        + [pltpu.VMEM(source.shape, f32) for source in sources]
        + [pltpu.SemaphoreType.DMA((len(sources),))],
        compiler_params=pltpu.CompilerParams(vmem_limit_bytes=(26 + 10 * len(near)) * MIB),
        name="forces",
    )(*blocks, *sources)


def mode_turns(bead_total):
    bead = np.arange(bead_total, dtype=np.float64)[:, None]
    mode = np.arange(bead_total, dtype=np.float64)[None, :]
    phase = 2.0 * np.pi * bead * mode / bead_total
    half_total = bead_total // 2
    table = math.sqrt(2.0 / bead_total) * np.where(mode < half_total, np.cos(phase), np.sin(phase))
    table = np.where(mode == half_total, np.cos(np.pi * bead) / math.sqrt(bead_total), table)
    table = np.where(mode == 0, 1.0 / math.sqrt(bead_total), table)
    angles = bead_total * np.sin(np.pi * mode[0] / bead_total)
    safe = np.where(mode[0] == 0, 1.0, angles)
    reach = np.where(mode[0] == 0, STEP, STEP * np.sin(angles) / safe)
    stiff = angles * np.sin(angles) / STEP
    return [[float(x) for x in (table * factor[None, :]) @ table[0]] for factor in (np.cos(angles), reach, stiff)]


def pack_kernel(coord_src, species_src, send_src, slot_src, block_ref, coord_ref, species_ref, send_ref, slot_ref, sems):
    pairs = ((coord_src, coord_ref), (species_src, species_ref), (send_src, send_ref), (slot_src, slot_ref))
    fetches = [pltpu.make_async_copy(src, dst, sems.at[i]) for i, (src, dst) in enumerate(pairs)]
    for fetch in fetches:
        fetch.start()
    for fetch in fetches:
        fetch.wait()
    atoms = block_ref.shape[1]
    for i in range(3):
        block_ref[i : i + 1, :] = coord_ref[i]
    block_ref[3:4, :] = species_ref[...].astype(f32)
    block_ref[4:5, :] = send_ref[...].astype(f32)
    block_ref[5:HEAD, :] = jnp.zeros((HEAD - 5, atoms), f32)
    block_ref[HEAD:, :] = slot_ref[...].astype(f32)


def turn_kernel(shape, bead_ref, mass_ref, *refs):
    outer, inner, n_wide = shape
    sources, messages = refs[:outer], refs[outer:]
    turns = mode_turns(outer * inner)
    lines = mass_ref.shape[0] // n_wide
    my_inner = jnp.full((lines, LANES), lax.rem(bead_ref[0], inner))
    for s in range(inner):
        wraps = my_inner + s >= inner
        weights = []
        for turn in turns:
            row_of = []
            for sh in range(outer):
                there = turn[(sh * inner + s) % (outer * inner)]
                round_it = turn[(sh * inner + s - inner) % (outer * inner)]
                row_of.append(jnp.where(wraps, jnp.full((lines, LANES), round_it), jnp.full((lines, LANES), there)))
            weights.append(row_of)
        for g in range(n_wide):
            mass = mass_ref[g * lines : (g + 1) * lines, :]
            turned = drift = spring = None
            for sh in range(outer):
                kick = sources[sh][(1 + g) * lines : (2 + g) * lines, :]
                turned = weights[0][sh] * kick if sh == 0 else turned + weights[0][sh] * kick
                drift = weights[1][sh] * kick if sh == 0 else drift + weights[1][sh] * kick
            new_q = drift / mass
            new_p = turned
            if g == 0:
                for sh in range(outer):
                    coord = sources[sh][0:lines, :]
                    new_q = new_q + weights[0][sh] * coord
                    spring = weights[2][sh] * coord if sh == 0 else spring + weights[2][sh] * coord
                new_p = new_p - mass * spring
            message = messages[g * inner + s]
            message[0:lines, :] = new_q
            message[lines:, :] = new_p


def sum_kernel(*refs):
    q_ref, p_ref = refs[-2:]
    total = refs[0][...]
    for ref in refs[1:-2]:
        total = total + ref[...]
    lines = total.shape[0] // 2
    tiles = q_ref.shape[2] // LANES
    for i in range(3):
        for t in range(tiles):
            at = i * tiles + t
            q_ref[i, :, t * LANES : (t + 1) * LANES] = total[at : at + 1]
            p_ref[i, :, t * LANES : (t + 1) * LANES] = total[lines + at : lines + at + 1]


def shards(
    positions, momenta, species, neighbours, send_list, embedding, radial_one, radial_two, mix_one, mix_two,
    read_one, read_two,
):
    slots, atoms = neighbours.shape
    domains = lax.axis_size("space")
    beads = lax.axis_size("bead")
    inner = next(d for d in range(1, beads + 1) if beads % d == 0 and d * d >= beads)
    outer = beads // inner
    plan = ring_plan(domains, atoms)
    wide = plan[2]
    vmem = pl.BlockSpec(memory_space=pltpu.VMEM)
    smem = pl.BlockSpec(memory_space=pltpu.SMEM)
    far = pl.BlockSpec(memory_space=pltpu.HBM)
    small = pltpu.CompilerParams(vmem_limit_bytes=4 * MIB)
    coord_rows = jnp.transpose(positions, (1, 0, 2))
    moment_rows = jnp.transpose(momenta, (1, 0, 2))
    block = pl.pallas_call(
        pack_kernel,
        out_shape=jax.ShapeDtypeStruct((HEAD + slots, atoms), f32),
        in_specs=[far] * 4,
        out_specs=vmem,
        scratch_shapes=[
            pltpu.VMEM(coord_rows.shape, f32),
            pltpu.VMEM((1, atoms), jnp.int32),
            pltpu.VMEM((1, atoms), jnp.int32),
            pltpu.VMEM((slots, atoms), jnp.int32),
            pltpu.SemaphoreType.DMA((4,)),
        ],
        compiler_params=small,
        name="pack",
    )(coord_rows, species[None], send_list[None], neighbours)
    blocks = [block]
    for offset in wide[1:]:
        blocks.append(lax.ppermute(block, "space", [(i, (i - offset) % domains) for i in range(domains)]))
    pushed, masses = pushes(
        plan, blocks, moment_rows, embedding, radial_one, radial_two, mix_one, mix_two, read_one, read_two
    )
    sources = [pushed]
    for sh in range(1, outer):
        sources.append(lax.ppermute(pushed, "bead", [(b, (b + sh * inner) % beads) for b in range(beads)]))
    bead = lax.axis_index("bead").astype(jnp.int32).reshape(1)
    lines = line_count(atoms)
    messages = pl.pallas_call(
        functools.partial(turn_kernel, (outer, inner, len(wide))),
        out_shape=(jax.ShapeDtypeStruct((2 * lines, LANES), f32),) * (inner * len(wide)),
        in_specs=[smem] + [vmem] * (1 + outer),
        out_specs=(vmem,) * (inner * len(wide)),
        compiler_params=small,
        name="turn",
    )(bead, masses, *sources)
    arrived = []
    for g, offset in enumerate(wide):
        for s in range(inner):
            message = messages[g * inner + s]
            if g or s:
                pairs = []
                for b in range(beads):
                    to_bead = b - b % inner + (b + s) % inner
                    for d in range(domains):
                        pairs.append((b * domains + d, to_bead * domains + (d + offset) % domains))
                message = lax.ppermute(message, ("bead", "space"), pairs)
            arrived.append(message)
    new_q, new_p = pl.pallas_call(
        sum_kernel,
        out_shape=(jax.ShapeDtypeStruct((3, 1, atoms), f32),) * 2,
        in_specs=[vmem] * len(arrived),
        out_specs=(vmem, vmem),
        compiler_params=small,
        name="sum",
    )(*arrived)
    return (jnp.transpose(new_q, (1, 0, 2)), jnp.transpose(new_p, (1, 0, 2)))


def solution(mesh):
    placed = (
        P("bead", None, "space"),
        P("bead", None, "space"),
        P("space"),
        P(None, "space"),
        P("space"),
        P(),
        P(),
        P(),
        P(),
        P(),
        P(),
        P(),
    )
    return jax.shard_map(
        shards,
        mesh=mesh,
        in_specs=placed,
        out_specs=(P("bead", None, "space"), P("bead", None, "space")),
        check_vma=False,
    )
```

```python
import functools
import math

import jax
import jax.numpy as jnp
import numpy as np
from jax import lax
from jax.experimental import pallas as pl
from jax.experimental.pallas import tpu as pltpu
from jax.sharding import PartitionSpec as P

STEP = 2.0
HALF_STEP = 1.0
HEAVY = 16.0
SQRT3 = math.sqrt(3.0)
SQRT5 = math.sqrt(5.0)
SQRT15 = math.sqrt(15.0)
LANES = 128
ORDERS = 9
GROUP = (0, 1, 1, 1, 2, 2, 2, 2, 2)
HEAD = 8
MIB = 1024 * 1024
f32 = jnp.float32
bf16 = jnp.bfloat16
HIGH = lax.Precision.HIGH


def split(x):
    hi = x.astype(bf16)
    return hi, (x - hi.astype(f32)).astype(bf16)


def split_rows(x):
    hi = x.astype(bf16).astype(f32)
    return jnp.concatenate([hi, x - hi], axis=0)


def dot(a, b, precision=None):
    return jnp.dot(a, b, preferred_element_type=f32, precision=precision)


def dot_nt(a, b):
    return lax.dot_general(a, b, (((1,), (1,)), ((), ())), preferred_element_type=f32)


def row(x, rows=8):
    return jnp.broadcast_to(x, (rows, x.shape[1]))


def lookup(chunks, wanted, position):
    out = None
    for number, chunk in chunks:
        got = jnp.take_along_axis(row(chunk), position, axis=1, mode="promise_in_bounds")
        out = got if out is None else jnp.where(wanted == number, got, out)
    return out


def harmonics(ux, uy, uz):
    return [
        None,
        SQRT3 * ux,
        SQRT3 * uy,
        SQRT3 * uz,
        SQRT15 * ux * uy,
        SQRT15 * uy * uz,
        0.5 * SQRT5 * (2.0 * uz * uz - ux * ux - uy * uy),
        SQRT15 * ux * uz,
        0.5 * SQRT15 * (ux * ux - uy * uy),
    ]


def silu_parts(v):
    gate = 1.0 / (1.0 + jnp.exp(-v))
    return v * gate, gate * (1.0 + v * (1.0 - gate))


def force_kernel(plan, *refs):
    atoms, near, wide, before, after = plan
    n_wide = len(wide)
    blocks = refs[:n_wide]
    sources = refs[n_wide : n_wide + 8]
    push_ref, mass_ref = refs[n_wide + 8 : n_wide + 10]
    (
        geo_ref, y_ref, yb_ref, bk_ref, bt_ref, gidx_ref, as_ref, m1_ref, sp1_ref, hs_ref, oh_ref,
        hj_ref, w_ref, car_ref, m2_ref, inv_ref, dinv_ref, p_ref, dhe_ref, dw_ref, da_ref, q_ref,
        val_ref, ohlo_ref, moment_ref, emb_ref, rad1_ref, rad2_ref, mix1_ref, mix2_ref, read1_ref, read2_ref, sems,
    ) = refs[n_wide + 10 :]
    held = (moment_ref, emb_ref, rad1_ref, rad2_ref, mix1_ref, mix2_ref, read1_ref, read2_ref)
    fetches = [pltpu.make_async_copy(src, dst, sems.at[i]) for i, (src, dst) in enumerate(zip(sources, held))]
    for fetch in fetches:
        fetch.start()
    chan = emb_ref.shape[1]
    bases = rad1_ref.shape[0]
    slots = gidx_ref.shape[0]
    n_near = len(near) * atoms
    tiles = atoms // LANES
    half = atoms // 2
    half_tiles = half // LANES
    edges = slots * atoms
    top_rows = val_ref.shape[0] // 6

    order_col = lax.broadcasted_iota(jnp.int32, (bases, LANES), 0).astype(f32)
    tables = []
    for quantity in range(4):
        chunks = []
        for g in range(n_wide):
            for t in range(tiles):
                chunks.append((g * tiles + t, blocks[g][quantity : quantity + 1, t * LANES : (t + 1) * LANES]))
        tables.append(chunks)
    for q in range(len(near)):
        ghosts = []
        for t in range(half_tiles):
            ghosts.append(
                (t, blocks[before[q]][4:5, half + t * LANES : half + (t + 1) * LANES] + float(before[q] * atoms))
            )
        for t in range(half_tiles):
            ghosts.append(
                (
                    half_tiles + tiles + t,
                    blocks[after[q]][4:5, t * LANES : (t + 1) * LANES] + float(after[q] * atoms),
                )
            )
        for t in range(tiles):
            cols = slice(t * LANES, (t + 1) * LANES)
            here = slice(q * atoms + t * LANES, q * atoms + (t + 1) * LANES)
            slot = blocks[q][HEAD : HEAD + slots, cols].astype(jnp.int32)
            chunk_no = slot >> 7
            far = lookup(ghosts, chunk_no, slot & 127).astype(jnp.int32)
            own = (slot >= half) & (slot < half + atoms)
            gidx = jnp.where(own, slot + (q * atoms - half), far)
            gidx_ref[:, here] = gidx
            chunk_no = gidx >> 7
            place = gidx & 127
            xj, yj, zj, fj = [lookup(tables[i], chunk_no, place) for i in range(4)]
            rx = xj - row(blocks[q][0:1, cols])
            ry = yj - row(blocks[q][1:2, cols])
            rz = zj - row(blocks[q][2:3, cols])
            soft = jnp.sqrt(rx * rx + ry * ry + rz * rz + 1.0)
            back = 1.0 / soft
            ux, uy, uz = rx * back, ry * back, rz * back
            for i, value in enumerate((ux, uy, uz, back, soft, fj)):
                geo_ref[i, :, here] = value
            sphere = harmonics(ux, uy, uz)
            for l in range(1, ORDERS):
                y_ref[l, :, here] = sphere[l]
                if q == 0:
                    for k in range(slots):
                        yb_ref[l, k, :, cols] = row(sphere[l][k : k + 1, :])
            for n in range(bases):
                bk_ref[n, :, here] = jnp.exp(-0.5 * (soft - (1.0 + n)) ** 2)
            for k in range(slots):
                basis = jnp.exp(-0.5 * (row(soft[k : k + 1, :], bases) - (1.0 + order_col)) ** 2)
                bt_ref[k, 0:bases, here] = basis
                bt_ref[k, bases : 2 * bases, here] = basis * row(fj[k : k + 1, :], bases)

    for fetch in fetches:
        fetch.wait()
    emb0 = emb_ref[0:1, :]
    emb_d = emb_ref[1:2, :] - emb0
    rr = jnp.concatenate([rad1_ref[...] * emb0, rad1_ref[...] * emb_d], axis=0) * (1.0 / slots)
    rr_hi = rr.astype(bf16).astype(f32)
    rr_lo = rr - rr_hi
    r2 = rad2_ref[...] * (1.0 / slots)
    r2_hi = r2.astype(bf16).astype(f32)
    r2_lo = r2 - r2_hi
    zeros = jnp.zeros((8, chan), f32)
    turned1 = jnp.concatenate([rr_hi, rr_hi, rr_lo, rr_lo] + [zeros] * 8, axis=0).T
    sides = jnp.concatenate([emb0, emb_d, read1_ref[...], read2_ref[...], zeros[:4]], axis=0)
    turned2 = jnp.concatenate([r2_hi, r2_hi, r2_lo, r2_lo, sides] + [zeros] * 11, axis=0).T
    rr_cols = turned1[:, : 8 * bases].astype(bf16)
    r2_cols = turned2[:, : 4 * bases].astype(bf16)
    emb0_col = turned2[:, 4 * bases : 4 * bases + 1]
    embd_col = turned2[:, 4 * bases + 1 : 4 * bases + 2]
    read1_col = turned2[:, 4 * bases + 2 : 4 * bases + 3]
    read2_col = turned2[:, 4 * bases + 3 : 4 * bases + 4]
    rr_rows = jnp.concatenate(
        [jnp.concatenate([rr_hi, rr_hi], axis=1), jnp.concatenate([rr_lo, jnp.zeros_like(rr_lo)], axis=1)], axis=0
    ).astype(bf16)
    r2_rows = jnp.concatenate(
        [jnp.concatenate([r2_hi, r2_hi], axis=1), jnp.concatenate([r2_lo, jnp.zeros_like(r2_lo)], axis=1)], axis=0
    ).astype(bf16)

    def sums(t, carry):
        here = pl.ds(pl.multiple_of(t * LANES, LANES), LANES)
        low = [None] * ORDERS
        for k in range(slots):
            basis = bt_ref[k, :, here]
            for l in range(ORDERS):
                term = basis if l == 0 else basis * row(y_ref[l, k : k + 1, here], 2 * bases)
                low[l] = term if low[l] is None else low[l] + term
        for l in range(ORDERS):
            both = split_rows(low[l]).astype(bf16)
            as_ref[l, 0 : 4 * bases, here] = both
            as_ref[l, 4 * bases : 8 * bases, here] = both
        return carry

    lax.fori_loop(0, n_near // LANES, sums, 0)

    flags_row = jnp.concatenate([blocks[q][3:4, :] for q in range(len(near))], axis=1)
    wide_cols = 2 * LANES

    def first(j, carry):
        here = pl.ds(pl.multiple_of(j * wide_cols, wide_cols), wide_cols)
        inv = [None, None, None]
        for l in range(ORDERS):
            m = dot(rr_cols, as_ref[l, :, here])
            m1_ref[l, :, here] = m
            inv[GROUP[l]] = m * m if inv[GROUP[l]] is None else inv[GROUP[l]] + m * m
        value = dot(mix1_ref[...], jnp.concatenate(inv, axis=0), HIGH)
        act, slope = silu_parts(value)
        sp1_ref[:, here] = slope
        hidden = act + emb0_col + embd_col * q_ref[0:1, here]
        hi, lo = split(hidden)
        hs_ref[0:chan, here] = hi
        hs_ref[chan : 2 * chan, here] = lo
        return carry

    q_ref[0:1, :] = flags_row
    lax.fori_loop(0, n_near // wide_cols, first, 0)

    def gather(k, carry):
        here = pl.ds(pl.multiple_of(k * atoms, atoms), atoms)
        wanted = gidx_ref[pl.ds(k, 1), 0:atoms]
        for r in range(n_near // LANES):
            ids = lax.broadcasted_iota(jnp.int32, (LANES, atoms), 0) + r * LANES
            oh_ref[r * LANES : (r + 1) * LANES, here] = jnp.where(ids == wanted, 1.0, 0.0).astype(bf16)
        both = dot(hs_ref[...], oh_ref[:, here])
        feat = both[:chan] + both[chan:]
        basis = split_rows(bt_ref[k, 0:bases, 0:atoms])
        weight = dot(r2_cols, jnp.concatenate([basis, basis], axis=0).astype(bf16))
        hj_ref[:, here] = feat
        w_ref[:, here] = weight
        car_ref[:, here] = feat * weight
        return carry

    lax.fori_loop(0, slots, gather, 0)

    pairs = chan // 16

    def moments(step, carry):
        t = step // pairs
        c = step % pairs
        cols = pl.ds(pl.multiple_of(t * LANES, LANES), LANES)
        base = pl.multiple_of(c * 16, 16)
        acc = [[None] * ORDERS, [None] * ORDERS]
        for k in range(slots):
            at = pl.ds(pl.multiple_of(k * atoms + t * LANES, LANES), LANES)
            got = car_ref[pl.ds(base, 16), at]
            for l in range(ORDERS):
                yb = yb_ref[l, k, :, cols] if l else None
                for h in range(2):
                    part = got[8 * h : 8 * h + 8]
                    term = part * yb if l else part
                    acc[h][l] = term if acc[h][l] is None else acc[h][l] + term
        inv = [[None] * 3, [None] * 3]
        for l in range(ORDERS):
            m2_ref[l, pl.ds(base, 16), cols] = jnp.concatenate([acc[0][l], acc[1][l]], axis=0)
            for h in range(2):
                sq = acc[h][l] * acc[h][l]
                g = GROUP[l]
                inv[h][g] = sq if inv[h][g] is None else inv[h][g] + sq
        for g in range(3):
            inv_ref[pl.ds(pl.multiple_of(g * chan + c * 16, 16), 16), cols] = jnp.concatenate(
                [inv[0][g], inv[1][g]], axis=0
            )
        return carry

    lax.fori_loop(0, tiles * pairs, moments, 0)

    for t in range(atoms // wide_cols):
        cols = slice(t * wide_cols, (t + 1) * wide_cols)
        value = dot(mix2_ref[...], inv_ref[:, cols], HIGH)
        _, slope = silu_parts(value)
        slope = slope * (2.0 * read2_col)
        for g in range(3):
            mixed = mix2_ref[:, g * chan : (g + 1) * chan].T
            dinv_ref[g * chan : (g + 1) * chan, cols] = dot(mixed, slope, HIGH)

    k_step = slots // 2

    def back_moments(step, carry):
        t = step // 2
        k0 = (step % 2) * k_step
        cols = pl.ds(pl.multiple_of(t * LANES, LANES), LANES)

        def over(c, acc):
            acc = list(acc)
            base = pl.multiple_of(c * 16, 16)
            dm = []
            scale = [dinv_ref[pl.ds(pl.multiple_of(g * chan + c * 16, 16), 16), cols] for g in range(3)]
            for l in range(ORDERS):
                dm.append(m2_ref[l, pl.ds(base, 16), cols] * scale[GROUP[l]])
            for kk in range(k_step):
                k = k0 + kk
                at = pl.ds(pl.multiple_of(k * atoms + t * LANES, LANES), LANES)
                got = car_ref[pl.ds(base, 16), at]
                out = [dm[0][:8], dm[0][8:]]
                for l in range(1, ORDERS):
                    yb = yb_ref[l, k, :, cols]
                    i = kk * (ORDERS - 1) + l - 1
                    for h in range(2):
                        part = dm[l][8 * h : 8 * h + 8]
                        out[h] = out[h] + part * yb
                        acc[i] = acc[i] + part * got[8 * h : 8 * h + 8]
                dcar = jnp.concatenate(out, axis=0)
                for ref, other in ((dhe_ref, w_ref), (dw_ref, hj_ref)):
                    hi, lo = split(dcar * other[pl.ds(base, 16), at])
                    ref[pl.ds(base, 16), at] = hi
                    ref[pl.ds(pl.multiple_of(chan + c * 16, 16), 16), at] = lo
            return tuple(acc)

        start = tuple(jnp.zeros((8, LANES), f32) for _ in range(k_step * (ORDERS - 1)))
        acc = lax.fori_loop(0, pairs, over, start)
        for kk in range(k_step):
            for l in range(1, ORDERS):
                p_ref[l, pl.ds(pl.multiple_of((k0 + kk) * 8, 8), 8), cols] = acc[kk * (ORDERS - 1) + l - 1]
        return carry

    lax.fori_loop(0, tiles * 2, back_moments, 0)

    for k in range(slots):
        here = slice(k * atoms, (k + 1) * atoms)
        both = dot(r2_rows, dw_ref[:, here])
        dbasis = both[:bases] + both[bases:]
        basis = bt_ref[k, 0:bases, 0:atoms]
        reach = 1.0 + lax.broadcasted_iota(jnp.int32, (bases, atoms), 0).astype(f32)
        p_ref[0, k * 8 : k * 8 + 8, :] = dbasis * basis * (reach - row(geo_ref[4, k : k + 1, 0:atoms], bases))

    def back_first(j, carry):
        start = pl.multiple_of(j * wide_cols, wide_cols)
        here = pl.ds(start, wide_cols)
        both = dot_nt(dhe_ref[...], oh_ref[here, :])
        dh = both[:chan] + both[chan:]
        mine = jnp.where(start < atoms, 1.0, 0.0)
        dtop = (dh + read1_col * mine) * sp1_ref[:, here] * 2.0
        scale = []
        for g in range(3):
            scale.append(dot(mix1_ref[:, g * chan : (g + 1) * chan].T, dtop, HIGH))
        for l in range(ORDERS):
            hi, lo = split(m1_ref[l, :, here] * scale[GROUP[l]])
            out = dot(rr_rows, jnp.concatenate([hi, lo], axis=0))
            da_ref[l, :, here] = out[: 2 * bases] + out[2 * bases :]
        return carry

    lax.fori_loop(0, n_near // wide_cols, back_first, 0)

    lane = lax.broadcasted_iota(jnp.int32, (slots, 16 * slots), 1)
    sub = lax.broadcasted_iota(jnp.int32, (slots, 16 * slots), 0)
    adder = jnp.where(((lane >> 3) & (slots - 1)) == sub, 1.0, 0.0).astype(bf16)
    for l in range(ORDERS):
        q_ref[8 * l : 8 * l + 8, 0:atoms] = dot(adder, split_rows(p_ref[l, :, :]).astype(bf16))

    def back_geometry(t, mine):
        here = pl.ds(pl.multiple_of(t * LANES, LANES), LANES)
        ux, uy, uz, back, soft, fj = [geo_ref[i, :, here] for i in range(6)]
        dy = [None] * ORDERS
        ds = None
        for n in range(bases):
            basis = bk_ref[n, :, here]
            db = None
            for l in range(ORDERS):
                g = row(da_ref[l, n : n + 1, here]) + fj * row(da_ref[l, bases + n : bases + n + 1, here])
                if l:
                    dy[l] = g * basis if dy[l] is None else dy[l] + g * basis
                    db = db + g * y_ref[l, :, here]
                else:
                    db = g
            db = db * basis * ((1.0 + n) - soft)
            ds = db if ds is None else ds + db
        if mine:
            ds = ds + q_ref[0:8, here]
            for l in range(1, ORDERS):
                dy[l] = dy[l] + q_ref[8 * l : 8 * l + 8, here]
        dux = SQRT3 * dy[1] + SQRT15 * (uy * dy[4] + uz * dy[7] + ux * dy[8]) - SQRT5 * ux * dy[6]
        duy = SQRT3 * dy[2] + SQRT15 * (ux * dy[4] + uz * dy[5] - uy * dy[8]) - SQRT5 * uy * dy[6]
        duz = SQRT3 * dy[3] + SQRT15 * (uy * dy[5] + ux * dy[7]) + 2.0 * SQRT5 * uz * dy[6]
        along = ds - (ux * dux + uy * duy + uz * duz) * back
        dr = [dux * back + along * ux, duy * back + along * uy, duz * back + along * uz]
        for i in range(3):
            geo_ref[i, :, here] = dr[i]
        return dr

    def mine_tile(t, carry):
        back_geometry(t, True)
        return carry

    def other_tile(t, carry):
        back_geometry(t, False)
        return carry

    lax.fori_loop(0, tiles, mine_tile, 0)
    lax.fori_loop(tiles, n_near // LANES, other_tile, 0)

    def place_tile(t, carry):
        here = pl.ds(pl.multiple_of(t * LANES, LANES), LANES)
        gidx = gidx_ref[:, here]
        chunk_no = gidx >> 7
        place = gidx & 127
        parts = []
        for i in range(3):
            value = geo_ref[i, :, here]
            hi = value.astype(bf16).astype(f32)
            parts.append((hi, value - hi))
        chunk_ids = lax.broadcasted_iota(jnp.int32, (top_rows, LANES), 0)
        place_ids = lax.broadcasted_iota(jnp.int32, (LANES, LANES), 0)
        for k in range(slots):
            at = pl.ds(pl.multiple_of(k * n_near + t * LANES, LANES), LANES)
            hit = chunk_ids == row(chunk_no[k : k + 1, :], top_rows)
            for i in range(3):
                both = [jnp.where(hit, row(part[k : k + 1, :], top_rows), 0.0) for part in parts[i]]
                val_ref[2 * i * top_rows : 2 * (i + 1) * top_rows, at] = jnp.concatenate(both, axis=0).astype(bf16)
            ohlo_ref[:, at] = jnp.where(place_ids == row(place[k : k + 1, :], LANES), 1.0, 0.0).astype(bf16)
        return carry

    lax.fori_loop(0, n_near // LANES, place_tile, 0)
    landed = dot_nt(val_ref[...], ohlo_ref[...])
    lines = push_ref.shape[1] // (n_wide + 1)
    one = push_ref.at[0]
    for i in range(3):
        total = (
            landed[2 * i * top_rows : (2 * i + 1) * top_rows] + landed[(2 * i + 1) * top_rows : (2 * i + 2) * top_rows]
        )
        for g in range(n_wide):
            for t in range(tiles):
                cols = slice(t * LANES, (t + 1) * LANES)
                line = total[g * tiles + t : g * tiles + t + 1, :]
                if g < len(near):
                    here = slice(g * atoms + t * LANES, g * atoms + (t + 1) * LANES)
                    line = line - jnp.sum(geo_ref[i, :, here], axis=0, keepdims=True)
                line = -HALF_STEP * line
                at = i * tiles + t
                if g == 0:
                    line = line + moment_ref[i, :, cols]
                    one[at : at + 1, :] = blocks[0][i : i + 1, cols]
                one[(1 + g) * lines + at : (1 + g) * lines + at + 1, :] = line
                mass = HEAVY - (HEAVY - 1.0) * blocks[g][3:4, cols]
                mass_ref[g * lines + at : g * lines + at + 1, :] = mass
    if lines > 3 * tiles:
        for g in range(n_wide + 1):
            blank = slice(g * lines + 3 * tiles, (g + 1) * lines)
            one[blank, :] = jnp.zeros((lines - 3 * tiles, LANES), f32)
            if g < n_wide:
                mass_ref[blank, :] = jnp.ones((lines - 3 * tiles, LANES), f32)
    whole = push_ref[0]
    for copy in range(1, push_ref.shape[0]):
        push_ref[copy] = whole


def line_count(atoms):
    return -(-3 * (atoms // LANES) // 8) * 8


def ring_plan(domains, atoms):
    near = list(dict.fromkeys(o % domains for o in (0, 1, -1)))
    wide = list(dict.fromkeys(near + [o % domains for o in (2, -2)]))
    before = tuple(wide.index((o - 1) % domains) for o in near)
    after = tuple(wide.index((o + 1) % domains) for o in near)
    return atoms, tuple(near), tuple(wide), before, after


def in_hbm(x):
    return pltpu.with_memory_space_constraint(x, pltpu.HBM)


def pushes(plan, outer, blocks, momenta, embedding, radial_one, radial_two, mix_one, mix_two, read_one, read_two):
    atoms, near, wide, _, _ = plan
    chan = embedding.shape[1]
    bases = radial_one.shape[0]
    slots = blocks[0].shape[0] - HEAD
    n_near = len(near) * atoms
    edges = slots * atoms
    top_rows = -(-len(wide) * atoms // LANES // 8) * 8
    lines = line_count(atoms)
    vmem = pl.BlockSpec(memory_space=pltpu.VMEM)
    far = pl.BlockSpec(memory_space=pltpu.HBM)
    sources = [
        in_hbm(x)
        for x in (momenta, embedding, radial_one, radial_two, mix_one, mix_two, read_one[None], read_two[None])
    ]
    return pl.pallas_call(
        functools.partial(force_kernel, plan),
        out_shape=(
            jax.ShapeDtypeStruct((outer, (len(wide) + 1) * lines, LANES), f32),
            jax.ShapeDtypeStruct((len(wide) * lines, LANES), f32),
        ),
        in_specs=[vmem] * len(wide) + [far] * len(sources),
        out_specs=(vmem, vmem),
        scratch_shapes=[
            pltpu.VMEM((6, slots, n_near), f32),
            pltpu.VMEM((ORDERS, slots, n_near), f32),
            pltpu.VMEM((ORDERS, slots, 8, atoms), f32),
            pltpu.VMEM((bases, slots, n_near), f32),
            pltpu.VMEM((slots, 2 * bases, n_near), f32),
            pltpu.VMEM((slots, n_near), jnp.int32),
            pltpu.VMEM((ORDERS, 8 * bases, n_near), bf16),
            pltpu.VMEM((ORDERS, chan, n_near), f32),
            pltpu.VMEM((chan, n_near), f32),
            pltpu.VMEM((2 * chan, n_near), bf16),
            pltpu.VMEM((n_near, edges), bf16),
            pltpu.VMEM((chan, edges), f32),
            pltpu.VMEM((chan, edges), f32),
            pltpu.VMEM((chan, edges), f32),
            pltpu.VMEM((ORDERS, chan, atoms), f32),
            pltpu.VMEM((3 * chan, atoms), f32),
            pltpu.VMEM((3 * chan, atoms), f32),
            pltpu.VMEM((ORDERS, 8 * slots, atoms), f32),
            pltpu.VMEM((2 * chan, edges), bf16),
            pltpu.VMEM((2 * chan, edges), bf16),
            pltpu.VMEM((ORDERS, 2 * bases, n_near), f32),
            pltpu.VMEM((8 * ORDERS, n_near), f32),
            pltpu.VMEM((6 * top_rows, slots * n_near), bf16),
            pltpu.VMEM((LANES, slots * n_near), bf16),
        ]
        + [pltpu.VMEM(source.shape, f32) for source in sources]
        + [pltpu.SemaphoreType.DMA((len(sources),))],
        compiler_params=pltpu.CompilerParams(vmem_limit_bytes=(26 + 10 * len(near)) * MIB),
        name="forces",
    )(*blocks, *sources)


def mode_turns(bead_total):
    bead = np.arange(bead_total, dtype=np.float64)[:, None]
    mode = np.arange(bead_total, dtype=np.float64)[None, :]
    phase = 2.0 * np.pi * bead * mode / bead_total
    half_total = bead_total // 2
    table = math.sqrt(2.0 / bead_total) * np.where(mode < half_total, np.cos(phase), np.sin(phase))
    table = np.where(mode == half_total, np.cos(np.pi * bead) / math.sqrt(bead_total), table)
    table = np.where(mode == 0, 1.0 / math.sqrt(bead_total), table)
    angles = bead_total * np.sin(np.pi * mode[0] / bead_total)
    safe = np.where(mode[0] == 0, 1.0, angles)
    reach = np.where(mode[0] == 0, STEP, STEP * np.sin(angles) / safe)
    stiff = angles * np.sin(angles) / STEP
    return [[float(x) for x in (table * factor[None, :]) @ table[0]] for factor in (np.cos(angles), reach, stiff)]


def pack_kernel(coord_src, species_src, send_src, slot_src, block_ref, coord_ref, species_ref, send_ref, slot_ref, sems):
    pairs = ((coord_src, coord_ref), (species_src, species_ref), (send_src, send_ref), (slot_src, slot_ref))
    fetches = [pltpu.make_async_copy(src, dst, sems.at[i]) for i, (src, dst) in enumerate(pairs)]
    for fetch in fetches:
        fetch.start()
    for fetch in fetches:
        fetch.wait()
    atoms = block_ref.shape[1]
    for i in range(3):
        block_ref[i : i + 1, :] = coord_ref[i]
    block_ref[3:4, :] = species_ref[...].astype(f32)
    block_ref[4:5, :] = send_ref[...].astype(f32)
    block_ref[5:HEAD, :] = jnp.zeros((HEAD - 5, atoms), f32)
    block_ref[HEAD:, :] = slot_ref[...].astype(f32)


def turn_kernel(shape, bead_ref, mass_ref, source_ref, message_ref):
    outer, inner, domains, wide = shape
    turns = mode_turns(outer * inner)
    lines = mass_ref.shape[0] // len(wide)
    my_domain = bead_ref[1]
    my_outer = bead_ref[0] // inner
    my_inner = bead_ref[0] - my_outer * inner
    if domains > len(wide):
        message_ref[...] = jnp.zeros_like(message_ref)
    masses = [mass_ref[g * lines : (g + 1) * lines, :] for g in range(len(wide))]
    sources = []
    for z in range(outer):
        at = lax.rem(my_outer + outer - z, outer)
        sources.append([source_ref[at, pl.ds(g * lines, lines), :] for g in range(len(wide) + 1)])
    for s in range(inner):
        wraps = jnp.full((lines, LANES), my_inner + s) >= inner
        weights = []
        for turn in turns:
            row_of = []
            for z in range(outer):
                there = turn[(z * inner + s) % (outer * inner)]
                round_it = turn[(z * inner + s - inner) % (outer * inner)]
                row_of.append(jnp.where(wraps, jnp.full((lines, LANES), round_it), jnp.full((lines, LANES), there)))
            weights.append(row_of)
        to_inner = lax.rem(my_inner + s, inner)
        for g in range(len(wide)):
            turned = sum(weights[0][z] * sources[z][1 + g] for z in range(outer))
            drift = sum(weights[1][z] * sources[z][1 + g] for z in range(outer))
            new_q = drift / masses[g]
            new_p = turned
            if g == 0:
                new_q = new_q + sum(weights[0][z] * sources[z][0] for z in range(outer))
                new_p = new_p - masses[g] * sum(weights[2][z] * sources[z][0] for z in range(outer))
            to = to_inner * domains + lax.rem(my_domain + wide[g], domains)
            message_ref[to, 0:lines, :] = new_q
            message_ref[to, lines:, :] = new_p


def sum_kernel(arrived_ref, q_ref, p_ref):
    total = arrived_ref[0]
    for i in range(1, arrived_ref.shape[0]):
        total = total + arrived_ref[i]
    lines = total.shape[0] // 2
    tiles = q_ref.shape[2] // LANES
    for i in range(3):
        for t in range(tiles):
            at = i * tiles + t
            q_ref[i, :, t * LANES : (t + 1) * LANES] = total[at : at + 1]
            p_ref[i, :, t * LANES : (t + 1) * LANES] = total[lines + at : lines + at + 1]


def shards(
    positions, momenta, species, neighbours, send_list, embedding, radial_one, radial_two, mix_one, mix_two,
    read_one, read_two,
):
    slots, atoms = neighbours.shape
    domains = lax.axis_size("space")
    beads = lax.axis_size("bead")
    inner = next(d for d in range(1, beads + 1) if beads % d == 0 and d * d >= beads)
    outer = beads // inner
    plan = ring_plan(domains, atoms)
    wide = plan[2]
    vmem = pl.BlockSpec(memory_space=pltpu.VMEM)
    smem = pl.BlockSpec(memory_space=pltpu.SMEM)
    far = pl.BlockSpec(memory_space=pltpu.HBM)
    small = pltpu.CompilerParams(vmem_limit_bytes=4 * MIB)
    coord_rows = jnp.transpose(positions, (1, 0, 2))
    moment_rows = jnp.transpose(momenta, (1, 0, 2))
    block = pl.pallas_call(
        pack_kernel,
        out_shape=jax.ShapeDtypeStruct((HEAD + slots, atoms), f32),
        in_specs=[far] * 4,
        out_specs=vmem,
        scratch_shapes=[
            pltpu.VMEM(coord_rows.shape, f32),
            pltpu.VMEM((1, atoms), jnp.int32),
            pltpu.VMEM((1, atoms), jnp.int32),
            pltpu.VMEM((slots, atoms), jnp.int32),
            pltpu.SemaphoreType.DMA((4,)),
        ],
        compiler_params=small,
        name="pack",
    )(in_hbm(coord_rows), in_hbm(species[None]), in_hbm(send_list[None]), in_hbm(neighbours))
    blocks = [block]
    for offset in wide[1:]:
        blocks.append(lax.ppermute(block, "space", [(i, (i - offset) % domains) for i in range(domains)]))
    pushed, masses = pushes(
        plan, outer, blocks, moment_rows, embedding, radial_one, radial_two, mix_one, mix_two, read_one, read_two
    )
    columns = [[z * inner + i for z in range(outer)] for i in range(inner)]
    sources = lax.all_to_all(pushed, "bead", 0, 0, axis_index_groups=columns, tiled=True)
    here = jnp.stack([lax.axis_index("bead"), lax.axis_index("space")]).astype(jnp.int32)
    lines = line_count(atoms)
    messages = pl.pallas_call(
        functools.partial(turn_kernel, (outer, inner, domains, wide)),
        out_shape=jax.ShapeDtypeStruct((inner * domains, 2 * lines, LANES), f32),
        in_specs=[smem, vmem, vmem],
        out_specs=vmem,
        compiler_params=small,
        name="turn",
    )(here, masses, sources)
    rows = [[z * inner * domains + i for i in range(inner * domains)] for z in range(outer)]
    arrived = lax.all_to_all(messages, ("bead", "space"), 0, 0, axis_index_groups=rows, tiled=True)
    new_q, new_p = pl.pallas_call(
        sum_kernel,
        out_shape=(jax.ShapeDtypeStruct((3, 1, atoms), f32),) * 2,
        in_specs=[vmem],
        out_specs=(vmem, vmem),
        compiler_params=small,
        name="sum",
    )(arrived)
    return (jnp.transpose(new_q, (1, 0, 2)), jnp.transpose(new_p, (1, 0, 2)))


def solution(mesh):
    placed = (
        P("bead", None, "space"),
        P("bead", None, "space"),
        P("space"),
        P(None, "space"),
        P("space"),
        P(),
        P(),
        P(),
        P(),
        P(),
        P(),
        P(),
    )
    return jax.shard_map(
        shards,
        mesh=mesh,
        in_specs=placed,
        out_specs=(P("bead", None, "space"), P("bead", None, "space")),
        check_vma=False,
    )
```

```python
import functools
import math

import jax
import jax.numpy as jnp
import numpy as np
from jax import lax
from jax.experimental import pallas as pl
from jax.experimental.pallas import tpu as pltpu
from jax.sharding import PartitionSpec as P

STEP = 2.0
HALF_STEP = 1.0
HEAVY = 16.0
SQRT3 = math.sqrt(3.0)
SQRT5 = math.sqrt(5.0)
SQRT15 = math.sqrt(15.0)
LANES = 128
ORDERS = 9
GROUP = (0, 1, 1, 1, 2, 2, 2, 2, 2)
HEAD = 8
MIB = 1024 * 1024
f32 = jnp.float32
bf16 = jnp.bfloat16
HIGH = lax.Precision.HIGH


def split(x):
    hi = x.astype(bf16)
    return hi, (x - hi.astype(f32)).astype(bf16)


def split_rows(x):
    hi = x.astype(bf16).astype(f32)
    return jnp.concatenate([hi, x - hi], axis=0)


def dot(a, b, precision=None):
    return jnp.dot(a, b, preferred_element_type=f32, precision=precision)


def dot_nt(a, b):
    return lax.dot_general(a, b, (((1,), (1,)), ((), ())), preferred_element_type=f32)


def row(x, rows=8):
    return jnp.broadcast_to(x, (rows, x.shape[1]))


def lookup(chunks, wanted, position):
    out = None
    for number, chunk in chunks:
        got = jnp.take_along_axis(row(chunk), position, axis=1, mode="promise_in_bounds")
        out = got if out is None else jnp.where(wanted == number, got, out)
    return out


def harmonics(ux, uy, uz):
    return [
        None,
        SQRT3 * ux,
        SQRT3 * uy,
        SQRT3 * uz,
        SQRT15 * ux * uy,
        SQRT15 * uy * uz,
        0.5 * SQRT5 * (2.0 * uz * uz - ux * ux - uy * uy),
        SQRT15 * ux * uz,
        0.5 * SQRT15 * (ux * ux - uy * uy),
    ]


def silu_parts(v):
    gate = 1.0 / (1.0 + jnp.exp(-v))
    return v * gate, gate * (1.0 + v * (1.0 - gate))


def force_kernel(plan, *refs):
    atoms, near, wide, before, after = plan
    n_wide = len(wide)
    blocks = refs[:n_wide]
    sources = refs[n_wide : n_wide + 8]
    push_ref, mass_ref = refs[n_wide + 8 : n_wide + 10]
    (
        geo_ref, y_ref, yb_ref, bk_ref, bt_ref, gidx_ref, as_ref, m1_ref, sp1_ref, hs_ref, oh_ref,
        hj_ref, w_ref, car_ref, m2_ref, inv_ref, dinv_ref, p_ref, dhe_ref, dw_ref, da_ref, q_ref,
        val_ref, ohlo_ref, moment_ref, emb_ref, rad1_ref, rad2_ref, mix1_ref, mix2_ref, read1_ref, read2_ref, sems,
    ) = refs[n_wide + 10 :]
    held = (moment_ref, emb_ref, rad1_ref, rad2_ref, mix1_ref, mix2_ref, read1_ref, read2_ref)
    fetches = [pltpu.make_async_copy(src, dst, sems.at[i]) for i, (src, dst) in enumerate(zip(sources, held))]
    for fetch in fetches:
        fetch.start()
    chan = emb_ref.shape[1]
    bases = rad1_ref.shape[0]
    slots = gidx_ref.shape[0]
    n_near = len(near) * atoms
    tiles = atoms // LANES
    half = atoms // 2
    half_tiles = half // LANES
    edges = slots * atoms
    top_rows = val_ref.shape[0] // 6

    order_col = lax.broadcasted_iota(jnp.int32, (bases, LANES), 0).astype(f32)
    tables = []
    for quantity in range(4):
        chunks = []
        for g in range(n_wide):
            for t in range(tiles):
                chunks.append((g * tiles + t, blocks[g][quantity : quantity + 1, t * LANES : (t + 1) * LANES]))
        tables.append(chunks)
    for q in range(len(near)):
        ghosts = []
        for t in range(half_tiles):
            ghosts.append(
                (t, blocks[before[q]][4:5, half + t * LANES : half + (t + 1) * LANES] + float(before[q] * atoms))
            )
        for t in range(half_tiles):
            ghosts.append(
                (
                    half_tiles + tiles + t,
                    blocks[after[q]][4:5, t * LANES : (t + 1) * LANES] + float(after[q] * atoms),
                )
            )
        for t in range(tiles):
            cols = slice(t * LANES, (t + 1) * LANES)
            here = slice(q * atoms + t * LANES, q * atoms + (t + 1) * LANES)
            slot = blocks[q][HEAD : HEAD + slots, cols].astype(jnp.int32)
            chunk_no = slot >> 7
            far = lookup(ghosts, chunk_no, slot & 127).astype(jnp.int32)
            own = (slot >= half) & (slot < half + atoms)
            gidx = jnp.where(own, slot + (q * atoms - half), far)
            gidx_ref[:, here] = gidx
            chunk_no = gidx >> 7
            place = gidx & 127
            xj, yj, zj, fj = [lookup(tables[i], chunk_no, place) for i in range(4)]
            rx = xj - row(blocks[q][0:1, cols])
            ry = yj - row(blocks[q][1:2, cols])
            rz = zj - row(blocks[q][2:3, cols])
            soft = jnp.sqrt(rx * rx + ry * ry + rz * rz + 1.0)
            back = 1.0 / soft
            ux, uy, uz = rx * back, ry * back, rz * back
            for i, value in enumerate((ux, uy, uz, back, soft, fj)):
                geo_ref[i, :, here] = value
            sphere = harmonics(ux, uy, uz)
            for l in range(1, ORDERS):
                y_ref[l, :, here] = sphere[l]
                if q == 0:
                    for k in range(slots):
                        yb_ref[l, k, :, cols] = row(sphere[l][k : k + 1, :])
            for n in range(bases):
                bk_ref[n, :, here] = jnp.exp(-0.5 * (soft - (1.0 + n)) ** 2)
            for k in range(slots):
                basis = jnp.exp(-0.5 * (row(soft[k : k + 1, :], bases) - (1.0 + order_col)) ** 2)
                bt_ref[k, 0:bases, here] = basis
                bt_ref[k, bases : 2 * bases, here] = basis * row(fj[k : k + 1, :], bases)

    for fetch in fetches:
        fetch.wait()
    emb0 = emb_ref[0:1, :]
    emb_d = emb_ref[1:2, :] - emb0
    rr = jnp.concatenate([rad1_ref[...] * emb0, rad1_ref[...] * emb_d], axis=0) * (1.0 / slots)
    rr_hi = rr.astype(bf16).astype(f32)
    rr_lo = rr - rr_hi
    r2 = rad2_ref[...] * (1.0 / slots)
    r2_hi = r2.astype(bf16).astype(f32)
    r2_lo = r2 - r2_hi
    zeros = jnp.zeros((8, chan), f32)
    turned1 = jnp.concatenate([rr_hi, rr_hi, rr_lo, rr_lo] + [zeros] * 8, axis=0).T
    sides = jnp.concatenate([emb0, emb_d, read1_ref[...], read2_ref[...], zeros[:4]], axis=0)
    turned2 = jnp.concatenate([r2_hi, r2_hi, r2_lo, r2_lo, sides] + [zeros] * 11, axis=0).T
    rr_cols = turned1[:, : 8 * bases].astype(bf16)
    r2_cols = turned2[:, : 4 * bases].astype(bf16)
    emb0_col = turned2[:, 4 * bases : 4 * bases + 1]
    embd_col = turned2[:, 4 * bases + 1 : 4 * bases + 2]
    read1_col = turned2[:, 4 * bases + 2 : 4 * bases + 3]
    read2_col = turned2[:, 4 * bases + 3 : 4 * bases + 4]
    rr_rows = jnp.concatenate(
        [jnp.concatenate([rr_hi, rr_hi], axis=1), jnp.concatenate([rr_lo, jnp.zeros_like(rr_lo)], axis=1)], axis=0
    ).astype(bf16)
    r2_rows = jnp.concatenate(
        [jnp.concatenate([r2_hi, r2_hi], axis=1), jnp.concatenate([r2_lo, jnp.zeros_like(r2_lo)], axis=1)], axis=0
    ).astype(bf16)

    def sums(t, carry):
        here = pl.ds(pl.multiple_of(t * LANES, LANES), LANES)
        low = [None] * ORDERS
        for k in range(slots):
            basis = bt_ref[k, :, here]
            for l in range(ORDERS):
                term = basis if l == 0 else basis * row(y_ref[l, k : k + 1, here], 2 * bases)
                low[l] = term if low[l] is None else low[l] + term
        for l in range(ORDERS):
            both = split_rows(low[l]).astype(bf16)
            as_ref[l, 0 : 4 * bases, here] = both
            as_ref[l, 4 * bases : 8 * bases, here] = both
        return carry

    lax.fori_loop(0, n_near // LANES, sums, 0)

    flags_row = jnp.concatenate([blocks[q][3:4, :] for q in range(len(near))], axis=1)
    wide_cols = 2 * LANES
    ids16 = lax.broadcasted_iota(jnp.int32, (LANES, atoms), 0).astype(jnp.int16)
    one16 = jnp.ones((LANES, atoms), bf16)
    zero16 = jnp.zeros((LANES, atoms), bf16)

    def row16(x, rows):
        return jnp.broadcast_to(x, (rows, x.shape[1])).astype(jnp.int16)

    blocks_of_rows = n_near // LANES
    builds = slots * blocks_of_rows // (n_near // wide_cols)

    def build(i):
        k = i // blocks_of_rows
        r = i % blocks_of_rows
        wanted = gidx_ref[pl.ds(k, 1), 0:atoms] - r * LANES
        hit = row16(wanted, LANES) == ids16
        at = pl.ds(pl.multiple_of(r * LANES, LANES), LANES)
        oh_ref[at, pl.ds(pl.multiple_of(k * atoms, LANES), atoms)] = jnp.where(hit, one16, zero16)

    def first(j, carry):
        here = pl.ds(pl.multiple_of(j * wide_cols, wide_cols), wide_cols)
        for i in range(builds):
            build(j * builds + i)
        inv = [None, None, None]
        for l in range(ORDERS):
            m = dot(rr_cols, as_ref[l, :, here])
            m1_ref[l, :, here] = m
            inv[GROUP[l]] = m * m if inv[GROUP[l]] is None else inv[GROUP[l]] + m * m
        value = dot(mix1_ref[...], jnp.concatenate(inv, axis=0), HIGH)
        act, slope = silu_parts(value)
        sp1_ref[:, here] = slope
        hidden = act + emb0_col + embd_col * q_ref[0:1, here]
        hi, lo = split(hidden)
        hs_ref[0:chan, here] = hi
        hs_ref[chan : 2 * chan, here] = lo
        return carry

    q_ref[0:1, :] = flags_row
    lax.fori_loop(0, n_near // wide_cols, first, 0)

    def gather(k, carry):
        here = pl.ds(pl.multiple_of(k * atoms, atoms), atoms)
        both = dot(hs_ref[...], oh_ref[:, here])
        feat = both[:chan] + both[chan:]
        basis = split_rows(bt_ref[k, 0:bases, 0:atoms])
        weight = dot(r2_cols, jnp.concatenate([basis, basis], axis=0).astype(bf16))
        hj_ref[:, here] = feat
        w_ref[:, here] = weight
        car_ref[:, here] = feat * weight
        return carry

    lax.fori_loop(0, slots, gather, 0)

    pairs = chan // 16

    def moments(step, carry):
        t = step // pairs
        c = step % pairs
        cols = pl.ds(pl.multiple_of(t * LANES, LANES), LANES)
        base = pl.multiple_of(c * 16, 16)
        acc = [[None] * ORDERS, [None] * ORDERS]
        for k in range(slots):
            at = pl.ds(pl.multiple_of(k * atoms + t * LANES, LANES), LANES)
            got = car_ref[pl.ds(base, 16), at]
            for l in range(ORDERS):
                yb = yb_ref[l, k, :, cols] if l else None
                for h in range(2):
                    part = got[8 * h : 8 * h + 8]
                    term = part * yb if l else part
                    acc[h][l] = term if acc[h][l] is None else acc[h][l] + term
        inv = [[None] * 3, [None] * 3]
        for l in range(ORDERS):
            m2_ref[l, pl.ds(base, 16), cols] = jnp.concatenate([acc[0][l], acc[1][l]], axis=0)
            for h in range(2):
                sq = acc[h][l] * acc[h][l]
                g = GROUP[l]
                inv[h][g] = sq if inv[h][g] is None else inv[h][g] + sq
        for g in range(3):
            inv_ref[pl.ds(pl.multiple_of(g * chan + c * 16, 16), 16), cols] = jnp.concatenate(
                [inv[0][g], inv[1][g]], axis=0
            )
        return carry

    lax.fori_loop(0, tiles * pairs, moments, 0)

    mix2_turned = [mix2_ref[:, g * chan : (g + 1) * chan].T for g in range(3)]
    for t in range(atoms // wide_cols):
        cols = slice(t * wide_cols, (t + 1) * wide_cols)
        value = dot(mix2_ref[...], inv_ref[:, cols], HIGH)
        _, slope = silu_parts(value)
        slope = slope * (2.0 * read2_col)
        for g in range(3):
            dinv_ref[g * chan : (g + 1) * chan, cols] = dot(mix2_turned[g], slope, HIGH)

    k_step = slots // 2

    def back_moments(step, carry):
        t = step // 2
        k0 = (step % 2) * k_step
        cols = pl.ds(pl.multiple_of(t * LANES, LANES), LANES)

        def over(c, acc):
            acc = list(acc)
            base = pl.multiple_of(c * 16, 16)
            dm = []
            scale = [dinv_ref[pl.ds(pl.multiple_of(g * chan + c * 16, 16), 16), cols] for g in range(3)]
            for l in range(ORDERS):
                dm.append(m2_ref[l, pl.ds(base, 16), cols] * scale[GROUP[l]])
            for kk in range(k_step):
                k = k0 + kk
                at = pl.ds(pl.multiple_of(k * atoms + t * LANES, LANES), LANES)
                got = car_ref[pl.ds(base, 16), at]
                out = [dm[0][:8], dm[0][8:]]
                for l in range(1, ORDERS):
                    yb = yb_ref[l, k, :, cols]
                    i = kk * (ORDERS - 1) + l - 1
                    for h in range(2):
                        part = dm[l][8 * h : 8 * h + 8]
                        out[h] = out[h] + part * yb
                        acc[i] = acc[i] + part * got[8 * h : 8 * h + 8]
                dcar = jnp.concatenate(out, axis=0)
                for ref, other in ((dhe_ref, w_ref), (dw_ref, hj_ref)):
                    hi, lo = split(dcar * other[pl.ds(base, 16), at])
                    ref[pl.ds(base, 16), at] = hi
                    ref[pl.ds(pl.multiple_of(chan + c * 16, 16), 16), at] = lo
            return tuple(acc)

        start = tuple(jnp.zeros((8, LANES), f32) for _ in range(k_step * (ORDERS - 1)))
        acc = lax.fori_loop(0, pairs, over, start)
        for kk in range(k_step):
            for l in range(1, ORDERS):
                p_ref[l, pl.ds(pl.multiple_of((k0 + kk) * 8, 8), 8), cols] = acc[kk * (ORDERS - 1) + l - 1]
        return carry

    lax.fori_loop(0, tiles * 2, back_moments, 0)

    for k in range(slots):
        here = slice(k * atoms, (k + 1) * atoms)
        both = dot(r2_rows, dw_ref[:, here])
        dbasis = both[:bases] + both[bases:]
        basis = bt_ref[k, 0:bases, 0:atoms]
        reach = 1.0 + lax.broadcasted_iota(jnp.int32, (bases, atoms), 0).astype(f32)
        p_ref[0, k * 8 : k * 8 + 8, :] = dbasis * basis * (reach - row(geo_ref[4, k : k + 1, 0:atoms], bases))

    mix1_turned = [mix1_ref[:, g * chan : (g + 1) * chan].T for g in range(3)]

    def back_first(j, carry):
        start = pl.multiple_of(j * wide_cols, wide_cols)
        here = pl.ds(start, wide_cols)
        both = dot_nt(oh_ref[here, :], dhe_ref[...])
        dh = (both[:, :chan] + both[:, chan:]).T
        mine = jnp.where(start < atoms, 1.0, 0.0)
        dtop = (dh + read1_col * mine) * sp1_ref[:, here] * 2.0
        scale = []
        for g in range(3):
            scale.append(dot(mix1_turned[g], dtop, HIGH))
        for l in range(ORDERS):
            hi, lo = split(m1_ref[l, :, here] * scale[GROUP[l]])
            out = dot(rr_rows, jnp.concatenate([hi, lo], axis=0))
            da_ref[l, :, here] = out[: 2 * bases] + out[2 * bases :]
        return carry

    lax.fori_loop(0, n_near // wide_cols, back_first, 0)

    lane = lax.broadcasted_iota(jnp.int32, (slots, 16 * slots), 1)
    sub = lax.broadcasted_iota(jnp.int32, (slots, 16 * slots), 0)
    adder = jnp.where(((lane >> 3) & (slots - 1)) == sub, 1.0, 0.0).astype(bf16)
    for l in range(ORDERS):
        q_ref[8 * l : 8 * l + 8, 0:atoms] = dot(adder, split_rows(p_ref[l, :, :]).astype(bf16))

    def back_geometry(t, mine):
        here = pl.ds(pl.multiple_of(t * LANES, LANES), LANES)
        ux, uy, uz, back, soft, fj = [geo_ref[i, :, here] for i in range(6)]
        dy = [None] * ORDERS
        ds = None
        for n in range(bases):
            basis = bk_ref[n, :, here]
            db = None
            for l in range(ORDERS):
                g = row(da_ref[l, n : n + 1, here]) + fj * row(da_ref[l, bases + n : bases + n + 1, here])
                if l:
                    dy[l] = g * basis if dy[l] is None else dy[l] + g * basis
                    db = db + g * y_ref[l, :, here]
                else:
                    db = g
            db = db * basis * ((1.0 + n) - soft)
            ds = db if ds is None else ds + db
        if mine:
            ds = ds + q_ref[0:8, here]
            for l in range(1, ORDERS):
                dy[l] = dy[l] + q_ref[8 * l : 8 * l + 8, here]
        dux = SQRT3 * dy[1] + SQRT15 * (uy * dy[4] + uz * dy[7] + ux * dy[8]) - SQRT5 * ux * dy[6]
        duy = SQRT3 * dy[2] + SQRT15 * (ux * dy[4] + uz * dy[5] - uy * dy[8]) - SQRT5 * uy * dy[6]
        duz = SQRT3 * dy[3] + SQRT15 * (uy * dy[5] + ux * dy[7]) + 2.0 * SQRT5 * uz * dy[6]
        along = ds - (ux * dux + uy * duy + uz * duz) * back
        dr = [dux * back + along * ux, duy * back + along * uy, duz * back + along * uz]
        for i in range(3):
            geo_ref[i, :, here] = dr[i]
        return dr

    def mine_tile(t, carry):
        back_geometry(t, True)
        return carry

    def other_tile(t, carry):
        back_geometry(t, False)
        return carry

    lax.fori_loop(0, tiles, mine_tile, 0)
    lax.fori_loop(tiles, n_near // LANES, other_tile, 0)

    def place_tile(t, carry):
        here = pl.ds(pl.multiple_of(t * LANES, LANES), LANES)
        gidx = gidx_ref[:, here]
        chunk_no = gidx >> 7
        place = gidx & 127
        parts = []
        for i in range(3):
            value = geo_ref[i, :, here]
            hi = value.astype(bf16).astype(f32)
            parts.append((hi, value - hi))
        chunk_ids = lax.broadcasted_iota(jnp.int32, (top_rows, LANES), 0)
        place_ids = lax.broadcasted_iota(jnp.int32, (LANES, LANES), 0)
        for k in range(slots):
            at = pl.ds(pl.multiple_of(k * n_near + t * LANES, LANES), LANES)
            hit = chunk_ids == row(chunk_no[k : k + 1, :], top_rows)
            for i in range(3):
                both = [jnp.where(hit, row(part[k : k + 1, :], top_rows), 0.0) for part in parts[i]]
                val_ref[2 * i * top_rows : 2 * (i + 1) * top_rows, at] = jnp.concatenate(both, axis=0).astype(bf16)
            ohlo_ref[:, at] = jnp.where(place_ids == row(place[k : k + 1, :], LANES), 1.0, 0.0).astype(bf16)
        return carry

    lax.fori_loop(0, n_near // LANES, place_tile, 0)
    landed = dot_nt(ohlo_ref[...], val_ref[...]).T
    lines = push_ref.shape[1] // (n_wide + 1)
    one = push_ref.at[0]
    for i in range(3):
        total = (
            landed[2 * i * top_rows : (2 * i + 1) * top_rows] + landed[(2 * i + 1) * top_rows : (2 * i + 2) * top_rows]
        )
        for g in range(n_wide):
            for t in range(tiles):
                cols = slice(t * LANES, (t + 1) * LANES)
                line = total[g * tiles + t : g * tiles + t + 1, :]
                if g < len(near):
                    here = slice(g * atoms + t * LANES, g * atoms + (t + 1) * LANES)
                    line = line - jnp.sum(geo_ref[i, :, here], axis=0, keepdims=True)
                line = -HALF_STEP * line
                at = i * tiles + t
                if g == 0:
                    line = line + moment_ref[i, :, cols]
                    one[at : at + 1, :] = blocks[0][i : i + 1, cols]
                one[(1 + g) * lines + at : (1 + g) * lines + at + 1, :] = line
                mass = HEAVY - (HEAVY - 1.0) * blocks[g][3:4, cols]
                mass_ref[g * lines + at : g * lines + at + 1, :] = mass
    if lines > 3 * tiles:
        for g in range(n_wide + 1):
            blank = slice(g * lines + 3 * tiles, (g + 1) * lines)
            one[blank, :] = jnp.zeros((lines - 3 * tiles, LANES), f32)
            if g < n_wide:
                mass_ref[blank, :] = jnp.ones((lines - 3 * tiles, LANES), f32)
    whole = push_ref[0]
    for copy in range(1, push_ref.shape[0]):
        push_ref[copy] = whole


def line_count(atoms):
    return -(-3 * (atoms // LANES) // 8) * 8


def ring_plan(domains, atoms):
    near = list(dict.fromkeys(o % domains for o in (0, 1, -1)))
    wide = list(dict.fromkeys(near + [o % domains for o in (2, -2)]))
    before = tuple(wide.index((o - 1) % domains) for o in near)
    after = tuple(wide.index((o + 1) % domains) for o in near)
    return atoms, tuple(near), tuple(wide), before, after


def in_hbm(x):
    return pltpu.with_memory_space_constraint(x, pltpu.HBM)


def pushes(plan, outer, blocks, momenta, embedding, radial_one, radial_two, mix_one, mix_two, read_one, read_two):
    atoms, near, wide, _, _ = plan
    chan = embedding.shape[1]
    bases = radial_one.shape[0]
    slots = blocks[0].shape[0] - HEAD
    n_near = len(near) * atoms
    edges = slots * atoms
    top_rows = -(-len(wide) * atoms // LANES // 8) * 8
    lines = line_count(atoms)
    vmem = pl.BlockSpec(memory_space=pltpu.VMEM)
    far = pl.BlockSpec(memory_space=pltpu.HBM)
    sources = [
        in_hbm(x)
        for x in (momenta, embedding, radial_one, radial_two, mix_one, mix_two, read_one[None], read_two[None])
    ]
    return pl.pallas_call(
        functools.partial(force_kernel, plan),
        out_shape=(
            jax.ShapeDtypeStruct((outer, (len(wide) + 1) * lines, LANES), f32),
            jax.ShapeDtypeStruct((len(wide) * lines, LANES), f32),
        ),
        in_specs=[vmem] * len(wide) + [far] * len(sources),
        out_specs=(vmem, vmem),
        scratch_shapes=[
            pltpu.VMEM((6, slots, n_near), f32),
            pltpu.VMEM((ORDERS, slots, n_near), f32),
            pltpu.VMEM((ORDERS, slots, 8, atoms), f32),
            pltpu.VMEM((bases, slots, n_near), f32),
            pltpu.VMEM((slots, 2 * bases, n_near), f32),
            pltpu.VMEM((slots, n_near), jnp.int32),
            pltpu.VMEM((ORDERS, 8 * bases, n_near), bf16),
            pltpu.VMEM((ORDERS, chan, n_near), f32),
            pltpu.VMEM((chan, n_near), f32),
            pltpu.VMEM((2 * chan, n_near), bf16),
            pltpu.VMEM((n_near, edges), bf16),
            pltpu.VMEM((chan, edges), f32),
            pltpu.VMEM((chan, edges), f32),
            pltpu.VMEM((chan, edges), f32),
            pltpu.VMEM((ORDERS, chan, atoms), f32),
            pltpu.VMEM((3 * chan, atoms), f32),
            pltpu.VMEM((3 * chan, atoms), f32),
            pltpu.VMEM((ORDERS, 8 * slots, atoms), f32),
            pltpu.VMEM((2 * chan, edges), bf16),
            pltpu.VMEM((2 * chan, edges), bf16),
            pltpu.VMEM((ORDERS, 2 * bases, n_near), f32),
            pltpu.VMEM((8 * ORDERS, n_near), f32),
            pltpu.VMEM((6 * top_rows, slots * n_near), bf16),
            pltpu.VMEM((LANES, slots * n_near), bf16),
        ]
        + [pltpu.VMEM(source.shape, f32) for source in sources]
        + [pltpu.SemaphoreType.DMA((len(sources),))],
        compiler_params=pltpu.CompilerParams(vmem_limit_bytes=(26 + 10 * len(near)) * MIB),
        name="forces",
    )(*blocks, *sources)


def mode_turns(bead_total):
    bead = np.arange(bead_total, dtype=np.float64)[:, None]
    mode = np.arange(bead_total, dtype=np.float64)[None, :]
    phase = 2.0 * np.pi * bead * mode / bead_total
    half_total = bead_total // 2
    table = math.sqrt(2.0 / bead_total) * np.where(mode < half_total, np.cos(phase), np.sin(phase))
    table = np.where(mode == half_total, np.cos(np.pi * bead) / math.sqrt(bead_total), table)
    table = np.where(mode == 0, 1.0 / math.sqrt(bead_total), table)
    angles = bead_total * np.sin(np.pi * mode[0] / bead_total)
    safe = np.where(mode[0] == 0, 1.0, angles)
    reach = np.where(mode[0] == 0, STEP, STEP * np.sin(angles) / safe)
    stiff = angles * np.sin(angles) / STEP
    return [[float(x) for x in (table * factor[None, :]) @ table[0]] for factor in (np.cos(angles), reach, stiff)]


def pack_kernel(coord_src, species_src, send_src, slot_src, block_ref, coord_ref, species_ref, send_ref, slot_ref, sems):
    pairs = ((coord_src, coord_ref), (species_src, species_ref), (send_src, send_ref), (slot_src, slot_ref))
    fetches = [pltpu.make_async_copy(src, dst, sems.at[i]) for i, (src, dst) in enumerate(pairs)]
    for fetch in fetches:
        fetch.start()
    for fetch in fetches:
        fetch.wait()
    atoms = block_ref.shape[1]
    for i in range(3):
        block_ref[i : i + 1, :] = coord_ref[i]
    block_ref[3:4, :] = species_ref[...].astype(f32)
    block_ref[4:5, :] = send_ref[...].astype(f32)
    block_ref[5:HEAD, :] = jnp.zeros((HEAD - 5, atoms), f32)
    block_ref[HEAD:, :] = slot_ref[...].astype(f32)


def turn_kernel(shape, bead_ref, mass_ref, source_ref, message_ref):
    outer, inner, domains, wide = shape
    turns = mode_turns(outer * inner)
    lines = mass_ref.shape[0] // len(wide)
    my_domain = bead_ref[1]
    my_outer = bead_ref[0] // inner
    my_inner = bead_ref[0] - my_outer * inner
    if domains > len(wide):
        message_ref[...] = jnp.zeros_like(message_ref)
    masses = [mass_ref[g * lines : (g + 1) * lines, :] for g in range(len(wide))]
    sources = []
    for z in range(outer):
        at = lax.rem(my_outer + outer - z, outer)
        sources.append([source_ref[at, pl.ds(g * lines, lines), :] for g in range(len(wide) + 1)])
    for s in range(inner):
        wraps = jnp.full((lines, LANES), my_inner + s) >= inner
        weights = []
        for turn in turns:
            row_of = []
            for z in range(outer):
                there = turn[(z * inner + s) % (outer * inner)]
                round_it = turn[(z * inner + s - inner) % (outer * inner)]
                row_of.append(jnp.where(wraps, jnp.full((lines, LANES), round_it), jnp.full((lines, LANES), there)))
            weights.append(row_of)
        to_inner = lax.rem(my_inner + s, inner)
        for g in range(len(wide)):
            turned = sum(weights[0][z] * sources[z][1 + g] for z in range(outer))
            drift = sum(weights[1][z] * sources[z][1 + g] for z in range(outer))
            new_q = drift / masses[g]
            new_p = turned
            if g == 0:
                new_q = new_q + sum(weights[0][z] * sources[z][0] for z in range(outer))
                new_p = new_p - masses[g] * sum(weights[2][z] * sources[z][0] for z in range(outer))
            to = to_inner * domains + lax.rem(my_domain + wide[g], domains)
            message_ref[to, 0:lines, :] = new_q
            message_ref[to, lines:, :] = new_p


def sum_kernel(arrived_ref, q_ref, p_ref):
    total = arrived_ref[0]
    for i in range(1, arrived_ref.shape[0]):
        total = total + arrived_ref[i]
    lines = total.shape[0] // 2
    tiles = q_ref.shape[2] // LANES
    for i in range(3):
        for t in range(tiles):
            at = i * tiles + t
            q_ref[i, :, t * LANES : (t + 1) * LANES] = total[at : at + 1]
            p_ref[i, :, t * LANES : (t + 1) * LANES] = total[lines + at : lines + at + 1]


def shards(
    positions, momenta, species, neighbours, send_list, embedding, radial_one, radial_two, mix_one, mix_two,
    read_one, read_two,
):
    slots, atoms = neighbours.shape
    domains = lax.axis_size("space")
    beads = lax.axis_size("bead")
    inner = next(d for d in range(1, beads + 1) if beads % d == 0 and d * d >= beads)
    outer = beads // inner
    plan = ring_plan(domains, atoms)
    wide = plan[2]
    vmem = pl.BlockSpec(memory_space=pltpu.VMEM)
    smem = pl.BlockSpec(memory_space=pltpu.SMEM)
    far = pl.BlockSpec(memory_space=pltpu.HBM)
    small = pltpu.CompilerParams(vmem_limit_bytes=4 * MIB)
    coord_rows = jnp.transpose(positions, (1, 0, 2))
    moment_rows = jnp.transpose(momenta, (1, 0, 2))
    block = pl.pallas_call(
        pack_kernel,
        out_shape=jax.ShapeDtypeStruct((HEAD + slots, atoms), f32),
        in_specs=[far] * 4,
        out_specs=vmem,
        scratch_shapes=[
            pltpu.VMEM(coord_rows.shape, f32),
            pltpu.VMEM((1, atoms), jnp.int32),
            pltpu.VMEM((1, atoms), jnp.int32),
            pltpu.VMEM((slots, atoms), jnp.int32),
            pltpu.SemaphoreType.DMA((4,)),
        ],
        compiler_params=small,
        name="pack",
    )(in_hbm(coord_rows), in_hbm(species[None]), in_hbm(send_list[None]), in_hbm(neighbours))
    blocks = [block]
    for offset in wide[1:]:
        blocks.append(lax.ppermute(block, "space", [(i, (i - offset) % domains) for i in range(domains)]))
    pushed, masses = pushes(
        plan, outer, blocks, moment_rows, embedding, radial_one, radial_two, mix_one, mix_two, read_one, read_two
    )
    columns = [[z * inner + i for z in range(outer)] for i in range(inner)]
    sources = lax.all_to_all(pushed, "bead", 0, 0, axis_index_groups=columns, tiled=True)
    here = jnp.stack([lax.axis_index("bead"), lax.axis_index("space")]).astype(jnp.int32)
    lines = line_count(atoms)
    messages = pl.pallas_call(
        functools.partial(turn_kernel, (outer, inner, domains, wide)),
        out_shape=jax.ShapeDtypeStruct((inner * domains, 2 * lines, LANES), f32),
        in_specs=[smem, vmem, vmem],
        out_specs=vmem,
        compiler_params=small,
        name="turn",
    )(here, masses, sources)
    rows = [[z * inner * domains + i for i in range(inner * domains)] for z in range(outer)]
    arrived = lax.all_to_all(messages, ("bead", "space"), 0, 0, axis_index_groups=rows, tiled=True)
    new_q, new_p = pl.pallas_call(
        sum_kernel,
        out_shape=(jax.ShapeDtypeStruct((3, 1, atoms), f32),) * 2,
        in_specs=[vmem],
        out_specs=(vmem, vmem),
        compiler_params=small,
        name="sum",
    )(arrived)
    return (jnp.transpose(new_q, (1, 0, 2)), jnp.transpose(new_p, (1, 0, 2)))


def solution(mesh):
    placed = (
        P("bead", None, "space"),
        P("bead", None, "space"),
        P("space"),
        P(None, "space"),
        P("space"),
        P(),
        P(),
        P(),
        P(),
        P(),
        P(),
        P(),
    )
    return jax.shard_map(
        shards,
        mesh=mesh,
        in_specs=placed,
        out_specs=(P("bead", None, "space"), P("bead", None, "space")),
        check_vma=False,
    )
```

```python
import functools
import math

import jax
import jax.numpy as jnp
import numpy as np
from jax import lax
from jax.experimental import pallas as pl
from jax.experimental.pallas import tpu as pltpu
from jax.sharding import PartitionSpec as P

STEP = 2.0
HALF_STEP = 1.0
HEAVY = 16.0
SQRT3 = math.sqrt(3.0)
SQRT5 = math.sqrt(5.0)
SQRT15 = math.sqrt(15.0)
LANES = 128
ORDERS = 9
GROUP = (0, 1, 1, 1, 2, 2, 2, 2, 2)
HEAD = 8
MIB = 1024 * 1024
f32 = jnp.float32
bf16 = jnp.bfloat16


def split(x):
    hi = x.astype(bf16)
    return hi, (x - hi.astype(f32)).astype(bf16)


def split_rows(x):
    hi = x.astype(bf16).astype(f32)
    return jnp.concatenate([hi, x - hi], axis=0)


def dot(a, b):
    return jnp.dot(a, b, preferred_element_type=f32)


def dot_nt(a, b):
    return lax.dot_general(a, b, (((1,), (1,)), ((), ())), preferred_element_type=f32)


def row(x, rows=8):
    return jnp.broadcast_to(x, (rows, x.shape[1]))


def lookup(chunks, wanted, position):
    out = None
    for number, chunk in chunks:
        got = jnp.take_along_axis(row(chunk), position, axis=1, mode="promise_in_bounds")
        out = got if out is None else jnp.where(wanted == number, got, out)
    return out


def harmonics(ux, uy, uz):
    return [
        None,
        SQRT3 * ux,
        SQRT3 * uy,
        SQRT3 * uz,
        SQRT15 * ux * uy,
        SQRT15 * uy * uz,
        0.5 * SQRT5 * (2.0 * uz * uz - ux * ux - uy * uy),
        SQRT15 * ux * uz,
        0.5 * SQRT15 * (ux * ux - uy * uy),
    ]


def silu_parts(v):
    gate = 1.0 / (1.0 + jnp.exp(-v))
    return v * gate, gate * (1.0 + v * (1.0 - gate))


def choose_kernel(block_ref, *refs):
    sources = refs[:7]
    oh_ref, rrc_ref, r2c_ref, side_ref, rrr_ref, r2r_ref, mixa_ref, mixt_ref = refs[7:15]
    held = refs[15:22]
    sems = refs[22]
    emb_ref, rad1_ref, rad2_ref, mix1_ref, mix2_ref, read1_ref, read2_ref = held
    fetches = [pltpu.make_async_copy(src, dst, sems.at[i]) for i, (src, dst) in enumerate(zip(sources, held))]
    for fetch in fetches:
        fetch.start()
    chan = emb_ref.shape[1]
    bases = rad1_ref.shape[0]
    atoms = block_ref.shape[1]
    slots = block_ref.shape[0] - HEAD

    ids16 = lax.broadcasted_iota(jnp.int32, (LANES, atoms), 0).astype(jnp.int16)
    one16 = jnp.ones((LANES, atoms), bf16)
    zero16 = jnp.zeros((LANES, atoms), bf16)
    for k in range(slots):
        slot = block_ref[HEAD + k : HEAD + k + 1, :].astype(jnp.int32)
        wanted = jnp.broadcast_to(slot, (LANES, atoms)).astype(jnp.int16)
        for r in range(oh_ref.shape[0] // LANES):
            hit = wanted - jnp.int16(r * LANES) == ids16
            oh_ref[r * LANES : (r + 1) * LANES, k * atoms : (k + 1) * atoms] = jnp.where(hit, one16, zero16)

    for fetch in fetches:
        fetch.wait()
    emb0 = emb_ref[0:1, :]
    emb_d = emb_ref[1:2, :] - emb0
    rr = jnp.concatenate([rad1_ref[...] * emb0, rad1_ref[...] * emb_d], axis=0) * (1.0 / slots)
    rr_hi = rr.astype(bf16).astype(f32)
    rr_lo = rr - rr_hi
    r2 = rad2_ref[...] * (1.0 / slots)
    r2_hi = r2.astype(bf16).astype(f32)
    r2_lo = r2 - r2_hi
    zeros = jnp.zeros((8, chan), f32)
    turned1 = jnp.concatenate([rr_hi, rr_hi, rr_lo, rr_lo] + [zeros] * 8, axis=0).T
    sides = jnp.concatenate([emb0, emb_d, read1_ref[...], read2_ref[...], zeros[:4]], axis=0)
    turned2 = jnp.concatenate([r2_hi, r2_hi, r2_lo, r2_lo] + [zeros] * 12, axis=0).T
    rrc_ref[...] = turned1[:, : 8 * bases].astype(bf16)
    r2c_ref[...] = turned2[:, : 4 * bases].astype(bf16)
    side_ref[...] = jnp.concatenate([sides] + [zeros] * 15, axis=0).T
    rrr_ref[...] = jnp.concatenate(
        [jnp.concatenate([rr_hi, rr_hi], axis=1), jnp.concatenate([rr_lo, jnp.zeros_like(rr_lo)], axis=1)], axis=0
    ).astype(bf16)
    r2r_ref[...] = jnp.concatenate(
        [jnp.concatenate([r2_hi, r2_hi], axis=1), jnp.concatenate([r2_lo, jnp.zeros_like(r2_lo)], axis=1)], axis=0
    ).astype(bf16)
    for i, ref in enumerate((mix1_ref, mix2_ref)):
        hi, lo = split(ref[...])
        mixa_ref[i, 0:chan, :] = hi
        mixa_ref[i, chan:, :] = lo
        for g in range(3):
            hi, lo = split(ref[:, g * chan : (g + 1) * chan].T)
            mixt_ref[i, g, 0:chan, :] = hi
            mixt_ref[i, g, chan:, :] = lo


def dot_parts(both, hi, lo):
    rows = both.shape[0] // 2
    first = dot(both, hi)
    return first[:rows] + first[rows:] + dot(both[:rows], lo)


def edge_kernel(plan, *refs):
    atoms, near, wide, before, after = plan
    n_wide = len(wide)
    blocks = refs[:n_wide]
    geo_ref, y_ref, yb_ref, bk_ref, bt_ref, gidx_ref, pick_ref = refs[n_wide:]
    bases = bk_ref.shape[0]
    slots = gidx_ref.shape[0]
    tiles = atoms // LANES
    half = atoms // 2
    half_tiles = half // LANES
    order_col = lax.broadcasted_iota(jnp.int32, (bases, LANES), 0).astype(f32)
    tables = []
    for quantity in range(4):
        chunks = []
        for g in range(n_wide):
            for t in range(tiles):
                chunks.append((g * tiles + t, blocks[g][quantity : quantity + 1, t * LANES : (t + 1) * LANES]))
        tables.append(chunks)
    for q in range(len(near)):
        ghosts = []
        for t in range(half_tiles):
            ghosts.append(
                (t, blocks[before[q]][4:5, half + t * LANES : half + (t + 1) * LANES] + float(before[q] * atoms))
            )
        for t in range(half_tiles):
            ghosts.append(
                (
                    half_tiles + tiles + t,
                    blocks[after[q]][4:5, t * LANES : (t + 1) * LANES] + float(after[q] * atoms),
                )
            )
        if q == 0:
            ids16 = lax.broadcasted_iota(jnp.int32, (pick_ref.shape[0], LANES), 0).astype(jnp.int16)
            one16 = jnp.ones(ids16.shape, bf16)
            zero16 = jnp.zeros(ids16.shape, bf16)
            for t, (_, chunk) in enumerate(ghosts):
                wanted = jnp.broadcast_to(chunk.astype(jnp.int32), ids16.shape).astype(jnp.int16)
                pick_ref[:, t * LANES : (t + 1) * LANES] = jnp.where(wanted == ids16, one16, zero16)
        for t in range(tiles):
            cols = slice(t * LANES, (t + 1) * LANES)
            here = slice(q * atoms + t * LANES, q * atoms + (t + 1) * LANES)
            slot = blocks[q][HEAD : HEAD + slots, cols].astype(jnp.int32)
            chunk_no = slot >> 7
            far = lookup(ghosts, chunk_no, slot & 127).astype(jnp.int32)
            own = (slot >= half) & (slot < half + atoms)
            gidx = jnp.where(own, slot + (q * atoms - half), far)
            gidx_ref[:, here] = gidx
            chunk_no = gidx >> 7
            place = gidx & 127
            xj, yj, zj, fj = [lookup(tables[i], chunk_no, place) for i in range(4)]
            rx = xj - row(blocks[q][0:1, cols])
            ry = yj - row(blocks[q][1:2, cols])
            rz = zj - row(blocks[q][2:3, cols])
            soft = jnp.sqrt(rx * rx + ry * ry + rz * rz + 1.0)
            back = 1.0 / soft
            ux, uy, uz = rx * back, ry * back, rz * back
            for i, value in enumerate((ux, uy, uz, back, soft, fj)):
                geo_ref[i, :, here] = value
            sphere = harmonics(ux, uy, uz)
            for l in range(1, ORDERS):
                y_ref[l - 1, :, here] = sphere[l]
                if q == 0:
                    for k in range(slots):
                        yb_ref[l - 1, k, :, cols] = row(sphere[l][k : k + 1, :])
            for n in range(bases):
                bk_ref[n, :, here] = jnp.exp(-0.5 * (soft - (1.0 + n)) ** 2)
            for k in range(slots):
                basis = jnp.exp(-0.5 * (row(soft[k : k + 1, :], bases) - (1.0 + order_col)) ** 2)
                bt_ref[k, 0:bases, here] = basis
                bt_ref[k, bases : 2 * bases, here] = basis * row(fj[k : k + 1, :], bases)


def first_kernel(plan, *refs):
    atoms, near, wide, _, _ = plan
    n_wide = len(wide)
    blocks = refs[:n_wide]
    y_ref, bt_ref, rrc_ref, side_ref, mixa_ref, m1_ref, sp1_ref, hs_ref, as_ref, flag_ref = refs[n_wide:]
    slots = bt_ref.shape[0]
    bases = bt_ref.shape[1] // 2
    chan = m1_ref.shape[1]
    n_near = m1_ref.shape[2]

    def sums(t, carry):
        here = pl.ds(pl.multiple_of(t * LANES, LANES), LANES)
        low = [None] * ORDERS
        for k in range(slots):
            basis = bt_ref[k, :, here]
            for l in range(ORDERS):
                term = basis if l == 0 else basis * row(y_ref[l - 1, k : k + 1, here], 2 * bases)
                low[l] = term if low[l] is None else low[l] + term
        for l in range(ORDERS):
            both = split_rows(low[l]).astype(bf16)
            as_ref[l, 0 : 4 * bases, here] = both
            as_ref[l, 4 * bases : 8 * bases, here] = both
        return carry

    lax.fori_loop(0, n_near // LANES, sums, 0)
    for q in range(len(near)):
        flag_ref[0:1, q * atoms : (q + 1) * atoms] = blocks[q][3:4, :]
    wide_cols = 2 * LANES
    emb0_col = side_ref[:, 0:1]
    embd_col = side_ref[:, 1:2]

    def first(j, carry):
        here = pl.ds(pl.multiple_of(j * wide_cols, wide_cols), wide_cols)
        inv = [None, None, None]
        for l in range(ORDERS):
            m = dot(rrc_ref[...], as_ref[l, :, here])
            m1_ref[l, :, here] = m
            inv[GROUP[l]] = m * m if inv[GROUP[l]] is None else inv[GROUP[l]] + m * m
        hi, lo = split(jnp.concatenate(inv, axis=0))
        value = dot_parts(mixa_ref[0], hi, lo)
        act, slope = silu_parts(value)
        sp1_ref[:, here] = slope
        hidden = act + emb0_col + embd_col * flag_ref[0:1, here]
        hi, lo = split(hidden)
        hs_ref[0:chan, here] = hi
        hs_ref[chan : 2 * chan, here] = lo
        return carry

    lax.fori_loop(0, n_near // wide_cols, first, 0)


def gather_kernel(hs_ref, oh_ref, pick_ref, bt_ref, r2c_ref, hj_ref, w_ref, car_ref, ext_ref):
    slots = bt_ref.shape[0]
    bases = bt_ref.shape[1] // 2
    chan = hj_ref.shape[0]
    atoms = hj_ref.shape[1] // slots
    half = atoms // 2
    ghosts = dot(hs_ref[...], pick_ref[...]).astype(bf16)
    ext_ref[:, 0:half] = ghosts[:, :half]
    ext_ref[:, half : half + atoms] = hs_ref[:, 0:atoms]
    ext_ref[:, half + atoms :] = ghosts[:, half:]

    def gather(k, carry):
        here = pl.ds(pl.multiple_of(k * atoms, LANES), atoms)
        both = dot(ext_ref[...], oh_ref[:, here])
        feat = both[:chan] + both[chan:]
        basis = split_rows(bt_ref[k, 0:bases, 0:atoms])
        weight = dot(r2c_ref[...], jnp.concatenate([basis, basis], axis=0).astype(bf16))
        hj_ref[:, here] = feat
        w_ref[:, here] = weight
        car_ref[:, here] = feat * weight
        return carry

    lax.fori_loop(0, slots, gather, 0)


def moment_kernel(car_ref, yb_ref, mixa_ref, mixt_ref, side_ref, m2_ref, dinv_ref, inv_ref):
    slots = yb_ref.shape[1]
    chan, atoms = m2_ref.shape[1:]
    tiles = atoms // LANES
    pairs = chan // 16
    wide_cols = 2 * LANES

    def moments(step, carry):
        t = step // pairs
        c = step % pairs
        cols = pl.ds(pl.multiple_of(t * LANES, LANES), LANES)
        base = pl.multiple_of(c * 16, 16)
        acc = [[None] * ORDERS, [None] * ORDERS]
        for k in range(slots):
            at = pl.ds(pl.multiple_of(k * atoms + t * LANES, LANES), LANES)
            got = car_ref[pl.ds(base, 16), at]
            for l in range(ORDERS):
                yb = yb_ref[l - 1, k, :, cols] if l else None
                for h in range(2):
                    part = got[8 * h : 8 * h + 8]
                    term = part * yb if l else part
                    acc[h][l] = term if acc[h][l] is None else acc[h][l] + term
        inv = [[None] * 3, [None] * 3]
        for l in range(ORDERS):
            m2_ref[l, pl.ds(base, 16), cols] = jnp.concatenate([acc[0][l], acc[1][l]], axis=0)
            for h in range(2):
                sq = acc[h][l] * acc[h][l]
                g = GROUP[l]
                inv[h][g] = sq if inv[h][g] is None else inv[h][g] + sq
        for g in range(3):
            inv_ref[pl.ds(pl.multiple_of(g * chan + c * 16, 16), 16), cols] = jnp.concatenate(
                [inv[0][g], inv[1][g]], axis=0
            )
        return carry

    lax.fori_loop(0, tiles * pairs, moments, 0)
    read2_col = side_ref[:, 3:4]
    for t in range(atoms // wide_cols):
        cols = slice(t * wide_cols, (t + 1) * wide_cols)
        hi, lo = split(inv_ref[:, cols])
        _, slope = silu_parts(dot_parts(mixa_ref[1], hi, lo))
        hi, lo = split(slope * (2.0 * read2_col))
        for g in range(3):
            dinv_ref[g * chan : (g + 1) * chan, cols] = dot_parts(mixt_ref[1, g], hi, lo)


def back_second_kernel(m2_ref, dinv_ref, car_ref, hj_ref, w_ref, yb_ref, bt_ref, geo_ref, r2r_ref,
                       dhe_ref, q_ref, dw_ref, p_ref):
    slots = yb_ref.shape[1]
    bases = bt_ref.shape[1] // 2
    chan, atoms = m2_ref.shape[1:]
    tiles = atoms // LANES
    pairs = chan // 16
    k_step = slots // 2

    def back_moments(step, carry):
        t = step // 2
        k0 = (step % 2) * k_step
        cols = pl.ds(pl.multiple_of(t * LANES, LANES), LANES)

        def over(c, acc):
            acc = list(acc)
            base = pl.multiple_of(c * 16, 16)
            dm = []
            scale = [dinv_ref[pl.ds(pl.multiple_of(g * chan + c * 16, 16), 16), cols] for g in range(3)]
            for l in range(ORDERS):
                dm.append(m2_ref[l, pl.ds(base, 16), cols] * scale[GROUP[l]])
            for kk in range(k_step):
                k = k0 + kk
                at = pl.ds(pl.multiple_of(k * atoms + t * LANES, LANES), LANES)
                got = car_ref[pl.ds(base, 16), at]
                out = [dm[0][:8], dm[0][8:]]
                for l in range(1, ORDERS):
                    yb = yb_ref[l - 1, k, :, cols]
                    i = kk * (ORDERS - 1) + l - 1
                    for h in range(2):
                        part = dm[l][8 * h : 8 * h + 8]
                        out[h] = out[h] + part * yb
                        acc[i] = acc[i] + part * got[8 * h : 8 * h + 8]
                dcar = jnp.concatenate(out, axis=0)
                for ref, other in ((dhe_ref, w_ref), (dw_ref, hj_ref)):
                    hi, lo = split(dcar * other[pl.ds(base, 16), at])
                    ref[pl.ds(base, 16), at] = hi
                    ref[pl.ds(pl.multiple_of(chan + c * 16, 16), 16), at] = lo
            return tuple(acc)

        start = tuple(jnp.zeros((8, LANES), f32) for _ in range(k_step * (ORDERS - 1)))
        acc = lax.fori_loop(0, pairs, over, start)
        for kk in range(k_step):
            for l in range(1, ORDERS):
                p_ref[l, pl.ds(pl.multiple_of((k0 + kk) * 8, 8), 8), cols] = acc[kk * (ORDERS - 1) + l - 1]
        return carry

    lax.fori_loop(0, tiles * 2, back_moments, 0)
    for k in range(slots):
        here = slice(k * atoms, (k + 1) * atoms)
        both = dot(r2r_ref[...], dw_ref[:, here])
        dbasis = both[:bases] + both[bases:]
        basis = bt_ref[k, 0:bases, 0:atoms]
        reach = 1.0 + lax.broadcasted_iota(jnp.int32, (bases, atoms), 0).astype(f32)
        p_ref[0, k * 8 : k * 8 + 8, :] = dbasis * basis * (reach - row(geo_ref[4, k : k + 1, 0:atoms], bases))
    lane = lax.broadcasted_iota(jnp.int32, (slots, 16 * slots), 1)
    sub = lax.broadcasted_iota(jnp.int32, (slots, 16 * slots), 0)
    adder = jnp.where(((lane >> 3) & (slots - 1)) == sub, 1.0, 0.0).astype(bf16)
    for l in range(ORDERS):
        q_ref[8 * l : 8 * l + 8, :] = dot(adder, split_rows(p_ref[l, :, :]).astype(bf16))


def back_first_kernel(oh_ref, pick_ref, dhe_ref, sp1_ref, m1_ref, mixt_ref, rrr_ref, side_ref, da_ref, dh_ref):
    chan, n_near = sp1_ref.shape
    atoms = pick_ref.shape[1]
    half = atoms // 2
    rows = rrr_ref.shape[0] // 2
    both = dot_nt(oh_ref[...], dhe_ref[...])
    ext = both[:, :chan] + both[:, chan:]
    hi, lo = split(jnp.concatenate([ext[:half], ext[half + atoms :]], axis=0))
    spread = dot(pick_ref[...], jnp.concatenate([hi, lo], axis=1))
    spread = spread[:, :chan] + spread[:, chan:]
    dh_ref[:, 0:atoms] = (spread[:atoms] + ext[half : half + atoms]).T + side_ref[:, 2:3]
    if n_near > atoms:
        dh_ref[:, atoms:] = spread[atoms:].T
    wide_cols = 2 * LANES

    def back_first(j, carry):
        here = pl.ds(pl.multiple_of(j * wide_cols, wide_cols), wide_cols)
        hi, lo = split(dh_ref[:, here] * sp1_ref[:, here] * 2.0)
        scale = [dot_parts(mixt_ref[0, g], hi, lo) for g in range(3)]
        for l in range(ORDERS):
            hi, lo = split(m1_ref[l, :, here] * scale[GROUP[l]])
            out = dot(rrr_ref[...], jnp.concatenate([hi, lo], axis=0))
            da_ref[l, :, here] = out[:rows] + out[rows:]
        return carry

    lax.fori_loop(0, n_near // wide_cols, back_first, 0)


def back_edge_kernel(plan, *refs):
    atoms, near, wide, _, _ = plan
    n_wide = len(wide)
    blocks = refs[:n_wide]
    moment_src, geo_ref, y_ref, bk_ref, gidx_ref, da_ref, q_ref = refs[n_wide : n_wide + 7]
    push_ref, mass_ref, val_ref, ohlo_ref, dr_ref, moment_ref, sem = refs[n_wide + 7 :]
    fetch = pltpu.make_async_copy(moment_src, moment_ref, sem)
    fetch.start()
    bases, slots, n_near = bk_ref.shape
    tiles = atoms // LANES
    top_rows = val_ref.shape[0] // 6

    def back_geometry(t, mine):
        here = pl.ds(pl.multiple_of(t * LANES, LANES), LANES)
        ux, uy, uz, back, soft, fj = [geo_ref[i, :, here] for i in range(6)]
        dy = [None] * ORDERS
        ds = None
        for n in range(bases):
            basis = bk_ref[n, :, here]
            db = None
            for l in range(ORDERS):
                g = row(da_ref[l, n : n + 1, here]) + fj * row(da_ref[l, bases + n : bases + n + 1, here])
                if l:
                    dy[l] = g * basis if dy[l] is None else dy[l] + g * basis
                    db = db + g * y_ref[l - 1, :, here]
                else:
                    db = g
            db = db * basis * ((1.0 + n) - soft)
            ds = db if ds is None else ds + db
        if mine:
            ds = ds + q_ref[0:8, here]
            for l in range(1, ORDERS):
                dy[l] = dy[l] + q_ref[8 * l : 8 * l + 8, here]
        dux = SQRT3 * dy[1] + SQRT15 * (uy * dy[4] + uz * dy[7] + ux * dy[8]) - SQRT5 * ux * dy[6]
        duy = SQRT3 * dy[2] + SQRT15 * (ux * dy[4] + uz * dy[5] - uy * dy[8]) - SQRT5 * uy * dy[6]
        duz = SQRT3 * dy[3] + SQRT15 * (uy * dy[5] + ux * dy[7]) + 2.0 * SQRT5 * uz * dy[6]
        along = ds - (ux * dux + uy * duy + uz * duz) * back
        for i, value in enumerate((dux * back + along * ux, duy * back + along * uy, duz * back + along * uz)):
            dr_ref[i, :, here] = value

    def mine_tile(t, carry):
        back_geometry(t, True)
        return carry

    def other_tile(t, carry):
        back_geometry(t, False)
        return carry

    lax.fori_loop(0, tiles, mine_tile, 0)
    lax.fori_loop(tiles, n_near // LANES, other_tile, 0)

    def place_tile(t, carry):
        here = pl.ds(pl.multiple_of(t * LANES, LANES), LANES)
        gidx = gidx_ref[:, here]
        chunk_no = gidx >> 7
        place = gidx & 127
        parts = []
        for i in range(3):
            value = dr_ref[i, :, here]
            hi = value.astype(bf16).astype(f32)
            parts.append((hi, value - hi))
        chunk_ids = lax.broadcasted_iota(jnp.int32, (top_rows, LANES), 0)
        place_ids = lax.broadcasted_iota(jnp.int32, (LANES, LANES), 0)
        for k in range(slots):
            at = pl.ds(pl.multiple_of(k * n_near + t * LANES, LANES), LANES)
            hit = chunk_ids == row(chunk_no[k : k + 1, :], top_rows)
            for i in range(3):
                both = [jnp.where(hit, row(part[k : k + 1, :], top_rows), 0.0) for part in parts[i]]
                val_ref[2 * i * top_rows : 2 * (i + 1) * top_rows, at] = jnp.concatenate(both, axis=0).astype(bf16)
            ohlo_ref[:, at] = jnp.where(place_ids == row(place[k : k + 1, :], LANES), 1.0, 0.0).astype(bf16)
        return carry

    lax.fori_loop(0, n_near // LANES, place_tile, 0)
    landed = dot_nt(ohlo_ref[...], val_ref[...]).T
    fetch.wait()
    lines = push_ref.shape[1] // (n_wide + 1)
    one = push_ref.at[0]
    for i in range(3):
        total = (
            landed[2 * i * top_rows : (2 * i + 1) * top_rows] + landed[(2 * i + 1) * top_rows : (2 * i + 2) * top_rows]
        )
        for g in range(n_wide):
            for t in range(tiles):
                cols = slice(t * LANES, (t + 1) * LANES)
                line = total[g * tiles + t : g * tiles + t + 1, :]
                if g < len(near):
                    here = slice(g * atoms + t * LANES, g * atoms + (t + 1) * LANES)
                    line = line - jnp.sum(dr_ref[i, :, here], axis=0, keepdims=True)
                line = -HALF_STEP * line
                at = i * tiles + t
                if g == 0:
                    line = line + moment_ref[i, :, cols]
                    one[at : at + 1, :] = blocks[0][i : i + 1, cols]
                one[(1 + g) * lines + at : (1 + g) * lines + at + 1, :] = line
                mass = HEAVY - (HEAVY - 1.0) * blocks[g][3:4, cols]
                mass_ref[g * lines + at : g * lines + at + 1, :] = mass
    if lines > 3 * tiles:
        for g in range(n_wide + 1):
            blank = slice(g * lines + 3 * tiles, (g + 1) * lines)
            one[blank, :] = jnp.zeros((lines - 3 * tiles, LANES), f32)
            if g < n_wide:
                mass_ref[blank, :] = jnp.ones((lines - 3 * tiles, LANES), f32)
    whole = push_ref[0]
    for copy in range(1, push_ref.shape[0]):
        push_ref[copy] = whole


def in_hbm(x):
    return pltpu.with_memory_space_constraint(x, pltpu.HBM)


def run(name, body, operands, results, scratch=(), far=(), mib=20, cost=None):
    specs = [pl.BlockSpec(memory_space=pltpu.HBM if i in far else pltpu.VMEM) for i in range(len(operands))]
    return pl.pallas_call(
        body,
        out_shape=tuple(jax.ShapeDtypeStruct(shape, dtype) for shape, dtype in results),
        in_specs=specs,
        out_specs=tuple(pl.BlockSpec(memory_space=pltpu.VMEM) for _ in results),
        scratch_shapes=list(scratch),
        compiler_params=pltpu.CompilerParams(vmem_limit_bytes=mib * MIB),
        cost_estimate=cost,
        name=name,
    )(*[in_hbm(x) if i in far else x for i, x in enumerate(operands)])


def choose(block, embedding, radial_one, radial_two, mix_one, mix_two, read_one, read_two):
    atoms = block.shape[1]
    slots = block.shape[0] - HEAD
    chan = embedding.shape[1]
    bases = radial_one.shape[0]
    weights = (embedding, radial_one, radial_two, mix_one, mix_two, read_one[None], read_two[None])
    return run(
        "choose",
        choose_kernel,
        (block, *weights),
        (
            ((2 * atoms, slots * atoms), bf16),
            ((chan, 8 * bases), bf16),
            ((chan, 4 * bases), bf16),
            ((chan, LANES), f32),
            ((4 * bases, 2 * chan), bf16),
            ((2 * bases, 2 * chan), bf16),
            ((2, 2 * chan, 3 * chan), bf16),
            ((2, 3, 2 * chan, chan), bf16),
        ),
        [pltpu.VMEM(w.shape, f32) for w in weights] + [pltpu.SemaphoreType.DMA((len(weights),))],
        range(1, 1 + len(weights)),
        cost=pl.CostEstimate(flops=2 * 10**9, bytes_accessed=2 * 10**6, transcendentals=0),
    )


def pushes(plan, outer, blocks, momenta, chosen):
    atoms, near, wide, _, _ = plan
    oh, rrc, r2c, sides, rrr, r2r, mixa, mixt = chosen
    chan = rrc.shape[0]
    bases = r2r.shape[0] // 2
    slots = blocks[0].shape[0] - HEAD
    n_near = len(near) * atoms
    edges = slots * atoms
    top_rows = -(-len(wide) * atoms // LANES // 8) * 8
    lines = line_count(atoms)
    mib = 12 + 6 * len(near)
    geo, y, yb, bk, bt, gidx, pick = run(
        "edges",
        functools.partial(edge_kernel, plan),
        blocks,
        (
            ((6, slots, n_near), f32),
            ((ORDERS - 1, slots, n_near), f32),
            ((ORDERS - 1, slots, 8, atoms), f32),
            ((bases, slots, n_near), f32),
            ((slots, 2 * bases, n_near), f32),
            ((slots, n_near), jnp.int32),
            ((n_near, atoms), bf16),
        ),
    )
    m1, sp1, hs = run(
        "first",
        functools.partial(first_kernel, plan),
        (*blocks, y, bt, rrc, sides, mixa),
        (((ORDERS, chan, n_near), f32), ((chan, n_near), f32), ((2 * chan, n_near), bf16)),
        [pltpu.VMEM((ORDERS, 8 * bases, n_near), bf16), pltpu.VMEM((8, n_near), f32)],
        mib=mib,
    )
    hj, w, car = run(
        "gather",
        gather_kernel,
        (hs, oh, pick, bt, r2c),
        (((chan, edges), f32),) * 3,
        [pltpu.VMEM((2 * chan, 2 * atoms), bf16)],
        mib=mib,
    )
    m2, dinv = run(
        "moments",
        moment_kernel,
        (car, yb, mixa, mixt, sides),
        (((ORDERS, chan, atoms), f32), ((3 * chan, atoms), f32)),
        [pltpu.VMEM((3 * chan, atoms), f32)],
        mib=mib,
    )
    dhe, q = run(
        "back_second",
        back_second_kernel,
        (m2, dinv, car, hj, w, yb, bt, geo, r2r),
        (((2 * chan, edges), bf16), ((8 * ORDERS, atoms), f32)),
        [pltpu.VMEM((2 * chan, edges), bf16), pltpu.VMEM((ORDERS, 8 * slots, atoms), f32)],
        mib=mib,
    )
    (da,) = run(
        "back_first",
        back_first_kernel,
        (oh, pick, dhe, sp1, m1, mixt, rrr, sides),
        (((ORDERS, 2 * bases, n_near), f32),),
        [pltpu.VMEM((chan, n_near), f32)],
        mib=mib,
    )
    return run(
        "back_edges",
        functools.partial(back_edge_kernel, plan),
        (*blocks, momenta, geo, y, bk, gidx, da, q),
        (((outer, (len(wide) + 1) * lines, LANES), f32), ((len(wide) * lines, LANES), f32)),
        [
            pltpu.VMEM((6 * top_rows, slots * n_near), bf16),
            pltpu.VMEM((LANES, slots * n_near), bf16),
            pltpu.VMEM((3, slots, n_near), f32),
            pltpu.VMEM(momenta.shape, f32),
            pltpu.SemaphoreType.DMA(()),
        ],
        (len(blocks),),
        mib=mib,
    )


def line_count(atoms):
    return -(-3 * (atoms // LANES) // 8) * 8


def ring_plan(domains, atoms):
    near = list(dict.fromkeys(o % domains for o in (0, 1, -1)))
    wide = list(dict.fromkeys(near + [o % domains for o in (2, -2)]))
    before = tuple(wide.index((o - 1) % domains) for o in near)
    after = tuple(wide.index((o + 1) % domains) for o in near)
    return atoms, tuple(near), tuple(wide), before, after


def mode_turns(bead_total):
    bead = np.arange(bead_total, dtype=np.float64)[:, None]
    mode = np.arange(bead_total, dtype=np.float64)[None, :]
    phase = 2.0 * np.pi * bead * mode / bead_total
    half_total = bead_total // 2
    table = math.sqrt(2.0 / bead_total) * np.where(mode < half_total, np.cos(phase), np.sin(phase))
    table = np.where(mode == half_total, np.cos(np.pi * bead) / math.sqrt(bead_total), table)
    table = np.where(mode == 0, 1.0 / math.sqrt(bead_total), table)
    angles = bead_total * np.sin(np.pi * mode[0] / bead_total)
    safe = np.where(mode[0] == 0, 1.0, angles)
    reach = np.where(mode[0] == 0, STEP, STEP * np.sin(angles) / safe)
    stiff = angles * np.sin(angles) / STEP
    return [[float(x) for x in (table * factor[None, :]) @ table[0]] for factor in (np.cos(angles), reach, stiff)]


def pack_kernel(coord_src, species_src, send_src, slot_src, block_ref, coord_ref, species_ref, send_ref, slot_ref, sems):
    pairs = ((coord_src, coord_ref), (species_src, species_ref), (send_src, send_ref), (slot_src, slot_ref))
    fetches = [pltpu.make_async_copy(src, dst, sems.at[i]) for i, (src, dst) in enumerate(pairs)]
    for fetch in fetches:
        fetch.start()
    for fetch in fetches:
        fetch.wait()
    atoms = block_ref.shape[1]
    for i in range(3):
        block_ref[i : i + 1, :] = coord_ref[i]
    block_ref[3:4, :] = species_ref[...].astype(f32)
    block_ref[4:5, :] = send_ref[...].astype(f32)
    block_ref[5:HEAD, :] = jnp.zeros((HEAD - 5, atoms), f32)
    block_ref[HEAD:, :] = slot_ref[...].astype(f32)


def turn_kernel(shape, bead_ref, mass_ref, source_ref, message_ref):
    outer, inner, domains, wide = shape
    turns = mode_turns(outer * inner)
    lines = mass_ref.shape[0] // len(wide)
    my_domain = bead_ref[1]
    my_outer = bead_ref[0] // inner
    my_inner = bead_ref[0] - my_outer * inner
    if domains > len(wide):
        message_ref[...] = jnp.zeros_like(message_ref)
    masses = [mass_ref[g * lines : (g + 1) * lines, :] for g in range(len(wide))]
    sources = []
    for z in range(outer):
        at = lax.rem(my_outer + outer - z, outer)
        sources.append([source_ref[at, pl.ds(g * lines, lines), :] for g in range(len(wide) + 1)])
    for s in range(inner):
        wraps = jnp.full((lines, LANES), my_inner + s) >= inner
        weights = []
        for turn in turns:
            row_of = []
            for z in range(outer):
                there = turn[(z * inner + s) % (outer * inner)]
                round_it = turn[(z * inner + s - inner) % (outer * inner)]
                row_of.append(jnp.where(wraps, jnp.full((lines, LANES), round_it), jnp.full((lines, LANES), there)))
            weights.append(row_of)
        to_inner = lax.rem(my_inner + s, inner)
        for g in range(len(wide)):
            turned = sum(weights[0][z] * sources[z][1 + g] for z in range(outer))
            drift = sum(weights[1][z] * sources[z][1 + g] for z in range(outer))
            new_q = drift / masses[g]
            new_p = turned
            if g == 0:
                new_q = new_q + sum(weights[0][z] * sources[z][0] for z in range(outer))
                new_p = new_p - masses[g] * sum(weights[2][z] * sources[z][0] for z in range(outer))
            to = to_inner * domains + lax.rem(my_domain + wide[g], domains)
            message_ref[to, 0:lines, :] = new_q
            message_ref[to, lines:, :] = new_p


def sum_kernel(arrived_ref, q_ref, p_ref):
    total = arrived_ref[0]
    for i in range(1, arrived_ref.shape[0]):
        total = total + arrived_ref[i]
    lines = total.shape[0] // 2
    tiles = q_ref.shape[2] // LANES
    for i in range(3):
        for t in range(tiles):
            at = i * tiles + t
            q_ref[i, :, t * LANES : (t + 1) * LANES] = total[at : at + 1]
            p_ref[i, :, t * LANES : (t + 1) * LANES] = total[lines + at : lines + at + 1]


def shards(
    positions, momenta, species, neighbours, send_list, embedding, radial_one, radial_two, mix_one, mix_two,
    read_one, read_two,
):
    slots, atoms = neighbours.shape
    domains = lax.axis_size("space")
    beads = lax.axis_size("bead")
    inner = next(d for d in range(1, beads + 1) if beads % d == 0 and d * d >= beads)
    outer = beads // inner
    plan = ring_plan(domains, atoms)
    wide = plan[2]
    vmem = pl.BlockSpec(memory_space=pltpu.VMEM)
    smem = pl.BlockSpec(memory_space=pltpu.SMEM)
    far = pl.BlockSpec(memory_space=pltpu.HBM)
    small = pltpu.CompilerParams(vmem_limit_bytes=4 * MIB)
    coord_rows = jnp.transpose(positions, (1, 0, 2))
    moment_rows = jnp.transpose(momenta, (1, 0, 2))
    block = pl.pallas_call(
        pack_kernel,
        out_shape=jax.ShapeDtypeStruct((HEAD + slots, atoms), f32),
        in_specs=[far] * 4,
        out_specs=vmem,
        scratch_shapes=[
            pltpu.VMEM(coord_rows.shape, f32),
            pltpu.VMEM((1, atoms), jnp.int32),
            pltpu.VMEM((1, atoms), jnp.int32),
            pltpu.VMEM((slots, atoms), jnp.int32),
            pltpu.SemaphoreType.DMA((4,)),
        ],
        compiler_params=small,
        name="pack",
    )(in_hbm(coord_rows), in_hbm(species[None]), in_hbm(send_list[None]), in_hbm(neighbours))
    blocks = [block]
    for offset in wide[1:]:
        blocks.append(lax.ppermute(block, "space", [(i, (i - offset) % domains) for i in range(domains)]))
    chosen = choose(block, embedding, radial_one, radial_two, mix_one, mix_two, read_one, read_two)
    pushed, masses = pushes(plan, outer, blocks, moment_rows, chosen)
    columns = [[z * inner + i for z in range(outer)] for i in range(inner)]
    sources = lax.all_to_all(pushed, "bead", 0, 0, axis_index_groups=columns, tiled=True)
    here = jnp.stack([lax.axis_index("bead"), lax.axis_index("space")]).astype(jnp.int32)
    lines = line_count(atoms)
    messages = pl.pallas_call(
        functools.partial(turn_kernel, (outer, inner, domains, wide)),
        out_shape=jax.ShapeDtypeStruct((inner * domains, 2 * lines, LANES), f32),
        in_specs=[smem, vmem, vmem],
        out_specs=vmem,
        compiler_params=small,
        name="turn",
    )(here, masses, sources)
    rows = [[z * inner * domains + i for i in range(inner * domains)] for z in range(outer)]
    arrived = lax.all_to_all(messages, ("bead", "space"), 0, 0, axis_index_groups=rows, tiled=True)
    new_q, new_p = pl.pallas_call(
        sum_kernel,
        out_shape=(jax.ShapeDtypeStruct((3, 1, atoms), f32),) * 2,
        in_specs=[vmem],
        out_specs=(vmem, vmem),
        compiler_params=small,
        name="sum",
    )(arrived)
    return (jnp.transpose(new_q, (1, 0, 2)), jnp.transpose(new_p, (1, 0, 2)))


def solution(mesh):
    placed = (
        P("bead", None, "space"),
        P("bead", None, "space"),
        P("space"),
        P(None, "space"),
        P("space"),
        P(),
        P(),
        P(),
        P(),
        P(),
        P(),
        P(),
    )
    return jax.shard_map(
        shards,
        mesh=mesh,
        in_specs=placed,
        out_specs=(P("bead", None, "space"), P("bead", None, "space")),
        check_vma=False,
    )
```

```python
import functools
import math

import jax
import jax.numpy as jnp
import numpy as np
from jax import lax
from jax.experimental import pallas as pl
from jax.experimental.pallas import tpu as pltpu
from jax.sharding import PartitionSpec as P

STEP = 2.0
HALF_STEP = 1.0
HEAVY = 16.0
SQRT3 = math.sqrt(3.0)
SQRT5 = math.sqrt(5.0)
SQRT15 = math.sqrt(15.0)
LANES = 128
ORDERS = 9
GROUP = (0, 1, 1, 1, 2, 2, 2, 2, 2)
HEAD = 8
MIB = 1024 * 1024
f32 = jnp.float32
bf16 = jnp.bfloat16


def split(x):
    hi = x.astype(bf16)
    return hi, (x - hi.astype(f32)).astype(bf16)


def split_rows(x):
    hi = x.astype(bf16).astype(f32)
    return jnp.concatenate([hi, x - hi], axis=0)


def dot(a, b):
    return jnp.dot(a, b, preferred_element_type=f32)


def dot_nt(a, b):
    return lax.dot_general(a, b, (((1,), (1,)), ((), ())), preferred_element_type=f32)


def in_pairs(start, stop, step):
    per_turn = 2 if (stop - start) % 2 == 0 else 1

    def turn(i, carry):
        for j in range(per_turn):
            step(start + i * per_turn + j)
        return carry

    lax.fori_loop(0, (stop - start) // per_turn, turn, 0)


def row(x, rows=8):
    return jnp.broadcast_to(x, (rows, x.shape[1]))


def lookup(chunks, wanted, position):
    out = None
    for number, chunk in chunks:
        got = jnp.take_along_axis(row(chunk), position, axis=1, mode="promise_in_bounds")
        out = got if out is None else jnp.where(wanted == number, got, out)
    return out


def harmonics(ux, uy, uz):
    return [
        None,
        SQRT3 * ux,
        SQRT3 * uy,
        SQRT3 * uz,
        SQRT15 * ux * uy,
        SQRT15 * uy * uz,
        0.5 * SQRT5 * (2.0 * uz * uz - ux * ux - uy * uy),
        SQRT15 * ux * uz,
        0.5 * SQRT15 * (ux * ux - uy * uy),
    ]


def silu_parts(v):
    gate = 1.0 / (1.0 + jnp.exp(-v))
    return v * gate, gate * (1.0 + v * (1.0 - gate))


def choose_kernel(block_ref, *refs):
    sources = refs[:7]
    oh_ref, rrc_ref, r2c_ref, side_ref, rrr_ref, r2r_ref, mixa_ref, mixt_ref = refs[7:15]
    held = refs[15:22]
    sems = refs[22]
    emb_ref, rad1_ref, rad2_ref, mix1_ref, mix2_ref, read1_ref, read2_ref = held
    fetches = [pltpu.make_async_copy(src, dst, sems.at[i]) for i, (src, dst) in enumerate(zip(sources, held))]
    for fetch in fetches:
        fetch.start()
    chan = emb_ref.shape[1]
    bases = rad1_ref.shape[0]
    atoms = block_ref.shape[1]
    slots = block_ref.shape[0] - HEAD

    ids16 = lax.broadcasted_iota(jnp.int32, (LANES, atoms), 0).astype(jnp.int16)
    one16 = jnp.ones((LANES, atoms), bf16)
    zero16 = jnp.zeros((LANES, atoms), bf16)
    for k in range(slots):
        slot = block_ref[HEAD + k : HEAD + k + 1, :].astype(jnp.int32)
        wanted = jnp.broadcast_to(slot, (LANES, atoms)).astype(jnp.int16)
        for r in range(oh_ref.shape[0] // LANES):
            hit = wanted - jnp.int16(r * LANES) == ids16
            oh_ref[r * LANES : (r + 1) * LANES, k * atoms : (k + 1) * atoms] = jnp.where(hit, one16, zero16)

    for fetch in fetches:
        fetch.wait()
    emb0 = emb_ref[0:1, :]
    emb_d = emb_ref[1:2, :] - emb0
    rr = jnp.concatenate([rad1_ref[...] * emb0, rad1_ref[...] * emb_d], axis=0) * (1.0 / slots)
    rr_hi = rr.astype(bf16).astype(f32)
    rr_lo = rr - rr_hi
    r2 = rad2_ref[...] * (1.0 / slots)
    r2_hi = r2.astype(bf16).astype(f32)
    r2_lo = r2 - r2_hi
    zeros = jnp.zeros((8, chan), f32)
    turned1 = jnp.concatenate([rr_hi, rr_hi, rr_lo, rr_lo] + [zeros] * 8, axis=0).T
    sides = jnp.concatenate([emb0, emb_d, read1_ref[...], read2_ref[...], zeros[:4]], axis=0)
    turned2 = jnp.concatenate([r2_hi, r2_hi, r2_lo, r2_lo] + [zeros] * 12, axis=0).T
    rrc_ref[...] = turned1[:, : 8 * bases].astype(bf16)
    r2c_ref[...] = turned2[:, : 4 * bases].astype(bf16)
    side_ref[...] = jnp.concatenate([sides] + [zeros] * 15, axis=0).T
    rrr_ref[...] = jnp.concatenate(
        [jnp.concatenate([rr_hi, rr_hi], axis=1), jnp.concatenate([rr_lo, jnp.zeros_like(rr_lo)], axis=1)], axis=0
    ).astype(bf16)
    r2r_ref[...] = jnp.concatenate(
        [jnp.concatenate([r2_hi, r2_hi], axis=1), jnp.concatenate([r2_lo, jnp.zeros_like(r2_lo)], axis=1)], axis=0
    ).astype(bf16)
    for i, ref in enumerate((mix1_ref, mix2_ref)):
        hi, lo = split(ref[...])
        mixa_ref[i, 0:chan, :] = hi
        mixa_ref[i, chan:, :] = lo
        for g in range(3):
            hi, lo = split(ref[:, g * chan : (g + 1) * chan].T)
            mixt_ref[i, g, 0:chan, :] = hi
            mixt_ref[i, g, chan:, :] = lo


def dot_parts(both, hi, lo):
    rows = both.shape[0] // 2
    first = dot(both, hi)
    return first[:rows] + first[rows:] + dot(both[:rows], lo)


def edge_kernel(plan, *refs):
    atoms, near, wide, before, after = plan
    n_wide = len(wide)
    blocks = refs[:n_wide]
    geo_ref, y_ref, yb_ref, bk_ref, bt_ref, gidx_ref, pick_ref = refs[n_wide:]
    bases = bk_ref.shape[0]
    slots = gidx_ref.shape[0]
    tiles = atoms // LANES
    half = atoms // 2
    half_tiles = half // LANES
    order_col = lax.broadcasted_iota(jnp.int32, (bases, LANES), 0).astype(f32)
    tables = []
    for quantity in range(4):
        chunks = []
        for g in range(n_wide):
            for t in range(tiles):
                chunks.append((g * tiles + t, blocks[g][quantity : quantity + 1, t * LANES : (t + 1) * LANES]))
        tables.append(chunks)
    for q in range(len(near)):
        ghosts = []
        for t in range(half_tiles):
            ghosts.append(
                (t, blocks[before[q]][4:5, half + t * LANES : half + (t + 1) * LANES] + float(before[q] * atoms))
            )
        for t in range(half_tiles):
            ghosts.append(
                (
                    half_tiles + tiles + t,
                    blocks[after[q]][4:5, t * LANES : (t + 1) * LANES] + float(after[q] * atoms),
                )
            )
        if q == 0:
            ids16 = lax.broadcasted_iota(jnp.int32, (pick_ref.shape[0], LANES), 0).astype(jnp.int16)
            one16 = jnp.ones(ids16.shape, bf16)
            zero16 = jnp.zeros(ids16.shape, bf16)
            for t, (_, chunk) in enumerate(ghosts):
                wanted = jnp.broadcast_to(chunk.astype(jnp.int32), ids16.shape).astype(jnp.int16)
                pick_ref[:, t * LANES : (t + 1) * LANES] = jnp.where(wanted == ids16, one16, zero16)
        for t in range(tiles):
            cols = slice(t * LANES, (t + 1) * LANES)
            here = slice(q * atoms + t * LANES, q * atoms + (t + 1) * LANES)
            slot = blocks[q][HEAD : HEAD + slots, cols].astype(jnp.int32)
            chunk_no = slot >> 7
            far = lookup(ghosts, chunk_no, slot & 127).astype(jnp.int32)
            own = (slot >= half) & (slot < half + atoms)
            gidx = jnp.where(own, slot + (q * atoms - half), far)
            gidx_ref[:, here] = gidx
            chunk_no = gidx >> 7
            place = gidx & 127
            xj, yj, zj, fj = [lookup(tables[i], chunk_no, place) for i in range(4)]
            rx = xj - row(blocks[q][0:1, cols])
            ry = yj - row(blocks[q][1:2, cols])
            rz = zj - row(blocks[q][2:3, cols])
            soft = jnp.sqrt(rx * rx + ry * ry + rz * rz + 1.0)
            back = 1.0 / soft
            ux, uy, uz = rx * back, ry * back, rz * back
            for i, value in enumerate((ux, uy, uz, back, soft, fj)):
                geo_ref[i, :, here] = value
            sphere = harmonics(ux, uy, uz)
            for l in range(1, ORDERS):
                y_ref[l - 1, :, here] = sphere[l]
                if q == 0:
                    for k in range(slots):
                        yb_ref[l - 1, k, :, cols] = row(sphere[l][k : k + 1, :])
            for n in range(bases):
                bk_ref[n, :, here] = jnp.exp(-0.5 * (soft - (1.0 + n)) ** 2)
            for k in range(slots):
                basis = jnp.exp(-0.5 * (row(soft[k : k + 1, :], bases) - (1.0 + order_col)) ** 2)
                bt_ref[k, 0:bases, here] = basis
                bt_ref[k, bases : 2 * bases, here] = basis * row(fj[k : k + 1, :], bases)


def first_kernel(plan, *refs):
    atoms, near, wide, _, _ = plan
    n_wide = len(wide)
    blocks = refs[:n_wide]
    y_ref, bt_ref, rrc_ref, side_ref, mixa_ref, m1_ref, sp1_ref, hs_ref, as_ref, flag_ref = refs[n_wide:]
    slots = bt_ref.shape[0]
    bases = bt_ref.shape[1] // 2
    chan = m1_ref.shape[1]
    n_near = m1_ref.shape[2]

    def sums(t):
        here = pl.ds(pl.multiple_of(t * LANES, LANES), LANES)
        low = [None] * ORDERS
        for k in range(slots):
            basis = bt_ref[k, :, here]
            for l in range(ORDERS):
                term = basis if l == 0 else basis * row(y_ref[l - 1, k : k + 1, here], 2 * bases)
                low[l] = term if low[l] is None else low[l] + term
        for l in range(ORDERS):
            both = split_rows(low[l]).astype(bf16)
            as_ref[l, 0 : 4 * bases, here] = both
            as_ref[l, 4 * bases : 8 * bases, here] = both

    in_pairs(0, n_near // LANES, sums)
    for q in range(len(near)):
        flag_ref[0:1, q * atoms : (q + 1) * atoms] = blocks[q][3:4, :]
    wide_cols = 2 * LANES
    emb0_col = side_ref[:, 0:1]
    embd_col = side_ref[:, 1:2]

    def first(j):
        here = pl.ds(pl.multiple_of(j * wide_cols, wide_cols), wide_cols)
        inv = [None, None, None]
        for l in range(ORDERS):
            m = dot(rrc_ref[...], as_ref[l, :, here])
            m1_ref[l, :, here] = m
            inv[GROUP[l]] = m * m if inv[GROUP[l]] is None else inv[GROUP[l]] + m * m
        hi, lo = split(jnp.concatenate(inv, axis=0))
        value = dot_parts(mixa_ref[0], hi, lo)
        act, slope = silu_parts(value)
        sp1_ref[:, here] = slope
        hidden = act + emb0_col + embd_col * flag_ref[0:1, here]
        hi, lo = split(hidden)
        hs_ref[0:chan, here] = hi
        hs_ref[chan : 2 * chan, here] = lo

    in_pairs(0, n_near // wide_cols, first)


def gather_kernel(hs_ref, oh_ref, pick_ref, bt_ref, r2c_ref, hj_ref, w_ref, car_ref, ext_ref):
    slots = bt_ref.shape[0]
    bases = bt_ref.shape[1] // 2
    chan = hj_ref.shape[0]
    atoms = hj_ref.shape[1] // slots
    half = atoms // 2
    ghosts = dot(hs_ref[...], pick_ref[...]).astype(bf16)
    ext_ref[:, 0:half] = ghosts[:, :half]
    ext_ref[:, half : half + atoms] = hs_ref[:, 0:atoms]
    ext_ref[:, half + atoms :] = ghosts[:, half:]

    def gather(k):
        here = pl.ds(pl.multiple_of(k * atoms, LANES), atoms)
        both = dot(ext_ref[...], oh_ref[:, here])
        feat = both[:chan] + both[chan:]
        basis = split_rows(bt_ref[k, 0:bases, 0:atoms])
        weight = dot(r2c_ref[...], jnp.concatenate([basis, basis], axis=0).astype(bf16))
        hj_ref[:, here] = feat
        w_ref[:, here] = weight
        car_ref[:, here] = feat * weight

    in_pairs(0, slots, gather)


def moment_kernel(car_ref, yb_ref, mixa_ref, mixt_ref, side_ref, m2_ref, dinv_ref, inv_ref):
    slots = yb_ref.shape[1]
    chan, atoms = m2_ref.shape[1:]
    tiles = atoms // LANES
    wide_cols = 2 * LANES
    rows = 32
    groups = chan // rows

    def moments(step, carry):
        t = step // groups
        c = step % groups
        cols = pl.ds(pl.multiple_of(t * LANES, LANES), LANES)
        base = pl.multiple_of(c * rows, rows)
        acc = [[None] * ORDERS for _ in range(rows // 8)]
        for k in range(slots):
            at = pl.ds(pl.multiple_of(k * atoms + t * LANES, LANES), LANES)
            got = car_ref[pl.ds(base, rows), at]
            for l in range(ORDERS):
                yb = yb_ref[l - 1, k, :, cols] if l else None
                for h in range(rows // 8):
                    part = got[8 * h : 8 * h + 8]
                    term = part * yb if l else part
                    acc[h][l] = term if acc[h][l] is None else acc[h][l] + term
        for h in range(rows // 8):
            inv = [None] * 3
            for l in range(ORDERS):
                m2_ref[l, pl.ds(pl.multiple_of(base + 8 * h, 8), 8), cols] = acc[h][l]
                sq = acc[h][l] * acc[h][l]
                g = GROUP[l]
                inv[g] = sq if inv[g] is None else inv[g] + sq
            for g in range(3):
                inv_ref[pl.ds(pl.multiple_of(g * chan + base + 8 * h, 8), 8), cols] = inv[g]
        return carry

    lax.fori_loop(0, tiles * groups, moments, 0)
    read2_col = side_ref[:, 3:4]
    for t in range(atoms // wide_cols):
        cols = slice(t * wide_cols, (t + 1) * wide_cols)
        hi, lo = split(inv_ref[:, cols])
        _, slope = silu_parts(dot_parts(mixa_ref[1], hi, lo))
        hi, lo = split(slope * (2.0 * read2_col))
        for g in range(3):
            dinv_ref[g * chan : (g + 1) * chan, cols] = dot_parts(mixt_ref[1, g], hi, lo)


def back_second_kernel(m2_ref, dinv_ref, car_ref, hj_ref, w_ref, yb_ref, bt_ref, geo_ref, r2r_ref,
                       dhe_ref, q_ref, dw_ref, p_ref):
    slots = yb_ref.shape[1]
    bases = bt_ref.shape[1] // 2
    chan, atoms = m2_ref.shape[1:]
    tiles = atoms // LANES
    pairs = chan // 16
    k_step = slots // 2

    def back_moments(step, carry):
        t = step // 2
        k0 = (step % 2) * k_step
        cols = pl.ds(pl.multiple_of(t * LANES, LANES), LANES)

        def one(c, acc):
            base = pl.multiple_of(c * 16, 16)
            dm = []
            scale = [dinv_ref[pl.ds(pl.multiple_of(g * chan + c * 16, 16), 16), cols] for g in range(3)]
            for l in range(ORDERS):
                dm.append(m2_ref[l, pl.ds(base, 16), cols] * scale[GROUP[l]])
            for kk in range(k_step):
                k = k0 + kk
                at = pl.ds(pl.multiple_of(k * atoms + t * LANES, LANES), LANES)
                got = car_ref[pl.ds(base, 16), at]
                out = [dm[0][:8], dm[0][8:]]
                for l in range(1, ORDERS):
                    yb = yb_ref[l - 1, k, :, cols]
                    i = kk * (ORDERS - 1) + l - 1
                    for h in range(2):
                        part = dm[l][8 * h : 8 * h + 8]
                        out[h] = out[h] + part * yb
                        acc[i] = acc[i] + part * got[8 * h : 8 * h + 8]
                dcar = jnp.concatenate(out, axis=0)
                for ref, other in ((dhe_ref, w_ref), (dw_ref, hj_ref)):
                    hi, lo = split(dcar * other[pl.ds(base, 16), at])
                    ref[pl.ds(base, 16), at] = hi
                    ref[pl.ds(pl.multiple_of(chan + c * 16, 16), 16), at] = lo

        def over(c, acc):
            acc = list(acc)
            one(2 * c, acc)
            one(2 * c + 1, acc)
            return tuple(acc)

        start = tuple(jnp.zeros((8, LANES), f32) for _ in range(k_step * (ORDERS - 1)))
        acc = lax.fori_loop(0, pairs // 2, over, start)
        for kk in range(k_step):
            for l in range(1, ORDERS):
                p_ref[l, pl.ds(pl.multiple_of((k0 + kk) * 8, 8), 8), cols] = acc[kk * (ORDERS - 1) + l - 1]
        return carry

    lax.fori_loop(0, tiles * 2, back_moments, 0)
    for k in range(slots):
        here = slice(k * atoms, (k + 1) * atoms)
        both = dot(r2r_ref[...], dw_ref[:, here])
        dbasis = both[:bases] + both[bases:]
        basis = bt_ref[k, 0:bases, 0:atoms]
        reach = 1.0 + lax.broadcasted_iota(jnp.int32, (bases, atoms), 0).astype(f32)
        p_ref[0, k * 8 : k * 8 + 8, :] = dbasis * basis * (reach - row(geo_ref[4, k : k + 1, 0:atoms], bases))
    lane = lax.broadcasted_iota(jnp.int32, (slots, 16 * slots), 1)
    sub = lax.broadcasted_iota(jnp.int32, (slots, 16 * slots), 0)
    adder = jnp.where(((lane >> 3) & (slots - 1)) == sub, 1.0, 0.0).astype(bf16)
    for l in range(ORDERS):
        q_ref[8 * l : 8 * l + 8, :] = dot(adder, split_rows(p_ref[l, :, :]).astype(bf16))


def back_first_kernel(oh_ref, pick_ref, dhe_ref, sp1_ref, m1_ref, mixt_ref, rrr_ref, side_ref, da_ref, dh_ref):
    chan, n_near = sp1_ref.shape
    atoms = pick_ref.shape[1]
    half = atoms // 2
    rows = rrr_ref.shape[0] // 2
    both = dot_nt(oh_ref[...], dhe_ref[...])
    ext = both[:, :chan] + both[:, chan:]
    hi, lo = split(jnp.concatenate([ext[:half], ext[half + atoms :]], axis=0))
    spread = dot(pick_ref[...], jnp.concatenate([hi, lo], axis=1))
    spread = spread[:, :chan] + spread[:, chan:]
    dh_ref[:, 0:atoms] = (spread[:atoms] + ext[half : half + atoms]).T + side_ref[:, 2:3]
    if n_near > atoms:
        dh_ref[:, atoms:] = spread[atoms:].T
    wide_cols = 2 * LANES

    def back_first(j):
        here = pl.ds(pl.multiple_of(j * wide_cols, wide_cols), wide_cols)
        hi, lo = split(dh_ref[:, here] * sp1_ref[:, here] * 2.0)
        scale = [dot_parts(mixt_ref[0, g], hi, lo) for g in range(3)]
        for l in range(ORDERS):
            hi, lo = split(m1_ref[l, :, here] * scale[GROUP[l]])
            out = dot(rrr_ref[...], jnp.concatenate([hi, lo], axis=0))
            da_ref[l, :, here] = out[:rows] + out[rows:]

    in_pairs(0, n_near // wide_cols, back_first)


def back_edge_kernel(plan, *refs):
    atoms, near, wide, _, _ = plan
    n_wide = len(wide)
    blocks = refs[:n_wide]
    moment_src, geo_ref, y_ref, bk_ref, gidx_ref, da_ref, q_ref = refs[n_wide : n_wide + 7]
    push_ref, mass_ref, val_ref, ohlo_ref, dr_ref, moment_ref, sem = refs[n_wide + 7 :]
    fetch = pltpu.make_async_copy(moment_src, moment_ref, sem)
    fetch.start()
    bases, slots, n_near = bk_ref.shape
    tiles = atoms // LANES
    top_rows = val_ref.shape[0] // 6

    def back_geometry(t, mine):
        here = pl.ds(pl.multiple_of(t * LANES, LANES), LANES)
        ux, uy, uz, back, soft, fj = [geo_ref[i, :, here] for i in range(6)]
        dy = [None] * ORDERS
        ds = None
        for n in range(bases):
            basis = bk_ref[n, :, here]
            db = None
            for l in range(ORDERS):
                g = row(da_ref[l, n : n + 1, here]) + fj * row(da_ref[l, bases + n : bases + n + 1, here])
                if l:
                    dy[l] = g * basis if dy[l] is None else dy[l] + g * basis
                    db = db + g * y_ref[l - 1, :, here]
                else:
                    db = g
            db = db * basis * ((1.0 + n) - soft)
            ds = db if ds is None else ds + db
        if mine:
            ds = ds + q_ref[0:8, here]
            for l in range(1, ORDERS):
                dy[l] = dy[l] + q_ref[8 * l : 8 * l + 8, here]
        dux = SQRT3 * dy[1] + SQRT15 * (uy * dy[4] + uz * dy[7] + ux * dy[8]) - SQRT5 * ux * dy[6]
        duy = SQRT3 * dy[2] + SQRT15 * (ux * dy[4] + uz * dy[5] - uy * dy[8]) - SQRT5 * uy * dy[6]
        duz = SQRT3 * dy[3] + SQRT15 * (uy * dy[5] + ux * dy[7]) + 2.0 * SQRT5 * uz * dy[6]
        along = ds - (ux * dux + uy * duy + uz * duz) * back
        for i, value in enumerate((dux * back + along * ux, duy * back + along * uy, duz * back + along * uz)):
            dr_ref[i, :, here] = value

    in_pairs(0, tiles, lambda t: back_geometry(t, True))
    in_pairs(tiles, n_near // LANES, lambda t: back_geometry(t, False))

    def place_tile(t):
        here = pl.ds(pl.multiple_of(t * LANES, LANES), LANES)
        gidx = gidx_ref[:, here]
        chunk_no = gidx >> 7
        place = gidx & 127
        parts = []
        for i in range(3):
            value = dr_ref[i, :, here]
            hi = value.astype(bf16).astype(f32)
            parts.append((hi, value - hi))
        chunk_ids = lax.broadcasted_iota(jnp.int32, (top_rows, LANES), 0)
        place_ids = lax.broadcasted_iota(jnp.int32, (LANES, LANES), 0)
        for k in range(slots):
            at = pl.ds(pl.multiple_of(k * n_near + t * LANES, LANES), LANES)
            hit = chunk_ids == row(chunk_no[k : k + 1, :], top_rows)
            for i in range(3):
                both = [jnp.where(hit, row(part[k : k + 1, :], top_rows), 0.0) for part in parts[i]]
                val_ref[2 * i * top_rows : 2 * (i + 1) * top_rows, at] = jnp.concatenate(both, axis=0).astype(bf16)
            ohlo_ref[:, at] = jnp.where(place_ids == row(place[k : k + 1, :], LANES), 1.0, 0.0).astype(bf16)

    in_pairs(0, n_near // LANES, place_tile)
    landed = dot_nt(ohlo_ref[...], val_ref[...]).T
    fetch.wait()
    lines = push_ref.shape[0] // (n_wide + 1)
    for i in range(3):
        total = (
            landed[2 * i * top_rows : (2 * i + 1) * top_rows] + landed[(2 * i + 1) * top_rows : (2 * i + 2) * top_rows]
        )
        for g in range(n_wide):
            for t in range(tiles):
                cols = slice(t * LANES, (t + 1) * LANES)
                line = total[g * tiles + t : g * tiles + t + 1, :]
                if g < len(near):
                    here = slice(g * atoms + t * LANES, g * atoms + (t + 1) * LANES)
                    line = line - jnp.sum(dr_ref[i, :, here], axis=0, keepdims=True)
                line = -HALF_STEP * line
                at = i * tiles + t
                if g == 0:
                    line = line + moment_ref[i, :, cols]
                    push_ref[at : at + 1, :] = blocks[0][i : i + 1, cols]
                push_ref[(1 + g) * lines + at : (1 + g) * lines + at + 1, :] = line
                mass = HEAVY - (HEAVY - 1.0) * blocks[g][3:4, cols]
                mass_ref[g * lines + at : g * lines + at + 1, :] = mass
    if lines > 3 * tiles:
        for g in range(n_wide + 1):
            blank = slice(g * lines + 3 * tiles, (g + 1) * lines)
            push_ref[blank, :] = jnp.zeros((lines - 3 * tiles, LANES), f32)
            if g < n_wide:
                mass_ref[blank, :] = jnp.ones((lines - 3 * tiles, LANES), f32)


def in_hbm(x):
    return pltpu.with_memory_space_constraint(x, pltpu.HBM)


def run(name, body, operands, results, scratch=(), far=(), mib=20, cost=None):
    specs = [pl.BlockSpec(memory_space=pltpu.HBM if i in far else pltpu.VMEM) for i in range(len(operands))]
    return pl.pallas_call(
        body,
        out_shape=tuple(jax.ShapeDtypeStruct(shape, dtype) for shape, dtype in results),
        in_specs=specs,
        out_specs=tuple(pl.BlockSpec(memory_space=pltpu.VMEM) for _ in results),
        scratch_shapes=list(scratch),
        compiler_params=pltpu.CompilerParams(vmem_limit_bytes=mib * MIB),
        cost_estimate=cost,
        name=name,
    )(*[in_hbm(x) if i in far else x for i, x in enumerate(operands)])


def choose(block, embedding, radial_one, radial_two, mix_one, mix_two, read_one, read_two):
    atoms = block.shape[1]
    slots = block.shape[0] - HEAD
    chan = embedding.shape[1]
    bases = radial_one.shape[0]
    weights = (embedding, radial_one, radial_two, mix_one, mix_two, read_one[None], read_two[None])
    return run(
        "choose",
        choose_kernel,
        (block, *weights),
        (
            ((2 * atoms, slots * atoms), bf16),
            ((chan, 8 * bases), bf16),
            ((chan, 4 * bases), bf16),
            ((chan, LANES), f32),
            ((4 * bases, 2 * chan), bf16),
            ((2 * bases, 2 * chan), bf16),
            ((2, 2 * chan, 3 * chan), bf16),
            ((2, 3, 2 * chan, chan), bf16),
        ),
        [pltpu.VMEM(w.shape, f32) for w in weights] + [pltpu.SemaphoreType.DMA((len(weights),))],
        range(1, 1 + len(weights)),
        cost=pl.CostEstimate(flops=2 * 10**9, bytes_accessed=2 * 10**6, transcendentals=0),
    )


def pushes(plan, blocks, momenta, chosen):
    atoms, near, wide, _, _ = plan
    oh, rrc, r2c, sides, rrr, r2r, mixa, mixt = chosen
    chan = rrc.shape[0]
    bases = r2r.shape[0] // 2
    slots = blocks[0].shape[0] - HEAD
    n_near = len(near) * atoms
    edges = slots * atoms
    top_rows = -(-len(wide) * atoms // LANES // 8) * 8
    lines = line_count(atoms)
    mib = 12 + 6 * len(near)
    geo, y, yb, bk, bt, gidx, pick = run(
        "edges",
        functools.partial(edge_kernel, plan),
        blocks,
        (
            ((6, slots, n_near), f32),
            ((ORDERS - 1, slots, n_near), f32),
            ((ORDERS - 1, slots, 8, atoms), f32),
            ((bases, slots, n_near), f32),
            ((slots, 2 * bases, n_near), f32),
            ((slots, n_near), jnp.int32),
            ((n_near, atoms), bf16),
        ),
    )
    m1, sp1, hs = run(
        "first",
        functools.partial(first_kernel, plan),
        (*blocks, y, bt, rrc, sides, mixa),
        (((ORDERS, chan, n_near), f32), ((chan, n_near), f32), ((2 * chan, n_near), bf16)),
        [pltpu.VMEM((ORDERS, 8 * bases, n_near), bf16), pltpu.VMEM((8, n_near), f32)],
        mib=mib,
    )
    hj, w, car = run(
        "gather",
        gather_kernel,
        (hs, oh, pick, bt, r2c),
        (((chan, edges), f32),) * 3,
        [pltpu.VMEM((2 * chan, 2 * atoms), bf16)],
        mib=mib,
    )
    m2, dinv = run(
        "moments",
        moment_kernel,
        (car, yb, mixa, mixt, sides),
        (((ORDERS, chan, atoms), f32), ((3 * chan, atoms), f32)),
        [pltpu.VMEM((3 * chan, atoms), f32)],
        mib=mib,
    )
    dhe, q = run(
        "back_second",
        back_second_kernel,
        (m2, dinv, car, hj, w, yb, bt, geo, r2r),
        (((2 * chan, edges), bf16), ((8 * ORDERS, atoms), f32)),
        [pltpu.VMEM((2 * chan, edges), bf16), pltpu.VMEM((ORDERS, 8 * slots, atoms), f32)],
        mib=mib,
    )
    (da,) = run(
        "back_first",
        back_first_kernel,
        (oh, pick, dhe, sp1, m1, mixt, rrr, sides),
        (((ORDERS, 2 * bases, n_near), f32),),
        [pltpu.VMEM((chan, n_near), f32)],
        mib=mib,
    )
    return run(
        "back_edges",
        functools.partial(back_edge_kernel, plan),
        (*blocks, momenta, geo, y, bk, gidx, da, q),
        ((((len(wide) + 1) * lines, LANES), f32), ((len(wide) * lines, LANES), f32)),
        [
            pltpu.VMEM((6 * top_rows, slots * n_near), bf16),
            pltpu.VMEM((LANES, slots * n_near), bf16),
            pltpu.VMEM((3, slots, n_near), f32),
            pltpu.VMEM(momenta.shape, f32),
            pltpu.SemaphoreType.DMA(()),
        ],
        (len(blocks),),
        mib=mib,
    )


def line_count(atoms):
    return -(-3 * (atoms // LANES) // 8) * 8


def ring_plan(domains, atoms):
    near = list(dict.fromkeys(o % domains for o in (0, 1, -1)))
    wide = list(dict.fromkeys(near + [o % domains for o in (2, -2)]))
    before = tuple(wide.index((o - 1) % domains) for o in near)
    after = tuple(wide.index((o + 1) % domains) for o in near)
    return atoms, tuple(near), tuple(wide), before, after


def mode_turns(bead_total):
    bead = np.arange(bead_total, dtype=np.float64)[:, None]
    mode = np.arange(bead_total, dtype=np.float64)[None, :]
    phase = 2.0 * np.pi * bead * mode / bead_total
    half_total = bead_total // 2
    table = math.sqrt(2.0 / bead_total) * np.where(mode < half_total, np.cos(phase), np.sin(phase))
    table = np.where(mode == half_total, np.cos(np.pi * bead) / math.sqrt(bead_total), table)
    table = np.where(mode == 0, 1.0 / math.sqrt(bead_total), table)
    angles = bead_total * np.sin(np.pi * mode[0] / bead_total)
    safe = np.where(mode[0] == 0, 1.0, angles)
    reach = np.where(mode[0] == 0, STEP, STEP * np.sin(angles) / safe)
    stiff = angles * np.sin(angles) / STEP
    return [[float(x) for x in (table * factor[None, :]) @ table[0]] for factor in (np.cos(angles), reach, stiff)]


def pack_kernel(coord_src, species_src, send_src, slot_src, block_ref, coord_ref, species_ref, send_ref, slot_ref, sems):
    pairs = ((coord_src, coord_ref), (species_src, species_ref), (send_src, send_ref), (slot_src, slot_ref))
    fetches = [pltpu.make_async_copy(src, dst, sems.at[i]) for i, (src, dst) in enumerate(pairs)]
    for fetch in fetches:
        fetch.start()
    for fetch in fetches:
        fetch.wait()
    atoms = block_ref.shape[1]
    for i in range(3):
        block_ref[i : i + 1, :] = coord_ref[i]
    block_ref[3:4, :] = species_ref[...].astype(f32)
    block_ref[4:5, :] = send_ref[...].astype(f32)
    block_ref[5:HEAD, :] = jnp.zeros((HEAD - 5, atoms), f32)
    block_ref[HEAD:, :] = slot_ref[...].astype(f32)


def turn_kernel(shape, bead_ref, domain_ref, mass_ref, source_ref, message_ref):
    outer, inner, domains, wide = shape
    turns = mode_turns(outer * inner)
    lines = mass_ref.shape[0] // len(wide)
    my_domain = domain_ref[0]
    my_outer = bead_ref[0] // inner
    my_inner = bead_ref[0] - my_outer * inner
    if domains > len(wide):
        message_ref[...] = jnp.zeros_like(message_ref)
    masses = [mass_ref[g * lines : (g + 1) * lines, :] for g in range(len(wide))]
    sources = []
    for z in range(outer):
        at = lax.rem(my_outer + outer - z, outer)
        sources.append([source_ref[at, pl.ds(g * lines, lines), :] for g in range(len(wide) + 1)])
    for s in range(inner):
        wraps = jnp.full((lines, LANES), my_inner + s) >= inner
        weights = []
        for turn in turns:
            row_of = []
            for z in range(outer):
                there = turn[(z * inner + s) % (outer * inner)]
                round_it = turn[(z * inner + s - inner) % (outer * inner)]
                row_of.append(jnp.where(wraps, jnp.full((lines, LANES), round_it), jnp.full((lines, LANES), there)))
            weights.append(row_of)
        to_inner = lax.rem(my_inner + s, inner)
        for g in range(len(wide)):
            turned = sum(weights[0][z] * sources[z][1 + g] for z in range(outer))
            drift = sum(weights[1][z] * sources[z][1 + g] for z in range(outer))
            new_q = drift / masses[g]
            new_p = turned
            if g == 0:
                new_q = new_q + sum(weights[0][z] * sources[z][0] for z in range(outer))
                new_p = new_p - masses[g] * sum(weights[2][z] * sources[z][0] for z in range(outer))
            to = to_inner * domains + lax.rem(my_domain + wide[g], domains)
            message_ref[to, 0:lines, :] = new_q
            message_ref[to, lines:, :] = new_p


def sum_kernel(arrived_ref, q_ref, p_ref):
    total = arrived_ref[0]
    for i in range(1, arrived_ref.shape[0]):
        total = total + arrived_ref[i]
    lines = total.shape[0] // 2
    tiles = q_ref.shape[2] // LANES
    for i in range(3):
        for t in range(tiles):
            at = i * tiles + t
            q_ref[i, :, t * LANES : (t + 1) * LANES] = total[at : at + 1]
            p_ref[i, :, t * LANES : (t + 1) * LANES] = total[lines + at : lines + at + 1]


def shards(
    positions, momenta, species, neighbours, send_list, embedding, radial_one, radial_two, mix_one, mix_two,
    read_one, read_two,
):
    slots, atoms = neighbours.shape
    domains = lax.axis_size("space")
    beads = lax.axis_size("bead")
    inner = next(d for d in range(1, beads + 1) if beads % d == 0 and d * d >= beads)
    outer = beads // inner
    plan = ring_plan(domains, atoms)
    wide = plan[2]
    vmem = pl.BlockSpec(memory_space=pltpu.VMEM)
    smem = pl.BlockSpec(memory_space=pltpu.SMEM)
    far = pl.BlockSpec(memory_space=pltpu.HBM)
    small = pltpu.CompilerParams(vmem_limit_bytes=4 * MIB)
    coord_rows = jnp.transpose(positions, (1, 0, 2))
    moment_rows = jnp.transpose(momenta, (1, 0, 2))
    block = pl.pallas_call(
        pack_kernel,
        out_shape=jax.ShapeDtypeStruct((HEAD + slots, atoms), f32),
        in_specs=[far] * 4,
        out_specs=vmem,
        scratch_shapes=[
            pltpu.VMEM(coord_rows.shape, f32),
            pltpu.VMEM((1, atoms), jnp.int32),
            pltpu.VMEM((1, atoms), jnp.int32),
            pltpu.VMEM((slots, atoms), jnp.int32),
            pltpu.SemaphoreType.DMA((4,)),
        ],
        compiler_params=small,
        name="pack",
    )(in_hbm(coord_rows), in_hbm(species[None]), in_hbm(send_list[None]), in_hbm(neighbours))
    blocks = [block]
    for offset in wide[1:]:
        blocks.append(lax.ppermute(block, "space", [(i, (i - offset) % domains) for i in range(domains)]))
    chosen = choose(block, embedding, radial_one, radial_two, mix_one, mix_two, read_one, read_two)
    pushed, masses = pushes(plan, blocks, moment_rows, chosen)
    columns = [[z * inner + i for z in range(outer)] for i in range(inner)]
    sources = lax.all_gather(pushed, "bead", axis=0, axis_index_groups=columns)
    here = [lax.axis_index(axis).astype(jnp.int32).reshape(1) for axis in ("bead", "space")]
    lines = line_count(atoms)
    messages = pl.pallas_call(
        functools.partial(turn_kernel, (outer, inner, domains, wide)),
        out_shape=jax.ShapeDtypeStruct((inner * domains, 2 * lines, LANES), f32),
        in_specs=[smem, smem, vmem, vmem],
        out_specs=vmem,
        compiler_params=small,
        name="turn",
    )(*here, masses, sources)
    rows = [[z * inner * domains + i for i in range(inner * domains)] for z in range(outer)]
    arrived = lax.all_to_all(messages, ("bead", "space"), 0, 0, axis_index_groups=rows, tiled=True)
    new_q, new_p = pl.pallas_call(
        sum_kernel,
        out_shape=(jax.ShapeDtypeStruct((3, 1, atoms), f32),) * 2,
        in_specs=[vmem],
        out_specs=(vmem, vmem),
        compiler_params=small,
        name="sum",
    )(arrived)
    return (jnp.transpose(new_q, (1, 0, 2)), jnp.transpose(new_p, (1, 0, 2)))


def solution(mesh):
    placed = (
        P("bead", None, "space"),
        P("bead", None, "space"),
        P("space"),
        P(None, "space"),
        P("space"),
        P(),
        P(),
        P(),
        P(),
        P(),
        P(),
        P(),
    )
    return jax.shard_map(
        shards,
        mesh=mesh,
        in_specs=placed,
        out_specs=(P("bead", None, "space"), P("bead", None, "space")),
        check_vma=False,
    )
```

```python
import functools
import math

import jax
import jax.numpy as jnp
import numpy as np
from jax import lax
from jax.experimental import pallas as pl
from jax.experimental.pallas import tpu as pltpu
from jax.sharding import PartitionSpec as P

STEP = 2.0
HALF_STEP = 1.0
HEAVY = 16.0
SQRT3 = math.sqrt(3.0)
SQRT5 = math.sqrt(5.0)
SQRT15 = math.sqrt(15.0)
LANES = 128
ORDERS = 9
GROUP = (0, 1, 1, 1, 2, 2, 2, 2, 2)
HEAD = 8
MIB = 1024 * 1024
f32 = jnp.float32
bf16 = jnp.bfloat16


def split(x):
    hi = x.astype(bf16)
    return hi, (x - hi.astype(f32)).astype(bf16)


def split_rows(x):
    hi = x.astype(bf16).astype(f32)
    return jnp.concatenate([hi, x - hi], axis=0)


def dot(a, b):
    return jnp.dot(a, b, preferred_element_type=f32)


def dot_nt(a, b):
    return lax.dot_general(a, b, (((1,), (1,)), ((), ())), preferred_element_type=f32)


def in_turns(start, stop, step, most=4):
    per_turn = next(n for n in range(most, 0, -1) if (stop - start) % n == 0)

    def turn(i, carry):
        for j in range(per_turn):
            step(start + i * per_turn + j)
        return carry

    lax.fori_loop(0, (stop - start) // per_turn, turn, 0)


def row(x, rows=8):
    return jnp.broadcast_to(x, (rows, x.shape[1]))


def lookup(chunks, wanted, position):
    out = None
    for number, chunk in chunks:
        got = jnp.take_along_axis(row(chunk), position, axis=1, mode="promise_in_bounds")
        out = got if out is None else jnp.where(wanted == number, got, out)
    return out


def harmonics(ux, uy, uz):
    return [
        None,
        SQRT3 * ux,
        SQRT3 * uy,
        SQRT3 * uz,
        SQRT15 * ux * uy,
        SQRT15 * uy * uz,
        0.5 * SQRT5 * (2.0 * uz * uz - ux * ux - uy * uy),
        SQRT15 * ux * uz,
        0.5 * SQRT15 * (ux * ux - uy * uy),
    ]


def silu_parts(v):
    gate = 1.0 / (1.0 + jnp.exp(-v))
    return v * gate, gate * (1.0 + v * (1.0 - gate))


def choose_kernel(block_ref, *refs):
    sources = refs[:7]
    oh_ref, rrc_ref, r2c_ref, side_ref, rrr_ref, r2r_ref, mixa_ref, mixt_ref = refs[7:15]
    held = refs[15:22]
    sems = refs[22]
    emb_ref, rad1_ref, rad2_ref, mix1_ref, mix2_ref, read1_ref, read2_ref = held
    fetches = [pltpu.make_async_copy(src, dst, sems.at[i]) for i, (src, dst) in enumerate(zip(sources, held))]
    for fetch in fetches:
        fetch.start()
    chan = emb_ref.shape[1]
    bases = rad1_ref.shape[0]
    atoms = block_ref.shape[1]
    slots = block_ref.shape[0] - HEAD

    ids16 = lax.broadcasted_iota(jnp.int32, (LANES, atoms), 0).astype(jnp.int16)
    one16 = jnp.ones((LANES, atoms), bf16)
    zero16 = jnp.zeros((LANES, atoms), bf16)
    for k in range(slots):
        slot = block_ref[HEAD + k : HEAD + k + 1, :].astype(jnp.int32)
        wanted = jnp.broadcast_to(slot, (LANES, atoms)).astype(jnp.int16)
        for r in range(oh_ref.shape[0] // LANES):
            hit = wanted - jnp.int16(r * LANES) == ids16
            oh_ref[r * LANES : (r + 1) * LANES, k * atoms : (k + 1) * atoms] = jnp.where(hit, one16, zero16)

    for fetch in fetches:
        fetch.wait()
    emb0 = emb_ref[0:1, :]
    emb_d = emb_ref[1:2, :] - emb0
    rr = jnp.concatenate([rad1_ref[...] * emb0, rad1_ref[...] * emb_d], axis=0) * (1.0 / slots)
    rr_hi = rr.astype(bf16).astype(f32)
    rr_lo = rr - rr_hi
    r2 = rad2_ref[...] * (1.0 / slots)
    r2_hi = r2.astype(bf16).astype(f32)
    r2_lo = r2 - r2_hi
    zeros = jnp.zeros((8, chan), f32)
    turned1 = jnp.concatenate([rr_hi, rr_hi, rr_lo, rr_lo] + [zeros] * 8, axis=0).T
    sides = jnp.concatenate([emb0, emb_d, read1_ref[...], read2_ref[...], zeros[:4]], axis=0)
    turned2 = jnp.concatenate([r2_hi, r2_hi, r2_lo, r2_lo] + [zeros] * 12, axis=0).T
    rrc_ref[...] = turned1[:, : 8 * bases].astype(bf16)
    r2c_ref[...] = turned2[:, : 4 * bases].astype(bf16)
    side_ref[...] = jnp.concatenate([sides] + [zeros] * 15, axis=0).T
    rrr_ref[...] = jnp.concatenate(
        [jnp.concatenate([rr_hi, rr_hi], axis=1), jnp.concatenate([rr_lo, jnp.zeros_like(rr_lo)], axis=1)], axis=0
    ).astype(bf16)
    r2r_ref[...] = jnp.concatenate(
        [jnp.concatenate([r2_hi, r2_hi], axis=1), jnp.concatenate([r2_lo, jnp.zeros_like(r2_lo)], axis=1)], axis=0
    ).astype(bf16)
    for i, ref in enumerate((mix1_ref, mix2_ref)):
        hi, lo = split(ref[...])
        mixa_ref[i, 0:chan, :] = hi
        mixa_ref[i, chan:, :] = lo
        for g in range(3):
            hi, lo = split(ref[:, g * chan : (g + 1) * chan].T)
            mixt_ref[i, g, 0:chan, :] = hi
            mixt_ref[i, g, chan:, :] = lo


def dot_parts(both, hi, lo):
    rows = both.shape[0] // 2
    first = dot(both, hi)
    return first[:rows] + first[rows:] + dot(both[:rows], lo)


def edge_kernel(plan, *refs):
    atoms, near, wide, before, after = plan
    n_wide = len(wide)
    blocks = refs[:n_wide]
    geo_ref, y_ref, yb_ref, bk_ref, bt_ref, gidx_ref, pick_ref = refs[n_wide:]
    bases = bk_ref.shape[0]
    slots = gidx_ref.shape[0]
    tiles = atoms // LANES
    half = atoms // 2
    half_tiles = half // LANES
    order_col = lax.broadcasted_iota(jnp.int32, (bases, LANES), 0).astype(f32)
    tables = []
    for quantity in range(4):
        chunks = []
        for g in range(n_wide):
            for t in range(tiles):
                chunks.append((g * tiles + t, blocks[g][quantity : quantity + 1, t * LANES : (t + 1) * LANES]))
        tables.append(chunks)
    for q in range(len(near)):
        ghosts = []
        for t in range(half_tiles):
            ghosts.append(
                (t, blocks[before[q]][4:5, half + t * LANES : half + (t + 1) * LANES] + float(before[q] * atoms))
            )
        for t in range(half_tiles):
            ghosts.append(
                (
                    half_tiles + tiles + t,
                    blocks[after[q]][4:5, t * LANES : (t + 1) * LANES] + float(after[q] * atoms),
                )
            )
        if q == 0:
            ids16 = lax.broadcasted_iota(jnp.int32, (pick_ref.shape[0], LANES), 0).astype(jnp.int16)
            one16 = jnp.ones(ids16.shape, bf16)
            zero16 = jnp.zeros(ids16.shape, bf16)
            for t, (_, chunk) in enumerate(ghosts):
                wanted = jnp.broadcast_to(chunk.astype(jnp.int32), ids16.shape).astype(jnp.int16)
                pick_ref[:, t * LANES : (t + 1) * LANES] = jnp.where(wanted == ids16, one16, zero16)
        for t in range(tiles):
            cols = slice(t * LANES, (t + 1) * LANES)
            here = slice(q * atoms + t * LANES, q * atoms + (t + 1) * LANES)
            slot = blocks[q][HEAD : HEAD + slots, cols].astype(jnp.int32)
            chunk_no = slot >> 7
            far = lookup(ghosts, chunk_no, slot & 127).astype(jnp.int32)
            own = (slot >= half) & (slot < half + atoms)
            gidx = jnp.where(own, slot + (q * atoms - half), far)
            gidx_ref[:, here] = gidx
            chunk_no = gidx >> 7
            place = gidx & 127
            xj, yj, zj, fj = [lookup(tables[i], chunk_no, place) for i in range(4)]
            rx = xj - row(blocks[q][0:1, cols])
            ry = yj - row(blocks[q][1:2, cols])
            rz = zj - row(blocks[q][2:3, cols])
            soft = jnp.sqrt(rx * rx + ry * ry + rz * rz + 1.0)
            back = 1.0 / soft
            ux, uy, uz = rx * back, ry * back, rz * back
            for i, value in enumerate((ux, uy, uz, back, soft, fj)):
                geo_ref[i, :, here] = value
            sphere = harmonics(ux, uy, uz)
            for l in range(1, ORDERS):
                y_ref[l - 1, :, here] = sphere[l]
                if q == 0:
                    for k in range(slots):
                        yb_ref[l - 1, k, :, cols] = row(sphere[l][k : k + 1, :])
            for n in range(bases):
                bk_ref[n, :, here] = jnp.exp(-0.5 * (soft - (1.0 + n)) ** 2)
            for k in range(slots):
                basis = jnp.exp(-0.5 * (row(soft[k : k + 1, :], bases) - (1.0 + order_col)) ** 2)
                bt_ref[k, 0:bases, here] = basis
                bt_ref[k, bases : 2 * bases, here] = basis * row(fj[k : k + 1, :], bases)


def first_kernel(plan, *refs):
    atoms, near, wide, _, _ = plan
    n_wide = len(wide)
    blocks = refs[:n_wide]
    y_ref, bt_ref, rrc_ref, side_ref, mixa_ref, m1_ref, sp1_ref, hs_ref, as_ref, flag_ref = refs[n_wide:]
    slots = bt_ref.shape[0]
    bases = bt_ref.shape[1] // 2
    chan = m1_ref.shape[1]
    n_near = m1_ref.shape[2]

    def sums(t):
        here = pl.ds(pl.multiple_of(t * LANES, LANES), LANES)
        low = [None] * ORDERS
        for k in range(slots):
            basis = bt_ref[k, :, here]
            for l in range(ORDERS):
                term = basis if l == 0 else basis * row(y_ref[l - 1, k : k + 1, here], 2 * bases)
                low[l] = term if low[l] is None else low[l] + term
        for l in range(ORDERS):
            both = split_rows(low[l]).astype(bf16)
            as_ref[l, 0 : 4 * bases, here] = both
            as_ref[l, 4 * bases : 8 * bases, here] = both

    in_turns(0, n_near // LANES, sums)
    for q in range(len(near)):
        flag_ref[0:1, q * atoms : (q + 1) * atoms] = blocks[q][3:4, :]
    wide_cols = 2 * LANES
    emb0_col = side_ref[:, 0:1]
    embd_col = side_ref[:, 1:2]

    def first(j):
        here = pl.ds(pl.multiple_of(j * wide_cols, wide_cols), wide_cols)
        inv = [None, None, None]
        for l in range(ORDERS):
            m = dot(rrc_ref[...], as_ref[l, :, here])
            m1_ref[l, :, here] = m
            inv[GROUP[l]] = m * m if inv[GROUP[l]] is None else inv[GROUP[l]] + m * m
        hi, lo = split(jnp.concatenate(inv, axis=0))
        value = dot_parts(mixa_ref[0], hi, lo)
        act, slope = silu_parts(value)
        sp1_ref[:, here] = slope
        hidden = act + emb0_col + embd_col * flag_ref[0:1, here]
        hi, lo = split(hidden)
        hs_ref[0:chan, here] = hi
        hs_ref[chan : 2 * chan, here] = lo

    in_turns(0, n_near // wide_cols, first)


def gather_kernel(hs_ref, oh_ref, pick_ref, bt_ref, r2c_ref, hj_ref, w_ref, car_ref, ext_ref):
    slots = bt_ref.shape[0]
    bases = bt_ref.shape[1] // 2
    chan = hj_ref.shape[0]
    atoms = hj_ref.shape[1] // slots
    half = atoms // 2
    ghosts = dot(hs_ref[...], pick_ref[...]).astype(bf16)
    ext_ref[:, 0:half] = ghosts[:, :half]
    ext_ref[:, half : half + atoms] = hs_ref[:, 0:atoms]
    ext_ref[:, half + atoms :] = ghosts[:, half:]

    def gather(k):
        here = pl.ds(pl.multiple_of(k * atoms, LANES), atoms)
        both = dot(ext_ref[...], oh_ref[:, here])
        feat = both[:chan] + both[chan:]
        basis = split_rows(bt_ref[k, 0:bases, 0:atoms])
        weight = dot(r2c_ref[...], jnp.concatenate([basis, basis], axis=0).astype(bf16))
        hj_ref[:, here] = feat
        w_ref[:, here] = weight
        car_ref[:, here] = feat * weight

    in_turns(0, slots, gather)


def moment_kernel(car_ref, yb_ref, mixa_ref, mixt_ref, side_ref, m2_ref, dinv_ref, inv_ref):
    slots = yb_ref.shape[1]
    chan, atoms = m2_ref.shape[1:]
    tiles = atoms // LANES
    wide_cols = 2 * LANES
    rows = 32
    groups = chan // rows

    def moments(step, carry):
        t = step // groups
        c = step % groups
        cols = pl.ds(pl.multiple_of(t * LANES, LANES), LANES)
        base = pl.multiple_of(c * rows, rows)
        acc = [[None] * ORDERS for _ in range(rows // 8)]
        for k in range(slots):
            at = pl.ds(pl.multiple_of(k * atoms + t * LANES, LANES), LANES)
            got = car_ref[pl.ds(base, rows), at]
            for l in range(ORDERS):
                yb = yb_ref[l - 1, k, :, cols] if l else None
                for h in range(rows // 8):
                    part = got[8 * h : 8 * h + 8]
                    term = part * yb if l else part
                    acc[h][l] = term if acc[h][l] is None else acc[h][l] + term
        for h in range(rows // 8):
            inv = [None] * 3
            for l in range(ORDERS):
                m2_ref[l, pl.ds(pl.multiple_of(base + 8 * h, 8), 8), cols] = acc[h][l]
                sq = acc[h][l] * acc[h][l]
                g = GROUP[l]
                inv[g] = sq if inv[g] is None else inv[g] + sq
            for g in range(3):
                inv_ref[pl.ds(pl.multiple_of(g * chan + base + 8 * h, 8), 8), cols] = inv[g]
        return carry

    lax.fori_loop(0, tiles * groups, moments, 0)
    read2_col = side_ref[:, 3:4]
    for t in range(atoms // wide_cols):
        cols = slice(t * wide_cols, (t + 1) * wide_cols)
        hi, lo = split(inv_ref[:, cols])
        _, slope = silu_parts(dot_parts(mixa_ref[1], hi, lo))
        hi, lo = split(slope * (2.0 * read2_col))
        for g in range(3):
            dinv_ref[g * chan : (g + 1) * chan, cols] = dot_parts(mixt_ref[1, g], hi, lo)


def back_second_kernel(m2_ref, dinv_ref, car_ref, hj_ref, w_ref, yb_ref, bt_ref, geo_ref, r2r_ref,
                       dhe_ref, q_ref, dw_ref, p_ref):
    slots = yb_ref.shape[1]
    bases = bt_ref.shape[1] // 2
    chan, atoms = m2_ref.shape[1:]
    tiles = atoms // LANES
    pairs = chan // 16
    k_step = slots // 2
    per_turn = 4 if pairs % 4 == 0 else 1

    def back_moments(step, carry):
        t = step // 2
        k0 = (step % 2) * k_step
        cols = pl.ds(pl.multiple_of(t * LANES, LANES), LANES)

        def one(c, acc):
            base = pl.multiple_of(c * 16, 16)
            dm = []
            scale = [dinv_ref[pl.ds(pl.multiple_of(g * chan + c * 16, 16), 16), cols] for g in range(3)]
            for l in range(ORDERS):
                dm.append(m2_ref[l, pl.ds(base, 16), cols] * scale[GROUP[l]])
            for kk in range(k_step):
                k = k0 + kk
                at = pl.ds(pl.multiple_of(k * atoms + t * LANES, LANES), LANES)
                got = car_ref[pl.ds(base, 16), at]
                out = [dm[0][:8], dm[0][8:]]
                for l in range(1, ORDERS):
                    yb = yb_ref[l - 1, k, :, cols]
                    i = kk * (ORDERS - 1) + l - 1
                    for h in range(2):
                        part = dm[l][8 * h : 8 * h + 8]
                        out[h] = out[h] + part * yb
                        acc[i] = acc[i] + part * got[8 * h : 8 * h + 8]
                dcar = jnp.concatenate(out, axis=0)
                for ref, other in ((dhe_ref, w_ref), (dw_ref, hj_ref)):
                    hi, lo = split(dcar * other[pl.ds(base, 16), at])
                    ref[pl.ds(base, 16), at] = hi
                    ref[pl.ds(pl.multiple_of(chan + c * 16, 16), 16), at] = lo

        def over(c, acc):
            acc = list(acc)
            for i in range(per_turn):
                one(per_turn * c + i, acc)
            return tuple(acc)

        start = tuple(jnp.zeros((8, LANES), f32) for _ in range(k_step * (ORDERS - 1)))
        acc = lax.fori_loop(0, pairs // per_turn, over, start)
        for kk in range(k_step):
            for l in range(1, ORDERS):
                p_ref[l, pl.ds(pl.multiple_of((k0 + kk) * 8, 8), 8), cols] = acc[kk * (ORDERS - 1) + l - 1]
        return carry

    lax.fori_loop(0, tiles * 2, back_moments, 0)
    for k in range(slots):
        here = slice(k * atoms, (k + 1) * atoms)
        both = dot(r2r_ref[...], dw_ref[:, here])
        dbasis = both[:bases] + both[bases:]
        basis = bt_ref[k, 0:bases, 0:atoms]
        reach = 1.0 + lax.broadcasted_iota(jnp.int32, (bases, atoms), 0).astype(f32)
        p_ref[0, k * 8 : k * 8 + 8, :] = dbasis * basis * (reach - row(geo_ref[4, k : k + 1, 0:atoms], bases))
    lane = lax.broadcasted_iota(jnp.int32, (slots, 16 * slots), 1)
    sub = lax.broadcasted_iota(jnp.int32, (slots, 16 * slots), 0)
    adder = jnp.where(((lane >> 3) & (slots - 1)) == sub, 1.0, 0.0).astype(bf16)
    for l in range(ORDERS):
        q_ref[8 * l : 8 * l + 8, :] = dot(adder, split_rows(p_ref[l, :, :]).astype(bf16))


def scatter_kernel(oh_ref, pick_ref, dhe_ref, side_ref, dh_ref):
    chan, n_near = dh_ref.shape
    atoms = pick_ref.shape[1]
    half = atoms // 2
    both = dot_nt(oh_ref[...], dhe_ref[...])
    ext = both[:, :chan] + both[:, chan:]
    hi, lo = split(jnp.concatenate([ext[:half], ext[half + atoms :]], axis=0))
    spread = dot(pick_ref[...], jnp.concatenate([hi, lo], axis=1))
    spread = spread[:, :chan] + spread[:, chan:]
    dh_ref[:, 0:atoms] = (spread[:atoms] + ext[half : half + atoms]).T + side_ref[:, 2:3]
    if n_near > atoms:
        dh_ref[:, atoms:] = spread[atoms:].T


def back_first_kernel(dh_ref, sp1_ref, m1_ref, mixt_ref, rrr_ref, da_ref):
    n_near = sp1_ref.shape[1]
    rows = rrr_ref.shape[0] // 2
    wide_cols = 2 * LANES

    def back_first(j):
        here = pl.ds(pl.multiple_of(j * wide_cols, wide_cols), wide_cols)
        hi, lo = split(dh_ref[:, here] * sp1_ref[:, here] * 2.0)
        scale = [dot_parts(mixt_ref[0, g], hi, lo) for g in range(3)]
        for l in range(ORDERS):
            hi, lo = split(m1_ref[l, :, here] * scale[GROUP[l]])
            out = dot(rrr_ref[...], jnp.concatenate([hi, lo], axis=0))
            da_ref[l, :, here] = out[:rows] + out[rows:]

    in_turns(0, n_near // wide_cols, back_first)


def back_edge_kernel(plan, *refs):
    atoms, near, wide, _, _ = plan
    n_wide = len(wide)
    blocks = refs[:n_wide]
    moment_src, geo_ref, y_ref, bk_ref, gidx_ref, da_ref, q_ref = refs[n_wide : n_wide + 7]
    push_ref, mass_ref, val_ref, ohlo_ref, dr_ref, moment_ref, sem = refs[n_wide + 7 :]
    fetch = pltpu.make_async_copy(moment_src, moment_ref, sem)
    fetch.start()
    bases, slots, n_near = bk_ref.shape
    tiles = atoms // LANES
    top_rows = val_ref.shape[0] // 6

    def back_geometry(t, mine):
        here = pl.ds(pl.multiple_of(t * LANES, LANES), LANES)
        ux, uy, uz, back, soft, fj = [geo_ref[i, :, here] for i in range(6)]
        dy = [None] * ORDERS
        ds = None
        for n in range(bases):
            basis = bk_ref[n, :, here]
            db = None
            for l in range(ORDERS):
                g = row(da_ref[l, n : n + 1, here]) + fj * row(da_ref[l, bases + n : bases + n + 1, here])
                if l:
                    dy[l] = g * basis if dy[l] is None else dy[l] + g * basis
                    db = db + g * y_ref[l - 1, :, here]
                else:
                    db = g
            db = db * basis * ((1.0 + n) - soft)
            ds = db if ds is None else ds + db
        if mine:
            ds = ds + q_ref[0:8, here]
            for l in range(1, ORDERS):
                dy[l] = dy[l] + q_ref[8 * l : 8 * l + 8, here]
        dux = SQRT3 * dy[1] + SQRT15 * (uy * dy[4] + uz * dy[7] + ux * dy[8]) - SQRT5 * ux * dy[6]
        duy = SQRT3 * dy[2] + SQRT15 * (ux * dy[4] + uz * dy[5] - uy * dy[8]) - SQRT5 * uy * dy[6]
        duz = SQRT3 * dy[3] + SQRT15 * (uy * dy[5] + ux * dy[7]) + 2.0 * SQRT5 * uz * dy[6]
        along = ds - (ux * dux + uy * duy + uz * duz) * back
        for i, value in enumerate((dux * back + along * ux, duy * back + along * uy, duz * back + along * uz)):
            dr_ref[i, :, here] = value

    in_turns(0, tiles, lambda t: back_geometry(t, True))
    in_turns(tiles, n_near // LANES, lambda t: back_geometry(t, False))

    def place_tile(t):
        here = pl.ds(pl.multiple_of(t * LANES, LANES), LANES)
        gidx = gidx_ref[:, here]
        chunk_no = gidx >> 7
        place = gidx & 127
        parts = []
        for i in range(3):
            value = dr_ref[i, :, here]
            hi = value.astype(bf16).astype(f32)
            parts.append((hi, value - hi))
        chunk_ids = lax.broadcasted_iota(jnp.int32, (top_rows, LANES), 0)
        place_ids = lax.broadcasted_iota(jnp.int32, (LANES, LANES), 0)
        for k in range(slots):
            at = pl.ds(pl.multiple_of(k * n_near + t * LANES, LANES), LANES)
            hit = chunk_ids == row(chunk_no[k : k + 1, :], top_rows)
            for i in range(3):
                both = [jnp.where(hit, row(part[k : k + 1, :], top_rows), 0.0) for part in parts[i]]
                val_ref[2 * i * top_rows : 2 * (i + 1) * top_rows, at] = jnp.concatenate(both, axis=0).astype(bf16)
            ohlo_ref[:, at] = jnp.where(place_ids == row(place[k : k + 1, :], LANES), 1.0, 0.0).astype(bf16)

    in_turns(0, n_near // LANES, place_tile)
    landed = dot_nt(ohlo_ref[...], val_ref[...]).T
    fetch.wait()
    lines = push_ref.shape[0] // (n_wide + 1)
    for i in range(3):
        total = (
            landed[2 * i * top_rows : (2 * i + 1) * top_rows] + landed[(2 * i + 1) * top_rows : (2 * i + 2) * top_rows]
        )
        for g in range(n_wide):
            for t in range(tiles):
                cols = slice(t * LANES, (t + 1) * LANES)
                line = total[g * tiles + t : g * tiles + t + 1, :]
                if g < len(near):
                    here = slice(g * atoms + t * LANES, g * atoms + (t + 1) * LANES)
                    line = line - jnp.sum(dr_ref[i, :, here], axis=0, keepdims=True)
                line = -HALF_STEP * line
                at = i * tiles + t
                if g == 0:
                    line = line + moment_ref[i, :, cols]
                    push_ref[at : at + 1, :] = blocks[0][i : i + 1, cols]
                push_ref[(1 + g) * lines + at : (1 + g) * lines + at + 1, :] = line
                mass = HEAVY - (HEAVY - 1.0) * blocks[g][3:4, cols]
                mass_ref[g * lines + at : g * lines + at + 1, :] = mass
    if lines > 3 * tiles:
        for g in range(n_wide + 1):
            blank = slice(g * lines + 3 * tiles, (g + 1) * lines)
            push_ref[blank, :] = jnp.zeros((lines - 3 * tiles, LANES), f32)
            if g < n_wide:
                mass_ref[blank, :] = jnp.ones((lines - 3 * tiles, LANES), f32)


def in_hbm(x):
    return pltpu.with_memory_space_constraint(x, pltpu.HBM)


def run(name, body, operands, results, scratch=(), far=(), cost=None):
    sizes = [math.prod(x.shape) * x.dtype.itemsize for i, x in enumerate(operands) if i not in far]
    sizes += [math.prod(shape) * jnp.dtype(dtype).itemsize for shape, dtype in results]
    sizes += [math.prod(x.shape) * x.dtype.itemsize for x in scratch if x.memory_space == pltpu.VMEM]
    limit = sum(sizes) + 4 * MIB
    specs = [pl.BlockSpec(memory_space=pltpu.HBM if i in far else pltpu.VMEM) for i in range(len(operands))]
    return pl.pallas_call(
        body,
        out_shape=tuple(jax.ShapeDtypeStruct(shape, dtype) for shape, dtype in results),
        in_specs=specs,
        out_specs=tuple(pl.BlockSpec(memory_space=pltpu.VMEM) for _ in results),
        scratch_shapes=list(scratch),
        compiler_params=pltpu.CompilerParams(vmem_limit_bytes=limit),
        cost_estimate=cost,
        name=name,
    )(*[in_hbm(x) if i in far else x for i, x in enumerate(operands)])


def choose(block, embedding, radial_one, radial_two, mix_one, mix_two, read_one, read_two):
    atoms = block.shape[1]
    slots = block.shape[0] - HEAD
    chan = embedding.shape[1]
    bases = radial_one.shape[0]
    weights = (embedding, radial_one, radial_two, mix_one, mix_two, read_one[None], read_two[None])
    return run(
        "choose",
        choose_kernel,
        (block, *weights),
        (
            ((2 * atoms, slots * atoms), bf16),
            ((chan, 8 * bases), bf16),
            ((chan, 4 * bases), bf16),
            ((chan, LANES), f32),
            ((4 * bases, 2 * chan), bf16),
            ((2 * bases, 2 * chan), bf16),
            ((2, 2 * chan, 3 * chan), bf16),
            ((2, 3, 2 * chan, chan), bf16),
        ),
        [pltpu.VMEM(w.shape, f32) for w in weights] + [pltpu.SemaphoreType.DMA((len(weights),))],
        range(1, 1 + len(weights)),
        cost=pl.CostEstimate(flops=2 * 10**9, bytes_accessed=2 * 10**6, transcendentals=0),
    )


def pushes(plan, blocks, momenta, chosen):
    atoms, near, wide, _, _ = plan
    oh, rrc, r2c, sides, rrr, r2r, mixa, mixt = chosen
    chan = rrc.shape[0]
    bases = r2r.shape[0] // 2
    slots = blocks[0].shape[0] - HEAD
    n_near = len(near) * atoms
    edges = slots * atoms
    top_rows = -(-len(wide) * atoms // LANES // 8) * 8
    lines = line_count(atoms)
    geo, y, yb, bk, bt, gidx, pick = run(
        "edges",
        functools.partial(edge_kernel, plan),
        blocks,
        (
            ((6, slots, n_near), f32),
            ((ORDERS - 1, slots, n_near), f32),
            ((ORDERS - 1, slots, 8, atoms), f32),
            ((bases, slots, n_near), f32),
            ((slots, 2 * bases, n_near), f32),
            ((slots, n_near), jnp.int32),
            ((n_near, atoms), bf16),
        ),
    )
    m1, sp1, hs = run(
        "first",
        functools.partial(first_kernel, plan),
        (*blocks, y, bt, rrc, sides, mixa),
        (((ORDERS, chan, n_near), f32), ((chan, n_near), f32), ((2 * chan, n_near), bf16)),
        [pltpu.VMEM((ORDERS, 8 * bases, n_near), bf16), pltpu.VMEM((8, n_near), f32)],
    )
    hj, w, car = run(
        "gather",
        gather_kernel,
        (hs, oh, pick, bt, r2c),
        (((chan, edges), f32),) * 3,
        [pltpu.VMEM((2 * chan, 2 * atoms), bf16)],
    )
    m2, dinv = run(
        "moments",
        moment_kernel,
        (car, yb, mixa, mixt, sides),
        (((ORDERS, chan, atoms), f32), ((3 * chan, atoms), f32)),
        [pltpu.VMEM((3 * chan, atoms), f32)],
    )
    dhe, q = run(
        "back_second",
        back_second_kernel,
        (m2, dinv, car, hj, w, yb, bt, geo, r2r),
        (((2 * chan, edges), bf16), ((8 * ORDERS, atoms), f32)),
        [pltpu.VMEM((2 * chan, edges), bf16), pltpu.VMEM((ORDERS, 8 * slots, atoms), f32)],
    )
    (dh,) = run("scatter", scatter_kernel, (oh, pick, dhe, sides), (((chan, n_near), f32),))
    (da,) = run("back_first", back_first_kernel, (dh, sp1, m1, mixt, rrr), (((ORDERS, 2 * bases, n_near), f32),))
    return run(
        "back_edges",
        functools.partial(back_edge_kernel, plan),
        (*blocks, momenta, geo, y, bk, gidx, da, q),
        ((((len(wide) + 1) * lines, LANES), f32), ((len(wide) * lines, LANES), f32)),
        [
            pltpu.VMEM((6 * top_rows, slots * n_near), bf16),
            pltpu.VMEM((LANES, slots * n_near), bf16),
            pltpu.VMEM((3, slots, n_near), f32),
            pltpu.VMEM(momenta.shape, f32),
            pltpu.SemaphoreType.DMA(()),
        ],
        (len(blocks),),
    )


def line_count(atoms):
    return -(-3 * (atoms // LANES) // 8) * 8


def ring_plan(domains, atoms):
    near = list(dict.fromkeys(o % domains for o in (0, 1, -1)))
    wide = list(dict.fromkeys(near + [o % domains for o in (2, -2)]))
    before = tuple(wide.index((o - 1) % domains) for o in near)
    after = tuple(wide.index((o + 1) % domains) for o in near)
    return atoms, tuple(near), tuple(wide), before, after


def mode_turns(bead_total):
    bead = np.arange(bead_total, dtype=np.float64)[:, None]
    mode = np.arange(bead_total, dtype=np.float64)[None, :]
    phase = 2.0 * np.pi * bead * mode / bead_total
    half_total = bead_total // 2
    table = math.sqrt(2.0 / bead_total) * np.where(mode < half_total, np.cos(phase), np.sin(phase))
    table = np.where(mode == half_total, np.cos(np.pi * bead) / math.sqrt(bead_total), table)
    table = np.where(mode == 0, 1.0 / math.sqrt(bead_total), table)
    angles = bead_total * np.sin(np.pi * mode[0] / bead_total)
    safe = np.where(mode[0] == 0, 1.0, angles)
    reach = np.where(mode[0] == 0, STEP, STEP * np.sin(angles) / safe)
    stiff = angles * np.sin(angles) / STEP
    return [[float(x) for x in (table * factor[None, :]) @ table[0]] for factor in (np.cos(angles), reach, stiff)]


def pack_kernel(coord_src, species_src, send_src, slot_src, block_ref, coord_ref, species_ref, send_ref, slot_ref, sems):
    pairs = ((coord_src, coord_ref), (species_src, species_ref), (send_src, send_ref), (slot_src, slot_ref))
    fetches = [pltpu.make_async_copy(src, dst, sems.at[i]) for i, (src, dst) in enumerate(pairs)]
    for fetch in fetches:
        fetch.start()
    for fetch in fetches:
        fetch.wait()
    atoms = block_ref.shape[1]
    for i in range(3):
        block_ref[i : i + 1, :] = coord_ref[i]
    block_ref[3:4, :] = species_ref[...].astype(f32)
    block_ref[4:5, :] = send_ref[...].astype(f32)
    block_ref[5:HEAD, :] = jnp.zeros((HEAD - 5, atoms), f32)
    block_ref[HEAD:, :] = slot_ref[...].astype(f32)


def turn_kernel(shape, bead_ref, domain_ref, mass_ref, *refs):
    outer, inner, domains, wide = shape
    message_ref = refs[outer]
    turns = mode_turns(outer * inner)
    lines = mass_ref.shape[0] // len(wide)
    my_domain = domain_ref[0]
    my_inner = lax.rem(bead_ref[0], inner)
    if domains > len(wide):
        message_ref[...] = jnp.zeros_like(message_ref)
    masses = [mass_ref[g * lines : (g + 1) * lines, :] for g in range(len(wide))]
    sources = []
    for z in range(outer):
        sources.append([refs[z][g * lines : (g + 1) * lines, :] for g in range(len(wide) + 1)])
    for s in range(inner):
        wraps = jnp.full((lines, LANES), my_inner + s) >= inner
        weights = []
        for turn in turns:
            row_of = []
            for z in range(outer):
                there = turn[(z * inner + s) % (outer * inner)]
                round_it = turn[(z * inner + s - inner) % (outer * inner)]
                row_of.append(jnp.where(wraps, jnp.full((lines, LANES), round_it), jnp.full((lines, LANES), there)))
            weights.append(row_of)
        to_inner = lax.rem(my_inner + s, inner)
        for g in range(len(wide)):
            turned = sum(weights[0][z] * sources[z][1 + g] for z in range(outer))
            drift = sum(weights[1][z] * sources[z][1 + g] for z in range(outer))
            new_q = drift / masses[g]
            new_p = turned
            if g == 0:
                new_q = new_q + sum(weights[0][z] * sources[z][0] for z in range(outer))
                new_p = new_p - masses[g] * sum(weights[2][z] * sources[z][0] for z in range(outer))
            to = to_inner * domains + lax.rem(my_domain + wide[g], domains)
            message_ref[to, 0:lines, :] = new_q
            message_ref[to, lines:, :] = new_p


def sum_kernel(arrived_ref, q_ref, p_ref):
    total = arrived_ref[0]
    for i in range(1, arrived_ref.shape[0]):
        total = total + arrived_ref[i]
    lines = total.shape[0] // 2
    tiles = q_ref.shape[2] // LANES
    for i in range(3):
        for t in range(tiles):
            at = i * tiles + t
            q_ref[i, :, t * LANES : (t + 1) * LANES] = total[at : at + 1]
            p_ref[i, :, t * LANES : (t + 1) * LANES] = total[lines + at : lines + at + 1]


def shards(
    positions, momenta, species, neighbours, send_list, embedding, radial_one, radial_two, mix_one, mix_two,
    read_one, read_two,
):
    slots, atoms = neighbours.shape
    domains = lax.axis_size("space")
    beads = lax.axis_size("bead")
    inner = next(d for d in range(1, beads + 1) if beads % d == 0 and d * d >= beads)
    outer = beads // inner
    plan = ring_plan(domains, atoms)
    wide = plan[2]
    vmem = pl.BlockSpec(memory_space=pltpu.VMEM)
    smem = pl.BlockSpec(memory_space=pltpu.SMEM)
    far = pl.BlockSpec(memory_space=pltpu.HBM)
    small = pltpu.CompilerParams(vmem_limit_bytes=4 * MIB)
    coord_rows = jnp.transpose(positions, (1, 0, 2))
    moment_rows = jnp.transpose(momenta, (1, 0, 2))
    block = pl.pallas_call(
        pack_kernel,
        out_shape=jax.ShapeDtypeStruct((HEAD + slots, atoms), f32),
        in_specs=[far] * 4,
        out_specs=vmem,
        scratch_shapes=[
            pltpu.VMEM(coord_rows.shape, f32),
            pltpu.VMEM((1, atoms), jnp.int32),
            pltpu.VMEM((1, atoms), jnp.int32),
            pltpu.VMEM((slots, atoms), jnp.int32),
            pltpu.SemaphoreType.DMA((4,)),
        ],
        compiler_params=small,
        name="pack",
    )(in_hbm(coord_rows), in_hbm(species[None]), in_hbm(send_list[None]), in_hbm(neighbours))
    blocks = [block]
    for offset in wide[1:]:
        blocks.append(lax.ppermute(block, "space", [(i, (i - offset) % domains) for i in range(domains)]))
    chosen = choose(block, embedding, radial_one, radial_two, mix_one, mix_two, read_one, read_two)
    pushed, masses = pushes(plan, blocks, moment_rows, chosen)
    sources = [pushed]
    for z in range(1, outer):
        sources.append(lax.ppermute(pushed, "bead", [(b, (b + z * inner) % beads) for b in range(beads)]))
    here = [lax.axis_index(axis).astype(jnp.int32).reshape(1) for axis in ("bead", "space")]
    lines = line_count(atoms)
    messages = pl.pallas_call(
        functools.partial(turn_kernel, (outer, inner, domains, wide)),
        out_shape=jax.ShapeDtypeStruct((inner * domains, 2 * lines, LANES), f32),
        in_specs=[smem, smem, vmem] + [vmem] * outer,
        out_specs=vmem,
        compiler_params=small,
        name="turn",
    )(*here, masses, *sources)
    rows = [[z * inner * domains + i for i in range(inner * domains)] for z in range(outer)]
    arrived = lax.all_to_all(messages, ("bead", "space"), 0, 0, axis_index_groups=rows, tiled=True)
    new_q, new_p = pl.pallas_call(
        sum_kernel,
        out_shape=(jax.ShapeDtypeStruct((3, 1, atoms), f32),) * 2,
        in_specs=[vmem],
        out_specs=(vmem, vmem),
        compiler_params=small,
        name="sum",
    )(arrived)
    return (jnp.transpose(new_q, (1, 0, 2)), jnp.transpose(new_p, (1, 0, 2)))


def solution(mesh):
    placed = (
        P("bead", None, "space"),
        P("bead", None, "space"),
        P("space"),
        P(None, "space"),
        P("space"),
        P(),
        P(),
        P(),
        P(),
        P(),
        P(),
        P(),
    )
    return jax.shard_map(
        shards,
        mesh=mesh,
        in_specs=placed,
        out_specs=(P("bead", None, "space"), P("bead", None, "space")),
        check_vma=False,
    )
```

```python
import functools
import math

import jax
import jax.numpy as jnp
import numpy as np
from jax import lax
from jax.experimental import pallas as pl
from jax.experimental.pallas import tpu as pltpu
from jax.sharding import PartitionSpec as P

STEP = 2.0
HALF_STEP = 1.0
HEAVY = 16.0
SQRT3 = math.sqrt(3.0)
SQRT5 = math.sqrt(5.0)
SQRT15 = math.sqrt(15.0)
LANES = 128
ORDERS = 9
GROUP = (0, 1, 1, 1, 2, 2, 2, 2, 2)
HEAD = 8
MIB = 1024 * 1024
f32 = jnp.float32
bf16 = jnp.bfloat16


def split(x):
    hi = x.astype(bf16)
    return hi, (x - hi.astype(f32)).astype(bf16)


def split_rows(x):
    hi = x.astype(bf16).astype(f32)
    return jnp.concatenate([hi, x - hi], axis=0)


def dot(a, b):
    return jnp.dot(a, b, preferred_element_type=f32)


def dot_nt(a, b):
    return lax.dot_general(a, b, (((1,), (1,)), ((), ())), preferred_element_type=f32)


def in_turns(start, stop, step, most=4):
    per_turn = next(n for n in range(most, 0, -1) if (stop - start) % n == 0)

    def turn(i, carry):
        for j in range(per_turn):
            step(start + i * per_turn + j)
        return carry

    lax.fori_loop(0, (stop - start) // per_turn, turn, 0)


def row(x, rows=8):
    return jnp.broadcast_to(x, (rows, x.shape[1]))


def lookup(chunks, wanted, position):
    out = None
    for number, chunk in chunks:
        got = jnp.take_along_axis(row(chunk), position, axis=1, mode="promise_in_bounds")
        out = got if out is None else jnp.where(wanted == number, got, out)
    return out


def harmonics(ux, uy, uz):
    return [
        None,
        SQRT3 * ux,
        SQRT3 * uy,
        SQRT3 * uz,
        SQRT15 * ux * uy,
        SQRT15 * uy * uz,
        0.5 * SQRT5 * (2.0 * uz * uz - ux * ux - uy * uy),
        SQRT15 * ux * uz,
        0.5 * SQRT15 * (ux * ux - uy * uy),
    ]


def silu_parts(v):
    gate = 1.0 / (1.0 + jnp.exp(-v))
    return v * gate, gate * (1.0 + v * (1.0 - gate))


def choose_kernel(block_ref, *refs):
    sources = refs[:7]
    oh_ref, rrc_ref, r2c_ref, side_ref, rrr_ref, r2r_ref, mixa_ref, mixt_ref = refs[7:15]
    held = refs[15:22]
    sems = refs[22]
    emb_ref, rad1_ref, rad2_ref, mix1_ref, mix2_ref, read1_ref, read2_ref = held
    fetches = [pltpu.make_async_copy(src, dst, sems.at[i]) for i, (src, dst) in enumerate(zip(sources, held))]
    for fetch in fetches:
        fetch.start()
    chan = emb_ref.shape[1]
    bases = rad1_ref.shape[0]
    atoms = block_ref.shape[1]
    slots = block_ref.shape[0] - HEAD

    ids16 = lax.broadcasted_iota(jnp.int32, (LANES, atoms), 0).astype(jnp.int16)
    one16 = jnp.ones((LANES, atoms), bf16)
    zero16 = jnp.zeros((LANES, atoms), bf16)
    for k in range(slots):
        slot = block_ref[HEAD + k : HEAD + k + 1, :].astype(jnp.int32)
        wanted = jnp.broadcast_to(slot, (LANES, atoms)).astype(jnp.int16)
        for r in range(oh_ref.shape[0] // LANES):
            hit = wanted - jnp.int16(r * LANES) == ids16
            oh_ref[r * LANES : (r + 1) * LANES, k * atoms : (k + 1) * atoms] = jnp.where(hit, one16, zero16)

    for fetch in fetches:
        fetch.wait()
    emb0 = emb_ref[0:1, :]
    emb_d = emb_ref[1:2, :] - emb0
    rr = jnp.concatenate([rad1_ref[...] * emb0, rad1_ref[...] * emb_d], axis=0) * (1.0 / slots)
    rr_hi = rr.astype(bf16).astype(f32)
    rr_lo = rr - rr_hi
    r2 = rad2_ref[...] * (1.0 / slots)
    r2_hi = r2.astype(bf16).astype(f32)
    r2_lo = r2 - r2_hi
    zeros = jnp.zeros((8, chan), f32)
    turned1 = jnp.concatenate([rr_hi, rr_hi, rr_lo, rr_lo] + [zeros] * 8, axis=0).T
    sides = jnp.concatenate([emb0, emb_d, read1_ref[...], read2_ref[...], zeros[:4]], axis=0)
    turned2 = jnp.concatenate([r2_hi, r2_hi, r2_lo, r2_lo] + [zeros] * 12, axis=0).T
    rrc_ref[...] = turned1[:, : 8 * bases].astype(bf16)
    r2c_ref[...] = turned2[:, : 4 * bases].astype(bf16)
    side_ref[...] = jnp.concatenate([sides] + [zeros] * 15, axis=0).T
    rrr_ref[...] = jnp.concatenate(
        [jnp.concatenate([rr_hi, rr_hi], axis=1), jnp.concatenate([rr_lo, jnp.zeros_like(rr_lo)], axis=1)], axis=0
    ).astype(bf16)
    r2r_ref[...] = jnp.concatenate(
        [jnp.concatenate([r2_hi, r2_hi], axis=1), jnp.concatenate([r2_lo, jnp.zeros_like(r2_lo)], axis=1)], axis=0
    ).astype(bf16)
    for i, ref in enumerate((mix1_ref, mix2_ref)):
        hi, lo = split(ref[...])
        mixa_ref[i, 0:chan, :] = hi
        mixa_ref[i, chan:, :] = lo
        for g in range(3):
            hi, lo = split(ref[:, g * chan : (g + 1) * chan].T)
            mixt_ref[i, g, 0:chan, :] = hi
            mixt_ref[i, g, chan:, :] = lo


def dot_parts(both, hi, lo):
    rows = both.shape[0] // 2
    first = dot(both, hi)
    return first[:rows] + first[rows:] + dot(both[:rows], lo)


def edge_kernel(plan, *refs):
    atoms, near, wide, before, after = plan
    n_wide = len(wide)
    blocks = refs[:n_wide]
    geo_ref, y_ref, yb_ref, bk_ref, bt_ref, gidx_ref, pick_ref = refs[n_wide:]
    bases = bk_ref.shape[0]
    slots = gidx_ref.shape[0]
    tiles = atoms // LANES
    half = atoms // 2
    half_tiles = half // LANES
    order_col = lax.broadcasted_iota(jnp.int32, (bases, LANES), 0).astype(f32)
    tables = []
    for quantity in range(4):
        chunks = []
        for g in range(n_wide):
            for t in range(tiles):
                chunks.append((g * tiles + t, blocks[g][quantity : quantity + 1, t * LANES : (t + 1) * LANES]))
        tables.append(chunks)
    for q in range(len(near)):
        ghosts = []
        for t in range(half_tiles):
            ghosts.append(
                (t, blocks[before[q]][4:5, half + t * LANES : half + (t + 1) * LANES] + float(before[q] * atoms))
            )
        for t in range(half_tiles):
            ghosts.append(
                (
                    half_tiles + tiles + t,
                    blocks[after[q]][4:5, t * LANES : (t + 1) * LANES] + float(after[q] * atoms),
                )
            )
        if q == 0:
            ids16 = lax.broadcasted_iota(jnp.int32, (pick_ref.shape[0], LANES), 0).astype(jnp.int16)
            one16 = jnp.ones(ids16.shape, bf16)
            zero16 = jnp.zeros(ids16.shape, bf16)
            for t, (_, chunk) in enumerate(ghosts):
                wanted = jnp.broadcast_to(chunk.astype(jnp.int32), ids16.shape).astype(jnp.int16)
                pick_ref[:, t * LANES : (t + 1) * LANES] = jnp.where(wanted == ids16, one16, zero16)
        for t in range(tiles):
            cols = slice(t * LANES, (t + 1) * LANES)
            here = slice(q * atoms + t * LANES, q * atoms + (t + 1) * LANES)
            slot = blocks[q][HEAD : HEAD + slots, cols].astype(jnp.int32)
            chunk_no = slot >> 7
            far = lookup(ghosts, chunk_no, slot & 127).astype(jnp.int32)
            own = (slot >= half) & (slot < half + atoms)
            gidx = jnp.where(own, slot + (q * atoms - half), far)
            gidx_ref[:, here] = gidx
            chunk_no = gidx >> 7
            place = gidx & 127
            xj, yj, zj, fj = [lookup(tables[i], chunk_no, place) for i in range(4)]
            rx = xj - row(blocks[q][0:1, cols])
            ry = yj - row(blocks[q][1:2, cols])
            rz = zj - row(blocks[q][2:3, cols])
            soft = jnp.sqrt(rx * rx + ry * ry + rz * rz + 1.0)
            back = 1.0 / soft
            ux, uy, uz = rx * back, ry * back, rz * back
            for i, value in enumerate((ux, uy, uz, back, soft, fj)):
                geo_ref[i, :, here] = value
            sphere = harmonics(ux, uy, uz)
            for l in range(1, ORDERS):
                y_ref[l - 1, :, here] = sphere[l]
                if q == 0:
                    for k in range(slots):
                        yb_ref[l - 1, k, :, cols] = row(sphere[l][k : k + 1, :])
            for n in range(bases):
                bk_ref[n, :, here] = jnp.exp(-0.5 * (soft - (1.0 + n)) ** 2)
            for k in range(slots):
                basis = jnp.exp(-0.5 * (row(soft[k : k + 1, :], bases) - (1.0 + order_col)) ** 2)
                bt_ref[k, 0:bases, here] = basis
                bt_ref[k, bases : 2 * bases, here] = basis * row(fj[k : k + 1, :], bases)


def first_kernel(plan, *refs):
    atoms, near, wide, _, _ = plan
    n_wide = len(wide)
    blocks = refs[:n_wide]
    y_ref, bt_ref, rrc_ref, side_ref, mixa_ref, m1_ref, sp1_ref, hid_ref, as_ref, flag_ref = refs[n_wide:]
    slots = bt_ref.shape[0]
    bases = bt_ref.shape[1] // 2
    chan = m1_ref.shape[1]
    n_near = m1_ref.shape[2]

    def sums(t):
        here = pl.ds(pl.multiple_of(t * LANES, LANES), LANES)
        low = [None] * ORDERS
        for k in range(slots):
            basis = bt_ref[k, :, here]
            for l in range(ORDERS):
                term = basis if l == 0 else basis * row(y_ref[l - 1, k : k + 1, here], 2 * bases)
                low[l] = term if low[l] is None else low[l] + term
        for l in range(ORDERS):
            both = split_rows(low[l]).astype(bf16)
            as_ref[l, 0 : 4 * bases, here] = both
            as_ref[l, 4 * bases : 8 * bases, here] = both

    in_turns(0, n_near // LANES, sums)
    for q in range(len(near)):
        flag_ref[0:1, q * atoms : (q + 1) * atoms] = blocks[q][3:4, :]
    wide_cols = 2 * LANES
    emb0_col = side_ref[:, 0:1]
    embd_col = side_ref[:, 1:2]

    def first(j):
        here = pl.ds(pl.multiple_of(j * wide_cols, wide_cols), wide_cols)
        inv = [None, None, None]
        for l in range(ORDERS):
            m = dot(rrc_ref[...], as_ref[l, :, here])
            m1_ref[l, :, here] = m
            inv[GROUP[l]] = m * m if inv[GROUP[l]] is None else inv[GROUP[l]] + m * m
        hi, lo = split(jnp.concatenate(inv, axis=0))
        value = dot_parts(mixa_ref[0], hi, lo)
        act, slope = silu_parts(value)
        sp1_ref[:, here] = slope
        hid_ref[:, here] = act + emb0_col + embd_col * flag_ref[0:1, here]

    in_turns(0, n_near // wide_cols, first)


def gather_kernel(hid_ref, gidx_ref, bt_ref, r2c_ref, hj_ref, w_ref, car_ref):
    slots = bt_ref.shape[0]
    bases = bt_ref.shape[1] // 2
    chan, n_near = hid_ref.shape
    atoms = hj_ref.shape[1] // slots

    for k in range(slots):
        here = slice(k * atoms, (k + 1) * atoms)
        basis = split_rows(bt_ref[k, 0:bases, 0:atoms])
        w_ref[:, here] = dot(r2c_ref[...], jnp.concatenate([basis, basis], axis=0).astype(bf16))

    def gather(t, carry):
        gidx = gidx_ref[:, pl.ds(pl.multiple_of(t * LANES, LANES), LANES)]
        for k in range(slots):
            at = pl.ds(pl.multiple_of(k * atoms + t * LANES, LANES), LANES)
            mine = row(gidx[k : k + 1, :])
            chunk_no = mine >> 7
            place = mine & 127
            for c in range(chan // 8):
                rows = slice(8 * c, 8 * c + 8)
                feat = None
                for chunk in range(n_near // LANES):
                    held = hid_ref[rows, chunk * LANES : (chunk + 1) * LANES]
                    got = jnp.take_along_axis(held, place, axis=1, mode="promise_in_bounds")
                    feat = got if feat is None else jnp.where(chunk_no == chunk, got, feat)
                hj_ref[rows, at] = feat
                car_ref[rows, at] = feat * w_ref[rows, at]
        return carry

    lax.fori_loop(0, atoms // LANES, gather, 0)


def moment_kernel(car_ref, yb_ref, mixa_ref, mixt_ref, side_ref, m2_ref, dinv_ref, inv_ref):
    slots = yb_ref.shape[1]
    chan, atoms = m2_ref.shape[1:]
    tiles = atoms // LANES
    wide_cols = 2 * LANES
    rows = 32
    groups = chan // rows

    def moments(step, carry):
        t = step // groups
        c = step % groups
        cols = pl.ds(pl.multiple_of(t * LANES, LANES), LANES)
        base = pl.multiple_of(c * rows, rows)
        acc = [[None] * ORDERS for _ in range(rows // 8)]
        for k in range(slots):
            at = pl.ds(pl.multiple_of(k * atoms + t * LANES, LANES), LANES)
            got = car_ref[pl.ds(base, rows), at]
            for l in range(ORDERS):
                yb = yb_ref[l - 1, k, :, cols] if l else None
                for h in range(rows // 8):
                    part = got[8 * h : 8 * h + 8]
                    term = part * yb if l else part
                    acc[h][l] = term if acc[h][l] is None else acc[h][l] + term
        for h in range(rows // 8):
            inv = [None] * 3
            for l in range(ORDERS):
                m2_ref[l, pl.ds(pl.multiple_of(base + 8 * h, 8), 8), cols] = acc[h][l]
                sq = acc[h][l] * acc[h][l]
                g = GROUP[l]
                inv[g] = sq if inv[g] is None else inv[g] + sq
            for g in range(3):
                inv_ref[pl.ds(pl.multiple_of(g * chan + base + 8 * h, 8), 8), cols] = inv[g]
        return carry

    lax.fori_loop(0, tiles * groups, moments, 0)
    read2_col = side_ref[:, 3:4]
    for t in range(atoms // wide_cols):
        cols = slice(t * wide_cols, (t + 1) * wide_cols)
        hi, lo = split(inv_ref[:, cols])
        _, slope = silu_parts(dot_parts(mixa_ref[1], hi, lo))
        hi, lo = split(slope * (2.0 * read2_col))
        for g in range(3):
            dinv_ref[g * chan : (g + 1) * chan, cols] = dot_parts(mixt_ref[1, g], hi, lo)


def back_second_kernel(m2_ref, dinv_ref, car_ref, hj_ref, w_ref, yb_ref, bt_ref, geo_ref, r2r_ref,
                       dhe_ref, q_ref, dw_ref, p_ref):
    slots = yb_ref.shape[1]
    bases = bt_ref.shape[1] // 2
    chan, atoms = m2_ref.shape[1:]
    tiles = atoms // LANES
    pairs = chan // 16
    k_step = slots // 2
    per_turn = 4 if pairs % 4 == 0 else 1

    def back_moments(step, carry):
        t = step // 2
        k0 = (step % 2) * k_step
        cols = pl.ds(pl.multiple_of(t * LANES, LANES), LANES)

        def one(c, acc):
            base = pl.multiple_of(c * 16, 16)
            dm = []
            scale = [dinv_ref[pl.ds(pl.multiple_of(g * chan + c * 16, 16), 16), cols] for g in range(3)]
            for l in range(ORDERS):
                dm.append(m2_ref[l, pl.ds(base, 16), cols] * scale[GROUP[l]])
            for kk in range(k_step):
                k = k0 + kk
                at = pl.ds(pl.multiple_of(k * atoms + t * LANES, LANES), LANES)
                got = car_ref[pl.ds(base, 16), at]
                out = [dm[0][:8], dm[0][8:]]
                for l in range(1, ORDERS):
                    yb = yb_ref[l - 1, k, :, cols]
                    i = kk * (ORDERS - 1) + l - 1
                    for h in range(2):
                        part = dm[l][8 * h : 8 * h + 8]
                        out[h] = out[h] + part * yb
                        acc[i] = acc[i] + part * got[8 * h : 8 * h + 8]
                dcar = jnp.concatenate(out, axis=0)
                for ref, other in ((dhe_ref, w_ref), (dw_ref, hj_ref)):
                    hi, lo = split(dcar * other[pl.ds(base, 16), at])
                    ref[pl.ds(base, 16), at] = hi
                    ref[pl.ds(pl.multiple_of(chan + c * 16, 16), 16), at] = lo

        def over(c, acc):
            acc = list(acc)
            for i in range(per_turn):
                one(per_turn * c + i, acc)
            return tuple(acc)

        start = tuple(jnp.zeros((8, LANES), f32) for _ in range(k_step * (ORDERS - 1)))
        acc = lax.fori_loop(0, pairs // per_turn, over, start)
        for kk in range(k_step):
            for l in range(1, ORDERS):
                p_ref[l, pl.ds(pl.multiple_of((k0 + kk) * 8, 8), 8), cols] = acc[kk * (ORDERS - 1) + l - 1]
        return carry

    lax.fori_loop(0, tiles * 2, back_moments, 0)
    for k in range(slots):
        here = slice(k * atoms, (k + 1) * atoms)
        both = dot(r2r_ref[...], dw_ref[:, here])
        dbasis = both[:bases] + both[bases:]
        basis = bt_ref[k, 0:bases, 0:atoms]
        reach = 1.0 + lax.broadcasted_iota(jnp.int32, (bases, atoms), 0).astype(f32)
        p_ref[0, k * 8 : k * 8 + 8, :] = dbasis * basis * (reach - row(geo_ref[4, k : k + 1, 0:atoms], bases))
    lane = lax.broadcasted_iota(jnp.int32, (slots, 16 * slots), 1)
    sub = lax.broadcasted_iota(jnp.int32, (slots, 16 * slots), 0)
    adder = jnp.where(((lane >> 3) & (slots - 1)) == sub, 1.0, 0.0).astype(bf16)
    for l in range(ORDERS):
        q_ref[8 * l : 8 * l + 8, :] = dot(adder, split_rows(p_ref[l, :, :]).astype(bf16))


def scatter_kernel(oh_ref, pick_ref, dhe_ref, side_ref, dh_ref):
    chan, n_near = dh_ref.shape
    atoms = pick_ref.shape[1]
    half = atoms // 2
    both = dot_nt(dhe_ref[...], oh_ref[...])
    ext = both[:chan] + both[chan:]
    hi, lo = split(jnp.concatenate([ext[:, :half], ext[:, half + atoms :]], axis=1))
    spread = dot_nt(jnp.concatenate([hi, lo], axis=0), pick_ref[...])
    spread = spread[:chan] + spread[chan:]
    dh_ref[:, 0:atoms] = spread[:, :atoms] + ext[:, half : half + atoms] + side_ref[:, 2:3]
    if n_near > atoms:
        dh_ref[:, atoms:] = spread[:, atoms:]


def back_first_kernel(dh_ref, sp1_ref, m1_ref, mixt_ref, rrr_ref, da_ref):
    n_near = sp1_ref.shape[1]
    rows = rrr_ref.shape[0] // 2
    wide_cols = 2 * LANES

    def back_first(j):
        here = pl.ds(pl.multiple_of(j * wide_cols, wide_cols), wide_cols)
        hi, lo = split(dh_ref[:, here] * sp1_ref[:, here] * 2.0)
        scale = [dot_parts(mixt_ref[0, g], hi, lo) for g in range(3)]
        for l in range(ORDERS):
            hi, lo = split(m1_ref[l, :, here] * scale[GROUP[l]])
            out = dot(rrr_ref[...], jnp.concatenate([hi, lo], axis=0))
            da_ref[l, :, here] = out[:rows] + out[rows:]

    in_turns(0, n_near // wide_cols, back_first)


def back_edge_kernel(plan, *refs):
    atoms, near, wide, _, _ = plan
    n_wide = len(wide)
    blocks = refs[:n_wide]
    moment_src, geo_ref, y_ref, bk_ref, gidx_ref, da_ref, q_ref = refs[n_wide : n_wide + 7]
    push_ref, mass_ref, val_ref, ohlo_ref, dr_ref, moment_ref, sem = refs[n_wide + 7 :]
    fetch = pltpu.make_async_copy(moment_src, moment_ref, sem)
    fetch.start()
    bases, slots, n_near = bk_ref.shape
    tiles = atoms // LANES
    top_rows = val_ref.shape[0] // 6

    def back_geometry(t, mine):
        here = pl.ds(pl.multiple_of(t * LANES, LANES), LANES)
        ux, uy, uz, back, soft, fj = [geo_ref[i, :, here] for i in range(6)]
        dy = [None] * ORDERS
        ds = None
        for n in range(bases):
            basis = bk_ref[n, :, here]
            db = None
            for l in range(ORDERS):
                g = row(da_ref[l, n : n + 1, here]) + fj * row(da_ref[l, bases + n : bases + n + 1, here])
                if l:
                    dy[l] = g * basis if dy[l] is None else dy[l] + g * basis
                    db = db + g * y_ref[l - 1, :, here]
                else:
                    db = g
            db = db * basis * ((1.0 + n) - soft)
            ds = db if ds is None else ds + db
        if mine:
            ds = ds + q_ref[0:8, here]
            for l in range(1, ORDERS):
                dy[l] = dy[l] + q_ref[8 * l : 8 * l + 8, here]
        dux = SQRT3 * dy[1] + SQRT15 * (uy * dy[4] + uz * dy[7] + ux * dy[8]) - SQRT5 * ux * dy[6]
        duy = SQRT3 * dy[2] + SQRT15 * (ux * dy[4] + uz * dy[5] - uy * dy[8]) - SQRT5 * uy * dy[6]
        duz = SQRT3 * dy[3] + SQRT15 * (uy * dy[5] + ux * dy[7]) + 2.0 * SQRT5 * uz * dy[6]
        along = ds - (ux * dux + uy * duy + uz * duz) * back
        for i, value in enumerate((dux * back + along * ux, duy * back + along * uy, duz * back + along * uz)):
            dr_ref[i, :, here] = value

    in_turns(0, tiles, lambda t: back_geometry(t, True))
    in_turns(tiles, n_near // LANES, lambda t: back_geometry(t, False))

    def place_tile(t):
        here = pl.ds(pl.multiple_of(t * LANES, LANES), LANES)
        gidx = gidx_ref[:, here]
        chunk_no = gidx >> 7
        place = gidx & 127
        parts = []
        for i in range(3):
            value = dr_ref[i, :, here]
            hi = value.astype(bf16).astype(f32)
            parts.append((hi, value - hi))
        chunk_ids = lax.broadcasted_iota(jnp.int32, (top_rows, LANES), 0)
        place_ids = lax.broadcasted_iota(jnp.int32, (LANES, LANES), 0)
        for k in range(slots):
            at = pl.ds(pl.multiple_of(k * n_near + t * LANES, LANES), LANES)
            hit = chunk_ids == row(chunk_no[k : k + 1, :], top_rows)
            for i in range(3):
                both = [jnp.where(hit, row(part[k : k + 1, :], top_rows), 0.0) for part in parts[i]]
                val_ref[2 * i * top_rows : 2 * (i + 1) * top_rows, at] = jnp.concatenate(both, axis=0).astype(bf16)
            ohlo_ref[:, at] = jnp.where(place_ids == row(place[k : k + 1, :], LANES), 1.0, 0.0).astype(bf16)

    in_turns(0, n_near // LANES, place_tile)
    landed = dot_nt(ohlo_ref[...], val_ref[...]).T
    fetch.wait()
    lines = push_ref.shape[0] // (n_wide + 1)
    for i in range(3):
        total = (
            landed[2 * i * top_rows : (2 * i + 1) * top_rows] + landed[(2 * i + 1) * top_rows : (2 * i + 2) * top_rows]
        )
        for g in range(n_wide):
            for t in range(tiles):
                cols = slice(t * LANES, (t + 1) * LANES)
                line = total[g * tiles + t : g * tiles + t + 1, :]
                if g < len(near):
                    here = slice(g * atoms + t * LANES, g * atoms + (t + 1) * LANES)
                    line = line - jnp.sum(dr_ref[i, :, here], axis=0, keepdims=True)
                line = -HALF_STEP * line
                at = i * tiles + t
                if g == 0:
                    line = line + moment_ref[i, :, cols]
                    push_ref[at : at + 1, :] = blocks[0][i : i + 1, cols]
                push_ref[(1 + g) * lines + at : (1 + g) * lines + at + 1, :] = line
                mass = HEAVY - (HEAVY - 1.0) * blocks[g][3:4, cols]
                mass_ref[g * lines + at : g * lines + at + 1, :] = mass
    if lines > 3 * tiles:
        for g in range(n_wide + 1):
            blank = slice(g * lines + 3 * tiles, (g + 1) * lines)
            push_ref[blank, :] = jnp.zeros((lines - 3 * tiles, LANES), f32)
            if g < n_wide:
                mass_ref[blank, :] = jnp.ones((lines - 3 * tiles, LANES), f32)


def in_hbm(x):
    return pltpu.with_memory_space_constraint(x, pltpu.HBM)


def run(name, body, operands, results, scratch=(), far=(), cost=None):
    sizes = [math.prod(x.shape) * x.dtype.itemsize for i, x in enumerate(operands) if i not in far]
    sizes += [math.prod(shape) * jnp.dtype(dtype).itemsize for shape, dtype in results]
    sizes += [math.prod(x.shape) * x.dtype.itemsize for x in scratch if x.memory_space == pltpu.VMEM]
    limit = sum(sizes) + 4 * MIB
    specs = [pl.BlockSpec(memory_space=pltpu.HBM if i in far else pltpu.VMEM) for i in range(len(operands))]
    return pl.pallas_call(
        body,
        out_shape=tuple(jax.ShapeDtypeStruct(shape, dtype) for shape, dtype in results),
        in_specs=specs,
        out_specs=tuple(pl.BlockSpec(memory_space=pltpu.VMEM) for _ in results),
        scratch_shapes=list(scratch),
        compiler_params=pltpu.CompilerParams(vmem_limit_bytes=limit),
        cost_estimate=cost,
        name=name,
    )(*[in_hbm(x) if i in far else x for i, x in enumerate(operands)])


def choose(block, embedding, radial_one, radial_two, mix_one, mix_two, read_one, read_two):
    atoms = block.shape[1]
    slots = block.shape[0] - HEAD
    chan = embedding.shape[1]
    bases = radial_one.shape[0]
    weights = (embedding, radial_one, radial_two, mix_one, mix_two, read_one[None], read_two[None])
    return run(
        "choose",
        choose_kernel,
        (block, *weights),
        (
            ((2 * atoms, slots * atoms), bf16),
            ((chan, 8 * bases), bf16),
            ((chan, 4 * bases), bf16),
            ((chan, LANES), f32),
            ((4 * bases, 2 * chan), bf16),
            ((2 * bases, 2 * chan), bf16),
            ((2, 2 * chan, 3 * chan), bf16),
            ((2, 3, 2 * chan, chan), bf16),
        ),
        [pltpu.VMEM(w.shape, f32) for w in weights] + [pltpu.SemaphoreType.DMA((len(weights),))],
        range(1, 1 + len(weights)),
        cost=pl.CostEstimate(flops=2 * 10**9, bytes_accessed=2 * 10**6, transcendentals=0),
    )


def pushes(plan, blocks, momenta, chosen):
    atoms, near, wide, _, _ = plan
    oh, rrc, r2c, sides, rrr, r2r, mixa, mixt = chosen
    chan = rrc.shape[0]
    bases = r2r.shape[0] // 2
    slots = blocks[0].shape[0] - HEAD
    n_near = len(near) * atoms
    edges = slots * atoms
    top_rows = -(-len(wide) * atoms // LANES // 8) * 8
    lines = line_count(atoms)
    geo, y, yb, bk, bt, gidx, pick = run(
        "edges",
        functools.partial(edge_kernel, plan),
        blocks,
        (
            ((6, slots, n_near), f32),
            ((ORDERS - 1, slots, n_near), f32),
            ((ORDERS - 1, slots, 8, atoms), f32),
            ((bases, slots, n_near), f32),
            ((slots, 2 * bases, n_near), f32),
            ((slots, n_near), jnp.int32),
            ((n_near, atoms), bf16),
        ),
    )
    m1, sp1, hid = run(
        "first",
        functools.partial(first_kernel, plan),
        (*blocks, y, bt, rrc, sides, mixa),
        (((ORDERS, chan, n_near), f32), ((chan, n_near), f32), ((chan, n_near), f32)),
        [pltpu.VMEM((ORDERS, 8 * bases, n_near), bf16), pltpu.VMEM((8, n_near), f32)],
    )
    hj, w, car = run(
        "gather",
        gather_kernel,
        (hid, gidx, bt, r2c),
        (((chan, edges), f32),) * 3,
    )
    m2, dinv = run(
        "moments",
        moment_kernel,
        (car, yb, mixa, mixt, sides),
        (((ORDERS, chan, atoms), f32), ((3 * chan, atoms), f32)),
        [pltpu.VMEM((3 * chan, atoms), f32)],
    )
    dhe, q = run(
        "back_second",
        back_second_kernel,
        (m2, dinv, car, hj, w, yb, bt, geo, r2r),
        (((2 * chan, edges), bf16), ((8 * ORDERS, atoms), f32)),
        [pltpu.VMEM((2 * chan, edges), bf16), pltpu.VMEM((ORDERS, 8 * slots, atoms), f32)],
    )
    (dh,) = run("scatter", scatter_kernel, (oh, pick, dhe, sides), (((chan, n_near), f32),))
    (da,) = run("back_first", back_first_kernel, (dh, sp1, m1, mixt, rrr), (((ORDERS, 2 * bases, n_near), f32),))
    return run(
        "back_edges",
        functools.partial(back_edge_kernel, plan),
        (*blocks, momenta, geo, y, bk, gidx, da, q),
        ((((len(wide) + 1) * lines, LANES), f32), ((len(wide) * lines, LANES), f32)),
        [
            pltpu.VMEM((6 * top_rows, slots * n_near), bf16),
            pltpu.VMEM((LANES, slots * n_near), bf16),
            pltpu.VMEM((3, slots, n_near), f32),
            pltpu.VMEM(momenta.shape, f32),
            pltpu.SemaphoreType.DMA(()),
        ],
        (len(blocks),),
    )


def line_count(atoms):
    return -(-3 * (atoms // LANES) // 8) * 8


def ring_plan(domains, atoms):
    near = list(dict.fromkeys(o % domains for o in (0, 1, -1)))
    wide = list(dict.fromkeys(near + [o % domains for o in (2, -2)]))
    before = tuple(wide.index((o - 1) % domains) for o in near)
    after = tuple(wide.index((o + 1) % domains) for o in near)
    return atoms, tuple(near), tuple(wide), before, after


def mode_turns(bead_total):
    bead = np.arange(bead_total, dtype=np.float64)[:, None]
    mode = np.arange(bead_total, dtype=np.float64)[None, :]
    phase = 2.0 * np.pi * bead * mode / bead_total
    half_total = bead_total // 2
    table = math.sqrt(2.0 / bead_total) * np.where(mode < half_total, np.cos(phase), np.sin(phase))
    table = np.where(mode == half_total, np.cos(np.pi * bead) / math.sqrt(bead_total), table)
    table = np.where(mode == 0, 1.0 / math.sqrt(bead_total), table)
    angles = bead_total * np.sin(np.pi * mode[0] / bead_total)
    safe = np.where(mode[0] == 0, 1.0, angles)
    reach = np.where(mode[0] == 0, STEP, STEP * np.sin(angles) / safe)
    stiff = angles * np.sin(angles) / STEP
    return [[float(x) for x in (table * factor[None, :]) @ table[0]] for factor in (np.cos(angles), reach, stiff)]


def pack_kernel(coord_src, species_src, send_src, slot_src, block_ref, coord_ref, species_ref, send_ref, slot_ref, sems):
    pairs = ((coord_src, coord_ref), (species_src, species_ref), (send_src, send_ref), (slot_src, slot_ref))
    fetches = [pltpu.make_async_copy(src, dst, sems.at[i]) for i, (src, dst) in enumerate(pairs)]
    for fetch in fetches:
        fetch.start()
    for fetch in fetches:
        fetch.wait()
    atoms = block_ref.shape[1]
    for i in range(3):
        block_ref[i : i + 1, :] = coord_ref[i]
    block_ref[3:4, :] = species_ref[...].astype(f32)
    block_ref[4:5, :] = send_ref[...].astype(f32)
    block_ref[5:HEAD, :] = jnp.zeros((HEAD - 5, atoms), f32)
    block_ref[HEAD:, :] = slot_ref[...].astype(f32)


def turn_kernel(shape, bead_ref, domain_ref, mass_ref, *refs):
    outer, inner, domains, wide = shape
    message_ref = refs[outer]
    turns = mode_turns(outer * inner)
    lines = mass_ref.shape[0] // len(wide)
    my_domain = domain_ref[0]
    my_inner = lax.rem(bead_ref[0], inner)
    if domains > len(wide):
        message_ref[...] = jnp.zeros_like(message_ref)
    masses = [mass_ref[g * lines : (g + 1) * lines, :] for g in range(len(wide))]
    sources = []
    for z in range(outer):
        sources.append([refs[z][g * lines : (g + 1) * lines, :] for g in range(len(wide) + 1)])
    for s in range(inner):
        wraps = jnp.full((lines, LANES), my_inner + s) >= inner
        weights = []
        for turn in turns:
            row_of = []
            for z in range(outer):
                there = turn[(z * inner + s) % (outer * inner)]
                round_it = turn[(z * inner + s - inner) % (outer * inner)]
                row_of.append(jnp.where(wraps, jnp.full((lines, LANES), round_it), jnp.full((lines, LANES), there)))
            weights.append(row_of)
        to_inner = lax.rem(my_inner + s, inner)
        for g in range(len(wide)):
            turned = sum(weights[0][z] * sources[z][1 + g] for z in range(outer))
            drift = sum(weights[1][z] * sources[z][1 + g] for z in range(outer))
            new_q = drift / masses[g]
            new_p = turned
            if g == 0:
                new_q = new_q + sum(weights[0][z] * sources[z][0] for z in range(outer))
                new_p = new_p - masses[g] * sum(weights[2][z] * sources[z][0] for z in range(outer))
            to = to_inner * domains + lax.rem(my_domain + wide[g], domains)
            message_ref[to, 0:lines, :] = new_q
            message_ref[to, lines:, :] = new_p


def sum_kernel(arrived_ref, q_ref, p_ref):
    total = arrived_ref[0]
    for i in range(1, arrived_ref.shape[0]):
        total = total + arrived_ref[i]
    lines = total.shape[0] // 2
    tiles = q_ref.shape[2] // LANES
    for i in range(3):
        for t in range(tiles):
            at = i * tiles + t
            q_ref[i, :, t * LANES : (t + 1) * LANES] = total[at : at + 1]
            p_ref[i, :, t * LANES : (t + 1) * LANES] = total[lines + at : lines + at + 1]


def shards(
    positions, momenta, species, neighbours, send_list, embedding, radial_one, radial_two, mix_one, mix_two,
    read_one, read_two,
):
    slots, atoms = neighbours.shape
    domains = lax.axis_size("space")
    beads = lax.axis_size("bead")
    inner = next(d for d in range(1, beads + 1) if beads % d == 0 and d * d >= beads)
    outer = beads // inner
    plan = ring_plan(domains, atoms)
    wide = plan[2]
    vmem = pl.BlockSpec(memory_space=pltpu.VMEM)
    smem = pl.BlockSpec(memory_space=pltpu.SMEM)
    far = pl.BlockSpec(memory_space=pltpu.HBM)
    small = pltpu.CompilerParams(vmem_limit_bytes=4 * MIB)
    coord_rows = jnp.transpose(positions, (1, 0, 2))
    moment_rows = jnp.transpose(momenta, (1, 0, 2))
    block = pl.pallas_call(
        pack_kernel,
        out_shape=jax.ShapeDtypeStruct((HEAD + slots, atoms), f32),
        in_specs=[far] * 4,
        out_specs=vmem,
        scratch_shapes=[
            pltpu.VMEM(coord_rows.shape, f32),
            pltpu.VMEM((1, atoms), jnp.int32),
            pltpu.VMEM((1, atoms), jnp.int32),
            pltpu.VMEM((slots, atoms), jnp.int32),
            pltpu.SemaphoreType.DMA((4,)),
        ],
        compiler_params=small,
        name="pack",
    )(in_hbm(coord_rows), in_hbm(species[None]), in_hbm(send_list[None]), in_hbm(neighbours))
    blocks = [block]
    for offset in wide[1:]:
        blocks.append(lax.ppermute(block, "space", [(i, (i - offset) % domains) for i in range(domains)]))
    chosen = choose(block, embedding, radial_one, radial_two, mix_one, mix_two, read_one, read_two)
    pushed, masses = pushes(plan, blocks, moment_rows, chosen)
    sources = [pushed]
    for z in range(1, outer):
        sources.append(lax.ppermute(pushed, "bead", [(b, (b + z * inner) % beads) for b in range(beads)]))
    here = [lax.axis_index(axis).astype(jnp.int32).reshape(1) for axis in ("bead", "space")]
    lines = line_count(atoms)
    messages = pl.pallas_call(
        functools.partial(turn_kernel, (outer, inner, domains, wide)),
        out_shape=jax.ShapeDtypeStruct((inner * domains, 2 * lines, LANES), f32),
        in_specs=[smem, smem, vmem] + [vmem] * outer,
        out_specs=vmem,
        compiler_params=small,
        name="turn",
    )(*here, masses, *sources)
    rows = [[z * inner * domains + i for i in range(inner * domains)] for z in range(outer)]
    arrived = lax.all_to_all(messages, ("bead", "space"), 0, 0, axis_index_groups=rows, tiled=True)
    new_q, new_p = pl.pallas_call(
        sum_kernel,
        out_shape=(jax.ShapeDtypeStruct((3, 1, atoms), f32),) * 2,
        in_specs=[vmem],
        out_specs=(vmem, vmem),
        compiler_params=small,
        name="sum",
    )(arrived)
    return (jnp.transpose(new_q, (1, 0, 2)), jnp.transpose(new_p, (1, 0, 2)))


def solution(mesh):
    placed = (
        P("bead", None, "space"),
        P("bead", None, "space"),
        P("space"),
        P(None, "space"),
        P("space"),
        P(),
        P(),
        P(),
        P(),
        P(),
        P(),
        P(),
    )
    return jax.shard_map(
        shards,
        mesh=mesh,
        in_specs=placed,
        out_specs=(P("bead", None, "space"), P("bead", None, "space")),
        check_vma=False,
    )
```

```python
import functools
import math

import jax
import jax.numpy as jnp
import numpy as np
from jax import lax
from jax.experimental import pallas as pl
from jax.experimental.pallas import tpu as pltpu
from jax.sharding import PartitionSpec as P

STEP = 2.0
HALF_STEP = 1.0
HEAVY = 16.0
SQRT3 = math.sqrt(3.0)
SQRT5 = math.sqrt(5.0)
SQRT15 = math.sqrt(15.0)
LANES = 128
ORDERS = 9
GROUP = (0, 1, 1, 1, 2, 2, 2, 2, 2)
HEAD = 8
MIB = 1024 * 1024
f32 = jnp.float32
bf16 = jnp.bfloat16


def split(x):
    hi = x.astype(bf16)
    return hi, (x - hi.astype(f32)).astype(bf16)


def split_rows(x):
    hi = x.astype(bf16).astype(f32)
    return jnp.concatenate([hi, x - hi], axis=0)


def dot(a, b):
    return jnp.dot(a, b, preferred_element_type=f32)


def dot_nt(a, b):
    return lax.dot_general(a, b, (((1,), (1,)), ((), ())), preferred_element_type=f32)


def in_turns(start, stop, step, most=4):
    per_turn = next(n for n in range(most, 0, -1) if (stop - start) % n == 0)

    def turn(i, carry):
        for j in range(per_turn):
            step(start + i * per_turn + j)
        return carry

    lax.fori_loop(0, (stop - start) // per_turn, turn, 0)


def row(x, rows=8):
    return jnp.broadcast_to(x, (rows, x.shape[1]))


def lookup(chunks, wanted, position):
    out = None
    for number, chunk in chunks:
        got = jnp.take_along_axis(row(chunk), position, axis=1, mode="promise_in_bounds")
        out = got if out is None else jnp.where(wanted == number, got, out)
    return out


def harmonics(ux, uy, uz):
    return [
        None,
        SQRT3 * ux,
        SQRT3 * uy,
        SQRT3 * uz,
        SQRT15 * ux * uy,
        SQRT15 * uy * uz,
        0.5 * SQRT5 * (2.0 * uz * uz - ux * ux - uy * uy),
        SQRT15 * ux * uz,
        0.5 * SQRT15 * (ux * ux - uy * uy),
    ]


def silu_parts(v):
    gate = 1.0 / (1.0 + jnp.exp(-v))
    return v * gate, gate * (1.0 + v * (1.0 - gate))


def choose_kernel(block_ref, *refs):
    sources = refs[:7]
    oh_ref, rrc_ref, r2c_ref, side_ref, rrr_ref, r2r_ref, mixa_ref, mixt_ref = refs[7:15]
    held = refs[15:22]
    sems = refs[22]
    emb_ref, rad1_ref, rad2_ref, mix1_ref, mix2_ref, read1_ref, read2_ref = held
    fetches = [pltpu.make_async_copy(src, dst, sems.at[i]) for i, (src, dst) in enumerate(zip(sources, held))]
    for fetch in fetches:
        fetch.start()
    chan = emb_ref.shape[1]
    bases = rad1_ref.shape[0]
    atoms = block_ref.shape[1]
    slots = block_ref.shape[0] - HEAD

    ids16 = lax.broadcasted_iota(jnp.int32, (LANES, atoms), 0).astype(jnp.int16)
    one16 = jnp.ones((LANES, atoms), bf16)
    zero16 = jnp.zeros((LANES, atoms), bf16)
    for k in range(slots):
        slot = block_ref[HEAD + k : HEAD + k + 1, :].astype(jnp.int32)
        wanted = jnp.broadcast_to(slot, (LANES, atoms)).astype(jnp.int16)
        for r in range(oh_ref.shape[0] // LANES):
            hit = wanted - jnp.int16(r * LANES) == ids16
            oh_ref[r * LANES : (r + 1) * LANES, k * atoms : (k + 1) * atoms] = jnp.where(hit, one16, zero16)

    for fetch in fetches:
        fetch.wait()
    emb0 = emb_ref[0:1, :]
    emb_d = emb_ref[1:2, :] - emb0
    rr = jnp.concatenate([rad1_ref[...] * emb0, rad1_ref[...] * emb_d], axis=0) * (1.0 / slots)
    rr_hi = rr.astype(bf16).astype(f32)
    rr_lo = rr - rr_hi
    r2 = rad2_ref[...] * (1.0 / slots)
    r2_hi = r2.astype(bf16).astype(f32)
    r2_lo = r2 - r2_hi
    zeros = jnp.zeros((8, chan), f32)
    turned1 = jnp.concatenate([rr_hi, rr_hi, rr_lo, rr_lo] + [zeros] * 8, axis=0).T
    sides = jnp.concatenate([emb0, emb_d, read1_ref[...], read2_ref[...], zeros[:4]], axis=0)
    turned2 = jnp.concatenate([r2_hi, r2_hi, r2_lo, r2_lo] + [zeros] * 12, axis=0).T
    rrc_ref[...] = turned1[:, : 8 * bases].astype(bf16)
    r2c_ref[...] = turned2[:, : 4 * bases].astype(bf16)
    side_ref[...] = jnp.concatenate([sides] + [zeros] * 15, axis=0).T
    rrr_ref[...] = jnp.concatenate(
        [jnp.concatenate([rr_hi, rr_hi], axis=1), jnp.concatenate([rr_lo, jnp.zeros_like(rr_lo)], axis=1)], axis=0
    ).astype(bf16)
    r2r_ref[...] = jnp.concatenate(
        [jnp.concatenate([r2_hi, r2_hi], axis=1), jnp.concatenate([r2_lo, jnp.zeros_like(r2_lo)], axis=1)], axis=0
    ).astype(bf16)
    for i, ref in enumerate((mix1_ref, mix2_ref)):
        hi, lo = split(ref[...])
        mixa_ref[i, 0:chan, :] = hi
        mixa_ref[i, chan:, :] = lo
        for g in range(3):
            hi, lo = split(ref[:, g * chan : (g + 1) * chan].T)
            mixt_ref[i, g, 0:chan, :] = hi
            mixt_ref[i, g, chan:, :] = lo


def dot_parts(both, hi, lo):
    rows = both.shape[0] // 2
    first = dot(both, hi)
    return first[:rows] + first[rows:] + dot(both[:rows], lo)


def edge_kernel(plan, *refs):
    atoms, near, wide, before, after = plan
    n_wide = len(wide)
    blocks = refs[:n_wide]
    geo_ref, y_ref, yb_ref, bk_ref, bt_ref, gidx_ref, pick_ref = refs[n_wide:]
    bases = bk_ref.shape[0]
    slots = gidx_ref.shape[0]
    tiles = atoms // LANES
    half = atoms // 2
    half_tiles = half // LANES
    order_col = lax.broadcasted_iota(jnp.int32, (bases, LANES), 0).astype(f32)
    tables = []
    for quantity in range(4):
        chunks = []
        for g in range(n_wide):
            for t in range(tiles):
                chunks.append((g * tiles + t, blocks[g][quantity : quantity + 1, t * LANES : (t + 1) * LANES]))
        tables.append(chunks)
    for q in range(len(near)):
        ghosts = []
        for t in range(half_tiles):
            ghosts.append(
                (t, blocks[before[q]][4:5, half + t * LANES : half + (t + 1) * LANES] + float(before[q] * atoms))
            )
        for t in range(half_tiles):
            ghosts.append(
                (
                    half_tiles + tiles + t,
                    blocks[after[q]][4:5, t * LANES : (t + 1) * LANES] + float(after[q] * atoms),
                )
            )
        if q == 0:
            ids16 = lax.broadcasted_iota(jnp.int32, (pick_ref.shape[0], LANES), 0).astype(jnp.int16)
            one16 = jnp.ones(ids16.shape, bf16)
            zero16 = jnp.zeros(ids16.shape, bf16)
            for t, (_, chunk) in enumerate(ghosts):
                wanted = jnp.broadcast_to(chunk.astype(jnp.int32), ids16.shape).astype(jnp.int16)
                pick_ref[:, t * LANES : (t + 1) * LANES] = jnp.where(wanted == ids16, one16, zero16)
        for t in range(tiles):
            cols = slice(t * LANES, (t + 1) * LANES)
            here = slice(q * atoms + t * LANES, q * atoms + (t + 1) * LANES)
            slot = blocks[q][HEAD : HEAD + slots, cols].astype(jnp.int32)
            chunk_no = slot >> 7
            far = lookup(ghosts, chunk_no, slot & 127).astype(jnp.int32)
            own = (slot >= half) & (slot < half + atoms)
            gidx = jnp.where(own, slot + (q * atoms - half), far)
            gidx_ref[:, here] = gidx
            chunk_no = gidx >> 7
            place = gidx & 127
            xj, yj, zj, fj = [lookup(tables[i], chunk_no, place) for i in range(4)]
            rx = xj - row(blocks[q][0:1, cols])
            ry = yj - row(blocks[q][1:2, cols])
            rz = zj - row(blocks[q][2:3, cols])
            soft = jnp.sqrt(rx * rx + ry * ry + rz * rz + 1.0)
            back = 1.0 / soft
            ux, uy, uz = rx * back, ry * back, rz * back
            for i, value in enumerate((ux, uy, uz, back, soft, fj)):
                geo_ref[i, :, here] = value
            sphere = harmonics(ux, uy, uz)
            for l in range(1, ORDERS):
                y_ref[l - 1, :, here] = sphere[l]
                if q == 0:
                    for k in range(slots):
                        yb_ref[l - 1, k, :, cols] = row(sphere[l][k : k + 1, :])
            for n in range(bases):
                bk_ref[n, :, here] = jnp.exp(-0.5 * (soft - (1.0 + n)) ** 2)
            for k in range(slots):
                basis = jnp.exp(-0.5 * (row(soft[k : k + 1, :], bases) - (1.0 + order_col)) ** 2)
                bt_ref[k, 0:bases, here] = basis
                bt_ref[k, bases : 2 * bases, here] = basis * row(fj[k : k + 1, :], bases)


def first_kernel(plan, *refs):
    atoms, near, wide, _, _ = plan
    n_wide = len(wide)
    blocks = refs[:n_wide]
    y_ref, bt_ref, rrc_ref, side_ref, mixa_ref, m1_ref, sp1_ref, hid_ref, hs_ref, as_ref, flag_ref = refs[n_wide:]
    slots = bt_ref.shape[0]
    bases = bt_ref.shape[1] // 2
    chan = m1_ref.shape[1]
    n_near = m1_ref.shape[2]

    def sums(t):
        here = pl.ds(pl.multiple_of(t * LANES, LANES), LANES)
        low = [None] * ORDERS
        for k in range(slots):
            basis = bt_ref[k, :, here]
            for l in range(ORDERS):
                term = basis if l == 0 else basis * row(y_ref[l - 1, k : k + 1, here], 2 * bases)
                low[l] = term if low[l] is None else low[l] + term
        for l in range(ORDERS):
            both = split_rows(low[l]).astype(bf16)
            as_ref[l, 0 : 4 * bases, here] = both
            as_ref[l, 4 * bases : 8 * bases, here] = both

    in_turns(0, n_near // LANES, sums)
    for q in range(len(near)):
        flag_ref[0:1, q * atoms : (q + 1) * atoms] = blocks[q][3:4, :]
    wide_cols = 2 * LANES
    emb0_col = side_ref[:, 0:1]
    embd_col = side_ref[:, 1:2]

    def first(j):
        here = pl.ds(pl.multiple_of(j * wide_cols, wide_cols), wide_cols)
        inv = [None, None, None]
        for l in range(ORDERS):
            m = dot(rrc_ref[...], as_ref[l, :, here])
            m1_ref[l, :, here] = m
            inv[GROUP[l]] = m * m if inv[GROUP[l]] is None else inv[GROUP[l]] + m * m
        hi, lo = split(jnp.concatenate(inv, axis=0))
        value = dot_parts(mixa_ref[0], hi, lo)
        act, slope = silu_parts(value)
        sp1_ref[:, here] = slope
        hidden = act + emb0_col + embd_col * flag_ref[0:1, here]
        hid_ref[:, here] = hidden
        hi, lo = split(hidden)
        hs_ref[0:chan, here] = hi
        hs_ref[chan : 2 * chan, here] = lo

    in_turns(0, n_near // wide_cols, first)


def gather_kernel(hid_ref, hs_ref, oh_ref, pick_ref, gidx_ref, bt_ref, r2c_ref, hj_ref, w_ref, car_ref, ext_ref):
    slots = bt_ref.shape[0]
    bases = bt_ref.shape[1] // 2
    chan, n_near = hid_ref.shape
    atoms = hj_ref.shape[1] // slots
    half = atoms // 2
    by_lane = 2 * LANES if atoms > 2 * LANES else 0
    by_product = 2 * atoms - by_lane
    ghosts = dot(hs_ref[...], pick_ref[...]).astype(bf16)
    ext_ref[:, 0:half] = ghosts[:, :half]
    ext_ref[:, half : half + atoms] = hs_ref[:, 0:atoms]
    ext_ref[:, half + atoms :] = ghosts[:, half:]
    for k in range(slots):
        here = slice(k * atoms, (k + 1) * atoms)
        basis = split_rows(bt_ref[k, 0:bases, 0:atoms])
        w_ref[:, here] = dot(r2c_ref[...], jnp.concatenate([basis, basis], axis=0).astype(bf16))

    def gather(pair, carry):
        first = pl.multiple_of(pair * 2 * atoms, LANES)
        here = pl.ds(first, by_product)
        both = dot(ext_ref[...], oh_ref[:, here])
        wanted = gidx_ref[pl.ds(2 * pair + 1, 1), 0:atoms]
        for t in range(by_lane // LANES):
            at = pl.ds(pl.multiple_of(first + (by_product + t * LANES), LANES), LANES)
            start = atoms - by_lane + t * LANES
            mine = row(wanted[:, start : start + LANES])
            chunk_no = mine >> 7
            place = mine & 127
            for c in range(chan // 8):
                rows = slice(8 * c, 8 * c + 8)
                feat = None
                for chunk in range(n_near // LANES):
                    held = hid_ref[rows, chunk * LANES : (chunk + 1) * LANES]
                    got = jnp.take_along_axis(held, place, axis=1, mode="promise_in_bounds")
                    feat = got if feat is None else jnp.where(chunk_no == chunk, got, feat)
                hj_ref[rows, at] = feat
                car_ref[rows, at] = feat * w_ref[rows, at]
        feat = both[:chan] + both[chan:]
        hj_ref[:, here] = feat
        car_ref[:, here] = feat * w_ref[:, here]
        return carry

    lax.fori_loop(0, slots // 2, gather, 0)


def moment_kernel(car_ref, yb_ref, mixa_ref, mixt_ref, side_ref, m2_ref, dinv_ref, inv_ref):
    slots = yb_ref.shape[1]
    chan, atoms = m2_ref.shape[1:]
    tiles = atoms // LANES
    wide_cols = 2 * LANES
    rows = 32
    groups = chan // rows

    def moments(step, carry):
        t = step // groups
        c = step % groups
        cols = pl.ds(pl.multiple_of(t * LANES, LANES), LANES)
        base = pl.multiple_of(c * rows, rows)
        acc = [[None] * ORDERS for _ in range(rows // 8)]
        for k in range(slots):
            at = pl.ds(pl.multiple_of(k * atoms + t * LANES, LANES), LANES)
            got = car_ref[pl.ds(base, rows), at]
            for l in range(ORDERS):
                yb = yb_ref[l - 1, k, :, cols] if l else None
                for h in range(rows // 8):
                    part = got[8 * h : 8 * h + 8]
                    term = part * yb if l else part
                    acc[h][l] = term if acc[h][l] is None else acc[h][l] + term
        for h in range(rows // 8):
            inv = [None] * 3
            for l in range(ORDERS):
                m2_ref[l, pl.ds(pl.multiple_of(base + 8 * h, 8), 8), cols] = acc[h][l]
                sq = acc[h][l] * acc[h][l]
                g = GROUP[l]
                inv[g] = sq if inv[g] is None else inv[g] + sq
            for g in range(3):
                inv_ref[pl.ds(pl.multiple_of(g * chan + base + 8 * h, 8), 8), cols] = inv[g]
        return carry

    lax.fori_loop(0, tiles * groups, moments, 0)
    read2_col = side_ref[:, 3:4]
    for t in range(atoms // wide_cols):
        cols = slice(t * wide_cols, (t + 1) * wide_cols)
        hi, lo = split(inv_ref[:, cols])
        _, slope = silu_parts(dot_parts(mixa_ref[1], hi, lo))
        hi, lo = split(slope * (2.0 * read2_col))
        for g in range(3):
            dinv_ref[g * chan : (g + 1) * chan, cols] = dot_parts(mixt_ref[1, g], hi, lo)


def back_second_kernel(m2_ref, dinv_ref, car_ref, hj_ref, w_ref, yb_ref, dhe_ref, dw_ref, p_ref):
    slots = yb_ref.shape[1]
    chan, atoms = m2_ref.shape[1:]
    tiles = atoms // LANES
    pairs = chan // 16
    k_step = slots // 2
    per_turn = 4 if pairs % 4 == 0 else 1

    def back_moments(step, carry):
        t = step // 2
        k0 = (step % 2) * k_step
        cols = pl.ds(pl.multiple_of(t * LANES, LANES), LANES)

        def one(c, acc):
            base = pl.multiple_of(c * 16, 16)
            dm = []
            scale = [dinv_ref[pl.ds(pl.multiple_of(g * chan + c * 16, 16), 16), cols] for g in range(3)]
            for l in range(ORDERS):
                dm.append(m2_ref[l, pl.ds(base, 16), cols] * scale[GROUP[l]])
            for kk in range(k_step):
                k = k0 + kk
                at = pl.ds(pl.multiple_of(k * atoms + t * LANES, LANES), LANES)
                got = car_ref[pl.ds(base, 16), at]
                out = [dm[0][:8], dm[0][8:]]
                for l in range(1, ORDERS):
                    yb = yb_ref[l - 1, k, :, cols]
                    i = kk * (ORDERS - 1) + l - 1
                    for h in range(2):
                        part = dm[l][8 * h : 8 * h + 8]
                        out[h] = out[h] + part * yb
                        acc[i] = acc[i] + part * got[8 * h : 8 * h + 8]
                dcar = jnp.concatenate(out, axis=0)
                for ref, other in ((dhe_ref, w_ref), (dw_ref, hj_ref)):
                    hi, lo = split(dcar * other[pl.ds(base, 16), at])
                    ref[pl.ds(base, 16), at] = hi
                    ref[pl.ds(pl.multiple_of(chan + c * 16, 16), 16), at] = lo

        def over(c, acc):
            acc = list(acc)
            for i in range(per_turn):
                one(per_turn * c + i, acc)
            return tuple(acc)

        start = tuple(jnp.zeros((8, LANES), f32) for _ in range(k_step * (ORDERS - 1)))
        acc = lax.fori_loop(0, pairs // per_turn, over, start)
        for kk in range(k_step):
            for l in range(1, ORDERS):
                p_ref[l - 1, pl.ds(pl.multiple_of((k0 + kk) * 8, 8), 8), cols] = acc[kk * (ORDERS - 1) + l - 1]
        return carry

    lax.fori_loop(0, tiles * 2, back_moments, 0)


def scatter_kernel(oh_ref, pick_ref, dhe_ref, side_ref, dw_ref, p_ref, bt_ref, geo_ref, r2r_ref, gidx_ref,
                   dh_ref, q_ref, ohlo_ref, ds_ref):
    chan, n_near = dh_ref.shape
    slots = bt_ref.shape[0]
    bases = bt_ref.shape[1] // 2
    atoms = pick_ref.shape[1]
    half = atoms // 2
    both = dot_nt(dhe_ref[...], oh_ref[...])
    ids16 = lax.broadcasted_iota(jnp.int32, (LANES, n_near), 0).astype(jnp.int16)
    one16 = jnp.ones((LANES, n_near), bf16)
    zero16 = jnp.zeros((LANES, n_near), bf16)
    for k in range(slots):
        place = jnp.broadcast_to(gidx_ref[k : k + 1, :] & 127, (LANES, n_near)).astype(jnp.int16)
        ohlo_ref[:, k * n_near : (k + 1) * n_near] = jnp.where(place == ids16, one16, zero16)
    for k in range(slots):
        here = slice(k * atoms, (k + 1) * atoms)
        small = dot(r2r_ref[...], dw_ref[:, here])
        dbasis = small[:bases] + small[bases:]
        basis = bt_ref[k, 0:bases, 0:atoms]
        reach = 1.0 + lax.broadcasted_iota(jnp.int32, (bases, atoms), 0).astype(f32)
        ds_ref[k * 8 : k * 8 + 8, :] = dbasis * basis * (reach - row(geo_ref[4, k : k + 1, 0:atoms], bases))
    lane = lax.broadcasted_iota(jnp.int32, (slots, 16 * slots), 1)
    sub = lax.broadcasted_iota(jnp.int32, (slots, 16 * slots), 0)
    adder = jnp.where(((lane >> 3) & (slots - 1)) == sub, 1.0, 0.0).astype(bf16)
    for l in range(ORDERS):
        q_ref[8 * l : 8 * l + 8, :] = dot(adder, split_rows(p_ref[l - 1, :, :] if l else ds_ref[...]).astype(bf16))
    ext = both[:chan] + both[chan:]
    hi, lo = split(jnp.concatenate([ext[:, :half], ext[:, half + atoms :]], axis=1))
    spread = dot_nt(jnp.concatenate([hi, lo], axis=0), pick_ref[...])
    spread = spread[:chan] + spread[chan:]
    dh_ref[:, 0:atoms] = spread[:, :atoms] + ext[:, half : half + atoms] + side_ref[:, 2:3]
    if n_near > atoms:
        dh_ref[:, atoms:] = spread[:, atoms:]


def back_first_kernel(dh_ref, sp1_ref, m1_ref, mixt_ref, rrr_ref, da_ref):
    n_near = sp1_ref.shape[1]
    rows = rrr_ref.shape[0] // 2
    wide_cols = 2 * LANES

    def back_first(j):
        here = pl.ds(pl.multiple_of(j * wide_cols, wide_cols), wide_cols)
        hi, lo = split(dh_ref[:, here] * sp1_ref[:, here] * 2.0)
        scale = [dot_parts(mixt_ref[0, g], hi, lo) for g in range(3)]
        for l in range(ORDERS):
            hi, lo = split(m1_ref[l, :, here] * scale[GROUP[l]])
            out = dot(rrr_ref[...], jnp.concatenate([hi, lo], axis=0))
            da_ref[l, :, here] = out[:rows] + out[rows:]

    in_turns(0, n_near // wide_cols, back_first)


def back_edge_kernel(plan, *refs):
    atoms, near, wide, _, _ = plan
    n_wide = len(wide)
    blocks = refs[:n_wide]
    moment_src, geo_ref, y_ref, bk_ref, gidx_ref, da_ref, q_ref, ohlo_ref = refs[n_wide : n_wide + 8]
    push_ref, mass_ref, val_ref, dr_ref, moment_ref, sem = refs[n_wide + 8 :]
    fetch = pltpu.make_async_copy(moment_src, moment_ref, sem)
    fetch.start()
    bases, slots, n_near = bk_ref.shape
    tiles = atoms // LANES
    top_rows = val_ref.shape[0] // 6

    def back_geometry(t, mine):
        here = pl.ds(pl.multiple_of(t * LANES, LANES), LANES)
        ux, uy, uz, back, soft, fj = [geo_ref[i, :, here] for i in range(6)]
        dy = [None] * ORDERS
        ds = None
        for n in range(bases):
            basis = bk_ref[n, :, here]
            db = None
            for l in range(ORDERS):
                g = row(da_ref[l, n : n + 1, here]) + fj * row(da_ref[l, bases + n : bases + n + 1, here])
                if l:
                    dy[l] = g * basis if dy[l] is None else dy[l] + g * basis
                    db = db + g * y_ref[l - 1, :, here]
                else:
                    db = g
            db = db * basis * ((1.0 + n) - soft)
            ds = db if ds is None else ds + db
        if mine:
            ds = ds + q_ref[0:8, here]
            for l in range(1, ORDERS):
                dy[l] = dy[l] + q_ref[8 * l : 8 * l + 8, here]
        dux = SQRT3 * dy[1] + SQRT15 * (uy * dy[4] + uz * dy[7] + ux * dy[8]) - SQRT5 * ux * dy[6]
        duy = SQRT3 * dy[2] + SQRT15 * (ux * dy[4] + uz * dy[5] - uy * dy[8]) - SQRT5 * uy * dy[6]
        duz = SQRT3 * dy[3] + SQRT15 * (uy * dy[5] + ux * dy[7]) + 2.0 * SQRT5 * uz * dy[6]
        along = ds - (ux * dux + uy * duy + uz * duz) * back
        for i, value in enumerate((dux * back + along * ux, duy * back + along * uy, duz * back + along * uz)):
            dr_ref[i, :, here] = value

    in_turns(0, tiles, lambda t: back_geometry(t, True))
    in_turns(tiles, n_near // LANES, lambda t: back_geometry(t, False))

    def place_tile(t):
        here = pl.ds(pl.multiple_of(t * LANES, LANES), LANES)
        gidx = gidx_ref[:, here]
        chunk_no = gidx >> 7
        parts = []
        for i in range(3):
            value = dr_ref[i, :, here]
            hi = value.astype(bf16).astype(f32)
            parts.append((hi, value - hi))
        chunk_ids = lax.broadcasted_iota(jnp.int32, (top_rows, LANES), 0)
        for k in range(slots):
            at = pl.ds(pl.multiple_of(k * n_near + t * LANES, LANES), LANES)
            hit = chunk_ids == row(chunk_no[k : k + 1, :], top_rows)
            for i in range(3):
                both = [jnp.where(hit, row(part[k : k + 1, :], top_rows), 0.0) for part in parts[i]]
                val_ref[2 * i * top_rows : 2 * (i + 1) * top_rows, at] = jnp.concatenate(both, axis=0).astype(bf16)

    in_turns(0, n_near // LANES, place_tile)
    landed = dot_nt(val_ref[...], ohlo_ref[...])
    fetch.wait()
    lines = push_ref.shape[0] // (n_wide + 1)
    for i in range(3):
        total = (
            landed[2 * i * top_rows : (2 * i + 1) * top_rows] + landed[(2 * i + 1) * top_rows : (2 * i + 2) * top_rows]
        )
        for g in range(n_wide):
            for t in range(tiles):
                cols = slice(t * LANES, (t + 1) * LANES)
                line = total[g * tiles + t : g * tiles + t + 1, :]
                if g < len(near):
                    here = slice(g * atoms + t * LANES, g * atoms + (t + 1) * LANES)
                    line = line - jnp.sum(dr_ref[i, :, here], axis=0, keepdims=True)
                line = -HALF_STEP * line
                at = i * tiles + t
                if g == 0:
                    line = line + moment_ref[i, :, cols]
                    push_ref[at : at + 1, :] = blocks[0][i : i + 1, cols]
                push_ref[(1 + g) * lines + at : (1 + g) * lines + at + 1, :] = line
                mass = HEAVY - (HEAVY - 1.0) * blocks[g][3:4, cols]
                mass_ref[g * lines + at : g * lines + at + 1, :] = mass
    if lines > 3 * tiles:
        for g in range(n_wide + 1):
            blank = slice(g * lines + 3 * tiles, (g + 1) * lines)
            push_ref[blank, :] = jnp.zeros((lines - 3 * tiles, LANES), f32)
            if g < n_wide:
                mass_ref[blank, :] = jnp.ones((lines - 3 * tiles, LANES), f32)


def in_hbm(x):
    return pltpu.with_memory_space_constraint(x, pltpu.HBM)


def run(name, body, operands, results, scratch=(), far=(), cost=None):
    sizes = [math.prod(x.shape) * x.dtype.itemsize for i, x in enumerate(operands) if i not in far]
    sizes += [math.prod(shape) * jnp.dtype(dtype).itemsize for shape, dtype in results]
    sizes += [math.prod(x.shape) * x.dtype.itemsize for x in scratch if x.memory_space == pltpu.VMEM]
    limit = sum(sizes) + 4 * MIB
    specs = [pl.BlockSpec(memory_space=pltpu.HBM if i in far else pltpu.VMEM) for i in range(len(operands))]
    return pl.pallas_call(
        body,
        out_shape=tuple(jax.ShapeDtypeStruct(shape, dtype) for shape, dtype in results),
        in_specs=specs,
        out_specs=tuple(pl.BlockSpec(memory_space=pltpu.VMEM) for _ in results),
        scratch_shapes=list(scratch),
        compiler_params=pltpu.CompilerParams(vmem_limit_bytes=limit),
        cost_estimate=cost,
        name=name,
    )(*[in_hbm(x) if i in far else x for i, x in enumerate(operands)])


def choose(block, embedding, radial_one, radial_two, mix_one, mix_two, read_one, read_two):
    atoms = block.shape[1]
    slots = block.shape[0] - HEAD
    chan = embedding.shape[1]
    bases = radial_one.shape[0]
    weights = (embedding, radial_one, radial_two, mix_one, mix_two, read_one[None], read_two[None])
    return run(
        "choose",
        choose_kernel,
        (block, *weights),
        (
            ((2 * atoms, slots * atoms), bf16),
            ((chan, 8 * bases), bf16),
            ((chan, 4 * bases), bf16),
            ((chan, LANES), f32),
            ((4 * bases, 2 * chan), bf16),
            ((2 * bases, 2 * chan), bf16),
            ((2, 2 * chan, 3 * chan), bf16),
            ((2, 3, 2 * chan, chan), bf16),
        ),
        [pltpu.VMEM(w.shape, f32) for w in weights] + [pltpu.SemaphoreType.DMA((len(weights),))],
        range(1, 1 + len(weights)),
        cost=pl.CostEstimate(flops=2 * 10**9, bytes_accessed=2 * 10**6, transcendentals=0),
    )


def pushes(plan, blocks, momenta, chosen):
    atoms, near, wide, _, _ = plan
    oh, rrc, r2c, sides, rrr, r2r, mixa, mixt = chosen
    chan = rrc.shape[0]
    bases = r2r.shape[0] // 2
    slots = blocks[0].shape[0] - HEAD
    n_near = len(near) * atoms
    edges = slots * atoms
    top_rows = -(-len(wide) * atoms // LANES // 8) * 8
    lines = line_count(atoms)
    geo, y, yb, bk, bt, gidx, pick = run(
        "edges",
        functools.partial(edge_kernel, plan),
        blocks,
        (
            ((6, slots, n_near), f32),
            ((ORDERS - 1, slots, n_near), f32),
            ((ORDERS - 1, slots, 8, atoms), f32),
            ((bases, slots, n_near), f32),
            ((slots, 2 * bases, n_near), f32),
            ((slots, n_near), jnp.int32),
            ((n_near, atoms), bf16),
        ),
    )
    m1, sp1, hid, hs = run(
        "first",
        functools.partial(first_kernel, plan),
        (*blocks, y, bt, rrc, sides, mixa),
        (((ORDERS, chan, n_near), f32), ((chan, n_near), f32), ((chan, n_near), f32), ((2 * chan, n_near), bf16)),
        [pltpu.VMEM((ORDERS, 8 * bases, n_near), bf16), pltpu.VMEM((8, n_near), f32)],
    )
    hj, w, car = run(
        "gather",
        gather_kernel,
        (hid, hs, oh, pick, gidx, bt, r2c),
        (((chan, edges), f32),) * 3,
        [pltpu.VMEM((2 * chan, 2 * atoms), bf16)],
    )
    m2, dinv = run(
        "moments",
        moment_kernel,
        (car, yb, mixa, mixt, sides),
        (((ORDERS, chan, atoms), f32), ((3 * chan, atoms), f32)),
        [pltpu.VMEM((3 * chan, atoms), f32)],
    )
    dhe, dw, p = run(
        "back_second",
        back_second_kernel,
        (m2, dinv, car, hj, w, yb),
        (((2 * chan, edges), bf16), ((2 * chan, edges), bf16), ((ORDERS - 1, 8 * slots, atoms), f32)),
    )
    dh, q, ohlo = run(
        "scatter",
        scatter_kernel,
        (oh, pick, dhe, sides, dw, p, bt, geo, r2r, gidx),
        (((chan, n_near), f32), ((8 * ORDERS, atoms), f32), ((LANES, slots * n_near), bf16)),
        [pltpu.VMEM((8 * slots, atoms), f32)],
    )
    (da,) = run("back_first", back_first_kernel, (dh, sp1, m1, mixt, rrr), (((ORDERS, 2 * bases, n_near), f32),))
    return run(
        "back_edges",
        functools.partial(back_edge_kernel, plan),
        (*blocks, momenta, geo, y, bk, gidx, da, q, ohlo),
        ((((len(wide) + 1) * lines, LANES), f32), ((len(wide) * lines, LANES), f32)),
        [
            pltpu.VMEM((6 * top_rows, slots * n_near), bf16),
            pltpu.VMEM((3, slots, n_near), f32),
            pltpu.VMEM(momenta.shape, f32),
            pltpu.SemaphoreType.DMA(()),
        ],
        (len(blocks),),
    )


def line_count(atoms):
    return -(-3 * (atoms // LANES) // 8) * 8


def ring_plan(domains, atoms):
    near = list(dict.fromkeys(o % domains for o in (0, 1, -1)))
    wide = list(dict.fromkeys(near + [o % domains for o in (2, -2)]))
    before = tuple(wide.index((o - 1) % domains) for o in near)
    after = tuple(wide.index((o + 1) % domains) for o in near)
    return atoms, tuple(near), tuple(wide), before, after


def mode_turns(bead_total):
    bead = np.arange(bead_total, dtype=np.float64)[:, None]
    mode = np.arange(bead_total, dtype=np.float64)[None, :]
    phase = 2.0 * np.pi * bead * mode / bead_total
    half_total = bead_total // 2
    table = math.sqrt(2.0 / bead_total) * np.where(mode < half_total, np.cos(phase), np.sin(phase))
    table = np.where(mode == half_total, np.cos(np.pi * bead) / math.sqrt(bead_total), table)
    table = np.where(mode == 0, 1.0 / math.sqrt(bead_total), table)
    angles = bead_total * np.sin(np.pi * mode[0] / bead_total)
    safe = np.where(mode[0] == 0, 1.0, angles)
    reach = np.where(mode[0] == 0, STEP, STEP * np.sin(angles) / safe)
    stiff = angles * np.sin(angles) / STEP
    return [[float(x) for x in (table * factor[None, :]) @ table[0]] for factor in (np.cos(angles), reach, stiff)]


def pack_kernel(coord_src, species_src, send_src, slot_src, block_ref, coord_ref, species_ref, send_ref, slot_ref, sems):
    pairs = ((coord_src, coord_ref), (species_src, species_ref), (send_src, send_ref), (slot_src, slot_ref))
    fetches = [pltpu.make_async_copy(src, dst, sems.at[i]) for i, (src, dst) in enumerate(pairs)]
    for fetch in fetches:
        fetch.start()
    for fetch in fetches:
        fetch.wait()
    atoms = block_ref.shape[1]
    for i in range(3):
        block_ref[i : i + 1, :] = coord_ref[i]
    block_ref[3:4, :] = species_ref[...].astype(f32)
    block_ref[4:5, :] = send_ref[...].astype(f32)
    block_ref[5:HEAD, :] = jnp.zeros((HEAD - 5, atoms), f32)
    block_ref[HEAD:, :] = slot_ref[...].astype(f32)


def turn_kernel(shape, bead_ref, domain_ref, mass_ref, *refs):
    outer, inner, domains, wide = shape
    message_ref = refs[outer]
    turns = mode_turns(outer * inner)
    lines = mass_ref.shape[0] // len(wide)
    my_domain = domain_ref[0]
    my_inner = lax.rem(bead_ref[0], inner)
    if domains > len(wide):
        message_ref[...] = jnp.zeros_like(message_ref)
    masses = [mass_ref[g * lines : (g + 1) * lines, :] for g in range(len(wide))]
    sources = []
    for z in range(outer):
        sources.append([refs[z][g * lines : (g + 1) * lines, :] for g in range(len(wide) + 1)])
    for s in range(inner):
        wraps = jnp.full((lines, LANES), my_inner + s) >= inner
        weights = []
        for turn in turns:
            row_of = []
            for z in range(outer):
                there = turn[(z * inner + s) % (outer * inner)]
                round_it = turn[(z * inner + s - inner) % (outer * inner)]
                row_of.append(jnp.where(wraps, jnp.full((lines, LANES), round_it), jnp.full((lines, LANES), there)))
            weights.append(row_of)
        to_inner = lax.rem(my_inner + s, inner)
        for g in range(len(wide)):
            turned = sum(weights[0][z] * sources[z][1 + g] for z in range(outer))
            drift = sum(weights[1][z] * sources[z][1 + g] for z in range(outer))
            new_q = drift / masses[g]
            new_p = turned
            if g == 0:
                new_q = new_q + sum(weights[0][z] * sources[z][0] for z in range(outer))
                new_p = new_p - masses[g] * sum(weights[2][z] * sources[z][0] for z in range(outer))
            to = to_inner * domains + lax.rem(my_domain + wide[g], domains)
            message_ref[to, 0:lines, :] = new_q
            message_ref[to, lines:, :] = new_p


def sum_kernel(arrived_ref, q_ref, p_ref):
    total = arrived_ref[0]
    for i in range(1, arrived_ref.shape[0]):
        total = total + arrived_ref[i]
    lines = total.shape[0] // 2
    tiles = q_ref.shape[2] // LANES
    for i in range(3):
        for t in range(tiles):
            at = i * tiles + t
            q_ref[i, :, t * LANES : (t + 1) * LANES] = total[at : at + 1]
            p_ref[i, :, t * LANES : (t + 1) * LANES] = total[lines + at : lines + at + 1]


def shards(
    positions, momenta, species, neighbours, send_list, embedding, radial_one, radial_two, mix_one, mix_two,
    read_one, read_two,
):
    slots, atoms = neighbours.shape
    domains = lax.axis_size("space")
    beads = lax.axis_size("bead")
    inner = next(d for d in range(1, beads + 1) if beads % d == 0 and d * d >= beads)
    outer = beads // inner
    plan = ring_plan(domains, atoms)
    wide = plan[2]
    vmem = pl.BlockSpec(memory_space=pltpu.VMEM)
    smem = pl.BlockSpec(memory_space=pltpu.SMEM)
    far = pl.BlockSpec(memory_space=pltpu.HBM)
    small = pltpu.CompilerParams(vmem_limit_bytes=4 * MIB)
    coord_rows = jnp.transpose(positions, (1, 0, 2))
    moment_rows = jnp.transpose(momenta, (1, 0, 2))
    block = pl.pallas_call(
        pack_kernel,
        out_shape=jax.ShapeDtypeStruct((HEAD + slots, atoms), f32),
        in_specs=[far] * 4,
        out_specs=vmem,
        scratch_shapes=[
            pltpu.VMEM(coord_rows.shape, f32),
            pltpu.VMEM((1, atoms), jnp.int32),
            pltpu.VMEM((1, atoms), jnp.int32),
            pltpu.VMEM((slots, atoms), jnp.int32),
            pltpu.SemaphoreType.DMA((4,)),
        ],
        compiler_params=small,
        name="pack",
    )(in_hbm(coord_rows), in_hbm(species[None]), in_hbm(send_list[None]), in_hbm(neighbours))
    blocks = [block]
    for offset in wide[1:]:
        blocks.append(lax.ppermute(block, "space", [(i, (i - offset) % domains) for i in range(domains)]))
    chosen = choose(block, embedding, radial_one, radial_two, mix_one, mix_two, read_one, read_two)
    pushed, masses = pushes(plan, blocks, moment_rows, chosen)
    sources = [pushed]
    for z in range(1, outer):
        sources.append(lax.ppermute(pushed, "bead", [(b, (b + z * inner) % beads) for b in range(beads)]))
    here = [lax.axis_index(axis).astype(jnp.int32).reshape(1) for axis in ("bead", "space")]
    lines = line_count(atoms)
    messages = pl.pallas_call(
        functools.partial(turn_kernel, (outer, inner, domains, wide)),
        out_shape=jax.ShapeDtypeStruct((inner * domains, 2 * lines, LANES), f32),
        in_specs=[smem, smem, vmem] + [vmem] * outer,
        out_specs=vmem,
        compiler_params=small,
        name="turn",
    )(*here, masses, *sources)
    rows = [[z * inner * domains + i for i in range(inner * domains)] for z in range(outer)]
    arrived = lax.all_to_all(messages, ("bead", "space"), 0, 0, axis_index_groups=rows, tiled=True)
    new_q, new_p = pl.pallas_call(
        sum_kernel,
        out_shape=(jax.ShapeDtypeStruct((3, 1, atoms), f32),) * 2,
        in_specs=[vmem],
        out_specs=(vmem, vmem),
        compiler_params=small,
        name="sum",
    )(arrived)
    return (jnp.transpose(new_q, (1, 0, 2)), jnp.transpose(new_p, (1, 0, 2)))


def solution(mesh):
    placed = (
        P("bead", None, "space"),
        P("bead", None, "space"),
        P("space"),
        P(None, "space"),
        P("space"),
        P(),
        P(),
        P(),
        P(),
        P(),
        P(),
        P(),
    )
    return jax.shard_map(
        shards,
        mesh=mesh,
        in_specs=placed,
        out_specs=(P("bead", None, "space"), P("bead", None, "space")),
        check_vma=False,
    )
```

```python
import functools
import math

import jax
import jax.numpy as jnp
import numpy as np
from jax import lax
from jax.experimental import pallas as pl
from jax.experimental.pallas import tpu as pltpu
from jax.sharding import PartitionSpec as P

STEP = 2.0
HALF_STEP = 1.0
HEAVY = 16.0
SQRT3 = math.sqrt(3.0)
SQRT5 = math.sqrt(5.0)
SQRT15 = math.sqrt(15.0)
LANES = 128
ORDERS = 9
GROUP = (0, 1, 1, 1, 2, 2, 2, 2, 2)
HEAD = 8
MIB = 1024 * 1024
f32 = jnp.float32
bf16 = jnp.bfloat16


def split(x):
    hi = x.astype(bf16)
    return hi, (x - hi.astype(f32)).astype(bf16)


def split_rows(x):
    hi = x.astype(bf16).astype(f32)
    return jnp.concatenate([hi, x - hi], axis=0)


def dot(a, b):
    return jnp.dot(a, b, preferred_element_type=f32)


def dot_nt(a, b):
    return lax.dot_general(a, b, (((1,), (1,)), ((), ())), preferred_element_type=f32)


def in_turns(start, stop, step, most=4):
    per_turn = next(n for n in range(most, 0, -1) if (stop - start) % n == 0)

    def turn(i, carry):
        for j in range(per_turn):
            step(start + i * per_turn + j)
        return carry

    lax.fori_loop(0, (stop - start) // per_turn, turn, 0)


def row(x, rows=8):
    return jnp.broadcast_to(x, (rows, x.shape[1]))


def lookup(chunks, wanted, position):
    out = None
    for number, chunk in chunks:
        got = jnp.take_along_axis(row(chunk), position, axis=1, mode="promise_in_bounds")
        out = got if out is None else jnp.where(wanted == number, got, out)
    return out


def harmonics(ux, uy, uz):
    return [
        None,
        SQRT3 * ux,
        SQRT3 * uy,
        SQRT3 * uz,
        SQRT15 * ux * uy,
        SQRT15 * uy * uz,
        0.5 * SQRT5 * (2.0 * uz * uz - ux * ux - uy * uy),
        SQRT15 * ux * uz,
        0.5 * SQRT15 * (ux * ux - uy * uy),
    ]


def silu_parts(v):
    gate = 1.0 / (1.0 + jnp.exp(-v))
    return v * gate, gate * (1.0 + v * (1.0 - gate))


def choose_kernel(block_ref, *refs):
    sources = refs[:7]
    oh_ref, rrc_ref, r2c_ref, side_ref, rrr_ref, r2r_ref, mixa_ref, mixt_ref = refs[7:15]
    held = refs[15:22]
    sems = refs[22]
    emb_ref, rad1_ref, rad2_ref, mix1_ref, mix2_ref, read1_ref, read2_ref = held
    fetches = [pltpu.make_async_copy(src, dst, sems.at[i]) for i, (src, dst) in enumerate(zip(sources, held))]
    for fetch in fetches:
        fetch.start()
    chan = emb_ref.shape[1]
    bases = rad1_ref.shape[0]
    atoms = block_ref.shape[1]
    slots = block_ref.shape[0] - HEAD

    ids16 = lax.broadcasted_iota(jnp.int32, (LANES, atoms), 0).astype(jnp.int16)
    one16 = jnp.ones((LANES, atoms), bf16)
    zero16 = jnp.zeros((LANES, atoms), bf16)
    for k in range(slots):
        slot = block_ref[HEAD + k : HEAD + k + 1, :].astype(jnp.int32)
        wanted = jnp.broadcast_to(slot, (LANES, atoms)).astype(jnp.int16)
        for r in range(oh_ref.shape[0] // LANES):
            hit = wanted - jnp.int16(r * LANES) == ids16
            oh_ref[r * LANES : (r + 1) * LANES, k * atoms : (k + 1) * atoms] = jnp.where(hit, one16, zero16)

    for fetch in fetches:
        fetch.wait()
    emb0 = emb_ref[0:1, :]
    emb_d = emb_ref[1:2, :] - emb0
    rr = jnp.concatenate([rad1_ref[...] * emb0, rad1_ref[...] * emb_d], axis=0) * (1.0 / slots)
    rr_hi = rr.astype(bf16).astype(f32)
    rr_lo = rr - rr_hi
    r2 = rad2_ref[...] * (1.0 / slots)
    r2_hi = r2.astype(bf16).astype(f32)
    r2_lo = r2 - r2_hi
    zeros = jnp.zeros((8, chan), f32)
    turned1 = jnp.concatenate([rr_hi, rr_hi, rr_lo, rr_lo] + [zeros] * 8, axis=0).T
    sides = jnp.concatenate([emb0, emb_d, read1_ref[...], read2_ref[...], zeros[:4]], axis=0)
    turned2 = jnp.concatenate([r2_hi, r2_hi, r2_lo, r2_lo] + [zeros] * 12, axis=0).T
    rrc_ref[...] = turned1[:, : 8 * bases].astype(bf16)
    r2c_ref[...] = turned2[:, : 4 * bases].astype(bf16)
    side_ref[...] = jnp.concatenate([sides] + [zeros] * 15, axis=0).T
    rrr_ref[...] = jnp.concatenate(
        [jnp.concatenate([rr_hi, rr_hi], axis=1), jnp.concatenate([rr_lo, jnp.zeros_like(rr_lo)], axis=1)], axis=0
    ).astype(bf16)
    r2r_ref[...] = jnp.concatenate(
        [jnp.concatenate([r2_hi, r2_hi], axis=1), jnp.concatenate([r2_lo, jnp.zeros_like(r2_lo)], axis=1)], axis=0
    ).astype(bf16)
    for i, ref in enumerate((mix1_ref, mix2_ref)):
        hi, lo = split(ref[...])
        mixa_ref[i, 0:chan, :] = hi
        mixa_ref[i, chan:, :] = lo
        for g in range(3):
            hi, lo = split(ref[:, g * chan : (g + 1) * chan].T)
            mixt_ref[i, g, 0:chan, :] = hi
            mixt_ref[i, g, chan:, :] = lo


def dot_parts(both, hi, lo):
    rows = both.shape[0] // 2
    first = dot(both, hi)
    return first[:rows] + first[rows:] + dot(both[:rows], lo)


def edge_kernel(plan, *refs):
    atoms, near, wide, before, after = plan
    n_wide = len(wide)
    blocks = refs[:n_wide]
    geo_ref, y_ref, yb_ref, ub_ref, bk_ref, bt_ref, gidx_ref, pick_ref, as_ref = refs[n_wide:]
    bases = bk_ref.shape[0]
    slots = gidx_ref.shape[0]
    tiles = atoms // LANES
    half = atoms // 2
    half_tiles = half // LANES
    order_col = lax.broadcasted_iota(jnp.int32, (bases, LANES), 0).astype(f32)
    tables = []
    for quantity in range(4):
        chunks = []
        for g in range(n_wide):
            for t in range(tiles):
                chunks.append((g * tiles + t, blocks[g][quantity : quantity + 1, t * LANES : (t + 1) * LANES]))
        tables.append(chunks)
    for q in range(len(near)):
        ghosts = []
        for t in range(half_tiles):
            ghosts.append(
                (t, blocks[before[q]][4:5, half + t * LANES : half + (t + 1) * LANES] + float(before[q] * atoms))
            )
        for t in range(half_tiles):
            ghosts.append(
                (
                    half_tiles + tiles + t,
                    blocks[after[q]][4:5, t * LANES : (t + 1) * LANES] + float(after[q] * atoms),
                )
            )
        if q == 0:
            ids16 = lax.broadcasted_iota(jnp.int32, (pick_ref.shape[0], LANES), 0).astype(jnp.int16)
            one16 = jnp.ones(ids16.shape, bf16)
            zero16 = jnp.zeros(ids16.shape, bf16)
            for t, (_, chunk) in enumerate(ghosts):
                wanted = jnp.broadcast_to(chunk.astype(jnp.int32), ids16.shape).astype(jnp.int16)
                pick_ref[:, t * LANES : (t + 1) * LANES] = jnp.where(wanted == ids16, one16, zero16)
        for t in range(tiles):
            cols = slice(t * LANES, (t + 1) * LANES)
            here = slice(q * atoms + t * LANES, q * atoms + (t + 1) * LANES)
            slot = blocks[q][HEAD : HEAD + slots, cols].astype(jnp.int32)
            chunk_no = slot >> 7
            far = lookup(ghosts, chunk_no, slot & 127).astype(jnp.int32)
            own = (slot >= half) & (slot < half + atoms)
            gidx = jnp.where(own, slot + (q * atoms - half), far)
            gidx_ref[:, here] = gidx
            chunk_no = gidx >> 7
            place = gidx & 127
            xj, yj, zj, fj = [lookup(tables[i], chunk_no, place) for i in range(4)]
            rx = xj - row(blocks[q][0:1, cols])
            ry = yj - row(blocks[q][1:2, cols])
            rz = zj - row(blocks[q][2:3, cols])
            soft = jnp.sqrt(rx * rx + ry * ry + rz * rz + 1.0)
            back = 1.0 / soft
            ux, uy, uz = rx * back, ry * back, rz * back
            for i, value in enumerate((ux, uy, uz, back, soft, fj)):
                geo_ref[i, :, here] = value
            if q == 0:
                for i, value in enumerate((ux, uy, uz)):
                    for k in range(slots):
                        ub_ref[i, k, :, cols] = row(value[k : k + 1, :])
            sphere = harmonics(ux, uy, uz)
            for l in range(1, ORDERS):
                y_ref[l - 1, :, here] = sphere[l]
                if q == 0:
                    for k in range(slots):
                        yb_ref[l - 1, k, :, cols] = row(sphere[l][k : k + 1, :])
            for n in range(bases):
                bk_ref[n, :, here] = jnp.exp(-0.5 * (soft - (1.0 + n)) ** 2)
            for k in range(slots):
                basis = jnp.exp(-0.5 * (row(soft[k : k + 1, :], bases) - (1.0 + order_col)) ** 2)
                bt_ref[k, 0:bases, here] = basis
                bt_ref[k, bases : 2 * bases, here] = basis * row(fj[k : k + 1, :], bases)
            low = [None] * ORDERS
            for k in range(slots):
                basis = bt_ref[k, :, here]
                for l in range(ORDERS):
                    term = basis if l == 0 else basis * row(y_ref[l - 1, k : k + 1, here], 2 * bases)
                    low[l] = term if low[l] is None else low[l] + term
            for l in range(ORDERS):
                both = split_rows(low[l]).astype(bf16)
                as_ref[l, 0 : 4 * bases, here] = both
                as_ref[l, 4 * bases : 8 * bases, here] = both


def first_kernel(plan, *refs):
    atoms, near, wide, _, _ = plan
    n_wide = len(wide)
    blocks = refs[:n_wide]
    as_ref, rrc_ref, side_ref, mixa_ref, m1_ref, sp1_ref, hid_ref, hs_ref, flag_ref = refs[n_wide:]
    chan = m1_ref.shape[1]
    n_near = m1_ref.shape[2]

    for q in range(len(near)):
        flag_ref[0:1, q * atoms : (q + 1) * atoms] = blocks[q][3:4, :]
    wide_cols = 2 * LANES
    emb0_col = side_ref[:, 0:1]
    embd_col = side_ref[:, 1:2]

    def first(j):
        here = pl.ds(pl.multiple_of(j * wide_cols, wide_cols), wide_cols)
        inv = [None, None, None]
        for l in range(ORDERS):
            m = dot(rrc_ref[...], as_ref[l, :, here])
            m1_ref[l, :, here] = m
            inv[GROUP[l]] = m * m if inv[GROUP[l]] is None else inv[GROUP[l]] + m * m
        hi, lo = split(jnp.concatenate(inv, axis=0))
        value = dot_parts(mixa_ref[0], hi, lo)
        act, slope = silu_parts(value)
        sp1_ref[:, here] = slope
        hidden = act + emb0_col + embd_col * flag_ref[0:1, here]
        hid_ref[:, here] = hidden
        hi, lo = split(hidden)
        hs_ref[0:chan, here] = hi
        hs_ref[chan : 2 * chan, here] = lo

    in_turns(0, n_near // wide_cols, first)


def gather_kernel(hid_ref, hs_ref, oh_ref, pick_ref, gidx_ref, bt_ref, r2c_ref, hj_ref, w_ref, car_ref, ext_ref):
    slots = bt_ref.shape[0]
    bases = bt_ref.shape[1] // 2
    chan, n_near = hid_ref.shape
    atoms = hj_ref.shape[1] // slots
    half = atoms // 2
    by_lane = 2 * LANES if atoms > 2 * LANES else 0
    by_product = 2 * atoms - by_lane
    ghosts = dot(hs_ref[...], pick_ref[...]).astype(bf16)
    ext_ref[:, 0:half] = ghosts[:, :half]
    ext_ref[:, half : half + atoms] = hs_ref[:, 0:atoms]
    ext_ref[:, half + atoms :] = ghosts[:, half:]
    for k in range(slots):
        here = slice(k * atoms, (k + 1) * atoms)
        basis = split_rows(bt_ref[k, 0:bases, 0:atoms])
        w_ref[:, here] = dot(r2c_ref[...], jnp.concatenate([basis, basis], axis=0).astype(bf16))

    def gather(pair, carry):
        first = pl.multiple_of(pair * 2 * atoms, LANES)
        here = pl.ds(first, by_product)
        both = dot(ext_ref[...], oh_ref[:, here])
        wanted = gidx_ref[pl.ds(2 * pair + 1, 1), 0:atoms]
        for t in range(by_lane // LANES):
            at = pl.ds(pl.multiple_of(first + (by_product + t * LANES), LANES), LANES)
            start = atoms - by_lane + t * LANES
            mine = row(wanted[:, start : start + LANES])
            chunk_no = mine >> 7
            place = mine & 127
            for c in range(chan // 8):
                rows = slice(8 * c, 8 * c + 8)
                feat = None
                for chunk in range(n_near // LANES):
                    held = hid_ref[rows, chunk * LANES : (chunk + 1) * LANES]
                    got = jnp.take_along_axis(held, place, axis=1, mode="promise_in_bounds")
                    feat = got if feat is None else jnp.where(chunk_no == chunk, got, feat)
                hj_ref[rows, at] = feat
                car_ref[rows, at] = feat * w_ref[rows, at]
        feat = both[:chan] + both[chan:]
        hj_ref[:, here] = feat
        car_ref[:, here] = feat * w_ref[:, here]
        return carry

    lax.fori_loop(0, slots // 2, gather, 0)


def moment_kernel(car_ref, yb_ref, mixa_ref, mixt_ref, side_ref, m2_ref, dinv_ref, inv_ref):
    slots = yb_ref.shape[1]
    chan, atoms = m2_ref.shape[1:]
    tiles = atoms // LANES
    wide_cols = 2 * LANES
    rows = 32
    groups = chan // rows

    def moments(step):
        t = step // groups
        c = step % groups
        cols = pl.ds(pl.multiple_of(t * LANES, LANES), LANES)
        base = pl.multiple_of(c * rows, rows)
        acc = [[None] * ORDERS for _ in range(rows // 8)]
        for k in range(slots):
            at = pl.ds(pl.multiple_of(k * atoms + t * LANES, LANES), LANES)
            got = car_ref[pl.ds(base, rows), at]
            for l in range(ORDERS):
                yb = yb_ref[l - 1, k, :, cols] if l else None
                for h in range(rows // 8):
                    part = got[8 * h : 8 * h + 8]
                    term = part * yb if l else part
                    acc[h][l] = term if acc[h][l] is None else acc[h][l] + term
        for h in range(rows // 8):
            inv = [None] * 3
            for l in range(ORDERS):
                m2_ref[l, pl.ds(pl.multiple_of(base + 8 * h, 8), 8), cols] = acc[h][l]
                sq = acc[h][l] * acc[h][l]
                g = GROUP[l]
                inv[g] = sq if inv[g] is None else inv[g] + sq
            for g in range(3):
                inv_ref[pl.ds(pl.multiple_of(g * chan + base + 8 * h, 8), 8), cols] = inv[g]

    in_turns(0, tiles * groups, moments, 2)
    read2_col = side_ref[:, 3:4]
    for t in range(atoms // wide_cols):
        cols = slice(t * wide_cols, (t + 1) * wide_cols)
        hi, lo = split(inv_ref[:, cols])
        _, slope = silu_parts(dot_parts(mixa_ref[1], hi, lo))
        hi, lo = split(slope * (2.0 * read2_col))
        for g, scale in enumerate((1.0, 0.5 * SQRT3, 0.5 * SQRT15)):
            dinv_ref[g * chan : (g + 1) * chan, cols] = scale * dot_parts(mixt_ref[1, g], hi, lo)


def back_second_kernel(m2_ref, dinv_ref, car_ref, hj_ref, w_ref, ub_ref, dhe_ref, dw_ref, p_ref):
    slots = ub_ref.shape[1]
    chan, atoms = m2_ref.shape[1:]
    tiles = atoms // LANES
    pairs = chan // 16
    per_turn = 2 if pairs % 2 == 0 else 1

    def back_moments(t, carry):
        cols = pl.ds(pl.multiple_of(t * LANES, LANES), LANES)

        def one(c, acc):
            forms = []
            for h in range(2):
                rows = pl.ds(pl.multiple_of(c * 16 + 8 * h, 8), 8)
                scale = [dinv_ref[pl.ds(pl.multiple_of(g * chan + c * 16 + 8 * h, 8), 8), cols] for g in range(3)]
                dm = [m2_ref[l, rows, cols] * scale[GROUP[l]] for l in range(ORDERS)]
                low = dm[6] * (1.0 / SQRT3)
                forms.append((dm[0], dm[1], dm[2], dm[3], dm[8] - low, -dm[8] - low, low + low, dm[4], dm[5], dm[7]))
            base = pl.multiple_of(c * 16, 16)
            for k in range(slots):
                at = pl.ds(pl.multiple_of(k * atoms + t * LANES, LANES), LANES)
                got = car_ref[pl.ds(base, 16), at]
                ux, uy, uz = [ub_ref[i, k, :, cols] for i in range(3)]
                out = []
                for h in range(2):
                    mid, dx, dy, dz, qxx, qyy, qzz, qxy, qyz, qxz = forms[h]
                    gx = dx + qxx * ux + qxy * uy + qxz * uz
                    gy = dy + qxy * ux + qyy * uy + qyz * uz
                    gz = dz + qxz * ux + qyz * uy + qzz * uz
                    out.append(mid + (gx + dx) * ux + (gy + dy) * uy + (gz + dz) * uz)
                    part = got[8 * h : 8 * h + 8]
                    for i, g in enumerate((gx, gy, gz)):
                        acc[3 * k + i] = acc[3 * k + i] + part * g
                dcar = jnp.concatenate(out, axis=0)
                for ref, other in ((dhe_ref, w_ref), (dw_ref, hj_ref)):
                    hi, lo = split(dcar * other[pl.ds(base, 16), at])
                    ref[pl.ds(base, 16), at] = hi
                    ref[pl.ds(pl.multiple_of(chan + c * 16, 16), 16), at] = lo

        def over(c, acc):
            acc = list(acc)
            for i in range(per_turn):
                one(per_turn * c + i, acc)
            return tuple(acc)

        start = tuple(jnp.zeros((8, LANES), f32) for _ in range(3 * slots))
        acc = lax.fori_loop(0, pairs // per_turn, over, start)
        for k in range(slots):
            for i in range(3):
                p_ref[i, 8 * k : 8 * k + 8, cols] = acc[3 * k + i]
        return carry

    lax.fori_loop(0, tiles, back_moments, 0)


def scatter_kernel(oh_ref, pick_ref, dhe_ref, side_ref, dw_ref, p_ref, bt_ref, geo_ref, r2r_ref, gidx_ref,
                   dh_ref, q_ref, ohlo_ref, ds_ref):
    chan, n_near = dh_ref.shape
    slots = bt_ref.shape[0]
    bases = bt_ref.shape[1] // 2
    atoms = pick_ref.shape[1]
    half = atoms // 2
    both = dot_nt(dhe_ref[...], oh_ref[...])
    ids16 = lax.broadcasted_iota(jnp.int32, (LANES, n_near), 0).astype(jnp.int16)
    one16 = jnp.ones((LANES, n_near), bf16)
    zero16 = jnp.zeros((LANES, n_near), bf16)
    for k in range(slots):
        place = jnp.broadcast_to(gidx_ref[k : k + 1, :] & 127, (LANES, n_near)).astype(jnp.int16)
        ohlo_ref[:, k * n_near : (k + 1) * n_near] = jnp.where(place == ids16, one16, zero16)
    for k in range(slots):
        here = slice(k * atoms, (k + 1) * atoms)
        small = dot(r2r_ref[...], dw_ref[:, here])
        dbasis = small[:bases] + small[bases:]
        basis = bt_ref[k, 0:bases, 0:atoms]
        reach = 1.0 + lax.broadcasted_iota(jnp.int32, (bases, atoms), 0).astype(f32)
        ds_ref[k * 8 : k * 8 + 8, :] = dbasis * basis * (reach - row(geo_ref[4, k : k + 1, 0:atoms], bases))
    lane = lax.broadcasted_iota(jnp.int32, (slots, 16 * slots), 1)
    sub = lax.broadcasted_iota(jnp.int32, (slots, 16 * slots), 0)
    adder = jnp.where(((lane >> 3) & (slots - 1)) == sub, 1.0, 0.0).astype(bf16)
    for i in range(4):
        total = dot(adder, split_rows(p_ref[i - 1, :, :] if i else ds_ref[...]).astype(bf16))
        q_ref[8 * i : 8 * i + 8, :] = 2.0 * total if i else total
    ext = both[:chan] + both[chan:]
    hi, lo = split(jnp.concatenate([ext[:, :half], ext[:, half + atoms :]], axis=1))
    spread = dot_nt(jnp.concatenate([hi, lo], axis=0), pick_ref[...])
    spread = spread[:chan] + spread[chan:]
    dh_ref[:, 0:atoms] = spread[:, :atoms] + ext[:, half : half + atoms] + side_ref[:, 2:3]
    if n_near > atoms:
        dh_ref[:, atoms:] = spread[:, atoms:]


def back_first_kernel(dh_ref, sp1_ref, m1_ref, mixt_ref, rrr_ref, da_ref):
    n_near = sp1_ref.shape[1]
    rows = rrr_ref.shape[0] // 2
    wide_cols = 2 * LANES

    def back_first(j):
        here = pl.ds(pl.multiple_of(j * wide_cols, wide_cols), wide_cols)
        hi, lo = split(dh_ref[:, here] * sp1_ref[:, here] * 2.0)
        scale = [dot_parts(mixt_ref[0, g], hi, lo) for g in range(3)]
        for l in range(ORDERS):
            hi, lo = split(m1_ref[l, :, here] * scale[GROUP[l]])
            out = dot(rrr_ref[...], jnp.concatenate([hi, lo], axis=0))
            da_ref[l, :, here] = out[:rows] + out[rows:]

    in_turns(0, n_near // wide_cols, back_first)


def back_edge_kernel(plan, *refs):
    atoms, near, wide, _, _ = plan
    n_wide = len(wide)
    blocks = refs[:n_wide]
    moment_src, geo_ref, y_ref, bk_ref, gidx_ref, da_ref, q_ref, ohlo_ref = refs[n_wide : n_wide + 8]
    push_ref, mass_ref, val_ref, dr_ref, moment_ref, sem = refs[n_wide + 8 :]
    fetch = pltpu.make_async_copy(moment_src, moment_ref, sem)
    fetch.start()
    bases, slots, n_near = bk_ref.shape
    tiles = atoms // LANES
    top_rows = val_ref.shape[0] // 6

    def back_geometry(t, mine):
        here = pl.ds(pl.multiple_of(t * LANES, LANES), LANES)
        ux, uy, uz, back, soft, fj = [geo_ref[i, :, here] for i in range(6)]
        dy = [None] * ORDERS
        ds = None
        for n in range(bases):
            basis = bk_ref[n, :, here]
            db = None
            for l in range(ORDERS):
                g = row(da_ref[l, n : n + 1, here]) + fj * row(da_ref[l, bases + n : bases + n + 1, here])
                if l:
                    dy[l] = g * basis if dy[l] is None else dy[l] + g * basis
                    db = db + g * y_ref[l - 1, :, here]
                else:
                    db = g
            db = db * basis * ((1.0 + n) - soft)
            ds = db if ds is None else ds + db
        if mine:
            ds = ds + q_ref[0:8, here]
        dux = SQRT3 * dy[1] + SQRT15 * (uy * dy[4] + uz * dy[7] + ux * dy[8]) - SQRT5 * ux * dy[6]
        duy = SQRT3 * dy[2] + SQRT15 * (ux * dy[4] + uz * dy[5] - uy * dy[8]) - SQRT5 * uy * dy[6]
        duz = SQRT3 * dy[3] + SQRT15 * (uy * dy[5] + ux * dy[7]) + 2.0 * SQRT5 * uz * dy[6]
        if mine:
            dux, duy, duz = [d + q_ref[8 * i : 8 * i + 8, here] for i, d in ((1, dux), (2, duy), (3, duz))]
        along = ds - (ux * dux + uy * duy + uz * duz) * back
        for i, value in enumerate((dux * back + along * ux, duy * back + along * uy, duz * back + along * uz)):
            dr_ref[i, :, here] = value

    in_turns(0, tiles, lambda t: back_geometry(t, True))
    in_turns(tiles, n_near // LANES, lambda t: back_geometry(t, False))

    def place_tile(t):
        here = pl.ds(pl.multiple_of(t * LANES, LANES), LANES)
        gidx = gidx_ref[:, here]
        chunk_no = gidx >> 7
        parts = []
        for i in range(3):
            value = dr_ref[i, :, here]
            hi = value.astype(bf16).astype(f32)
            parts.append((hi, value - hi))
        chunk_ids = lax.broadcasted_iota(jnp.int32, (top_rows, LANES), 0)
        for k in range(slots):
            at = pl.ds(pl.multiple_of(k * n_near + t * LANES, LANES), LANES)
            hit = chunk_ids == row(chunk_no[k : k + 1, :], top_rows)
            for i in range(3):
                both = [jnp.where(hit, row(part[k : k + 1, :], top_rows), 0.0) for part in parts[i]]
                val_ref[2 * i * top_rows : 2 * (i + 1) * top_rows, at] = jnp.concatenate(both, axis=0).astype(bf16)

    in_turns(0, n_near // LANES, place_tile)
    landed = dot_nt(val_ref[...], ohlo_ref[...])
    fetch.wait()
    lines = push_ref.shape[0] // (n_wide + 1)
    for i in range(3):
        total = (
            landed[2 * i * top_rows : (2 * i + 1) * top_rows] + landed[(2 * i + 1) * top_rows : (2 * i + 2) * top_rows]
        )
        for g in range(n_wide):
            for t in range(tiles):
                cols = slice(t * LANES, (t + 1) * LANES)
                line = total[g * tiles + t : g * tiles + t + 1, :]
                if g < len(near):
                    here = slice(g * atoms + t * LANES, g * atoms + (t + 1) * LANES)
                    line = line - jnp.sum(dr_ref[i, :, here], axis=0, keepdims=True)
                line = -HALF_STEP * line
                at = i * tiles + t
                if g == 0:
                    line = line + moment_ref[i, :, cols]
                    push_ref[at : at + 1, :] = blocks[0][i : i + 1, cols]
                push_ref[(1 + g) * lines + at : (1 + g) * lines + at + 1, :] = line
                mass = HEAVY - (HEAVY - 1.0) * blocks[g][3:4, cols]
                mass_ref[g * lines + at : g * lines + at + 1, :] = mass
    if lines > 3 * tiles:
        for g in range(n_wide + 1):
            blank = slice(g * lines + 3 * tiles, (g + 1) * lines)
            push_ref[blank, :] = jnp.zeros((lines - 3 * tiles, LANES), f32)
            if g < n_wide:
                mass_ref[blank, :] = jnp.ones((lines - 3 * tiles, LANES), f32)


def in_hbm(x):
    return pltpu.with_memory_space_constraint(x, pltpu.HBM)


def run(name, body, operands, results, scratch=(), far=(), cost=None):
    sizes = [math.prod(x.shape) * x.dtype.itemsize for i, x in enumerate(operands) if i not in far]
    sizes += [math.prod(shape) * jnp.dtype(dtype).itemsize for shape, dtype in results]
    sizes += [math.prod(x.shape) * x.dtype.itemsize for x in scratch if x.memory_space == pltpu.VMEM]
    limit = sum(sizes) + 4 * MIB
    specs = [pl.BlockSpec(memory_space=pltpu.HBM if i in far else pltpu.VMEM) for i in range(len(operands))]
    return pl.pallas_call(
        body,
        out_shape=tuple(jax.ShapeDtypeStruct(shape, dtype) for shape, dtype in results),
        in_specs=specs,
        out_specs=tuple(pl.BlockSpec(memory_space=pltpu.VMEM) for _ in results),
        scratch_shapes=list(scratch),
        compiler_params=pltpu.CompilerParams(vmem_limit_bytes=limit),
        cost_estimate=cost,
        name=name,
    )(*[in_hbm(x) if i in far else x for i, x in enumerate(operands)])


def choose(block, embedding, radial_one, radial_two, mix_one, mix_two, read_one, read_two):
    atoms = block.shape[1]
    slots = block.shape[0] - HEAD
    chan = embedding.shape[1]
    bases = radial_one.shape[0]
    weights = (embedding, radial_one, radial_two, mix_one, mix_two, read_one[None], read_two[None])
    return run(
        "choose",
        choose_kernel,
        (block, *weights),
        (
            ((2 * atoms, slots * atoms), bf16),
            ((chan, 8 * bases), bf16),
            ((chan, 4 * bases), bf16),
            ((chan, LANES), f32),
            ((4 * bases, 2 * chan), bf16),
            ((2 * bases, 2 * chan), bf16),
            ((2, 2 * chan, 3 * chan), bf16),
            ((2, 3, 2 * chan, chan), bf16),
        ),
        [pltpu.VMEM(w.shape, f32) for w in weights] + [pltpu.SemaphoreType.DMA((len(weights),))],
        range(1, 1 + len(weights)),
        cost=pl.CostEstimate(flops=2 * 10**9, bytes_accessed=2 * 10**6, transcendentals=0),
    )


def pushes(plan, blocks, momenta, chosen):
    atoms, near, wide, _, _ = plan
    oh, rrc, r2c, sides, rrr, r2r, mixa, mixt = chosen
    chan = rrc.shape[0]
    bases = r2r.shape[0] // 2
    slots = blocks[0].shape[0] - HEAD
    n_near = len(near) * atoms
    edges = slots * atoms
    top_rows = -(-len(wide) * atoms // LANES // 8) * 8
    lines = line_count(atoms)
    geo, y, yb, ub, bk, bt, gidx, pick, as1 = run(
        "edges",
        functools.partial(edge_kernel, plan),
        blocks,
        (
            ((6, slots, n_near), f32),
            ((ORDERS - 1, slots, n_near), f32),
            ((ORDERS - 1, slots, 8, atoms), f32),
            ((3, slots, 8, atoms), f32),
            ((bases, slots, n_near), f32),
            ((slots, 2 * bases, n_near), f32),
            ((slots, n_near), jnp.int32),
            ((n_near, atoms), bf16),
            ((ORDERS, 8 * bases, n_near), bf16),
        ),
    )
    m1, sp1, hid, hs = run(
        "first",
        functools.partial(first_kernel, plan),
        (*blocks, as1, rrc, sides, mixa),
        (((ORDERS, chan, n_near), f32), ((chan, n_near), f32), ((chan, n_near), f32), ((2 * chan, n_near), bf16)),
        [pltpu.VMEM((8, n_near), f32)],
    )
    hj, w, car = run(
        "gather",
        gather_kernel,
        (hid, hs, oh, pick, gidx, bt, r2c),
        (((chan, edges), f32),) * 3,
        [pltpu.VMEM((2 * chan, 2 * atoms), bf16)],
    )
    m2, dinv = run(
        "moments",
        moment_kernel,
        (car, yb, mixa, mixt, sides),
        (((ORDERS, chan, atoms), f32), ((3 * chan, atoms), f32)),
        [pltpu.VMEM((3 * chan, atoms), f32)],
    )
    dhe, dw, p = run(
        "back_second",
        back_second_kernel,
        (m2, dinv, car, hj, w, ub),
        (((2 * chan, edges), bf16), ((2 * chan, edges), bf16), ((3, 8 * slots, atoms), f32)),
    )
    dh, q, ohlo = run(
        "scatter",
        scatter_kernel,
        (oh, pick, dhe, sides, dw, p, bt, geo, r2r, gidx),
        (((chan, n_near), f32), ((4 * slots, atoms), f32), ((LANES, slots * n_near), bf16)),
        [pltpu.VMEM((8 * slots, atoms), f32)],
    )
    (da,) = run("back_first", back_first_kernel, (dh, sp1, m1, mixt, rrr), (((ORDERS, 2 * bases, n_near), f32),))
    return run(
        "back_edges",
        functools.partial(back_edge_kernel, plan),
        (*blocks, momenta, geo, y, bk, gidx, da, q, ohlo),
        ((((len(wide) + 1) * lines, LANES), f32), ((len(wide) * lines, LANES), f32)),
        [
            pltpu.VMEM((6 * top_rows, slots * n_near), bf16),
            pltpu.VMEM((3, slots, n_near), f32),
            pltpu.VMEM(momenta.shape, f32),
            pltpu.SemaphoreType.DMA(()),
        ],
        (len(blocks),),
    )


def line_count(atoms):
    return -(-3 * (atoms // LANES) // 8) * 8


def ring_plan(domains, atoms):
    near = list(dict.fromkeys(o % domains for o in (0, 1, -1)))
    wide = list(dict.fromkeys(near + [o % domains for o in (2, -2)]))
    before = tuple(wide.index((o - 1) % domains) for o in near)
    after = tuple(wide.index((o + 1) % domains) for o in near)
    return atoms, tuple(near), tuple(wide), before, after


def mode_turns(bead_total):
    bead = np.arange(bead_total, dtype=np.float64)[:, None]
    mode = np.arange(bead_total, dtype=np.float64)[None, :]
    phase = 2.0 * np.pi * bead * mode / bead_total
    half_total = bead_total // 2
    table = math.sqrt(2.0 / bead_total) * np.where(mode < half_total, np.cos(phase), np.sin(phase))
    table = np.where(mode == half_total, np.cos(np.pi * bead) / math.sqrt(bead_total), table)
    table = np.where(mode == 0, 1.0 / math.sqrt(bead_total), table)
    angles = bead_total * np.sin(np.pi * mode[0] / bead_total)
    safe = np.where(mode[0] == 0, 1.0, angles)
    reach = np.where(mode[0] == 0, STEP, STEP * np.sin(angles) / safe)
    stiff = angles * np.sin(angles) / STEP
    return [[float(x) for x in (table * factor[None, :]) @ table[0]] for factor in (np.cos(angles), reach, stiff)]


def pack_kernel(coord_src, species_src, send_src, slot_src, block_ref, coord_ref, species_ref, send_ref, slot_ref, sems):
    pairs = ((coord_src, coord_ref), (species_src, species_ref), (send_src, send_ref), (slot_src, slot_ref))
    fetches = [pltpu.make_async_copy(src, dst, sems.at[i]) for i, (src, dst) in enumerate(pairs)]
    for fetch in fetches:
        fetch.start()
    for fetch in fetches:
        fetch.wait()
    atoms = block_ref.shape[1]
    for i in range(3):
        block_ref[i : i + 1, :] = coord_ref[i]
    block_ref[3:4, :] = species_ref[...].astype(f32)
    block_ref[4:5, :] = send_ref[...].astype(f32)
    block_ref[5:HEAD, :] = jnp.zeros((HEAD - 5, atoms), f32)
    block_ref[HEAD:, :] = slot_ref[...].astype(f32)


def turn_kernel(shape, bead_ref, domain_ref, mass_ref, *refs):
    outer, inner, domains, wide = shape
    message_ref = refs[outer]
    turns = mode_turns(outer * inner)
    lines = mass_ref.shape[0] // len(wide)
    my_domain = domain_ref[0]
    my_inner = lax.rem(bead_ref[0], inner)
    if domains > len(wide):
        message_ref[...] = jnp.zeros_like(message_ref)
    masses = [mass_ref[g * lines : (g + 1) * lines, :] for g in range(len(wide))]
    sources = []
    for z in range(outer):
        sources.append([refs[z][g * lines : (g + 1) * lines, :] for g in range(len(wide) + 1)])
    for s in range(inner):
        wraps = jnp.full((lines, LANES), my_inner + s) >= inner
        weights = []
        for turn in turns:
            row_of = []
            for z in range(outer):
                there = turn[(z * inner + s) % (outer * inner)]
                round_it = turn[(z * inner + s - inner) % (outer * inner)]
                row_of.append(jnp.where(wraps, jnp.full((lines, LANES), round_it), jnp.full((lines, LANES), there)))
            weights.append(row_of)
        to_inner = lax.rem(my_inner + s, inner)
        for g in range(len(wide)):
            turned = sum(weights[0][z] * sources[z][1 + g] for z in range(outer))
            drift = sum(weights[1][z] * sources[z][1 + g] for z in range(outer))
            new_q = drift / masses[g]
            new_p = turned
            if g == 0:
                new_q = new_q + sum(weights[0][z] * sources[z][0] for z in range(outer))
                new_p = new_p - masses[g] * sum(weights[2][z] * sources[z][0] for z in range(outer))
            to = to_inner * domains + lax.rem(my_domain + wide[g], domains)
            message_ref[to, 0:lines, :] = new_q
            message_ref[to, lines:, :] = new_p


def sum_kernel(arrived_ref, q_ref, p_ref):
    total = arrived_ref[0]
    for i in range(1, arrived_ref.shape[0]):
        total = total + arrived_ref[i]
    lines = total.shape[0] // 2
    tiles = q_ref.shape[2] // LANES
    for i in range(3):
        for t in range(tiles):
            at = i * tiles + t
            q_ref[i, :, t * LANES : (t + 1) * LANES] = total[at : at + 1]
            p_ref[i, :, t * LANES : (t + 1) * LANES] = total[lines + at : lines + at + 1]


def shards(
    positions, momenta, species, neighbours, send_list, embedding, radial_one, radial_two, mix_one, mix_two,
    read_one, read_two,
):
    slots, atoms = neighbours.shape
    domains = lax.axis_size("space")
    beads = lax.axis_size("bead")
    inner = next(d for d in range(1, beads + 1) if beads % d == 0 and d * d >= beads)
    outer = beads // inner
    plan = ring_plan(domains, atoms)
    wide = plan[2]
    vmem = pl.BlockSpec(memory_space=pltpu.VMEM)
    smem = pl.BlockSpec(memory_space=pltpu.SMEM)
    far = pl.BlockSpec(memory_space=pltpu.HBM)
    small = pltpu.CompilerParams(vmem_limit_bytes=4 * MIB)
    coord_rows = jnp.transpose(positions, (1, 0, 2))
    moment_rows = jnp.transpose(momenta, (1, 0, 2))
    block = pl.pallas_call(
        pack_kernel,
        out_shape=jax.ShapeDtypeStruct((HEAD + slots, atoms), f32),
        in_specs=[far] * 4,
        out_specs=vmem,
        scratch_shapes=[
            pltpu.VMEM(coord_rows.shape, f32),
            pltpu.VMEM((1, atoms), jnp.int32),
            pltpu.VMEM((1, atoms), jnp.int32),
            pltpu.VMEM((slots, atoms), jnp.int32),
            pltpu.SemaphoreType.DMA((4,)),
        ],
        compiler_params=small,
        name="pack",
    )(in_hbm(coord_rows), in_hbm(species[None]), in_hbm(send_list[None]), in_hbm(neighbours))
    blocks = [block]
    for offset in wide[1:]:
        blocks.append(lax.ppermute(block, "space", [(i, (i - offset) % domains) for i in range(domains)]))
    chosen = choose(block, embedding, radial_one, radial_two, mix_one, mix_two, read_one, read_two)
    pushed, masses = pushes(plan, blocks, moment_rows, chosen)
    sources = [pushed]
    for z in range(1, outer):
        sources.append(lax.ppermute(pushed, "bead", [(b, (b + z * inner) % beads) for b in range(beads)]))
    here = [lax.axis_index(axis).astype(jnp.int32).reshape(1) for axis in ("bead", "space")]
    lines = line_count(atoms)
    messages = pl.pallas_call(
        functools.partial(turn_kernel, (outer, inner, domains, wide)),
        out_shape=jax.ShapeDtypeStruct((inner * domains, 2 * lines, LANES), f32),
        in_specs=[smem, smem, vmem] + [vmem] * outer,
        out_specs=vmem,
        compiler_params=small,
        name="turn",
    )(*here, masses, *sources)
    rows = [[z * inner * domains + i for i in range(inner * domains)] for z in range(outer)]
    arrived = lax.all_to_all(messages, ("bead", "space"), 0, 0, axis_index_groups=rows, tiled=True)
    new_q, new_p = pl.pallas_call(
        sum_kernel,
        out_shape=(jax.ShapeDtypeStruct((3, 1, atoms), f32),) * 2,
        in_specs=[vmem],
        out_specs=(vmem, vmem),
        compiler_params=small,
        name="sum",
    )(arrived)
    return (jnp.transpose(new_q, (1, 0, 2)), jnp.transpose(new_p, (1, 0, 2)))


def solution(mesh):
    placed = (
        P("bead", None, "space"),
        P("bead", None, "space"),
        P("space"),
        P(None, "space"),
        P("space"),
        P(),
        P(),
        P(),
        P(),
        P(),
        P(),
        P(),
    )
    return jax.shard_map(
        shards,
        mesh=mesh,
        in_specs=placed,
        out_specs=(P("bead", None, "space"), P("bead", None, "space")),
        check_vma=False,
    )
```

```python
import functools
import math

import jax
import jax.numpy as jnp
import numpy as np
from jax import lax
from jax.experimental import pallas as pl
from jax.experimental.pallas import tpu as pltpu
from jax.sharding import PartitionSpec as P

STEP = 2.0
HALF_STEP = 1.0
HEAVY = 16.0
SQRT3 = math.sqrt(3.0)
SQRT5 = math.sqrt(5.0)
SQRT15 = math.sqrt(15.0)
LANES = 128
ORDERS = 9
GROUP = (0, 1, 1, 1, 2, 2, 2, 2, 2)
HEAD = 8
MIB = 1024 * 1024
f32 = jnp.float32
bf16 = jnp.bfloat16


def split(x):
    hi = x.astype(bf16)
    return hi, (x - hi.astype(f32)).astype(bf16)


def split_rows(x):
    hi = x.astype(bf16).astype(f32)
    return jnp.concatenate([hi, x - hi], axis=0)


def dot(a, b):
    return jnp.dot(a, b, preferred_element_type=f32)


def dot_nt(a, b):
    return lax.dot_general(a, b, (((1,), (1,)), ((), ())), preferred_element_type=f32)


def in_turns(start, stop, step, most=4):
    per_turn = next(n for n in range(most, 0, -1) if (stop - start) % n == 0)

    def turn(i, carry):
        for j in range(per_turn):
            step(start + i * per_turn + j)
        return carry

    lax.fori_loop(0, (stop - start) // per_turn, turn, 0)


def row(x, rows=8):
    return jnp.broadcast_to(x, (rows, x.shape[1]))


def lookup(chunks, wanted, position):
    out = None
    for number, chunk in chunks:
        got = jnp.take_along_axis(row(chunk), position, axis=1, mode="promise_in_bounds")
        out = got if out is None else jnp.where(wanted == number, got, out)
    return out


def harmonics(ux, uy, uz):
    return [
        None,
        SQRT3 * ux,
        SQRT3 * uy,
        SQRT3 * uz,
        SQRT15 * ux * uy,
        SQRT15 * uy * uz,
        0.5 * SQRT5 * (2.0 * uz * uz - ux * ux - uy * uy),
        SQRT15 * ux * uz,
        0.5 * SQRT15 * (ux * ux - uy * uy),
    ]


def silu_parts(v):
    gate = 1.0 / (1.0 + jnp.exp(-v))
    return v * gate, gate * (1.0 + v * (1.0 - gate))


def choose_kernel(block_ref, *refs):
    sources = refs[:7]
    oh_ref, rrc_ref, r2c_ref, side_ref, rrr_ref, r2r_ref, mixa_ref, mixt_ref = refs[7:15]
    held = refs[15:22]
    sems = refs[22]
    emb_ref, rad1_ref, rad2_ref, mix1_ref, mix2_ref, read1_ref, read2_ref = held
    fetches = [pltpu.make_async_copy(src, dst, sems.at[i]) for i, (src, dst) in enumerate(zip(sources, held))]
    for fetch in fetches:
        fetch.start()
    chan = emb_ref.shape[1]
    bases = rad1_ref.shape[0]
    atoms = block_ref.shape[1]
    slots = block_ref.shape[0] - HEAD

    ids16 = lax.broadcasted_iota(jnp.int32, (LANES, atoms), 0).astype(jnp.int16)
    one16 = jnp.ones((LANES, atoms), bf16)
    zero16 = jnp.zeros((LANES, atoms), bf16)
    for k in range(slots):
        slot = block_ref[HEAD + k : HEAD + k + 1, :].astype(jnp.int32)
        wanted = jnp.broadcast_to(slot, (LANES, atoms)).astype(jnp.int16)
        for r in range(oh_ref.shape[0] // LANES):
            hit = wanted - jnp.int16(r * LANES) == ids16
            oh_ref[r * LANES : (r + 1) * LANES, k * atoms : (k + 1) * atoms] = jnp.where(hit, one16, zero16)

    for fetch in fetches:
        fetch.wait()
    emb0 = emb_ref[0:1, :]
    emb_d = emb_ref[1:2, :] - emb0
    rr = jnp.concatenate([rad1_ref[...] * emb0, rad1_ref[...] * emb_d], axis=0) * (1.0 / slots)
    rr_hi = rr.astype(bf16).astype(f32)
    rr_lo = rr - rr_hi
    r2 = rad2_ref[...] * (1.0 / slots)
    r2_hi = r2.astype(bf16).astype(f32)
    r2_lo = r2 - r2_hi
    zeros = jnp.zeros((8, chan), f32)
    turned1 = jnp.concatenate([rr_hi, rr_hi, rr_lo, rr_lo] + [zeros] * 8, axis=0).T
    sides = jnp.concatenate([emb0, emb_d, read1_ref[...], read2_ref[...], zeros[:4]], axis=0)
    turned2 = jnp.concatenate([r2_hi, r2_hi, r2_lo, r2_lo] + [zeros] * 12, axis=0).T
    rrc_ref[...] = turned1[:, : 8 * bases].astype(bf16)
    r2c_ref[...] = turned2[:, : 4 * bases].astype(bf16)
    side_ref[...] = jnp.concatenate([sides] + [zeros] * 15, axis=0).T
    rrr_ref[...] = jnp.concatenate(
        [jnp.concatenate([rr_hi, rr_hi], axis=1), jnp.concatenate([rr_lo, jnp.zeros_like(rr_lo)], axis=1)], axis=0
    ).astype(bf16)
    r2r_ref[...] = jnp.concatenate(
        [jnp.concatenate([r2_hi, r2_hi], axis=1), jnp.concatenate([r2_lo, jnp.zeros_like(r2_lo)], axis=1)], axis=0
    ).astype(bf16)
    for i, ref in enumerate((mix1_ref, mix2_ref)):
        hi, lo = split(ref[...])
        mixa_ref[i, 0:chan, :] = hi
        mixa_ref[i, chan:, :] = lo
        for g in range(3):
            hi, lo = split(ref[:, g * chan : (g + 1) * chan].T)
            mixt_ref[i, g, 0:chan, :] = hi
            mixt_ref[i, g, chan:, :] = lo


def dot_parts(both, hi, lo):
    rows = both.shape[0] // 2
    first = dot(both, hi)
    return first[:rows] + first[rows:] + dot(both[:rows], lo)


def edge_kernel(plan, *refs):
    atoms, near, wide, before, after = plan
    n_wide = len(wide)
    blocks = refs[:n_wide]
    geo_ref, y_ref, yb_ref, ub_ref, bk_ref, bt_ref, gidx_ref, pick_ref, as_ref = refs[n_wide:]
    bases = bk_ref.shape[0]
    slots = gidx_ref.shape[0]
    tiles = atoms // LANES
    half = atoms // 2
    half_tiles = half // LANES
    order_col = lax.broadcasted_iota(jnp.int32, (bases, LANES), 0).astype(f32)
    tables = []
    for quantity in range(4):
        chunks = []
        for g in range(n_wide):
            for t in range(tiles):
                chunks.append((g * tiles + t, blocks[g][quantity : quantity + 1, t * LANES : (t + 1) * LANES]))
        tables.append(chunks)
    for q in range(len(near)):
        ghosts = []
        for t in range(half_tiles):
            ghosts.append(
                (t, blocks[before[q]][4:5, half + t * LANES : half + (t + 1) * LANES] + float(before[q] * atoms))
            )
        for t in range(half_tiles):
            ghosts.append(
                (
                    half_tiles + tiles + t,
                    blocks[after[q]][4:5, t * LANES : (t + 1) * LANES] + float(after[q] * atoms),
                )
            )
        if q == 0:
            ids16 = lax.broadcasted_iota(jnp.int32, (pick_ref.shape[0], LANES), 0).astype(jnp.int16)
            one16 = jnp.ones(ids16.shape, bf16)
            zero16 = jnp.zeros(ids16.shape, bf16)
            for t, (_, chunk) in enumerate(ghosts):
                wanted = jnp.broadcast_to(chunk.astype(jnp.int32), ids16.shape).astype(jnp.int16)
                pick_ref[:, t * LANES : (t + 1) * LANES] = jnp.where(wanted == ids16, one16, zero16)
        for t in range(tiles):
            cols = slice(t * LANES, (t + 1) * LANES)
            here = slice(q * atoms + t * LANES, q * atoms + (t + 1) * LANES)
            slot = blocks[q][HEAD : HEAD + slots, cols].astype(jnp.int32)
            chunk_no = slot >> 7
            far = lookup(ghosts, chunk_no, slot & 127).astype(jnp.int32)
            own = (slot >= half) & (slot < half + atoms)
            gidx = jnp.where(own, slot + (q * atoms - half), far)
            gidx_ref[:, here] = gidx
            chunk_no = gidx >> 7
            place = gidx & 127
            xj, yj, zj, fj = [lookup(tables[i], chunk_no, place) for i in range(4)]
            rx = xj - row(blocks[q][0:1, cols])
            ry = yj - row(blocks[q][1:2, cols])
            rz = zj - row(blocks[q][2:3, cols])
            soft = jnp.sqrt(rx * rx + ry * ry + rz * rz + 1.0)
            back = 1.0 / soft
            ux, uy, uz = rx * back, ry * back, rz * back
            for i, value in enumerate((ux, uy, uz, back, soft, fj)):
                geo_ref[i, :, here] = value
            if q == 0:
                for i, value in enumerate((ux, uy, uz)):
                    for k in range(slots):
                        ub_ref[i, k, :, cols] = row(value[k : k + 1, :])
            sphere = harmonics(ux, uy, uz)
            for l in range(1, ORDERS):
                y_ref[l - 1, :, here] = sphere[l]
                if q == 0:
                    for k in range(slots):
                        yb_ref[l - 1, k, :, cols] = row(sphere[l][k : k + 1, :])
            for n in range(bases):
                bk_ref[n, :, here] = jnp.exp(-0.5 * (soft - (1.0 + n)) ** 2)
            for k in range(slots):
                basis = jnp.exp(-0.5 * (row(soft[k : k + 1, :], bases) - (1.0 + order_col)) ** 2)
                bt_ref[k, 0:bases, here] = basis
                bt_ref[k, bases : 2 * bases, here] = basis * row(fj[k : k + 1, :], bases)
            low = [None] * ORDERS
            for k in range(slots):
                basis = bt_ref[k, :, here]
                for l in range(ORDERS):
                    term = basis if l == 0 else basis * row(y_ref[l - 1, k : k + 1, here], 2 * bases)
                    low[l] = term if low[l] is None else low[l] + term
            for l in range(ORDERS):
                both = split_rows(low[l]).astype(bf16)
                as_ref[l, 0 : 4 * bases, here] = both
                as_ref[l, 4 * bases : 8 * bases, here] = both


def first_kernel(plan, *refs):
    atoms, near, wide, _, _ = plan
    n_wide = len(wide)
    blocks = refs[:n_wide]
    as_ref, rrc_ref, side_ref, mixa_ref, m1_ref, sp1_ref, hid_ref, hs_ref, flag_ref = refs[n_wide:]
    chan = m1_ref.shape[1]
    n_near = m1_ref.shape[2]

    for q in range(len(near)):
        flag_ref[0:1, q * atoms : (q + 1) * atoms] = blocks[q][3:4, :]
    wide_cols = 2 * LANES
    emb0_col = side_ref[:, 0:1]
    embd_col = side_ref[:, 1:2]

    def first(j):
        here = pl.ds(pl.multiple_of(j * wide_cols, wide_cols), wide_cols)
        inv = [None, None, None]
        for l in range(ORDERS):
            m = dot(rrc_ref[...], as_ref[l, :, here])
            m1_ref[l, :, here] = m
            inv[GROUP[l]] = m * m if inv[GROUP[l]] is None else inv[GROUP[l]] + m * m
        hi, lo = split(jnp.concatenate(inv, axis=0))
        value = dot_parts(mixa_ref[0], hi, lo)
        act, slope = silu_parts(value)
        sp1_ref[:, here] = slope
        hidden = act + emb0_col + embd_col * flag_ref[0:1, here]
        hid_ref[:, here] = hidden
        hi, lo = split(hidden)
        hs_ref[0:chan, here] = hi
        hs_ref[chan : 2 * chan, here] = lo

    in_turns(0, n_near // wide_cols, first)


def gather_kernel(hid_ref, hs_ref, oh_ref, pick_ref, gidx_ref, bt_ref, r2c_ref, hj_ref, w_ref, car_ref, ext_ref):
    slots = bt_ref.shape[0]
    bases = bt_ref.shape[1] // 2
    chan, n_near = hid_ref.shape
    atoms = hj_ref.shape[1] // slots
    half = atoms // 2
    by_lane = 2 * LANES if atoms > 2 * LANES else 0
    by_product = 2 * atoms - by_lane
    ghosts = dot(hs_ref[...], pick_ref[...]).astype(bf16)
    ext_ref[:, 0:half] = ghosts[:, :half]
    ext_ref[:, half : half + atoms] = hs_ref[:, 0:atoms]
    ext_ref[:, half + atoms :] = ghosts[:, half:]
    for k in range(slots):
        here = slice(k * atoms, (k + 1) * atoms)
        basis = split_rows(bt_ref[k, 0:bases, 0:atoms])
        w_ref[:, here] = dot(r2c_ref[...], jnp.concatenate([basis, basis], axis=0).astype(bf16))

    def gather(pair, carry):
        first = pl.multiple_of(pair * 2 * atoms, LANES)
        here = pl.ds(first, by_product)
        both = dot(ext_ref[...], oh_ref[:, here])
        wanted = gidx_ref[pl.ds(2 * pair + 1, 1), 0:atoms]
        for t in range(by_lane // LANES):
            at = pl.ds(pl.multiple_of(first + (by_product + t * LANES), LANES), LANES)
            start = atoms - by_lane + t * LANES
            mine = row(wanted[:, start : start + LANES])
            chunk_no = mine >> 7
            place = mine & 127
            for c in range(chan // 8):
                rows = slice(8 * c, 8 * c + 8)
                feat = None
                for chunk in range(n_near // LANES):
                    held = hid_ref[rows, chunk * LANES : (chunk + 1) * LANES]
                    got = jnp.take_along_axis(held, place, axis=1, mode="promise_in_bounds")
                    feat = got if feat is None else jnp.where(chunk_no == chunk, got, feat)
                hj_ref[rows, at] = feat
                car_ref[rows, at] = feat * w_ref[rows, at]
        feat = both[:chan] + both[chan:]
        hj_ref[:, here] = feat
        car_ref[:, here] = feat * w_ref[:, here]
        return carry

    lax.fori_loop(0, slots // 2, gather, 0)


def moment_kernel(car_ref, yb_ref, mixa_ref, mixt_ref, side_ref, m2_ref, dinv_ref, inv_ref):
    slots = yb_ref.shape[1]
    chan, atoms = m2_ref.shape[1:]
    tiles = atoms // LANES
    wide_cols = 2 * LANES
    rows = 32
    groups = chan // rows

    def moments(step):
        t = step // groups
        c = step % groups
        cols = pl.ds(pl.multiple_of(t * LANES, LANES), LANES)
        base = pl.multiple_of(c * rows, rows)
        acc = [[None] * ORDERS for _ in range(rows // 8)]
        for k in range(slots):
            at = pl.ds(pl.multiple_of(k * atoms + t * LANES, LANES), LANES)
            got = car_ref[pl.ds(base, rows), at]
            for l in range(ORDERS):
                yb = yb_ref[l - 1, k, :, cols] if l else None
                for h in range(rows // 8):
                    part = got[8 * h : 8 * h + 8]
                    term = part * yb if l else part
                    acc[h][l] = term if acc[h][l] is None else acc[h][l] + term
        for h in range(rows // 8):
            inv = [None] * 3
            for l in range(ORDERS):
                m2_ref[l, pl.ds(pl.multiple_of(base + 8 * h, 8), 8), cols] = acc[h][l]
                sq = acc[h][l] * acc[h][l]
                g = GROUP[l]
                inv[g] = sq if inv[g] is None else inv[g] + sq
            for g in range(3):
                inv_ref[pl.ds(pl.multiple_of(g * chan + base + 8 * h, 8), 8), cols] = inv[g]

    in_turns(0, tiles * groups, moments, 2)
    read2_col = side_ref[:, 3:4]
    for t in range(atoms // wide_cols):
        cols = slice(t * wide_cols, (t + 1) * wide_cols)
        hi, lo = split(inv_ref[:, cols])
        _, slope = silu_parts(dot_parts(mixa_ref[1], hi, lo))
        hi, lo = split(slope * (2.0 * read2_col))
        for g, scale in enumerate((1.0, 0.5 * SQRT3, 0.5 * SQRT15)):
            dinv_ref[g * chan : (g + 1) * chan, cols] = scale * dot_parts(mixt_ref[1, g], hi, lo)


def back_second_kernel(m2_ref, dinv_ref, car_ref, hj_ref, w_ref, ub_ref, dhe_ref, dw_ref, p_ref):
    slots = ub_ref.shape[1]
    chan, atoms = m2_ref.shape[1:]
    tiles = atoms // LANES
    pairs = chan // 16
    per_turn = 2 if pairs % 2 == 0 else 1

    def back_moments(t, carry):
        cols = pl.ds(pl.multiple_of(t * LANES, LANES), LANES)

        def one(c, acc):
            forms = []
            for h in range(2):
                rows = pl.ds(pl.multiple_of(c * 16 + 8 * h, 8), 8)
                scale = [dinv_ref[pl.ds(pl.multiple_of(g * chan + c * 16 + 8 * h, 8), 8), cols] for g in range(3)]
                dm = [m2_ref[l, rows, cols] * scale[GROUP[l]] for l in range(ORDERS)]
                low = dm[6] * (1.0 / SQRT3)
                forms.append((dm[0], dm[1], dm[2], dm[3], dm[8] - low, -dm[8] - low, low + low, dm[4], dm[5], dm[7]))
            base = pl.multiple_of(c * 16, 16)
            for k in range(slots):
                at = pl.ds(pl.multiple_of(k * atoms + t * LANES, LANES), LANES)
                got = car_ref[pl.ds(base, 16), at]
                ux, uy, uz = [ub_ref[i, k, :, cols] for i in range(3)]
                out = []
                for h in range(2):
                    mid, dx, dy, dz, qxx, qyy, qzz, qxy, qyz, qxz = forms[h]
                    gx = dx + qxx * ux + qxy * uy + qxz * uz
                    gy = dy + qxy * ux + qyy * uy + qyz * uz
                    gz = dz + qxz * ux + qyz * uy + qzz * uz
                    out.append(mid + (gx + dx) * ux + (gy + dy) * uy + (gz + dz) * uz)
                    part = got[8 * h : 8 * h + 8]
                    for i, g in enumerate((gx, gy, gz)):
                        acc[3 * k + i] = acc[3 * k + i] + part * g
                dcar = jnp.concatenate(out, axis=0)
                for ref, other in ((dhe_ref, w_ref), (dw_ref, hj_ref)):
                    hi, lo = split(dcar * other[pl.ds(base, 16), at])
                    ref[pl.ds(base, 16), at] = hi
                    ref[pl.ds(pl.multiple_of(chan + c * 16, 16), 16), at] = lo

        def over(c, acc):
            acc = list(acc)
            for i in range(per_turn):
                one(per_turn * c + i, acc)
            return tuple(acc)

        start = tuple(jnp.zeros((8, LANES), f32) for _ in range(3 * slots))
        acc = lax.fori_loop(0, pairs // per_turn, over, start)
        for k in range(slots):
            for i in range(3):
                p_ref[i, 8 * k : 8 * k + 8, cols] = acc[3 * k + i]
        return carry

    lax.fori_loop(0, tiles, back_moments, 0)


def scatter_kernel(oh_ref, pick_ref, dhe_ref, side_ref, dw_ref, p_ref, bt_ref, geo_ref, r2r_ref, gidx_ref,
                   dh_ref, q_ref, ohlo_ref, ds_ref):
    chan, n_near = dh_ref.shape
    slots = bt_ref.shape[0]
    bases = bt_ref.shape[1] // 2
    atoms = pick_ref.shape[1]
    half = atoms // 2
    both = dot_nt(dhe_ref[...], oh_ref[...])
    ids16 = lax.broadcasted_iota(jnp.int32, (LANES, n_near), 0).astype(jnp.int16)
    one16 = jnp.ones((LANES, n_near), bf16)
    zero16 = jnp.zeros((LANES, n_near), bf16)
    for k in range(slots):
        place = jnp.broadcast_to(gidx_ref[k : k + 1, :] & 127, (LANES, n_near)).astype(jnp.int16)
        ohlo_ref[:, k * n_near : (k + 1) * n_near] = jnp.where(place == ids16, one16, zero16)
    for k in range(slots):
        here = slice(k * atoms, (k + 1) * atoms)
        small = dot(r2r_ref[...], dw_ref[:, here])
        dbasis = small[:bases] + small[bases:]
        basis = bt_ref[k, 0:bases, 0:atoms]
        reach = 1.0 + lax.broadcasted_iota(jnp.int32, (bases, atoms), 0).astype(f32)
        ds_ref[k * 8 : k * 8 + 8, :] = dbasis * basis * (reach - row(geo_ref[4, k : k + 1, 0:atoms], bases))
    lane = lax.broadcasted_iota(jnp.int32, (slots, 16 * slots), 1)
    sub = lax.broadcasted_iota(jnp.int32, (slots, 16 * slots), 0)
    adder = jnp.where(((lane >> 3) & (slots - 1)) == sub, 1.0, 0.0).astype(bf16)
    for i in range(4):
        total = dot(adder, split_rows(p_ref[i - 1, :, :] if i else ds_ref[...]).astype(bf16))
        q_ref[8 * i : 8 * i + 8, :] = 2.0 * total if i else total
    ext = both[:chan] + both[chan:]
    hi, lo = split(jnp.concatenate([ext[:, :half], ext[:, half + atoms :]], axis=1))
    spread = dot_nt(jnp.concatenate([hi, lo], axis=0), pick_ref[...])
    spread = spread[:chan] + spread[chan:]
    dh_ref[:, 0:atoms] = spread[:, :atoms] + ext[:, half : half + atoms] + side_ref[:, 2:3]
    if n_near > atoms:
        dh_ref[:, atoms:] = spread[:, atoms:]


def back_first_kernel(dh_ref, sp1_ref, m1_ref, mixt_ref, rrr_ref, da_ref):
    n_near = sp1_ref.shape[1]
    rows = rrr_ref.shape[0] // 2
    wide_cols = 2 * LANES

    def back_first(j):
        here = pl.ds(pl.multiple_of(j * wide_cols, wide_cols), wide_cols)
        hi, lo = split(dh_ref[:, here] * sp1_ref[:, here] * 2.0)
        scale = [dot_parts(mixt_ref[0, g], hi, lo) for g in range(3)]
        for l in range(ORDERS):
            hi, lo = split(m1_ref[l, :, here] * scale[GROUP[l]])
            out = dot(rrr_ref[...], jnp.concatenate([hi, lo], axis=0))
            da_ref[l, :, here] = out[:rows] + out[rows:]

    in_turns(0, n_near // wide_cols, back_first)


def back_edge_kernel(plan, *refs):
    atoms, near, wide, _, _ = plan
    n_wide = len(wide)
    blocks = refs[:n_wide]
    moment_src, geo_ref, y_ref, bk_ref, gidx_ref, da_ref, q_ref, ohlo_ref = refs[n_wide : n_wide + 8]
    push_ref, mass_ref, val_ref, dr_ref, moment_ref, sem = refs[n_wide + 8 :]
    fetch = pltpu.make_async_copy(moment_src, moment_ref, sem)
    fetch.start()
    bases, slots, n_near = bk_ref.shape
    tiles = atoms // LANES
    top_rows = val_ref.shape[0] // 6

    def back_geometry(t, mine):
        here = pl.ds(pl.multiple_of(t * LANES, LANES), LANES)
        ux, uy, uz, back, soft, fj = [geo_ref[i, :, here] for i in range(6)]
        dy = [None] * ORDERS
        ds = None
        for n in range(bases):
            basis = bk_ref[n, :, here]
            db = None
            for l in range(ORDERS):
                g = row(da_ref[l, n : n + 1, here]) + fj * row(da_ref[l, bases + n : bases + n + 1, here])
                if l:
                    dy[l] = g * basis if dy[l] is None else dy[l] + g * basis
                    db = db + g * y_ref[l - 1, :, here]
                else:
                    db = g
            db = db * basis * ((1.0 + n) - soft)
            ds = db if ds is None else ds + db
        if mine:
            ds = ds + q_ref[0:8, here]
        dux = SQRT3 * dy[1] + SQRT15 * (uy * dy[4] + uz * dy[7] + ux * dy[8]) - SQRT5 * ux * dy[6]
        duy = SQRT3 * dy[2] + SQRT15 * (ux * dy[4] + uz * dy[5] - uy * dy[8]) - SQRT5 * uy * dy[6]
        duz = SQRT3 * dy[3] + SQRT15 * (uy * dy[5] + ux * dy[7]) + 2.0 * SQRT5 * uz * dy[6]
        if mine:
            dux, duy, duz = [d + q_ref[8 * i : 8 * i + 8, here] for i, d in ((1, dux), (2, duy), (3, duz))]
        along = ds - (ux * dux + uy * duy + uz * duz) * back
        for i, value in enumerate((dux * back + along * ux, duy * back + along * uy, duz * back + along * uz)):
            dr_ref[i, :, here] = value

    in_turns(0, tiles, lambda t: back_geometry(t, True))
    in_turns(tiles, n_near // LANES, lambda t: back_geometry(t, False))

    def place_tile(t):
        here = pl.ds(pl.multiple_of(t * LANES, LANES), LANES)
        gidx = gidx_ref[:, here]
        chunk_no = gidx >> 7
        parts = []
        for i in range(3):
            value = dr_ref[i, :, here]
            hi = value.astype(bf16).astype(f32)
            parts.append((hi, value - hi))
        chunk_ids = lax.broadcasted_iota(jnp.int32, (top_rows, LANES), 0)
        for k in range(slots):
            at = pl.ds(pl.multiple_of(k * n_near + t * LANES, LANES), LANES)
            hit = chunk_ids == row(chunk_no[k : k + 1, :], top_rows)
            for i in range(3):
                both = [jnp.where(hit, row(part[k : k + 1, :], top_rows), 0.0) for part in parts[i]]
                val_ref[2 * i * top_rows : 2 * (i + 1) * top_rows, at] = jnp.concatenate(both, axis=0).astype(bf16)

    in_turns(0, n_near // LANES, place_tile)
    landed = dot_nt(val_ref[...], ohlo_ref[...])
    fetch.wait()
    lines = push_ref.shape[0] // (n_wide + 1)
    for i in range(3):
        total = (
            landed[2 * i * top_rows : (2 * i + 1) * top_rows] + landed[(2 * i + 1) * top_rows : (2 * i + 2) * top_rows]
        )
        for g in range(n_wide):
            for t in range(tiles):
                cols = slice(t * LANES, (t + 1) * LANES)
                line = total[g * tiles + t : g * tiles + t + 1, :]
                if g < len(near):
                    here = slice(g * atoms + t * LANES, g * atoms + (t + 1) * LANES)
                    line = line - jnp.sum(dr_ref[i, :, here], axis=0, keepdims=True)
                line = -HALF_STEP * line
                at = i * tiles + t
                if g == 0:
                    line = line + moment_ref[i, :, cols]
                    push_ref[at : at + 1, :] = blocks[0][i : i + 1, cols]
                push_ref[(1 + g) * lines + at : (1 + g) * lines + at + 1, :] = line
                mass = HEAVY - (HEAVY - 1.0) * blocks[g][3:4, cols]
                mass_ref[g * lines + at : g * lines + at + 1, :] = mass
    if lines > 3 * tiles:
        for g in range(n_wide + 1):
            blank = slice(g * lines + 3 * tiles, (g + 1) * lines)
            push_ref[blank, :] = jnp.zeros((lines - 3 * tiles, LANES), f32)
            if g < n_wide:
                mass_ref[blank, :] = jnp.ones((lines - 3 * tiles, LANES), f32)


def in_hbm(x):
    return pltpu.with_memory_space_constraint(x, pltpu.HBM)


def run(name, body, operands, results, scratch=(), far=(), cost=None):
    sizes = [math.prod(x.shape) * x.dtype.itemsize for i, x in enumerate(operands) if i not in far]
    sizes += [math.prod(shape) * jnp.dtype(dtype).itemsize for shape, dtype in results]
    sizes += [math.prod(x.shape) * x.dtype.itemsize for x in scratch if x.memory_space == pltpu.VMEM]
    limit = sum(sizes) + 4 * MIB
    specs = [pl.BlockSpec(memory_space=pltpu.HBM if i in far else pltpu.VMEM) for i in range(len(operands))]
    return pl.pallas_call(
        body,
        out_shape=tuple(jax.ShapeDtypeStruct(shape, dtype) for shape, dtype in results),
        in_specs=specs,
        out_specs=tuple(pl.BlockSpec(memory_space=pltpu.VMEM) for _ in results),
        scratch_shapes=list(scratch),
        compiler_params=pltpu.CompilerParams(vmem_limit_bytes=limit),
        cost_estimate=cost,
        name=name,
    )(*[in_hbm(x) if i in far else x for i, x in enumerate(operands)])


def choose(block, embedding, radial_one, radial_two, mix_one, mix_two, read_one, read_two):
    atoms = block.shape[1]
    slots = block.shape[0] - HEAD
    chan = embedding.shape[1]
    bases = radial_one.shape[0]
    weights = (embedding, radial_one, radial_two, mix_one, mix_two, read_one[None], read_two[None])
    return run(
        "choose",
        choose_kernel,
        (block, *weights),
        (
            ((2 * atoms, slots * atoms), bf16),
            ((chan, 8 * bases), bf16),
            ((chan, 4 * bases), bf16),
            ((chan, LANES), f32),
            ((4 * bases, 2 * chan), bf16),
            ((2 * bases, 2 * chan), bf16),
            ((2, 2 * chan, 3 * chan), bf16),
            ((2, 3, 2 * chan, chan), bf16),
        ),
        [pltpu.VMEM(w.shape, f32) for w in weights] + [pltpu.SemaphoreType.DMA((len(weights),))],
        range(1, 1 + len(weights)),
        cost=pl.CostEstimate(flops=2 * 10**9, bytes_accessed=2 * 10**6, transcendentals=0),
    )


def pushes(plan, blocks, momenta, chosen):
    atoms, near, wide, _, _ = plan
    oh, rrc, r2c, sides, rrr, r2r, mixa, mixt = chosen
    chan = rrc.shape[0]
    bases = r2r.shape[0] // 2
    slots = blocks[0].shape[0] - HEAD
    n_near = len(near) * atoms
    edges = slots * atoms
    top_rows = -(-len(wide) * atoms // LANES // 8) * 8
    lines = line_count(atoms)
    geo, y, yb, ub, bk, bt, gidx, pick, as1 = run(
        "edges",
        functools.partial(edge_kernel, plan),
        blocks,
        (
            ((6, slots, n_near), f32),
            ((ORDERS - 1, slots, n_near), f32),
            ((ORDERS - 1, slots, 8, atoms), f32),
            ((3, slots, 8, atoms), f32),
            ((bases, slots, n_near), f32),
            ((slots, 2 * bases, n_near), f32),
            ((slots, n_near), jnp.int32),
            ((n_near, atoms), bf16),
            ((ORDERS, 8 * bases, n_near), bf16),
        ),
    )
    m1, sp1, hid, hs = run(
        "first",
        functools.partial(first_kernel, plan),
        (*blocks, as1, rrc, sides, mixa),
        (((ORDERS, chan, n_near), f32), ((chan, n_near), f32), ((chan, n_near), f32), ((2 * chan, n_near), bf16)),
        [pltpu.VMEM((8, n_near), f32)],
    )
    hj, w, car = run(
        "gather",
        gather_kernel,
        (hid, hs, oh, pick, gidx, bt, r2c),
        (((chan, edges), f32),) * 3,
        [pltpu.VMEM((2 * chan, 2 * atoms), bf16)],
    )
    m2, dinv = run(
        "moments",
        moment_kernel,
        (car, yb, mixa, mixt, sides),
        (((ORDERS, chan, atoms), f32), ((3 * chan, atoms), f32)),
        [pltpu.VMEM((3 * chan, atoms), f32)],
    )
    dhe, dw, p = run(
        "back_second",
        back_second_kernel,
        (m2, dinv, car, hj, w, ub),
        (((2 * chan, edges), bf16), ((2 * chan, edges), bf16), ((3, 8 * slots, atoms), f32)),
    )
    dh, q, ohlo = run(
        "scatter",
        scatter_kernel,
        (oh, pick, dhe, sides, dw, p, bt, geo, r2r, gidx),
        (((chan, n_near), f32), ((4 * slots, atoms), f32), ((LANES, slots * n_near), bf16)),
        [pltpu.VMEM((8 * slots, atoms), f32)],
    )
    (da,) = run("back_first", back_first_kernel, (dh, sp1, m1, mixt, rrr), (((ORDERS, 2 * bases, n_near), f32),))
    return run(
        "back_edges",
        functools.partial(back_edge_kernel, plan),
        (*blocks, momenta, geo, y, bk, gidx, da, q, ohlo),
        ((((len(wide) + 1) * lines, LANES), f32), ((len(wide) * lines, LANES), f32)),
        [
            pltpu.VMEM((6 * top_rows, slots * n_near), bf16),
            pltpu.VMEM((3, slots, n_near), f32),
            pltpu.VMEM(momenta.shape, f32),
            pltpu.SemaphoreType.DMA(()),
        ],
        (len(blocks),),
    )


def line_count(atoms):
    return -(-3 * (atoms // LANES) // 8) * 8


def ring_plan(domains, atoms):
    near = list(dict.fromkeys(o % domains for o in (0, 1, -1)))
    wide = list(dict.fromkeys(near + [o % domains for o in (2, -2)]))
    before = tuple(wide.index((o - 1) % domains) for o in near)
    after = tuple(wide.index((o + 1) % domains) for o in near)
    return atoms, tuple(near), tuple(wide), before, after


def mode_turns(bead_total):
    bead = np.arange(bead_total, dtype=np.float64)[:, None]
    mode = np.arange(bead_total, dtype=np.float64)[None, :]
    phase = 2.0 * np.pi * bead * mode / bead_total
    half_total = bead_total // 2
    table = math.sqrt(2.0 / bead_total) * np.where(mode < half_total, np.cos(phase), np.sin(phase))
    table = np.where(mode == half_total, np.cos(np.pi * bead) / math.sqrt(bead_total), table)
    table = np.where(mode == 0, 1.0 / math.sqrt(bead_total), table)
    angles = bead_total * np.sin(np.pi * mode[0] / bead_total)
    safe = np.where(mode[0] == 0, 1.0, angles)
    reach = np.where(mode[0] == 0, STEP, STEP * np.sin(angles) / safe)
    stiff = angles * np.sin(angles) / STEP
    return [[float(x) for x in (table * factor[None, :]) @ table[0]] for factor in (np.cos(angles), reach, stiff)]


def pack_kernel(coord_src, species_src, send_src, slot_src, block_ref, coord_ref, species_ref, send_ref, slot_ref, sems):
    pairs = ((coord_src, coord_ref), (species_src, species_ref), (send_src, send_ref), (slot_src, slot_ref))
    fetches = [pltpu.make_async_copy(src, dst, sems.at[i]) for i, (src, dst) in enumerate(pairs)]
    for fetch in fetches:
        fetch.start()
    for fetch in fetches:
        fetch.wait()
    atoms = block_ref.shape[1]
    for i in range(3):
        block_ref[i : i + 1, :] = coord_ref[i]
    block_ref[3:4, :] = species_ref[...].astype(f32)
    block_ref[4:5, :] = send_ref[...].astype(f32)
    block_ref[5:HEAD, :] = jnp.zeros((HEAD - 5, atoms), f32)
    block_ref[HEAD:, :] = slot_ref[...].astype(f32)


def turn_kernel(shape, bead_ref, domain_ref, mass_ref, *refs):
    outer, inner, domains, wide = shape
    sources, message_ref = refs[:inner], refs[inner]
    beads = outer * inner
    turns = mode_turns(beads)
    lines = mass_ref.shape[0] // len(wide)
    my_domain = domain_ref[0]
    my_inner = lax.rem(bead_ref[0], inner)
    my_outer = (bead_ref[0] - my_inner) // inner
    if domains > len(wide):
        message_ref[...] = jnp.zeros_like(message_ref)
    masses = [mass_ref[g * lines : (g + 1) * lines, :] for g in range(len(wide))]
    held = [[source[g * lines : (g + 1) * lines, :] for g in range(len(wide) + 1)] for source in sources]
    wraps = [jnp.full((lines, LANES), my_inner) < s for s in range(inner)]
    for z in range(outer):
        weights = []
        for turn in turns:
            row_of = []
            for s in range(inner):
                there = turn[(z * inner + s) % beads]
                round_it = turn[(z * inner + s - inner) % beads]
                row_of.append(jnp.where(wraps[s], jnp.full((lines, LANES), round_it), jnp.full((lines, LANES), there)))
            weights.append(row_of)
        to_outer = lax.rem(my_outer + z, outer)
        for g in range(len(wide)):
            turned = sum(weights[0][s] * held[s][1 + g] for s in range(inner))
            drift = sum(weights[1][s] * held[s][1 + g] for s in range(inner))
            new_q = drift / masses[g]
            new_p = turned
            if g == 0:
                new_q = new_q + sum(weights[0][s] * held[s][0] for s in range(inner))
                new_p = new_p - masses[g] * sum(weights[2][s] * held[s][0] for s in range(inner))
            to = to_outer * domains + lax.rem(my_domain + wide[g], domains)
            message_ref[to, 0:lines, :] = new_q
            message_ref[to, lines:, :] = new_p


def sum_kernel(arrived_ref, q_ref, p_ref):
    total = arrived_ref[0]
    for i in range(1, arrived_ref.shape[0]):
        total = total + arrived_ref[i]
    lines = total.shape[0] // 2
    tiles = q_ref.shape[2] // LANES
    for i in range(3):
        for t in range(tiles):
            at = i * tiles + t
            q_ref[i, :, t * LANES : (t + 1) * LANES] = total[at : at + 1]
            p_ref[i, :, t * LANES : (t + 1) * LANES] = total[lines + at : lines + at + 1]


def shards(
    positions, momenta, species, neighbours, send_list, embedding, radial_one, radial_two, mix_one, mix_two,
    read_one, read_two,
):
    slots, atoms = neighbours.shape
    domains = lax.axis_size("space")
    beads = lax.axis_size("bead")
    outer = next(d for d in range(1, beads + 1) if beads % d == 0 and d * d >= beads)
    inner = beads // outer
    plan = ring_plan(domains, atoms)
    wide = plan[2]
    vmem = pl.BlockSpec(memory_space=pltpu.VMEM)
    smem = pl.BlockSpec(memory_space=pltpu.SMEM)
    far = pl.BlockSpec(memory_space=pltpu.HBM)
    small = pltpu.CompilerParams(vmem_limit_bytes=4 * MIB)
    coord_rows = jnp.transpose(positions, (1, 0, 2))
    moment_rows = jnp.transpose(momenta, (1, 0, 2))
    block = pl.pallas_call(
        pack_kernel,
        out_shape=jax.ShapeDtypeStruct((HEAD + slots, atoms), f32),
        in_specs=[far] * 4,
        out_specs=vmem,
        scratch_shapes=[
            pltpu.VMEM(coord_rows.shape, f32),
            pltpu.VMEM((1, atoms), jnp.int32),
            pltpu.VMEM((1, atoms), jnp.int32),
            pltpu.VMEM((slots, atoms), jnp.int32),
            pltpu.SemaphoreType.DMA((4,)),
        ],
        compiler_params=small,
        name="pack",
    )(in_hbm(coord_rows), in_hbm(species[None]), in_hbm(send_list[None]), in_hbm(neighbours))
    blocks = [block]
    for offset in wide[1:]:
        blocks.append(lax.ppermute(block, "space", [(i, (i - offset) % domains) for i in range(domains)]))
    chosen = choose(block, embedding, radial_one, radial_two, mix_one, mix_two, read_one, read_two)
    pushed, masses = pushes(plan, blocks, moment_rows, chosen)
    sources = [pushed]
    for shift in range(1, inner):
        pairs = [(b, b - b % inner + (b + shift) % inner) for b in range(beads)]
        sources.append(lax.ppermute(pushed, "bead", pairs))
    here = [lax.axis_index(axis).astype(jnp.int32).reshape(1) for axis in ("bead", "space")]
    lines = line_count(atoms)
    messages = pl.pallas_call(
        functools.partial(turn_kernel, (outer, inner, domains, wide)),
        out_shape=jax.ShapeDtypeStruct((outer * domains, 2 * lines, LANES), f32),
        in_specs=[smem, smem, vmem] + [vmem] * inner,
        out_specs=vmem,
        compiler_params=small,
        name="turn",
    )(*here, masses, *sources)
    rows = [[(z * inner + i) * domains + d for z in range(outer) for d in range(domains)] for i in range(inner)]
    arrived = lax.all_to_all(messages, ("bead", "space"), 0, 0, axis_index_groups=rows, tiled=True)
    new_q, new_p = pl.pallas_call(
        sum_kernel,
        out_shape=(jax.ShapeDtypeStruct((3, 1, atoms), f32),) * 2,
        in_specs=[vmem],
        out_specs=(vmem, vmem),
        compiler_params=small,
        name="sum",
    )(arrived)
    return (jnp.transpose(new_q, (1, 0, 2)), jnp.transpose(new_p, (1, 0, 2)))


def solution(mesh):
    placed = (
        P("bead", None, "space"),
        P("bead", None, "space"),
        P("space"),
        P(None, "space"),
        P("space"),
        P(),
        P(),
        P(),
        P(),
        P(),
        P(),
        P(),
    )
    return jax.shard_map(
        shards,
        mesh=mesh,
        in_specs=placed,
        out_specs=(P("bead", None, "space"), P("bead", None, "space")),
        check_vma=False,
    )
```

```python
import functools
import math

import jax
import jax.numpy as jnp
import numpy as np
from jax import lax
from jax.experimental import pallas as pl
from jax.experimental.pallas import tpu as pltpu
from jax.sharding import PartitionSpec as P

STEP = 2.0
HALF_STEP = 1.0
HEAVY = 16.0
SQRT3 = math.sqrt(3.0)
SQRT5 = math.sqrt(5.0)
SQRT15 = math.sqrt(15.0)
LANES = 128
ORDERS = 9
GROUP = (0, 1, 1, 1, 2, 2, 2, 2, 2)
HEAD = 8
MIB = 1024 * 1024
f32 = jnp.float32
bf16 = jnp.bfloat16


def split(x):
    hi = x.astype(bf16)
    return hi, (x - hi.astype(f32)).astype(bf16)


def split_rows(x):
    hi = x.astype(bf16).astype(f32)
    return jnp.concatenate([hi, x - hi], axis=0)


def dot(a, b):
    return jnp.dot(a, b, preferred_element_type=f32)


def dot_nt(a, b):
    return lax.dot_general(a, b, (((1,), (1,)), ((), ())), preferred_element_type=f32)


def in_turns(start, stop, step, most=4):
    per_turn = next(n for n in range(most, 0, -1) if (stop - start) % n == 0)

    def turn(i, carry):
        for j in range(per_turn):
            step(start + i * per_turn + j)
        return carry

    lax.fori_loop(0, (stop - start) // per_turn, turn, 0)


def row(x, rows=8):
    return jnp.broadcast_to(x, (rows, x.shape[1]))


def lookup(chunks, wanted, position):
    out = None
    for number, chunk in chunks:
        got = jnp.take_along_axis(row(chunk), position, axis=1, mode="promise_in_bounds")
        out = got if out is None else jnp.where(wanted == number, got, out)
    return out


def harmonics(ux, uy, uz):
    return [
        None,
        SQRT3 * ux,
        SQRT3 * uy,
        SQRT3 * uz,
        SQRT15 * ux * uy,
        SQRT15 * uy * uz,
        0.5 * SQRT5 * (2.0 * uz * uz - ux * ux - uy * uy),
        SQRT15 * ux * uz,
        0.5 * SQRT15 * (ux * ux - uy * uy),
    ]


def silu_parts(v):
    gate = 1.0 / (1.0 + jnp.exp(-v))
    return v * gate, gate * (1.0 + v * (1.0 - gate))


def choose_kernel(block_ref, *refs):
    sources = refs[:7]
    oh_ref, rrc_ref, r2c_ref, side_ref, rrr_ref, r2r_ref, mixa_ref, mixt_ref = refs[7:15]
    held = refs[15:22]
    sems = refs[22]
    emb_ref, rad1_ref, rad2_ref, mix1_ref, mix2_ref, read1_ref, read2_ref = held
    fetches = [pltpu.make_async_copy(src, dst, sems.at[i]) for i, (src, dst) in enumerate(zip(sources, held))]
    for fetch in fetches:
        fetch.start()
    chan = emb_ref.shape[1]
    bases = rad1_ref.shape[0]
    atoms = block_ref.shape[1]
    slots = block_ref.shape[0] - HEAD

    tile_edges = slots * LANES
    ids16 = lax.broadcasted_iota(jnp.int32, (LANES, tile_edges), 0).astype(jnp.int16)
    one16 = jnp.ones((LANES, tile_edges), bf16)
    zero16 = jnp.zeros((LANES, tile_edges), bf16)
    for t in range(atoms // LANES):
        slot = block_ref[HEAD : HEAD + slots, t * LANES : (t + 1) * LANES].astype(jnp.int32)
        line = jnp.concatenate([slot[k : k + 1, :] for k in range(slots)], axis=1)
        wanted = jnp.broadcast_to(line, (LANES, tile_edges)).astype(jnp.int16)
        for r in range(oh_ref.shape[0] // LANES):
            hit = wanted - jnp.int16(r * LANES) == ids16
            oh_ref[r * LANES : (r + 1) * LANES, t * tile_edges : (t + 1) * tile_edges] = jnp.where(hit, one16, zero16)

    for fetch in fetches:
        fetch.wait()
    emb0 = emb_ref[0:1, :]
    emb_d = emb_ref[1:2, :] - emb0
    rr = jnp.concatenate([rad1_ref[...] * emb0, rad1_ref[...] * emb_d], axis=0) * (1.0 / slots)
    rr_hi = rr.astype(bf16).astype(f32)
    rr_lo = rr - rr_hi
    r2 = rad2_ref[...] * (1.0 / slots)
    r2_hi = r2.astype(bf16).astype(f32)
    r2_lo = r2 - r2_hi
    zeros = jnp.zeros((8, chan), f32)
    turned1 = jnp.concatenate([rr_hi, rr_hi, rr_lo, rr_lo] + [zeros] * 8, axis=0).T
    sides = jnp.concatenate([emb0, emb_d, read1_ref[...], read2_ref[...], zeros[:4]], axis=0)
    turned2 = jnp.concatenate([r2_hi, r2_hi, r2_lo, r2_lo] + [zeros] * 12, axis=0).T
    rrc_ref[...] = turned1[:, : 8 * bases].astype(bf16)
    r2c_ref[...] = turned2[:, : 4 * bases].astype(bf16)
    side_ref[...] = jnp.concatenate([sides] + [zeros] * 15, axis=0).T
    rrr_ref[...] = jnp.concatenate(
        [jnp.concatenate([rr_hi, rr_hi], axis=1), jnp.concatenate([rr_lo, jnp.zeros_like(rr_lo)], axis=1)], axis=0
    ).astype(bf16)
    r2r_ref[...] = jnp.concatenate(
        [jnp.concatenate([r2_hi, r2_hi], axis=1), jnp.concatenate([r2_lo, jnp.zeros_like(r2_lo)], axis=1)], axis=0
    ).astype(bf16)
    for i, ref in enumerate((mix1_ref, mix2_ref)):
        hi, lo = split(ref[...])
        mixa_ref[i, 0:chan, :] = hi
        mixa_ref[i, chan:, :] = lo
        for g in range(3):
            hi, lo = split(ref[:, g * chan : (g + 1) * chan].T)
            mixt_ref[i, g, 0:chan, :] = hi
            mixt_ref[i, g, chan:, :] = lo


def dot_parts(both, hi, lo):
    rows = both.shape[0] // 2
    first = dot(both, hi)
    return first[:rows] + first[rows:] + dot(both[:rows], lo)


def edge_kernel(plan, *refs):
    atoms, near, wide, before, after = plan
    n_wide = len(wide)
    blocks = refs[:n_wide]
    geo_ref, y_ref, yb_ref, ub_ref, bk_ref, bt_ref, gidx_ref, pick_ref, as_ref = refs[n_wide:]
    bases = bk_ref.shape[0]
    slots = gidx_ref.shape[0]
    tiles = atoms // LANES
    half = atoms // 2
    half_tiles = half // LANES
    order_col = lax.broadcasted_iota(jnp.int32, (bases, LANES), 0).astype(f32)
    tables = []
    for quantity in range(4):
        chunks = []
        for g in range(n_wide):
            for t in range(tiles):
                chunks.append((g * tiles + t, blocks[g][quantity : quantity + 1, t * LANES : (t + 1) * LANES]))
        tables.append(chunks)
    for q in range(len(near)):
        ghosts = []
        for t in range(half_tiles):
            ghosts.append(
                (t, blocks[before[q]][4:5, half + t * LANES : half + (t + 1) * LANES] + float(before[q] * atoms))
            )
        for t in range(half_tiles):
            ghosts.append(
                (
                    half_tiles + tiles + t,
                    blocks[after[q]][4:5, t * LANES : (t + 1) * LANES] + float(after[q] * atoms),
                )
            )
        if q == 0:
            ids16 = lax.broadcasted_iota(jnp.int32, (pick_ref.shape[0], LANES), 0).astype(jnp.int16)
            one16 = jnp.ones(ids16.shape, bf16)
            zero16 = jnp.zeros(ids16.shape, bf16)
            for t, (_, chunk) in enumerate(ghosts):
                wanted = jnp.broadcast_to(chunk.astype(jnp.int32), ids16.shape).astype(jnp.int16)
                pick_ref[:, t * LANES : (t + 1) * LANES] = jnp.where(wanted == ids16, one16, zero16)
        for t in range(tiles):
            cols = slice(t * LANES, (t + 1) * LANES)
            here = slice(q * atoms + t * LANES, q * atoms + (t + 1) * LANES)
            slot = blocks[q][HEAD : HEAD + slots, cols].astype(jnp.int32)
            chunk_no = slot >> 7
            far = lookup(ghosts, chunk_no, slot & 127).astype(jnp.int32)
            own = (slot >= half) & (slot < half + atoms)
            gidx = jnp.where(own, slot + (q * atoms - half), far)
            gidx_ref[:, here] = gidx
            chunk_no = gidx >> 7
            place = gidx & 127
            xj, yj, zj, fj = [lookup(tables[i], chunk_no, place) for i in range(4)]
            rx = xj - row(blocks[q][0:1, cols])
            ry = yj - row(blocks[q][1:2, cols])
            rz = zj - row(blocks[q][2:3, cols])
            soft = jnp.sqrt(rx * rx + ry * ry + rz * rz + 1.0)
            back = 1.0 / soft
            ux, uy, uz = rx * back, ry * back, rz * back
            for i, value in enumerate((ux, uy, uz, back, soft, fj)):
                geo_ref[i, :, here] = value
            if q == 0:
                for i, value in enumerate((ux, uy, uz)):
                    for k in range(slots):
                        ub_ref[i, k, :, cols] = row(value[k : k + 1, :])
            sphere = harmonics(ux, uy, uz)
            for l in range(1, ORDERS):
                y_ref[l - 1, :, here] = sphere[l]
                if q == 0:
                    for k in range(slots):
                        yb_ref[l - 1, k, :, cols] = row(sphere[l][k : k + 1, :])
            for n in range(bases):
                bk_ref[n, :, here] = jnp.exp(-0.5 * (soft - (1.0 + n)) ** 2)
            for k in range(slots):
                basis = jnp.exp(-0.5 * (row(soft[k : k + 1, :], bases) - (1.0 + order_col)) ** 2)
                bt_ref[k, 0:bases, here] = basis
                bt_ref[k, bases : 2 * bases, here] = basis * row(fj[k : k + 1, :], bases)
            low = [None] * ORDERS
            for k in range(slots):
                basis = bt_ref[k, :, here]
                for l in range(ORDERS):
                    term = basis if l == 0 else basis * row(y_ref[l - 1, k : k + 1, here], 2 * bases)
                    low[l] = term if low[l] is None else low[l] + term
            for l in range(ORDERS):
                both = split_rows(low[l]).astype(bf16)
                as_ref[l, 0 : 4 * bases, here] = both
                as_ref[l, 4 * bases : 8 * bases, here] = both


def first_kernel(plan, *refs):
    atoms, near, wide, _, _ = plan
    n_wide = len(wide)
    blocks = refs[:n_wide]
    as_ref, rrc_ref, side_ref, mixa_ref, m1_ref, sp1_ref, hs_ref, flag_ref = refs[n_wide:]
    chan = m1_ref.shape[1]
    n_near = m1_ref.shape[2]

    for q in range(len(near)):
        flag_ref[0:1, q * atoms : (q + 1) * atoms] = blocks[q][3:4, :]
    wide_cols = 2 * LANES
    emb0_col = side_ref[:, 0:1]
    embd_col = side_ref[:, 1:2]

    def first(j):
        here = pl.ds(pl.multiple_of(j * wide_cols, wide_cols), wide_cols)
        inv = [None, None, None]
        for l in range(ORDERS):
            m = dot(rrc_ref[...], as_ref[l, :, here])
            m1_ref[l, :, here] = m
            inv[GROUP[l]] = m * m if inv[GROUP[l]] is None else inv[GROUP[l]] + m * m
        hi, lo = split(jnp.concatenate(inv, axis=0))
        value = dot_parts(mixa_ref[0], hi, lo)
        act, slope = silu_parts(value)
        sp1_ref[:, here] = slope
        hidden = act + emb0_col + embd_col * flag_ref[0:1, here]
        hi, lo = split(hidden)
        hs_ref[0:chan, here] = hi
        hs_ref[chan : 2 * chan, here] = lo

    in_turns(0, n_near // wide_cols, first)


def second_kernel(hs_ref, oh_ref, pick_ref, bt_ref, r2c_ref, yb_ref, mixa_ref, mixt_ref, side_ref,
                  hj_ref, w_ref, car_ref, m2_ref, dinv_ref, ext_ref, inv_ref):
    slots = yb_ref.shape[1]
    bases = bt_ref.shape[1] // 2
    chan, atoms = m2_ref.shape[1:]
    tiles = atoms // LANES
    half = atoms // 2
    wide_cols = 2 * LANES
    tile_edges = slots * LANES
    turns = tile_edges // wide_cols
    rows = chan // turns
    ghosts = dot(hs_ref[...], pick_ref[...]).astype(bf16)
    ext_ref[:, 0:half] = ghosts[:, :half]
    ext_ref[:, half : half + atoms] = hs_ref[:, 0:atoms]
    ext_ref[:, half + atoms :] = ghosts[:, half:]
    for t in range(tiles):
        cols = slice(t * LANES, (t + 1) * LANES)
        basis = jnp.concatenate([split_rows(bt_ref[k, 0:bases, cols]) for k in range(slots)], axis=1)
        w_ref[:, t * tile_edges : (t + 1) * tile_edges] = dot(
            r2c_ref[...], jnp.concatenate([basis, basis], axis=0).astype(bf16)
        )

    def gather(t, turn):
        here = pl.ds(pl.multiple_of(t * tile_edges + turn * wide_cols, LANES), wide_cols)
        both = dot(ext_ref[...], oh_ref[:, here])
        feat = both[:chan] + both[chan:]
        hj_ref[:, here] = feat
        car_ref[:, here] = feat * w_ref[:, here]

    def moments(t, turn):
        cols = slice(t * LANES, (t + 1) * LANES)
        base = pl.multiple_of(turn * rows, rows)
        acc = [[None] * ORDERS for _ in range(rows // 8)]
        for k in range(slots):
            at = t * tile_edges + k * LANES
            got = car_ref[pl.ds(base, rows), at : at + LANES]
            for l in range(ORDERS):
                yb = yb_ref[l - 1, k, :, cols] if l else None
                for h in range(rows // 8):
                    part = got[8 * h : 8 * h + 8]
                    term = part * yb if l else part
                    acc[h][l] = term if acc[h][l] is None else acc[h][l] + term
        for h in range(rows // 8):
            inv = [None] * 3
            for l in range(ORDERS):
                m2_ref[l, pl.ds(pl.multiple_of(base + 8 * h, 8), 8), cols] = acc[h][l]
                sq = acc[h][l] * acc[h][l]
                g = GROUP[l]
                inv[g] = sq if inv[g] is None else inv[g] + sq
            for g in range(3):
                inv_ref[pl.ds(pl.multiple_of(g * chan + base + 8 * h, 8), 8), cols] = inv[g]

    for turn in range(turns):
        gather(0, turn)
    for t in range(tiles):

        def both_parts(turn, carry, t=t):
            moments(t, turn)
            if t + 1 < tiles:
                gather(t + 1, turn)
            return carry

        lax.fori_loop(0, turns, both_parts, 0)
    read2_col = side_ref[:, 3:4]
    for t in range(atoms // wide_cols):
        cols = slice(t * wide_cols, (t + 1) * wide_cols)
        hi, lo = split(inv_ref[:, cols])
        _, slope = silu_parts(dot_parts(mixa_ref[1], hi, lo))
        hi, lo = split(slope * (2.0 * read2_col))
        for g, scale in enumerate((1.0, 0.5 * SQRT3, 0.5 * SQRT15)):
            dinv_ref[g * chan : (g + 1) * chan, cols] = scale * dot_parts(mixt_ref[1, g], hi, lo)


def back_second_kernel(m2_ref, dinv_ref, car_ref, hj_ref, w_ref, ub_ref, oh_ref, pick_ref, side_ref, bt_ref, geo_ref,
                       r2r_ref, gidx_ref, dh_ref, q_ref, ohlo_ref, ds_ref, p_ref, sum_ref, *tile_refs):
    slots = ub_ref.shape[1]
    bases = bt_ref.shape[1] // 2
    chan, atoms = m2_ref.shape[1:]
    n_near = dh_ref.shape[1]
    tiles = atoms // LANES
    half = atoms // 2
    tile_edges = slots * LANES
    dhe_refs, dw_refs = tile_refs[:tiles], tile_refs[tiles:]
    turns, _, span = sum_ref.shape
    per_turn = chan // 16 // turns

    def spread_part(t, turn):
        picked = oh_ref[pl.ds(pl.multiple_of(turn * span, span), span), t * tile_edges : (t + 1) * tile_edges]
        part = dot_nt(dhe_refs[t][...], picked)
        return part if t == 0 else sum_ref[turn] + part

    def one(t, c, acc):
        cols = slice(t * LANES, (t + 1) * LANES)
        forms = []
        for h in range(2):
            rows = pl.ds(pl.multiple_of(c * 16 + 8 * h, 8), 8)
            scale = [dinv_ref[pl.ds(pl.multiple_of(g * chan + c * 16 + 8 * h, 8), 8), cols] for g in range(3)]
            dm = [m2_ref[l, rows, cols] * scale[GROUP[l]] for l in range(ORDERS)]
            low = dm[6] * (1.0 / SQRT3)
            forms.append((dm[0], dm[1], dm[2], dm[3], dm[8] - low, -dm[8] - low, low + low, dm[4], dm[5], dm[7]))
        base = pl.multiple_of(c * 16, 16)
        for k in range(slots):
            at = slice(t * tile_edges + k * LANES, t * tile_edges + (k + 1) * LANES)
            in_tile = slice(k * LANES, (k + 1) * LANES)
            got = car_ref[pl.ds(base, 16), at]
            ux, uy, uz = [ub_ref[i, k, :, cols] for i in range(3)]
            out = []
            for h in range(2):
                mid, dx, dy, dz, qxx, qyy, qzz, qxy, qyz, qxz = forms[h]
                gx = dx + qxx * ux + qxy * uy + qxz * uz
                gy = dy + qxy * ux + qyy * uy + qyz * uz
                gz = dz + qxz * ux + qyz * uy + qzz * uz
                out.append(mid + (gx + dx) * ux + (gy + dy) * uy + (gz + dz) * uz)
                part = got[8 * h : 8 * h + 8]
                for i, g in enumerate((gx, gy, gz)):
                    acc[3 * k + i] = acc[3 * k + i] + part * g
            dcar = jnp.concatenate(out, axis=0)
            for ref, other in ((dhe_refs[t], w_ref), (dw_refs[t], hj_ref)):
                hi, lo = split(dcar * other[pl.ds(base, 16), at])
                ref[pl.ds(base, 16), in_tile] = hi
                ref[pl.ds(pl.multiple_of(chan + c * 16, 16), 16), in_tile] = lo

    for t in range(tiles):
        cols = slice(t * LANES, (t + 1) * LANES)

        def both_parts(turn, acc, t=t):
            acc = list(acc)
            for i in range(per_turn):
                one(t, per_turn * turn + i, acc)
            if t:
                sum_ref[turn] = spread_part(t - 1, turn)
            return tuple(acc)

        start = tuple(jnp.zeros((8, LANES), f32) for _ in range(3 * slots))
        acc = lax.fori_loop(0, turns, both_parts, start)
        for k in range(slots):
            for i in range(3):
                p_ref[i, 8 * k : 8 * k + 8, cols] = acc[3 * k + i]
    both = jnp.concatenate([spread_part(tiles - 1, turn) for turn in range(turns)], axis=1)
    ext = both[:chan] + both[chan:]
    hi, lo = split(jnp.concatenate([ext[:, :half], ext[:, half + atoms :]], axis=1))
    spread = dot_nt(jnp.concatenate([hi, lo], axis=0), pick_ref[...])
    spread = spread[:chan] + spread[chan:]
    dh_ref[:, 0:atoms] = spread[:, :atoms] + ext[:, half : half + atoms] + side_ref[:, 2:3]
    if n_near > atoms:
        dh_ref[:, atoms:] = spread[:, atoms:]

    ids16 = lax.broadcasted_iota(jnp.int32, (LANES, n_near), 0).astype(jnp.int16)
    one16 = jnp.ones((LANES, n_near), bf16)
    zero16 = jnp.zeros((LANES, n_near), bf16)
    for k in range(slots):
        place = jnp.broadcast_to(gidx_ref[k : k + 1, :] & 127, (LANES, n_near)).astype(jnp.int16)
        ohlo_ref[:, k * n_near : (k + 1) * n_near] = jnp.where(place == ids16, one16, zero16)
    reach = 1.0 + lax.broadcasted_iota(jnp.int32, (bases, LANES), 0).astype(f32)
    for t in range(tiles):
        cols = slice(t * LANES, (t + 1) * LANES)
        small = dot(r2r_ref[...], dw_refs[t][...])
        dbasis = small[:bases] + small[bases:]
        for k in range(slots):
            far = reach - row(geo_ref[4, k : k + 1, cols], bases)
            ds_ref[k * 8 : k * 8 + 8, cols] = dbasis[:, k * LANES : (k + 1) * LANES] * bt_ref[k, 0:bases, cols] * far
    lane = lax.broadcasted_iota(jnp.int32, (slots, 16 * slots), 1)
    sub = lax.broadcasted_iota(jnp.int32, (slots, 16 * slots), 0)
    adder = jnp.where(((lane >> 3) & (slots - 1)) == sub, 1.0, 0.0).astype(bf16)
    for i in range(4):
        total = dot(adder, split_rows(p_ref[i - 1, :, :] if i else ds_ref[...]).astype(bf16))
        q_ref[8 * i : 8 * i + 8, :] = 2.0 * total if i else total


def back_first_kernel(dh_ref, sp1_ref, m1_ref, mixt_ref, rrr_ref, da_ref):
    n_near = sp1_ref.shape[1]
    rows = rrr_ref.shape[0] // 2
    wide_cols = 2 * LANES

    def back_first(j):
        here = pl.ds(pl.multiple_of(j * wide_cols, wide_cols), wide_cols)
        hi, lo = split(dh_ref[:, here] * sp1_ref[:, here] * 2.0)
        scale = [dot_parts(mixt_ref[0, g], hi, lo) for g in range(3)]
        for l in range(ORDERS):
            hi, lo = split(m1_ref[l, :, here] * scale[GROUP[l]])
            out = dot(rrr_ref[...], jnp.concatenate([hi, lo], axis=0))
            da_ref[l, :, here] = out[:rows] + out[rows:]

    in_turns(0, n_near // wide_cols, back_first)


def back_edge_kernel(plan, *refs):
    atoms, near, wide, _, _ = plan
    n_wide = len(wide)
    blocks = refs[:n_wide]
    moment_src, geo_ref, y_ref, bk_ref, gidx_ref, da_ref, q_ref, ohlo_ref = refs[n_wide : n_wide + 8]
    push_ref, mass_ref, val_ref, dr_ref, moment_ref, sem = refs[n_wide + 8 :]
    fetch = pltpu.make_async_copy(moment_src, moment_ref, sem)
    fetch.start()
    bases, slots, n_near = bk_ref.shape
    tiles = atoms // LANES
    top_rows = val_ref.shape[0] // 6

    def back_geometry(t, mine):
        here = pl.ds(pl.multiple_of(t * LANES, LANES), LANES)
        ux, uy, uz, back, soft, fj = [geo_ref[i, :, here] for i in range(6)]
        dy = [None] * ORDERS
        ds = None
        for n in range(bases):
            basis = bk_ref[n, :, here]
            db = None
            for l in range(ORDERS):
                g = row(da_ref[l, n : n + 1, here]) + fj * row(da_ref[l, bases + n : bases + n + 1, here])
                if l:
                    dy[l] = g * basis if dy[l] is None else dy[l] + g * basis
                    db = db + g * y_ref[l - 1, :, here]
                else:
                    db = g
            db = db * basis * ((1.0 + n) - soft)
            ds = db if ds is None else ds + db
        if mine:
            ds = ds + q_ref[0:8, here]
        dux = SQRT3 * dy[1] + SQRT15 * (uy * dy[4] + uz * dy[7] + ux * dy[8]) - SQRT5 * ux * dy[6]
        duy = SQRT3 * dy[2] + SQRT15 * (ux * dy[4] + uz * dy[5] - uy * dy[8]) - SQRT5 * uy * dy[6]
        duz = SQRT3 * dy[3] + SQRT15 * (uy * dy[5] + ux * dy[7]) + 2.0 * SQRT5 * uz * dy[6]
        if mine:
            dux, duy, duz = [d + q_ref[8 * i : 8 * i + 8, here] for i, d in ((1, dux), (2, duy), (3, duz))]
        along = ds - (ux * dux + uy * duy + uz * duz) * back
        for i, value in enumerate((dux * back + along * ux, duy * back + along * uy, duz * back + along * uz)):
            dr_ref[i, :, here] = value

    in_turns(0, tiles, lambda t: back_geometry(t, True))
    in_turns(tiles, n_near // LANES, lambda t: back_geometry(t, False))

    def place_tile(t):
        here = pl.ds(pl.multiple_of(t * LANES, LANES), LANES)
        gidx = gidx_ref[:, here]
        chunk_no = gidx >> 7
        parts = []
        for i in range(3):
            value = dr_ref[i, :, here]
            hi = value.astype(bf16).astype(f32)
            parts.append((hi, value - hi))
        chunk_ids = lax.broadcasted_iota(jnp.int32, (top_rows, LANES), 0)
        for k in range(slots):
            at = pl.ds(pl.multiple_of(k * n_near + t * LANES, LANES), LANES)
            hit = chunk_ids == row(chunk_no[k : k + 1, :], top_rows)
            for i in range(3):
                both = [jnp.where(hit, row(part[k : k + 1, :], top_rows), 0.0) for part in parts[i]]
                val_ref[2 * i * top_rows : 2 * (i + 1) * top_rows, at] = jnp.concatenate(both, axis=0).astype(bf16)

    in_turns(0, n_near // LANES, place_tile)
    landed = dot_nt(val_ref[...], ohlo_ref[...])
    fetch.wait()
    lines = push_ref.shape[0] // (n_wide + 1)
    for i in range(3):
        total = (
            landed[2 * i * top_rows : (2 * i + 1) * top_rows] + landed[(2 * i + 1) * top_rows : (2 * i + 2) * top_rows]
        )
        for g in range(n_wide):
            for t in range(tiles):
                cols = slice(t * LANES, (t + 1) * LANES)
                line = total[g * tiles + t : g * tiles + t + 1, :]
                if g < len(near):
                    here = slice(g * atoms + t * LANES, g * atoms + (t + 1) * LANES)
                    line = line - jnp.sum(dr_ref[i, :, here], axis=0, keepdims=True)
                line = -HALF_STEP * line
                at = i * tiles + t
                if g == 0:
                    line = line + moment_ref[i, :, cols]
                    push_ref[at : at + 1, :] = blocks[0][i : i + 1, cols]
                push_ref[(1 + g) * lines + at : (1 + g) * lines + at + 1, :] = line
                mass = HEAVY - (HEAVY - 1.0) * blocks[g][3:4, cols]
                mass_ref[g * lines + at : g * lines + at + 1, :] = mass
    if lines > 3 * tiles:
        for g in range(n_wide + 1):
            blank = slice(g * lines + 3 * tiles, (g + 1) * lines)
            push_ref[blank, :] = jnp.zeros((lines - 3 * tiles, LANES), f32)
            if g < n_wide:
                mass_ref[blank, :] = jnp.ones((lines - 3 * tiles, LANES), f32)


def in_hbm(x):
    return pltpu.with_memory_space_constraint(x, pltpu.HBM)


def run(name, body, operands, results, scratch=(), far=(), cost=None):
    sizes = [math.prod(x.shape) * x.dtype.itemsize // 3 for i, x in enumerate(operands) if i not in far]
    sizes += [math.prod(shape) * jnp.dtype(dtype).itemsize for shape, dtype in results]
    sizes += [math.prod(x.shape) * x.dtype.itemsize for x in scratch if x.memory_space == pltpu.VMEM]
    limit = sum(sizes) + 4 * MIB
    specs = [pl.BlockSpec(memory_space=pltpu.HBM if i in far else pltpu.VMEM) for i in range(len(operands))]
    return pl.pallas_call(
        body,
        out_shape=tuple(jax.ShapeDtypeStruct(shape, dtype) for shape, dtype in results),
        in_specs=specs,
        out_specs=tuple(pl.BlockSpec(memory_space=pltpu.VMEM) for _ in results),
        scratch_shapes=list(scratch),
        compiler_params=pltpu.CompilerParams(vmem_limit_bytes=limit),
        cost_estimate=cost,
        name=name,
    )(*[in_hbm(x) if i in far else x for i, x in enumerate(operands)])


def choose(block, embedding, radial_one, radial_two, mix_one, mix_two, read_one, read_two):
    atoms = block.shape[1]
    slots = block.shape[0] - HEAD
    chan = embedding.shape[1]
    bases = radial_one.shape[0]
    weights = (embedding, radial_one, radial_two, mix_one, mix_two, read_one[None], read_two[None])
    return run(
        "choose",
        choose_kernel,
        (block, *weights),
        (
            ((2 * atoms, slots * atoms), bf16),
            ((chan, 8 * bases), bf16),
            ((chan, 4 * bases), bf16),
            ((chan, LANES), f32),
            ((4 * bases, 2 * chan), bf16),
            ((2 * bases, 2 * chan), bf16),
            ((2, 2 * chan, 3 * chan), bf16),
            ((2, 3, 2 * chan, chan), bf16),
        ),
        [pltpu.VMEM(w.shape, f32) for w in weights] + [pltpu.SemaphoreType.DMA((len(weights),))],
        range(1, 1 + len(weights)),
        cost=pl.CostEstimate(flops=2 * 10**9, bytes_accessed=2 * 10**6, transcendentals=0),
    )


def pushes(plan, blocks, momenta, chosen):
    atoms, near, wide, _, _ = plan
    oh, rrc, r2c, sides, rrr, r2r, mixa, mixt = chosen
    chan = rrc.shape[0]
    bases = r2r.shape[0] // 2
    slots = blocks[0].shape[0] - HEAD
    n_near = len(near) * atoms
    edges = slots * atoms
    top_rows = -(-len(wide) * atoms // LANES // 8) * 8
    lines = line_count(atoms)
    geo, y, yb, ub, bk, bt, gidx, pick, as1 = run(
        "edges",
        functools.partial(edge_kernel, plan),
        blocks,
        (
            ((6, slots, n_near), f32),
            ((ORDERS - 1, slots, n_near), f32),
            ((ORDERS - 1, slots, 8, atoms), f32),
            ((3, slots, 8, atoms), f32),
            ((bases, slots, n_near), f32),
            ((slots, 2 * bases, n_near), f32),
            ((slots, n_near), jnp.int32),
            ((n_near, atoms), bf16),
            ((ORDERS, 8 * bases, n_near), bf16),
        ),
    )
    m1, sp1, hs = run(
        "first",
        functools.partial(first_kernel, plan),
        (*blocks, as1, rrc, sides, mixa),
        (((ORDERS, chan, n_near), f32), ((chan, n_near), f32), ((2 * chan, n_near), bf16)),
        [pltpu.VMEM((8, n_near), f32)],
    )
    tiles = atoms // LANES
    turns = slots // 2
    hj, w, car, m2, dinv = run(
        "second",
        second_kernel,
        (hs, oh, pick, bt, r2c, yb, mixa, mixt, sides),
        (((chan, edges), f32),) * 3 + (((ORDERS, chan, atoms), f32), ((3 * chan, atoms), f32)),
        [pltpu.VMEM((2 * chan, 2 * atoms), bf16), pltpu.VMEM((3 * chan, atoms), f32)],
    )
    dh, q, ohlo = run(
        "back_second",
        back_second_kernel,
        (m2, dinv, car, hj, w, ub, oh, pick, sides, bt, geo, r2r, gidx),
        (((chan, n_near), f32), ((4 * slots, atoms), f32), ((LANES, slots * n_near), bf16)),
        [
            pltpu.VMEM((8 * slots, atoms), f32),
            pltpu.VMEM((3, 8 * slots, atoms), f32),
            pltpu.VMEM((turns, 2 * chan, 2 * atoms // turns), f32),
        ]
        + [pltpu.VMEM((2 * chan, slots * LANES), bf16)] * (2 * tiles),
    )
    (da,) = run("back_first", back_first_kernel, (dh, sp1, m1, mixt, rrr), (((ORDERS, 2 * bases, n_near), f32),))
    return run(
        "back_edges",
        functools.partial(back_edge_kernel, plan),
        (*blocks, momenta, geo, y, bk, gidx, da, q, ohlo),
        ((((len(wide) + 1) * lines, LANES), f32), ((len(wide) * lines, LANES), f32)),
        [
            pltpu.VMEM((6 * top_rows, slots * n_near), bf16),
            pltpu.VMEM((3, slots, n_near), f32),
            pltpu.VMEM(momenta.shape, f32),
            pltpu.SemaphoreType.DMA(()),
        ],
        (len(blocks),),
    )


def line_count(atoms):
    return -(-3 * (atoms // LANES) // 8) * 8


def ring_plan(domains, atoms):
    near = list(dict.fromkeys(o % domains for o in (0, 1, -1)))
    wide = list(dict.fromkeys(near + [o % domains for o in (2, -2)]))
    before = tuple(wide.index((o - 1) % domains) for o in near)
    after = tuple(wide.index((o + 1) % domains) for o in near)
    return atoms, tuple(near), tuple(wide), before, after


def mode_turns(bead_total):
    bead = np.arange(bead_total, dtype=np.float64)[:, None]
    mode = np.arange(bead_total, dtype=np.float64)[None, :]
    phase = 2.0 * np.pi * bead * mode / bead_total
    half_total = bead_total // 2
    table = math.sqrt(2.0 / bead_total) * np.where(mode < half_total, np.cos(phase), np.sin(phase))
    table = np.where(mode == half_total, np.cos(np.pi * bead) / math.sqrt(bead_total), table)
    table = np.where(mode == 0, 1.0 / math.sqrt(bead_total), table)
    angles = bead_total * np.sin(np.pi * mode[0] / bead_total)
    safe = np.where(mode[0] == 0, 1.0, angles)
    reach = np.where(mode[0] == 0, STEP, STEP * np.sin(angles) / safe)
    stiff = angles * np.sin(angles) / STEP
    return [[float(x) for x in (table * factor[None, :]) @ table[0]] for factor in (np.cos(angles), reach, stiff)]


def pack_kernel(coord_src, species_src, send_src, slot_src, block_ref, coord_ref, species_ref, send_ref, slot_ref, sems):
    pairs = ((coord_src, coord_ref), (species_src, species_ref), (send_src, send_ref), (slot_src, slot_ref))
    fetches = [pltpu.make_async_copy(src, dst, sems.at[i]) for i, (src, dst) in enumerate(pairs)]
    for fetch in fetches:
        fetch.start()
    for fetch in fetches:
        fetch.wait()
    atoms = block_ref.shape[1]
    for i in range(3):
        block_ref[i : i + 1, :] = coord_ref[i]
    block_ref[3:4, :] = species_ref[...].astype(f32)
    block_ref[4:5, :] = send_ref[...].astype(f32)
    block_ref[5:HEAD, :] = jnp.zeros((HEAD - 5, atoms), f32)
    block_ref[HEAD:, :] = slot_ref[...].astype(f32)


def turn_kernel(shape, bead_ref, domain_ref, mass_ref, *refs):
    outer, inner, domains, wide = shape
    message_ref = refs[outer]
    turns = mode_turns(outer * inner)
    lines = mass_ref.shape[0] // len(wide)
    my_domain = domain_ref[0]
    my_inner = lax.rem(bead_ref[0], inner)
    if domains > len(wide):
        message_ref[...] = jnp.zeros_like(message_ref)
    masses = [mass_ref[g * lines : (g + 1) * lines, :] for g in range(len(wide))]
    sources = []
    for z in range(outer):
        sources.append([refs[z][g * lines : (g + 1) * lines, :] for g in range(len(wide) + 1)])
    for s in range(inner):
        wraps = jnp.full((lines, LANES), my_inner + s) >= inner
        weights = []
        for turn in turns:
            row_of = []
            for z in range(outer):
                there = turn[(z * inner + s) % (outer * inner)]
                round_it = turn[(z * inner + s - inner) % (outer * inner)]
                row_of.append(jnp.where(wraps, jnp.full((lines, LANES), round_it), jnp.full((lines, LANES), there)))
            weights.append(row_of)
        to_inner = lax.rem(my_inner + s, inner)
        for g in range(len(wide)):
            turned = sum(weights[0][z] * sources[z][1 + g] for z in range(outer))
            drift = sum(weights[1][z] * sources[z][1 + g] for z in range(outer))
            new_q = drift / masses[g]
            new_p = turned
            if g == 0:
                new_q = new_q + sum(weights[0][z] * sources[z][0] for z in range(outer))
                new_p = new_p - masses[g] * sum(weights[2][z] * sources[z][0] for z in range(outer))
            to = to_inner * domains + lax.rem(my_domain + wide[g], domains)
            message_ref[to, 0:lines, :] = new_q
            message_ref[to, lines:, :] = new_p


def sum_kernel(arrived_ref, q_ref, p_ref):
    total = arrived_ref[0]
    for i in range(1, arrived_ref.shape[0]):
        total = total + arrived_ref[i]
    lines = total.shape[0] // 2
    tiles = q_ref.shape[2] // LANES
    for i in range(3):
        for t in range(tiles):
            at = i * tiles + t
            q_ref[i, :, t * LANES : (t + 1) * LANES] = total[at : at + 1]
            p_ref[i, :, t * LANES : (t + 1) * LANES] = total[lines + at : lines + at + 1]


def shards(
    positions, momenta, species, neighbours, send_list, embedding, radial_one, radial_two, mix_one, mix_two,
    read_one, read_two,
):
    slots, atoms = neighbours.shape
    domains = lax.axis_size("space")
    beads = lax.axis_size("bead")
    inner = next(d for d in range(1, beads + 1) if beads % d == 0 and d * d >= beads)
    outer = beads // inner
    plan = ring_plan(domains, atoms)
    wide = plan[2]
    vmem = pl.BlockSpec(memory_space=pltpu.VMEM)
    smem = pl.BlockSpec(memory_space=pltpu.SMEM)
    far = pl.BlockSpec(memory_space=pltpu.HBM)
    small = pltpu.CompilerParams(vmem_limit_bytes=4 * MIB)
    coord_rows = jnp.transpose(positions, (1, 0, 2))
    moment_rows = jnp.transpose(momenta, (1, 0, 2))
    block = pl.pallas_call(
        pack_kernel,
        out_shape=jax.ShapeDtypeStruct((HEAD + slots, atoms), f32),
        in_specs=[far] * 4,
        out_specs=vmem,
        scratch_shapes=[
            pltpu.VMEM(coord_rows.shape, f32),
            pltpu.VMEM((1, atoms), jnp.int32),
            pltpu.VMEM((1, atoms), jnp.int32),
            pltpu.VMEM((slots, atoms), jnp.int32),
            pltpu.SemaphoreType.DMA((4,)),
        ],
        compiler_params=small,
        name="pack",
    )(in_hbm(coord_rows), in_hbm(species[None]), in_hbm(send_list[None]), in_hbm(neighbours))
    blocks = [block]
    for offset in wide[1:]:
        blocks.append(lax.ppermute(block, "space", [(i, (i - offset) % domains) for i in range(domains)]))
    chosen = choose(block, embedding, radial_one, radial_two, mix_one, mix_two, read_one, read_two)
    pushed, masses = pushes(plan, blocks, moment_rows, chosen)
    sources = [pushed]
    for z in range(1, outer):
        sources.append(lax.ppermute(pushed, "bead", [(b, (b + z * inner) % beads) for b in range(beads)]))
    here = [lax.axis_index(axis).astype(jnp.int32).reshape(1) for axis in ("bead", "space")]
    lines = line_count(atoms)
    messages = pl.pallas_call(
        functools.partial(turn_kernel, (outer, inner, domains, wide)),
        out_shape=jax.ShapeDtypeStruct((inner * domains, 2 * lines, LANES), f32),
        in_specs=[smem, smem, vmem] + [vmem] * outer,
        out_specs=vmem,
        compiler_params=small,
        name="turn",
    )(*here, masses, *sources)
    rows = [[z * inner * domains + i for i in range(inner * domains)] for z in range(outer)]
    arrived = lax.all_to_all(messages, ("bead", "space"), 0, 0, axis_index_groups=rows, tiled=True)
    new_q, new_p = pl.pallas_call(
        sum_kernel,
        out_shape=(jax.ShapeDtypeStruct((3, 1, atoms), f32),) * 2,
        in_specs=[vmem],
        out_specs=(vmem, vmem),
        compiler_params=small,
        name="sum",
    )(arrived)
    return (jnp.transpose(new_q, (1, 0, 2)), jnp.transpose(new_p, (1, 0, 2)))


def solution(mesh):
    placed = (
        P("bead", None, "space"),
        P("bead", None, "space"),
        P("space"),
        P(None, "space"),
        P("space"),
        P(),
        P(),
        P(),
        P(),
        P(),
        P(),
        P(),
    )
    return jax.shard_map(
        shards,
        mesh=mesh,
        in_specs=placed,
        out_specs=(P("bead", None, "space"), P("bead", None, "space")),
        check_vma=False,
    )
```

```python
import functools
import math

import jax
import jax.numpy as jnp
import numpy as np
from jax import lax
from jax.experimental import pallas as pl
from jax.experimental.pallas import tpu as pltpu
from jax.sharding import PartitionSpec as P

STEP = 2.0
HALF_STEP = 1.0
HEAVY = 16.0
SQRT3 = math.sqrt(3.0)
SQRT5 = math.sqrt(5.0)
SQRT15 = math.sqrt(15.0)
LANES = 128
ORDERS = 9
GROUP = (0, 1, 1, 1, 2, 2, 2, 2, 2)
HEAD = 8
MIB = 1024 * 1024
f32 = jnp.float32
bf16 = jnp.bfloat16


def split(x):
    hi = x.astype(bf16)
    return hi, (x - hi.astype(f32)).astype(bf16)


def split_rows(x):
    hi = x.astype(bf16).astype(f32)
    return jnp.concatenate([hi, x - hi], axis=0)


def dot(a, b):
    return jnp.dot(a, b, preferred_element_type=f32)


def dot_nt(a, b):
    return lax.dot_general(a, b, (((1,), (1,)), ((), ())), preferred_element_type=f32)


def in_turns(start, stop, step, most=4):
    per_turn = next(n for n in range(most, 0, -1) if (stop - start) % n == 0)

    def turn(i, carry):
        for j in range(per_turn):
            step(start + i * per_turn + j)
        return carry

    lax.fori_loop(0, (stop - start) // per_turn, turn, 0)


def row(x, rows=8):
    return jnp.broadcast_to(x, (rows, x.shape[1]))


def lookup(chunks, wanted, position):
    out = None
    for number, chunk in chunks:
        got = jnp.take_along_axis(row(chunk), position, axis=1, mode="promise_in_bounds")
        out = got if out is None else jnp.where(wanted == number, got, out)
    return out


def harmonics(ux, uy, uz):
    return [
        None,
        SQRT3 * ux,
        SQRT3 * uy,
        SQRT3 * uz,
        SQRT15 * ux * uy,
        SQRT15 * uy * uz,
        0.5 * SQRT5 * (2.0 * uz * uz - ux * ux - uy * uy),
        SQRT15 * ux * uz,
        0.5 * SQRT15 * (ux * ux - uy * uy),
    ]


def silu_parts(v):
    gate = 1.0 / (1.0 + jnp.exp(-v))
    return v * gate, gate * (1.0 + v * (1.0 - gate))


def choose_kernel(block_ref, *refs):
    sources = refs[:7]
    oh_ref, rrc_ref, r2c_ref, side_ref, rrr_ref, r2r_ref, mixa_ref, mixt_ref = refs[7:15]
    held = refs[15:22]
    sems = refs[22]
    emb_ref, rad1_ref, rad2_ref, mix1_ref, mix2_ref, read1_ref, read2_ref = held
    fetches = [pltpu.make_async_copy(src, dst, sems.at[i]) for i, (src, dst) in enumerate(zip(sources, held))]
    for fetch in fetches:
        fetch.start()
    chan = emb_ref.shape[1]
    bases = rad1_ref.shape[0]
    atoms = block_ref.shape[1]
    slots = block_ref.shape[0] - HEAD

    ids16 = lax.broadcasted_iota(jnp.int32, (LANES, atoms), 0).astype(jnp.int16)
    one16 = jnp.ones((LANES, atoms), bf16)
    zero16 = jnp.zeros((LANES, atoms), bf16)
    for k in range(slots):
        slot = block_ref[HEAD + k : HEAD + k + 1, :].astype(jnp.int32)
        wanted = jnp.broadcast_to(slot, (LANES, atoms)).astype(jnp.int16)
        for r in range(oh_ref.shape[0] // LANES):
            hit = wanted - jnp.int16(r * LANES) == ids16
            oh_ref[r * LANES : (r + 1) * LANES, k * atoms : (k + 1) * atoms] = jnp.where(hit, one16, zero16)

    for fetch in fetches:
        fetch.wait()
    emb0 = emb_ref[0:1, :]
    emb_d = emb_ref[1:2, :] - emb0
    rr = jnp.concatenate([rad1_ref[...] * emb0, rad1_ref[...] * emb_d], axis=0) * (1.0 / slots)
    rr_hi = rr.astype(bf16).astype(f32)
    rr_lo = rr - rr_hi
    r2 = rad2_ref[...] * (1.0 / slots)
    r2_hi = r2.astype(bf16).astype(f32)
    r2_lo = r2 - r2_hi
    zeros = jnp.zeros((8, chan), f32)
    turned1 = jnp.concatenate([rr_hi, rr_hi, rr_lo, rr_lo] + [zeros] * 8, axis=0).T
    sides = jnp.concatenate([emb0, emb_d, read1_ref[...], read2_ref[...], zeros[:4]], axis=0)
    turned2 = jnp.concatenate([r2_hi, r2_hi, r2_lo, r2_lo] + [zeros] * 12, axis=0).T
    rrc_ref[...] = turned1[:, : 8 * bases].astype(bf16)
    r2c_ref[...] = turned2[:, : 4 * bases].astype(bf16)
    side_ref[...] = jnp.concatenate([sides] + [zeros] * 15, axis=0).T
    rrr_ref[...] = jnp.concatenate(
        [jnp.concatenate([rr_hi, rr_hi], axis=1), jnp.concatenate([rr_lo, jnp.zeros_like(rr_lo)], axis=1)], axis=0
    ).astype(bf16)
    r2r_ref[...] = jnp.concatenate(
        [jnp.concatenate([r2_hi, r2_hi], axis=1), jnp.concatenate([r2_lo, jnp.zeros_like(r2_lo)], axis=1)], axis=0
    ).astype(bf16)
    for i, ref in enumerate((mix1_ref, mix2_ref)):
        hi, lo = split(ref[...])
        mixa_ref[i, 0:chan, :] = hi
        mixa_ref[i, chan:, :] = lo
        for g in range(3):
            hi, lo = split(ref[:, g * chan : (g + 1) * chan].T)
            mixt_ref[i, g, 0:chan, :] = hi
            mixt_ref[i, g, chan:, :] = lo


def dot_parts(both, hi, lo):
    rows = both.shape[0] // 2
    first = dot(both, hi)
    return first[:rows] + first[rows:] + dot(both[:rows], lo)


def edge_kernel(plan, *refs):
    atoms, near, wide, before, after = plan
    n_wide = len(wide)
    blocks = refs[:n_wide]
    geo_ref, y_ref, yb_ref, ub_ref, bk_ref, bt_ref, gidx_ref, pick_ref, as_ref = refs[n_wide:]
    bases = bk_ref.shape[0]
    slots = gidx_ref.shape[0]
    tiles = atoms // LANES
    half = atoms // 2
    half_tiles = half // LANES
    order_col = lax.broadcasted_iota(jnp.int32, (bases, LANES), 0).astype(f32)
    tables = []
    for quantity in range(4):
        chunks = []
        for g in range(n_wide):
            for t in range(tiles):
                chunks.append((g * tiles + t, blocks[g][quantity : quantity + 1, t * LANES : (t + 1) * LANES]))
        tables.append(chunks)
    for q in range(len(near)):
        ghosts = []
        for t in range(half_tiles):
            ghosts.append(
                (t, blocks[before[q]][4:5, half + t * LANES : half + (t + 1) * LANES] + float(before[q] * atoms))
            )
        for t in range(half_tiles):
            ghosts.append(
                (
                    half_tiles + tiles + t,
                    blocks[after[q]][4:5, t * LANES : (t + 1) * LANES] + float(after[q] * atoms),
                )
            )
        if q == 0:
            ids16 = lax.broadcasted_iota(jnp.int32, (pick_ref.shape[0], LANES), 0).astype(jnp.int16)
            one16 = jnp.ones(ids16.shape, bf16)
            zero16 = jnp.zeros(ids16.shape, bf16)
            for t, (_, chunk) in enumerate(ghosts):
                wanted = jnp.broadcast_to(chunk.astype(jnp.int32), ids16.shape).astype(jnp.int16)
                pick_ref[:, t * LANES : (t + 1) * LANES] = jnp.where(wanted == ids16, one16, zero16)
        for t in range(tiles):
            cols = slice(t * LANES, (t + 1) * LANES)
            here = slice(q * atoms + t * LANES, q * atoms + (t + 1) * LANES)
            slot = blocks[q][HEAD : HEAD + slots, cols].astype(jnp.int32)
            chunk_no = slot >> 7
            far = lookup(ghosts, chunk_no, slot & 127).astype(jnp.int32)
            own = (slot >= half) & (slot < half + atoms)
            gidx = jnp.where(own, slot + (q * atoms - half), far)
            gidx_ref[:, here] = gidx
            chunk_no = gidx >> 7
            place = gidx & 127
            xj, yj, zj, fj = [lookup(tables[i], chunk_no, place) for i in range(4)]
            rx = xj - row(blocks[q][0:1, cols])
            ry = yj - row(blocks[q][1:2, cols])
            rz = zj - row(blocks[q][2:3, cols])
            soft = jnp.sqrt(rx * rx + ry * ry + rz * rz + 1.0)
            back = 1.0 / soft
            ux, uy, uz = rx * back, ry * back, rz * back
            for i, value in enumerate((ux, uy, uz, back, soft, fj)):
                geo_ref[i, :, here] = value
            if q == 0:
                for i, value in enumerate((ux, uy, uz)):
                    for k in range(slots):
                        ub_ref[i, k, :, cols] = row(value[k : k + 1, :])
            sphere = harmonics(ux, uy, uz)
            for l in range(1, ORDERS):
                y_ref[l - 1, :, here] = sphere[l]
                if q == 0:
                    for k in range(slots):
                        yb_ref[l - 1, k, :, cols] = row(sphere[l][k : k + 1, :])
            for n in range(bases):
                bk_ref[n, :, here] = jnp.exp(-0.5 * (soft - (1.0 + n)) ** 2)
            for k in range(slots):
                basis = jnp.exp(-0.5 * (row(soft[k : k + 1, :], bases) - (1.0 + order_col)) ** 2)
                bt_ref[k, 0:bases, here] = basis
                bt_ref[k, bases : 2 * bases, here] = basis * row(fj[k : k + 1, :], bases)
            low = [None] * ORDERS
            for k in range(slots):
                basis = bt_ref[k, :, here]
                for l in range(ORDERS):
                    term = basis if l == 0 else basis * row(y_ref[l - 1, k : k + 1, here], 2 * bases)
                    low[l] = term if low[l] is None else low[l] + term
            for l in range(ORDERS):
                both = split_rows(low[l]).astype(bf16)
                as_ref[l, 0 : 4 * bases, here] = both
                as_ref[l, 4 * bases : 8 * bases, here] = both


def first_kernel(plan, *refs):
    atoms, near, wide, _, _ = plan
    n_wide = len(wide)
    blocks = refs[:n_wide]
    as_ref, rrc_ref, side_ref, mixa_ref, m1_ref, sp1_ref, hid_ref, hs_ref, flag_ref = refs[n_wide:]
    chan = m1_ref.shape[1]
    n_near = m1_ref.shape[2]

    for q in range(len(near)):
        flag_ref[0:1, q * atoms : (q + 1) * atoms] = blocks[q][3:4, :]
    wide_cols = 2 * LANES
    emb0_col = side_ref[:, 0:1]
    embd_col = side_ref[:, 1:2]

    def first(j):
        here = pl.ds(pl.multiple_of(j * wide_cols, wide_cols), wide_cols)
        inv = [None, None, None]
        for l in range(ORDERS):
            m = dot(rrc_ref[...], as_ref[l, :, here])
            m1_ref[l, :, here] = m
            inv[GROUP[l]] = m * m if inv[GROUP[l]] is None else inv[GROUP[l]] + m * m
        hi, lo = split(jnp.concatenate(inv, axis=0))
        value = dot_parts(mixa_ref[0], hi, lo)
        act, slope = silu_parts(value)
        sp1_ref[:, here] = slope
        hidden = act + emb0_col + embd_col * flag_ref[0:1, here]
        hid_ref[:, here] = hidden
        hi, lo = split(hidden)
        hs_ref[0:chan, here] = hi
        hs_ref[chan : 2 * chan, here] = lo

    in_turns(0, n_near // wide_cols, first)


def gather_kernel(hid_ref, hs_ref, oh_ref, pick_ref, gidx_ref, bt_ref, r2c_ref, hj_ref, w_ref, car_ref, ext_ref):
    slots = bt_ref.shape[0]
    bases = bt_ref.shape[1] // 2
    chan, n_near = hid_ref.shape
    atoms = hj_ref.shape[1] // slots
    half = atoms // 2
    by_lane = 2 * LANES if atoms > 2 * LANES else 0
    by_product = 2 * atoms - by_lane
    ghosts = dot(hs_ref[...], pick_ref[...]).astype(bf16)
    ext_ref[:, 0:half] = ghosts[:, :half]
    ext_ref[:, half : half + atoms] = hs_ref[:, 0:atoms]
    ext_ref[:, half + atoms :] = ghosts[:, half:]
    for k in range(slots):
        here = slice(k * atoms, (k + 1) * atoms)
        basis = split_rows(bt_ref[k, 0:bases, 0:atoms])
        w_ref[:, here] = dot(r2c_ref[...], jnp.concatenate([basis, basis], axis=0).astype(bf16))

    for pair in range(slots // 2):
        first = pair * 2 * atoms
        here = slice(first, first + by_product)
        both = dot(ext_ref[...], oh_ref[:, here])
        wanted = gidx_ref[2 * pair + 1 : 2 * pair + 2, 0:atoms]
        for t in range(by_lane // LANES):
            at = slice(first + by_product + t * LANES, first + by_product + (t + 1) * LANES)
            start = atoms - by_lane + t * LANES
            mine = row(wanted[:, start : start + LANES])
            chunk_no = mine >> 7
            place = mine & 127
            for c in range(chan // 8):
                rows = slice(8 * c, 8 * c + 8)
                feat = None
                for chunk in range(n_near // LANES):
                    held = hid_ref[rows, chunk * LANES : (chunk + 1) * LANES]
                    got = jnp.take_along_axis(held, place, axis=1, mode="promise_in_bounds")
                    feat = got if feat is None else jnp.where(chunk_no == chunk, got, feat)
                hj_ref[rows, at] = feat
                car_ref[rows, at] = feat * w_ref[rows, at]
        feat = both[:chan] + both[chan:]
        hj_ref[:, here] = feat
        car_ref[:, here] = feat * w_ref[:, here]


def moment_kernel(car_ref, yb_ref, mixa_ref, mixt_ref, side_ref, m2_ref, dinv_ref, inv_ref):
    slots = yb_ref.shape[1]
    chan, atoms = m2_ref.shape[1:]
    tiles = atoms // LANES
    wide_cols = 2 * LANES
    rows = 32
    groups = chan // rows

    def moments(step):
        t = step // groups
        c = step % groups
        cols = pl.ds(pl.multiple_of(t * LANES, LANES), LANES)
        base = pl.multiple_of(c * rows, rows)
        acc = [[None] * ORDERS for _ in range(rows // 8)]
        for k in range(slots):
            at = pl.ds(pl.multiple_of(k * atoms + t * LANES, LANES), LANES)
            got = car_ref[pl.ds(base, rows), at]
            for l in range(ORDERS):
                yb = yb_ref[l - 1, k, :, cols] if l else None
                for h in range(rows // 8):
                    part = got[8 * h : 8 * h + 8]
                    term = part * yb if l else part
                    acc[h][l] = term if acc[h][l] is None else acc[h][l] + term
        for h in range(rows // 8):
            inv = [None] * 3
            for l in range(ORDERS):
                m2_ref[l, pl.ds(pl.multiple_of(base + 8 * h, 8), 8), cols] = acc[h][l]
                sq = acc[h][l] * acc[h][l]
                g = GROUP[l]
                inv[g] = sq if inv[g] is None else inv[g] + sq
            for g in range(3):
                inv_ref[pl.ds(pl.multiple_of(g * chan + base + 8 * h, 8), 8), cols] = inv[g]

    in_turns(0, tiles * groups, moments, 4)
    read2_col = side_ref[:, 3:4]
    for t in range(atoms // wide_cols):
        cols = slice(t * wide_cols, (t + 1) * wide_cols)
        hi, lo = split(inv_ref[:, cols])
        _, slope = silu_parts(dot_parts(mixa_ref[1], hi, lo))
        hi, lo = split(slope * (2.0 * read2_col))
        for g, scale in enumerate((1.0, 0.5 * SQRT3, 0.5 * SQRT15)):
            dinv_ref[g * chan : (g + 1) * chan, cols] = scale * dot_parts(mixt_ref[1, g], hi, lo)


def back_second_kernel(m2_ref, dinv_ref, car_ref, hj_ref, w_ref, ub_ref, dhe_ref, dw_ref, p_ref):
    slots = ub_ref.shape[1]
    chan, atoms = m2_ref.shape[1:]
    tiles = atoms // LANES
    pairs = chan // 16
    per_turn = 4 if pairs % 4 == 0 else 1

    def back_moments(t, carry):
        cols = pl.ds(pl.multiple_of(t * LANES, LANES), LANES)

        def one(c, acc):
            forms = []
            for h in range(2):
                rows = pl.ds(pl.multiple_of(c * 16 + 8 * h, 8), 8)
                scale = [dinv_ref[pl.ds(pl.multiple_of(g * chan + c * 16 + 8 * h, 8), 8), cols] for g in range(3)]
                dm = [m2_ref[l, rows, cols] * scale[GROUP[l]] for l in range(ORDERS)]
                low = dm[6] * (1.0 / SQRT3)
                forms.append((dm[0], dm[1], dm[2], dm[3], dm[8] - low, -dm[8] - low, low + low, dm[4], dm[5], dm[7]))
            base = pl.multiple_of(c * 16, 16)
            for k in range(slots):
                at = pl.ds(pl.multiple_of(k * atoms + t * LANES, LANES), LANES)
                got = car_ref[pl.ds(base, 16), at]
                ux, uy, uz = [ub_ref[i, k, :, cols] for i in range(3)]
                out = []
                for h in range(2):
                    mid, dx, dy, dz, qxx, qyy, qzz, qxy, qyz, qxz = forms[h]
                    gx = dx + qxx * ux + qxy * uy + qxz * uz
                    gy = dy + qxy * ux + qyy * uy + qyz * uz
                    gz = dz + qxz * ux + qyz * uy + qzz * uz
                    out.append(mid + (gx + dx) * ux + (gy + dy) * uy + (gz + dz) * uz)
                    part = got[8 * h : 8 * h + 8]
                    for i, g in enumerate((gx, gy, gz)):
                        acc[3 * k + i] = acc[3 * k + i] + part * g
                dcar = jnp.concatenate(out, axis=0)
                for ref, other in ((dhe_ref, w_ref), (dw_ref, hj_ref)):
                    hi, lo = split(dcar * other[pl.ds(base, 16), at])
                    ref[pl.ds(base, 16), at] = hi
                    ref[pl.ds(pl.multiple_of(chan + c * 16, 16), 16), at] = lo

        def over(c, acc):
            acc = list(acc)
            for i in range(per_turn):
                one(per_turn * c + i, acc)
            return tuple(acc)

        start = tuple(jnp.zeros((8, LANES), f32) for _ in range(3 * slots))
        acc = lax.fori_loop(0, pairs // per_turn, over, start)
        for k in range(slots):
            for i in range(3):
                p_ref[i, 8 * k : 8 * k + 8, cols] = acc[3 * k + i]
        return carry

    lax.fori_loop(0, tiles, back_moments, 0)


def scatter_kernel(oh_ref, pick_ref, dhe_ref, side_ref, dw_ref, p_ref, bt_ref, geo_ref, r2r_ref, gidx_ref,
                   dh_ref, q_ref, ohlo_ref, ds_ref):
    chan, n_near = dh_ref.shape
    slots = bt_ref.shape[0]
    bases = bt_ref.shape[1] // 2
    atoms = pick_ref.shape[1]
    half = atoms // 2
    both = dot_nt(dhe_ref[...], jnp.concatenate([oh_ref[:half], oh_ref[half + atoms :]], axis=0))
    hi, lo = split(both[:chan] + both[chan:])
    spread = dot_nt(jnp.concatenate([hi, lo], axis=0), pick_ref[...])
    spread = spread[:chan] + spread[chan:]
    both = dot_nt(dhe_ref[...], oh_ref[half : half + atoms])
    dh_ref[:, 0:atoms] = spread[:, :atoms] + both[:chan] + both[chan:] + side_ref[:, 2:3]
    if n_near > atoms:
        dh_ref[:, atoms:] = spread[:, atoms:]
    ids16 = lax.broadcasted_iota(jnp.int32, (LANES, n_near), 0).astype(jnp.int16)
    one16 = jnp.ones((LANES, n_near), bf16)
    zero16 = jnp.zeros((LANES, n_near), bf16)
    for k in range(slots):
        place = jnp.broadcast_to(gidx_ref[k : k + 1, :] & 127, (LANES, n_near)).astype(jnp.int16)
        ohlo_ref[:, k * n_near : (k + 1) * n_near] = jnp.where(place == ids16, one16, zero16)
    for k in range(slots):
        here = slice(k * atoms, (k + 1) * atoms)
        small = dot(r2r_ref[...], dw_ref[:, here])
        dbasis = small[:bases] + small[bases:]
        basis = bt_ref[k, 0:bases, 0:atoms]
        reach = 1.0 + lax.broadcasted_iota(jnp.int32, (bases, atoms), 0).astype(f32)
        ds_ref[k * 8 : k * 8 + 8, :] = dbasis * basis * (reach - row(geo_ref[4, k : k + 1, 0:atoms], bases))
    lane = lax.broadcasted_iota(jnp.int32, (slots, 16 * slots), 1)
    sub = lax.broadcasted_iota(jnp.int32, (slots, 16 * slots), 0)
    adder = jnp.where(((lane >> 3) & (slots - 1)) == sub, 1.0, 0.0).astype(bf16)
    for i in range(4):
        total = dot(adder, split_rows(p_ref[i - 1, :, :] if i else ds_ref[...]).astype(bf16))
        q_ref[8 * i : 8 * i + 8, :] = 2.0 * total if i else total


def back_first_kernel(dh_ref, sp1_ref, m1_ref, mixt_ref, rrr_ref, da_ref):
    n_near = sp1_ref.shape[1]
    rows = rrr_ref.shape[0] // 2
    wide_cols = 2 * LANES

    def back_first(j):
        here = pl.ds(pl.multiple_of(j * wide_cols, wide_cols), wide_cols)
        hi, lo = split(dh_ref[:, here] * sp1_ref[:, here] * 2.0)
        scale = [dot_parts(mixt_ref[0, g], hi, lo) for g in range(3)]
        for l in range(ORDERS):
            hi, lo = split(m1_ref[l, :, here] * scale[GROUP[l]])
            out = dot(rrr_ref[...], jnp.concatenate([hi, lo], axis=0))
            da_ref[l, :, here] = out[:rows] + out[rows:]

    in_turns(0, n_near // wide_cols, back_first)


def back_edge_kernel(plan, *refs):
    atoms, near, wide, _, _ = plan
    n_wide = len(wide)
    blocks = refs[:n_wide]
    moment_src, geo_ref, y_ref, bk_ref, gidx_ref, da_ref, q_ref, ohlo_ref = refs[n_wide : n_wide + 8]
    push_ref, mass_ref, val_ref, dr_ref, moment_ref, sem = refs[n_wide + 8 :]
    fetch = pltpu.make_async_copy(moment_src, moment_ref, sem)
    fetch.start()
    bases, slots, n_near = bk_ref.shape
    tiles = atoms // LANES
    top_rows = val_ref.shape[0] // 6

    def back_geometry(t, mine):
        here = pl.ds(pl.multiple_of(t * LANES, LANES), LANES)
        ux, uy, uz, back, soft, fj = [geo_ref[i, :, here] for i in range(6)]
        dy = [None] * ORDERS
        ds = None
        for n in range(bases):
            basis = bk_ref[n, :, here]
            db = None
            for l in range(ORDERS):
                g = row(da_ref[l, n : n + 1, here]) + fj * row(da_ref[l, bases + n : bases + n + 1, here])
                if l:
                    dy[l] = g * basis if dy[l] is None else dy[l] + g * basis
                    db = db + g * y_ref[l - 1, :, here]
                else:
                    db = g
            db = db * basis * ((1.0 + n) - soft)
            ds = db if ds is None else ds + db
        if mine:
            ds = ds + q_ref[0:8, here]
        dux = SQRT3 * dy[1] + SQRT15 * (uy * dy[4] + uz * dy[7] + ux * dy[8]) - SQRT5 * ux * dy[6]
        duy = SQRT3 * dy[2] + SQRT15 * (ux * dy[4] + uz * dy[5] - uy * dy[8]) - SQRT5 * uy * dy[6]
        duz = SQRT3 * dy[3] + SQRT15 * (uy * dy[5] + ux * dy[7]) + 2.0 * SQRT5 * uz * dy[6]
        if mine:
            dux, duy, duz = [d + q_ref[8 * i : 8 * i + 8, here] for i, d in ((1, dux), (2, duy), (3, duz))]
        along = ds - (ux * dux + uy * duy + uz * duz) * back
        for i, value in enumerate((dux * back + along * ux, duy * back + along * uy, duz * back + along * uz)):
            dr_ref[i, :, here] = value

    in_turns(0, tiles, lambda t: back_geometry(t, True))
    in_turns(tiles, n_near // LANES, lambda t: back_geometry(t, False))

    def place_tile(t):
        here = pl.ds(pl.multiple_of(t * LANES, LANES), LANES)
        gidx = gidx_ref[:, here]
        chunk_no = gidx >> 7
        parts = []
        for i in range(3):
            value = dr_ref[i, :, here]
            hi = value.astype(bf16).astype(f32)
            parts.append((hi, value - hi))
        chunk_ids = lax.broadcasted_iota(jnp.int32, (top_rows, LANES), 0)
        for k in range(slots):
            at = pl.ds(pl.multiple_of(k * n_near + t * LANES, LANES), LANES)
            hit = chunk_ids == row(chunk_no[k : k + 1, :], top_rows)
            for i in range(3):
                both = [jnp.where(hit, row(part[k : k + 1, :], top_rows), 0.0) for part in parts[i]]
                val_ref[2 * i * top_rows : 2 * (i + 1) * top_rows, at] = jnp.concatenate(both, axis=0).astype(bf16)

    in_turns(0, n_near // LANES, place_tile)
    landed = dot_nt(val_ref[...], ohlo_ref[...])
    fetch.wait()
    lines = push_ref.shape[0] // (n_wide + 1)
    for i in range(3):
        total = (
            landed[2 * i * top_rows : (2 * i + 1) * top_rows] + landed[(2 * i + 1) * top_rows : (2 * i + 2) * top_rows]
        )
        for g in range(n_wide):
            for t in range(tiles):
                cols = slice(t * LANES, (t + 1) * LANES)
                line = total[g * tiles + t : g * tiles + t + 1, :]
                if g < len(near):
                    here = slice(g * atoms + t * LANES, g * atoms + (t + 1) * LANES)
                    line = line - jnp.sum(dr_ref[i, :, here], axis=0, keepdims=True)
                line = -HALF_STEP * line
                at = i * tiles + t
                if g == 0:
                    line = line + moment_ref[i, :, cols]
                    push_ref[at : at + 1, :] = blocks[0][i : i + 1, cols]
                push_ref[(1 + g) * lines + at : (1 + g) * lines + at + 1, :] = line
                mass = HEAVY - (HEAVY - 1.0) * blocks[g][3:4, cols]
                mass_ref[g * lines + at : g * lines + at + 1, :] = mass
    if lines > 3 * tiles:
        for g in range(n_wide + 1):
            blank = slice(g * lines + 3 * tiles, (g + 1) * lines)
            push_ref[blank, :] = jnp.zeros((lines - 3 * tiles, LANES), f32)
            if g < n_wide:
                mass_ref[blank, :] = jnp.ones((lines - 3 * tiles, LANES), f32)


def in_hbm(x):
    return pltpu.with_memory_space_constraint(x, pltpu.HBM)


def run(name, body, operands, results, scratch=(), far=(), cost=None):
    sizes = [math.prod(x.shape) * x.dtype.itemsize // 2 for i, x in enumerate(operands) if i not in far]
    sizes += [math.prod(shape) * jnp.dtype(dtype).itemsize for shape, dtype in results]
    sizes += [math.prod(x.shape) * x.dtype.itemsize for x in scratch if x.memory_space == pltpu.VMEM]
    limit = sum(sizes) + 4 * MIB
    specs = [pl.BlockSpec(memory_space=pltpu.HBM if i in far else pltpu.VMEM) for i in range(len(operands))]
    return pl.pallas_call(
        body,
        out_shape=tuple(jax.ShapeDtypeStruct(shape, dtype) for shape, dtype in results),
        in_specs=specs,
        out_specs=tuple(pl.BlockSpec(memory_space=pltpu.VMEM) for _ in results),
        scratch_shapes=list(scratch),
        compiler_params=pltpu.CompilerParams(vmem_limit_bytes=limit),
        cost_estimate=cost,
        name=name,
    )(*[in_hbm(x) if i in far else x for i, x in enumerate(operands)])


def choose(block, embedding, radial_one, radial_two, mix_one, mix_two, read_one, read_two):
    atoms = block.shape[1]
    slots = block.shape[0] - HEAD
    chan = embedding.shape[1]
    bases = radial_one.shape[0]
    weights = (embedding, radial_one, radial_two, mix_one, mix_two, read_one[None], read_two[None])
    return run(
        "choose",
        choose_kernel,
        (block, *weights),
        (
            ((2 * atoms, slots * atoms), bf16),
            ((chan, 8 * bases), bf16),
            ((chan, 4 * bases), bf16),
            ((chan, LANES), f32),
            ((4 * bases, 2 * chan), bf16),
            ((2 * bases, 2 * chan), bf16),
            ((2, 2 * chan, 3 * chan), bf16),
            ((2, 3, 2 * chan, chan), bf16),
        ),
        [pltpu.VMEM(w.shape, f32) for w in weights] + [pltpu.SemaphoreType.DMA((len(weights),))],
        range(1, 1 + len(weights)),
        cost=pl.CostEstimate(flops=2 * 10**9, bytes_accessed=2 * 10**6, transcendentals=0),
    )


def pushes(plan, blocks, momenta, chosen):
    atoms, near, wide, _, _ = plan
    oh, rrc, r2c, sides, rrr, r2r, mixa, mixt = chosen
    chan = rrc.shape[0]
    bases = r2r.shape[0] // 2
    slots = blocks[0].shape[0] - HEAD
    n_near = len(near) * atoms
    edges = slots * atoms
    top_rows = -(-len(wide) * atoms // LANES // 8) * 8
    lines = line_count(atoms)
    geo, y, yb, ub, bk, bt, gidx, pick, as1 = run(
        "edges",
        functools.partial(edge_kernel, plan),
        blocks,
        (
            ((6, slots, n_near), f32),
            ((ORDERS - 1, slots, n_near), f32),
            ((ORDERS - 1, slots, 8, atoms), f32),
            ((3, slots, 8, atoms), f32),
            ((bases, slots, n_near), f32),
            ((slots, 2 * bases, n_near), f32),
            ((slots, n_near), jnp.int32),
            ((n_near, atoms), bf16),
            ((ORDERS, 8 * bases, n_near), bf16),
        ),
    )
    m1, sp1, hid, hs = run(
        "first",
        functools.partial(first_kernel, plan),
        (*blocks, as1, rrc, sides, mixa),
        (((ORDERS, chan, n_near), f32), ((chan, n_near), f32), ((chan, n_near), f32), ((2 * chan, n_near), bf16)),
        [pltpu.VMEM((8, n_near), f32)],
    )
    hj, w, car = run(
        "gather",
        gather_kernel,
        (hid, hs, oh, pick, gidx, bt, r2c),
        (((chan, edges), f32),) * 3,
        [pltpu.VMEM((2 * chan, 2 * atoms), bf16)],
    )
    m2, dinv = run(
        "moments",
        moment_kernel,
        (car, yb, mixa, mixt, sides),
        (((ORDERS, chan, atoms), f32), ((3 * chan, atoms), f32)),
        [pltpu.VMEM((3 * chan, atoms), f32)],
    )
    dhe, dw, p = run(
        "back_second",
        back_second_kernel,
        (m2, dinv, car, hj, w, ub),
        (((2 * chan, edges), bf16), ((2 * chan, edges), bf16), ((3, 8 * slots, atoms), f32)),
    )
    dh, q, ohlo = run(
        "scatter",
        scatter_kernel,
        (oh, pick, dhe, sides, dw, p, bt, geo, r2r, gidx),
        (((chan, n_near), f32), ((4 * slots, atoms), f32), ((LANES, slots * n_near), bf16)),
        [pltpu.VMEM((8 * slots, atoms), f32)],
    )
    (da,) = run("back_first", back_first_kernel, (dh, sp1, m1, mixt, rrr), (((ORDERS, 2 * bases, n_near), f32),))
    return run(
        "back_edges",
        functools.partial(back_edge_kernel, plan),
        (*blocks, momenta, geo, y, bk, gidx, da, q, ohlo),
        ((((len(wide) + 1) * lines, LANES), f32), ((len(wide) * lines, LANES), f32)),
        [
            pltpu.VMEM((6 * top_rows, slots * n_near), bf16),
            pltpu.VMEM((3, slots, n_near), f32),
            pltpu.VMEM(momenta.shape, f32),
            pltpu.SemaphoreType.DMA(()),
        ],
        (len(blocks),),
    )


def line_count(atoms):
    return -(-3 * (atoms // LANES) // 8) * 8


def ring_plan(domains, atoms):
    near = list(dict.fromkeys(o % domains for o in (0, 1, -1)))
    wide = list(dict.fromkeys(near + [o % domains for o in (2, -2)]))
    before = tuple(wide.index((o - 1) % domains) for o in near)
    after = tuple(wide.index((o + 1) % domains) for o in near)
    return atoms, tuple(near), tuple(wide), before, after


def mode_turns(bead_total):
    bead = np.arange(bead_total, dtype=np.float64)[:, None]
    mode = np.arange(bead_total, dtype=np.float64)[None, :]
    phase = 2.0 * np.pi * bead * mode / bead_total
    half_total = bead_total // 2
    table = math.sqrt(2.0 / bead_total) * np.where(mode < half_total, np.cos(phase), np.sin(phase))
    table = np.where(mode == half_total, np.cos(np.pi * bead) / math.sqrt(bead_total), table)
    table = np.where(mode == 0, 1.0 / math.sqrt(bead_total), table)
    angles = bead_total * np.sin(np.pi * mode[0] / bead_total)
    safe = np.where(mode[0] == 0, 1.0, angles)
    reach = np.where(mode[0] == 0, STEP, STEP * np.sin(angles) / safe)
    stiff = angles * np.sin(angles) / STEP
    return [[float(x) for x in (table * factor[None, :]) @ table[0]] for factor in (np.cos(angles), reach, stiff)]


def pack_kernel(coord_src, species_src, send_src, slot_src, block_ref, coord_ref, species_ref, send_ref, slot_ref, sems):
    pairs = ((coord_src, coord_ref), (species_src, species_ref), (send_src, send_ref), (slot_src, slot_ref))
    fetches = [pltpu.make_async_copy(src, dst, sems.at[i]) for i, (src, dst) in enumerate(pairs)]
    for fetch in fetches:
        fetch.start()
    for fetch in fetches:
        fetch.wait()
    atoms = block_ref.shape[1]
    for i in range(3):
        block_ref[i : i + 1, :] = coord_ref[i]
    block_ref[3:4, :] = species_ref[...].astype(f32)
    block_ref[4:5, :] = send_ref[...].astype(f32)
    block_ref[5:HEAD, :] = jnp.zeros((HEAD - 5, atoms), f32)
    block_ref[HEAD:, :] = slot_ref[...].astype(f32)


def turn_kernel(shape, bead_ref, domain_ref, mass_ref, *refs):
    outer, inner, domains, wide = shape
    message_ref = refs[outer]
    turns = mode_turns(outer * inner)
    lines = mass_ref.shape[0] // len(wide)
    my_domain = domain_ref[0]
    my_inner = lax.rem(bead_ref[0], inner)
    if domains > len(wide):
        message_ref[...] = jnp.zeros_like(message_ref)
    masses = [mass_ref[g * lines : (g + 1) * lines, :] for g in range(len(wide))]
    sources = []
    for z in range(outer):
        sources.append([refs[z][g * lines : (g + 1) * lines, :] for g in range(len(wide) + 1)])
    for s in range(inner):
        wraps = jnp.full((lines, LANES), my_inner + s) >= inner
        weights = []
        for turn in turns:
            row_of = []
            for z in range(outer):
                there = turn[(z * inner + s) % (outer * inner)]
                round_it = turn[(z * inner + s - inner) % (outer * inner)]
                row_of.append(jnp.where(wraps, jnp.full((lines, LANES), round_it), jnp.full((lines, LANES), there)))
            weights.append(row_of)
        to_inner = lax.rem(my_inner + s, inner)
        for g in range(len(wide)):
            turned = sum(weights[0][z] * sources[z][1 + g] for z in range(outer))
            drift = sum(weights[1][z] * sources[z][1 + g] for z in range(outer))
            new_q = drift / masses[g]
            new_p = turned
            if g == 0:
                new_q = new_q + sum(weights[0][z] * sources[z][0] for z in range(outer))
                new_p = new_p - masses[g] * sum(weights[2][z] * sources[z][0] for z in range(outer))
            to = to_inner * domains + lax.rem(my_domain + wide[g], domains)
            message_ref[to, 0:lines, :] = new_q
            message_ref[to, lines:, :] = new_p


def sum_kernel(arrived_ref, q_ref, p_ref):
    total = arrived_ref[0]
    for i in range(1, arrived_ref.shape[0]):
        total = total + arrived_ref[i]
    lines = total.shape[0] // 2
    tiles = q_ref.shape[2] // LANES
    for i in range(3):
        for t in range(tiles):
            at = i * tiles + t
            q_ref[i, :, t * LANES : (t + 1) * LANES] = total[at : at + 1]
            p_ref[i, :, t * LANES : (t + 1) * LANES] = total[lines + at : lines + at + 1]


def shards(
    positions, momenta, species, neighbours, send_list, embedding, radial_one, radial_two, mix_one, mix_two,
    read_one, read_two,
):
    slots, atoms = neighbours.shape
    domains = lax.axis_size("space")
    beads = lax.axis_size("bead")
    inner = next(d for d in range(1, beads + 1) if beads % d == 0 and d * d >= beads)
    outer = beads // inner
    plan = ring_plan(domains, atoms)
    wide = plan[2]
    vmem = pl.BlockSpec(memory_space=pltpu.VMEM)
    smem = pl.BlockSpec(memory_space=pltpu.SMEM)
    far = pl.BlockSpec(memory_space=pltpu.HBM)
    small = pltpu.CompilerParams(vmem_limit_bytes=4 * MIB)
    coord_rows = jnp.transpose(positions, (1, 0, 2))
    moment_rows = jnp.transpose(momenta, (1, 0, 2))
    block = pl.pallas_call(
        pack_kernel,
        out_shape=jax.ShapeDtypeStruct((HEAD + slots, atoms), f32),
        in_specs=[far] * 4,
        out_specs=vmem,
        scratch_shapes=[
            pltpu.VMEM(coord_rows.shape, f32),
            pltpu.VMEM((1, atoms), jnp.int32),
            pltpu.VMEM((1, atoms), jnp.int32),
            pltpu.VMEM((slots, atoms), jnp.int32),
            pltpu.SemaphoreType.DMA((4,)),
        ],
        compiler_params=small,
        name="pack",
    )(in_hbm(coord_rows), in_hbm(species[None]), in_hbm(send_list[None]), in_hbm(neighbours))
    blocks = [block]
    for offset in wide[1:]:
        blocks.append(lax.ppermute(block, "space", [(i, (i - offset) % domains) for i in range(domains)]))
    chosen = choose(block, embedding, radial_one, radial_two, mix_one, mix_two, read_one, read_two)
    pushed, masses = pushes(plan, blocks, moment_rows, chosen)
    sources = [pushed]
    for z in range(1, outer):
        sources.append(lax.ppermute(pushed, "bead", [(b, (b + z * inner) % beads) for b in range(beads)]))
    here = [lax.axis_index(axis).astype(jnp.int32).reshape(1) for axis in ("bead", "space")]
    lines = line_count(atoms)
    messages = pl.pallas_call(
        functools.partial(turn_kernel, (outer, inner, domains, wide)),
        out_shape=jax.ShapeDtypeStruct((inner * domains, 2 * lines, LANES), f32),
        in_specs=[smem, smem, vmem] + [vmem] * outer,
        out_specs=vmem,
        compiler_params=small,
        name="turn",
    )(*here, masses, *sources)
    rows = [[z * inner * domains + i for i in range(inner * domains)] for z in range(outer)]
    arrived = lax.all_to_all(messages, ("bead", "space"), 0, 0, axis_index_groups=rows, tiled=True)
    new_q, new_p = pl.pallas_call(
        sum_kernel,
        out_shape=(jax.ShapeDtypeStruct((3, 1, atoms), f32),) * 2,
        in_specs=[vmem],
        out_specs=(vmem, vmem),
        compiler_params=small,
        name="sum",
    )(arrived)
    return (jnp.transpose(new_q, (1, 0, 2)), jnp.transpose(new_p, (1, 0, 2)))


def solution(mesh):
    placed = (
        P("bead", None, "space"),
        P("bead", None, "space"),
        P("space"),
        P(None, "space"),
        P("space"),
        P(),
        P(),
        P(),
        P(),
        P(),
        P(),
        P(),
    )
    return jax.shard_map(
        shards,
        mesh=mesh,
        in_specs=placed,
        out_specs=(P("bead", None, "space"), P("bead", None, "space")),
        check_vma=False,
    )
```

```python
import functools
import math

import jax
import jax.numpy as jnp
import numpy as np
from jax import lax
from jax.experimental import pallas as pl
from jax.experimental.pallas import tpu as pltpu
from jax.sharding import PartitionSpec as P

STEP = 2.0
HALF_STEP = 1.0
HEAVY = 16.0
SQRT3 = math.sqrt(3.0)
SQRT5 = math.sqrt(5.0)
SQRT15 = math.sqrt(15.0)
LANES = 128
ORDERS = 9
GROUP = (0, 1, 1, 1, 2, 2, 2, 2, 2)
HEAD = 8
MIB = 1024 * 1024
f32 = jnp.float32
bf16 = jnp.bfloat16


def split(x):
    hi = x.astype(bf16)
    return hi, (x - hi.astype(f32)).astype(bf16)


def split_rows(x):
    hi = x.astype(bf16).astype(f32)
    return jnp.concatenate([hi, x - hi], axis=0)


def dot(a, b):
    return jnp.dot(a, b, preferred_element_type=f32)


def dot_nt(a, b):
    return lax.dot_general(a, b, (((1,), (1,)), ((), ())), preferred_element_type=f32)


def in_turns(start, stop, step, most=4):
    per_turn = next(n for n in range(most, 0, -1) if (stop - start) % n == 0)

    def turn(i, carry):
        for j in range(per_turn):
            step(start + i * per_turn + j)
        return carry

    lax.fori_loop(0, (stop - start) // per_turn, turn, 0)


def row(x, rows=8):
    return jnp.broadcast_to(x, (rows, x.shape[1]))


def lookup(chunks, wanted, position):
    out = None
    for number, chunk in chunks:
        got = jnp.take_along_axis(row(chunk), position, axis=1, mode="promise_in_bounds")
        out = got if out is None else jnp.where(wanted == number, got, out)
    return out


def harmonics(ux, uy, uz):
    return [
        None,
        SQRT3 * ux,
        SQRT3 * uy,
        SQRT3 * uz,
        SQRT15 * ux * uy,
        SQRT15 * uy * uz,
        0.5 * SQRT5 * (2.0 * uz * uz - ux * ux - uy * uy),
        SQRT15 * ux * uz,
        0.5 * SQRT15 * (ux * ux - uy * uy),
    ]


def silu_parts(v):
    gate = 1.0 / (1.0 + jnp.exp(-v))
    return v * gate, gate * (1.0 + v * (1.0 - gate))


def choose_kernel(block_ref, *refs):
    sources = refs[:7]
    oh_ref, rrc_ref, r2c_ref, side_ref, rrr_ref, mixa_ref, mixt_ref = refs[7:14]
    held = refs[14:21]
    sems = refs[21]
    emb_ref, rad1_ref, rad2_ref, mix1_ref, mix2_ref, read1_ref, read2_ref = held
    fetches = [pltpu.make_async_copy(src, dst, sems.at[i]) for i, (src, dst) in enumerate(zip(sources, held))]
    for fetch in fetches:
        fetch.start()
    chan = emb_ref.shape[1]
    bases = rad1_ref.shape[0]
    atoms = block_ref.shape[1]
    slots = block_ref.shape[0] - HEAD

    ids16 = lax.broadcasted_iota(jnp.int32, (LANES, atoms), 0).astype(jnp.int16)
    one16 = jnp.ones((LANES, atoms), bf16)
    zero16 = jnp.zeros((LANES, atoms), bf16)
    for k in range(slots):
        slot = block_ref[HEAD + k : HEAD + k + 1, :].astype(jnp.int32)
        wanted = jnp.broadcast_to(slot, (LANES, atoms)).astype(jnp.int16)
        for r in range(oh_ref.shape[0] // LANES):
            hit = wanted - jnp.int16(r * LANES) == ids16
            oh_ref[r * LANES : (r + 1) * LANES, k * atoms : (k + 1) * atoms] = jnp.where(hit, one16, zero16)

    for fetch in fetches:
        fetch.wait()
    emb0 = emb_ref[0:1, :]
    emb_d = emb_ref[1:2, :] - emb0
    rr = jnp.concatenate([rad1_ref[...] * emb0, rad1_ref[...] * emb_d], axis=0) * (1.0 / slots)
    rr_hi = rr.astype(bf16).astype(f32)
    rr_lo = rr - rr_hi
    r2 = rad2_ref[...] * (1.0 / slots)
    r2_hi = r2.astype(bf16).astype(f32)
    r2_lo = r2 - r2_hi
    zeros = jnp.zeros((8, chan), f32)
    turned1 = jnp.concatenate([rr_hi, rr_hi, rr_lo, rr_lo] + [zeros] * 8, axis=0).T
    sides = jnp.concatenate([emb0, emb_d, read1_ref[...], read2_ref[...], zeros[:4]], axis=0)
    turned2 = jnp.concatenate([r2_hi, r2_hi, r2_lo, r2_lo] + [zeros] * 12, axis=0).T
    rrc_ref[...] = turned1[:, : 8 * bases].astype(bf16)
    r2c_ref[...] = turned2[:, : 4 * bases].astype(bf16)
    side_ref[...] = jnp.concatenate([sides] + [zeros] * 15, axis=0).T
    rrr_ref[...] = jnp.concatenate(
        [jnp.concatenate([rr_hi, rr_hi], axis=1), jnp.concatenate([rr_lo, jnp.zeros_like(rr_lo)], axis=1)], axis=0
    ).astype(bf16)
    for i, ref in enumerate((mix1_ref, mix2_ref)):
        hi, lo = split(ref[...])
        mixa_ref[i, 0:chan, :] = hi
        mixa_ref[i, chan:, :] = lo
        for g in range(3):
            hi, lo = split(ref[:, g * chan : (g + 1) * chan].T)
            mixt_ref[i, g, 0:chan, :] = hi
            mixt_ref[i, g, chan:, :] = lo


def dot_parts(both, hi, lo):
    rows = both.shape[0] // 2
    first = dot(both, hi)
    return first[:rows] + first[rows:] + dot(both[:rows], lo)


def edge_kernel(plan, *refs):
    atoms, near, wide, before, after = plan
    n_wide = len(wide)
    blocks = refs[:n_wide]
    geo_ref, y_ref, yb_ref, ub_ref, bk_ref, bt_ref, gidx_ref, pick_ref, as_ref = refs[n_wide:]
    bases = bk_ref.shape[0]
    slots = gidx_ref.shape[0]
    tiles = atoms // LANES
    half = atoms // 2
    half_tiles = half // LANES
    order_col = lax.broadcasted_iota(jnp.int32, (bases, LANES), 0).astype(f32)
    tables = []
    for quantity in range(4):
        chunks = []
        for g in range(n_wide):
            for t in range(tiles):
                chunks.append((g * tiles + t, blocks[g][quantity : quantity + 1, t * LANES : (t + 1) * LANES]))
        tables.append(chunks)
    for q in range(len(near)):
        ghosts = []
        for t in range(half_tiles):
            ghosts.append(
                (t, blocks[before[q]][4:5, half + t * LANES : half + (t + 1) * LANES] + float(before[q] * atoms))
            )
        for t in range(half_tiles):
            ghosts.append(
                (
                    half_tiles + tiles + t,
                    blocks[after[q]][4:5, t * LANES : (t + 1) * LANES] + float(after[q] * atoms),
                )
            )
        if q == 0:
            ids16 = lax.broadcasted_iota(jnp.int32, (pick_ref.shape[0], LANES), 0).astype(jnp.int16)
            one16 = jnp.ones(ids16.shape, bf16)
            zero16 = jnp.zeros(ids16.shape, bf16)
            for t, (_, chunk) in enumerate(ghosts):
                wanted = jnp.broadcast_to(chunk.astype(jnp.int32), ids16.shape).astype(jnp.int16)
                pick_ref[:, t * LANES : (t + 1) * LANES] = jnp.where(wanted == ids16, one16, zero16)
        for t in range(tiles):
            cols = slice(t * LANES, (t + 1) * LANES)
            here = slice(q * atoms + t * LANES, q * atoms + (t + 1) * LANES)
            slot = blocks[q][HEAD : HEAD + slots, cols].astype(jnp.int32)
            chunk_no = slot >> 7
            far = lookup(ghosts, chunk_no, slot & 127).astype(jnp.int32)
            own = (slot >= half) & (slot < half + atoms)
            gidx = jnp.where(own, slot + (q * atoms - half), far)
            gidx_ref[:, here] = gidx
            chunk_no = gidx >> 7
            place = gidx & 127
            xj, yj, zj, fj = [lookup(tables[i], chunk_no, place) for i in range(4)]
            rx = xj - row(blocks[q][0:1, cols])
            ry = yj - row(blocks[q][1:2, cols])
            rz = zj - row(blocks[q][2:3, cols])
            soft = jnp.sqrt(rx * rx + ry * ry + rz * rz + 1.0)
            back = 1.0 / soft
            ux, uy, uz = rx * back, ry * back, rz * back
            for i, value in enumerate((ux, uy, uz, back, soft, fj)):
                geo_ref[i, :, here] = value
            if q == 0:
                for i, value in enumerate((ux, uy, uz)):
                    for k in range(slots):
                        ub_ref[i, k, :, cols] = row(value[k : k + 1, :])
            sphere = harmonics(ux, uy, uz)
            for l in range(1, ORDERS):
                y_ref[l - 1, :, here] = sphere[l]
                if q == 0:
                    for k in range(slots):
                        yb_ref[l - 1, k, :, cols] = row(sphere[l][k : k + 1, :])
            for n in range(bases):
                bk_ref[n, :, here] = jnp.exp(-0.5 * (soft - (1.0 + n)) ** 2)
            for k in range(slots):
                basis = jnp.exp(-0.5 * (row(soft[k : k + 1, :], bases) - (1.0 + order_col)) ** 2)
                bt_ref[k, 0:bases, here] = basis
                bt_ref[k, bases : 2 * bases, here] = basis * row(fj[k : k + 1, :], bases)
            low = [None] * ORDERS
            for k in range(slots):
                basis = bt_ref[k, :, here]
                for l in range(ORDERS):
                    term = basis if l == 0 else basis * row(y_ref[l - 1, k : k + 1, here], 2 * bases)
                    low[l] = term if low[l] is None else low[l] + term
            for l in range(ORDERS):
                both = split_rows(low[l]).astype(bf16)
                as_ref[l, 0 : 4 * bases, here] = both
                as_ref[l, 4 * bases : 8 * bases, here] = both


def first_kernel(plan, *refs):
    atoms, near, wide, _, _ = plan
    n_wide = len(wide)
    blocks = refs[:n_wide]
    as_ref, rrc_ref, side_ref, mixa_ref, m1_ref, sp1_ref, hid_ref, hs_ref, flag_ref = refs[n_wide:]
    chan = m1_ref.shape[1]
    n_near = m1_ref.shape[2]

    for q in range(len(near)):
        flag_ref[0:1, q * atoms : (q + 1) * atoms] = blocks[q][3:4, :]
    wide_cols = 2 * LANES
    emb0_col = side_ref[:, 0:1]
    embd_col = side_ref[:, 1:2]

    def first(j):
        here = pl.ds(pl.multiple_of(j * wide_cols, wide_cols), wide_cols)
        inv = [None, None, None]
        for l in range(ORDERS):
            m = dot(rrc_ref[...], as_ref[l, :, here])
            m1_ref[l, :, here] = m
            inv[GROUP[l]] = m * m if inv[GROUP[l]] is None else inv[GROUP[l]] + m * m
        hi, lo = split(jnp.concatenate(inv, axis=0))
        value = dot_parts(mixa_ref[0], hi, lo)
        act, slope = silu_parts(value)
        sp1_ref[:, here] = slope
        hidden = act + emb0_col + embd_col * flag_ref[0:1, here]
        hid_ref[:, here] = hidden
        hi, lo = split(hidden)
        hs_ref[0:chan, here] = hi
        hs_ref[chan : 2 * chan, here] = lo

    in_turns(0, n_near // wide_cols, first)


def gather_kernel(hid_ref, hs_ref, oh_ref, pick_ref, gidx_ref, bt_ref, geo_ref, r2c_ref,
                  hj_ref, w_ref, slope_ref, car_ref, ext_ref):
    slots = bt_ref.shape[0]
    bases = bt_ref.shape[1] // 2
    chan, n_near = hid_ref.shape
    atoms = hj_ref.shape[1] // slots
    half = atoms // 2
    ghosts = dot(hs_ref[...], pick_ref[...]).astype(bf16)
    ext_ref[:, 0:half] = ghosts[:, :half]
    ext_ref[:, half : half + atoms] = hs_ref[:, 0:atoms]
    ext_ref[:, half + atoms :] = ghosts[:, half:]
    reach = 1.0 + lax.broadcasted_iota(jnp.int32, (bases, atoms), 0).astype(f32)
    for k in range(slots):
        here = slice(k * atoms, (k + 1) * atoms)
        basis = bt_ref[k, 0:bases, 0:atoms]
        for ref, value in ((w_ref, basis), (slope_ref, basis * (reach - row(geo_ref[4, k : k + 1, 0:atoms], bases)))):
            both = split_rows(value)
            ref[:, here] = dot(r2c_ref[...], jnp.concatenate([both, both], axis=0).astype(bf16))

    for pair in range(slots // 2):
        by_lane = (2 + 2 * (pair % 2)) * LANES if atoms >= 4 * LANES else 0
        by_product = 2 * atoms - by_lane
        first = pair * 2 * atoms
        here = slice(first, first + by_product)
        both = dot(ext_ref[...], oh_ref[:, here])
        wanted = gidx_ref[2 * pair + 1 : 2 * pair + 2, 0:atoms]
        for t in range(by_lane // LANES):
            at = slice(first + by_product + t * LANES, first + by_product + (t + 1) * LANES)
            start = atoms - by_lane + t * LANES
            mine = row(wanted[:, start : start + LANES])
            chunk_no = mine >> 7
            place = mine & 127
            for c in range(chan // 8):
                rows = slice(8 * c, 8 * c + 8)
                feat = None
                for chunk in range(n_near // LANES):
                    held = hid_ref[rows, chunk * LANES : (chunk + 1) * LANES]
                    got = jnp.take_along_axis(held, place, axis=1, mode="promise_in_bounds")
                    feat = got if feat is None else jnp.where(chunk_no == chunk, got, feat)
                hj_ref[rows, at] = feat
                car_ref[rows, at] = feat * w_ref[rows, at]
        feat = both[:chan] + both[chan:]
        hj_ref[:, here] = feat
        car_ref[:, here] = feat * w_ref[:, here]


def moment_kernel(car_ref, yb_ref, mixa_ref, mixt_ref, side_ref, m2_ref, dinv_ref, inv_ref):
    slots = yb_ref.shape[1]
    chan, atoms = m2_ref.shape[1:]
    tiles = atoms // LANES
    wide_cols = 2 * LANES
    rows = 32
    groups = chan // rows

    def moments(step):
        t = step // groups
        c = step % groups
        cols = pl.ds(pl.multiple_of(t * LANES, LANES), LANES)
        base = pl.multiple_of(c * rows, rows)
        acc = [[None] * ORDERS for _ in range(rows // 8)]
        for k in range(slots):
            at = pl.ds(pl.multiple_of(k * atoms + t * LANES, LANES), LANES)
            got = car_ref[pl.ds(base, rows), at]
            for l in range(ORDERS):
                yb = yb_ref[l - 1, k, :, cols] if l else None
                for h in range(rows // 8):
                    part = got[8 * h : 8 * h + 8]
                    term = part * yb if l else part
                    acc[h][l] = term if acc[h][l] is None else acc[h][l] + term
        for h in range(rows // 8):
            inv = [None] * 3
            for l in range(ORDERS):
                m2_ref[l, pl.ds(pl.multiple_of(base + 8 * h, 8), 8), cols] = acc[h][l]
                sq = acc[h][l] * acc[h][l]
                g = GROUP[l]
                inv[g] = sq if inv[g] is None else inv[g] + sq
            for g in range(3):
                inv_ref[pl.ds(pl.multiple_of(g * chan + base + 8 * h, 8), 8), cols] = inv[g]

    in_turns(0, tiles * groups, moments, 2)
    read2_col = side_ref[:, 3:4]
    for t in range(atoms // wide_cols):
        cols = slice(t * wide_cols, (t + 1) * wide_cols)
        hi, lo = split(inv_ref[:, cols])
        _, slope = silu_parts(dot_parts(mixa_ref[1], hi, lo))
        hi, lo = split(slope * (2.0 * read2_col))
        for g, scale in enumerate((1.0, 0.5 * SQRT3, 0.5 * SQRT15)):
            dinv_ref[g * chan : (g + 1) * chan, cols] = scale * dot_parts(mixt_ref[1, g], hi, lo)


def back_second_kernel(m2_ref, dinv_ref, car_ref, hj_ref, w_ref, slope_ref, ub_ref, dhe_ref, p_ref):
    slots = ub_ref.shape[1]
    chan, atoms = m2_ref.shape[1:]
    tiles = atoms // LANES
    pairs = chan // 16
    per_turn = 4 if pairs % 4 == 0 else 1
    k_step = slots // 2

    def back_moments(t, carry):
        cols = pl.ds(pl.multiple_of(t * LANES, LANES), LANES)

        def one(c, acc, k0):
            forms = []
            for h in range(2):
                rows = pl.ds(pl.multiple_of(c * 16 + 8 * h, 8), 8)
                scale = [dinv_ref[pl.ds(pl.multiple_of(g * chan + c * 16 + 8 * h, 8), 8), cols] for g in range(3)]
                dm = [m2_ref[l, rows, cols] * scale[GROUP[l]] for l in range(ORDERS)]
                low = dm[6] * (1.0 / SQRT3)
                forms.append((dm[0], dm[1], dm[2], dm[3], dm[8] - low, -dm[8] - low, low + low, dm[4], dm[5], dm[7]))
            base = pl.multiple_of(c * 16, 16)
            for k in range(k0, k0 + k_step):
                at = pl.ds(pl.multiple_of(k * atoms + t * LANES, LANES), LANES)
                got = car_ref[pl.ds(base, 16), at]
                stretch = hj_ref[pl.ds(base, 16), at] * slope_ref[pl.ds(base, 16), at]
                ux, uy, uz = [ub_ref[i, k, :, cols] for i in range(3)]
                out = []
                for h in range(2):
                    mid, dx, dy, dz, qxx, qyy, qzz, qxy, qyz, qxz = forms[h]
                    gx = dx + qxx * ux + qxy * uy + qxz * uz
                    gy = dy + qxy * ux + qyy * uy + qyz * uz
                    gz = dz + qxz * ux + qyz * uy + qzz * uz
                    out.append(mid + (gx + dx) * ux + (gy + dy) * uy + (gz + dz) * uz)
                    part = got[8 * h : 8 * h + 8]
                    at_acc = 4 * (k - k0)
                    for i, g in enumerate((gx, gy, gz)):
                        acc[at_acc + i] = acc[at_acc + i] + part * g
                    acc[at_acc + 3] = acc[at_acc + 3] + out[h] * stretch[8 * h : 8 * h + 8]
                hi, lo = split(jnp.concatenate(out, axis=0) * w_ref[pl.ds(base, 16), at])
                dhe_ref[pl.ds(base, 16), at] = hi
                dhe_ref[pl.ds(pl.multiple_of(chan + c * 16, 16), 16), at] = lo

        for k0 in range(0, slots, k_step):

            def over(c, acc, k0=k0):
                acc = list(acc)
                for i in range(per_turn):
                    one(per_turn * c + i, acc, k0)
                return tuple(acc)

            start = tuple(jnp.zeros((8, LANES), f32) for _ in range(4 * k_step))
            acc = lax.fori_loop(0, pairs // per_turn, over, start)
            for k in range(k_step):
                for i in range(4):
                    p_ref[i, 8 * (k0 + k) : 8 * (k0 + k) + 8, cols] = acc[4 * k + i]
        return carry

    lax.fori_loop(0, tiles, back_moments, 0)


def scatter_kernel(oh_ref, pick_ref, dhe_ref, side_ref, p_ref, gidx_ref, dh_ref, q_ref, ohlo_ref):
    chan, n_near = dh_ref.shape
    slots = gidx_ref.shape[0]
    atoms = pick_ref.shape[1]
    half = atoms // 2
    both = dot_nt(dhe_ref[...], jnp.concatenate([oh_ref[:half], oh_ref[half + atoms :]], axis=0))
    hi, lo = split(both[:chan] + both[chan:])
    spread = dot_nt(jnp.concatenate([hi, lo], axis=0), pick_ref[...])
    spread = spread[:chan] + spread[chan:]
    both = dot_nt(dhe_ref[...], oh_ref[half : half + atoms])
    dh_ref[:, 0:atoms] = spread[:, :atoms] + both[:chan] + both[chan:] + side_ref[:, 2:3]
    if n_near > atoms:
        dh_ref[:, atoms:] = spread[:, atoms:]
    ids16 = lax.broadcasted_iota(jnp.int32, (LANES, n_near), 0).astype(jnp.int16)
    one16 = jnp.ones((LANES, n_near), bf16)
    zero16 = jnp.zeros((LANES, n_near), bf16)
    for k in range(slots):
        place = jnp.broadcast_to(gidx_ref[k : k + 1, :] & 127, (LANES, n_near)).astype(jnp.int16)
        ohlo_ref[:, k * n_near : (k + 1) * n_near] = jnp.where(place == ids16, one16, zero16)
    lane = lax.broadcasted_iota(jnp.int32, (slots, 16 * slots), 1)
    sub = lax.broadcasted_iota(jnp.int32, (slots, 16 * slots), 0)
    adder = jnp.where(((lane >> 3) & (slots - 1)) == sub, 1.0, 0.0).astype(bf16)
    for i in range(4):
        total = dot(adder, split_rows(p_ref[i]).astype(bf16))
        q_ref[8 * i : 8 * i + 8, :] = 2.0 * total if i < 3 else total


def back_first_kernel(dh_ref, sp1_ref, m1_ref, mixt_ref, rrr_ref, da_ref):
    n_near = sp1_ref.shape[1]
    rows = rrr_ref.shape[0] // 2
    wide_cols = 2 * LANES

    def back_first(j):
        here = pl.ds(pl.multiple_of(j * wide_cols, wide_cols), wide_cols)
        hi, lo = split(dh_ref[:, here] * sp1_ref[:, here] * 2.0)
        scale = [dot_parts(mixt_ref[0, g], hi, lo) for g in range(3)]
        for l in range(ORDERS):
            hi, lo = split(m1_ref[l, :, here] * scale[GROUP[l]])
            out = dot(rrr_ref[...], jnp.concatenate([hi, lo], axis=0))
            da_ref[l, :, here] = out[:rows] + out[rows:]

    in_turns(0, n_near // wide_cols, back_first)


def back_edge_kernel(plan, *refs):
    atoms, near, wide, _, _ = plan
    n_wide = len(wide)
    blocks = refs[:n_wide]
    moment_src, geo_ref, y_ref, bk_ref, gidx_ref, da_ref, q_ref, ohlo_ref = refs[n_wide : n_wide + 8]
    push_ref, mass_ref, val_ref, dr_ref, moment_ref, sem = refs[n_wide + 8 :]
    fetch = pltpu.make_async_copy(moment_src, moment_ref, sem)
    fetch.start()
    bases, slots, n_near = bk_ref.shape
    tiles = atoms // LANES
    top_rows = val_ref.shape[0] // 6

    def back_geometry(t, mine):
        here = pl.ds(pl.multiple_of(t * LANES, LANES), LANES)
        ux, uy, uz, back, soft, fj = [geo_ref[i, :, here] for i in range(6)]
        dy = [None] * ORDERS
        ds = None
        for n in range(bases):
            basis = bk_ref[n, :, here]
            db = None
            for l in range(ORDERS):
                g = row(da_ref[l, n : n + 1, here]) + fj * row(da_ref[l, bases + n : bases + n + 1, here])
                if l:
                    dy[l] = g * basis if dy[l] is None else dy[l] + g * basis
                    db = db + g * y_ref[l - 1, :, here]
                else:
                    db = g
            db = db * basis * ((1.0 + n) - soft)
            ds = db if ds is None else ds + db
        if mine:
            ds = ds + q_ref[24:32, here]
        dux = SQRT3 * dy[1] + SQRT15 * (uy * dy[4] + uz * dy[7] + ux * dy[8]) - SQRT5 * ux * dy[6]
        duy = SQRT3 * dy[2] + SQRT15 * (ux * dy[4] + uz * dy[5] - uy * dy[8]) - SQRT5 * uy * dy[6]
        duz = SQRT3 * dy[3] + SQRT15 * (uy * dy[5] + ux * dy[7]) + 2.0 * SQRT5 * uz * dy[6]
        if mine:
            dux, duy, duz = [d + q_ref[8 * i : 8 * i + 8, here] for i, d in enumerate((dux, duy, duz))]
        along = ds - (ux * dux + uy * duy + uz * duz) * back
        for i, value in enumerate((dux * back + along * ux, duy * back + along * uy, duz * back + along * uz)):
            dr_ref[i, :, here] = value

    in_turns(0, tiles, lambda t: back_geometry(t, True))
    in_turns(tiles, n_near // LANES, lambda t: back_geometry(t, False))

    def place_tile(t):
        here = pl.ds(pl.multiple_of(t * LANES, LANES), LANES)
        gidx = gidx_ref[:, here]
        chunk_no = gidx >> 7
        parts = []
        for i in range(3):
            value = dr_ref[i, :, here]
            hi = value.astype(bf16).astype(f32)
            parts.append((hi, value - hi))
        chunk_ids = lax.broadcasted_iota(jnp.int32, (top_rows, LANES), 0)
        for k in range(slots):
            at = pl.ds(pl.multiple_of(k * n_near + t * LANES, LANES), LANES)
            hit = chunk_ids == row(chunk_no[k : k + 1, :], top_rows)
            for i in range(3):
                both = [jnp.where(hit, row(part[k : k + 1, :], top_rows), 0.0) for part in parts[i]]
                val_ref[2 * i * top_rows : 2 * (i + 1) * top_rows, at] = jnp.concatenate(both, axis=0).astype(bf16)

    in_turns(0, n_near // LANES, place_tile)
    landed = dot_nt(val_ref[...], ohlo_ref[...])
    fetch.wait()
    lines = push_ref.shape[0] // (n_wide + 1)
    for i in range(3):
        total = (
            landed[2 * i * top_rows : (2 * i + 1) * top_rows] + landed[(2 * i + 1) * top_rows : (2 * i + 2) * top_rows]
        )
        for g in range(n_wide):
            for t in range(tiles):
                cols = slice(t * LANES, (t + 1) * LANES)
                line = total[g * tiles + t : g * tiles + t + 1, :]
                if g < len(near):
                    here = slice(g * atoms + t * LANES, g * atoms + (t + 1) * LANES)
                    line = line - jnp.sum(dr_ref[i, :, here], axis=0, keepdims=True)
                line = -HALF_STEP * line
                at = i * tiles + t
                if g == 0:
                    line = line + moment_ref[i, :, cols]
                    push_ref[at : at + 1, :] = blocks[0][i : i + 1, cols]
                push_ref[(1 + g) * lines + at : (1 + g) * lines + at + 1, :] = line
                mass = HEAVY - (HEAVY - 1.0) * blocks[g][3:4, cols]
                mass_ref[g * lines + at : g * lines + at + 1, :] = mass
    if lines > 3 * tiles:
        for g in range(n_wide + 1):
            blank = slice(g * lines + 3 * tiles, (g + 1) * lines)
            push_ref[blank, :] = jnp.zeros((lines - 3 * tiles, LANES), f32)
            if g < n_wide:
                mass_ref[blank, :] = jnp.ones((lines - 3 * tiles, LANES), f32)


def in_hbm(x):
    return pltpu.with_memory_space_constraint(x, pltpu.HBM)


def run(name, body, operands, results, scratch=(), far=(), cost=None):
    sizes = [math.prod(x.shape) * x.dtype.itemsize // 2 for i, x in enumerate(operands) if i not in far]
    sizes += [math.prod(shape) * jnp.dtype(dtype).itemsize for shape, dtype in results]
    sizes += [math.prod(x.shape) * x.dtype.itemsize for x in scratch if x.memory_space == pltpu.VMEM]
    limit = sum(sizes) + 4 * MIB
    specs = [pl.BlockSpec(memory_space=pltpu.HBM if i in far else pltpu.VMEM) for i in range(len(operands))]
    return pl.pallas_call(
        body,
        out_shape=tuple(jax.ShapeDtypeStruct(shape, dtype) for shape, dtype in results),
        in_specs=specs,
        out_specs=tuple(pl.BlockSpec(memory_space=pltpu.VMEM) for _ in results),
        scratch_shapes=list(scratch),
        compiler_params=pltpu.CompilerParams(vmem_limit_bytes=limit),
        cost_estimate=cost,
        name=name,
    )(*[in_hbm(x) if i in far else x for i, x in enumerate(operands)])


def choose(block, embedding, radial_one, radial_two, mix_one, mix_two, read_one, read_two):
    atoms = block.shape[1]
    slots = block.shape[0] - HEAD
    chan = embedding.shape[1]
    bases = radial_one.shape[0]
    weights = (embedding, radial_one, radial_two, mix_one, mix_two, read_one[None], read_two[None])
    return run(
        "choose",
        choose_kernel,
        (block, *weights),
        (
            ((2 * atoms, slots * atoms), bf16),
            ((chan, 8 * bases), bf16),
            ((chan, 4 * bases), bf16),
            ((chan, LANES), f32),
            ((4 * bases, 2 * chan), bf16),
            ((2, 2 * chan, 3 * chan), bf16),
            ((2, 3, 2 * chan, chan), bf16),
        ),
        [pltpu.VMEM(w.shape, f32) for w in weights] + [pltpu.SemaphoreType.DMA((len(weights),))],
        range(1, 1 + len(weights)),
        cost=pl.CostEstimate(flops=2 * 10**9, bytes_accessed=2 * 10**6, transcendentals=0),
    )


def pushes(plan, blocks, momenta, chosen):
    atoms, near, wide, _, _ = plan
    oh, rrc, r2c, sides, rrr, mixa, mixt = chosen
    chan = rrc.shape[0]
    bases = rrr.shape[0] // 4
    slots = blocks[0].shape[0] - HEAD
    n_near = len(near) * atoms
    edges = slots * atoms
    top_rows = -(-len(wide) * atoms // LANES // 8) * 8
    lines = line_count(atoms)
    geo, y, yb, ub, bk, bt, gidx, pick, as1 = run(
        "edges",
        functools.partial(edge_kernel, plan),
        blocks,
        (
            ((6, slots, n_near), f32),
            ((ORDERS - 1, slots, n_near), f32),
            ((ORDERS - 1, slots, 8, atoms), f32),
            ((3, slots, 8, atoms), f32),
            ((bases, slots, n_near), f32),
            ((slots, 2 * bases, n_near), f32),
            ((slots, n_near), jnp.int32),
            ((n_near, atoms), bf16),
            ((ORDERS, 8 * bases, n_near), bf16),
        ),
    )
    m1, sp1, hid, hs = run(
        "first",
        functools.partial(first_kernel, plan),
        (*blocks, as1, rrc, sides, mixa),
        (((ORDERS, chan, n_near), f32), ((chan, n_near), f32), ((chan, n_near), f32), ((2 * chan, n_near), bf16)),
        [pltpu.VMEM((8, n_near), f32)],
    )
    hj, w, slope, car = run(
        "gather",
        gather_kernel,
        (hid, hs, oh, pick, gidx, bt, geo, r2c),
        (((chan, edges), f32),) * 4,
        [pltpu.VMEM((2 * chan, 2 * atoms), bf16)],
    )
    m2, dinv = run(
        "moments",
        moment_kernel,
        (car, yb, mixa, mixt, sides),
        (((ORDERS, chan, atoms), f32), ((3 * chan, atoms), f32)),
        [pltpu.VMEM((3 * chan, atoms), f32)],
    )
    dhe, p = run(
        "back_second",
        back_second_kernel,
        (m2, dinv, car, hj, w, slope, ub),
        (((2 * chan, edges), bf16), ((4, 8 * slots, atoms), f32)),
    )
    dh, q, ohlo = run(
        "scatter",
        scatter_kernel,
        (oh, pick, dhe, sides, p, gidx),
        (((chan, n_near), f32), ((4 * slots, atoms), f32), ((LANES, slots * n_near), bf16)),
    )
    (da,) = run("back_first", back_first_kernel, (dh, sp1, m1, mixt, rrr), (((ORDERS, 2 * bases, n_near), f32),))
    return run(
        "back_edges",
        functools.partial(back_edge_kernel, plan),
        (*blocks, momenta, geo, y, bk, gidx, da, q, ohlo),
        ((((len(wide) + 1) * lines, LANES), f32), ((len(wide) * lines, LANES), f32)),
        [
            pltpu.VMEM((6 * top_rows, slots * n_near), bf16),
            pltpu.VMEM((3, slots, n_near), f32),
            pltpu.VMEM(momenta.shape, f32),
            pltpu.SemaphoreType.DMA(()),
        ],
        (len(blocks),),
    )


def line_count(atoms):
    return -(-3 * (atoms // LANES) // 8) * 8


def ring_plan(domains, atoms):
    near = list(dict.fromkeys(o % domains for o in (0, 1, -1)))
    wide = list(dict.fromkeys(near + [o % domains for o in (2, -2)]))
    before = tuple(wide.index((o - 1) % domains) for o in near)
    after = tuple(wide.index((o + 1) % domains) for o in near)
    return atoms, tuple(near), tuple(wide), before, after


def mode_turns(bead_total):
    bead = np.arange(bead_total, dtype=np.float64)[:, None]
    mode = np.arange(bead_total, dtype=np.float64)[None, :]
    phase = 2.0 * np.pi * bead * mode / bead_total
    half_total = bead_total // 2
    table = math.sqrt(2.0 / bead_total) * np.where(mode < half_total, np.cos(phase), np.sin(phase))
    table = np.where(mode == half_total, np.cos(np.pi * bead) / math.sqrt(bead_total), table)
    table = np.where(mode == 0, 1.0 / math.sqrt(bead_total), table)
    angles = bead_total * np.sin(np.pi * mode[0] / bead_total)
    safe = np.where(mode[0] == 0, 1.0, angles)
    reach = np.where(mode[0] == 0, STEP, STEP * np.sin(angles) / safe)
    stiff = angles * np.sin(angles) / STEP
    return [[float(x) for x in (table * factor[None, :]) @ table[0]] for factor in (np.cos(angles), reach, stiff)]


def pack_kernel(coord_src, species_src, send_src, slot_src, block_ref, coord_ref, species_ref, send_ref, slot_ref, sems):
    pairs = ((coord_src, coord_ref), (species_src, species_ref), (send_src, send_ref), (slot_src, slot_ref))
    fetches = [pltpu.make_async_copy(src, dst, sems.at[i]) for i, (src, dst) in enumerate(pairs)]
    for fetch in fetches:
        fetch.start()
    for fetch in fetches:
        fetch.wait()
    atoms = block_ref.shape[1]
    for i in range(3):
        block_ref[i : i + 1, :] = coord_ref[i]
    block_ref[3:4, :] = species_ref[...].astype(f32)
    block_ref[4:5, :] = send_ref[...].astype(f32)
    block_ref[5:HEAD, :] = jnp.zeros((HEAD - 5, atoms), f32)
    block_ref[HEAD:, :] = slot_ref[...].astype(f32)


def turn_kernel(shape, bead_ref, domain_ref, mass_ref, *refs):
    outer, inner, domains, wide = shape
    message_ref = refs[outer]
    turns = mode_turns(outer * inner)
    lines = mass_ref.shape[0] // len(wide)
    my_domain = domain_ref[0]
    my_inner = lax.rem(bead_ref[0], inner)
    if domains > len(wide):
        message_ref[...] = jnp.zeros_like(message_ref)
    masses = [mass_ref[g * lines : (g + 1) * lines, :] for g in range(len(wide))]
    sources = []
    for z in range(outer):
        sources.append([refs[z][g * lines : (g + 1) * lines, :] for g in range(len(wide) + 1)])
    for s in range(inner):
        wraps = jnp.full((lines, LANES), my_inner + s) >= inner
        weights = []
        for turn in turns:
            row_of = []
            for z in range(outer):
                there = turn[(z * inner + s) % (outer * inner)]
                round_it = turn[(z * inner + s - inner) % (outer * inner)]
                row_of.append(jnp.where(wraps, jnp.full((lines, LANES), round_it), jnp.full((lines, LANES), there)))
            weights.append(row_of)
        to_inner = lax.rem(my_inner + s, inner)
        for g in range(len(wide)):
            turned = sum(weights[0][z] * sources[z][1 + g] for z in range(outer))
            drift = sum(weights[1][z] * sources[z][1 + g] for z in range(outer))
            new_q = drift / masses[g]
            new_p = turned
            if g == 0:
                new_q = new_q + sum(weights[0][z] * sources[z][0] for z in range(outer))
                new_p = new_p - masses[g] * sum(weights[2][z] * sources[z][0] for z in range(outer))
            to = to_inner * domains + lax.rem(my_domain + wide[g], domains)
            message_ref[to, 0:lines, :] = new_q
            message_ref[to, lines:, :] = new_p


def sum_kernel(arrived_ref, q_ref, p_ref):
    total = arrived_ref[0]
    for i in range(1, arrived_ref.shape[0]):
        total = total + arrived_ref[i]
    lines = total.shape[0] // 2
    tiles = q_ref.shape[2] // LANES
    for i in range(3):
        for t in range(tiles):
            at = i * tiles + t
            q_ref[i, :, t * LANES : (t + 1) * LANES] = total[at : at + 1]
            p_ref[i, :, t * LANES : (t + 1) * LANES] = total[lines + at : lines + at + 1]


def shards(
    positions, momenta, species, neighbours, send_list, embedding, radial_one, radial_two, mix_one, mix_two,
    read_one, read_two,
):
    slots, atoms = neighbours.shape
    domains = lax.axis_size("space")
    beads = lax.axis_size("bead")
    inner = next(d for d in range(1, beads + 1) if beads % d == 0 and d * d >= beads)
    outer = beads // inner
    plan = ring_plan(domains, atoms)
    wide = plan[2]
    vmem = pl.BlockSpec(memory_space=pltpu.VMEM)
    smem = pl.BlockSpec(memory_space=pltpu.SMEM)
    far = pl.BlockSpec(memory_space=pltpu.HBM)
    small = pltpu.CompilerParams(vmem_limit_bytes=4 * MIB)
    coord_rows = jnp.transpose(positions, (1, 0, 2))
    moment_rows = jnp.transpose(momenta, (1, 0, 2))
    block = pl.pallas_call(
        pack_kernel,
        out_shape=jax.ShapeDtypeStruct((HEAD + slots, atoms), f32),
        in_specs=[far] * 4,
        out_specs=vmem,
        scratch_shapes=[
            pltpu.VMEM(coord_rows.shape, f32),
            pltpu.VMEM((1, atoms), jnp.int32),
            pltpu.VMEM((1, atoms), jnp.int32),
            pltpu.VMEM((slots, atoms), jnp.int32),
            pltpu.SemaphoreType.DMA((4,)),
        ],
        compiler_params=small,
        name="pack",
    )(in_hbm(coord_rows), in_hbm(species[None]), in_hbm(send_list[None]), in_hbm(neighbours))
    blocks = [block]
    for offset in wide[1:]:
        blocks.append(lax.ppermute(block, "space", [(i, (i - offset) % domains) for i in range(domains)]))
    chosen = choose(block, embedding, radial_one, radial_two, mix_one, mix_two, read_one, read_two)
    pushed, masses = pushes(plan, blocks, moment_rows, chosen)
    sources = [pushed]
    for z in range(1, outer):
        sources.append(lax.ppermute(pushed, "bead", [(b, (b + z * inner) % beads) for b in range(beads)]))
    here = [lax.axis_index(axis).astype(jnp.int32).reshape(1) for axis in ("bead", "space")]
    lines = line_count(atoms)
    messages = pl.pallas_call(
        functools.partial(turn_kernel, (outer, inner, domains, wide)),
        out_shape=jax.ShapeDtypeStruct((inner * domains, 2 * lines, LANES), f32),
        in_specs=[smem, smem, vmem] + [vmem] * outer,
        out_specs=vmem,
        compiler_params=small,
        name="turn",
    )(*here, masses, *sources)
    rows = [[z * inner * domains + i for i in range(inner * domains)] for z in range(outer)]
    arrived = lax.all_to_all(messages, ("bead", "space"), 0, 0, axis_index_groups=rows, tiled=True)
    new_q, new_p = pl.pallas_call(
        sum_kernel,
        out_shape=(jax.ShapeDtypeStruct((3, 1, atoms), f32),) * 2,
        in_specs=[vmem],
        out_specs=(vmem, vmem),
        compiler_params=small,
        name="sum",
    )(arrived)
    return (jnp.transpose(new_q, (1, 0, 2)), jnp.transpose(new_p, (1, 0, 2)))


def solution(mesh):
    placed = (
        P("bead", None, "space"),
        P("bead", None, "space"),
        P("space"),
        P(None, "space"),
        P("space"),
        P(),
        P(),
        P(),
        P(),
        P(),
        P(),
        P(),
    )
    return jax.shard_map(
        shards,
        mesh=mesh,
        in_specs=placed,
        out_specs=(P("bead", None, "space"), P("bead", None, "space")),
        check_vma=False,
    )
```

```python
import functools
import math

import jax
import jax.numpy as jnp
import numpy as np
from jax import lax
from jax.experimental import pallas as pl
from jax.experimental.pallas import tpu as pltpu
from jax.sharding import PartitionSpec as P

STEP = 2.0
HALF_STEP = 1.0
HEAVY = 16.0
SQRT3 = math.sqrt(3.0)
SQRT5 = math.sqrt(5.0)
SQRT15 = math.sqrt(15.0)
LANES = 128
ORDERS = 9
GROUP = (0, 1, 1, 1, 2, 2, 2, 2, 2)
HEAD = 8
MIB = 1024 * 1024
f32 = jnp.float32
bf16 = jnp.bfloat16


def split(x):
    hi = x.astype(bf16)
    return hi, (x - hi.astype(f32)).astype(bf16)


def split_rows(x):
    hi = x.astype(bf16).astype(f32)
    return jnp.concatenate([hi, x - hi], axis=0)


def dot(a, b):
    return jnp.dot(a, b, preferred_element_type=f32)


def dot_nt(a, b):
    return lax.dot_general(a, b, (((1,), (1,)), ((), ())), preferred_element_type=f32)


def in_turns(start, stop, step, most=4):
    per_turn = next(n for n in range(most, 0, -1) if (stop - start) % n == 0)

    def turn(i, carry):
        for j in range(per_turn):
            step(start + i * per_turn + j)
        return carry

    lax.fori_loop(0, (stop - start) // per_turn, turn, 0)


def row(x, rows=8):
    return jnp.broadcast_to(x, (rows, x.shape[1]))


def lookup(chunks, wanted, position):
    out = None
    for number, chunk in chunks:
        got = jnp.take_along_axis(row(chunk), position, axis=1, mode="promise_in_bounds")
        out = got if out is None else jnp.where(wanted == number, got, out)
    return out


def harmonics(ux, uy, uz):
    return [
        None,
        SQRT3 * ux,
        SQRT3 * uy,
        SQRT3 * uz,
        SQRT15 * ux * uy,
        SQRT15 * uy * uz,
        0.5 * SQRT5 * (2.0 * uz * uz - ux * ux - uy * uy),
        SQRT15 * ux * uz,
        0.5 * SQRT15 * (ux * ux - uy * uy),
    ]


def silu_parts(v):
    gate = 1.0 / (1.0 + jnp.exp(-v))
    return v * gate, gate * (1.0 + v * (1.0 - gate))


def choose_kernel(block_ref, *refs):
    sources = refs[:7]
    oh_ref, rrc_ref, r2c_ref, side_ref, rrr_ref, mixa_ref, mixt_ref = refs[7:14]
    held = refs[14:21]
    sems = refs[21]
    emb_ref, rad1_ref, rad2_ref, mix1_ref, mix2_ref, read1_ref, read2_ref = held
    fetches = [pltpu.make_async_copy(src, dst, sems.at[i]) for i, (src, dst) in enumerate(zip(sources, held))]
    for fetch in fetches:
        fetch.start()
    chan = emb_ref.shape[1]
    bases = rad1_ref.shape[0]
    atoms = block_ref.shape[1]
    slots = block_ref.shape[0] - HEAD

    tile_edges = slots * LANES
    ids16 = lax.broadcasted_iota(jnp.int32, (LANES, tile_edges), 0).astype(jnp.int16)
    one16 = jnp.ones((LANES, tile_edges), bf16)
    zero16 = jnp.zeros((LANES, tile_edges), bf16)
    for t in range(atoms // LANES):
        slot = block_ref[HEAD : HEAD + slots, t * LANES : (t + 1) * LANES].astype(jnp.int32)
        line = jnp.concatenate([slot[k : k + 1, :] for k in range(slots)], axis=1)
        wanted = jnp.broadcast_to(line, (LANES, tile_edges)).astype(jnp.int16)
        for r in range(oh_ref.shape[0] // LANES):
            hit = wanted - jnp.int16(r * LANES) == ids16
            oh_ref[r * LANES : (r + 1) * LANES, t * tile_edges : (t + 1) * tile_edges] = jnp.where(hit, one16, zero16)

    for fetch in fetches:
        fetch.wait()
    emb0 = emb_ref[0:1, :]
    emb_d = emb_ref[1:2, :] - emb0
    rr = jnp.concatenate([rad1_ref[...] * emb0, rad1_ref[...] * emb_d], axis=0) * (1.0 / slots)
    rr_hi = rr.astype(bf16).astype(f32)
    rr_lo = rr - rr_hi
    r2 = rad2_ref[...] * (1.0 / slots)
    r2_hi = r2.astype(bf16).astype(f32)
    r2_lo = r2 - r2_hi
    zeros = jnp.zeros((8, chan), f32)
    turned1 = jnp.concatenate([rr_hi, rr_hi, rr_lo, rr_lo] + [zeros] * 8, axis=0).T
    sides = jnp.concatenate([emb0, emb_d, read1_ref[...], read2_ref[...], zeros[:4]], axis=0)
    turned2 = jnp.concatenate([r2_hi, r2_hi, r2_lo, r2_lo] + [zeros] * 12, axis=0).T
    rrc_ref[...] = turned1[:, : 8 * bases].astype(bf16)
    r2c_ref[...] = turned2[:, : 4 * bases].astype(bf16)
    side_ref[...] = jnp.concatenate([sides] + [zeros] * 15, axis=0).T
    rrr_ref[...] = jnp.concatenate(
        [jnp.concatenate([rr_hi, rr_hi], axis=1), jnp.concatenate([rr_lo, jnp.zeros_like(rr_lo)], axis=1)], axis=0
    ).astype(bf16)
    for i, ref in enumerate((mix1_ref, mix2_ref)):
        hi, lo = split(ref[...])
        mixa_ref[i, 0:chan, :] = hi
        mixa_ref[i, chan:, :] = lo
        for g in range(3):
            hi, lo = split(ref[:, g * chan : (g + 1) * chan].T)
            mixt_ref[i, g, 0:chan, :] = hi
            mixt_ref[i, g, chan:, :] = lo


def dot_parts(both, hi, lo):
    rows = both.shape[0] // 2
    first = dot(both, hi)
    return first[:rows] + first[rows:] + dot(both[:rows], lo)


def edge_kernel(plan, *refs):
    atoms, near, wide, before, after = plan
    n_wide = len(wide)
    blocks = refs[:n_wide]
    geo_ref, y_ref, yb_ref, ub_ref, bk_ref, bt_ref, gidx_ref, pick_ref, as_ref = refs[n_wide:]
    bases = bk_ref.shape[0]
    slots = gidx_ref.shape[0]
    tiles = atoms // LANES
    half = atoms // 2
    half_tiles = half // LANES
    order_col = lax.broadcasted_iota(jnp.int32, (bases, LANES), 0).astype(f32)
    tables = []
    for quantity in range(4):
        chunks = []
        for g in range(n_wide):
            for t in range(tiles):
                chunks.append((g * tiles + t, blocks[g][quantity : quantity + 1, t * LANES : (t + 1) * LANES]))
        tables.append(chunks)
    for q in range(len(near)):
        ghosts = []
        for t in range(half_tiles):
            ghosts.append(
                (t, blocks[before[q]][4:5, half + t * LANES : half + (t + 1) * LANES] + float(before[q] * atoms))
            )
        for t in range(half_tiles):
            ghosts.append(
                (
                    half_tiles + tiles + t,
                    blocks[after[q]][4:5, t * LANES : (t + 1) * LANES] + float(after[q] * atoms),
                )
            )
        if q == 0:
            ids16 = lax.broadcasted_iota(jnp.int32, (pick_ref.shape[0], LANES), 0).astype(jnp.int16)
            one16 = jnp.ones(ids16.shape, bf16)
            zero16 = jnp.zeros(ids16.shape, bf16)
            for t, (_, chunk) in enumerate(ghosts):
                wanted = jnp.broadcast_to(chunk.astype(jnp.int32), ids16.shape).astype(jnp.int16)
                pick_ref[:, t * LANES : (t + 1) * LANES] = jnp.where(wanted == ids16, one16, zero16)
        for t in range(tiles):
            cols = slice(t * LANES, (t + 1) * LANES)
            here = slice(q * atoms + t * LANES, q * atoms + (t + 1) * LANES)
            slot = blocks[q][HEAD : HEAD + slots, cols].astype(jnp.int32)
            chunk_no = slot >> 7
            far = lookup(ghosts, chunk_no, slot & 127).astype(jnp.int32)
            own = (slot >= half) & (slot < half + atoms)
            gidx = jnp.where(own, slot + (q * atoms - half), far)
            gidx_ref[:, here] = gidx
            chunk_no = gidx >> 7
            place = gidx & 127
            xj, yj, zj, fj = [lookup(tables[i], chunk_no, place) for i in range(4)]
            rx = xj - row(blocks[q][0:1, cols])
            ry = yj - row(blocks[q][1:2, cols])
            rz = zj - row(blocks[q][2:3, cols])
            soft = jnp.sqrt(rx * rx + ry * ry + rz * rz + 1.0)
            back = 1.0 / soft
            ux, uy, uz = rx * back, ry * back, rz * back
            for i, value in enumerate((ux, uy, uz, back, soft, fj)):
                geo_ref[i, :, here] = value
            if q == 0:
                for i, value in enumerate((ux, uy, uz)):
                    for k in range(slots):
                        ub_ref[i, k, :, cols] = row(value[k : k + 1, :])
            sphere = harmonics(ux, uy, uz)
            for l in range(1, ORDERS):
                y_ref[l - 1, :, here] = sphere[l]
                if q == 0:
                    for k in range(slots):
                        yb_ref[l - 1, k, :, cols] = row(sphere[l][k : k + 1, :])
            for n in range(bases):
                bk_ref[n, :, here] = jnp.exp(-0.5 * (soft - (1.0 + n)) ** 2)
            for k in range(slots):
                basis = jnp.exp(-0.5 * (row(soft[k : k + 1, :], bases) - (1.0 + order_col)) ** 2)
                bt_ref[k, 0:bases, here] = basis
                bt_ref[k, bases : 2 * bases, here] = basis * row(fj[k : k + 1, :], bases)
            low = [None] * ORDERS
            for k in range(slots):
                basis = bt_ref[k, :, here]
                for l in range(ORDERS):
                    term = basis if l == 0 else basis * row(y_ref[l - 1, k : k + 1, here], 2 * bases)
                    low[l] = term if low[l] is None else low[l] + term
            for l in range(ORDERS):
                both = split_rows(low[l]).astype(bf16)
                as_ref[l, 0 : 4 * bases, here] = both
                as_ref[l, 4 * bases : 8 * bases, here] = both


def first_kernel(plan, *refs):
    atoms, near, wide, _, _ = plan
    n_wide = len(wide)
    blocks = refs[:n_wide]
    as_ref, rrc_ref, side_ref, mixa_ref, m1_ref, sp1_ref, hid_ref, hs_ref, flag_ref = refs[n_wide:]
    chan = m1_ref.shape[1]
    n_near = m1_ref.shape[2]

    for q in range(len(near)):
        flag_ref[0:1, q * atoms : (q + 1) * atoms] = blocks[q][3:4, :]
    wide_cols = 2 * LANES
    emb0_col = side_ref[:, 0:1]
    embd_col = side_ref[:, 1:2]

    def first(j):
        here = pl.ds(pl.multiple_of(j * wide_cols, wide_cols), wide_cols)
        inv = [None, None, None]
        for l in range(ORDERS):
            m = dot(rrc_ref[...], as_ref[l, :, here])
            m1_ref[l, :, here] = m
            inv[GROUP[l]] = m * m if inv[GROUP[l]] is None else inv[GROUP[l]] + m * m
        hi, lo = split(jnp.concatenate(inv, axis=0))
        value = dot_parts(mixa_ref[0], hi, lo)
        act, slope = silu_parts(value)
        sp1_ref[:, here] = slope
        hidden = act + emb0_col + embd_col * flag_ref[0:1, here]
        hid_ref[:, here] = hidden
        hi, lo = split(hidden)
        hs_ref[0:chan, here] = hi
        hs_ref[chan : 2 * chan, here] = lo

    in_turns(0, n_near // wide_cols, first)


def second_kernel(hid_ref, hs_ref, oh_ref, pick_ref, gidx_ref, bt_ref, geo_ref, r2c_ref, yb_ref, mixa_ref, mixt_ref,
                  side_ref, hj_ref, w_ref, slope_ref, car_ref, m2_ref, dinv_ref, ext_ref, inv_ref):
    slots = bt_ref.shape[0]
    bases = bt_ref.shape[1] // 2
    chan, n_near = hid_ref.shape
    atoms = hj_ref.shape[1] // slots
    half = atoms // 2
    tile_edges = slots * LANES
    wide_cols = 2 * LANES
    rows = 32
    reach = 1.0 + lax.broadcasted_iota(jnp.int32, (bases, LANES), 0).astype(f32)
    ghosts = dot(hs_ref[...], pick_ref[...]).astype(bf16)
    ext_ref[:, 0:half] = ghosts[:, :half]
    ext_ref[:, half : half + atoms] = hs_ref[:, 0:atoms]
    ext_ref[:, half + atoms :] = ghosts[:, half:]

    def weights(t):
        cols = slice(t * LANES, (t + 1) * LANES)
        here = slice(t * tile_edges, (t + 1) * tile_edges)
        basis = [bt_ref[k, 0:bases, cols] for k in range(slots)]
        slopes = [basis[k] * (reach - row(geo_ref[4, k : k + 1, cols], bases)) for k in range(slots)]
        for ref, values in ((w_ref, basis), (slope_ref, slopes)):
            both = split_rows(jnp.concatenate(values, axis=1))
            ref[:, here] = dot(r2c_ref[...], jnp.concatenate([both, both], axis=0).astype(bf16))

    def gather(t):
        by_lane = 2 + 2 * (t % 2)
        here = slice(t * tile_edges, t * tile_edges + (slots - by_lane) * LANES)
        both = dot(ext_ref[...], oh_ref[:, here])
        for k in range(slots - by_lane, slots):
            at = slice(t * tile_edges + k * LANES, t * tile_edges + (k + 1) * LANES)
            mine = row(gidx_ref[k : k + 1, t * LANES : (t + 1) * LANES])
            chunk_no = mine >> 7
            place = mine & 127
            for c in range(chan // 8):
                lines = slice(8 * c, 8 * c + 8)
                feat = None
                for chunk in range(n_near // LANES):
                    held = hid_ref[lines, chunk * LANES : (chunk + 1) * LANES]
                    got = jnp.take_along_axis(held, place, axis=1, mode="promise_in_bounds")
                    feat = got if feat is None else jnp.where(chunk_no == chunk, got, feat)
                hj_ref[lines, at] = feat
                car_ref[lines, at] = feat * w_ref[lines, at]
        feat = both[:chan] + both[chan:]
        hj_ref[:, here] = feat
        car_ref[:, here] = feat * w_ref[:, here]

    def moments(t, base):
        cols = slice(t * LANES, (t + 1) * LANES)
        acc = [[None] * ORDERS for _ in range(rows // 8)]
        for k in range(slots):
            at = slice(t * tile_edges + k * LANES, t * tile_edges + (k + 1) * LANES)
            got = car_ref[base : base + rows, at]
            for l in range(ORDERS):
                yb = yb_ref[l - 1, k, :, cols] if l else None
                for h in range(rows // 8):
                    part = got[8 * h : 8 * h + 8]
                    term = part * yb if l else part
                    acc[h][l] = term if acc[h][l] is None else acc[h][l] + term
        for h in range(rows // 8):
            inv = [None] * 3
            for l in range(ORDERS):
                m2_ref[l, base + 8 * h : base + 8 * h + 8, cols] = acc[h][l]
                sq = acc[h][l] * acc[h][l]
                g = GROUP[l]
                inv[g] = sq if inv[g] is None else inv[g] + sq
            for g in range(3):
                inv_ref[g * chan + base + 8 * h : g * chan + base + 8 * h + 8, cols] = inv[g]

    read2_col = side_ref[:, 3:4]
    for t in range(atoms // LANES):
        weights(t)
        gather(t)
        for base in range(0, chan, rows):
            moments(t, base)
        if t % 2:
            cols = slice((t - 1) * LANES, (t + 1) * LANES)
            hi, lo = split(inv_ref[:, cols])
            _, slope = silu_parts(dot_parts(mixa_ref[1], hi, lo))
            hi, lo = split(slope * (2.0 * read2_col))
            for g, scale in enumerate((1.0, 0.5 * SQRT3, 0.5 * SQRT15)):
                dinv_ref[g * chan : (g + 1) * chan, cols] = scale * dot_parts(mixt_ref[1, g], hi, lo)


def back_second_kernel(m2_ref, dinv_ref, car_ref, hj_ref, w_ref, slope_ref, ub_ref, dhe_ref, p_ref):
    slots = ub_ref.shape[1]
    chan, atoms = m2_ref.shape[1:]
    tiles = atoms // LANES
    pairs = chan // 16
    per_turn = 4 if pairs % 4 == 0 else 1
    k_step = slots // 2

    def back_moments(t, carry):
        cols = pl.ds(pl.multiple_of(t * LANES, LANES), LANES)

        def one(c, acc, k0):
            forms = []
            for h in range(2):
                rows = pl.ds(pl.multiple_of(c * 16 + 8 * h, 8), 8)
                scale = [dinv_ref[pl.ds(pl.multiple_of(g * chan + c * 16 + 8 * h, 8), 8), cols] for g in range(3)]
                dm = [m2_ref[l, rows, cols] * scale[GROUP[l]] for l in range(ORDERS)]
                low = dm[6] * (1.0 / SQRT3)
                forms.append((dm[0], dm[1], dm[2], dm[3], dm[8] - low, -dm[8] - low, low + low, dm[4], dm[5], dm[7]))
            base = pl.multiple_of(c * 16, 16)
            for k in range(k0, k0 + k_step):
                at = pl.ds(pl.multiple_of((t * slots + k) * LANES, LANES), LANES)
                got = car_ref[pl.ds(base, 16), at]
                stretch = hj_ref[pl.ds(base, 16), at] * slope_ref[pl.ds(base, 16), at]
                ux, uy, uz = [ub_ref[i, k, :, cols] for i in range(3)]
                out = []
                for h in range(2):
                    mid, dx, dy, dz, qxx, qyy, qzz, qxy, qyz, qxz = forms[h]
                    gx = dx + qxx * ux + qxy * uy + qxz * uz
                    gy = dy + qxy * ux + qyy * uy + qyz * uz
                    gz = dz + qxz * ux + qyz * uy + qzz * uz
                    out.append(mid + (gx + dx) * ux + (gy + dy) * uy + (gz + dz) * uz)
                    part = got[8 * h : 8 * h + 8]
                    at_acc = 4 * (k - k0)
                    for i, g in enumerate((gx, gy, gz)):
                        acc[at_acc + i] = acc[at_acc + i] + part * g
                    acc[at_acc + 3] = acc[at_acc + 3] + out[h] * stretch[8 * h : 8 * h + 8]
                hi, lo = split(jnp.concatenate(out, axis=0) * w_ref[pl.ds(base, 16), at])
                dhe_ref[pl.ds(base, 16), at] = hi
                dhe_ref[pl.ds(pl.multiple_of(chan + c * 16, 16), 16), at] = lo

        for k0 in range(0, slots, k_step):

            def over(c, acc, k0=k0):
                acc = list(acc)
                for i in range(per_turn):
                    one(per_turn * c + i, acc, k0)
                return tuple(acc)

            start = tuple(jnp.zeros((8, LANES), f32) for _ in range(4 * k_step))
            acc = lax.fori_loop(0, pairs // per_turn, over, start)
            for k in range(k_step):
                for i in range(4):
                    p_ref[i, 8 * (k0 + k) : 8 * (k0 + k) + 8, cols] = acc[4 * k + i]
        return carry

    lax.fori_loop(0, tiles, back_moments, 0)


def scatter_kernel(oh_ref, pick_ref, dhe_ref, side_ref, p_ref, gidx_ref, dh_ref, q_ref, ohlo_ref):
    chan, n_near = dh_ref.shape
    slots = gidx_ref.shape[0]
    atoms = pick_ref.shape[1]
    half = atoms // 2
    both = dot_nt(dhe_ref[...], jnp.concatenate([oh_ref[:half], oh_ref[half + atoms :]], axis=0))
    hi, lo = split(both[:chan] + both[chan:])
    spread = dot_nt(jnp.concatenate([hi, lo], axis=0), pick_ref[...])
    spread = spread[:chan] + spread[chan:]
    both = dot_nt(dhe_ref[...], oh_ref[half : half + atoms])
    dh_ref[:, 0:atoms] = spread[:, :atoms] + both[:chan] + both[chan:] + side_ref[:, 2:3]
    if n_near > atoms:
        dh_ref[:, atoms:] = spread[:, atoms:]
    ids16 = lax.broadcasted_iota(jnp.int32, (LANES, n_near), 0).astype(jnp.int16)
    one16 = jnp.ones((LANES, n_near), bf16)
    zero16 = jnp.zeros((LANES, n_near), bf16)
    for k in range(slots):
        place = jnp.broadcast_to(gidx_ref[k : k + 1, :] & 127, (LANES, n_near)).astype(jnp.int16)
        ohlo_ref[:, k * n_near : (k + 1) * n_near] = jnp.where(place == ids16, one16, zero16)
    lane = lax.broadcasted_iota(jnp.int32, (slots, 16 * slots), 1)
    sub = lax.broadcasted_iota(jnp.int32, (slots, 16 * slots), 0)
    adder = jnp.where(((lane >> 3) & (slots - 1)) == sub, 1.0, 0.0).astype(bf16)
    for i in range(4):
        total = dot(adder, split_rows(p_ref[i]).astype(bf16))
        q_ref[8 * i : 8 * i + 8, :] = 2.0 * total if i < 3 else total


def back_first_kernel(dh_ref, sp1_ref, m1_ref, mixt_ref, rrr_ref, da_ref):
    n_near = sp1_ref.shape[1]
    rows = rrr_ref.shape[0] // 2
    wide_cols = 2 * LANES

    def back_first(j):
        here = pl.ds(pl.multiple_of(j * wide_cols, wide_cols), wide_cols)
        hi, lo = split(dh_ref[:, here] * sp1_ref[:, here] * 2.0)
        scale = [dot_parts(mixt_ref[0, g], hi, lo) for g in range(3)]
        for l in range(ORDERS):
            hi, lo = split(m1_ref[l, :, here] * scale[GROUP[l]])
            out = dot(rrr_ref[...], jnp.concatenate([hi, lo], axis=0))
            da_ref[l, :, here] = out[:rows] + out[rows:]

    in_turns(0, n_near // wide_cols, back_first)


def back_edge_kernel(plan, *refs):
    atoms, near, wide, _, _ = plan
    n_wide = len(wide)
    blocks = refs[:n_wide]
    moment_src, geo_ref, y_ref, bk_ref, gidx_ref, da_ref, q_ref, ohlo_ref = refs[n_wide : n_wide + 8]
    push_ref, mass_ref, val_ref, dr_ref, moment_ref, sem = refs[n_wide + 8 :]
    fetch = pltpu.make_async_copy(moment_src, moment_ref, sem)
    fetch.start()
    bases, slots, n_near = bk_ref.shape
    tiles = atoms // LANES
    top_rows = val_ref.shape[0] // 6

    def back_geometry(t, mine):
        here = pl.ds(pl.multiple_of(t * LANES, LANES), LANES)
        ux, uy, uz, back, soft, fj = [geo_ref[i, :, here] for i in range(6)]
        dy = [None] * ORDERS
        ds = None
        for n in range(bases):
            basis = bk_ref[n, :, here]
            db = None
            for l in range(ORDERS):
                g = row(da_ref[l, n : n + 1, here]) + fj * row(da_ref[l, bases + n : bases + n + 1, here])
                if l:
                    dy[l] = g * basis if dy[l] is None else dy[l] + g * basis
                    db = db + g * y_ref[l - 1, :, here]
                else:
                    db = g
            db = db * basis * ((1.0 + n) - soft)
            ds = db if ds is None else ds + db
        if mine:
            ds = ds + q_ref[24:32, here]
        dux = SQRT3 * dy[1] + SQRT15 * (uy * dy[4] + uz * dy[7] + ux * dy[8]) - SQRT5 * ux * dy[6]
        duy = SQRT3 * dy[2] + SQRT15 * (ux * dy[4] + uz * dy[5] - uy * dy[8]) - SQRT5 * uy * dy[6]
        duz = SQRT3 * dy[3] + SQRT15 * (uy * dy[5] + ux * dy[7]) + 2.0 * SQRT5 * uz * dy[6]
        if mine:
            dux, duy, duz = [d + q_ref[8 * i : 8 * i + 8, here] for i, d in enumerate((dux, duy, duz))]
        along = ds - (ux * dux + uy * duy + uz * duz) * back
        for i, value in enumerate((dux * back + along * ux, duy * back + along * uy, duz * back + along * uz)):
            dr_ref[i, :, here] = value

    in_turns(0, tiles, lambda t: back_geometry(t, True))
    in_turns(tiles, n_near // LANES, lambda t: back_geometry(t, False))

    def place_tile(t):
        here = pl.ds(pl.multiple_of(t * LANES, LANES), LANES)
        gidx = gidx_ref[:, here]
        chunk_no = gidx >> 7
        parts = []
        for i in range(3):
            value = dr_ref[i, :, here]
            hi = value.astype(bf16).astype(f32)
            parts.append((hi, value - hi))
        chunk_ids = lax.broadcasted_iota(jnp.int32, (top_rows, LANES), 0)
        for k in range(slots):
            at = pl.ds(pl.multiple_of(k * n_near + t * LANES, LANES), LANES)
            hit = chunk_ids == row(chunk_no[k : k + 1, :], top_rows)
            for i in range(3):
                both = [jnp.where(hit, row(part[k : k + 1, :], top_rows), 0.0) for part in parts[i]]
                val_ref[2 * i * top_rows : 2 * (i + 1) * top_rows, at] = jnp.concatenate(both, axis=0).astype(bf16)

    in_turns(0, n_near // LANES, place_tile)
    landed = dot_nt(val_ref[...], ohlo_ref[...])
    fetch.wait()
    lines = push_ref.shape[0] // (n_wide + 1)
    for i in range(3):
        total = (
            landed[2 * i * top_rows : (2 * i + 1) * top_rows] + landed[(2 * i + 1) * top_rows : (2 * i + 2) * top_rows]
        )
        for g in range(n_wide):
            for t in range(tiles):
                cols = slice(t * LANES, (t + 1) * LANES)
                line = total[g * tiles + t : g * tiles + t + 1, :]
                if g < len(near):
                    here = slice(g * atoms + t * LANES, g * atoms + (t + 1) * LANES)
                    line = line - jnp.sum(dr_ref[i, :, here], axis=0, keepdims=True)
                line = -HALF_STEP * line
                at = i * tiles + t
                if g == 0:
                    line = line + moment_ref[i, :, cols]
                    push_ref[at : at + 1, :] = blocks[0][i : i + 1, cols]
                push_ref[(1 + g) * lines + at : (1 + g) * lines + at + 1, :] = line
                mass = HEAVY - (HEAVY - 1.0) * blocks[g][3:4, cols]
                mass_ref[g * lines + at : g * lines + at + 1, :] = mass
    if lines > 3 * tiles:
        for g in range(n_wide + 1):
            blank = slice(g * lines + 3 * tiles, (g + 1) * lines)
            push_ref[blank, :] = jnp.zeros((lines - 3 * tiles, LANES), f32)
            if g < n_wide:
                mass_ref[blank, :] = jnp.ones((lines - 3 * tiles, LANES), f32)


def in_hbm(x):
    return pltpu.with_memory_space_constraint(x, pltpu.HBM)


def run(name, body, operands, results, scratch=(), far=(), cost=None):
    sizes = [math.prod(x.shape) * x.dtype.itemsize // 2 for i, x in enumerate(operands) if i not in far]
    sizes += [math.prod(shape) * jnp.dtype(dtype).itemsize for shape, dtype in results]
    sizes += [math.prod(x.shape) * x.dtype.itemsize for x in scratch if x.memory_space == pltpu.VMEM]
    limit = sum(sizes) + 4 * MIB
    specs = [pl.BlockSpec(memory_space=pltpu.HBM if i in far else pltpu.VMEM) for i in range(len(operands))]
    return pl.pallas_call(
        body,
        out_shape=tuple(jax.ShapeDtypeStruct(shape, dtype) for shape, dtype in results),
        in_specs=specs,
        out_specs=tuple(pl.BlockSpec(memory_space=pltpu.VMEM) for _ in results),
        scratch_shapes=list(scratch),
        compiler_params=pltpu.CompilerParams(vmem_limit_bytes=limit),
        cost_estimate=cost,
        name=name,
    )(*[in_hbm(x) if i in far else x for i, x in enumerate(operands)])


def choose(block, embedding, radial_one, radial_two, mix_one, mix_two, read_one, read_two):
    atoms = block.shape[1]
    slots = block.shape[0] - HEAD
    chan = embedding.shape[1]
    bases = radial_one.shape[0]
    weights = (embedding, radial_one, radial_two, mix_one, mix_two, read_one[None], read_two[None])
    return run(
        "choose",
        choose_kernel,
        (block, *weights),
        (
            ((2 * atoms, slots * atoms), bf16),
            ((chan, 8 * bases), bf16),
            ((chan, 4 * bases), bf16),
            ((chan, LANES), f32),
            ((4 * bases, 2 * chan), bf16),
            ((2, 2 * chan, 3 * chan), bf16),
            ((2, 3, 2 * chan, chan), bf16),
        ),
        [pltpu.VMEM(w.shape, f32) for w in weights] + [pltpu.SemaphoreType.DMA((len(weights),))],
        range(1, 1 + len(weights)),
        cost=pl.CostEstimate(flops=2 * 10**9, bytes_accessed=2 * 10**6, transcendentals=0),
    )


def pushes(plan, blocks, momenta, chosen):
    atoms, near, wide, _, _ = plan
    oh, rrc, r2c, sides, rrr, mixa, mixt = chosen
    chan = rrc.shape[0]
    bases = rrr.shape[0] // 4
    slots = blocks[0].shape[0] - HEAD
    n_near = len(near) * atoms
    edges = slots * atoms
    top_rows = -(-len(wide) * atoms // LANES // 8) * 8
    lines = line_count(atoms)
    geo, y, yb, ub, bk, bt, gidx, pick, as1 = run(
        "edges",
        functools.partial(edge_kernel, plan),
        blocks,
        (
            ((6, slots, n_near), f32),
            ((ORDERS - 1, slots, n_near), f32),
            ((ORDERS - 1, slots, 8, atoms), f32),
            ((3, slots, 8, atoms), f32),
            ((bases, slots, n_near), f32),
            ((slots, 2 * bases, n_near), f32),
            ((slots, n_near), jnp.int32),
            ((n_near, atoms), bf16),
            ((ORDERS, 8 * bases, n_near), bf16),
        ),
    )
    m1, sp1, hid, hs = run(
        "first",
        functools.partial(first_kernel, plan),
        (*blocks, as1, rrc, sides, mixa),
        (((ORDERS, chan, n_near), f32), ((chan, n_near), f32), ((chan, n_near), f32), ((2 * chan, n_near), bf16)),
        [pltpu.VMEM((8, n_near), f32)],
    )
    hj, w, slope, car, m2, dinv = run(
        "second",
        second_kernel,
        (hid, hs, oh, pick, gidx, bt, geo, r2c, yb, mixa, mixt, sides),
        (((chan, edges), f32),) * 4 + (((ORDERS, chan, atoms), f32), ((3 * chan, atoms), f32)),
        [pltpu.VMEM((2 * chan, 2 * atoms), bf16), pltpu.VMEM((3 * chan, atoms), f32)],
    )
    dhe, p = run(
        "back_second",
        back_second_kernel,
        (m2, dinv, car, hj, w, slope, ub),
        (((2 * chan, edges), bf16), ((4, 8 * slots, atoms), f32)),
    )
    dh, q, ohlo = run(
        "scatter",
        scatter_kernel,
        (oh, pick, dhe, sides, p, gidx),
        (((chan, n_near), f32), ((4 * slots, atoms), f32), ((LANES, slots * n_near), bf16)),
    )
    (da,) = run("back_first", back_first_kernel, (dh, sp1, m1, mixt, rrr), (((ORDERS, 2 * bases, n_near), f32),))
    return run(
        "back_edges",
        functools.partial(back_edge_kernel, plan),
        (*blocks, momenta, geo, y, bk, gidx, da, q, ohlo),
        ((((len(wide) + 1) * lines, LANES), f32), ((len(wide) * lines, LANES), f32)),
        [
            pltpu.VMEM((6 * top_rows, slots * n_near), bf16),
            pltpu.VMEM((3, slots, n_near), f32),
            pltpu.VMEM(momenta.shape, f32),
            pltpu.SemaphoreType.DMA(()),
        ],
        (len(blocks),),
    )


def line_count(atoms):
    return -(-3 * (atoms // LANES) // 8) * 8


def ring_plan(domains, atoms):
    near = list(dict.fromkeys(o % domains for o in (0, 1, -1)))
    wide = list(dict.fromkeys(near + [o % domains for o in (2, -2)]))
    before = tuple(wide.index((o - 1) % domains) for o in near)
    after = tuple(wide.index((o + 1) % domains) for o in near)
    return atoms, tuple(near), tuple(wide), before, after


def mode_turns(bead_total):
    bead = np.arange(bead_total, dtype=np.float64)[:, None]
    mode = np.arange(bead_total, dtype=np.float64)[None, :]
    phase = 2.0 * np.pi * bead * mode / bead_total
    half_total = bead_total // 2
    table = math.sqrt(2.0 / bead_total) * np.where(mode < half_total, np.cos(phase), np.sin(phase))
    table = np.where(mode == half_total, np.cos(np.pi * bead) / math.sqrt(bead_total), table)
    table = np.where(mode == 0, 1.0 / math.sqrt(bead_total), table)
    angles = bead_total * np.sin(np.pi * mode[0] / bead_total)
    safe = np.where(mode[0] == 0, 1.0, angles)
    reach = np.where(mode[0] == 0, STEP, STEP * np.sin(angles) / safe)
    stiff = angles * np.sin(angles) / STEP
    return [[float(x) for x in (table * factor[None, :]) @ table[0]] for factor in (np.cos(angles), reach, stiff)]


def pack_kernel(coord_src, species_src, send_src, slot_src, block_ref, coord_ref, species_ref, send_ref, slot_ref, sems):
    pairs = ((coord_src, coord_ref), (species_src, species_ref), (send_src, send_ref), (slot_src, slot_ref))
    fetches = [pltpu.make_async_copy(src, dst, sems.at[i]) for i, (src, dst) in enumerate(pairs)]
    for fetch in fetches:
        fetch.start()
    for fetch in fetches:
        fetch.wait()
    atoms = block_ref.shape[1]
    for i in range(3):
        block_ref[i : i + 1, :] = coord_ref[i]
    block_ref[3:4, :] = species_ref[...].astype(f32)
    block_ref[4:5, :] = send_ref[...].astype(f32)
    block_ref[5:HEAD, :] = jnp.zeros((HEAD - 5, atoms), f32)
    block_ref[HEAD:, :] = slot_ref[...].astype(f32)


def turn_kernel(shape, bead_ref, domain_ref, mass_ref, *refs):
    outer, inner, domains, wide = shape
    message_ref = refs[outer]
    turns = mode_turns(outer * inner)
    lines = mass_ref.shape[0] // len(wide)
    my_domain = domain_ref[0]
    my_inner = lax.rem(bead_ref[0], inner)
    if domains > len(wide):
        message_ref[...] = jnp.zeros_like(message_ref)
    masses = [mass_ref[g * lines : (g + 1) * lines, :] for g in range(len(wide))]
    sources = []
    for z in range(outer):
        sources.append([refs[z][g * lines : (g + 1) * lines, :] for g in range(len(wide) + 1)])
    for s in range(inner):
        wraps = jnp.full((lines, LANES), my_inner + s) >= inner
        weights = []
        for turn in turns:
            row_of = []
            for z in range(outer):
                there = turn[(z * inner + s) % (outer * inner)]
                round_it = turn[(z * inner + s - inner) % (outer * inner)]
                row_of.append(jnp.where(wraps, jnp.full((lines, LANES), round_it), jnp.full((lines, LANES), there)))
            weights.append(row_of)
        to_inner = lax.rem(my_inner + s, inner)
        for g in range(len(wide)):
            turned = sum(weights[0][z] * sources[z][1 + g] for z in range(outer))
            drift = sum(weights[1][z] * sources[z][1 + g] for z in range(outer))
            new_q = drift / masses[g]
            new_p = turned
            if g == 0:
                new_q = new_q + sum(weights[0][z] * sources[z][0] for z in range(outer))
                new_p = new_p - masses[g] * sum(weights[2][z] * sources[z][0] for z in range(outer))
            to = to_inner * domains + lax.rem(my_domain + wide[g], domains)
            message_ref[to, 0:lines, :] = new_q
            message_ref[to, lines:, :] = new_p


def sum_kernel(arrived_ref, q_ref, p_ref):
    total = arrived_ref[0]
    for i in range(1, arrived_ref.shape[0]):
        total = total + arrived_ref[i]
    lines = total.shape[0] // 2
    tiles = q_ref.shape[2] // LANES
    for i in range(3):
        for t in range(tiles):
            at = i * tiles + t
            q_ref[i, :, t * LANES : (t + 1) * LANES] = total[at : at + 1]
            p_ref[i, :, t * LANES : (t + 1) * LANES] = total[lines + at : lines + at + 1]


def shards(
    positions, momenta, species, neighbours, send_list, embedding, radial_one, radial_two, mix_one, mix_two,
    read_one, read_two,
):
    slots, atoms = neighbours.shape
    domains = lax.axis_size("space")
    beads = lax.axis_size("bead")
    inner = next(d for d in range(1, beads + 1) if beads % d == 0 and d * d >= beads)
    outer = beads // inner
    plan = ring_plan(domains, atoms)
    wide = plan[2]
    vmem = pl.BlockSpec(memory_space=pltpu.VMEM)
    smem = pl.BlockSpec(memory_space=pltpu.SMEM)
    far = pl.BlockSpec(memory_space=pltpu.HBM)
    small = pltpu.CompilerParams(vmem_limit_bytes=4 * MIB)
    coord_rows = jnp.transpose(positions, (1, 0, 2))
    moment_rows = jnp.transpose(momenta, (1, 0, 2))
    block = pl.pallas_call(
        pack_kernel,
        out_shape=jax.ShapeDtypeStruct((HEAD + slots, atoms), f32),
        in_specs=[far] * 4,
        out_specs=vmem,
        scratch_shapes=[
            pltpu.VMEM(coord_rows.shape, f32),
            pltpu.VMEM((1, atoms), jnp.int32),
            pltpu.VMEM((1, atoms), jnp.int32),
            pltpu.VMEM((slots, atoms), jnp.int32),
            pltpu.SemaphoreType.DMA((4,)),
        ],
        compiler_params=small,
        name="pack",
    )(in_hbm(coord_rows), in_hbm(species[None]), in_hbm(send_list[None]), in_hbm(neighbours))
    blocks = [block]
    for offset in wide[1:]:
        blocks.append(lax.ppermute(block, "space", [(i, (i - offset) % domains) for i in range(domains)]))
    chosen = choose(block, embedding, radial_one, radial_two, mix_one, mix_two, read_one, read_two)
    pushed, masses = pushes(plan, blocks, moment_rows, chosen)
    sources = [pushed]
    for z in range(1, outer):
        sources.append(lax.ppermute(pushed, "bead", [(b, (b + z * inner) % beads) for b in range(beads)]))
    here = [lax.axis_index(axis).astype(jnp.int32).reshape(1) for axis in ("bead", "space")]
    lines = line_count(atoms)
    messages = pl.pallas_call(
        functools.partial(turn_kernel, (outer, inner, domains, wide)),
        out_shape=jax.ShapeDtypeStruct((inner * domains, 2 * lines, LANES), f32),
        in_specs=[smem, smem, vmem] + [vmem] * outer,
        out_specs=vmem,
        compiler_params=small,
        name="turn",
    )(*here, masses, *sources)
    rows = [[z * inner * domains + i for i in range(inner * domains)] for z in range(outer)]
    arrived = lax.all_to_all(messages, ("bead", "space"), 0, 0, axis_index_groups=rows, tiled=True)
    new_q, new_p = pl.pallas_call(
        sum_kernel,
        out_shape=(jax.ShapeDtypeStruct((3, 1, atoms), f32),) * 2,
        in_specs=[vmem],
        out_specs=(vmem, vmem),
        compiler_params=small,
        name="sum",
    )(arrived)
    return (jnp.transpose(new_q, (1, 0, 2)), jnp.transpose(new_p, (1, 0, 2)))


def solution(mesh):
    placed = (
        P("bead", None, "space"),
        P("bead", None, "space"),
        P("space"),
        P(None, "space"),
        P("space"),
        P(),
        P(),
        P(),
        P(),
        P(),
        P(),
        P(),
    )
    return jax.shard_map(
        shards,
        mesh=mesh,
        in_specs=placed,
        out_specs=(P("bead", None, "space"), P("bead", None, "space")),
        check_vma=False,
    )
```

```python
import functools
import math

import jax
import jax.numpy as jnp
import numpy as np
from jax import lax
from jax.experimental import pallas as pl
from jax.experimental.pallas import tpu as pltpu
from jax.sharding import PartitionSpec as P

STEP = 2.0
HALF_STEP = 1.0
HEAVY = 16.0
SQRT3 = math.sqrt(3.0)
SQRT5 = math.sqrt(5.0)
SQRT15 = math.sqrt(15.0)
LANES = 128
ORDERS = 9
GROUP = (0, 1, 1, 1, 2, 2, 2, 2, 2)
HEAD = 8
MIB = 1024 * 1024
f32 = jnp.float32
bf16 = jnp.bfloat16


def split(x):
    hi = x.astype(bf16)
    return hi, (x - hi.astype(f32)).astype(bf16)


def split_rows(x):
    hi = x.astype(bf16).astype(f32)
    return jnp.concatenate([hi, x - hi], axis=0)


def split3(x):
    hi = x.astype(bf16)
    rest = x - hi.astype(f32)
    mid = rest.astype(bf16)
    return hi, mid, (rest - mid.astype(f32)).astype(bf16)


def six_rows(x, order):
    hi = x.astype(bf16).astype(f32)
    mid = (x - hi).astype(bf16).astype(f32)
    parts = (hi, mid, x - hi - mid)
    return jnp.concatenate([parts[i] for i in order], axis=0)


VALUE_ORDER = (0, 1, 0, 1, 2, 0)
WEIGHT_ORDER = (0, 0, 1, 1, 0, 2)


def dot(a, b):
    return jnp.dot(a, b, preferred_element_type=f32)


def dot_nt(a, b):
    return lax.dot_general(a, b, (((1,), (1,)), ((), ())), preferred_element_type=f32)


def in_turns(start, stop, step, most=4):
    per_turn = next(n for n in range(most, 0, -1) if (stop - start) % n == 0)

    def turn(i, carry):
        for j in range(per_turn):
            step(start + i * per_turn + j)
        return carry

    lax.fori_loop(0, (stop - start) // per_turn, turn, 0)


def row(x, rows=8):
    return jnp.broadcast_to(x, (rows, x.shape[1]))


def lookup(chunks, wanted, position):
    out = None
    for number, chunk in chunks:
        got = jnp.take_along_axis(row(chunk), position, axis=1, mode="promise_in_bounds")
        out = got if out is None else jnp.where(wanted == number, got, out)
    return out


def harmonics(ux, uy, uz):
    return [
        None,
        SQRT3 * ux,
        SQRT3 * uy,
        SQRT3 * uz,
        SQRT15 * ux * uy,
        SQRT15 * uy * uz,
        0.5 * SQRT5 * (2.0 * uz * uz - ux * ux - uy * uy),
        SQRT15 * ux * uz,
        0.5 * SQRT15 * (ux * ux - uy * uy),
    ]


def silu_parts(v):
    gate = 1.0 / (1.0 + jnp.exp(-v))
    return v * gate, gate * (1.0 + v * (1.0 - gate))


def choose_kernel(block_ref, *refs):
    sources = refs[:7]
    oh_ref, rrc_ref, r2c_ref, side_ref, rrr_ref, mixa_ref, mixt_ref = refs[7:14]
    held = refs[14:21]
    sems = refs[21]
    emb_ref, rad1_ref, rad2_ref, mix1_ref, mix2_ref, read1_ref, read2_ref = held
    fetches = [pltpu.make_async_copy(src, dst, sems.at[i]) for i, (src, dst) in enumerate(zip(sources, held))]
    for fetch in fetches:
        fetch.start()
    chan = emb_ref.shape[1]
    bases = rad1_ref.shape[0]
    atoms = block_ref.shape[1]
    slots = block_ref.shape[0] - HEAD

    ids16 = lax.broadcasted_iota(jnp.int32, (LANES, atoms), 0).astype(jnp.int16)
    one16 = jnp.ones((LANES, atoms), bf16)
    zero16 = jnp.zeros((LANES, atoms), bf16)
    for k in range(slots):
        slot = block_ref[HEAD + k : HEAD + k + 1, :].astype(jnp.int32)
        wanted = jnp.broadcast_to(slot, (LANES, atoms)).astype(jnp.int16)
        for r in range(oh_ref.shape[0] // LANES):
            hit = wanted - jnp.int16(r * LANES) == ids16
            oh_ref[r * LANES : (r + 1) * LANES, k * atoms : (k + 1) * atoms] = jnp.where(hit, one16, zero16)

    for fetch in fetches:
        fetch.wait()
    emb0 = emb_ref[0:1, :]
    emb_d = emb_ref[1:2, :] - emb0
    rr = jnp.concatenate([rad1_ref[...] * emb0, rad1_ref[...] * emb_d], axis=0) * (1.0 / slots)
    rr_hi = rr.astype(bf16).astype(f32)
    rr_lo = rr - rr_hi
    r2 = rad2_ref[...] * (1.0 / slots)
    zeros = jnp.zeros((8, chan), f32)
    turned1 = jnp.concatenate([six_rows(rr, WEIGHT_ORDER)] + [zeros] * (16 - 12 * bases // 8), axis=0).T
    sides = jnp.concatenate([emb0, emb_d, read1_ref[...], read2_ref[...], zeros[:4]], axis=0)
    turned2 = jnp.concatenate([six_rows(r2, WEIGHT_ORDER)] + [zeros] * (16 - 6 * bases // 8), axis=0).T
    rrc_ref[...] = turned1[:, : 12 * bases].astype(bf16)
    r2c_ref[...] = turned2[:, : 6 * bases].astype(bf16)
    side_ref[...] = jnp.concatenate([sides] + [zeros] * 15, axis=0).T
    rrr_ref[...] = jnp.concatenate(
        [jnp.concatenate([rr_hi, rr_hi], axis=1), jnp.concatenate([rr_lo, jnp.zeros_like(rr_lo)], axis=1)], axis=0
    ).astype(bf16)
    for i, ref in enumerate((mix1_ref, mix2_ref)):
        for part, value in enumerate(split3(ref[...])):
            mixa_ref[i, part * chan : (part + 1) * chan, :] = value
        for g in range(3):
            hi, lo = split(ref[:, g * chan : (g + 1) * chan].T)
            mixt_ref[i, g, 0:chan, :] = hi
            mixt_ref[i, g, chan:, :] = lo


def dot_parts(both, hi, lo):
    rows = both.shape[0] // 2
    first = dot(both, hi)
    return first[:rows] + first[rows:] + dot(both[:rows], lo)


def dot_three(parts, hi, mid, lo):
    rows = parts.shape[0] // 3
    first = dot(parts, hi)
    second = dot(parts[: 2 * rows], mid)
    third = dot(parts[:rows], lo)
    return first[:rows] + (first[rows : 2 * rows] + second[:rows]) + (first[2 * rows :] + second[rows:] + third)


def edge_kernel(plan, *refs):
    atoms, near, wide, before, after = plan
    n_wide = len(wide)
    blocks = refs[:n_wide]
    geo_ref, y_ref, yb_ref, ub_ref, bk_ref, bt_ref, gidx_ref, pick_ref, as_ref = refs[n_wide:]
    bases = bk_ref.shape[0]
    slots = gidx_ref.shape[0]
    tiles = atoms // LANES
    half = atoms // 2
    half_tiles = half // LANES
    order_col = lax.broadcasted_iota(jnp.int32, (bases, LANES), 0).astype(f32)
    tables = []
    for quantity in range(4):
        chunks = []
        for g in range(n_wide):
            for t in range(tiles):
                chunks.append((g * tiles + t, blocks[g][quantity : quantity + 1, t * LANES : (t + 1) * LANES]))
        tables.append(chunks)
    for q in range(len(near)):
        ghosts = []
        for t in range(half_tiles):
            ghosts.append(
                (t, blocks[before[q]][4:5, half + t * LANES : half + (t + 1) * LANES] + float(before[q] * atoms))
            )
        for t in range(half_tiles):
            ghosts.append(
                (
                    half_tiles + tiles + t,
                    blocks[after[q]][4:5, t * LANES : (t + 1) * LANES] + float(after[q] * atoms),
                )
            )
        if q == 0:
            ids16 = lax.broadcasted_iota(jnp.int32, (pick_ref.shape[0], LANES), 0).astype(jnp.int16)
            one16 = jnp.ones(ids16.shape, bf16)
            zero16 = jnp.zeros(ids16.shape, bf16)
            for t, (_, chunk) in enumerate(ghosts):
                wanted = jnp.broadcast_to(chunk.astype(jnp.int32), ids16.shape).astype(jnp.int16)
                pick_ref[:, t * LANES : (t + 1) * LANES] = jnp.where(wanted == ids16, one16, zero16)
        for t in range(tiles):
            cols = slice(t * LANES, (t + 1) * LANES)
            here = slice(q * atoms + t * LANES, q * atoms + (t + 1) * LANES)
            slot = blocks[q][HEAD : HEAD + slots, cols].astype(jnp.int32)
            chunk_no = slot >> 7
            far = lookup(ghosts, chunk_no, slot & 127).astype(jnp.int32)
            own = (slot >= half) & (slot < half + atoms)
            gidx = jnp.where(own, slot + (q * atoms - half), far)
            gidx_ref[:, here] = gidx
            chunk_no = gidx >> 7
            place = gidx & 127
            xj, yj, zj, fj = [lookup(tables[i], chunk_no, place) for i in range(4)]
            rx = xj - row(blocks[q][0:1, cols])
            ry = yj - row(blocks[q][1:2, cols])
            rz = zj - row(blocks[q][2:3, cols])
            soft = jnp.sqrt(rx * rx + ry * ry + rz * rz + 1.0)
            back = 1.0 / soft
            ux, uy, uz = rx * back, ry * back, rz * back
            for i, value in enumerate((ux, uy, uz, back, soft, fj)):
                geo_ref[i, :, here] = value
            if q == 0:
                for i, value in enumerate((ux, uy, uz)):
                    for k in range(slots):
                        ub_ref[i, k, :, cols] = row(value[k : k + 1, :])
            sphere = harmonics(ux, uy, uz)
            for l in range(1, ORDERS):
                y_ref[l - 1, :, here] = sphere[l]
                if q == 0:
                    for k in range(slots):
                        yb_ref[l - 1, k, :, cols] = row(sphere[l][k : k + 1, :])
            for n in range(bases):
                bk_ref[n, :, here] = jnp.exp(-0.5 * (soft - (1.0 + n)) ** 2)
            for k in range(slots):
                basis = jnp.exp(-0.5 * (row(soft[k : k + 1, :], bases) - (1.0 + order_col)) ** 2)
                bt_ref[k, 0:bases, here] = basis
                bt_ref[k, bases : 2 * bases, here] = basis * row(fj[k : k + 1, :], bases)
            low = [None] * ORDERS
            for k in range(slots):
                basis = bt_ref[k, :, here]
                for l in range(ORDERS):
                    term = basis if l == 0 else basis * row(y_ref[l - 1, k : k + 1, here], 2 * bases)
                    low[l] = term if low[l] is None else low[l] + term
            for l in range(ORDERS):
                as_ref[l, :, here] = six_rows(low[l], VALUE_ORDER).astype(bf16)


def first_kernel(plan, *refs):
    atoms, near, wide, _, _ = plan
    n_wide = len(wide)
    blocks = refs[:n_wide]
    as_ref, rrc_ref, side_ref, mixa_ref, m1_ref, sp1_ref, hid_ref, hs_ref, flag_ref = refs[n_wide:]
    chan = m1_ref.shape[1]
    n_near = m1_ref.shape[2]

    for q in range(len(near)):
        flag_ref[0:1, q * atoms : (q + 1) * atoms] = blocks[q][3:4, :]
    wide_cols = 2 * LANES
    emb0_col = side_ref[:, 0:1]
    embd_col = side_ref[:, 1:2]

    def first(j):
        here = pl.ds(pl.multiple_of(j * wide_cols, wide_cols), wide_cols)
        inv = [None, None, None]
        for l in range(ORDERS):
            m = dot(rrc_ref[...], as_ref[l, :, here])
            m1_ref[l, :, here] = m
            inv[GROUP[l]] = m * m if inv[GROUP[l]] is None else inv[GROUP[l]] + m * m
        value = dot_three(mixa_ref[0], *split3(jnp.concatenate(inv, axis=0)))
        act, slope = silu_parts(value)
        sp1_ref[:, here] = slope
        hidden = act + emb0_col + embd_col * flag_ref[0:1, here]
        hid_ref[:, here] = hidden
        for part, piece in enumerate(split3(hidden)):
            hs_ref[part * chan : (part + 1) * chan, here] = piece

    in_turns(0, n_near // wide_cols, first)


def gather_kernel(hid_ref, hs_ref, oh_ref, pick_ref, gidx_ref, bt_ref, geo_ref, r2c_ref,
                  hj_ref, w_ref, slope_ref, car_ref, ext_ref):
    slots = bt_ref.shape[0]
    bases = bt_ref.shape[1] // 2
    chan, n_near = hid_ref.shape
    atoms = hj_ref.shape[1] // slots
    half = atoms // 2
    ghosts = dot(hs_ref[...], pick_ref[...]).astype(bf16)
    ext_ref[:, 0:half] = ghosts[:, :half]
    ext_ref[:, half : half + atoms] = hs_ref[:, 0:atoms]
    ext_ref[:, half + atoms :] = ghosts[:, half:]
    reach = 1.0 + lax.broadcasted_iota(jnp.int32, (bases, atoms), 0).astype(f32)
    for k in range(slots):
        here = slice(k * atoms, (k + 1) * atoms)
        basis = bt_ref[k, 0:bases, 0:atoms]
        for ref, value in ((w_ref, basis), (slope_ref, basis * (reach - row(geo_ref[4, k : k + 1, 0:atoms], bases)))):
            ref[:, here] = dot(r2c_ref[...], six_rows(value, VALUE_ORDER).astype(bf16))

    for pair in range(slots // 2):
        by_lane = (2 + 2 * (pair % 2)) * LANES if atoms >= 4 * LANES else 0
        by_product = 2 * atoms - by_lane
        first = pair * 2 * atoms
        here = slice(first, first + by_product)
        both = dot(ext_ref[...], oh_ref[:, here])
        wanted = gidx_ref[2 * pair + 1 : 2 * pair + 2, 0:atoms]
        for t in range(by_lane // LANES):
            at = slice(first + by_product + t * LANES, first + by_product + (t + 1) * LANES)
            start = atoms - by_lane + t * LANES
            mine = row(wanted[:, start : start + LANES])
            chunk_no = mine >> 7
            place = mine & 127
            for c in range(chan // 8):
                rows = slice(8 * c, 8 * c + 8)
                feat = None
                for chunk in range(n_near // LANES):
                    held = hid_ref[rows, chunk * LANES : (chunk + 1) * LANES]
                    got = jnp.take_along_axis(held, place, axis=1, mode="promise_in_bounds")
                    feat = got if feat is None else jnp.where(chunk_no == chunk, got, feat)
                hj_ref[rows, at] = feat
                car_ref[rows, at] = feat * w_ref[rows, at]
        feat = both[:chan] + (both[chan : 2 * chan] + both[2 * chan :])
        hj_ref[:, here] = feat
        car_ref[:, here] = feat * w_ref[:, here]


def moment_kernel(car_ref, yb_ref, mixa_ref, mixt_ref, side_ref, m2_ref, dinv_ref, inv_ref):
    slots = yb_ref.shape[1]
    chan, atoms = m2_ref.shape[1:]
    tiles = atoms // LANES
    wide_cols = 2 * LANES
    rows = 32
    groups = chan // rows

    def moments(step):
        t = step // groups
        c = step % groups
        cols = pl.ds(pl.multiple_of(t * LANES, LANES), LANES)
        base = pl.multiple_of(c * rows, rows)
        acc = [[None] * ORDERS for _ in range(rows // 8)]
        for k in range(slots):
            at = pl.ds(pl.multiple_of(k * atoms + t * LANES, LANES), LANES)
            got = car_ref[pl.ds(base, rows), at]
            for l in range(ORDERS):
                yb = yb_ref[l - 1, k, :, cols] if l else None
                for h in range(rows // 8):
                    part = got[8 * h : 8 * h + 8]
                    term = part * yb if l else part
                    acc[h][l] = term if acc[h][l] is None else acc[h][l] + term
        for h in range(rows // 8):
            inv = [None] * 3
            for l in range(ORDERS):
                m2_ref[l, pl.ds(pl.multiple_of(base + 8 * h, 8), 8), cols] = acc[h][l]
                sq = acc[h][l] * acc[h][l]
                g = GROUP[l]
                inv[g] = sq if inv[g] is None else inv[g] + sq
            for g in range(3):
                inv_ref[pl.ds(pl.multiple_of(g * chan + base + 8 * h, 8), 8), cols] = inv[g]

    in_turns(0, tiles * groups, moments, 2)
    read2_col = side_ref[:, 3:4]
    for t in range(atoms // wide_cols):
        cols = slice(t * wide_cols, (t + 1) * wide_cols)
        _, slope = silu_parts(dot_three(mixa_ref[1], *split3(inv_ref[:, cols])))
        hi, lo = split(slope * (2.0 * read2_col))
        for g, scale in enumerate((1.0, 0.5 * SQRT3, 0.5 * SQRT15)):
            dinv_ref[g * chan : (g + 1) * chan, cols] = scale * dot_parts(mixt_ref[1, g], hi, lo)


def back_second_kernel(m2_ref, dinv_ref, car_ref, hj_ref, w_ref, slope_ref, ub_ref, dhe_ref, p_ref):
    slots = ub_ref.shape[1]
    chan, atoms = m2_ref.shape[1:]
    tiles = atoms // LANES
    pairs = chan // 16
    per_turn = 4 if pairs % 4 == 0 else 1
    k_step = slots // 2

    def back_moments(t, carry):
        cols = pl.ds(pl.multiple_of(t * LANES, LANES), LANES)

        def one(c, acc, k0):
            forms = []
            for h in range(2):
                rows = pl.ds(pl.multiple_of(c * 16 + 8 * h, 8), 8)
                scale = [dinv_ref[pl.ds(pl.multiple_of(g * chan + c * 16 + 8 * h, 8), 8), cols] for g in range(3)]
                dm = [m2_ref[l, rows, cols] * scale[GROUP[l]] for l in range(ORDERS)]
                low = dm[6] * (1.0 / SQRT3)
                forms.append((dm[0], dm[1], dm[2], dm[3], dm[8] - low, -dm[8] - low, low + low, dm[4], dm[5], dm[7]))
            base = pl.multiple_of(c * 16, 16)
            for k in range(k0, k0 + k_step):
                at = pl.ds(pl.multiple_of(k * atoms + t * LANES, LANES), LANES)
                got = car_ref[pl.ds(base, 16), at]
                stretch = hj_ref[pl.ds(base, 16), at] * slope_ref[pl.ds(base, 16), at]
                ux, uy, uz = [ub_ref[i, k, :, cols] for i in range(3)]
                out = []
                for h in range(2):
                    mid, dx, dy, dz, qxx, qyy, qzz, qxy, qyz, qxz = forms[h]
                    gx = dx + qxx * ux + qxy * uy + qxz * uz
                    gy = dy + qxy * ux + qyy * uy + qyz * uz
                    gz = dz + qxz * ux + qyz * uy + qzz * uz
                    out.append(mid + (gx + dx) * ux + (gy + dy) * uy + (gz + dz) * uz)
                    part = got[8 * h : 8 * h + 8]
                    at_acc = 4 * (k - k0)
                    for i, g in enumerate((gx, gy, gz)):
                        acc[at_acc + i] = acc[at_acc + i] + part * g
                    acc[at_acc + 3] = acc[at_acc + 3] + out[h] * stretch[8 * h : 8 * h + 8]
                hi, lo = split(jnp.concatenate(out, axis=0) * w_ref[pl.ds(base, 16), at])
                dhe_ref[pl.ds(base, 16), at] = hi
                dhe_ref[pl.ds(pl.multiple_of(chan + c * 16, 16), 16), at] = lo

        for k0 in range(0, slots, k_step):

            def over(c, acc, k0=k0):
                acc = list(acc)
                for i in range(per_turn):
                    one(per_turn * c + i, acc, k0)
                return tuple(acc)

            start = tuple(jnp.zeros((8, LANES), f32) for _ in range(4 * k_step))
            acc = lax.fori_loop(0, pairs // per_turn, over, start)
            for k in range(k_step):
                for i in range(4):
                    p_ref[i, 8 * (k0 + k) : 8 * (k0 + k) + 8, cols] = acc[4 * k + i]
        return carry

    lax.fori_loop(0, tiles, back_moments, 0)


def scatter_kernel(oh_ref, pick_ref, dhe_ref, side_ref, p_ref, gidx_ref, dh_ref, q_ref, ohlo_ref):
    chan, n_near = dh_ref.shape
    slots = gidx_ref.shape[0]
    atoms = pick_ref.shape[1]
    half = atoms // 2
    both = dot_nt(dhe_ref[...], jnp.concatenate([oh_ref[:half], oh_ref[half + atoms :]], axis=0))
    hi, lo = split(both[:chan] + both[chan:])
    spread = dot_nt(jnp.concatenate([hi, lo], axis=0), pick_ref[...])
    spread = spread[:chan] + spread[chan:]
    both = dot_nt(dhe_ref[...], oh_ref[half : half + atoms])
    dh_ref[:, 0:atoms] = spread[:, :atoms] + both[:chan] + both[chan:] + side_ref[:, 2:3]
    if n_near > atoms:
        dh_ref[:, atoms:] = spread[:, atoms:]
    ids16 = lax.broadcasted_iota(jnp.int32, (LANES, n_near), 0).astype(jnp.int16)
    one16 = jnp.ones((LANES, n_near), bf16)
    zero16 = jnp.zeros((LANES, n_near), bf16)
    for k in range(slots):
        place = jnp.broadcast_to(gidx_ref[k : k + 1, :] & 127, (LANES, n_near)).astype(jnp.int16)
        ohlo_ref[:, k * n_near : (k + 1) * n_near] = jnp.where(place == ids16, one16, zero16)
    lane = lax.broadcasted_iota(jnp.int32, (slots, 16 * slots), 1)
    sub = lax.broadcasted_iota(jnp.int32, (slots, 16 * slots), 0)
    adder = jnp.where(((lane >> 3) & (slots - 1)) == sub, 1.0, 0.0).astype(bf16)
    for i in range(4):
        total = dot(adder, split_rows(p_ref[i]).astype(bf16))
        q_ref[8 * i : 8 * i + 8, :] = 2.0 * total if i < 3 else total


def back_first_kernel(dh_ref, sp1_ref, m1_ref, mixt_ref, rrr_ref, da_ref):
    n_near = sp1_ref.shape[1]
    rows = rrr_ref.shape[0] // 2
    wide_cols = 2 * LANES

    def back_first(j):
        here = pl.ds(pl.multiple_of(j * wide_cols, wide_cols), wide_cols)
        hi, lo = split(dh_ref[:, here] * sp1_ref[:, here] * 2.0)
        scale = [dot_parts(mixt_ref[0, g], hi, lo) for g in range(3)]
        for l in range(ORDERS):
            hi, lo = split(m1_ref[l, :, here] * scale[GROUP[l]])
            out = dot(rrr_ref[...], jnp.concatenate([hi, lo], axis=0))
            da_ref[l, :, here] = out[:rows] + out[rows:]

    in_turns(0, n_near // wide_cols, back_first)


def back_edge_kernel(plan, *refs):
    atoms, near, wide, _, _ = plan
    n_wide = len(wide)
    blocks = refs[:n_wide]
    moment_src, geo_ref, y_ref, bk_ref, gidx_ref, da_ref, q_ref, ohlo_ref = refs[n_wide : n_wide + 8]
    push_ref, mass_ref, val_ref, dr_ref, moment_ref, sem = refs[n_wide + 8 :]
    fetch = pltpu.make_async_copy(moment_src, moment_ref, sem)
    fetch.start()
    bases, slots, n_near = bk_ref.shape
    tiles = atoms // LANES
    top_rows = val_ref.shape[0] // 6

    def back_geometry(t, mine):
        here = pl.ds(pl.multiple_of(t * LANES, LANES), LANES)
        ux, uy, uz, back, soft, fj = [geo_ref[i, :, here] for i in range(6)]
        dy = [None] * ORDERS
        ds = None
        for n in range(bases):
            basis = bk_ref[n, :, here]
            db = None
            for l in range(ORDERS):
                g = row(da_ref[l, n : n + 1, here]) + fj * row(da_ref[l, bases + n : bases + n + 1, here])
                if l:
                    dy[l] = g * basis if dy[l] is None else dy[l] + g * basis
                    db = db + g * y_ref[l - 1, :, here]
                else:
                    db = g
            db = db * basis * ((1.0 + n) - soft)
            ds = db if ds is None else ds + db
        if mine:
            ds = ds + q_ref[24:32, here]
        dux = SQRT3 * dy[1] + SQRT15 * (uy * dy[4] + uz * dy[7] + ux * dy[8]) - SQRT5 * ux * dy[6]
        duy = SQRT3 * dy[2] + SQRT15 * (ux * dy[4] + uz * dy[5] - uy * dy[8]) - SQRT5 * uy * dy[6]
        duz = SQRT3 * dy[3] + SQRT15 * (uy * dy[5] + ux * dy[7]) + 2.0 * SQRT5 * uz * dy[6]
        if mine:
            dux, duy, duz = [d + q_ref[8 * i : 8 * i + 8, here] for i, d in enumerate((dux, duy, duz))]
        along = ds - (ux * dux + uy * duy + uz * duz) * back
        for i, value in enumerate((dux * back + along * ux, duy * back + along * uy, duz * back + along * uz)):
            dr_ref[i, :, here] = value

    in_turns(0, tiles, lambda t: back_geometry(t, True))
    in_turns(tiles, n_near // LANES, lambda t: back_geometry(t, False))

    def place_tile(t):
        here = pl.ds(pl.multiple_of(t * LANES, LANES), LANES)
        gidx = gidx_ref[:, here]
        chunk_no = gidx >> 7
        parts = []
        for i in range(3):
            value = dr_ref[i, :, here]
            hi = value.astype(bf16).astype(f32)
            parts.append((hi, value - hi))
        chunk_ids = lax.broadcasted_iota(jnp.int32, (top_rows, LANES), 0)
        for k in range(slots):
            at = pl.ds(pl.multiple_of(k * n_near + t * LANES, LANES), LANES)
            hit = chunk_ids == row(chunk_no[k : k + 1, :], top_rows)
            for i in range(3):
                both = [jnp.where(hit, row(part[k : k + 1, :], top_rows), 0.0) for part in parts[i]]
                val_ref[2 * i * top_rows : 2 * (i + 1) * top_rows, at] = jnp.concatenate(both, axis=0).astype(bf16)

    in_turns(0, n_near // LANES, place_tile)
    landed = dot_nt(val_ref[...], ohlo_ref[...])
    fetch.wait()
    lines = push_ref.shape[0] // (n_wide + 1)
    for i in range(3):
        total = (
            landed[2 * i * top_rows : (2 * i + 1) * top_rows] + landed[(2 * i + 1) * top_rows : (2 * i + 2) * top_rows]
        )
        for g in range(n_wide):
            for t in range(tiles):
                cols = slice(t * LANES, (t + 1) * LANES)
                line = total[g * tiles + t : g * tiles + t + 1, :]
                if g < len(near):
                    here = slice(g * atoms + t * LANES, g * atoms + (t + 1) * LANES)
                    line = line - jnp.sum(dr_ref[i, :, here], axis=0, keepdims=True)
                line = -HALF_STEP * line
                at = i * tiles + t
                if g == 0:
                    line = line + moment_ref[i, :, cols]
                    push_ref[at : at + 1, :] = blocks[0][i : i + 1, cols]
                push_ref[(1 + g) * lines + at : (1 + g) * lines + at + 1, :] = line
                mass = HEAVY - (HEAVY - 1.0) * blocks[g][3:4, cols]
                mass_ref[g * lines + at : g * lines + at + 1, :] = mass
    if lines > 3 * tiles:
        for g in range(n_wide + 1):
            blank = slice(g * lines + 3 * tiles, (g + 1) * lines)
            push_ref[blank, :] = jnp.zeros((lines - 3 * tiles, LANES), f32)
            if g < n_wide:
                mass_ref[blank, :] = jnp.ones((lines - 3 * tiles, LANES), f32)


def in_hbm(x):
    return pltpu.with_memory_space_constraint(x, pltpu.HBM)


def run(name, body, operands, results, scratch=(), far=(), cost=None):
    sizes = [math.prod(x.shape) * x.dtype.itemsize // 2 for i, x in enumerate(operands) if i not in far]
    sizes += [math.prod(shape) * jnp.dtype(dtype).itemsize for shape, dtype in results]
    sizes += [math.prod(x.shape) * x.dtype.itemsize for x in scratch if x.memory_space == pltpu.VMEM]
    limit = sum(sizes) + 4 * MIB
    specs = [pl.BlockSpec(memory_space=pltpu.HBM if i in far else pltpu.VMEM) for i in range(len(operands))]
    return pl.pallas_call(
        body,
        out_shape=tuple(jax.ShapeDtypeStruct(shape, dtype) for shape, dtype in results),
        in_specs=specs,
        out_specs=tuple(pl.BlockSpec(memory_space=pltpu.VMEM) for _ in results),
        scratch_shapes=list(scratch),
        compiler_params=pltpu.CompilerParams(vmem_limit_bytes=limit),
        cost_estimate=cost,
        name=name,
    )(*[in_hbm(x) if i in far else x for i, x in enumerate(operands)])


def choose(block, embedding, radial_one, radial_two, mix_one, mix_two, read_one, read_two):
    atoms = block.shape[1]
    slots = block.shape[0] - HEAD
    chan = embedding.shape[1]
    bases = radial_one.shape[0]
    weights = (embedding, radial_one, radial_two, mix_one, mix_two, read_one[None], read_two[None])
    return run(
        "choose",
        choose_kernel,
        (block, *weights),
        (
            ((2 * atoms, slots * atoms), bf16),
            ((chan, 12 * bases), bf16),
            ((chan, 6 * bases), bf16),
            ((chan, LANES), f32),
            ((4 * bases, 2 * chan), bf16),
            ((2, 3 * chan, 3 * chan), bf16),
            ((2, 3, 2 * chan, chan), bf16),
        ),
        [pltpu.VMEM(w.shape, f32) for w in weights] + [pltpu.SemaphoreType.DMA((len(weights),))],
        range(1, 1 + len(weights)),
        cost=pl.CostEstimate(flops=2 * 10**9, bytes_accessed=2 * 10**6, transcendentals=0),
    )


def pushes(plan, blocks, momenta, chosen):
    atoms, near, wide, _, _ = plan
    oh, rrc, r2c, sides, rrr, mixa, mixt = chosen
    chan = rrc.shape[0]
    bases = rrr.shape[0] // 4
    slots = blocks[0].shape[0] - HEAD
    n_near = len(near) * atoms
    edges = slots * atoms
    top_rows = -(-len(wide) * atoms // LANES // 8) * 8
    lines = line_count(atoms)
    geo, y, yb, ub, bk, bt, gidx, pick, as1 = run(
        "edges",
        functools.partial(edge_kernel, plan),
        blocks,
        (
            ((6, slots, n_near), f32),
            ((ORDERS - 1, slots, n_near), f32),
            ((ORDERS - 1, slots, 8, atoms), f32),
            ((3, slots, 8, atoms), f32),
            ((bases, slots, n_near), f32),
            ((slots, 2 * bases, n_near), f32),
            ((slots, n_near), jnp.int32),
            ((n_near, atoms), bf16),
            ((ORDERS, 12 * bases, n_near), bf16),
        ),
    )
    m1, sp1, hid, hs = run(
        "first",
        functools.partial(first_kernel, plan),
        (*blocks, as1, rrc, sides, mixa),
        (((ORDERS, chan, n_near), f32), ((chan, n_near), f32), ((chan, n_near), f32), ((3 * chan, n_near), bf16)),
        [pltpu.VMEM((8, n_near), f32)],
    )
    hj, w, slope, car = run(
        "gather",
        gather_kernel,
        (hid, hs, oh, pick, gidx, bt, geo, r2c),
        (((chan, edges), f32),) * 4,
        [pltpu.VMEM((3 * chan, 2 * atoms), bf16)],
    )
    m2, dinv = run(
        "moments",
        moment_kernel,
        (car, yb, mixa, mixt, sides),
        (((ORDERS, chan, atoms), f32), ((3 * chan, atoms), f32)),
        [pltpu.VMEM((3 * chan, atoms), f32)],
    )
    dhe, p = run(
        "back_second",
        back_second_kernel,
        (m2, dinv, car, hj, w, slope, ub),
        (((2 * chan, edges), bf16), ((4, 8 * slots, atoms), f32)),
    )
    dh, q, ohlo = run(
        "scatter",
        scatter_kernel,
        (oh, pick, dhe, sides, p, gidx),
        (((chan, n_near), f32), ((4 * slots, atoms), f32), ((LANES, slots * n_near), bf16)),
    )
    (da,) = run("back_first", back_first_kernel, (dh, sp1, m1, mixt, rrr), (((ORDERS, 2 * bases, n_near), f32),))
    return run(
        "back_edges",
        functools.partial(back_edge_kernel, plan),
        (*blocks, momenta, geo, y, bk, gidx, da, q, ohlo),
        ((((len(wide) + 1) * lines, LANES), f32), ((len(wide) * lines, LANES), f32)),
        [
            pltpu.VMEM((6 * top_rows, slots * n_near), bf16),
            pltpu.VMEM((3, slots, n_near), f32),
            pltpu.VMEM(momenta.shape, f32),
            pltpu.SemaphoreType.DMA(()),
        ],
        (len(blocks),),
    )


def line_count(atoms):
    return -(-3 * (atoms // LANES) // 8) * 8


def ring_plan(domains, atoms):
    near = list(dict.fromkeys(o % domains for o in (0, 1, -1)))
    wide = list(dict.fromkeys(near + [o % domains for o in (2, -2)]))
    before = tuple(wide.index((o - 1) % domains) for o in near)
    after = tuple(wide.index((o + 1) % domains) for o in near)
    return atoms, tuple(near), tuple(wide), before, after


def mode_turns(bead_total):
    bead = np.arange(bead_total, dtype=np.float64)[:, None]
    mode = np.arange(bead_total, dtype=np.float64)[None, :]
    phase = 2.0 * np.pi * bead * mode / bead_total
    half_total = bead_total // 2
    table = math.sqrt(2.0 / bead_total) * np.where(mode < half_total, np.cos(phase), np.sin(phase))
    table = np.where(mode == half_total, np.cos(np.pi * bead) / math.sqrt(bead_total), table)
    table = np.where(mode == 0, 1.0 / math.sqrt(bead_total), table)
    angles = bead_total * np.sin(np.pi * mode[0] / bead_total)
    safe = np.where(mode[0] == 0, 1.0, angles)
    reach = np.where(mode[0] == 0, STEP, STEP * np.sin(angles) / safe)
    stiff = angles * np.sin(angles) / STEP
    return [[float(x) for x in (table * factor[None, :]) @ table[0]] for factor in (np.cos(angles), reach, stiff)]


def pack_kernel(coord_src, species_src, send_src, slot_src, block_ref, coord_ref, species_ref, send_ref, slot_ref, sems):
    pairs = ((coord_src, coord_ref), (species_src, species_ref), (send_src, send_ref), (slot_src, slot_ref))
    fetches = [pltpu.make_async_copy(src, dst, sems.at[i]) for i, (src, dst) in enumerate(pairs)]
    for fetch in fetches:
        fetch.start()
    for fetch in fetches:
        fetch.wait()
    atoms = block_ref.shape[1]
    for i in range(3):
        block_ref[i : i + 1, :] = coord_ref[i]
    block_ref[3:4, :] = species_ref[...].astype(f32)
    block_ref[4:5, :] = send_ref[...].astype(f32)
    block_ref[5:HEAD, :] = jnp.zeros((HEAD - 5, atoms), f32)
    block_ref[HEAD:, :] = slot_ref[...].astype(f32)


def turn_kernel(shape, bead_ref, domain_ref, mass_ref, *refs):
    outer, inner, domains, wide = shape
    message_ref = refs[outer]
    turns = mode_turns(outer * inner)
    lines = mass_ref.shape[0] // len(wide)
    my_domain = domain_ref[0]
    my_inner = lax.rem(bead_ref[0], inner)
    if domains > len(wide):
        message_ref[...] = jnp.zeros_like(message_ref)
    masses = [mass_ref[g * lines : (g + 1) * lines, :] for g in range(len(wide))]
    sources = []
    for z in range(outer):
        sources.append([refs[z][g * lines : (g + 1) * lines, :] for g in range(len(wide) + 1)])
    for s in range(inner):
        wraps = jnp.full((lines, LANES), my_inner + s) >= inner
        weights = []
        for turn in turns:
            row_of = []
            for z in range(outer):
                there = turn[(z * inner + s) % (outer * inner)]
                round_it = turn[(z * inner + s - inner) % (outer * inner)]
                row_of.append(jnp.where(wraps, jnp.full((lines, LANES), round_it), jnp.full((lines, LANES), there)))
            weights.append(row_of)
        to_inner = lax.rem(my_inner + s, inner)
        for g in range(len(wide)):
            turned = sum(weights[0][z] * sources[z][1 + g] for z in range(outer))
            drift = sum(weights[1][z] * sources[z][1 + g] for z in range(outer))
            new_q = drift / masses[g]
            new_p = turned
            if g == 0:
                new_q = new_q + sum(weights[0][z] * sources[z][0] for z in range(outer))
                new_p = new_p - masses[g] * sum(weights[2][z] * sources[z][0] for z in range(outer))
            to = to_inner * domains + lax.rem(my_domain + wide[g], domains)
            message_ref[to, 0:lines, :] = new_q
            message_ref[to, lines:, :] = new_p


def sum_kernel(arrived_ref, q_ref, p_ref):
    total = arrived_ref[0]
    for i in range(1, arrived_ref.shape[0]):
        total = total + arrived_ref[i]
    lines = total.shape[0] // 2
    tiles = q_ref.shape[2] // LANES
    for i in range(3):
        for t in range(tiles):
            at = i * tiles + t
            q_ref[i, :, t * LANES : (t + 1) * LANES] = total[at : at + 1]
            p_ref[i, :, t * LANES : (t + 1) * LANES] = total[lines + at : lines + at + 1]


def shards(
    positions, momenta, species, neighbours, send_list, embedding, radial_one, radial_two, mix_one, mix_two,
    read_one, read_two,
):
    slots, atoms = neighbours.shape
    domains = lax.axis_size("space")
    beads = lax.axis_size("bead")
    inner = next(d for d in range(1, beads + 1) if beads % d == 0 and d * d >= beads)
    outer = beads // inner
    plan = ring_plan(domains, atoms)
    wide = plan[2]
    vmem = pl.BlockSpec(memory_space=pltpu.VMEM)
    smem = pl.BlockSpec(memory_space=pltpu.SMEM)
    far = pl.BlockSpec(memory_space=pltpu.HBM)
    small = pltpu.CompilerParams(vmem_limit_bytes=4 * MIB)
    coord_rows = jnp.transpose(positions, (1, 0, 2))
    moment_rows = jnp.transpose(momenta, (1, 0, 2))
    block = pl.pallas_call(
        pack_kernel,
        out_shape=jax.ShapeDtypeStruct((HEAD + slots, atoms), f32),
        in_specs=[far] * 4,
        out_specs=vmem,
        scratch_shapes=[
            pltpu.VMEM(coord_rows.shape, f32),
            pltpu.VMEM((1, atoms), jnp.int32),
            pltpu.VMEM((1, atoms), jnp.int32),
            pltpu.VMEM((slots, atoms), jnp.int32),
            pltpu.SemaphoreType.DMA((4,)),
        ],
        compiler_params=small,
        name="pack",
    )(in_hbm(coord_rows), in_hbm(species[None]), in_hbm(send_list[None]), in_hbm(neighbours))
    blocks = [block]
    for offset in wide[1:]:
        blocks.append(lax.ppermute(block, "space", [(i, (i - offset) % domains) for i in range(domains)]))
    chosen = choose(block, embedding, radial_one, radial_two, mix_one, mix_two, read_one, read_two)
    pushed, masses = pushes(plan, blocks, moment_rows, chosen)
    sources = [pushed]
    for z in range(1, outer):
        sources.append(lax.ppermute(pushed, "bead", [(b, (b + z * inner) % beads) for b in range(beads)]))
    here = [lax.axis_index(axis).astype(jnp.int32).reshape(1) for axis in ("bead", "space")]
    lines = line_count(atoms)
    messages = pl.pallas_call(
        functools.partial(turn_kernel, (outer, inner, domains, wide)),
        out_shape=jax.ShapeDtypeStruct((inner * domains, 2 * lines, LANES), f32),
        in_specs=[smem, smem, vmem] + [vmem] * outer,
        out_specs=vmem,
        compiler_params=small,
        name="turn",
    )(*here, masses, *sources)
    rows = [[z * inner * domains + i for i in range(inner * domains)] for z in range(outer)]
    arrived = lax.all_to_all(messages, ("bead", "space"), 0, 0, axis_index_groups=rows, tiled=True)
    new_q, new_p = pl.pallas_call(
        sum_kernel,
        out_shape=(jax.ShapeDtypeStruct((3, 1, atoms), f32),) * 2,
        in_specs=[vmem],
        out_specs=(vmem, vmem),
        compiler_params=small,
        name="sum",
    )(arrived)
    return (jnp.transpose(new_q, (1, 0, 2)), jnp.transpose(new_p, (1, 0, 2)))


def solution(mesh):
    placed = (
        P("bead", None, "space"),
        P("bead", None, "space"),
        P("space"),
        P(None, "space"),
        P("space"),
        P(),
        P(),
        P(),
        P(),
        P(),
        P(),
        P(),
    )
    return jax.shard_map(
        shards,
        mesh=mesh,
        in_specs=placed,
        out_specs=(P("bead", None, "space"), P("bead", None, "space")),
        check_vma=False,
    )
```

```python
import functools
import math

import jax
import jax.numpy as jnp
import numpy as np
from jax import lax
from jax.experimental import pallas as pl
from jax.experimental.pallas import tpu as pltpu
from jax.sharding import PartitionSpec as P

STEP = 2.0
HALF_STEP = 1.0
HEAVY = 16.0
SQRT3 = math.sqrt(3.0)
SQRT5 = math.sqrt(5.0)
SQRT15 = math.sqrt(15.0)
LANES = 128
ORDERS = 9
GROUP = (0, 1, 1, 1, 2, 2, 2, 2, 2)
HEAD = 8
MIB = 1024 * 1024
f32 = jnp.float32
bf16 = jnp.bfloat16


def split(x):
    hi = x.astype(bf16)
    return hi, (x - hi.astype(f32)).astype(bf16)


def split_rows(x):
    hi = x.astype(bf16).astype(f32)
    return jnp.concatenate([hi, x - hi], axis=0)


def split3(x):
    hi = x.astype(bf16)
    rest = x - hi.astype(f32)
    mid = rest.astype(bf16)
    return hi, mid, (rest - mid.astype(f32)).astype(bf16)


def six_rows(x, order):
    hi = x.astype(bf16).astype(f32)
    mid = (x - hi).astype(bf16).astype(f32)
    parts = (hi, mid, x - hi - mid)
    return jnp.concatenate([parts[i] for i in order], axis=0)


VALUE_ORDER = (0, 1, 0, 1, 2, 0)
WEIGHT_ORDER = (0, 0, 1, 1, 0, 2)


def dot(a, b):
    return jnp.dot(a, b, preferred_element_type=f32)


def dot_nt(a, b):
    return lax.dot_general(a, b, (((1,), (1,)), ((), ())), preferred_element_type=f32)


def in_turns(start, stop, step, most=4):
    per_turn = next(n for n in range(most, 0, -1) if (stop - start) % n == 0)

    def turn(i, carry):
        for j in range(per_turn):
            step(start + i * per_turn + j)
        return carry

    lax.fori_loop(0, (stop - start) // per_turn, turn, 0)


def row(x, rows=8):
    return jnp.broadcast_to(x, (rows, x.shape[1]))


def lookup(chunks, wanted, position):
    out = None
    for number, chunk in chunks:
        got = jnp.take_along_axis(row(chunk), position, axis=1, mode="promise_in_bounds")
        out = got if out is None else jnp.where(wanted == number, got, out)
    return out


def harmonics(ux, uy, uz):
    return [
        None,
        SQRT3 * ux,
        SQRT3 * uy,
        SQRT3 * uz,
        SQRT15 * ux * uy,
        SQRT15 * uy * uz,
        0.5 * SQRT5 * (2.0 * uz * uz - ux * ux - uy * uy),
        SQRT15 * ux * uz,
        0.5 * SQRT15 * (ux * ux - uy * uy),
    ]


def silu_parts(v):
    gate = 1.0 / (1.0 + jnp.exp(-v))
    return v * gate, gate * (1.0 + v * (1.0 - gate))


def choose_kernel(block_ref, *refs):
    sources = refs[:7]
    oh_ref, rrc_ref, r2c_ref, side_ref, rrr_ref, mixa_ref, mixt_ref = refs[7:14]
    held = refs[14:21]
    sems = refs[21]
    emb_ref, rad1_ref, rad2_ref, mix1_ref, mix2_ref, read1_ref, read2_ref = held
    fetches = [pltpu.make_async_copy(src, dst, sems.at[i]) for i, (src, dst) in enumerate(zip(sources, held))]
    for fetch in fetches:
        fetch.start()
    chan = emb_ref.shape[1]
    bases = rad1_ref.shape[0]
    atoms = block_ref.shape[1]
    slots = block_ref.shape[0] - HEAD

    ids16 = lax.broadcasted_iota(jnp.int32, (LANES, atoms), 0).astype(jnp.int16)
    one16 = jnp.ones((LANES, atoms), bf16)
    zero16 = jnp.zeros((LANES, atoms), bf16)
    for k in range(slots):
        slot = block_ref[HEAD + k : HEAD + k + 1, :].astype(jnp.int32)
        wanted = jnp.broadcast_to(slot, (LANES, atoms)).astype(jnp.int16)
        for r in range(oh_ref.shape[0] // LANES):
            hit = wanted - jnp.int16(r * LANES) == ids16
            oh_ref[r * LANES : (r + 1) * LANES, k * atoms : (k + 1) * atoms] = jnp.where(hit, one16, zero16)

    for fetch in fetches:
        fetch.wait()
    emb0 = emb_ref[0:1, :]
    emb_d = emb_ref[1:2, :] - emb0
    rr = jnp.concatenate([rad1_ref[...] * emb0, rad1_ref[...] * emb_d], axis=0) * (1.0 / slots)
    rr_hi = rr.astype(bf16).astype(f32)
    rr_lo = rr - rr_hi
    r2 = rad2_ref[...] * (1.0 / slots)
    zeros = jnp.zeros((8, chan), f32)
    turned1 = jnp.concatenate([six_rows(rr, WEIGHT_ORDER)] + [zeros] * (16 - 12 * bases // 8), axis=0).T
    sides = jnp.concatenate([emb0, emb_d, read1_ref[...], read2_ref[...], zeros[:4]], axis=0)
    turned2 = jnp.concatenate([six_rows(r2, WEIGHT_ORDER)] + [zeros] * (16 - 6 * bases // 8), axis=0).T
    rrc_ref[...] = turned1[:, : 12 * bases].astype(bf16)
    r2c_ref[...] = turned2[:, : 6 * bases].astype(bf16)
    side_ref[...] = jnp.concatenate([sides] + [zeros] * 15, axis=0).T
    rrr_ref[...] = jnp.concatenate(
        [jnp.concatenate([rr_hi, rr_hi], axis=1), jnp.concatenate([rr_lo, jnp.zeros_like(rr_lo)], axis=1)], axis=0
    ).astype(bf16)
    for i, ref in enumerate((mix1_ref, mix2_ref)):
        parts = split3(ref[...])
        for at, part in enumerate(WEIGHT_ORDER):
            mixa_ref[i, :, at * 3 * chan : (at + 1) * 3 * chan] = parts[part]
        for g in range(3):
            hi, lo = split(ref[:, g * chan : (g + 1) * chan].T)
            mixt_ref[i, g] = jnp.concatenate([hi, hi, lo], axis=1)


def six_deep(x):
    parts = split3(x)
    return jnp.concatenate([parts[i] for i in VALUE_ORDER], axis=0)


def three_deep(x):
    hi, lo = split(x)
    return jnp.concatenate([hi, lo, hi], axis=0)


def edge_kernel(plan, *refs):
    atoms, near, wide, before, after = plan
    n_wide = len(wide)
    blocks = refs[:n_wide]
    geo_ref, y_ref, yb_ref, ub_ref, bk_ref, bt_ref, gidx_ref, pick_ref, as_ref = refs[n_wide:]
    bases = bk_ref.shape[0]
    slots = gidx_ref.shape[0]
    tiles = atoms // LANES
    half = atoms // 2
    half_tiles = half // LANES
    order_col = lax.broadcasted_iota(jnp.int32, (bases, LANES), 0).astype(f32)
    tables = []
    for quantity in range(4):
        chunks = []
        for g in range(n_wide):
            for t in range(tiles):
                chunks.append((g * tiles + t, blocks[g][quantity : quantity + 1, t * LANES : (t + 1) * LANES]))
        tables.append(chunks)
    for q in range(len(near)):
        ghosts = []
        for t in range(half_tiles):
            ghosts.append(
                (t, blocks[before[q]][4:5, half + t * LANES : half + (t + 1) * LANES] + float(before[q] * atoms))
            )
        for t in range(half_tiles):
            ghosts.append(
                (
                    half_tiles + tiles + t,
                    blocks[after[q]][4:5, t * LANES : (t + 1) * LANES] + float(after[q] * atoms),
                )
            )
        if q == 0:
            ids16 = lax.broadcasted_iota(jnp.int32, (pick_ref.shape[0], LANES), 0).astype(jnp.int16)
            one16 = jnp.ones(ids16.shape, bf16)
            zero16 = jnp.zeros(ids16.shape, bf16)
            for t, (_, chunk) in enumerate(ghosts):
                wanted = jnp.broadcast_to(chunk.astype(jnp.int32), ids16.shape).astype(jnp.int16)
                pick_ref[:, t * LANES : (t + 1) * LANES] = jnp.where(wanted == ids16, one16, zero16)
        for t in range(tiles):
            cols = slice(t * LANES, (t + 1) * LANES)
            here = slice(q * atoms + t * LANES, q * atoms + (t + 1) * LANES)
            slot = blocks[q][HEAD : HEAD + slots, cols].astype(jnp.int32)
            chunk_no = slot >> 7
            far = lookup(ghosts, chunk_no, slot & 127).astype(jnp.int32)
            own = (slot >= half) & (slot < half + atoms)
            gidx = jnp.where(own, slot + (q * atoms - half), far)
            gidx_ref[:, here] = gidx
            chunk_no = gidx >> 7
            place = gidx & 127
            xj, yj, zj, fj = [lookup(tables[i], chunk_no, place) for i in range(4)]
            rx = xj - row(blocks[q][0:1, cols])
            ry = yj - row(blocks[q][1:2, cols])
            rz = zj - row(blocks[q][2:3, cols])
            soft = jnp.sqrt(rx * rx + ry * ry + rz * rz + 1.0)
            back = 1.0 / soft
            ux, uy, uz = rx * back, ry * back, rz * back
            for i, value in enumerate((ux, uy, uz, back, soft, fj)):
                geo_ref[i, :, here] = value
            if q == 0:
                for i, value in enumerate((ux, uy, uz)):
                    for k in range(slots):
                        ub_ref[i, k, :, cols] = row(value[k : k + 1, :])
            sphere = harmonics(ux, uy, uz)
            for l in range(1, ORDERS):
                y_ref[l - 1, :, here] = sphere[l]
                if q == 0:
                    for k in range(slots):
                        yb_ref[l - 1, k, :, cols] = row(sphere[l][k : k + 1, :])
            for n in range(bases):
                bk_ref[n, :, here] = jnp.exp(-0.5 * (soft - (1.0 + n)) ** 2)
            for k in range(slots):
                basis = jnp.exp(-0.5 * (row(soft[k : k + 1, :], bases) - (1.0 + order_col)) ** 2)
                bt_ref[k, 0:bases, here] = basis
                bt_ref[k, bases : 2 * bases, here] = basis * row(fj[k : k + 1, :], bases)
            low = [None] * ORDERS
            for k in range(slots):
                basis = bt_ref[k, :, here]
                for l in range(ORDERS):
                    term = basis if l == 0 else basis * row(y_ref[l - 1, k : k + 1, here], 2 * bases)
                    low[l] = term if low[l] is None else low[l] + term
            for l in range(ORDERS):
                as_ref[l, :, here] = six_rows(low[l], VALUE_ORDER).astype(bf16)


def first_kernel(plan, *refs):
    atoms, near, wide, _, _ = plan
    n_wide = len(wide)
    blocks = refs[:n_wide]
    as_ref, rrc_ref, side_ref, mixa_ref, m1_ref, sp1_ref, hid_ref, hs_ref, flag_ref = refs[n_wide:]
    chan = m1_ref.shape[1]
    n_near = m1_ref.shape[2]

    for q in range(len(near)):
        flag_ref[0:1, q * atoms : (q + 1) * atoms] = blocks[q][3:4, :]
    wide_cols = 2 * LANES
    emb0_col = side_ref[:, 0:1]
    embd_col = side_ref[:, 1:2]

    def first(j):
        here = pl.ds(pl.multiple_of(j * wide_cols, wide_cols), wide_cols)
        inv = [None, None, None]
        for l in range(ORDERS):
            m = dot(rrc_ref[...], as_ref[l, :, here])
            m1_ref[l, :, here] = m
            inv[GROUP[l]] = m * m if inv[GROUP[l]] is None else inv[GROUP[l]] + m * m
        value = dot(mixa_ref[0], six_deep(jnp.concatenate(inv, axis=0)))
        act, slope = silu_parts(value)
        sp1_ref[:, here] = slope
        hidden = act + emb0_col + embd_col * flag_ref[0:1, here]
        hid_ref[:, here] = hidden
        for part, piece in enumerate(split3(hidden)):
            hs_ref[part * chan : (part + 1) * chan, here] = piece

    in_turns(0, n_near // wide_cols, first)


def gather_kernel(hid_ref, hs_ref, oh_ref, pick_ref, gidx_ref, bt_ref, geo_ref, r2c_ref,
                  hj_ref, w_ref, slope_ref, car_ref, ext_ref):
    slots = bt_ref.shape[0]
    bases = bt_ref.shape[1] // 2
    chan, n_near = hid_ref.shape
    atoms = hj_ref.shape[1] // slots
    half = atoms // 2
    ghosts = dot(hs_ref[...], pick_ref[...]).astype(bf16)
    ext_ref[:, 0:half] = ghosts[:, :half]
    ext_ref[:, half : half + atoms] = hs_ref[:, 0:atoms]
    ext_ref[:, half + atoms :] = ghosts[:, half:]
    reach = 1.0 + lax.broadcasted_iota(jnp.int32, (bases, atoms), 0).astype(f32)
    for k in range(slots):
        here = slice(k * atoms, (k + 1) * atoms)
        basis = bt_ref[k, 0:bases, 0:atoms]
        for ref, value in ((w_ref, basis), (slope_ref, basis * (reach - row(geo_ref[4, k : k + 1, 0:atoms], bases)))):
            ref[:, here] = dot(r2c_ref[...], six_rows(value, VALUE_ORDER).astype(bf16))

    for pair in range(slots // 2):
        by_lane = 4 * LANES if atoms >= 4 * LANES else 0
        by_product = 2 * atoms - by_lane
        first = pair * 2 * atoms
        here = slice(first, first + by_product)
        both = dot(ext_ref[...], oh_ref[:, here])
        wanted = gidx_ref[2 * pair + 1 : 2 * pair + 2, 0:atoms]
        for t in range(by_lane // LANES):
            at = slice(first + by_product + t * LANES, first + by_product + (t + 1) * LANES)
            start = atoms - by_lane + t * LANES
            mine = row(wanted[:, start : start + LANES])
            chunk_no = mine >> 7
            place = mine & 127
            for c in range(chan // 8):
                rows = slice(8 * c, 8 * c + 8)
                feat = None
                for chunk in range(n_near // LANES):
                    held = hid_ref[rows, chunk * LANES : (chunk + 1) * LANES]
                    got = jnp.take_along_axis(held, place, axis=1, mode="promise_in_bounds")
                    feat = got if feat is None else jnp.where(chunk_no == chunk, got, feat)
                hj_ref[rows, at] = feat
                car_ref[rows, at] = feat * w_ref[rows, at]
        feat = both[:chan] + (both[chan : 2 * chan] + both[2 * chan :])
        hj_ref[:, here] = feat
        car_ref[:, here] = feat * w_ref[:, here]


def moment_kernel(car_ref, yb_ref, mixa_ref, mixt_ref, side_ref, m2_ref, dinv_ref, inv_ref):
    slots = yb_ref.shape[1]
    chan, atoms = m2_ref.shape[1:]
    tiles = atoms // LANES
    wide_cols = 2 * LANES
    rows = 32
    groups = chan // rows

    def moments(step):
        t = step // groups
        c = step % groups
        cols = pl.ds(pl.multiple_of(t * LANES, LANES), LANES)
        base = pl.multiple_of(c * rows, rows)
        acc = [[None] * ORDERS for _ in range(rows // 8)]
        for k in range(slots):
            at = pl.ds(pl.multiple_of(k * atoms + t * LANES, LANES), LANES)
            got = car_ref[pl.ds(base, rows), at]
            for l in range(ORDERS):
                yb = yb_ref[l - 1, k, :, cols] if l else None
                for h in range(rows // 8):
                    part = got[8 * h : 8 * h + 8]
                    term = part * yb if l else part
                    acc[h][l] = term if acc[h][l] is None else acc[h][l] + term
        for h in range(rows // 8):
            inv = [None] * 3
            for l in range(ORDERS):
                m2_ref[l, pl.ds(pl.multiple_of(base + 8 * h, 8), 8), cols] = acc[h][l]
                sq = acc[h][l] * acc[h][l]
                g = GROUP[l]
                inv[g] = sq if inv[g] is None else inv[g] + sq
            for g in range(3):
                inv_ref[pl.ds(pl.multiple_of(g * chan + base + 8 * h, 8), 8), cols] = inv[g]

    in_turns(0, tiles * groups, moments, 2)
    read2_col = side_ref[:, 3:4]
    for t in range(atoms // wide_cols):
        cols = slice(t * wide_cols, (t + 1) * wide_cols)
        _, slope = silu_parts(dot(mixa_ref[1], six_deep(inv_ref[:, cols])))
        slope = three_deep(slope * (2.0 * read2_col))
        for g, scale in enumerate((1.0, 0.5 * SQRT3, 0.5 * SQRT15)):
            dinv_ref[g * chan : (g + 1) * chan, cols] = scale * dot(mixt_ref[1, g], slope)


def back_second_kernel(m2_ref, dinv_ref, car_ref, hj_ref, w_ref, slope_ref, ub_ref, dhe_ref, p_ref):
    slots = ub_ref.shape[1]
    chan, atoms = m2_ref.shape[1:]
    tiles = atoms // LANES
    pairs = chan // 16
    per_turn = 4 if pairs % 4 == 0 else 1
    k_step = slots // 2

    def back_moments(t, carry):
        cols = pl.ds(pl.multiple_of(t * LANES, LANES), LANES)

        def one(c, acc, k0):
            forms = []
            for h in range(2):
                rows = pl.ds(pl.multiple_of(c * 16 + 8 * h, 8), 8)
                scale = [dinv_ref[pl.ds(pl.multiple_of(g * chan + c * 16 + 8 * h, 8), 8), cols] for g in range(3)]
                dm = [m2_ref[l, rows, cols] * scale[GROUP[l]] for l in range(ORDERS)]
                low = dm[6] * (1.0 / SQRT3)
                forms.append((dm[0], dm[1], dm[2], dm[3], dm[8] - low, -dm[8] - low, low + low, dm[4], dm[5], dm[7]))
            base = pl.multiple_of(c * 16, 16)
            for k in range(k0, k0 + k_step):
                at = pl.ds(pl.multiple_of(k * atoms + t * LANES, LANES), LANES)
                got = car_ref[pl.ds(base, 16), at]
                stretch = hj_ref[pl.ds(base, 16), at] * slope_ref[pl.ds(base, 16), at]
                ux, uy, uz = [ub_ref[i, k, :, cols] for i in range(3)]
                out = []
                for h in range(2):
                    mid, dx, dy, dz, qxx, qyy, qzz, qxy, qyz, qxz = forms[h]
                    gx = dx + qxx * ux + qxy * uy + qxz * uz
                    gy = dy + qxy * ux + qyy * uy + qyz * uz
                    gz = dz + qxz * ux + qyz * uy + qzz * uz
                    out.append(mid + (gx + dx) * ux + (gy + dy) * uy + (gz + dz) * uz)
                    part = got[8 * h : 8 * h + 8]
                    at_acc = 4 * (k - k0)
                    for i, g in enumerate((gx, gy, gz)):
                        acc[at_acc + i] = acc[at_acc + i] + part * g
                    acc[at_acc + 3] = acc[at_acc + 3] + out[h] * stretch[8 * h : 8 * h + 8]
                hi, lo = split(jnp.concatenate(out, axis=0) * w_ref[pl.ds(base, 16), at])
                dhe_ref[pl.ds(base, 16), at] = hi
                dhe_ref[pl.ds(pl.multiple_of(chan + c * 16, 16), 16), at] = lo

        for k0 in range(0, slots, k_step):

            def over(c, acc, k0=k0):
                acc = list(acc)
                for i in range(per_turn):
                    one(per_turn * c + i, acc, k0)
                return tuple(acc)

            start = tuple(jnp.zeros((8, LANES), f32) for _ in range(4 * k_step))
            acc = lax.fori_loop(0, pairs // per_turn, over, start)
            for k in range(k_step):
                for i in range(4):
                    p_ref[i, 8 * (k0 + k) : 8 * (k0 + k) + 8, cols] = acc[4 * k + i]
        return carry

    lax.fori_loop(0, tiles, back_moments, 0)


def scatter_kernel(oh_ref, pick_ref, dhe_ref, side_ref, p_ref, gidx_ref, dh_ref, q_ref, ohlo_ref):
    chan, n_near = dh_ref.shape
    slots = gidx_ref.shape[0]
    atoms = pick_ref.shape[1]
    half = atoms // 2
    both = dot_nt(dhe_ref[...], jnp.concatenate([oh_ref[:half], oh_ref[half + atoms :]], axis=0))
    hi, lo = split(both[:chan] + both[chan:])
    spread = dot_nt(jnp.concatenate([hi, lo], axis=0), pick_ref[...])
    spread = spread[:chan] + spread[chan:]
    both = dot_nt(dhe_ref[...], oh_ref[half : half + atoms])
    dh_ref[:, 0:atoms] = spread[:, :atoms] + both[:chan] + both[chan:] + side_ref[:, 2:3]
    if n_near > atoms:
        dh_ref[:, atoms:] = spread[:, atoms:]
    ids16 = lax.broadcasted_iota(jnp.int32, (LANES, n_near), 0).astype(jnp.int16)
    one16 = jnp.ones((LANES, n_near), bf16)
    zero16 = jnp.zeros((LANES, n_near), bf16)
    for k in range(slots):
        place = jnp.broadcast_to(gidx_ref[k : k + 1, :] & 127, (LANES, n_near)).astype(jnp.int16)
        ohlo_ref[:, k * n_near : (k + 1) * n_near] = jnp.where(place == ids16, one16, zero16)
    lane = lax.broadcasted_iota(jnp.int32, (slots, 16 * slots), 1)
    sub = lax.broadcasted_iota(jnp.int32, (slots, 16 * slots), 0)
    adder = jnp.where(((lane >> 3) & (slots - 1)) == sub, 1.0, 0.0).astype(bf16)
    for i in range(4):
        total = dot(adder, split_rows(p_ref[i]).astype(bf16))
        q_ref[8 * i : 8 * i + 8, :] = 2.0 * total if i < 3 else total


def back_first_kernel(dh_ref, sp1_ref, m1_ref, mixt_ref, rrr_ref, da_ref):
    n_near = sp1_ref.shape[1]
    rows = rrr_ref.shape[0] // 2
    wide_cols = 2 * LANES

    def back_first(j):
        here = pl.ds(pl.multiple_of(j * wide_cols, wide_cols), wide_cols)
        slope = three_deep(dh_ref[:, here] * sp1_ref[:, here] * 2.0)
        scale = [dot(mixt_ref[0, g], slope) for g in range(3)]
        for l in range(ORDERS):
            hi, lo = split(m1_ref[l, :, here] * scale[GROUP[l]])
            out = dot(rrr_ref[...], jnp.concatenate([hi, lo], axis=0))
            da_ref[l, :, here] = out[:rows] + out[rows:]

    in_turns(0, n_near // wide_cols, back_first)


def back_edge_kernel(plan, *refs):
    atoms, near, wide, _, _ = plan
    n_wide = len(wide)
    blocks = refs[:n_wide]
    moment_src, geo_ref, y_ref, bk_ref, gidx_ref, da_ref, q_ref, ohlo_ref = refs[n_wide : n_wide + 8]
    push_ref, mass_ref, val_ref, dr_ref, moment_ref, sem = refs[n_wide + 8 :]
    fetch = pltpu.make_async_copy(moment_src, moment_ref, sem)
    fetch.start()
    bases, slots, n_near = bk_ref.shape
    tiles = atoms // LANES
    top_rows = val_ref.shape[0] // 6

    def back_geometry(t, mine):
        here = pl.ds(pl.multiple_of(t * LANES, LANES), LANES)
        ux, uy, uz, back, soft, fj = [geo_ref[i, :, here] for i in range(6)]
        dy = [None] * ORDERS
        ds = None
        for n in range(bases):
            basis = bk_ref[n, :, here]
            db = None
            for l in range(ORDERS):
                g = row(da_ref[l, n : n + 1, here]) + fj * row(da_ref[l, bases + n : bases + n + 1, here])
                if l:
                    dy[l] = g * basis if dy[l] is None else dy[l] + g * basis
                    db = db + g * y_ref[l - 1, :, here]
                else:
                    db = g
            db = db * basis * ((1.0 + n) - soft)
            ds = db if ds is None else ds + db
        if mine:
            ds = ds + q_ref[24:32, here]
        dux = SQRT3 * dy[1] + SQRT15 * (uy * dy[4] + uz * dy[7] + ux * dy[8]) - SQRT5 * ux * dy[6]
        duy = SQRT3 * dy[2] + SQRT15 * (ux * dy[4] + uz * dy[5] - uy * dy[8]) - SQRT5 * uy * dy[6]
        duz = SQRT3 * dy[3] + SQRT15 * (uy * dy[5] + ux * dy[7]) + 2.0 * SQRT5 * uz * dy[6]
        if mine:
            dux, duy, duz = [d + q_ref[8 * i : 8 * i + 8, here] for i, d in enumerate((dux, duy, duz))]
        along = ds - (ux * dux + uy * duy + uz * duz) * back
        for i, value in enumerate((dux * back + along * ux, duy * back + along * uy, duz * back + along * uz)):
            dr_ref[i, :, here] = value

    in_turns(0, tiles, lambda t: back_geometry(t, True))
    in_turns(tiles, n_near // LANES, lambda t: back_geometry(t, False))

    def place_tile(t):
        here = pl.ds(pl.multiple_of(t * LANES, LANES), LANES)
        gidx = gidx_ref[:, here]
        chunk_no = gidx >> 7
        parts = []
        for i in range(3):
            value = dr_ref[i, :, here]
            hi = value.astype(bf16).astype(f32)
            parts.append((hi, value - hi))
        chunk_ids = lax.broadcasted_iota(jnp.int32, (top_rows, LANES), 0)
        for k in range(slots):
            at = pl.ds(pl.multiple_of(k * n_near + t * LANES, LANES), LANES)
            hit = chunk_ids == row(chunk_no[k : k + 1, :], top_rows)
            for i in range(3):
                both = [jnp.where(hit, row(part[k : k + 1, :], top_rows), 0.0) for part in parts[i]]
                val_ref[2 * i * top_rows : 2 * (i + 1) * top_rows, at] = jnp.concatenate(both, axis=0).astype(bf16)

    in_turns(0, n_near // LANES, place_tile)
    landed = dot_nt(val_ref[...], ohlo_ref[...])
    fetch.wait()
    lines = push_ref.shape[0] // (n_wide + 1)
    for i in range(3):
        total = (
            landed[2 * i * top_rows : (2 * i + 1) * top_rows] + landed[(2 * i + 1) * top_rows : (2 * i + 2) * top_rows]
        )
        for g in range(n_wide):
            for t in range(tiles):
                cols = slice(t * LANES, (t + 1) * LANES)
                line = total[g * tiles + t : g * tiles + t + 1, :]
                if g < len(near):
                    here = slice(g * atoms + t * LANES, g * atoms + (t + 1) * LANES)
                    line = line - jnp.sum(dr_ref[i, :, here], axis=0, keepdims=True)
                line = -HALF_STEP * line
                at = i * tiles + t
                if g == 0:
                    line = line + moment_ref[i, :, cols]
                    push_ref[at : at + 1, :] = blocks[0][i : i + 1, cols]
                push_ref[(1 + g) * lines + at : (1 + g) * lines + at + 1, :] = line
                mass = HEAVY - (HEAVY - 1.0) * blocks[g][3:4, cols]
                mass_ref[g * lines + at : g * lines + at + 1, :] = mass
    if lines > 3 * tiles:
        for g in range(n_wide + 1):
            blank = slice(g * lines + 3 * tiles, (g + 1) * lines)
            push_ref[blank, :] = jnp.zeros((lines - 3 * tiles, LANES), f32)
            if g < n_wide:
                mass_ref[blank, :] = jnp.ones((lines - 3 * tiles, LANES), f32)


def in_hbm(x):
    return pltpu.with_memory_space_constraint(x, pltpu.HBM)


def run(name, body, operands, results, scratch=(), far=(), cost=None):
    sizes = [math.prod(x.shape) * x.dtype.itemsize // 2 for i, x in enumerate(operands) if i not in far]
    sizes += [math.prod(shape) * jnp.dtype(dtype).itemsize for shape, dtype in results]
    sizes += [math.prod(x.shape) * x.dtype.itemsize for x in scratch if x.memory_space == pltpu.VMEM]
    limit = sum(sizes) + 4 * MIB
    specs = [pl.BlockSpec(memory_space=pltpu.HBM if i in far else pltpu.VMEM) for i in range(len(operands))]
    return pl.pallas_call(
        body,
        out_shape=tuple(jax.ShapeDtypeStruct(shape, dtype) for shape, dtype in results),
        in_specs=specs,
        out_specs=tuple(pl.BlockSpec(memory_space=pltpu.VMEM) for _ in results),
        scratch_shapes=list(scratch),
        compiler_params=pltpu.CompilerParams(vmem_limit_bytes=limit),
        cost_estimate=cost,
        name=name,
    )(*[in_hbm(x) if i in far else x for i, x in enumerate(operands)])


def choose(block, embedding, radial_one, radial_two, mix_one, mix_two, read_one, read_two):
    atoms = block.shape[1]
    slots = block.shape[0] - HEAD
    chan = embedding.shape[1]
    bases = radial_one.shape[0]
    weights = (embedding, radial_one, radial_two, mix_one, mix_two, read_one[None], read_two[None])
    return run(
        "choose",
        choose_kernel,
        (block, *weights),
        (
            ((2 * atoms, slots * atoms), bf16),
            ((chan, 12 * bases), bf16),
            ((chan, 6 * bases), bf16),
            ((chan, LANES), f32),
            ((4 * bases, 2 * chan), bf16),
            ((2, chan, 18 * chan), bf16),
            ((2, 3, chan, 3 * chan), bf16),
        ),
        [pltpu.VMEM(w.shape, f32) for w in weights] + [pltpu.SemaphoreType.DMA((len(weights),))],
        range(1, 1 + len(weights)),
        cost=pl.CostEstimate(flops=2 * 10**9, bytes_accessed=2 * 10**6, transcendentals=0),
    )


def pushes(plan, blocks, momenta, chosen):
    atoms, near, wide, _, _ = plan
    oh, rrc, r2c, sides, rrr, mixa, mixt = chosen
    chan = rrc.shape[0]
    bases = rrr.shape[0] // 4
    slots = blocks[0].shape[0] - HEAD
    n_near = len(near) * atoms
    edges = slots * atoms
    top_rows = -(-len(wide) * atoms // LANES // 8) * 8
    lines = line_count(atoms)
    geo, y, yb, ub, bk, bt, gidx, pick, as1 = run(
        "edges",
        functools.partial(edge_kernel, plan),
        blocks,
        (
            ((6, slots, n_near), f32),
            ((ORDERS - 1, slots, n_near), f32),
            ((ORDERS - 1, slots, 8, atoms), f32),
            ((3, slots, 8, atoms), f32),
            ((bases, slots, n_near), f32),
            ((slots, 2 * bases, n_near), f32),
            ((slots, n_near), jnp.int32),
            ((n_near, atoms), bf16),
            ((ORDERS, 12 * bases, n_near), bf16),
        ),
    )
    m1, sp1, hid, hs = run(
        "first",
        functools.partial(first_kernel, plan),
        (*blocks, as1, rrc, sides, mixa),
        (((ORDERS, chan, n_near), f32), ((chan, n_near), f32), ((chan, n_near), f32), ((3 * chan, n_near), bf16)),
        [pltpu.VMEM((8, n_near), f32)],
    )
    hj, w, slope, car = run(
        "gather",
        gather_kernel,
        (hid, hs, oh, pick, gidx, bt, geo, r2c),
        (((chan, edges), f32),) * 4,
        [pltpu.VMEM((3 * chan, 2 * atoms), bf16)],
    )
    m2, dinv = run(
        "moments",
        moment_kernel,
        (car, yb, mixa, mixt, sides),
        (((ORDERS, chan, atoms), f32), ((3 * chan, atoms), f32)),
        [pltpu.VMEM((3 * chan, atoms), f32)],
    )
    dhe, p = run(
        "back_second",
        back_second_kernel,
        (m2, dinv, car, hj, w, slope, ub),
        (((2 * chan, edges), bf16), ((4, 8 * slots, atoms), f32)),
    )
    dh, q, ohlo = run(
        "scatter",
        scatter_kernel,
        (oh, pick, dhe, sides, p, gidx),
        (((chan, n_near), f32), ((4 * slots, atoms), f32), ((LANES, slots * n_near), bf16)),
    )
    (da,) = run("back_first", back_first_kernel, (dh, sp1, m1, mixt, rrr), (((ORDERS, 2 * bases, n_near), f32),))
    return run(
        "back_edges",
        functools.partial(back_edge_kernel, plan),
        (*blocks, momenta, geo, y, bk, gidx, da, q, ohlo),
        ((((len(wide) + 1) * lines, LANES), f32), ((len(wide) * lines, LANES), f32)),
        [
            pltpu.VMEM((6 * top_rows, slots * n_near), bf16),
            pltpu.VMEM((3, slots, n_near), f32),
            pltpu.VMEM(momenta.shape, f32),
            pltpu.SemaphoreType.DMA(()),
        ],
        (len(blocks),),
    )


def line_count(atoms):
    return -(-3 * (atoms // LANES) // 8) * 8


def ring_plan(domains, atoms):
    near = list(dict.fromkeys(o % domains for o in (0, 1, -1)))
    wide = list(dict.fromkeys(near + [o % domains for o in (2, -2)]))
    before = tuple(wide.index((o - 1) % domains) for o in near)
    after = tuple(wide.index((o + 1) % domains) for o in near)
    return atoms, tuple(near), tuple(wide), before, after


def mode_turns(bead_total):
    bead = np.arange(bead_total, dtype=np.float64)[:, None]
    mode = np.arange(bead_total, dtype=np.float64)[None, :]
    phase = 2.0 * np.pi * bead * mode / bead_total
    half_total = bead_total // 2
    table = math.sqrt(2.0 / bead_total) * np.where(mode < half_total, np.cos(phase), np.sin(phase))
    table = np.where(mode == half_total, np.cos(np.pi * bead) / math.sqrt(bead_total), table)
    table = np.where(mode == 0, 1.0 / math.sqrt(bead_total), table)
    angles = bead_total * np.sin(np.pi * mode[0] / bead_total)
    safe = np.where(mode[0] == 0, 1.0, angles)
    reach = np.where(mode[0] == 0, STEP, STEP * np.sin(angles) / safe)
    stiff = angles * np.sin(angles) / STEP
    return [[float(x) for x in (table * factor[None, :]) @ table[0]] for factor in (np.cos(angles), reach, stiff)]


def pack_kernel(coord_src, species_src, send_src, slot_src, block_ref, coord_ref, species_ref, send_ref, slot_ref, sems):
    pairs = ((coord_src, coord_ref), (species_src, species_ref), (send_src, send_ref), (slot_src, slot_ref))
    fetches = [pltpu.make_async_copy(src, dst, sems.at[i]) for i, (src, dst) in enumerate(pairs)]
    for fetch in fetches:
        fetch.start()
    for fetch in fetches:
        fetch.wait()
    atoms = block_ref.shape[1]
    for i in range(3):
        block_ref[i : i + 1, :] = coord_ref[i]
    block_ref[3:4, :] = species_ref[...].astype(f32)
    block_ref[4:5, :] = send_ref[...].astype(f32)
    block_ref[5:HEAD, :] = jnp.zeros((HEAD - 5, atoms), f32)
    block_ref[HEAD:, :] = slot_ref[...].astype(f32)


def turn_kernel(shape, bead_ref, domain_ref, mass_ref, *refs):
    outer, inner, domains, wide = shape
    message_ref = refs[outer]
    turns = mode_turns(outer * inner)
    lines = mass_ref.shape[0] // len(wide)
    my_domain = domain_ref[0]
    my_inner = lax.rem(bead_ref[0], inner)
    if domains > len(wide):
        message_ref[...] = jnp.zeros_like(message_ref)
    masses = [mass_ref[g * lines : (g + 1) * lines, :] for g in range(len(wide))]
    sources = []
    for z in range(outer):
        sources.append([refs[z][g * lines : (g + 1) * lines, :] for g in range(len(wide) + 1)])
    for s in range(inner):
        wraps = jnp.full((lines, LANES), my_inner + s) >= inner
        weights = []
        for turn in turns:
            row_of = []
            for z in range(outer):
                there = turn[(z * inner + s) % (outer * inner)]
                round_it = turn[(z * inner + s - inner) % (outer * inner)]
                row_of.append(jnp.where(wraps, jnp.full((lines, LANES), round_it), jnp.full((lines, LANES), there)))
            weights.append(row_of)
        to_inner = lax.rem(my_inner + s, inner)
        for g in range(len(wide)):
            turned = sum(weights[0][z] * sources[z][1 + g] for z in range(outer))
            drift = sum(weights[1][z] * sources[z][1 + g] for z in range(outer))
            new_q = drift / masses[g]
            new_p = turned
            if g == 0:
                new_q = new_q + sum(weights[0][z] * sources[z][0] for z in range(outer))
                new_p = new_p - masses[g] * sum(weights[2][z] * sources[z][0] for z in range(outer))
            to = to_inner * domains + lax.rem(my_domain + wide[g], domains)
            message_ref[to, 0:lines, :] = new_q
            message_ref[to, lines:, :] = new_p


def sum_kernel(arrived_ref, q_ref, p_ref):
    total = arrived_ref[0]
    for i in range(1, arrived_ref.shape[0]):
        total = total + arrived_ref[i]
    lines = total.shape[0] // 2
    tiles = q_ref.shape[2] // LANES
    for i in range(3):
        for t in range(tiles):
            at = i * tiles + t
            q_ref[i, :, t * LANES : (t + 1) * LANES] = total[at : at + 1]
            p_ref[i, :, t * LANES : (t + 1) * LANES] = total[lines + at : lines + at + 1]


def shards(
    positions, momenta, species, neighbours, send_list, embedding, radial_one, radial_two, mix_one, mix_two,
    read_one, read_two,
):
    slots, atoms = neighbours.shape
    domains = lax.axis_size("space")
    beads = lax.axis_size("bead")
    inner = next(d for d in range(1, beads + 1) if beads % d == 0 and d * d >= beads)
    outer = beads // inner
    plan = ring_plan(domains, atoms)
    wide = plan[2]
    vmem = pl.BlockSpec(memory_space=pltpu.VMEM)
    smem = pl.BlockSpec(memory_space=pltpu.SMEM)
    far = pl.BlockSpec(memory_space=pltpu.HBM)
    small = pltpu.CompilerParams(vmem_limit_bytes=4 * MIB)
    coord_rows = jnp.transpose(positions, (1, 0, 2))
    moment_rows = jnp.transpose(momenta, (1, 0, 2))
    block = pl.pallas_call(
        pack_kernel,
        out_shape=jax.ShapeDtypeStruct((HEAD + slots, atoms), f32),
        in_specs=[far] * 4,
        out_specs=vmem,
        scratch_shapes=[
            pltpu.VMEM(coord_rows.shape, f32),
            pltpu.VMEM((1, atoms), jnp.int32),
            pltpu.VMEM((1, atoms), jnp.int32),
            pltpu.VMEM((slots, atoms), jnp.int32),
            pltpu.SemaphoreType.DMA((4,)),
        ],
        compiler_params=small,
        name="pack",
    )(in_hbm(coord_rows), in_hbm(species[None]), in_hbm(send_list[None]), in_hbm(neighbours))
    blocks = [block]
    for offset in wide[1:]:
        blocks.append(lax.ppermute(block, "space", [(i, (i - offset) % domains) for i in range(domains)]))
    chosen = choose(block, embedding, radial_one, radial_two, mix_one, mix_two, read_one, read_two)
    pushed, masses = pushes(plan, blocks, moment_rows, chosen)
    sources = [pushed]
    for z in range(1, outer):
        sources.append(lax.ppermute(pushed, "bead", [(b, (b + z * inner) % beads) for b in range(beads)]))
    here = [lax.axis_index(axis).astype(jnp.int32).reshape(1) for axis in ("bead", "space")]
    lines = line_count(atoms)
    messages = pl.pallas_call(
        functools.partial(turn_kernel, (outer, inner, domains, wide)),
        out_shape=jax.ShapeDtypeStruct((inner * domains, 2 * lines, LANES), f32),
        in_specs=[smem, smem, vmem] + [vmem] * outer,
        out_specs=vmem,
        compiler_params=small,
        name="turn",
    )(*here, masses, *sources)
    rows = [[z * inner * domains + i for i in range(inner * domains)] for z in range(outer)]
    arrived = lax.all_to_all(messages, ("bead", "space"), 0, 0, axis_index_groups=rows, tiled=True)
    new_q, new_p = pl.pallas_call(
        sum_kernel,
        out_shape=(jax.ShapeDtypeStruct((3, 1, atoms), f32),) * 2,
        in_specs=[vmem],
        out_specs=(vmem, vmem),
        compiler_params=small,
        name="sum",
    )(arrived)
    return (jnp.transpose(new_q, (1, 0, 2)), jnp.transpose(new_p, (1, 0, 2)))


def solution(mesh):
    placed = (
        P("bead", None, "space"),
        P("bead", None, "space"),
        P("space"),
        P(None, "space"),
        P("space"),
        P(),
        P(),
        P(),
        P(),
        P(),
        P(),
        P(),
    )
    return jax.shard_map(
        shards,
        mesh=mesh,
        in_specs=placed,
        out_specs=(P("bead", None, "space"), P("bead", None, "space")),
        check_vma=False,
    )
```

```python
import functools
import math

import jax
import jax.numpy as jnp
import numpy as np
from jax import lax
from jax.experimental import pallas as pl
from jax.experimental.pallas import tpu as pltpu
from jax.sharding import PartitionSpec as P

STEP = 2.0
HALF_STEP = 1.0
HEAVY = 16.0
SQRT3 = math.sqrt(3.0)
SQRT5 = math.sqrt(5.0)
SQRT15 = math.sqrt(15.0)
LANES = 128
ORDERS = 9
GROUP = (0, 1, 1, 1, 2, 2, 2, 2, 2)
HEAD = 8
MIB = 1024 * 1024
f32 = jnp.float32
bf16 = jnp.bfloat16


def split(x):
    hi = x.astype(bf16)
    return hi, (x - hi.astype(f32)).astype(bf16)


def split_rows(x):
    hi = x.astype(bf16).astype(f32)
    return jnp.concatenate([hi, x - hi], axis=0)


def split3(x):
    hi = x.astype(bf16)
    rest = x - hi.astype(f32)
    mid = rest.astype(bf16)
    return hi, mid, (rest - mid.astype(f32)).astype(bf16)


def six_rows(x, order):
    hi = x.astype(bf16).astype(f32)
    mid = (x - hi).astype(bf16).astype(f32)
    parts = (hi, mid, x - hi - mid)
    return jnp.concatenate([parts[i] for i in order], axis=0)


VALUE_ORDER = (0, 1, 0, 1, 2, 0)
WEIGHT_ORDER = (0, 0, 1, 1, 0, 2)


def dot(a, b):
    return jnp.dot(a, b, preferred_element_type=f32)


def dot_nt(a, b):
    return lax.dot_general(a, b, (((1,), (1,)), ((), ())), preferred_element_type=f32)


def in_turns(start, stop, step, most=4):
    per_turn = next(n for n in range(most, 0, -1) if (stop - start) % n == 0)

    def turn(i, carry):
        for j in range(per_turn):
            step(start + i * per_turn + j)
        return carry

    lax.fori_loop(0, (stop - start) // per_turn, turn, 0)


def row(x, rows=8):
    return jnp.broadcast_to(x, (rows, x.shape[1]))


def lookup(chunks, wanted, position):
    out = None
    for number, chunk in chunks:
        got = jnp.take_along_axis(row(chunk), position, axis=1, mode="promise_in_bounds")
        out = got if out is None else jnp.where(wanted == number, got, out)
    return out


def harmonics(ux, uy, uz):
    return [
        None,
        SQRT3 * ux,
        SQRT3 * uy,
        SQRT3 * uz,
        SQRT15 * ux * uy,
        SQRT15 * uy * uz,
        0.5 * SQRT5 * (2.0 * uz * uz - ux * ux - uy * uy),
        SQRT15 * ux * uz,
        0.5 * SQRT15 * (ux * ux - uy * uy),
    ]


def silu_parts(v):
    gate = 1.0 / (1.0 + jnp.exp(-v))
    return v * gate, gate * (1.0 + v * (1.0 - gate))


def choose_kernel(block_ref, *refs):
    sources = refs[:7]
    oh_ref, rrc_ref, r2c_ref, side_ref, rrr_ref, mixa_ref, mixt_ref = refs[7:14]
    held = refs[14:21]
    sems = refs[21]
    emb_ref, rad1_ref, rad2_ref, mix1_ref, mix2_ref, read1_ref, read2_ref = held
    fetches = [pltpu.make_async_copy(src, dst, sems.at[i]) for i, (src, dst) in enumerate(zip(sources, held))]
    for fetch in fetches:
        fetch.start()
    chan = emb_ref.shape[1]
    bases = rad1_ref.shape[0]
    atoms = block_ref.shape[1]
    slots = block_ref.shape[0] - HEAD

    ids16 = lax.broadcasted_iota(jnp.int32, (LANES, atoms), 0).astype(jnp.int16)
    one16 = jnp.ones((LANES, atoms), bf16)
    zero16 = jnp.zeros((LANES, atoms), bf16)
    for k in range(slots):
        slot = block_ref[HEAD + k : HEAD + k + 1, :].astype(jnp.int32)
        wanted = jnp.broadcast_to(slot, (LANES, atoms)).astype(jnp.int16)
        for r in range(oh_ref.shape[0] // LANES):
            hit = wanted - jnp.int16(r * LANES) == ids16
            oh_ref[r * LANES : (r + 1) * LANES, k * atoms : (k + 1) * atoms] = jnp.where(hit, one16, zero16)

    for fetch in fetches:
        fetch.wait()
    emb0 = emb_ref[0:1, :]
    emb_d = emb_ref[1:2, :] - emb0
    rr = jnp.concatenate([rad1_ref[...] * emb0, rad1_ref[...] * emb_d], axis=0) * (1.0 / slots)
    rr_hi = rr.astype(bf16).astype(f32)
    rr_lo = rr - rr_hi
    r2 = rad2_ref[...] * (1.0 / slots)
    zeros = jnp.zeros((8, chan), f32)
    turned1 = jnp.concatenate([six_rows(rr, WEIGHT_ORDER)] + [zeros] * (16 - 12 * bases // 8), axis=0).T
    sides = jnp.concatenate([emb0, emb_d, read1_ref[...], read2_ref[...], zeros[:4]], axis=0)
    turned2 = jnp.concatenate([six_rows(r2, WEIGHT_ORDER)] + [zeros] * (16 - 6 * bases // 8), axis=0).T
    rrc_ref[...] = turned1[:, : 12 * bases].astype(bf16)
    r2c_ref[...] = turned2[:, : 6 * bases].astype(bf16)
    side_ref[...] = jnp.concatenate([sides] + [zeros] * 15, axis=0).T
    rrr_ref[...] = jnp.concatenate(
        [jnp.concatenate([rr_hi, rr_hi], axis=1), jnp.concatenate([rr_lo, jnp.zeros_like(rr_lo)], axis=1)], axis=0
    ).astype(bf16)
    for i, ref in enumerate((mix1_ref, mix2_ref)):
        parts = split3(ref[...])
        for at, part in enumerate(WEIGHT_ORDER):
            mixa_ref[i, :, at * 3 * chan : (at + 1) * 3 * chan] = parts[part]
        for g in range(3):
            hi, lo = split(ref[:, g * chan : (g + 1) * chan].T)
            mixt_ref[i, g] = jnp.concatenate([hi, hi, lo], axis=1)


def six_deep(x):
    parts = split3(x)
    return jnp.concatenate([parts[i] for i in VALUE_ORDER], axis=0)


def three_deep(x):
    hi, lo = split(x)
    return jnp.concatenate([hi, lo, hi], axis=0)


def edge_kernel(plan, *refs):
    atoms, near, wide, before, after = plan
    n_wide = len(wide)
    blocks = refs[:n_wide]
    geo_ref, y_ref, yb_ref, ub_ref, bk_ref, bt_ref, gidx_ref, pick_ref, as_ref = refs[n_wide:]
    bases = bk_ref.shape[0]
    slots = gidx_ref.shape[0]
    tiles = atoms // LANES
    half = atoms // 2
    half_tiles = half // LANES
    order_col = lax.broadcasted_iota(jnp.int32, (bases, LANES), 0).astype(f32)
    tables = []
    for quantity in range(4):
        chunks = []
        for g in range(n_wide):
            for t in range(tiles):
                chunks.append((g * tiles + t, blocks[g][quantity : quantity + 1, t * LANES : (t + 1) * LANES]))
        tables.append(chunks)
    for q in range(len(near)):
        ghosts = []
        for t in range(half_tiles):
            ghosts.append(
                (t, blocks[before[q]][4:5, half + t * LANES : half + (t + 1) * LANES] + float(before[q] * atoms))
            )
        for t in range(half_tiles):
            ghosts.append(
                (
                    half_tiles + tiles + t,
                    blocks[after[q]][4:5, t * LANES : (t + 1) * LANES] + float(after[q] * atoms),
                )
            )
        if q == 0:
            ids16 = lax.broadcasted_iota(jnp.int32, (pick_ref.shape[0], LANES), 0).astype(jnp.int16)
            one16 = jnp.ones(ids16.shape, bf16)
            zero16 = jnp.zeros(ids16.shape, bf16)
            for t, (_, chunk) in enumerate(ghosts):
                wanted = jnp.broadcast_to(chunk.astype(jnp.int32), ids16.shape).astype(jnp.int16)
                pick_ref[:, t * LANES : (t + 1) * LANES] = jnp.where(wanted == ids16, one16, zero16)
        for t in range(tiles):
            cols = slice(t * LANES, (t + 1) * LANES)
            here = slice(q * atoms + t * LANES, q * atoms + (t + 1) * LANES)
            slot = blocks[q][HEAD : HEAD + slots, cols].astype(jnp.int32)
            chunk_no = slot >> 7
            far = lookup(ghosts, chunk_no, slot & 127).astype(jnp.int32)
            own = (slot >= half) & (slot < half + atoms)
            gidx = jnp.where(own, slot + (q * atoms - half), far)
            gidx_ref[:, here] = gidx
            chunk_no = gidx >> 7
            place = gidx & 127
            xj, yj, zj, fj = [lookup(tables[i], chunk_no, place) for i in range(4)]
            rx = xj - row(blocks[q][0:1, cols])
            ry = yj - row(blocks[q][1:2, cols])
            rz = zj - row(blocks[q][2:3, cols])
            soft = jnp.sqrt(rx * rx + ry * ry + rz * rz + 1.0)
            back = 1.0 / soft
            ux, uy, uz = rx * back, ry * back, rz * back
            for i, value in enumerate((ux, uy, uz, back, soft, fj)):
                geo_ref[i, :, here] = value
            if q == 0:
                for i, value in enumerate((ux, uy, uz)):
                    for k in range(slots):
                        ub_ref[i, k, :, cols] = row(value[k : k + 1, :])
            sphere = harmonics(ux, uy, uz)
            for l in range(1, ORDERS):
                y_ref[l - 1, :, here] = sphere[l]
                if q == 0:
                    for k in range(slots):
                        yb_ref[l - 1, k, :, cols] = row(sphere[l][k : k + 1, :])
            for n in range(bases):
                bk_ref[n, :, here] = jnp.exp(-0.5 * (soft - (1.0 + n)) ** 2)
            for k in range(slots):
                basis = jnp.exp(-0.5 * (row(soft[k : k + 1, :], bases) - (1.0 + order_col)) ** 2)
                bt_ref[k, 0:bases, here] = basis
                bt_ref[k, bases : 2 * bases, here] = basis * row(fj[k : k + 1, :], bases)
            low = [None] * ORDERS
            for k in range(slots):
                basis = bt_ref[k, :, here]
                for l in range(ORDERS):
                    term = basis if l == 0 else basis * row(y_ref[l - 1, k : k + 1, here], 2 * bases)
                    low[l] = term if low[l] is None else low[l] + term
            for l in range(ORDERS):
                as_ref[l, :, here] = six_rows(low[l], VALUE_ORDER).astype(bf16)


def first_kernel(plan, *refs):
    atoms, near, wide, _, _ = plan
    n_wide = len(wide)
    blocks = refs[:n_wide]
    as_ref, rrc_ref, side_ref, mixa_ref, m1_ref, sp1_ref, hid_ref, hs_ref, flag_ref = refs[n_wide:]
    chan = m1_ref.shape[1]
    n_near = m1_ref.shape[2]

    for q in range(len(near)):
        flag_ref[0:1, q * atoms : (q + 1) * atoms] = blocks[q][3:4, :]
    wide_cols = 2 * LANES
    emb0_col = side_ref[:, 0:1]
    embd_col = side_ref[:, 1:2]

    def first(j):
        here = pl.ds(pl.multiple_of(j * wide_cols, wide_cols), wide_cols)
        inv = [None, None, None]
        for l in range(ORDERS):
            m = dot(rrc_ref[...], as_ref[l, :, here])
            m1_ref[l, :, here] = m
            inv[GROUP[l]] = m * m if inv[GROUP[l]] is None else inv[GROUP[l]] + m * m
        value = dot(mixa_ref[0], six_deep(jnp.concatenate(inv, axis=0)))
        act, slope = silu_parts(value)
        sp1_ref[:, here] = slope
        hidden = act + emb0_col + embd_col * flag_ref[0:1, here]
        hid_ref[:, here] = hidden
        for part, piece in enumerate(split3(hidden)):
            hs_ref[part * chan : (part + 1) * chan, here] = piece

    in_turns(0, n_near // wide_cols, first)


def gather_kernel(hid_ref, hs_ref, oh_ref, pick_ref, gidx_ref, bt_ref, geo_ref, r2c_ref,
                  hj_ref, w_ref, slope_ref, car_ref, ext_ref):
    slots = bt_ref.shape[0]
    bases = bt_ref.shape[1] // 2
    chan, n_near = hid_ref.shape
    atoms = hj_ref.shape[1] // slots
    half = atoms // 2
    ghosts = dot(hs_ref[...], pick_ref[...]).astype(bf16)
    ext_ref[:, 0:half] = ghosts[:, :half]
    ext_ref[:, half : half + atoms] = hs_ref[:, 0:atoms]
    ext_ref[:, half + atoms :] = ghosts[:, half:]
    reach = 1.0 + lax.broadcasted_iota(jnp.int32, (bases, atoms), 0).astype(f32)
    for k in range(slots):
        here = slice(k * atoms, (k + 1) * atoms)
        basis = bt_ref[k, 0:bases, 0:atoms]
        for ref, value in ((w_ref, basis), (slope_ref, basis * (reach - row(geo_ref[4, k : k + 1, 0:atoms], bases)))):
            ref[:, here] = dot(r2c_ref[...], six_rows(value, VALUE_ORDER).astype(bf16))

    for pair in range(slots // 2):
        by_lane = 4 * LANES if atoms >= 4 * LANES else 0
        by_product = 2 * atoms - by_lane
        first = pair * 2 * atoms
        here = slice(first, first + by_product)
        both = dot(ext_ref[...], oh_ref[:, here])
        wanted = gidx_ref[2 * pair + 1 : 2 * pair + 2, 0:atoms]
        for t in range(by_lane // LANES):
            at = slice(first + by_product + t * LANES, first + by_product + (t + 1) * LANES)
            start = atoms - by_lane + t * LANES
            mine = row(wanted[:, start : start + LANES])
            chunk_no = mine >> 7
            place = mine & 127
            for c in range(chan // 8):
                rows = slice(8 * c, 8 * c + 8)
                feat = None
                for chunk in range(n_near // LANES):
                    held = hid_ref[rows, chunk * LANES : (chunk + 1) * LANES]
                    got = jnp.take_along_axis(held, place, axis=1, mode="promise_in_bounds")
                    feat = got if feat is None else jnp.where(chunk_no == chunk, got, feat)
                hj_ref[rows, at] = feat
                car_ref[rows, at] = feat * w_ref[rows, at]
        feat = both[:chan] + (both[chan : 2 * chan] + both[2 * chan :])
        hj_ref[:, here] = feat
        car_ref[:, here] = feat * w_ref[:, here]


def moment_kernel(car_ref, yb_ref, mixa_ref, mixt_ref, side_ref, m2_ref, dinv_ref, inv_ref):
    slots = yb_ref.shape[1]
    chan, atoms = m2_ref.shape[1:]
    tiles = atoms // LANES
    wide_cols = 2 * LANES
    rows = 32
    groups = chan // rows

    def moments(step):
        t = step // groups
        c = step % groups
        cols = pl.ds(pl.multiple_of(t * LANES, LANES), LANES)
        base = pl.multiple_of(c * rows, rows)
        acc = [[None] * ORDERS for _ in range(rows // 8)]
        for k in range(slots):
            at = pl.ds(pl.multiple_of(k * atoms + t * LANES, LANES), LANES)
            got = car_ref[pl.ds(base, rows), at]
            for l in range(ORDERS):
                yb = yb_ref[l - 1, k, :, cols] if l else None
                for h in range(rows // 8):
                    part = got[8 * h : 8 * h + 8]
                    term = part * yb if l else part
                    acc[h][l] = term if acc[h][l] is None else acc[h][l] + term
        for h in range(rows // 8):
            inv = [None] * 3
            for l in range(ORDERS):
                m2_ref[l, pl.ds(pl.multiple_of(base + 8 * h, 8), 8), cols] = acc[h][l]
                sq = acc[h][l] * acc[h][l]
                g = GROUP[l]
                inv[g] = sq if inv[g] is None else inv[g] + sq
            for g in range(3):
                inv_ref[pl.ds(pl.multiple_of(g * chan + base + 8 * h, 8), 8), cols] = inv[g]

    in_turns(0, tiles * groups, moments, 2)
    read2_col = side_ref[:, 3:4]
    for t in range(atoms // wide_cols):
        cols = slice(t * wide_cols, (t + 1) * wide_cols)
        _, slope = silu_parts(dot(mixa_ref[1], six_deep(inv_ref[:, cols])))
        slope = three_deep(slope * (2.0 * read2_col))
        for g, scale in enumerate((1.0, 0.5 * SQRT3, 0.5 * SQRT15)):
            dinv_ref[g * chan : (g + 1) * chan, cols] = scale * dot(mixt_ref[1, g], slope)


def back_second_kernel(m2_ref, dinv_ref, car_ref, hj_ref, w_ref, slope_ref, ub_ref, dhe_ref, p_ref):
    slots = ub_ref.shape[1]
    chan, atoms = m2_ref.shape[1:]
    tiles = atoms // LANES
    pairs = chan // 16
    per_turn = 4 if pairs % 4 == 0 else 1
    k_step = slots // 2

    def back_moments(t, carry):
        cols = pl.ds(pl.multiple_of(t * LANES, LANES), LANES)

        def one(c, acc, k0):
            forms = []
            for h in range(2):
                rows = pl.ds(pl.multiple_of(c * 16 + 8 * h, 8), 8)
                scale = [dinv_ref[pl.ds(pl.multiple_of(g * chan + c * 16 + 8 * h, 8), 8), cols] for g in range(3)]
                dm = [m2_ref[l, rows, cols] * scale[GROUP[l]] for l in range(ORDERS)]
                low = dm[6] * (1.0 / SQRT3)
                forms.append((dm[0], dm[1], dm[2], dm[3], dm[8] - low, -dm[8] - low, low + low, dm[4], dm[5], dm[7]))
            base = pl.multiple_of(c * 16, 16)
            for k in range(k0, k0 + k_step):
                at = pl.ds(pl.multiple_of(k * atoms + t * LANES, LANES), LANES)
                got = car_ref[pl.ds(base, 16), at]
                stretch = hj_ref[pl.ds(base, 16), at] * slope_ref[pl.ds(base, 16), at]
                ux, uy, uz = [ub_ref[i, k, :, cols] for i in range(3)]
                out = []
                for h in range(2):
                    mid, dx, dy, dz, qxx, qyy, qzz, qxy, qyz, qxz = forms[h]
                    gx = dx + qxx * ux + qxy * uy + qxz * uz
                    gy = dy + qxy * ux + qyy * uy + qyz * uz
                    gz = dz + qxz * ux + qyz * uy + qzz * uz
                    out.append(mid + (gx + dx) * ux + (gy + dy) * uy + (gz + dz) * uz)
                    part = got[8 * h : 8 * h + 8]
                    at_acc = 4 * (k - k0)
                    for i, g in enumerate((gx, gy, gz)):
                        acc[at_acc + i] = acc[at_acc + i] + part * g
                    acc[at_acc + 3] = acc[at_acc + 3] + out[h] * stretch[8 * h : 8 * h + 8]
                hi, lo = split(jnp.concatenate(out, axis=0) * w_ref[pl.ds(base, 16), at])
                dhe_ref[pl.ds(base, 16), at] = hi
                dhe_ref[pl.ds(pl.multiple_of(chan + c * 16, 16), 16), at] = lo

        for k0 in range(0, slots, k_step):

            def over(c, acc, k0=k0):
                acc = list(acc)
                for i in range(per_turn):
                    one(per_turn * c + i, acc, k0)
                return tuple(acc)

            start = tuple(jnp.zeros((8, LANES), f32) for _ in range(4 * k_step))
            acc = lax.fori_loop(0, pairs // per_turn, over, start)
            for k in range(k_step):
                for i in range(4):
                    p_ref[i, 8 * (k0 + k) : 8 * (k0 + k) + 8, cols] = acc[4 * k + i]
        return carry

    lax.fori_loop(0, tiles, back_moments, 0)


def scatter_kernel(oh_ref, pick_ref, dhe_ref, side_ref, p_ref, gidx_ref, dh_ref, q_ref, ohlo_ref):
    chan, n_near = dh_ref.shape
    slots = gidx_ref.shape[0]
    atoms = pick_ref.shape[1]
    half = atoms // 2
    both = dot_nt(dhe_ref[...], jnp.concatenate([oh_ref[:half], oh_ref[half + atoms :]], axis=0))
    hi, lo = split(both[:chan] + both[chan:])
    spread = dot_nt(jnp.concatenate([hi, lo], axis=0), pick_ref[...])
    spread = spread[:chan] + spread[chan:]
    both = dot_nt(dhe_ref[...], oh_ref[half : half + atoms])
    dh_ref[:, 0:atoms] = spread[:, :atoms] + both[:chan] + both[chan:] + side_ref[:, 2:3]
    if n_near > atoms:
        dh_ref[:, atoms:] = spread[:, atoms:]
    ids16 = lax.broadcasted_iota(jnp.int32, (LANES, n_near), 0).astype(jnp.int16)
    one16 = jnp.ones((LANES, n_near), bf16)
    zero16 = jnp.zeros((LANES, n_near), bf16)
    for k in range(slots):
        place = jnp.broadcast_to(gidx_ref[k : k + 1, :] & 127, (LANES, n_near)).astype(jnp.int16)
        ohlo_ref[:, k * n_near : (k + 1) * n_near] = jnp.where(place == ids16, one16, zero16)
    lane = lax.broadcasted_iota(jnp.int32, (slots, 16 * slots), 1)
    sub = lax.broadcasted_iota(jnp.int32, (slots, 16 * slots), 0)
    adder = jnp.where(((lane >> 3) & (slots - 1)) == sub, 1.0, 0.0).astype(bf16)
    for i in range(4):
        total = dot(adder, split_rows(p_ref[i]).astype(bf16))
        q_ref[8 * i : 8 * i + 8, :] = 2.0 * total if i < 3 else total


def back_first_kernel(dh_ref, sp1_ref, m1_ref, mixt_ref, rrr_ref, da_ref):
    n_near = sp1_ref.shape[1]
    rows = rrr_ref.shape[0] // 2
    wide_cols = 2 * LANES

    def back_first(j):
        here = pl.ds(pl.multiple_of(j * wide_cols, wide_cols), wide_cols)
        slope = three_deep(dh_ref[:, here] * sp1_ref[:, here] * 2.0)
        scale = [dot(mixt_ref[0, g], slope) for g in range(3)]
        for l in range(ORDERS):
            hi, lo = split(m1_ref[l, :, here] * scale[GROUP[l]])
            out = dot(rrr_ref[...], jnp.concatenate([hi, lo], axis=0))
            da_ref[l, :, here] = out[:rows] + out[rows:]

    in_turns(0, n_near // wide_cols, back_first)


def back_edge_kernel(plan, *refs):
    atoms, near, wide, _, _ = plan
    n_wide = len(wide)
    blocks = refs[:n_wide]
    moment_src, geo_ref, y_ref, bk_ref, gidx_ref, da_ref, q_ref, ohlo_ref = refs[n_wide : n_wide + 8]
    push_ref, mass_ref, val_ref, dr_ref, moment_ref, sem = refs[n_wide + 8 :]
    fetch = pltpu.make_async_copy(moment_src, moment_ref, sem)
    fetch.start()
    bases, slots, n_near = bk_ref.shape
    tiles = atoms // LANES
    top_rows = val_ref.shape[0] // 6

    def back_geometry(t, mine):
        here = pl.ds(pl.multiple_of(t * LANES, LANES), LANES)
        ux, uy, uz, back, soft, fj = [geo_ref[i, :, here] for i in range(6)]
        dy = [None] * ORDERS
        ds = None
        for n in range(bases):
            basis = bk_ref[n, :, here]
            db = None
            for l in range(ORDERS):
                g = row(da_ref[l, n : n + 1, here]) + fj * row(da_ref[l, bases + n : bases + n + 1, here])
                if l:
                    dy[l] = g * basis if dy[l] is None else dy[l] + g * basis
                    db = db + g * y_ref[l - 1, :, here]
                else:
                    db = g
            db = db * basis * ((1.0 + n) - soft)
            ds = db if ds is None else ds + db
        if mine:
            ds = ds + q_ref[24:32, here]
        dux = SQRT3 * dy[1] + SQRT15 * (uy * dy[4] + uz * dy[7] + ux * dy[8]) - SQRT5 * ux * dy[6]
        duy = SQRT3 * dy[2] + SQRT15 * (ux * dy[4] + uz * dy[5] - uy * dy[8]) - SQRT5 * uy * dy[6]
        duz = SQRT3 * dy[3] + SQRT15 * (uy * dy[5] + ux * dy[7]) + 2.0 * SQRT5 * uz * dy[6]
        if mine:
            dux, duy, duz = [d + q_ref[8 * i : 8 * i + 8, here] for i, d in enumerate((dux, duy, duz))]
        along = ds - (ux * dux + uy * duy + uz * duz) * back
        for i, value in enumerate((dux * back + along * ux, duy * back + along * uy, duz * back + along * uz)):
            dr_ref[i, :, here] = value

    in_turns(0, tiles, lambda t: back_geometry(t, True))
    in_turns(tiles, n_near // LANES, lambda t: back_geometry(t, False))

    def place_tile(t):
        here = pl.ds(pl.multiple_of(t * LANES, LANES), LANES)
        gidx = gidx_ref[:, here]
        chunk_no = gidx >> 7
        parts = []
        for i in range(3):
            value = dr_ref[i, :, here]
            hi = value.astype(bf16).astype(f32)
            parts.append((hi, value - hi))
        chunk_ids = lax.broadcasted_iota(jnp.int32, (top_rows, LANES), 0)
        for k in range(slots):
            at = pl.ds(pl.multiple_of(k * n_near + t * LANES, LANES), LANES)
            hit = chunk_ids == row(chunk_no[k : k + 1, :], top_rows)
            for i in range(3):
                both = [jnp.where(hit, row(part[k : k + 1, :], top_rows), 0.0) for part in parts[i]]
                val_ref[2 * i * top_rows : 2 * (i + 1) * top_rows, at] = jnp.concatenate(both, axis=0).astype(bf16)

    in_turns(0, n_near // LANES, place_tile)
    landed = dot_nt(val_ref[...], ohlo_ref[...])
    fetch.wait()
    lines = push_ref.shape[0] // (n_wide + 1)
    for i in range(3):
        total = (
            landed[2 * i * top_rows : (2 * i + 1) * top_rows] + landed[(2 * i + 1) * top_rows : (2 * i + 2) * top_rows]
        )
        for g in range(n_wide):
            for t in range(tiles):
                cols = slice(t * LANES, (t + 1) * LANES)
                line = total[g * tiles + t : g * tiles + t + 1, :]
                if g < len(near):
                    here = slice(g * atoms + t * LANES, g * atoms + (t + 1) * LANES)
                    line = line - jnp.sum(dr_ref[i, :, here], axis=0, keepdims=True)
                line = -HALF_STEP * line
                at = i * tiles + t
                if g == 0:
                    line = line + moment_ref[i, :, cols]
                    push_ref[at : at + 1, :] = blocks[0][i : i + 1, cols]
                push_ref[(1 + g) * lines + at : (1 + g) * lines + at + 1, :] = line
                mass = HEAVY - (HEAVY - 1.0) * blocks[g][3:4, cols]
                mass_ref[g * lines + at : g * lines + at + 1, :] = mass


def in_hbm(x):
    return pltpu.with_memory_space_constraint(x, pltpu.HBM)


def run(name, body, operands, results, scratch=(), far=(), cost=None):
    sizes = [math.prod(x.shape) * x.dtype.itemsize // 2 for i, x in enumerate(operands) if i not in far]
    sizes += [math.prod(shape) * jnp.dtype(dtype).itemsize for shape, dtype in results]
    sizes += [math.prod(x.shape) * x.dtype.itemsize for x in scratch if x.memory_space == pltpu.VMEM]
    limit = sum(sizes) + 4 * MIB
    specs = [pl.BlockSpec(memory_space=pltpu.HBM if i in far else pltpu.VMEM) for i in range(len(operands))]
    return pl.pallas_call(
        body,
        out_shape=tuple(jax.ShapeDtypeStruct(shape, dtype) for shape, dtype in results),
        in_specs=specs,
        out_specs=tuple(pl.BlockSpec(memory_space=pltpu.VMEM) for _ in results),
        scratch_shapes=list(scratch),
        compiler_params=pltpu.CompilerParams(vmem_limit_bytes=limit),
        cost_estimate=cost,
        name=name,
    )(*[in_hbm(x) if i in far else x for i, x in enumerate(operands)])


def choose(block, embedding, radial_one, radial_two, mix_one, mix_two, read_one, read_two):
    atoms = block.shape[1]
    slots = block.shape[0] - HEAD
    chan = embedding.shape[1]
    bases = radial_one.shape[0]
    weights = (embedding, radial_one, radial_two, mix_one, mix_two, read_one[None], read_two[None])
    return run(
        "choose",
        choose_kernel,
        (block, *weights),
        (
            ((2 * atoms, slots * atoms), bf16),
            ((chan, 12 * bases), bf16),
            ((chan, 6 * bases), bf16),
            ((chan, LANES), f32),
            ((4 * bases, 2 * chan), bf16),
            ((2, chan, 18 * chan), bf16),
            ((2, 3, chan, 3 * chan), bf16),
        ),
        [pltpu.VMEM(w.shape, f32) for w in weights] + [pltpu.SemaphoreType.DMA((len(weights),))],
        range(1, 1 + len(weights)),
        cost=pl.CostEstimate(flops=2 * 10**9, bytes_accessed=2 * 10**6, transcendentals=0),
    )


def pushes(plan, blocks, momenta, chosen):
    atoms, near, wide, _, _ = plan
    oh, rrc, r2c, sides, rrr, mixa, mixt = chosen
    chan = rrc.shape[0]
    bases = rrr.shape[0] // 4
    slots = blocks[0].shape[0] - HEAD
    n_near = len(near) * atoms
    edges = slots * atoms
    top_rows = -(-len(wide) * atoms // LANES // 8) * 8
    lines = line_count(atoms)
    geo, y, yb, ub, bk, bt, gidx, pick, as1 = run(
        "edges",
        functools.partial(edge_kernel, plan),
        blocks,
        (
            ((6, slots, n_near), f32),
            ((ORDERS - 1, slots, n_near), f32),
            ((ORDERS - 1, slots, 8, atoms), f32),
            ((3, slots, 8, atoms), f32),
            ((bases, slots, n_near), f32),
            ((slots, 2 * bases, n_near), f32),
            ((slots, n_near), jnp.int32),
            ((n_near, atoms), bf16),
            ((ORDERS, 12 * bases, n_near), bf16),
        ),
    )
    m1, sp1, hid, hs = run(
        "first",
        functools.partial(first_kernel, plan),
        (*blocks, as1, rrc, sides, mixa),
        (((ORDERS, chan, n_near), f32), ((chan, n_near), f32), ((chan, n_near), f32), ((3 * chan, n_near), bf16)),
        [pltpu.VMEM((8, n_near), f32)],
    )
    hj, w, slope, car = run(
        "gather",
        gather_kernel,
        (hid, hs, oh, pick, gidx, bt, geo, r2c),
        (((chan, edges), f32),) * 4,
        [pltpu.VMEM((3 * chan, 2 * atoms), bf16)],
    )
    m2, dinv = run(
        "moments",
        moment_kernel,
        (car, yb, mixa, mixt, sides),
        (((ORDERS, chan, atoms), f32), ((3 * chan, atoms), f32)),
        [pltpu.VMEM((3 * chan, atoms), f32)],
    )
    dhe, p = run(
        "back_second",
        back_second_kernel,
        (m2, dinv, car, hj, w, slope, ub),
        (((2 * chan, edges), bf16), ((4, 8 * slots, atoms), f32)),
    )
    dh, q, ohlo = run(
        "scatter",
        scatter_kernel,
        (oh, pick, dhe, sides, p, gidx),
        (((chan, n_near), f32), ((4 * slots, atoms), f32), ((LANES, slots * n_near), bf16)),
    )
    (da,) = run("back_first", back_first_kernel, (dh, sp1, m1, mixt, rrr), (((ORDERS, 2 * bases, n_near), f32),))
    return run(
        "back_edges",
        functools.partial(back_edge_kernel, plan),
        (*blocks, momenta, geo, y, bk, gidx, da, q, ohlo),
        ((((len(wide) + 1) * lines, LANES), f32), ((len(wide) * lines, LANES), f32)),
        [
            pltpu.VMEM((6 * top_rows, slots * n_near), bf16),
            pltpu.VMEM((3, slots, n_near), f32),
            pltpu.VMEM(momenta.shape, f32),
            pltpu.SemaphoreType.DMA(()),
        ],
        (len(blocks),),
    )


def line_count(atoms):
    return 3 * (atoms // LANES)


def ring_plan(domains, atoms):
    near = list(dict.fromkeys(o % domains for o in (0, 1, -1)))
    wide = list(dict.fromkeys(near + [o % domains for o in (2, -2)]))
    before = tuple(wide.index((o - 1) % domains) for o in near)
    after = tuple(wide.index((o + 1) % domains) for o in near)
    return atoms, tuple(near), tuple(wide), before, after


def mode_turns(bead_total):
    bead = np.arange(bead_total, dtype=np.float64)[:, None]
    mode = np.arange(bead_total, dtype=np.float64)[None, :]
    phase = 2.0 * np.pi * bead * mode / bead_total
    half_total = bead_total // 2
    table = math.sqrt(2.0 / bead_total) * np.where(mode < half_total, np.cos(phase), np.sin(phase))
    table = np.where(mode == half_total, np.cos(np.pi * bead) / math.sqrt(bead_total), table)
    table = np.where(mode == 0, 1.0 / math.sqrt(bead_total), table)
    angles = bead_total * np.sin(np.pi * mode[0] / bead_total)
    safe = np.where(mode[0] == 0, 1.0, angles)
    reach = np.where(mode[0] == 0, STEP, STEP * np.sin(angles) / safe)
    stiff = angles * np.sin(angles) / STEP
    return [[float(x) for x in (table * factor[None, :]) @ table[0]] for factor in (np.cos(angles), reach, stiff)]


def pack_kernel(coord_src, species_src, send_src, slot_src, block_ref, coord_ref, species_ref, send_ref, slot_ref, sems):
    pairs = ((coord_src, coord_ref), (species_src, species_ref), (send_src, send_ref), (slot_src, slot_ref))
    fetches = [pltpu.make_async_copy(src, dst, sems.at[i]) for i, (src, dst) in enumerate(pairs)]
    for fetch in fetches:
        fetch.start()
    for fetch in fetches:
        fetch.wait()
    atoms = block_ref.shape[1]
    for i in range(3):
        block_ref[i : i + 1, :] = coord_ref[i]
    block_ref[3:4, :] = species_ref[...].astype(f32)
    block_ref[4:5, :] = send_ref[...].astype(f32)
    block_ref[5:HEAD, :] = jnp.zeros((HEAD - 5, atoms), f32)
    block_ref[HEAD:, :] = slot_ref[...].astype(f32)


def turn_kernel(shape, bead_ref, domain_ref, mass_ref, *refs):
    outer, inner, domains, wide = shape
    message_ref = refs[outer]
    turns = mode_turns(outer * inner)
    lines = mass_ref.shape[0] // len(wide)
    my_domain = domain_ref[0]
    my_inner = lax.rem(bead_ref[0], inner)
    if domains > len(wide):
        message_ref[...] = jnp.zeros_like(message_ref)
    masses = [mass_ref[g * lines : (g + 1) * lines, :] for g in range(len(wide))]
    sources = []
    for z in range(outer):
        sources.append([refs[z][g * lines : (g + 1) * lines, :] for g in range(len(wide) + 1)])
    for s in range(inner):
        wraps = jnp.full((lines, LANES), my_inner + s) >= inner
        weights = []
        for turn in turns:
            row_of = []
            for z in range(outer):
                there = turn[(z * inner + s) % (outer * inner)]
                round_it = turn[(z * inner + s - inner) % (outer * inner)]
                row_of.append(jnp.where(wraps, jnp.full((lines, LANES), round_it), jnp.full((lines, LANES), there)))
            weights.append(row_of)
        to_inner = lax.rem(my_inner + s, inner)
        for g in range(len(wide)):
            turned = sum(weights[0][z] * sources[z][1 + g] for z in range(outer))
            drift = sum(weights[1][z] * sources[z][1 + g] for z in range(outer))
            new_q = drift / masses[g]
            new_p = turned
            if g == 0:
                new_q = new_q + sum(weights[0][z] * sources[z][0] for z in range(outer))
                new_p = new_p - masses[g] * sum(weights[2][z] * sources[z][0] for z in range(outer))
            to = to_inner * domains + lax.rem(my_domain + wide[g], domains)
            message_ref[to, 0:lines, :] = new_q
            message_ref[to, lines:, :] = new_p


def sum_kernel(arrived_ref, q_ref, p_ref):
    total = arrived_ref[0]
    for i in range(1, arrived_ref.shape[0]):
        total = total + arrived_ref[i]
    lines = total.shape[0] // 2
    tiles = q_ref.shape[2] // LANES
    for i in range(3):
        for t in range(tiles):
            at = i * tiles + t
            q_ref[i, :, t * LANES : (t + 1) * LANES] = total[at : at + 1]
            p_ref[i, :, t * LANES : (t + 1) * LANES] = total[lines + at : lines + at + 1]


def shards(
    positions, momenta, species, neighbours, send_list, embedding, radial_one, radial_two, mix_one, mix_two,
    read_one, read_two,
):
    slots, atoms = neighbours.shape
    domains = lax.axis_size("space")
    beads = lax.axis_size("bead")
    inner = next(d for d in range(1, beads + 1) if beads % d == 0 and d * d >= beads)
    outer = beads // inner
    plan = ring_plan(domains, atoms)
    wide = plan[2]
    vmem = pl.BlockSpec(memory_space=pltpu.VMEM)
    smem = pl.BlockSpec(memory_space=pltpu.SMEM)
    far = pl.BlockSpec(memory_space=pltpu.HBM)
    small = pltpu.CompilerParams(vmem_limit_bytes=4 * MIB)
    coord_rows = jnp.transpose(positions, (1, 0, 2))
    moment_rows = jnp.transpose(momenta, (1, 0, 2))
    block = pl.pallas_call(
        pack_kernel,
        out_shape=jax.ShapeDtypeStruct((HEAD + slots, atoms), f32),
        in_specs=[far] * 4,
        out_specs=vmem,
        scratch_shapes=[
            pltpu.VMEM(coord_rows.shape, f32),
            pltpu.VMEM((1, atoms), jnp.int32),
            pltpu.VMEM((1, atoms), jnp.int32),
            pltpu.VMEM((slots, atoms), jnp.int32),
            pltpu.SemaphoreType.DMA((4,)),
        ],
        compiler_params=small,
        name="pack",
    )(in_hbm(coord_rows), in_hbm(species[None]), in_hbm(send_list[None]), in_hbm(neighbours))
    blocks = [block]
    for offset in wide[1:]:
        blocks.append(lax.ppermute(block, "space", [(i, (i - offset) % domains) for i in range(domains)]))
    chosen = choose(block, embedding, radial_one, radial_two, mix_one, mix_two, read_one, read_two)
    pushed, masses = pushes(plan, blocks, moment_rows, chosen)
    sources = [pushed]
    for z in range(1, outer):
        sources.append(lax.ppermute(pushed, "bead", [(b, (b + z * inner) % beads) for b in range(beads)]))
    here = [lax.axis_index(axis).astype(jnp.int32).reshape(1) for axis in ("bead", "space")]
    lines = line_count(atoms)
    messages = pl.pallas_call(
        functools.partial(turn_kernel, (outer, inner, domains, wide)),
        out_shape=jax.ShapeDtypeStruct((inner * domains, 2 * lines, LANES), f32),
        in_specs=[smem, smem, vmem] + [vmem] * outer,
        out_specs=vmem,
        compiler_params=small,
        name="turn",
    )(*here, masses, *sources)
    rows = [[z * inner * domains + i for i in range(inner * domains)] for z in range(outer)]
    arrived = lax.all_to_all(messages, ("bead", "space"), 0, 0, axis_index_groups=rows, tiled=True)
    new_q, new_p = pl.pallas_call(
        sum_kernel,
        out_shape=(jax.ShapeDtypeStruct((3, 1, atoms), f32),) * 2,
        in_specs=[vmem],
        out_specs=(vmem, vmem),
        compiler_params=small,
        name="sum",
    )(arrived)
    return (jnp.transpose(new_q, (1, 0, 2)), jnp.transpose(new_p, (1, 0, 2)))


def solution(mesh):
    placed = (
        P("bead", None, "space"),
        P("bead", None, "space"),
        P("space"),
        P(None, "space"),
        P("space"),
        P(),
        P(),
        P(),
        P(),
        P(),
        P(),
        P(),
    )
    return jax.shard_map(
        shards,
        mesh=mesh,
        in_specs=placed,
        out_specs=(P("bead", None, "space"), P("bead", None, "space")),
        check_vma=False,
    )
```

```python
import functools
import math

import jax
import jax.numpy as jnp
import numpy as np
from jax import lax
from jax.experimental import pallas as pl
from jax.experimental.pallas import tpu as pltpu
from jax.sharding import PartitionSpec as P

STEP = 2.0
HALF_STEP = 1.0
HEAVY = 16.0
SQRT3 = math.sqrt(3.0)
SQRT5 = math.sqrt(5.0)
SQRT15 = math.sqrt(15.0)
LANES = 128
ORDERS = 9
GROUP = (0, 1, 1, 1, 2, 2, 2, 2, 2)
HEAD = 8
MIB = 1024 * 1024
f32 = jnp.float32
bf16 = jnp.bfloat16


def split(x):
    hi = x.astype(bf16)
    return hi, (x - hi.astype(f32)).astype(bf16)


def split_rows(x):
    hi = x.astype(bf16).astype(f32)
    return jnp.concatenate([hi, x - hi], axis=0)


def split3(x):
    hi = x.astype(bf16)
    rest = x - hi.astype(f32)
    mid = rest.astype(bf16)
    return hi, mid, (rest - mid.astype(f32)).astype(bf16)


def six_rows(x, order):
    hi = x.astype(bf16).astype(f32)
    mid = (x - hi).astype(bf16).astype(f32)
    parts = (hi, mid, x - hi - mid)
    return jnp.concatenate([parts[i] for i in order], axis=0)


VALUE_ORDER = (0, 1, 0, 1, 2, 0)
WEIGHT_ORDER = (0, 0, 1, 1, 0, 2)


def dot(a, b):
    return jnp.dot(a, b, preferred_element_type=f32)


def dot_nt(a, b):
    return lax.dot_general(a, b, (((1,), (1,)), ((), ())), preferred_element_type=f32)


def in_turns(start, stop, step, most=4):
    per_turn = next(n for n in range(most, 0, -1) if (stop - start) % n == 0)

    def turn(i, carry):
        for j in range(per_turn):
            step(start + i * per_turn + j)
        return carry

    lax.fori_loop(0, (stop - start) // per_turn, turn, 0)


def row(x, rows=8):
    return jnp.broadcast_to(x, (rows, x.shape[1]))


def lookup(chunks, wanted, position):
    out = None
    for number, chunk in chunks:
        got = jnp.take_along_axis(row(chunk), position, axis=1, mode="promise_in_bounds")
        out = got if out is None else jnp.where(wanted == number, got, out)
    return out


def harmonics(ux, uy, uz):
    return [
        None,
        SQRT3 * ux,
        SQRT3 * uy,
        SQRT3 * uz,
        SQRT15 * ux * uy,
        SQRT15 * uy * uz,
        0.5 * SQRT5 * (2.0 * uz * uz - ux * ux - uy * uy),
        SQRT15 * ux * uz,
        0.5 * SQRT15 * (ux * ux - uy * uy),
    ]


def silu_parts(v):
    gate = 1.0 / (1.0 + jnp.exp(-v))
    return v * gate, gate * (1.0 + v * (1.0 - gate))


def choose_kernel(block_ref, *refs):
    sources = refs[:7]
    oh_ref, rrc_ref, r2c_ref, side_ref, rrr_ref, mixa_ref, mixt_ref = refs[7:14]
    held = refs[14:21]
    sems = refs[21]
    emb_ref, rad1_ref, rad2_ref, mix1_ref, mix2_ref, read1_ref, read2_ref = held
    fetches = [pltpu.make_async_copy(src, dst, sems.at[i]) for i, (src, dst) in enumerate(zip(sources, held))]
    for fetch in fetches:
        fetch.start()
    chan = emb_ref.shape[1]
    bases = rad1_ref.shape[0]
    atoms = block_ref.shape[1]
    slots = block_ref.shape[0] - HEAD

    ids16 = lax.broadcasted_iota(jnp.int32, (LANES, atoms), 0).astype(jnp.int16)
    one16 = jnp.ones((LANES, atoms), bf16)
    zero16 = jnp.zeros((LANES, atoms), bf16)
    for k in range(slots):
        slot = block_ref[HEAD + k : HEAD + k + 1, :].astype(jnp.int32)
        wanted = jnp.broadcast_to(slot, (LANES, atoms)).astype(jnp.int16)
        for r in range(oh_ref.shape[0] // LANES):
            hit = wanted - jnp.int16(r * LANES) == ids16
            oh_ref[r * LANES : (r + 1) * LANES, k * atoms : (k + 1) * atoms] = jnp.where(hit, one16, zero16)

    for fetch in fetches:
        fetch.wait()
    emb0 = emb_ref[0:1, :]
    emb_d = emb_ref[1:2, :] - emb0
    rr = jnp.concatenate([rad1_ref[...] * emb0, rad1_ref[...] * emb_d], axis=0) * (1.0 / slots)
    rr_hi = rr.astype(bf16).astype(f32)
    rr_lo = rr - rr_hi
    r2 = rad2_ref[...] * (1.0 / slots)
    zeros = jnp.zeros((8, chan), f32)
    turned1 = jnp.concatenate([six_rows(rr, WEIGHT_ORDER)] + [zeros] * (16 - 12 * bases // 8), axis=0).T
    sides = jnp.concatenate([emb0, emb_d, read1_ref[...], read2_ref[...], zeros[:4]], axis=0)
    turned2 = jnp.concatenate([six_rows(r2, WEIGHT_ORDER)] + [zeros] * (16 - 6 * bases // 8), axis=0).T
    rrc_ref[...] = turned1[:, : 12 * bases].astype(bf16)
    r2c_ref[...] = turned2[:, : 6 * bases].astype(bf16)
    side_ref[...] = jnp.concatenate([sides] + [zeros] * 15, axis=0).T
    rrr_ref[...] = jnp.concatenate(
        [jnp.concatenate([rr_hi, rr_hi], axis=1), jnp.concatenate([rr_lo, jnp.zeros_like(rr_lo)], axis=1)], axis=0
    ).astype(bf16)
    for i, ref in enumerate((mix1_ref, mix2_ref)):
        hi, mid, lo = split3(ref[...])
        for at, pair in enumerate(((hi, hi), (mid, mid), (hi, lo))):
            mixa_ref[i, at * chan : (at + 1) * chan, :] = jnp.concatenate(pair, axis=1)
        for g in range(3):
            hi, lo = split(ref[:, g * chan : (g + 1) * chan].T)
            mixt_ref[i, g * chan : (g + 1) * chan, :] = jnp.concatenate([hi, hi, lo], axis=1)


def mixed(weights, x):
    hi, mid, lo = split3(x)
    rows = weights.shape[0] // 3
    large = dot(weights[: 2 * rows], jnp.concatenate([hi, mid], axis=0))
    small = dot(weights[2 * rows :], jnp.concatenate([lo, hi], axis=0))
    return large[:rows] + (large[rows:] + small)


def three_deep(x):
    hi, lo = split(x)
    return jnp.concatenate([hi, lo, hi], axis=0)


def edge_kernel(plan, *refs):
    atoms, near, wide, before, after = plan
    n_wide = len(wide)
    blocks = refs[:n_wide]
    geo_ref, y_ref, yb_ref, ub_ref, bk_ref, bt_ref, gidx_ref, pick_ref, as_ref = refs[n_wide:]
    bases = bk_ref.shape[0]
    slots = gidx_ref.shape[0]
    tiles = atoms // LANES
    half = atoms // 2
    half_tiles = half // LANES
    order_col = lax.broadcasted_iota(jnp.int32, (bases, LANES), 0).astype(f32)
    tables = []
    for quantity in range(4):
        chunks = []
        for g in range(n_wide):
            for t in range(tiles):
                chunks.append((g * tiles + t, blocks[g][quantity : quantity + 1, t * LANES : (t + 1) * LANES]))
        tables.append(chunks)
    for q in range(len(near)):
        ghosts = []
        for t in range(half_tiles):
            ghosts.append(
                (t, blocks[before[q]][4:5, half + t * LANES : half + (t + 1) * LANES] + float(before[q] * atoms))
            )
        for t in range(half_tiles):
            ghosts.append(
                (
                    half_tiles + tiles + t,
                    blocks[after[q]][4:5, t * LANES : (t + 1) * LANES] + float(after[q] * atoms),
                )
            )
        if q == 0:
            ids16 = lax.broadcasted_iota(jnp.int32, (pick_ref.shape[0], LANES), 0).astype(jnp.int16)
            one16 = jnp.ones(ids16.shape, bf16)
            zero16 = jnp.zeros(ids16.shape, bf16)
            for t, (_, chunk) in enumerate(ghosts):
                wanted = jnp.broadcast_to(chunk.astype(jnp.int32), ids16.shape).astype(jnp.int16)
                pick_ref[:, t * LANES : (t + 1) * LANES] = jnp.where(wanted == ids16, one16, zero16)
        for t in range(tiles):
            cols = slice(t * LANES, (t + 1) * LANES)
            here = slice(q * atoms + t * LANES, q * atoms + (t + 1) * LANES)
            slot = blocks[q][HEAD : HEAD + slots, cols].astype(jnp.int32)
            chunk_no = slot >> 7
            far = lookup(ghosts, chunk_no, slot & 127).astype(jnp.int32)
            own = (slot >= half) & (slot < half + atoms)
            gidx = jnp.where(own, slot + (q * atoms - half), far)
            gidx_ref[:, here] = gidx
            chunk_no = gidx >> 7
            place = gidx & 127
            xj, yj, zj, fj = [lookup(tables[i], chunk_no, place) for i in range(4)]
            rx = xj - row(blocks[q][0:1, cols])
            ry = yj - row(blocks[q][1:2, cols])
            rz = zj - row(blocks[q][2:3, cols])
            soft = jnp.sqrt(rx * rx + ry * ry + rz * rz + 1.0)
            back = 1.0 / soft
            ux, uy, uz = rx * back, ry * back, rz * back
            for i, value in enumerate((ux, uy, uz, back, soft, fj)):
                geo_ref[i, :, here] = value
            if q == 0:
                for i, value in enumerate((ux, uy, uz)):
                    for k in range(slots):
                        ub_ref[i, k, :, cols] = row(value[k : k + 1, :])
            sphere = harmonics(ux, uy, uz)
            for l in range(1, ORDERS):
                y_ref[l - 1, :, here] = sphere[l]
                if q == 0:
                    for k in range(slots):
                        yb_ref[l - 1, k, :, cols] = row(sphere[l][k : k + 1, :])
            for n in range(bases):
                bk_ref[n, :, here] = jnp.exp(-0.5 * (soft - (1.0 + n)) ** 2)
            for k in range(slots):
                basis = jnp.exp(-0.5 * (row(soft[k : k + 1, :], bases) - (1.0 + order_col)) ** 2)
                bt_ref[k, 0:bases, here] = basis
                bt_ref[k, bases : 2 * bases, here] = basis * row(fj[k : k + 1, :], bases)
            low = [None] * ORDERS
            for k in range(slots):
                basis = bt_ref[k, :, here]
                for l in range(ORDERS):
                    term = basis if l == 0 else basis * row(y_ref[l - 1, k : k + 1, here], 2 * bases)
                    low[l] = term if low[l] is None else low[l] + term
            for l in range(ORDERS):
                as_ref[l, :, here] = six_rows(low[l], VALUE_ORDER).astype(bf16)


def first_kernel(plan, *refs):
    atoms, near, wide, _, _ = plan
    n_wide = len(wide)
    blocks = refs[:n_wide]
    as_ref, rrc_ref, side_ref, mixa_ref, m1_ref, sp1_ref, hid_ref, hs_ref, flag_ref = refs[n_wide:]
    chan = m1_ref.shape[1]
    n_near = m1_ref.shape[2]

    for q in range(len(near)):
        flag_ref[0:1, q * atoms : (q + 1) * atoms] = blocks[q][3:4, :]
    wide_cols = 2 * LANES
    emb0_col = side_ref[:, 0:1]
    embd_col = side_ref[:, 1:2]

    def first(j):
        here = pl.ds(pl.multiple_of(j * wide_cols, wide_cols), wide_cols)
        inv = [None, None, None]
        for l in range(ORDERS):
            m = dot(rrc_ref[...], as_ref[l, :, here])
            m1_ref[l, :, here] = m
            inv[GROUP[l]] = m * m if inv[GROUP[l]] is None else inv[GROUP[l]] + m * m
        value = mixed(mixa_ref[0], jnp.concatenate(inv, axis=0))
        act, slope = silu_parts(value)
        sp1_ref[:, here] = slope
        hidden = act + emb0_col + embd_col * flag_ref[0:1, here]
        hid_ref[:, here] = hidden
        for part, piece in enumerate(split3(hidden)):
            hs_ref[part * chan : (part + 1) * chan, here] = piece

    in_turns(0, n_near // wide_cols, first)


def gather_kernel(hid_ref, hs_ref, oh_ref, pick_ref, gidx_ref, bt_ref, geo_ref, r2c_ref,
                  hj_ref, w_ref, slope_ref, car_ref, ext_ref):
    slots = bt_ref.shape[0]
    bases = bt_ref.shape[1] // 2
    chan, n_near = hid_ref.shape
    atoms = hj_ref.shape[1] // slots
    half = atoms // 2
    ghosts = dot(hs_ref[...], pick_ref[...]).astype(bf16)
    ext_ref[:, 0:half] = ghosts[:, :half]
    ext_ref[:, half : half + atoms] = hs_ref[:, 0:atoms]
    ext_ref[:, half + atoms :] = ghosts[:, half:]
    reach = 1.0 + lax.broadcasted_iota(jnp.int32, (bases, atoms), 0).astype(f32)
    for k in range(slots):
        here = slice(k * atoms, (k + 1) * atoms)
        basis = bt_ref[k, 0:bases, 0:atoms]
        for ref, value in ((w_ref, basis), (slope_ref, basis * (reach - row(geo_ref[4, k : k + 1, 0:atoms], bases)))):
            ref[:, here] = dot(r2c_ref[...], six_rows(value, VALUE_ORDER).astype(bf16))

    for pair in range(slots // 2):
        by_lane = 4 * LANES if atoms >= 4 * LANES else 0
        by_product = 2 * atoms - by_lane
        first = pair * 2 * atoms
        here = slice(first, first + by_product)
        both = dot(ext_ref[...], oh_ref[:, here])
        wanted = gidx_ref[2 * pair + 1 : 2 * pair + 2, 0:atoms]
        for t in range(by_lane // LANES):
            at = slice(first + by_product + t * LANES, first + by_product + (t + 1) * LANES)
            start = atoms - by_lane + t * LANES
            mine = row(wanted[:, start : start + LANES])
            chunk_no = mine >> 7
            place = mine & 127
            for c in range(chan // 8):
                rows = slice(8 * c, 8 * c + 8)
                feat = None
                for chunk in range(n_near // LANES):
                    held = hid_ref[rows, chunk * LANES : (chunk + 1) * LANES]
                    got = jnp.take_along_axis(held, place, axis=1, mode="promise_in_bounds")
                    feat = got if feat is None else jnp.where(chunk_no == chunk, got, feat)
                hj_ref[rows, at] = feat
                car_ref[rows, at] = feat * w_ref[rows, at]
        feat = both[:chan] + (both[chan : 2 * chan] + both[2 * chan :])
        hj_ref[:, here] = feat
        car_ref[:, here] = feat * w_ref[:, here]


def moment_kernel(car_ref, yb_ref, mixa_ref, mixt_ref, side_ref, m2_ref, dinv_ref, inv_ref):
    slots = yb_ref.shape[1]
    chan, atoms = m2_ref.shape[1:]
    tiles = atoms // LANES
    wide_cols = 2 * LANES
    rows = 32
    groups = chan // rows

    def moments(step):
        t = step // groups
        c = step % groups
        cols = pl.ds(pl.multiple_of(t * LANES, LANES), LANES)
        base = pl.multiple_of(c * rows, rows)
        acc = [[None] * ORDERS for _ in range(rows // 8)]
        for k in range(slots):
            at = pl.ds(pl.multiple_of(k * atoms + t * LANES, LANES), LANES)
            got = car_ref[pl.ds(base, rows), at]
            for l in range(ORDERS):
                yb = yb_ref[l - 1, k, :, cols] if l else None
                for h in range(rows // 8):
                    part = got[8 * h : 8 * h + 8]
                    term = part * yb if l else part
                    acc[h][l] = term if acc[h][l] is None else acc[h][l] + term
        for h in range(rows // 8):
            inv = [None] * 3
            for l in range(ORDERS):
                m2_ref[l, pl.ds(pl.multiple_of(base + 8 * h, 8), 8), cols] = acc[h][l]
                sq = acc[h][l] * acc[h][l]
                g = GROUP[l]
                inv[g] = sq if inv[g] is None else inv[g] + sq
            for g in range(3):
                inv_ref[pl.ds(pl.multiple_of(g * chan + base + 8 * h, 8), 8), cols] = inv[g]

    in_turns(0, tiles * groups, moments, 2)
    read2_col = side_ref[:, 3:4]
    for t in range(atoms // wide_cols):
        cols = slice(t * wide_cols, (t + 1) * wide_cols)
        _, slope = silu_parts(mixed(mixa_ref[1], inv_ref[:, cols]))
        groups_slope = dot(mixt_ref[1], three_deep(slope * (2.0 * read2_col)))
        for g, scale in enumerate((1.0, 0.5 * SQRT3, 0.5 * SQRT15)):
            dinv_ref[g * chan : (g + 1) * chan, cols] = scale * groups_slope[g * chan : (g + 1) * chan]


def back_second_kernel(m2_ref, dinv_ref, car_ref, hj_ref, w_ref, slope_ref, ub_ref, dhe_ref, p_ref):
    slots = ub_ref.shape[1]
    chan, atoms = m2_ref.shape[1:]
    tiles = atoms // LANES
    pairs = chan // 16
    per_turn = 4 if pairs % 4 == 0 else 1
    k_step = slots // 2

    def back_moments(t, carry):
        cols = pl.ds(pl.multiple_of(t * LANES, LANES), LANES)

        def one(c, acc, k0):
            forms = []
            for h in range(2):
                rows = pl.ds(pl.multiple_of(c * 16 + 8 * h, 8), 8)
                scale = [dinv_ref[pl.ds(pl.multiple_of(g * chan + c * 16 + 8 * h, 8), 8), cols] for g in range(3)]
                dm = [m2_ref[l, rows, cols] * scale[GROUP[l]] for l in range(ORDERS)]
                low = dm[6] * (1.0 / SQRT3)
                forms.append((dm[0], dm[1], dm[2], dm[3], dm[8] - low, -dm[8] - low, low + low, dm[4], dm[5], dm[7]))
            base = pl.multiple_of(c * 16, 16)
            for k in range(k0, k0 + k_step):
                at = pl.ds(pl.multiple_of(k * atoms + t * LANES, LANES), LANES)
                got = car_ref[pl.ds(base, 16), at]
                stretch = hj_ref[pl.ds(base, 16), at] * slope_ref[pl.ds(base, 16), at]
                ux, uy, uz = [ub_ref[i, k, :, cols] for i in range(3)]
                out = []
                for h in range(2):
                    mid, dx, dy, dz, qxx, qyy, qzz, qxy, qyz, qxz = forms[h]
                    gx = dx + qxx * ux + qxy * uy + qxz * uz
                    gy = dy + qxy * ux + qyy * uy + qyz * uz
                    gz = dz + qxz * ux + qyz * uy + qzz * uz
                    out.append(mid + (gx + dx) * ux + (gy + dy) * uy + (gz + dz) * uz)
                    part = got[8 * h : 8 * h + 8]
                    at_acc = 4 * (k - k0)
                    for i, g in enumerate((gx, gy, gz)):
                        acc[at_acc + i] = acc[at_acc + i] + part * g
                    acc[at_acc + 3] = acc[at_acc + 3] + out[h] * stretch[8 * h : 8 * h + 8]
                hi, lo = split(jnp.concatenate(out, axis=0) * w_ref[pl.ds(base, 16), at])
                dhe_ref[pl.ds(base, 16), at] = hi
                dhe_ref[pl.ds(pl.multiple_of(chan + c * 16, 16), 16), at] = lo

        for k0 in range(0, slots, k_step):

            def over(c, acc, k0=k0):
                acc = list(acc)
                for i in range(per_turn):
                    one(per_turn * c + i, acc, k0)
                return tuple(acc)

            start = tuple(jnp.zeros((8, LANES), f32) for _ in range(4 * k_step))
            acc = lax.fori_loop(0, pairs // per_turn, over, start)
            for k in range(k_step):
                for i in range(4):
                    p_ref[i, 8 * (k0 + k) : 8 * (k0 + k) + 8, cols] = acc[4 * k + i]
        return carry

    lax.fori_loop(0, tiles, back_moments, 0)


def scatter_kernel(oh_ref, pick_ref, dhe_ref, side_ref, p_ref, gidx_ref, dh_ref, q_ref, ohlo_ref):
    chan, n_near = dh_ref.shape
    slots = gidx_ref.shape[0]
    atoms = pick_ref.shape[1]
    half = atoms // 2
    both = dot_nt(dhe_ref[...], jnp.concatenate([oh_ref[:half], oh_ref[half + atoms :]], axis=0))
    hi, lo = split(both[:chan] + both[chan:])
    spread = dot_nt(jnp.concatenate([hi, lo], axis=0), pick_ref[...])
    spread = spread[:chan] + spread[chan:]
    both = dot_nt(dhe_ref[...], oh_ref[half : half + atoms])
    dh_ref[:, 0:atoms] = spread[:, :atoms] + both[:chan] + both[chan:] + side_ref[:, 2:3]
    if n_near > atoms:
        dh_ref[:, atoms:] = spread[:, atoms:]
    ids16 = lax.broadcasted_iota(jnp.int32, (LANES, n_near), 0).astype(jnp.int16)
    one16 = jnp.ones((LANES, n_near), bf16)
    zero16 = jnp.zeros((LANES, n_near), bf16)
    for k in range(slots):
        place = jnp.broadcast_to(gidx_ref[k : k + 1, :] & 127, (LANES, n_near)).astype(jnp.int16)
        ohlo_ref[:, k * n_near : (k + 1) * n_near] = jnp.where(place == ids16, one16, zero16)
    lane = lax.broadcasted_iota(jnp.int32, (slots, 16 * slots), 1)
    sub = lax.broadcasted_iota(jnp.int32, (slots, 16 * slots), 0)
    adder = jnp.where(((lane >> 3) & (slots - 1)) == sub, 1.0, 0.0).astype(bf16)
    for i in range(4):
        total = dot(adder, split_rows(p_ref[i]).astype(bf16))
        q_ref[8 * i : 8 * i + 8, :] = 2.0 * total if i < 3 else total


def back_first_kernel(dh_ref, sp1_ref, m1_ref, mixt_ref, rrr_ref, da_ref):
    n_near = sp1_ref.shape[1]
    rows = rrr_ref.shape[0] // 2
    wide_cols = 2 * LANES

    def back_first(j):
        here = pl.ds(pl.multiple_of(j * wide_cols, wide_cols), wide_cols)
        slope = three_deep(dh_ref[:, here] * sp1_ref[:, here] * 2.0)
        groups_slope = dot(mixt_ref[0], slope)
        chan = sp1_ref.shape[0]
        scale = [groups_slope[g * chan : (g + 1) * chan] for g in range(3)]
        for l in range(ORDERS):
            hi, lo = split(m1_ref[l, :, here] * scale[GROUP[l]])
            out = dot(rrr_ref[...], jnp.concatenate([hi, lo], axis=0))
            da_ref[l, :, here] = out[:rows] + out[rows:]

    in_turns(0, n_near // wide_cols, back_first)


def back_edge_kernel(plan, *refs):
    atoms, near, wide, _, _ = plan
    n_wide = len(wide)
    blocks = refs[:n_wide]
    moment_src, geo_ref, y_ref, bk_ref, gidx_ref, da_ref, q_ref, ohlo_ref = refs[n_wide : n_wide + 8]
    push_ref, mass_ref, val_ref, dr_ref, moment_ref, sem = refs[n_wide + 8 :]
    fetch = pltpu.make_async_copy(moment_src, moment_ref, sem)
    fetch.start()
    bases, slots, n_near = bk_ref.shape
    tiles = atoms // LANES
    top_rows = val_ref.shape[0] // 6

    def back_geometry(t, mine):
        here = pl.ds(pl.multiple_of(t * LANES, LANES), LANES)
        ux, uy, uz, back, soft, fj = [geo_ref[i, :, here] for i in range(6)]
        dy = [None] * ORDERS
        ds = None
        for n in range(bases):
            basis = bk_ref[n, :, here]
            db = None
            for l in range(ORDERS):
                g = row(da_ref[l, n : n + 1, here]) + fj * row(da_ref[l, bases + n : bases + n + 1, here])
                if l:
                    dy[l] = g * basis if dy[l] is None else dy[l] + g * basis
                    db = db + g * y_ref[l - 1, :, here]
                else:
                    db = g
            db = db * basis * ((1.0 + n) - soft)
            ds = db if ds is None else ds + db
        if mine:
            ds = ds + q_ref[24:32, here]
        dux = SQRT3 * dy[1] + SQRT15 * (uy * dy[4] + uz * dy[7] + ux * dy[8]) - SQRT5 * ux * dy[6]
        duy = SQRT3 * dy[2] + SQRT15 * (ux * dy[4] + uz * dy[5] - uy * dy[8]) - SQRT5 * uy * dy[6]
        duz = SQRT3 * dy[3] + SQRT15 * (uy * dy[5] + ux * dy[7]) + 2.0 * SQRT5 * uz * dy[6]
        if mine:
            dux, duy, duz = [d + q_ref[8 * i : 8 * i + 8, here] for i, d in enumerate((dux, duy, duz))]
        along = ds - (ux * dux + uy * duy + uz * duz) * back
        for i, value in enumerate((dux * back + along * ux, duy * back + along * uy, duz * back + along * uz)):
            dr_ref[i, :, here] = value

    in_turns(0, tiles, lambda t: back_geometry(t, True))
    in_turns(tiles, n_near // LANES, lambda t: back_geometry(t, False))

    def place_tile(t):
        here = pl.ds(pl.multiple_of(t * LANES, LANES), LANES)
        gidx = gidx_ref[:, here]
        chunk_no = gidx >> 7
        parts = []
        for i in range(3):
            value = dr_ref[i, :, here]
            hi = value.astype(bf16).astype(f32)
            parts.append((hi, value - hi))
        chunk_ids = lax.broadcasted_iota(jnp.int32, (top_rows, LANES), 0)
        for k in range(slots):
            at = pl.ds(pl.multiple_of(k * n_near + t * LANES, LANES), LANES)
            hit = chunk_ids == row(chunk_no[k : k + 1, :], top_rows)
            for i in range(3):
                both = [jnp.where(hit, row(part[k : k + 1, :], top_rows), 0.0) for part in parts[i]]
                val_ref[2 * i * top_rows : 2 * (i + 1) * top_rows, at] = jnp.concatenate(both, axis=0).astype(bf16)

    in_turns(0, n_near // LANES, place_tile)
    landed = dot_nt(val_ref[...], ohlo_ref[...])
    fetch.wait()
    lines = push_ref.shape[0] // (n_wide + 1)
    for i in range(3):
        total = (
            landed[2 * i * top_rows : (2 * i + 1) * top_rows] + landed[(2 * i + 1) * top_rows : (2 * i + 2) * top_rows]
        )
        for g in range(n_wide):
            for t in range(tiles):
                cols = slice(t * LANES, (t + 1) * LANES)
                line = total[g * tiles + t : g * tiles + t + 1, :]
                if g < len(near):
                    here = slice(g * atoms + t * LANES, g * atoms + (t + 1) * LANES)
                    line = line - jnp.sum(dr_ref[i, :, here], axis=0, keepdims=True)
                line = -HALF_STEP * line
                at = i * tiles + t
                if g == 0:
                    line = line + moment_ref[i, :, cols]
                    push_ref[at : at + 1, :] = blocks[0][i : i + 1, cols]
                push_ref[(1 + g) * lines + at : (1 + g) * lines + at + 1, :] = line
                mass = HEAVY - (HEAVY - 1.0) * blocks[g][3:4, cols]
                mass_ref[g * lines + at : g * lines + at + 1, :] = mass


def in_hbm(x):
    return pltpu.with_memory_space_constraint(x, pltpu.HBM)


def run(name, body, operands, results, scratch=(), far=(), cost=None):
    sizes = [math.prod(x.shape) * x.dtype.itemsize // 2 for i, x in enumerate(operands) if i not in far]
    sizes += [math.prod(shape) * jnp.dtype(dtype).itemsize for shape, dtype in results]
    sizes += [math.prod(x.shape) * x.dtype.itemsize for x in scratch if x.memory_space == pltpu.VMEM]
    limit = sum(sizes) + 4 * MIB
    specs = [pl.BlockSpec(memory_space=pltpu.HBM if i in far else pltpu.VMEM) for i in range(len(operands))]
    return pl.pallas_call(
        body,
        out_shape=tuple(jax.ShapeDtypeStruct(shape, dtype) for shape, dtype in results),
        in_specs=specs,
        out_specs=tuple(pl.BlockSpec(memory_space=pltpu.VMEM) for _ in results),
        scratch_shapes=list(scratch),
        compiler_params=pltpu.CompilerParams(vmem_limit_bytes=limit),
        cost_estimate=cost,
        name=name,
    )(*[in_hbm(x) if i in far else x for i, x in enumerate(operands)])


def choose(block, embedding, radial_one, radial_two, mix_one, mix_two, read_one, read_two):
    atoms = block.shape[1]
    slots = block.shape[0] - HEAD
    chan = embedding.shape[1]
    bases = radial_one.shape[0]
    weights = (embedding, radial_one, radial_two, mix_one, mix_two, read_one[None], read_two[None])
    return run(
        "choose",
        choose_kernel,
        (block, *weights),
        (
            ((2 * atoms, slots * atoms), bf16),
            ((chan, 12 * bases), bf16),
            ((chan, 6 * bases), bf16),
            ((chan, LANES), f32),
            ((4 * bases, 2 * chan), bf16),
            ((2, 3 * chan, 6 * chan), bf16),
            ((2, 3 * chan, 3 * chan), bf16),
        ),
        [pltpu.VMEM(w.shape, f32) for w in weights] + [pltpu.SemaphoreType.DMA((len(weights),))],
        range(1, 1 + len(weights)),
        cost=pl.CostEstimate(flops=2 * 10**9, bytes_accessed=2 * 10**6, transcendentals=0),
    )


def pushes(plan, blocks, momenta, chosen):
    atoms, near, wide, _, _ = plan
    oh, rrc, r2c, sides, rrr, mixa, mixt = chosen
    chan = rrc.shape[0]
    bases = rrr.shape[0] // 4
    slots = blocks[0].shape[0] - HEAD
    n_near = len(near) * atoms
    edges = slots * atoms
    top_rows = -(-len(wide) * atoms // LANES // 8) * 8
    lines = line_count(atoms)
    geo, y, yb, ub, bk, bt, gidx, pick, as1 = run(
        "edges",
        functools.partial(edge_kernel, plan),
        blocks,
        (
            ((6, slots, n_near), f32),
            ((ORDERS - 1, slots, n_near), f32),
            ((ORDERS - 1, slots, 8, atoms), f32),
            ((3, slots, 8, atoms), f32),
            ((bases, slots, n_near), f32),
            ((slots, 2 * bases, n_near), f32),
            ((slots, n_near), jnp.int32),
            ((n_near, atoms), bf16),
            ((ORDERS, 12 * bases, n_near), bf16),
        ),
    )
    m1, sp1, hid, hs = run(
        "first",
        functools.partial(first_kernel, plan),
        (*blocks, as1, rrc, sides, mixa),
        (((ORDERS, chan, n_near), f32), ((chan, n_near), f32), ((chan, n_near), f32), ((3 * chan, n_near), bf16)),
        [pltpu.VMEM((8, n_near), f32)],
    )
    hj, w, slope, car = run(
        "gather",
        gather_kernel,
        (hid, hs, oh, pick, gidx, bt, geo, r2c),
        (((chan, edges), f32),) * 4,
        [pltpu.VMEM((3 * chan, 2 * atoms), bf16)],
    )
    m2, dinv = run(
        "moments",
        moment_kernel,
        (car, yb, mixa, mixt, sides),
        (((ORDERS, chan, atoms), f32), ((3 * chan, atoms), f32)),
        [pltpu.VMEM((3 * chan, atoms), f32)],
    )
    dhe, p = run(
        "back_second",
        back_second_kernel,
        (m2, dinv, car, hj, w, slope, ub),
        (((2 * chan, edges), bf16), ((4, 8 * slots, atoms), f32)),
    )
    dh, q, ohlo = run(
        "scatter",
        scatter_kernel,
        (oh, pick, dhe, sides, p, gidx),
        (((chan, n_near), f32), ((4 * slots, atoms), f32), ((LANES, slots * n_near), bf16)),
    )
    (da,) = run("back_first", back_first_kernel, (dh, sp1, m1, mixt, rrr), (((ORDERS, 2 * bases, n_near), f32),))
    return run(
        "back_edges",
        functools.partial(back_edge_kernel, plan),
        (*blocks, momenta, geo, y, bk, gidx, da, q, ohlo),
        ((((len(wide) + 1) * lines, LANES), f32), ((len(wide) * lines, LANES), f32)),
        [
            pltpu.VMEM((6 * top_rows, slots * n_near), bf16),
            pltpu.VMEM((3, slots, n_near), f32),
            pltpu.VMEM(momenta.shape, f32),
            pltpu.SemaphoreType.DMA(()),
        ],
        (len(blocks),),
    )


def line_count(atoms):
    return 3 * (atoms // LANES)


def ring_plan(domains, atoms):
    near = list(dict.fromkeys(o % domains for o in (0, 1, -1)))
    wide = list(dict.fromkeys(near + [o % domains for o in (2, -2)]))
    before = tuple(wide.index((o - 1) % domains) for o in near)
    after = tuple(wide.index((o + 1) % domains) for o in near)
    return atoms, tuple(near), tuple(wide), before, after


def mode_turns(bead_total):
    bead = np.arange(bead_total, dtype=np.float64)[:, None]
    mode = np.arange(bead_total, dtype=np.float64)[None, :]
    phase = 2.0 * np.pi * bead * mode / bead_total
    half_total = bead_total // 2
    table = math.sqrt(2.0 / bead_total) * np.where(mode < half_total, np.cos(phase), np.sin(phase))
    table = np.where(mode == half_total, np.cos(np.pi * bead) / math.sqrt(bead_total), table)
    table = np.where(mode == 0, 1.0 / math.sqrt(bead_total), table)
    angles = bead_total * np.sin(np.pi * mode[0] / bead_total)
    safe = np.where(mode[0] == 0, 1.0, angles)
    reach = np.where(mode[0] == 0, STEP, STEP * np.sin(angles) / safe)
    stiff = angles * np.sin(angles) / STEP
    return [[float(x) for x in (table * factor[None, :]) @ table[0]] for factor in (np.cos(angles), reach, stiff)]


def pack_kernel(coord_src, species_src, send_src, slot_src, block_ref, coord_ref, species_ref, send_ref, slot_ref, sems):
    pairs = ((coord_src, coord_ref), (species_src, species_ref), (send_src, send_ref), (slot_src, slot_ref))
    fetches = [pltpu.make_async_copy(src, dst, sems.at[i]) for i, (src, dst) in enumerate(pairs)]
    for fetch in fetches:
        fetch.start()
    for fetch in fetches:
        fetch.wait()
    atoms = block_ref.shape[1]
    for i in range(3):
        block_ref[i : i + 1, :] = coord_ref[i]
    block_ref[3:4, :] = species_ref[...].astype(f32)
    block_ref[4:5, :] = send_ref[...].astype(f32)
    block_ref[5:HEAD, :] = jnp.zeros((HEAD - 5, atoms), f32)
    block_ref[HEAD:, :] = slot_ref[...].astype(f32)


def turn_kernel(shape, bead_ref, domain_ref, mass_ref, *refs):
    outer, inner, domains, wide = shape
    message_ref = refs[outer]
    turns = mode_turns(outer * inner)
    lines = mass_ref.shape[0] // len(wide)
    my_domain = domain_ref[0]
    my_inner = lax.rem(bead_ref[0], inner)
    if domains > len(wide):
        message_ref[...] = jnp.zeros_like(message_ref)
    masses = [mass_ref[g * lines : (g + 1) * lines, :] for g in range(len(wide))]
    sources = []
    for z in range(outer):
        sources.append([refs[z][g * lines : (g + 1) * lines, :] for g in range(len(wide) + 1)])
    for s in range(inner):
        wraps = jnp.full((lines, LANES), my_inner + s) >= inner
        weights = []
        for turn in turns:
            row_of = []
            for z in range(outer):
                there = turn[(z * inner + s) % (outer * inner)]
                round_it = turn[(z * inner + s - inner) % (outer * inner)]
                row_of.append(jnp.where(wraps, jnp.full((lines, LANES), round_it), jnp.full((lines, LANES), there)))
            weights.append(row_of)
        to_inner = lax.rem(my_inner + s, inner)
        for g in range(len(wide)):
            turned = sum(weights[0][z] * sources[z][1 + g] for z in range(outer))
            drift = sum(weights[1][z] * sources[z][1 + g] for z in range(outer))
            new_q = drift / masses[g]
            new_p = turned
            if g == 0:
                new_q = new_q + sum(weights[0][z] * sources[z][0] for z in range(outer))
                new_p = new_p - masses[g] * sum(weights[2][z] * sources[z][0] for z in range(outer))
            to = to_inner * domains + lax.rem(my_domain + wide[g], domains)
            message_ref[to, 0:lines, :] = new_q
            message_ref[to, lines:, :] = new_p


def sum_kernel(arrived_ref, q_ref, p_ref):
    total = arrived_ref[0]
    for i in range(1, arrived_ref.shape[0]):
        total = total + arrived_ref[i]
    lines = total.shape[0] // 2
    tiles = q_ref.shape[2] // LANES
    for i in range(3):
        for t in range(tiles):
            at = i * tiles + t
            q_ref[i, :, t * LANES : (t + 1) * LANES] = total[at : at + 1]
            p_ref[i, :, t * LANES : (t + 1) * LANES] = total[lines + at : lines + at + 1]


def shards(
    positions, momenta, species, neighbours, send_list, embedding, radial_one, radial_two, mix_one, mix_two,
    read_one, read_two,
):
    slots, atoms = neighbours.shape
    domains = lax.axis_size("space")
    beads = lax.axis_size("bead")
    inner = next(d for d in range(1, beads + 1) if beads % d == 0 and d * d >= beads)
    outer = beads // inner
    plan = ring_plan(domains, atoms)
    wide = plan[2]
    vmem = pl.BlockSpec(memory_space=pltpu.VMEM)
    smem = pl.BlockSpec(memory_space=pltpu.SMEM)
    far = pl.BlockSpec(memory_space=pltpu.HBM)
    small = pltpu.CompilerParams(vmem_limit_bytes=4 * MIB)
    coord_rows = jnp.transpose(positions, (1, 0, 2))
    moment_rows = jnp.transpose(momenta, (1, 0, 2))
    block = pl.pallas_call(
        pack_kernel,
        out_shape=jax.ShapeDtypeStruct((HEAD + slots, atoms), f32),
        in_specs=[far] * 4,
        out_specs=vmem,
        scratch_shapes=[
            pltpu.VMEM(coord_rows.shape, f32),
            pltpu.VMEM((1, atoms), jnp.int32),
            pltpu.VMEM((1, atoms), jnp.int32),
            pltpu.VMEM((slots, atoms), jnp.int32),
            pltpu.SemaphoreType.DMA((4,)),
        ],
        compiler_params=small,
        name="pack",
    )(in_hbm(coord_rows), in_hbm(species[None]), in_hbm(send_list[None]), in_hbm(neighbours))
    blocks = [block]
    for offset in wide[1:]:
        blocks.append(lax.ppermute(block, "space", [(i, (i - offset) % domains) for i in range(domains)]))
    chosen = choose(block, embedding, radial_one, radial_two, mix_one, mix_two, read_one, read_two)
    pushed, masses = pushes(plan, blocks, moment_rows, chosen)
    sources = [pushed]
    for z in range(1, outer):
        sources.append(lax.ppermute(pushed, "bead", [(b, (b + z * inner) % beads) for b in range(beads)]))
    here = [lax.axis_index(axis).astype(jnp.int32).reshape(1) for axis in ("bead", "space")]
    lines = line_count(atoms)
    messages = pl.pallas_call(
        functools.partial(turn_kernel, (outer, inner, domains, wide)),
        out_shape=jax.ShapeDtypeStruct((inner * domains, 2 * lines, LANES), f32),
        in_specs=[smem, smem, vmem] + [vmem] * outer,
        out_specs=vmem,
        compiler_params=small,
        name="turn",
    )(*here, masses, *sources)
    rows = [[z * inner * domains + i for i in range(inner * domains)] for z in range(outer)]
    arrived = lax.all_to_all(messages, ("bead", "space"), 0, 0, axis_index_groups=rows, tiled=True)
    new_q, new_p = pl.pallas_call(
        sum_kernel,
        out_shape=(jax.ShapeDtypeStruct((3, 1, atoms), f32),) * 2,
        in_specs=[vmem],
        out_specs=(vmem, vmem),
        compiler_params=small,
        name="sum",
    )(arrived)
    return (jnp.transpose(new_q, (1, 0, 2)), jnp.transpose(new_p, (1, 0, 2)))


def solution(mesh):
    placed = (
        P("bead", None, "space"),
        P("bead", None, "space"),
        P("space"),
        P(None, "space"),
        P("space"),
        P(),
        P(),
        P(),
        P(),
        P(),
        P(),
        P(),
    )
    return jax.shard_map(
        shards,
        mesh=mesh,
        in_specs=placed,
        out_specs=(P("bead", None, "space"), P("bead", None, "space")),
        check_vma=False,
    )
```

```python
import functools
import math

import jax
import jax.numpy as jnp
import numpy as np
from jax import lax
from jax.experimental import pallas as pl
from jax.experimental.pallas import tpu as pltpu
from jax.sharding import PartitionSpec as P

STEP = 2.0
HALF_STEP = 1.0
HEAVY = 16.0
SQRT3 = math.sqrt(3.0)
SQRT5 = math.sqrt(5.0)
SQRT15 = math.sqrt(15.0)
LANES = 128
ORDERS = 9
GROUP = (0, 1, 1, 1, 2, 2, 2, 2, 2)
HEAD = 8
MIB = 1024 * 1024
f32 = jnp.float32
bf16 = jnp.bfloat16


def split(x):
    hi = x.astype(bf16)
    return hi, (x - hi.astype(f32)).astype(bf16)


def split_rows(x):
    hi = x.astype(bf16).astype(f32)
    return jnp.concatenate([hi, x - hi], axis=0)


def split3(x):
    hi = x.astype(bf16)
    rest = x - hi.astype(f32)
    mid = rest.astype(bf16)
    return hi, mid, (rest - mid.astype(f32)).astype(bf16)


def six_rows(x, order):
    hi = x.astype(bf16).astype(f32)
    mid = (x - hi).astype(bf16).astype(f32)
    parts = (hi, mid, x - hi - mid)
    return jnp.concatenate([parts[i] for i in order], axis=0)


VALUE_ORDER = (0, 1, 0, 1, 2, 0)
WEIGHT_ORDER = (0, 0, 1, 1, 0, 2)


def dot(a, b):
    return jnp.dot(a, b, preferred_element_type=f32)


def dot_nt(a, b):
    return lax.dot_general(a, b, (((1,), (1,)), ((), ())), preferred_element_type=f32)


def in_turns(start, stop, step, most=4):
    per_turn = next(n for n in range(most, 0, -1) if (stop - start) % n == 0)

    def turn(i, carry):
        for j in range(per_turn):
            step(start + i * per_turn + j)
        return carry

    lax.fori_loop(0, (stop - start) // per_turn, turn, 0)


def row(x, rows=8):
    return jnp.broadcast_to(x, (rows, x.shape[1]))


def lookup(chunks, wanted, position):
    out = None
    for number, chunk in chunks:
        got = jnp.take_along_axis(row(chunk), position, axis=1, mode="promise_in_bounds")
        out = got if out is None else jnp.where(wanted == number, got, out)
    return out


def harmonics(ux, uy, uz):
    return [
        None,
        SQRT3 * ux,
        SQRT3 * uy,
        SQRT3 * uz,
        SQRT15 * ux * uy,
        SQRT15 * uy * uz,
        0.5 * SQRT5 * (2.0 * uz * uz - ux * ux - uy * uy),
        SQRT15 * ux * uz,
        0.5 * SQRT15 * (ux * ux - uy * uy),
    ]


def silu_parts(v):
    gate = 1.0 / (1.0 + jnp.exp(-v))
    return v * gate, gate * (1.0 + v * (1.0 - gate))


def choose_kernel(block_ref, *refs):
    sources = refs[:7]
    oh_ref, rrc_ref, r2c_ref, side_ref, rrr_ref, mixa_ref, mixt_ref = refs[7:14]
    held = refs[14:21]
    sems = refs[21]
    emb_ref, rad1_ref, rad2_ref, mix1_ref, mix2_ref, read1_ref, read2_ref = held
    fetches = [pltpu.make_async_copy(src, dst, sems.at[i]) for i, (src, dst) in enumerate(zip(sources, held))]
    for fetch in fetches:
        fetch.start()
    chan = emb_ref.shape[1]
    bases = rad1_ref.shape[0]
    atoms = block_ref.shape[1]
    slots = block_ref.shape[0] - HEAD

    ids16 = lax.broadcasted_iota(jnp.int32, (LANES, atoms), 0).astype(jnp.int16)
    one16 = jnp.ones((LANES, atoms), bf16)
    zero16 = jnp.zeros((LANES, atoms), bf16)
    for k in range(slots):
        slot = block_ref[HEAD + k : HEAD + k + 1, :].astype(jnp.int32)
        wanted = jnp.broadcast_to(slot, (LANES, atoms)).astype(jnp.int16)
        for r in range(oh_ref.shape[0] // LANES):
            hit = wanted - jnp.int16(r * LANES) == ids16
            oh_ref[r * LANES : (r + 1) * LANES, k * atoms : (k + 1) * atoms] = jnp.where(hit, one16, zero16)

    for fetch in fetches:
        fetch.wait()
    emb0 = emb_ref[0:1, :]
    emb_d = emb_ref[1:2, :] - emb0
    rr = jnp.concatenate([rad1_ref[...] * emb0, rad1_ref[...] * emb_d], axis=0) * (1.0 / slots)
    rr_hi = rr.astype(bf16).astype(f32)
    rr_lo = rr - rr_hi
    r2 = rad2_ref[...] * (1.0 / slots)
    zeros = jnp.zeros((8, chan), f32)
    turned1 = jnp.concatenate([six_rows(rr, WEIGHT_ORDER)] + [zeros] * (16 - 12 * bases // 8), axis=0).T
    sides = jnp.concatenate([emb0, emb_d, read1_ref[...], read2_ref[...], zeros[:4]], axis=0)
    turned2 = jnp.concatenate([six_rows(r2, WEIGHT_ORDER)] + [zeros] * (16 - 6 * bases // 8), axis=0).T
    rrc_ref[...] = turned1[:, : 12 * bases].astype(bf16)
    r2c_ref[...] = turned2[:, : 6 * bases].astype(bf16)
    side_ref[...] = jnp.concatenate([sides] + [zeros] * 15, axis=0).T
    rrr_ref[...] = jnp.concatenate(
        [jnp.concatenate([rr_hi, rr_hi], axis=1), jnp.concatenate([rr_lo, jnp.zeros_like(rr_lo)], axis=1)], axis=0
    ).astype(bf16)
    for i, ref in enumerate((mix1_ref, mix2_ref)):
        parts = split3(ref[...])
        for at, part in enumerate(WEIGHT_ORDER):
            mixa_ref[i, :, at * 3 * chan : (at + 1) * 3 * chan] = parts[part]
        for g in range(3):
            hi, lo = split(ref[:, g * chan : (g + 1) * chan].T)
            mixt_ref[i, g] = jnp.concatenate([hi, hi, lo], axis=1)


def six_deep(x):
    parts = split3(x)
    return jnp.concatenate([parts[i] for i in VALUE_ORDER], axis=0)


def three_deep(x):
    hi, lo = split(x)
    return jnp.concatenate([hi, lo, hi], axis=0)


def edge_kernel(plan, *refs):
    atoms, near, wide, before, after = plan
    n_wide = len(wide)
    blocks = refs[:n_wide]
    geo_ref, y_ref, yb_ref, ub_ref, bk_ref, bt_ref, gidx_ref, pick_ref, as_ref = refs[n_wide:]
    bases = bk_ref.shape[0]
    slots = gidx_ref.shape[0]
    tiles = atoms // LANES
    half = atoms // 2
    half_tiles = half // LANES
    order_col = lax.broadcasted_iota(jnp.int32, (bases, LANES), 0).astype(f32)
    tables = []
    for quantity in range(4):
        chunks = []
        for g in range(n_wide):
            for t in range(tiles):
                chunks.append((g * tiles + t, blocks[g][quantity : quantity + 1, t * LANES : (t + 1) * LANES]))
        tables.append(chunks)
    for q in range(len(near)):
        ghosts = []
        for t in range(half_tiles):
            ghosts.append(
                (t, blocks[before[q]][4:5, half + t * LANES : half + (t + 1) * LANES] + float(before[q] * atoms))
            )
        for t in range(half_tiles):
            ghosts.append(
                (
                    half_tiles + tiles + t,
                    blocks[after[q]][4:5, t * LANES : (t + 1) * LANES] + float(after[q] * atoms),
                )
            )
        if q == 0:
            ids16 = lax.broadcasted_iota(jnp.int32, (pick_ref.shape[0], LANES), 0).astype(jnp.int16)
            one16 = jnp.ones(ids16.shape, bf16)
            zero16 = jnp.zeros(ids16.shape, bf16)
            for t, (_, chunk) in enumerate(ghosts):
                wanted = jnp.broadcast_to(chunk.astype(jnp.int32), ids16.shape).astype(jnp.int16)
                pick_ref[:, t * LANES : (t + 1) * LANES] = jnp.where(wanted == ids16, one16, zero16)
        for t in range(tiles):
            cols = slice(t * LANES, (t + 1) * LANES)
            here = slice(q * atoms + t * LANES, q * atoms + (t + 1) * LANES)
            slot = blocks[q][HEAD : HEAD + slots, cols].astype(jnp.int32)
            chunk_no = slot >> 7
            far = lookup(ghosts, chunk_no, slot & 127).astype(jnp.int32)
            own = (slot >= half) & (slot < half + atoms)
            gidx = jnp.where(own, slot + (q * atoms - half), far)
            gidx_ref[:, here] = gidx
            chunk_no = gidx >> 7
            place = gidx & 127
            xj, yj, zj, fj = [lookup(tables[i], chunk_no, place) for i in range(4)]
            rx = xj - row(blocks[q][0:1, cols])
            ry = yj - row(blocks[q][1:2, cols])
            rz = zj - row(blocks[q][2:3, cols])
            soft = jnp.sqrt(rx * rx + ry * ry + rz * rz + 1.0)
            back = 1.0 / soft
            ux, uy, uz = rx * back, ry * back, rz * back
            for i, value in enumerate((ux, uy, uz, back, soft, fj)):
                geo_ref[i, :, here] = value
            if q == 0:
                for i, value in enumerate((ux, uy, uz)):
                    for k in range(slots):
                        ub_ref[i, k, :, cols] = row(value[k : k + 1, :])
            sphere = harmonics(ux, uy, uz)
            for l in range(1, ORDERS):
                y_ref[l - 1, :, here] = sphere[l]
                if q == 0:
                    for k in range(slots):
                        yb_ref[l - 1, k, :, cols] = row(sphere[l][k : k + 1, :])
            for n in range(bases):
                bk_ref[n, :, here] = jnp.exp(-0.5 * (soft - (1.0 + n)) ** 2)
            for k in range(slots):
                basis = jnp.exp(-0.5 * (row(soft[k : k + 1, :], bases) - (1.0 + order_col)) ** 2)
                bt_ref[k, 0:bases, here] = basis
                bt_ref[k, bases : 2 * bases, here] = basis * row(fj[k : k + 1, :], bases)
            low = [None] * ORDERS
            for k in range(slots):
                basis = bt_ref[k, :, here]
                for l in range(ORDERS):
                    term = basis if l == 0 else basis * row(y_ref[l - 1, k : k + 1, here], 2 * bases)
                    low[l] = term if low[l] is None else low[l] + term
            for l in range(ORDERS):
                as_ref[l, :, here] = six_rows(low[l], VALUE_ORDER).astype(bf16)


def first_kernel(plan, *refs):
    atoms, near, wide, _, _ = plan
    n_wide = len(wide)
    blocks = refs[:n_wide]
    as_ref, rrc_ref, side_ref, mixa_ref, m1_ref, sp1_ref, hid_ref, hs_ref, flag_ref = refs[n_wide:]
    chan = m1_ref.shape[1]
    n_near = m1_ref.shape[2]

    for q in range(len(near)):
        flag_ref[0:1, q * atoms : (q + 1) * atoms] = blocks[q][3:4, :]
    wide_cols = 2 * LANES
    emb0_col = side_ref[:, 0:1]
    embd_col = side_ref[:, 1:2]

    def first(j):
        here = pl.ds(pl.multiple_of(j * wide_cols, wide_cols), wide_cols)
        inv = [None, None, None]
        for l in range(ORDERS):
            m = dot(rrc_ref[...], as_ref[l, :, here])
            m1_ref[l, :, here] = m
            inv[GROUP[l]] = m * m if inv[GROUP[l]] is None else inv[GROUP[l]] + m * m
        value = dot(mixa_ref[0], six_deep(jnp.concatenate(inv, axis=0)))
        act, slope = silu_parts(value)
        sp1_ref[:, here] = slope
        hidden = act + emb0_col + embd_col * flag_ref[0:1, here]
        hid_ref[:, here] = hidden
        for part, piece in enumerate(split3(hidden)):
            hs_ref[part * chan : (part + 1) * chan, here] = piece

    in_turns(0, n_near // wide_cols, first)


def gather_kernel(hid_ref, hs_ref, oh_ref, pick_ref, gidx_ref, bt_ref, geo_ref, r2c_ref,
                  hj_ref, w_ref, slope_ref, car_ref, ext_ref):
    slots = bt_ref.shape[0]
    bases = bt_ref.shape[1] // 2
    chan, n_near = hid_ref.shape
    atoms = hj_ref.shape[1] // slots
    half = atoms // 2
    ghosts = dot(hs_ref[...], pick_ref[...]).astype(bf16)
    ext_ref[:, 0:half] = ghosts[:, :half]
    ext_ref[:, half : half + atoms] = hs_ref[:, 0:atoms]
    ext_ref[:, half + atoms :] = ghosts[:, half:]
    reach = 1.0 + lax.broadcasted_iota(jnp.int32, (bases, atoms), 0).astype(f32)
    for k in range(slots):
        here = slice(k * atoms, (k + 1) * atoms)
        basis = bt_ref[k, 0:bases, 0:atoms]
        for ref, value in ((w_ref, basis), (slope_ref, basis * (reach - row(geo_ref[4, k : k + 1, 0:atoms], bases)))):
            ref[:, here] = dot(r2c_ref[...], six_rows(value, VALUE_ORDER).astype(bf16))

    for pair in range(slots // 2):
        by_lane = 4 * LANES if atoms >= 4 * LANES else 0
        by_product = 2 * atoms - by_lane
        first = pair * 2 * atoms
        here = slice(first, first + by_product)
        both = dot(ext_ref[...], oh_ref[:, here])
        wanted = gidx_ref[2 * pair + 1 : 2 * pair + 2, 0:atoms]
        for t in range(by_lane // LANES):
            at = slice(first + by_product + t * LANES, first + by_product + (t + 1) * LANES)
            start = atoms - by_lane + t * LANES
            mine = row(wanted[:, start : start + LANES])
            chunk_no = mine >> 7
            place = mine & 127
            for c in range(chan // 8):
                rows = slice(8 * c, 8 * c + 8)
                feat = None
                for chunk in range(n_near // LANES):
                    held = hid_ref[rows, chunk * LANES : (chunk + 1) * LANES]
                    got = jnp.take_along_axis(held, place, axis=1, mode="promise_in_bounds")
                    feat = got if feat is None else jnp.where(chunk_no == chunk, got, feat)
                hj_ref[rows, at] = feat
                car_ref[rows, at] = feat * w_ref[rows, at]
        feat = both[:chan] + (both[chan : 2 * chan] + both[2 * chan :])
        hj_ref[:, here] = feat
        car_ref[:, here] = feat * w_ref[:, here]


def moment_kernel(car_ref, yb_ref, mixa_ref, mixt_ref, side_ref, m2_ref, dinv_ref, inv_ref):
    slots = yb_ref.shape[1]
    chan, atoms = m2_ref.shape[1:]
    tiles = atoms // LANES
    wide_cols = 2 * LANES
    rows = 32
    groups = chan // rows

    def moments(step):
        t = step // groups
        c = step % groups
        cols = pl.ds(pl.multiple_of(t * LANES, LANES), LANES)
        base = pl.multiple_of(c * rows, rows)
        acc = [[None] * ORDERS for _ in range(rows // 8)]
        for k in range(slots):
            at = pl.ds(pl.multiple_of(k * atoms + t * LANES, LANES), LANES)
            got = car_ref[pl.ds(base, rows), at]
            for l in range(ORDERS):
                yb = yb_ref[l - 1, k, :, cols] if l else None
                for h in range(rows // 8):
                    part = got[8 * h : 8 * h + 8]
                    term = part * yb if l else part
                    acc[h][l] = term if acc[h][l] is None else acc[h][l] + term
        for h in range(rows // 8):
            inv = [None] * 3
            for l in range(ORDERS):
                m2_ref[l, pl.ds(pl.multiple_of(base + 8 * h, 8), 8), cols] = acc[h][l]
                sq = acc[h][l] * acc[h][l]
                g = GROUP[l]
                inv[g] = sq if inv[g] is None else inv[g] + sq
            for g in range(3):
                inv_ref[pl.ds(pl.multiple_of(g * chan + base + 8 * h, 8), 8), cols] = inv[g]

    in_turns(0, tiles * groups, moments, 2)
    read2_col = side_ref[:, 3:4]
    for t in range(atoms // wide_cols):
        cols = slice(t * wide_cols, (t + 1) * wide_cols)
        _, slope = silu_parts(dot(mixa_ref[1], six_deep(inv_ref[:, cols])))
        slope = three_deep(slope * (2.0 * read2_col))
        for g, scale in enumerate((1.0, 0.5 * SQRT3, 0.5 * SQRT15)):
            dinv_ref[g * chan : (g + 1) * chan, cols] = scale * dot(mixt_ref[1, g], slope)


def back_second_kernel(m2_ref, dinv_ref, car_ref, hj_ref, w_ref, slope_ref, ub_ref, dhe_ref, p_ref):
    slots = ub_ref.shape[1]
    chan, atoms = m2_ref.shape[1:]
    tiles = atoms // LANES
    pairs = chan // 16
    per_turn = 4 if pairs % 4 == 0 else 1
    k_step = slots // 2

    def back_moments(t, carry):
        cols = pl.ds(pl.multiple_of(t * LANES, LANES), LANES)

        def one(c, acc, k0):
            forms = []
            for h in range(2):
                rows = pl.ds(pl.multiple_of(c * 16 + 8 * h, 8), 8)
                scale = [dinv_ref[pl.ds(pl.multiple_of(g * chan + c * 16 + 8 * h, 8), 8), cols] for g in range(3)]
                dm = [m2_ref[l, rows, cols] * scale[GROUP[l]] for l in range(ORDERS)]
                low = dm[6] * (1.0 / SQRT3)
                forms.append((dm[0], dm[1], dm[2], dm[3], dm[8] - low, -dm[8] - low, low + low, dm[4], dm[5], dm[7]))
            base = pl.multiple_of(c * 16, 16)
            for k in range(k0, k0 + k_step):
                at = pl.ds(pl.multiple_of(k * atoms + t * LANES, LANES), LANES)
                got = car_ref[pl.ds(base, 16), at]
                stretch = hj_ref[pl.ds(base, 16), at] * slope_ref[pl.ds(base, 16), at]
                ux, uy, uz = [ub_ref[i, k, :, cols] for i in range(3)]
                out = []
                for h in range(2):
                    mid, dx, dy, dz, qxx, qyy, qzz, qxy, qyz, qxz = forms[h]
                    gx = dx + qxx * ux + qxy * uy + qxz * uz
                    gy = dy + qxy * ux + qyy * uy + qyz * uz
                    gz = dz + qxz * ux + qyz * uy + qzz * uz
                    out.append(mid + (gx + dx) * ux + (gy + dy) * uy + (gz + dz) * uz)
                    part = got[8 * h : 8 * h + 8]
                    at_acc = 4 * (k - k0)
                    for i, g in enumerate((gx, gy, gz)):
                        acc[at_acc + i] = acc[at_acc + i] + part * g
                    acc[at_acc + 3] = acc[at_acc + 3] + out[h] * stretch[8 * h : 8 * h + 8]
                hi, lo = split(jnp.concatenate(out, axis=0) * w_ref[pl.ds(base, 16), at])
                dhe_ref[pl.ds(base, 16), at] = hi
                dhe_ref[pl.ds(pl.multiple_of(chan + c * 16, 16), 16), at] = lo

        for k0 in range(0, slots, k_step):

            def over(c, acc, k0=k0):
                acc = list(acc)
                for i in range(per_turn):
                    one(per_turn * c + i, acc, k0)
                return tuple(acc)

            start = tuple(jnp.zeros((8, LANES), f32) for _ in range(4 * k_step))
            acc = lax.fori_loop(0, pairs // per_turn, over, start)
            for k in range(k_step):
                for i in range(4):
                    p_ref[i, 8 * (k0 + k) : 8 * (k0 + k) + 8, cols] = acc[4 * k + i]
        return carry

    lax.fori_loop(0, tiles, back_moments, 0)


def scatter_kernel(oh_ref, pick_ref, dhe_ref, side_ref, p_ref, gidx_ref, dh_ref, q_ref, ohlo_ref):
    chan, n_near = dh_ref.shape
    slots = gidx_ref.shape[0]
    atoms = pick_ref.shape[1]
    half = atoms // 2
    both = dot_nt(dhe_ref[...], jnp.concatenate([oh_ref[:half], oh_ref[half + atoms :]], axis=0))
    hi, lo = split(both[:chan] + both[chan:])
    spread = dot_nt(jnp.concatenate([hi, lo], axis=0), pick_ref[...])
    spread = spread[:chan] + spread[chan:]
    both = dot_nt(dhe_ref[...], oh_ref[half : half + atoms])
    dh_ref[:, 0:atoms] = spread[:, :atoms] + both[:chan] + both[chan:] + side_ref[:, 2:3]
    if n_near > atoms:
        dh_ref[:, atoms:] = spread[:, atoms:]
    ids16 = lax.broadcasted_iota(jnp.int32, (LANES, n_near), 0).astype(jnp.int16)
    one16 = jnp.ones((LANES, n_near), bf16)
    zero16 = jnp.zeros((LANES, n_near), bf16)
    for k in range(slots):
        place = jnp.broadcast_to(gidx_ref[k : k + 1, :] & 127, (LANES, n_near)).astype(jnp.int16)
        ohlo_ref[:, k * n_near : (k + 1) * n_near] = jnp.where(place == ids16, one16, zero16)
    lane = lax.broadcasted_iota(jnp.int32, (slots, 16 * slots), 1)
    sub = lax.broadcasted_iota(jnp.int32, (slots, 16 * slots), 0)
    adder = jnp.where(((lane >> 3) & (slots - 1)) == sub, 1.0, 0.0).astype(bf16)
    for i in range(4):
        total = dot(adder, split_rows(p_ref[i]).astype(bf16))
        q_ref[8 * i : 8 * i + 8, :] = 2.0 * total if i < 3 else total


def back_first_kernel(dh_ref, sp1_ref, m1_ref, mixt_ref, rrr_ref, da_ref):
    n_near = sp1_ref.shape[1]
    rows = rrr_ref.shape[0] // 2
    wide_cols = 2 * LANES

    def back_first(j):
        here = pl.ds(pl.multiple_of(j * wide_cols, wide_cols), wide_cols)
        slope = three_deep(dh_ref[:, here] * sp1_ref[:, here] * 2.0)
        scale = [dot(mixt_ref[0, g], slope) for g in range(3)]
        for l in range(ORDERS):
            hi, lo = split(m1_ref[l, :, here] * scale[GROUP[l]])
            out = dot(rrr_ref[...], jnp.concatenate([hi, lo], axis=0))
            da_ref[l, :, here] = out[:rows] + out[rows:]

    in_turns(0, n_near // wide_cols, back_first)


def back_edge_kernel(plan, *refs):
    atoms, near, wide, _, _ = plan
    n_wide = len(wide)
    blocks = refs[:n_wide]
    moment_src, geo_ref, y_ref, bk_ref, gidx_ref, da_ref, q_ref, ohlo_ref = refs[n_wide : n_wide + 8]
    push_ref, mass_ref, val_ref, dr_ref, moment_ref, sem = refs[n_wide + 8 :]
    fetch = pltpu.make_async_copy(moment_src, moment_ref, sem)
    fetch.start()
    bases, slots, n_near = bk_ref.shape
    tiles = atoms // LANES
    top_rows = val_ref.shape[0] // 6

    def back_geometry(t, mine):
        here = pl.ds(pl.multiple_of(t * LANES, LANES), LANES)
        ux, uy, uz, back, soft, fj = [geo_ref[i, :, here] for i in range(6)]
        dy = [None] * ORDERS
        ds = None
        for n in range(bases):
            basis = bk_ref[n, :, here]
            db = None
            for l in range(ORDERS):
                g = row(da_ref[l, n : n + 1, here]) + fj * row(da_ref[l, bases + n : bases + n + 1, here])
                if l:
                    dy[l] = g * basis if dy[l] is None else dy[l] + g * basis
                    db = db + g * y_ref[l - 1, :, here]
                else:
                    db = g
            db = db * basis * ((1.0 + n) - soft)
            ds = db if ds is None else ds + db
        if mine:
            ds = ds + q_ref[24:32, here]
        dux = SQRT3 * dy[1] + SQRT15 * (uy * dy[4] + uz * dy[7] + ux * dy[8]) - SQRT5 * ux * dy[6]
        duy = SQRT3 * dy[2] + SQRT15 * (ux * dy[4] + uz * dy[5] - uy * dy[8]) - SQRT5 * uy * dy[6]
        duz = SQRT3 * dy[3] + SQRT15 * (uy * dy[5] + ux * dy[7]) + 2.0 * SQRT5 * uz * dy[6]
        if mine:
            dux, duy, duz = [d + q_ref[8 * i : 8 * i + 8, here] for i, d in enumerate((dux, duy, duz))]
        along = ds - (ux * dux + uy * duy + uz * duz) * back
        for i, value in enumerate((dux * back + along * ux, duy * back + along * uy, duz * back + along * uz)):
            dr_ref[i, :, here] = value

    in_turns(0, tiles, lambda t: back_geometry(t, True))
    in_turns(tiles, n_near // LANES, lambda t: back_geometry(t, False))

    def place_tile(t):
        here = pl.ds(pl.multiple_of(t * LANES, LANES), LANES)
        gidx = gidx_ref[:, here]
        chunk_no = gidx >> 7
        parts = []
        for i in range(3):
            value = dr_ref[i, :, here]
            hi = value.astype(bf16).astype(f32)
            parts.append((hi, value - hi))
        chunk_ids = lax.broadcasted_iota(jnp.int32, (top_rows, LANES), 0)
        for k in range(slots):
            at = pl.ds(pl.multiple_of(k * n_near + t * LANES, LANES), LANES)
            hit = chunk_ids == row(chunk_no[k : k + 1, :], top_rows)
            for i in range(3):
                both = [jnp.where(hit, row(part[k : k + 1, :], top_rows), 0.0) for part in parts[i]]
                val_ref[2 * i * top_rows : 2 * (i + 1) * top_rows, at] = jnp.concatenate(both, axis=0).astype(bf16)

    in_turns(0, n_near // LANES, place_tile)
    landed = dot_nt(val_ref[...], ohlo_ref[...])
    fetch.wait()
    lines = push_ref.shape[0] // (n_wide + 1)
    for i in range(3):
        total = (
            landed[2 * i * top_rows : (2 * i + 1) * top_rows] + landed[(2 * i + 1) * top_rows : (2 * i + 2) * top_rows]
        )
        for g in range(n_wide):
            for t in range(tiles):
                cols = slice(t * LANES, (t + 1) * LANES)
                line = total[g * tiles + t : g * tiles + t + 1, :]
                if g < len(near):
                    here = slice(g * atoms + t * LANES, g * atoms + (t + 1) * LANES)
                    line = line - jnp.sum(dr_ref[i, :, here], axis=0, keepdims=True)
                line = -HALF_STEP * line
                at = i * tiles + t
                if g == 0:
                    line = line + moment_ref[i, :, cols]
                    push_ref[at : at + 1, :] = blocks[0][i : i + 1, cols]
                push_ref[(1 + g) * lines + at : (1 + g) * lines + at + 1, :] = line
                mass = HEAVY - (HEAVY - 1.0) * blocks[g][3:4, cols]
                mass_ref[g * lines + at : g * lines + at + 1, :] = mass


def in_hbm(x):
    return pltpu.with_memory_space_constraint(x, pltpu.HBM)


def run(name, body, operands, results, scratch=(), far=(), cost=None):
    sizes = [math.prod(x.shape) * x.dtype.itemsize // 2 for i, x in enumerate(operands) if i not in far]
    sizes += [math.prod(shape) * jnp.dtype(dtype).itemsize for shape, dtype in results]
    sizes += [math.prod(x.shape) * x.dtype.itemsize for x in scratch if x.memory_space == pltpu.VMEM]
    limit = sum(sizes) + 4 * MIB
    specs = [pl.BlockSpec(memory_space=pltpu.HBM if i in far else pltpu.VMEM) for i in range(len(operands))]
    return pl.pallas_call(
        body,
        out_shape=tuple(jax.ShapeDtypeStruct(shape, dtype) for shape, dtype in results),
        in_specs=specs,
        out_specs=tuple(pl.BlockSpec(memory_space=pltpu.VMEM) for _ in results),
        scratch_shapes=list(scratch),
        compiler_params=pltpu.CompilerParams(vmem_limit_bytes=limit),
        cost_estimate=cost,
        name=name,
    )(*[in_hbm(x) if i in far else x for i, x in enumerate(operands)])


def choose(block, embedding, radial_one, radial_two, mix_one, mix_two, read_one, read_two):
    atoms = block.shape[1]
    slots = block.shape[0] - HEAD
    chan = embedding.shape[1]
    bases = radial_one.shape[0]
    weights = (embedding, radial_one, radial_two, mix_one, mix_two, read_one[None], read_two[None])
    return run(
        "choose",
        choose_kernel,
        (block, *weights),
        (
            ((2 * atoms, slots * atoms), bf16),
            ((chan, 12 * bases), bf16),
            ((chan, 6 * bases), bf16),
            ((chan, LANES), f32),
            ((4 * bases, 2 * chan), bf16),
            ((2, chan, 18 * chan), bf16),
            ((2, 3, chan, 3 * chan), bf16),
        ),
        [pltpu.VMEM(w.shape, f32) for w in weights] + [pltpu.SemaphoreType.DMA((len(weights),))],
        range(1, 1 + len(weights)),
        cost=pl.CostEstimate(flops=2 * 10**9, bytes_accessed=2 * 10**6, transcendentals=0),
    )


def pushes(plan, blocks, momenta, chosen):
    atoms, near, wide, _, _ = plan
    oh, rrc, r2c, sides, rrr, mixa, mixt = chosen
    chan = rrc.shape[0]
    bases = rrr.shape[0] // 4
    slots = blocks[0].shape[0] - HEAD
    n_near = len(near) * atoms
    edges = slots * atoms
    top_rows = -(-len(wide) * atoms // LANES // 8) * 8
    lines = line_count(atoms)
    geo, y, yb, ub, bk, bt, gidx, pick, as1 = run(
        "edges",
        functools.partial(edge_kernel, plan),
        blocks,
        (
            ((6, slots, n_near), f32),
            ((ORDERS - 1, slots, n_near), f32),
            ((ORDERS - 1, slots, 8, atoms), f32),
            ((3, slots, 8, atoms), f32),
            ((bases, slots, n_near), f32),
            ((slots, 2 * bases, n_near), f32),
            ((slots, n_near), jnp.int32),
            ((n_near, atoms), bf16),
            ((ORDERS, 12 * bases, n_near), bf16),
        ),
    )
    m1, sp1, hid, hs = run(
        "first",
        functools.partial(first_kernel, plan),
        (*blocks, as1, rrc, sides, mixa),
        (((ORDERS, chan, n_near), f32), ((chan, n_near), f32), ((chan, n_near), f32), ((3 * chan, n_near), bf16)),
        [pltpu.VMEM((8, n_near), f32)],
    )
    hj, w, slope, car = run(
        "gather",
        gather_kernel,
        (hid, hs, oh, pick, gidx, bt, geo, r2c),
        (((chan, edges), f32),) * 4,
        [pltpu.VMEM((3 * chan, 2 * atoms), bf16)],
    )
    m2, dinv = run(
        "moments",
        moment_kernel,
        (car, yb, mixa, mixt, sides),
        (((ORDERS, chan, atoms), f32), ((3 * chan, atoms), f32)),
        [pltpu.VMEM((3 * chan, atoms), f32)],
    )
    dhe, p = run(
        "back_second",
        back_second_kernel,
        (m2, dinv, car, hj, w, slope, ub),
        (((2 * chan, edges), bf16), ((4, 8 * slots, atoms), f32)),
    )
    dh, q, ohlo = run(
        "scatter",
        scatter_kernel,
        (oh, pick, dhe, sides, p, gidx),
        (((chan, n_near), f32), ((4 * slots, atoms), f32), ((LANES, slots * n_near), bf16)),
    )
    (da,) = run("back_first", back_first_kernel, (dh, sp1, m1, mixt, rrr), (((ORDERS, 2 * bases, n_near), f32),))
    return run(
        "back_edges",
        functools.partial(back_edge_kernel, plan),
        (*blocks, momenta, geo, y, bk, gidx, da, q, ohlo),
        ((((len(wide) + 1) * lines, LANES), f32), ((len(wide) * lines, LANES), f32)),
        [
            pltpu.VMEM((6 * top_rows, slots * n_near), bf16),
            pltpu.VMEM((3, slots, n_near), f32),
            pltpu.VMEM(momenta.shape, f32),
            pltpu.SemaphoreType.DMA(()),
        ],
        (len(blocks),),
    )


def line_count(atoms):
    return 3 * (atoms // LANES)


def ring_plan(domains, atoms):
    near = list(dict.fromkeys(o % domains for o in (0, 1, -1)))
    wide = list(dict.fromkeys(near + [o % domains for o in (2, -2)]))
    before = tuple(wide.index((o - 1) % domains) for o in near)
    after = tuple(wide.index((o + 1) % domains) for o in near)
    return atoms, tuple(near), tuple(wide), before, after


def mode_turns(bead_total):
    bead = np.arange(bead_total, dtype=np.float64)[:, None]
    mode = np.arange(bead_total, dtype=np.float64)[None, :]
    phase = 2.0 * np.pi * bead * mode / bead_total
    half_total = bead_total // 2
    table = math.sqrt(2.0 / bead_total) * np.where(mode < half_total, np.cos(phase), np.sin(phase))
    table = np.where(mode == half_total, np.cos(np.pi * bead) / math.sqrt(bead_total), table)
    table = np.where(mode == 0, 1.0 / math.sqrt(bead_total), table)
    angles = bead_total * np.sin(np.pi * mode[0] / bead_total)
    safe = np.where(mode[0] == 0, 1.0, angles)
    reach = np.where(mode[0] == 0, STEP, STEP * np.sin(angles) / safe)
    stiff = angles * np.sin(angles) / STEP
    return [[float(x) for x in (table * factor[None, :]) @ table[0]] for factor in (np.cos(angles), reach, stiff)]


def pack_kernel(coord_src, species_src, send_src, slot_src, block_ref, coord_ref, species_ref, send_ref, slot_ref, sems):
    pairs = ((coord_src, coord_ref), (species_src, species_ref), (send_src, send_ref), (slot_src, slot_ref))
    fetches = [pltpu.make_async_copy(src, dst, sems.at[i]) for i, (src, dst) in enumerate(pairs)]
    for fetch in fetches:
        fetch.start()
    for fetch in fetches:
        fetch.wait()
    atoms = block_ref.shape[1]
    for i in range(3):
        block_ref[i : i + 1, :] = coord_ref[i]
    block_ref[3:4, :] = species_ref[...].astype(f32)
    block_ref[4:5, :] = send_ref[...].astype(f32)
    block_ref[5:HEAD, :] = jnp.zeros((HEAD - 5, atoms), f32)
    block_ref[HEAD:, :] = slot_ref[...].astype(f32)


def turn_kernel(shape, bead_ref, domain_ref, mass_ref, *refs):
    outer, inner, domains, wide = shape
    message_ref = refs[outer]
    turns = mode_turns(outer * inner)
    lines = mass_ref.shape[0] // len(wide)
    my_domain = domain_ref[0]
    my_inner = lax.rem(bead_ref[0], inner)
    if domains > len(wide):
        message_ref[...] = jnp.zeros_like(message_ref)
    masses = [mass_ref[g * lines : (g + 1) * lines, :] for g in range(len(wide))]
    sources = []
    for z in range(outer):
        sources.append([refs[z][g * lines : (g + 1) * lines, :] for g in range(len(wide) + 1)])
    for s in range(inner):
        wraps = jnp.full((lines, LANES), my_inner + s) >= inner
        weights = []
        for turn in turns:
            row_of = []
            for z in range(outer):
                there = turn[(z * inner + s) % (outer * inner)]
                round_it = turn[(z * inner + s - inner) % (outer * inner)]
                row_of.append(jnp.where(wraps, jnp.full((lines, LANES), round_it), jnp.full((lines, LANES), there)))
            weights.append(row_of)
        to_inner = lax.rem(my_inner + s, inner)
        for g in range(len(wide)):
            turned = sum(weights[0][z] * sources[z][1 + g] for z in range(outer))
            drift = sum(weights[1][z] * sources[z][1 + g] for z in range(outer))
            new_q = drift / masses[g]
            new_p = turned
            if g == 0:
                new_q = new_q + sum(weights[0][z] * sources[z][0] for z in range(outer))
                new_p = new_p - masses[g] * sum(weights[2][z] * sources[z][0] for z in range(outer))
            to = to_inner * domains + lax.rem(my_domain + wide[g], domains)
            message_ref[to, 0:lines, :] = new_q
            message_ref[to, lines:, :] = new_p


def sum_kernel(arrived_ref, q_ref, p_ref):
    total = arrived_ref[0]
    for i in range(1, arrived_ref.shape[0]):
        total = total + arrived_ref[i]
    lines = total.shape[0] // 2
    tiles = q_ref.shape[2] // LANES
    for i in range(3):
        for t in range(tiles):
            at = i * tiles + t
            q_ref[i, :, t * LANES : (t + 1) * LANES] = total[at : at + 1]
            p_ref[i, :, t * LANES : (t + 1) * LANES] = total[lines + at : lines + at + 1]


def shards(
    positions, momenta, species, neighbours, send_list, embedding, radial_one, radial_two, mix_one, mix_two,
    read_one, read_two,
):
    slots, atoms = neighbours.shape
    domains = lax.axis_size("space")
    beads = lax.axis_size("bead")
    inner = next(d for d in range(1, beads + 1) if beads % d == 0 and d * d >= beads)
    outer = beads // inner
    plan = ring_plan(domains, atoms)
    wide = plan[2]
    vmem = pl.BlockSpec(memory_space=pltpu.VMEM)
    smem = pl.BlockSpec(memory_space=pltpu.SMEM)
    far = pl.BlockSpec(memory_space=pltpu.HBM)
    small = pltpu.CompilerParams(vmem_limit_bytes=4 * MIB)
    coord_rows = jnp.transpose(positions, (1, 0, 2))
    moment_rows = jnp.transpose(momenta, (1, 0, 2))
    block = pl.pallas_call(
        pack_kernel,
        out_shape=jax.ShapeDtypeStruct((HEAD + slots, atoms), f32),
        in_specs=[far] * 4,
        out_specs=vmem,
        scratch_shapes=[
            pltpu.VMEM(coord_rows.shape, f32),
            pltpu.VMEM((1, atoms), jnp.int32),
            pltpu.VMEM((1, atoms), jnp.int32),
            pltpu.VMEM((slots, atoms), jnp.int32),
            pltpu.SemaphoreType.DMA((4,)),
        ],
        compiler_params=small,
        name="pack",
    )(in_hbm(coord_rows), in_hbm(species[None]), in_hbm(send_list[None]), in_hbm(neighbours))
    blocks = [block]
    for offset in wide[1:]:
        blocks.append(lax.ppermute(block, "space", [(i, (i - offset) % domains) for i in range(domains)]))
    chosen = choose(block, embedding, radial_one, radial_two, mix_one, mix_two, read_one, read_two)
    pushed, masses = pushes(plan, blocks, moment_rows, chosen)
    sources = [pushed] * outer
    for z in sorted(range(1, outer), key=lambda z: -min(z, outer - z)):
        sources[z] = lax.ppermute(pushed, "bead", [(b, (b + z * inner) % beads) for b in range(beads)])
    here = [lax.axis_index(axis).astype(jnp.int32).reshape(1) for axis in ("bead", "space")]
    lines = line_count(atoms)
    messages = pl.pallas_call(
        functools.partial(turn_kernel, (outer, inner, domains, wide)),
        out_shape=jax.ShapeDtypeStruct((inner * domains, 2 * lines, LANES), f32),
        in_specs=[smem, smem, vmem] + [vmem] * outer,
        out_specs=vmem,
        compiler_params=small,
        name="turn",
    )(*here, masses, *sources)
    rows = [[z * inner * domains + i for i in range(inner * domains)] for z in range(outer)]
    arrived = lax.all_to_all(messages, ("bead", "space"), 0, 0, axis_index_groups=rows, tiled=True)
    new_q, new_p = pl.pallas_call(
        sum_kernel,
        out_shape=(jax.ShapeDtypeStruct((3, 1, atoms), f32),) * 2,
        in_specs=[vmem],
        out_specs=(vmem, vmem),
        compiler_params=small,
        name="sum",
    )(arrived)
    return (jnp.transpose(new_q, (1, 0, 2)), jnp.transpose(new_p, (1, 0, 2)))


def solution(mesh):
    placed = (
        P("bead", None, "space"),
        P("bead", None, "space"),
        P("space"),
        P(None, "space"),
        P("space"),
        P(),
        P(),
        P(),
        P(),
        P(),
        P(),
        P(),
    )
    return jax.shard_map(
        shards,
        mesh=mesh,
        in_specs=placed,
        out_specs=(P("bead", None, "space"), P("bead", None, "space")),
        check_vma=False,
    )
```

```python
import functools
import math

import jax
import jax.numpy as jnp
import numpy as np
from jax import lax
from jax.experimental import pallas as pl
from jax.experimental.pallas import tpu as pltpu
from jax.sharding import PartitionSpec as P

STEP = 2.0
HALF_STEP = 1.0
HEAVY = 16.0
SQRT3 = math.sqrt(3.0)
SQRT5 = math.sqrt(5.0)
SQRT15 = math.sqrt(15.0)
LANES = 128
ORDERS = 9
GROUP = (0, 1, 1, 1, 2, 2, 2, 2, 2)
HEAD = 8
MIB = 1024 * 1024
f32 = jnp.float32
bf16 = jnp.bfloat16


def split(x):
    hi = x.astype(bf16)
    return hi, (x - hi.astype(f32)).astype(bf16)


def split_rows(x):
    hi = x.astype(bf16).astype(f32)
    return jnp.concatenate([hi, x - hi], axis=0)


def split3(x):
    hi = x.astype(bf16)
    rest = x - hi.astype(f32)
    mid = rest.astype(bf16)
    return hi, mid, (rest - mid.astype(f32)).astype(bf16)


def six_rows(x, order):
    hi = x.astype(bf16).astype(f32)
    mid = (x - hi).astype(bf16).astype(f32)
    parts = (hi, mid, x - hi - mid)
    return jnp.concatenate([parts[i] for i in order], axis=0)


VALUE_ORDER = (0, 1, 0, 1, 2, 0)
WEIGHT_ORDER = (0, 0, 1, 1, 0, 2)


def dot(a, b):
    return jnp.dot(a, b, preferred_element_type=f32)


def dot_nt(a, b):
    return lax.dot_general(a, b, (((1,), (1,)), ((), ())), preferred_element_type=f32)


def in_turns(start, stop, step, most=4):
    per_turn = next(n for n in range(most, 0, -1) if (stop - start) % n == 0)

    def turn(i, carry):
        for j in range(per_turn):
            step(start + i * per_turn + j)
        return carry

    lax.fori_loop(0, (stop - start) // per_turn, turn, 0)


def row(x, rows=8):
    return jnp.broadcast_to(x, (rows, x.shape[1]))


def lookup(chunks, wanted, position):
    out = None
    for number, chunk in chunks:
        got = jnp.take_along_axis(row(chunk), position, axis=1, mode="promise_in_bounds")
        out = got if out is None else jnp.where(wanted == number, got, out)
    return out


def harmonics(ux, uy, uz):
    return [
        None,
        SQRT3 * ux,
        SQRT3 * uy,
        SQRT3 * uz,
        SQRT15 * ux * uy,
        SQRT15 * uy * uz,
        0.5 * SQRT5 * (2.0 * uz * uz - ux * ux - uy * uy),
        SQRT15 * ux * uz,
        0.5 * SQRT15 * (ux * ux - uy * uy),
    ]


def silu_parts(v):
    gate = 1.0 / (1.0 + jnp.exp(-v))
    return v * gate, gate * (1.0 + v * (1.0 - gate))


def choose_kernel(block_ref, *refs):
    sources = refs[:7]
    oh_ref, rrc_ref, r2c_ref, side_ref, rrr_ref, mixa_ref, mixt_ref = refs[7:14]
    held = refs[14:21]
    sems = refs[21]
    emb_ref, rad1_ref, rad2_ref, mix1_ref, mix2_ref, read1_ref, read2_ref = held
    fetches = [pltpu.make_async_copy(src, dst, sems.at[i]) for i, (src, dst) in enumerate(zip(sources, held))]
    for fetch in fetches:
        fetch.start()
    chan = emb_ref.shape[1]
    bases = rad1_ref.shape[0]
    atoms = block_ref.shape[1]
    slots = block_ref.shape[0] - HEAD

    ids16 = lax.broadcasted_iota(jnp.int32, (LANES, atoms), 0).astype(jnp.int16)
    one16 = jnp.ones((LANES, atoms), bf16)
    zero16 = jnp.zeros((LANES, atoms), bf16)
    for k in range(slots):
        slot = block_ref[HEAD + k : HEAD + k + 1, :].astype(jnp.int32)
        wanted = jnp.broadcast_to(slot, (LANES, atoms)).astype(jnp.int16)
        for r in range(oh_ref.shape[0] // LANES):
            hit = wanted - jnp.int16(r * LANES) == ids16
            oh_ref[r * LANES : (r + 1) * LANES, k * atoms : (k + 1) * atoms] = jnp.where(hit, one16, zero16)

    for fetch in fetches:
        fetch.wait()
    emb0 = emb_ref[0:1, :]
    emb_d = emb_ref[1:2, :] - emb0
    rr = jnp.concatenate([rad1_ref[...] * emb0, rad1_ref[...] * emb_d], axis=0) * (1.0 / slots)
    rr_hi = rr.astype(bf16).astype(f32)
    rr_lo = rr - rr_hi
    r2 = rad2_ref[...] * (1.0 / slots)
    zeros = jnp.zeros((8, chan), f32)
    turned1 = jnp.concatenate([six_rows(rr, WEIGHT_ORDER)] + [zeros] * (16 - 12 * bases // 8), axis=0).T
    sides = jnp.concatenate([emb0, emb_d, read1_ref[...], read2_ref[...], zeros[:4]], axis=0)
    turned2 = jnp.concatenate([six_rows(r2, WEIGHT_ORDER)] + [zeros] * (16 - 6 * bases // 8), axis=0).T
    rrc_ref[...] = turned1[:, : 12 * bases].astype(bf16)
    r2c_ref[...] = turned2[:, : 6 * bases].astype(bf16)
    side_ref[...] = jnp.concatenate([sides] + [zeros] * 15, axis=0).T
    rrr_ref[...] = jnp.concatenate(
        [jnp.concatenate([rr_hi, rr_hi], axis=1), jnp.concatenate([rr_lo, jnp.zeros_like(rr_lo)], axis=1)], axis=0
    ).astype(bf16)
    for i, ref in enumerate((mix1_ref, mix2_ref)):
        parts = split3(ref[...])
        for at, part in enumerate(WEIGHT_ORDER):
            mixa_ref[i, :, at * 3 * chan : (at + 1) * 3 * chan] = parts[part]
        for g in range(3):
            hi, lo = split(ref[:, g * chan : (g + 1) * chan].T)
            mixt_ref[i, g] = jnp.concatenate([hi, hi, lo], axis=1)


def six_deep(x):
    parts = split3(x)
    return jnp.concatenate([parts[i] for i in VALUE_ORDER], axis=0)


def three_deep(x):
    hi, lo = split(x)
    return jnp.concatenate([hi, lo, hi], axis=0)


def edge_kernel(plan, *refs):
    atoms, near, wide, before, after = plan
    n_wide = len(wide)
    blocks = refs[:n_wide]
    geo_ref, y_ref, yb_ref, ub_ref, bk_ref, bt_ref, gidx_ref, pick_ref, as_ref = refs[n_wide:]
    bases = bk_ref.shape[0]
    slots = gidx_ref.shape[0]
    tiles = atoms // LANES
    half = atoms // 2
    half_tiles = half // LANES
    order_col = lax.broadcasted_iota(jnp.int32, (bases, LANES), 0).astype(f32)
    tables = []
    for quantity in range(4):
        chunks = []
        for g in range(n_wide):
            for t in range(tiles):
                chunks.append((g * tiles + t, blocks[g][quantity : quantity + 1, t * LANES : (t + 1) * LANES]))
        tables.append(chunks)
    for q in range(len(near)):
        ghosts = []
        for t in range(half_tiles):
            ghosts.append(
                (t, blocks[before[q]][4:5, half + t * LANES : half + (t + 1) * LANES] + float(before[q] * atoms))
            )
        for t in range(half_tiles):
            ghosts.append(
                (
                    half_tiles + tiles + t,
                    blocks[after[q]][4:5, t * LANES : (t + 1) * LANES] + float(after[q] * atoms),
                )
            )
        if q == 0:
            ids16 = lax.broadcasted_iota(jnp.int32, (pick_ref.shape[0], LANES), 0).astype(jnp.int16)
            one16 = jnp.ones(ids16.shape, bf16)
            zero16 = jnp.zeros(ids16.shape, bf16)
            for t, (_, chunk) in enumerate(ghosts):
                wanted = jnp.broadcast_to(chunk.astype(jnp.int32), ids16.shape).astype(jnp.int16)
                pick_ref[:, t * LANES : (t + 1) * LANES] = jnp.where(wanted == ids16, one16, zero16)
        for t in range(tiles):
            cols = slice(t * LANES, (t + 1) * LANES)
            here = slice(q * atoms + t * LANES, q * atoms + (t + 1) * LANES)
            slot = blocks[q][HEAD : HEAD + slots, cols].astype(jnp.int32)
            chunk_no = slot >> 7
            far = lookup(ghosts, chunk_no, slot & 127).astype(jnp.int32)
            own = (slot >= half) & (slot < half + atoms)
            gidx = jnp.where(own, slot + (q * atoms - half), far)
            gidx_ref[:, here] = gidx
            chunk_no = gidx >> 7
            place = gidx & 127
            xj, yj, zj, fj = [lookup(tables[i], chunk_no, place) for i in range(4)]
            rx = xj - row(blocks[q][0:1, cols])
            ry = yj - row(blocks[q][1:2, cols])
            rz = zj - row(blocks[q][2:3, cols])
            soft = jnp.sqrt(rx * rx + ry * ry + rz * rz + 1.0)
            back = 1.0 / soft
            ux, uy, uz = rx * back, ry * back, rz * back
            for i, value in enumerate((ux, uy, uz, back, soft, fj)):
                geo_ref[i, :, here] = value
            if q == 0:
                for i, value in enumerate((ux, uy, uz)):
                    for k in range(slots):
                        ub_ref[i, k, :, cols] = row(value[k : k + 1, :])
            sphere = harmonics(ux, uy, uz)
            for l in range(1, ORDERS):
                y_ref[l - 1, :, here] = sphere[l]
                if q == 0:
                    for k in range(slots):
                        yb_ref[l - 1, k, :, cols] = row(sphere[l][k : k + 1, :])
            for n in range(bases):
                bk_ref[n, :, here] = jnp.exp(-0.5 * (soft - (1.0 + n)) ** 2)
            for k in range(slots):
                basis = jnp.exp(-0.5 * (row(soft[k : k + 1, :], bases) - (1.0 + order_col)) ** 2)
                bt_ref[k, 0:bases, here] = basis
                bt_ref[k, bases : 2 * bases, here] = basis * row(fj[k : k + 1, :], bases)
            low = [None] * ORDERS
            for k in range(slots):
                basis = bt_ref[k, :, here]
                for l in range(ORDERS):
                    term = basis if l == 0 else basis * row(y_ref[l - 1, k : k + 1, here], 2 * bases)
                    low[l] = term if low[l] is None else low[l] + term
            for l in range(ORDERS):
                as_ref[l, :, here] = six_rows(low[l], VALUE_ORDER).astype(bf16)


def first_kernel(plan, *refs):
    atoms, near, wide, _, _ = plan
    n_wide = len(wide)
    blocks = refs[:n_wide]
    as_ref, rrc_ref, side_ref, mixa_ref, m1_ref, sp1_ref, hid_ref, hs_ref, flag_ref = refs[n_wide:]
    chan = m1_ref.shape[1]
    n_near = m1_ref.shape[2]

    for q in range(len(near)):
        flag_ref[0:1, q * atoms : (q + 1) * atoms] = blocks[q][3:4, :]
    wide_cols = 2 * LANES
    emb0_col = side_ref[:, 0:1]
    embd_col = side_ref[:, 1:2]

    def first(j):
        here = pl.ds(pl.multiple_of(j * wide_cols, wide_cols), wide_cols)
        inv = [None, None, None]
        for l in range(ORDERS):
            m = dot(rrc_ref[...], as_ref[l, :, here])
            m1_ref[l, :, here] = m
            inv[GROUP[l]] = m * m if inv[GROUP[l]] is None else inv[GROUP[l]] + m * m
        value = dot(mixa_ref[0], six_deep(jnp.concatenate(inv, axis=0)))
        act, slope = silu_parts(value)
        sp1_ref[:, here] = slope
        hidden = act + emb0_col + embd_col * flag_ref[0:1, here]
        hid_ref[:, here] = hidden
        for part, piece in enumerate(split3(hidden)):
            hs_ref[part * chan : (part + 1) * chan, here] = piece

    in_turns(0, n_near // wide_cols, first)


def gather_kernel(hid_ref, hs_ref, oh_ref, pick_ref, gidx_ref, bt_ref, geo_ref, r2c_ref,
                  hj_ref, w_ref, slope_ref, car_ref, ext_ref):
    slots = bt_ref.shape[0]
    bases = bt_ref.shape[1] // 2
    chan, n_near = hid_ref.shape
    atoms = hj_ref.shape[1] // slots
    half = atoms // 2
    ghosts = dot(hs_ref[...], pick_ref[...]).astype(bf16)
    ext_ref[:, 0:half] = ghosts[:, :half]
    ext_ref[:, half : half + atoms] = hs_ref[:, 0:atoms]
    ext_ref[:, half + atoms :] = ghosts[:, half:]
    reach = 1.0 + lax.broadcasted_iota(jnp.int32, (bases, atoms), 0).astype(f32)
    for k in range(slots):
        here = slice(k * atoms, (k + 1) * atoms)
        basis = bt_ref[k, 0:bases, 0:atoms]
        for ref, value in ((w_ref, basis), (slope_ref, basis * (reach - row(geo_ref[4, k : k + 1, 0:atoms], bases)))):
            ref[:, here] = dot(r2c_ref[...], six_rows(value, VALUE_ORDER).astype(bf16))

    for pair in range(slots // 2):
        by_lane = 4 * LANES if atoms >= 4 * LANES else 0
        by_product = 2 * atoms - by_lane
        first = pair * 2 * atoms
        here = slice(first, first + by_product)
        both = dot(ext_ref[...], oh_ref[:, here])
        wanted = gidx_ref[2 * pair + 1 : 2 * pair + 2, 0:atoms]
        for t in range(by_lane // LANES):
            at = slice(first + by_product + t * LANES, first + by_product + (t + 1) * LANES)
            start = atoms - by_lane + t * LANES
            mine = row(wanted[:, start : start + LANES])
            chunk_no = mine >> 7
            place = mine & 127
            for c in range(chan // 8):
                rows = slice(8 * c, 8 * c + 8)
                feat = None
                for chunk in range(n_near // LANES):
                    held = hid_ref[rows, chunk * LANES : (chunk + 1) * LANES]
                    got = jnp.take_along_axis(held, place, axis=1, mode="promise_in_bounds")
                    feat = got if feat is None else jnp.where(chunk_no == chunk, got, feat)
                hj_ref[rows, at] = feat
                car_ref[rows, at] = feat * w_ref[rows, at]
        feat = both[:chan] + (both[chan : 2 * chan] + both[2 * chan :])
        hj_ref[:, here] = feat
        car_ref[:, here] = feat * w_ref[:, here]


def moment_kernel(car_ref, yb_ref, mixa_ref, mixt_ref, side_ref, m2_ref, dinv_ref, inv_ref):
    slots = yb_ref.shape[1]
    chan, atoms = m2_ref.shape[1:]
    tiles = atoms // LANES
    wide_cols = 2 * LANES
    rows = 32
    groups = chan // rows

    def moments(step):
        t = step // groups
        c = step % groups
        cols = pl.ds(pl.multiple_of(t * LANES, LANES), LANES)
        base = pl.multiple_of(c * rows, rows)
        acc = [[None] * ORDERS for _ in range(rows // 8)]
        for k in range(slots):
            at = pl.ds(pl.multiple_of(k * atoms + t * LANES, LANES), LANES)
            got = car_ref[pl.ds(base, rows), at]
            for l in range(ORDERS):
                yb = yb_ref[l - 1, k, :, cols] if l else None
                for h in range(rows // 8):
                    part = got[8 * h : 8 * h + 8]
                    term = part * yb if l else part
                    acc[h][l] = term if acc[h][l] is None else acc[h][l] + term
        for h in range(rows // 8):
            inv = [None] * 3
            for l in range(ORDERS):
                m2_ref[l, pl.ds(pl.multiple_of(base + 8 * h, 8), 8), cols] = acc[h][l]
                sq = acc[h][l] * acc[h][l]
                g = GROUP[l]
                inv[g] = sq if inv[g] is None else inv[g] + sq
            for g in range(3):
                inv_ref[pl.ds(pl.multiple_of(g * chan + base + 8 * h, 8), 8), cols] = inv[g]

    in_turns(0, tiles * groups, moments, 2)
    read2_col = side_ref[:, 3:4]
    for t in range(atoms // wide_cols):
        cols = slice(t * wide_cols, (t + 1) * wide_cols)
        _, slope = silu_parts(dot(mixa_ref[1], six_deep(inv_ref[:, cols])))
        slope = three_deep(slope * (2.0 * read2_col))
        for g, scale in enumerate((1.0, 0.5 * SQRT3, 0.5 * SQRT15)):
            dinv_ref[g * chan : (g + 1) * chan, cols] = scale * dot(mixt_ref[1, g], slope)


def back_second_kernel(m2_ref, dinv_ref, car_ref, hj_ref, w_ref, slope_ref, ub_ref, dhe_ref, p_ref):
    slots = ub_ref.shape[1]
    chan, atoms = m2_ref.shape[1:]
    tiles = atoms // LANES
    pairs = chan // 16
    per_turn = 8 if pairs % 8 == 0 else 1
    k_step = slots // 2

    def back_moments(t, carry):
        cols = pl.ds(pl.multiple_of(t * LANES, LANES), LANES)

        def one(c, acc, k0):
            forms = []
            for h in range(2):
                rows = pl.ds(pl.multiple_of(c * 16 + 8 * h, 8), 8)
                scale = [dinv_ref[pl.ds(pl.multiple_of(g * chan + c * 16 + 8 * h, 8), 8), cols] for g in range(3)]
                dm = [m2_ref[l, rows, cols] * scale[GROUP[l]] for l in range(ORDERS)]
                low = dm[6] * (1.0 / SQRT3)
                forms.append((dm[0], dm[1], dm[2], dm[3], dm[8] - low, -dm[8] - low, low + low, dm[4], dm[5], dm[7]))
            base = pl.multiple_of(c * 16, 16)
            for k in range(k0, k0 + k_step):
                at = pl.ds(pl.multiple_of(k * atoms + t * LANES, LANES), LANES)
                got = car_ref[pl.ds(base, 16), at]
                stretch = hj_ref[pl.ds(base, 16), at] * slope_ref[pl.ds(base, 16), at]
                ux, uy, uz = [ub_ref[i, k, :, cols] for i in range(3)]
                out = []
                for h in range(2):
                    mid, dx, dy, dz, qxx, qyy, qzz, qxy, qyz, qxz = forms[h]
                    gx = dx + qxx * ux + qxy * uy + qxz * uz
                    gy = dy + qxy * ux + qyy * uy + qyz * uz
                    gz = dz + qxz * ux + qyz * uy + qzz * uz
                    out.append(mid + (gx + dx) * ux + (gy + dy) * uy + (gz + dz) * uz)
                    part = got[8 * h : 8 * h + 8]
                    at_acc = 4 * (k - k0)
                    for i, g in enumerate((gx, gy, gz)):
                        acc[at_acc + i] = acc[at_acc + i] + part * g
                    acc[at_acc + 3] = acc[at_acc + 3] + out[h] * stretch[8 * h : 8 * h + 8]
                hi, lo = split(jnp.concatenate(out, axis=0) * w_ref[pl.ds(base, 16), at])
                dhe_ref[pl.ds(base, 16), at] = hi
                dhe_ref[pl.ds(pl.multiple_of(chan + c * 16, 16), 16), at] = lo

        for k0 in range(0, slots, k_step):

            def over(c, acc, k0=k0):
                acc = list(acc)
                for i in range(per_turn):
                    one(per_turn * c + i, acc, k0)
                return tuple(acc)

            start = tuple(jnp.zeros((8, LANES), f32) for _ in range(4 * k_step))
            acc = lax.fori_loop(0, pairs // per_turn, over, start)
            for k in range(k_step):
                for i in range(4):
                    p_ref[i, 8 * (k0 + k) : 8 * (k0 + k) + 8, cols] = acc[4 * k + i]
        return carry

    lax.fori_loop(0, tiles, back_moments, 0)


def scatter_kernel(oh_ref, pick_ref, dhe_ref, side_ref, p_ref, gidx_ref, dh_ref, q_ref, ohlo_ref):
    chan, n_near = dh_ref.shape
    slots = gidx_ref.shape[0]
    atoms = pick_ref.shape[1]
    half = atoms // 2
    both = dot_nt(dhe_ref[...], jnp.concatenate([oh_ref[:half], oh_ref[half + atoms :]], axis=0))
    hi, lo = split(both[:chan] + both[chan:])
    spread = dot_nt(jnp.concatenate([hi, lo], axis=0), pick_ref[...])
    spread = spread[:chan] + spread[chan:]
    both = dot_nt(dhe_ref[...], oh_ref[half : half + atoms])
    dh_ref[:, 0:atoms] = spread[:, :atoms] + both[:chan] + both[chan:] + side_ref[:, 2:3]
    if n_near > atoms:
        dh_ref[:, atoms:] = spread[:, atoms:]
    ids16 = lax.broadcasted_iota(jnp.int32, (LANES, n_near), 0).astype(jnp.int16)
    one16 = jnp.ones((LANES, n_near), bf16)
    zero16 = jnp.zeros((LANES, n_near), bf16)
    for k in range(slots):
        place = jnp.broadcast_to(gidx_ref[k : k + 1, :] & 127, (LANES, n_near)).astype(jnp.int16)
        ohlo_ref[:, k * n_near : (k + 1) * n_near] = jnp.where(place == ids16, one16, zero16)
    lane = lax.broadcasted_iota(jnp.int32, (slots, 16 * slots), 1)
    sub = lax.broadcasted_iota(jnp.int32, (slots, 16 * slots), 0)
    adder = jnp.where(((lane >> 3) & (slots - 1)) == sub, 1.0, 0.0).astype(bf16)
    for i in range(4):
        total = dot(adder, split_rows(p_ref[i]).astype(bf16))
        q_ref[8 * i : 8 * i + 8, :] = 2.0 * total if i < 3 else total


def back_first_kernel(dh_ref, sp1_ref, m1_ref, mixt_ref, rrr_ref, da_ref):
    n_near = sp1_ref.shape[1]
    rows = rrr_ref.shape[0] // 2
    wide_cols = 2 * LANES

    def back_first(j):
        here = pl.ds(pl.multiple_of(j * wide_cols, wide_cols), wide_cols)
        slope = three_deep(dh_ref[:, here] * sp1_ref[:, here] * 2.0)
        scale = [dot(mixt_ref[0, g], slope) for g in range(3)]
        for l in range(ORDERS):
            hi, lo = split(m1_ref[l, :, here] * scale[GROUP[l]])
            out = dot(rrr_ref[...], jnp.concatenate([hi, lo], axis=0))
            da_ref[l, :, here] = out[:rows] + out[rows:]

    in_turns(0, n_near // wide_cols, back_first)


def back_edge_kernel(plan, *refs):
    atoms, near, wide, _, _ = plan
    n_wide = len(wide)
    blocks = refs[:n_wide]
    moment_src, geo_ref, y_ref, bk_ref, gidx_ref, da_ref, q_ref, ohlo_ref = refs[n_wide : n_wide + 8]
    push_ref, mass_ref, val_ref, dr_ref, moment_ref, sem = refs[n_wide + 8 :]
    fetch = pltpu.make_async_copy(moment_src, moment_ref, sem)
    fetch.start()
    bases, slots, n_near = bk_ref.shape
    tiles = atoms // LANES
    top_rows = val_ref.shape[0] // 6

    def back_geometry(t, mine):
        here = pl.ds(pl.multiple_of(t * LANES, LANES), LANES)
        ux, uy, uz, back, soft, fj = [geo_ref[i, :, here] for i in range(6)]
        dy = [None] * ORDERS
        ds = None
        for n in range(bases):
            basis = bk_ref[n, :, here]
            db = None
            for l in range(ORDERS):
                g = row(da_ref[l, n : n + 1, here]) + fj * row(da_ref[l, bases + n : bases + n + 1, here])
                if l:
                    dy[l] = g * basis if dy[l] is None else dy[l] + g * basis
                    db = db + g * y_ref[l - 1, :, here]
                else:
                    db = g
            db = db * basis * ((1.0 + n) - soft)
            ds = db if ds is None else ds + db
        if mine:
            ds = ds + q_ref[24:32, here]
        dux = SQRT3 * dy[1] + SQRT15 * (uy * dy[4] + uz * dy[7] + ux * dy[8]) - SQRT5 * ux * dy[6]
        duy = SQRT3 * dy[2] + SQRT15 * (ux * dy[4] + uz * dy[5] - uy * dy[8]) - SQRT5 * uy * dy[6]
        duz = SQRT3 * dy[3] + SQRT15 * (uy * dy[5] + ux * dy[7]) + 2.0 * SQRT5 * uz * dy[6]
        if mine:
            dux, duy, duz = [d + q_ref[8 * i : 8 * i + 8, here] for i, d in enumerate((dux, duy, duz))]
        along = ds - (ux * dux + uy * duy + uz * duz) * back
        for i, value in enumerate((dux * back + along * ux, duy * back + along * uy, duz * back + along * uz)):
            dr_ref[i, :, here] = value

    in_turns(0, tiles, lambda t: back_geometry(t, True))
    in_turns(tiles, n_near // LANES, lambda t: back_geometry(t, False))

    def place_tile(t):
        here = pl.ds(pl.multiple_of(t * LANES, LANES), LANES)
        gidx = gidx_ref[:, here]
        chunk_no = gidx >> 7
        parts = []
        for i in range(3):
            value = dr_ref[i, :, here]
            hi = value.astype(bf16).astype(f32)
            parts.append((hi, value - hi))
        chunk_ids = lax.broadcasted_iota(jnp.int32, (top_rows, LANES), 0)
        for k in range(slots):
            at = pl.ds(pl.multiple_of(k * n_near + t * LANES, LANES), LANES)
            hit = chunk_ids == row(chunk_no[k : k + 1, :], top_rows)
            for i in range(3):
                both = [jnp.where(hit, row(part[k : k + 1, :], top_rows), 0.0) for part in parts[i]]
                val_ref[2 * i * top_rows : 2 * (i + 1) * top_rows, at] = jnp.concatenate(both, axis=0).astype(bf16)

    in_turns(0, n_near // LANES, place_tile)
    landed = dot_nt(val_ref[...], ohlo_ref[...])
    fetch.wait()
    lines = push_ref.shape[0] // (n_wide + 1)
    for i in range(3):
        total = (
            landed[2 * i * top_rows : (2 * i + 1) * top_rows] + landed[(2 * i + 1) * top_rows : (2 * i + 2) * top_rows]
        )
        for g in range(n_wide):
            for t in range(tiles):
                cols = slice(t * LANES, (t + 1) * LANES)
                line = total[g * tiles + t : g * tiles + t + 1, :]
                if g < len(near):
                    here = slice(g * atoms + t * LANES, g * atoms + (t + 1) * LANES)
                    line = line - jnp.sum(dr_ref[i, :, here], axis=0, keepdims=True)
                line = -HALF_STEP * line
                at = i * tiles + t
                if g == 0:
                    line = line + moment_ref[i, :, cols]
                    push_ref[at : at + 1, :] = blocks[0][i : i + 1, cols]
                push_ref[(1 + g) * lines + at : (1 + g) * lines + at + 1, :] = line
                mass = HEAVY - (HEAVY - 1.0) * blocks[g][3:4, cols]
                mass_ref[g * lines + at : g * lines + at + 1, :] = mass


def in_hbm(x):
    return pltpu.with_memory_space_constraint(x, pltpu.HBM)


def run(name, body, operands, results, scratch=(), far=(), cost=None):
    sizes = [math.prod(x.shape) * x.dtype.itemsize // 2 for i, x in enumerate(operands) if i not in far]
    sizes += [math.prod(shape) * jnp.dtype(dtype).itemsize for shape, dtype in results]
    sizes += [math.prod(x.shape) * x.dtype.itemsize for x in scratch if x.memory_space == pltpu.VMEM]
    limit = sum(sizes) + 4 * MIB
    specs = [pl.BlockSpec(memory_space=pltpu.HBM if i in far else pltpu.VMEM) for i in range(len(operands))]
    return pl.pallas_call(
        body,
        out_shape=tuple(jax.ShapeDtypeStruct(shape, dtype) for shape, dtype in results),
        in_specs=specs,
        out_specs=tuple(pl.BlockSpec(memory_space=pltpu.VMEM) for _ in results),
        scratch_shapes=list(scratch),
        compiler_params=pltpu.CompilerParams(vmem_limit_bytes=limit),
        cost_estimate=cost,
        name=name,
    )(*[in_hbm(x) if i in far else x for i, x in enumerate(operands)])


def choose(block, embedding, radial_one, radial_two, mix_one, mix_two, read_one, read_two):
    atoms = block.shape[1]
    slots = block.shape[0] - HEAD
    chan = embedding.shape[1]
    bases = radial_one.shape[0]
    weights = (embedding, radial_one, radial_two, mix_one, mix_two, read_one[None], read_two[None])
    return run(
        "choose",
        choose_kernel,
        (block, *weights),
        (
            ((2 * atoms, slots * atoms), bf16),
            ((chan, 12 * bases), bf16),
            ((chan, 6 * bases), bf16),
            ((chan, LANES), f32),
            ((4 * bases, 2 * chan), bf16),
            ((2, chan, 18 * chan), bf16),
            ((2, 3, chan, 3 * chan), bf16),
        ),
        [pltpu.VMEM(w.shape, f32) for w in weights] + [pltpu.SemaphoreType.DMA((len(weights),))],
        range(1, 1 + len(weights)),
        cost=pl.CostEstimate(flops=2 * 10**9, bytes_accessed=2 * 10**6, transcendentals=0),
    )


def pushes(plan, blocks, momenta, chosen):
    atoms, near, wide, _, _ = plan
    oh, rrc, r2c, sides, rrr, mixa, mixt = chosen
    chan = rrc.shape[0]
    bases = rrr.shape[0] // 4
    slots = blocks[0].shape[0] - HEAD
    n_near = len(near) * atoms
    edges = slots * atoms
    top_rows = -(-len(wide) * atoms // LANES // 8) * 8
    lines = line_count(atoms)
    geo, y, yb, ub, bk, bt, gidx, pick, as1 = run(
        "edges",
        functools.partial(edge_kernel, plan),
        blocks,
        (
            ((6, slots, n_near), f32),
            ((ORDERS - 1, slots, n_near), f32),
            ((ORDERS - 1, slots, 8, atoms), f32),
            ((3, slots, 8, atoms), f32),
            ((bases, slots, n_near), f32),
            ((slots, 2 * bases, n_near), f32),
            ((slots, n_near), jnp.int32),
            ((n_near, atoms), bf16),
            ((ORDERS, 12 * bases, n_near), bf16),
        ),
    )
    m1, sp1, hid, hs = run(
        "first",
        functools.partial(first_kernel, plan),
        (*blocks, as1, rrc, sides, mixa),
        (((ORDERS, chan, n_near), f32), ((chan, n_near), f32), ((chan, n_near), f32), ((3 * chan, n_near), bf16)),
        [pltpu.VMEM((8, n_near), f32)],
    )
    hj, w, slope, car = run(
        "gather",
        gather_kernel,
        (hid, hs, oh, pick, gidx, bt, geo, r2c),
        (((chan, edges), f32),) * 4,
        [pltpu.VMEM((3 * chan, 2 * atoms), bf16)],
    )
    m2, dinv = run(
        "moments",
        moment_kernel,
        (car, yb, mixa, mixt, sides),
        (((ORDERS, chan, atoms), f32), ((3 * chan, atoms), f32)),
        [pltpu.VMEM((3 * chan, atoms), f32)],
    )
    dhe, p = run(
        "back_second",
        back_second_kernel,
        (m2, dinv, car, hj, w, slope, ub),
        (((2 * chan, edges), bf16), ((4, 8 * slots, atoms), f32)),
    )
    dh, q, ohlo = run(
        "scatter",
        scatter_kernel,
        (oh, pick, dhe, sides, p, gidx),
        (((chan, n_near), f32), ((4 * slots, atoms), f32), ((LANES, slots * n_near), bf16)),
    )
    (da,) = run("back_first", back_first_kernel, (dh, sp1, m1, mixt, rrr), (((ORDERS, 2 * bases, n_near), f32),))
    return run(
        "back_edges",
        functools.partial(back_edge_kernel, plan),
        (*blocks, momenta, geo, y, bk, gidx, da, q, ohlo),
        ((((len(wide) + 1) * lines, LANES), f32), ((len(wide) * lines, LANES), f32)),
        [
            pltpu.VMEM((6 * top_rows, slots * n_near), bf16),
            pltpu.VMEM((3, slots, n_near), f32),
            pltpu.VMEM(momenta.shape, f32),
            pltpu.SemaphoreType.DMA(()),
        ],
        (len(blocks),),
    )


def line_count(atoms):
    return 3 * (atoms // LANES)


def ring_plan(domains, atoms):
    near = list(dict.fromkeys(o % domains for o in (0, 1, -1)))
    wide = list(dict.fromkeys(near + [o % domains for o in (2, -2)]))
    before = tuple(wide.index((o - 1) % domains) for o in near)
    after = tuple(wide.index((o + 1) % domains) for o in near)
    return atoms, tuple(near), tuple(wide), before, after


def mode_turns(bead_total):
    bead = np.arange(bead_total, dtype=np.float64)[:, None]
    mode = np.arange(bead_total, dtype=np.float64)[None, :]
    phase = 2.0 * np.pi * bead * mode / bead_total
    half_total = bead_total // 2
    table = math.sqrt(2.0 / bead_total) * np.where(mode < half_total, np.cos(phase), np.sin(phase))
    table = np.where(mode == half_total, np.cos(np.pi * bead) / math.sqrt(bead_total), table)
    table = np.where(mode == 0, 1.0 / math.sqrt(bead_total), table)
    angles = bead_total * np.sin(np.pi * mode[0] / bead_total)
    safe = np.where(mode[0] == 0, 1.0, angles)
    reach = np.where(mode[0] == 0, STEP, STEP * np.sin(angles) / safe)
    stiff = angles * np.sin(angles) / STEP
    return [[float(x) for x in (table * factor[None, :]) @ table[0]] for factor in (np.cos(angles), reach, stiff)]


def pack_kernel(coord_src, species_src, send_src, slot_src, block_ref, coord_ref, species_ref, send_ref, slot_ref, sems):
    pairs = ((coord_src, coord_ref), (species_src, species_ref), (send_src, send_ref), (slot_src, slot_ref))
    fetches = [pltpu.make_async_copy(src, dst, sems.at[i]) for i, (src, dst) in enumerate(pairs)]
    for fetch in fetches:
        fetch.start()
    for fetch in fetches:
        fetch.wait()
    atoms = block_ref.shape[1]
    for i in range(3):
        block_ref[i : i + 1, :] = coord_ref[i]
    block_ref[3:4, :] = species_ref[...].astype(f32)
    block_ref[4:5, :] = send_ref[...].astype(f32)
    block_ref[5:HEAD, :] = jnp.zeros((HEAD - 5, atoms), f32)
    block_ref[HEAD:, :] = slot_ref[...].astype(f32)


def turn_kernel(shape, bead_ref, domain_ref, mass_ref, *refs):
    outer, inner, domains, wide = shape
    message_ref = refs[outer]
    turns = mode_turns(outer * inner)
    lines = mass_ref.shape[0] // len(wide)
    my_domain = domain_ref[0]
    my_inner = lax.rem(bead_ref[0], inner)
    if domains > len(wide):
        message_ref[...] = jnp.zeros_like(message_ref)
    masses = [mass_ref[g * lines : (g + 1) * lines, :] for g in range(len(wide))]
    sources = []
    for z in range(outer):
        sources.append([refs[z][g * lines : (g + 1) * lines, :] for g in range(len(wide) + 1)])
    for s in range(inner):
        wraps = jnp.full((lines, LANES), my_inner + s) >= inner
        weights = []
        for turn in turns:
            row_of = []
            for z in range(outer):
                there = turn[(z * inner + s) % (outer * inner)]
                round_it = turn[(z * inner + s - inner) % (outer * inner)]
                row_of.append(jnp.where(wraps, jnp.full((lines, LANES), round_it), jnp.full((lines, LANES), there)))
            weights.append(row_of)
        to_inner = lax.rem(my_inner + s, inner)
        for g in range(len(wide)):
            turned = sum(weights[0][z] * sources[z][1 + g] for z in range(outer))
            drift = sum(weights[1][z] * sources[z][1 + g] for z in range(outer))
            new_q = drift / masses[g]
            new_p = turned
            if g == 0:
                new_q = new_q + sum(weights[0][z] * sources[z][0] for z in range(outer))
                new_p = new_p - masses[g] * sum(weights[2][z] * sources[z][0] for z in range(outer))
            to = to_inner * domains + lax.rem(my_domain + wide[g], domains)
            message_ref[to, 0:lines, :] = new_q
            message_ref[to, lines:, :] = new_p


def sum_kernel(arrived_ref, q_ref, p_ref):
    total = arrived_ref[0]
    for i in range(1, arrived_ref.shape[0]):
        total = total + arrived_ref[i]
    lines = total.shape[0] // 2
    tiles = q_ref.shape[2] // LANES
    for i in range(3):
        for t in range(tiles):
            at = i * tiles + t
            q_ref[i, :, t * LANES : (t + 1) * LANES] = total[at : at + 1]
            p_ref[i, :, t * LANES : (t + 1) * LANES] = total[lines + at : lines + at + 1]


def shards(
    positions, momenta, species, neighbours, send_list, embedding, radial_one, radial_two, mix_one, mix_two,
    read_one, read_two,
):
    slots, atoms = neighbours.shape
    domains = lax.axis_size("space")
    beads = lax.axis_size("bead")
    inner = next(d for d in range(1, beads + 1) if beads % d == 0 and d * d >= beads)
    outer = beads // inner
    plan = ring_plan(domains, atoms)
    wide = plan[2]
    vmem = pl.BlockSpec(memory_space=pltpu.VMEM)
    smem = pl.BlockSpec(memory_space=pltpu.SMEM)
    far = pl.BlockSpec(memory_space=pltpu.HBM)
    small = pltpu.CompilerParams(vmem_limit_bytes=4 * MIB)
    coord_rows = jnp.transpose(positions, (1, 0, 2))
    moment_rows = jnp.transpose(momenta, (1, 0, 2))
    block = pl.pallas_call(
        pack_kernel,
        out_shape=jax.ShapeDtypeStruct((HEAD + slots, atoms), f32),
        in_specs=[far] * 4,
        out_specs=vmem,
        scratch_shapes=[
            pltpu.VMEM(coord_rows.shape, f32),
            pltpu.VMEM((1, atoms), jnp.int32),
            pltpu.VMEM((1, atoms), jnp.int32),
            pltpu.VMEM((slots, atoms), jnp.int32),
            pltpu.SemaphoreType.DMA((4,)),
        ],
        compiler_params=small,
        name="pack",
    )(in_hbm(coord_rows), in_hbm(species[None]), in_hbm(send_list[None]), in_hbm(neighbours))
    blocks = [block]
    for offset in wide[1:]:
        blocks.append(lax.ppermute(block, "space", [(i, (i - offset) % domains) for i in range(domains)]))
    chosen = choose(block, embedding, radial_one, radial_two, mix_one, mix_two, read_one, read_two)
    pushed, masses = pushes(plan, blocks, moment_rows, chosen)
    sources = [pushed] * outer
    for z in sorted(range(1, outer), key=lambda z: -min(z, outer - z)):
        sources[z] = lax.ppermute(pushed, "bead", [(b, (b + z * inner) % beads) for b in range(beads)])
    here = [lax.axis_index(axis).astype(jnp.int32).reshape(1) for axis in ("bead", "space")]
    lines = line_count(atoms)
    messages = pl.pallas_call(
        functools.partial(turn_kernel, (outer, inner, domains, wide)),
        out_shape=jax.ShapeDtypeStruct((inner * domains, 2 * lines, LANES), f32),
        in_specs=[smem, smem, vmem] + [vmem] * outer,
        out_specs=vmem,
        compiler_params=small,
        name="turn",
    )(*here, masses, *sources)
    rows = [[z * inner * domains + i for i in range(inner * domains)] for z in range(outer)]
    arrived = lax.all_to_all(messages, ("bead", "space"), 0, 0, axis_index_groups=rows, tiled=True)
    new_q, new_p = pl.pallas_call(
        sum_kernel,
        out_shape=(jax.ShapeDtypeStruct((3, 1, atoms), f32),) * 2,
        in_specs=[vmem],
        out_specs=(vmem, vmem),
        compiler_params=small,
        name="sum",
    )(arrived)
    return (jnp.transpose(new_q, (1, 0, 2)), jnp.transpose(new_p, (1, 0, 2)))


def solution(mesh):
    placed = (
        P("bead", None, "space"),
        P("bead", None, "space"),
        P("space"),
        P(None, "space"),
        P("space"),
        P(),
        P(),
        P(),
        P(),
        P(),
        P(),
        P(),
    )
    return jax.shard_map(
        shards,
        mesh=mesh,
        in_specs=placed,
        out_specs=(P("bead", None, "space"), P("bead", None, "space")),
        check_vma=False,
    )
```
